32 devices in a mesh: gx: 4 (over z), gy: 8 (over y, x, core).
Axes of the slice: x: 2, y: 2, z: 4, core: 2. Of those that a mesh axis runs over, the one named last changes fastest.
Arguments:
- temps: float32 [2, 128, 96, 128], P(None, 'gx', 'gy'), may hold values from 0.5 to 2
- right_side: float32 [2, 128, 96, 128], P(None, 'gx', 'gy'), may hold values from -5 to 5
- exchange: float32 [128, 96, 128], P('gx', 'gy'), may hold values from 0.1 to 1
- coupling: float32 [128, 96, 128], P('gx', 'gy'), may hold values from 0.05 to 0.5
Outputs:
- fields: float32 [2, 128, 96, 128], P(None, 'gx', 'gy')
The draws below stay inside these ranges and needn't reach their ends.
All inputs are finite; a program needn't handle non-finite values.
Results may differ from the reference program's by a relative error of at most 0.000027.
Values sent between devices are 32-bit elements; how exact they have to be, the bound alone decides.
No kernel may reach another device: no remote copies, remote signals or barrier semaphores. Data moves between devices by JAX's collectives and lax.ppermute only.
A program may use at most 64 MiB of HBM per device.

```python
import math
import jax
import jax.numpy as jnp
from jax import lax

NZ = 128
SWEEPS = 2
NX = 128
NY = 96


def draw_right_side(key, part):
    shape = (2, NX, NY, NZ)
    return jnp.clip(jax.random.normal(key, shape, jnp.float32), -5.0, 5.0)


def shard_levels(key, shape, shards, least, top_value):
    gain, own = 1.0, jax.random.fold_in(key, 6)
    for axis_at, parts in shards:
        draws = jnp.exp(jax.random.uniform(jax.random.fold_in(own, axis_at), (parts,), jnp.float32, least / len(shards), top_value / len(shards)))
        gain = gain * jnp.repeat(draws, shape[axis_at] // parts).reshape([-1 if axis == axis_at else 1 for axis in range(len(shape))])
    return gain


def setup_inputs(seed: int = 0) -> dict:
    key_list = jax.random.split(jax.random.key(seed), 5)
    return {
        "temps": jnp.clip(0.5 + 1.5 * jax.random.uniform(key_list[0], (2, NX, NY, NZ), jnp.float32) ** shard_levels(key_list[0], (2, NX, NY, NZ), ((1, 4), (2, 8)), -0.2, 0.2), 0.5, 2.0),
        "right_side": draw_right_side(jax.random.fold_in(key_list[4], 71), 0),
        "exchange": jnp.clip(jnp.exp(math.log(1.0) - 2.3025851 * jax.random.uniform(key_list[2], (NX, NY, NZ), jnp.float32) ** shard_levels(key_list[2], (NX, NY, NZ), ((0, 4), (1, 8)), -0.2, 0.2)), 0.1, 1.0),
        "coupling": jnp.clip(jnp.exp(math.log(0.5) - 2.3025851 * jax.random.uniform(key_list[3], (NX, NY, NZ), jnp.float32) ** shard_levels(key_list[3], (NX, NY, NZ), ((0, 4), (1, 8)), -0.2, 0.2)), 0.05, 0.5),
    }


solid_cap = 0.5
gas_cap = 0.02
flow_rate = 40.0
gas_conduct = 0.05
axis_weights = (1.0, 1.0, 1.0, 1.0, 0.25, 0.25)
relaxation = 0.8
lump_factor = 0.25


def neighbours(padded):
    center = padded[1:-1, 1:-1]
    z_padded = jnp.pad(center, ((0, 0), (0, 0), (1, 1)))
    return center, (padded[2:, 1:-1], padded[:-2, 1:-1], padded[1:-1, 2:], padded[1:-1, :-2], z_padded[:, :, 2:], z_padded[:, :, :-2])


def face_weights(cond_padded):
    conductivity, beside_all = neighbours(cond_padded)
    return tuple(weight * 0.5 * (conductivity + other) for weight, other in zip(axis_weights, beside_all))


def apply_operator(fields_padded, face_list, coupling):
    solid, solid_around = neighbours(fields_padded[0])
    gas, gas_around = neighbours(fields_padded[1])
    exchange_term = coupling * (solid - gas)
    solid_out = solid_cap * solid + exchange_term
    gas_out = gas_cap * gas - exchange_term + flow_rate * (gas - gas_around[3])
    for face, weight, other_solid, other_gas in zip(face_list, axis_weights, solid_around, gas_around):
        solid_out = solid_out + face * (solid - other_solid)
        gas_out = gas_out + gas_conduct * weight * (gas - other_gas)
    return jnp.stack([solid_out, gas_out])


def relax_step(fields, residual, solid_diag, coupling):
    gas_diag = gas_cap + coupling + flow_rate + gas_conduct * 2.0 * 2.25
    determinant = solid_diag * gas_diag - coupling * coupling
    delta_solid = (gas_diag * residual[0] + coupling * residual[1]) / determinant
    delta_gas = (coupling * residual[0] + solid_diag * residual[1]) / determinant
    return fields + relaxation * jnp.stack([delta_solid, delta_gas])


def coarse_sum(array):
    shape = array.shape
    lead = shape[:-3]
    return array.reshape(lead + (shape[-3] // 2, 2, shape[-2] // 2, 2, shape[-1])).sum(axis=(-4, -2))


def spread(coarse):
    shape = coarse.shape
    wide = jnp.broadcast_to(coarse[:, :, None, :, None, :], (shape[0], shape[1], 2, shape[2], 2, shape[3]))
    return wide.reshape((shape[0], shape[1] * 2, shape[2] * 2, shape[3]))


def line_combine(earlier, later):
    return (later[0] * earlier[0], later[0] * earlier[1] + later[1])


def reference(temps, right_side, exchange, coupling):
    conductivity = 1.0 + 4.0 * exchange * temps[0] ** 3
    face_list = face_weights(jnp.pad(conductivity, ((1, 1), (1, 1), (0, 0))))
    solid_diag = solid_cap + coupling + sum(face_list)

    def residual_of(fields):
        padded = jnp.pad(fields, ((0, 0), (1, 1), (1, 1), (0, 0)))
        return right_side - apply_operator(padded, face_list, coupling)

    fields = temps
    for sweep_index in range(SWEEPS):
        fields = relax_step(fields, residual_of(fields), solid_diag, coupling)
    coarse_res = coarse_sum(residual_of(fields))
    coupling_sum = coarse_sum(coupling)
    solid_coarse = 4.0 * solid_cap + coupling_sum + lump_factor * coarse_sum(conductivity)
    gas_coarse = 4.0 * gas_cap + coupling_sum + 2.0 * flow_rate
    denominator = gas_coarse - coupling_sum * coupling_sum / solid_coarse
    slope = 2.0 * flow_rate / denominator
    offset = (coarse_res[1] + coupling_sum * coarse_res[0] / solid_coarse) / denominator
    slope_cum, gas_error = lax.associative_scan(line_combine, (slope, offset), axis=1)
    solid_error = (coarse_res[0] + coupling_sum * gas_error) / solid_coarse
    fields = fields + spread(jnp.stack([solid_error, gas_error]))
    for sweep_index in range(SWEEPS):
        fields = relax_step(fields, residual_of(fields), solid_diag, coupling)
    return fields
```

```python
import jax
import jax.numpy as jnp
from jax import lax
from jax.sharding import PartitionSpec as P

solid_cap = 0.5
gas_cap = 0.02
flow_rate = 40.0
gas_conduct = 0.05
relaxation = 0.8
lump_factor = 0.25

WX, WY = 5, 4


def swap_pairs(count, first):
    pairs = []
    for i in range(first, count - 1, 2):
        pairs += [(i, i + 1), (i + 1, i)]
    return pairs


def edges_of(x, axis, dim, width):
    count, length = lax.axis_size(axis), x.shape[dim]
    even = lax.axis_index(axis) % 2 == 0
    first = lax.slice_in_dim(x, 0, width, axis=dim)
    last = lax.slice_in_dim(x, length - width, length, axis=dim)
    one = lax.ppermute(jnp.where(even, last, first), axis, swap_pairs(count, 0))
    two = lax.ppermute(jnp.where(even, first, last), axis, swap_pairs(count, 1))
    return jnp.where(even, two, one), jnp.where(even, one, two)


def widened(x, axis, dim, width):
    before, after = edges_of(x, axis, dim, width)
    return jnp.concatenate([before, x, after], axis=dim)


def inside(axis, length, width):
    at = lax.axis_index(axis) * length + jnp.arange(-width, length + width)
    return ((at >= 0) & (at < lax.axis_size(axis) * length)).astype(jnp.float32)


def z_next(x):
    return jnp.pad(x[..., 1:], ((0, 0), (0, 0), (0, 1)))


def z_prev(x):
    return jnp.pad(x[..., :-1], ((0, 0), (0, 0), (1, 0)))


def crop(x, dx, dy):
    return x[dx : x.shape[0] - dx, dy : x.shape[1] - dy]


def residual(s, g, rs, rg, c, fx, fy, fz, diag):
    sc, gc = s[1:-1, 1:-1], g[1:-1, 1:-1]
    around_s = (
        fx[1:] * s[2:, 1:-1]
        + fx[:-1] * s[:-2, 1:-1]
        + fy[:, 1:] * s[1:-1, 2:]
        + fy[:, :-1] * s[1:-1, :-2]
        + fz * z_next(sc)
        + z_prev(fz * sc)
    )
    gas_diag = gas_cap + c + flow_rate + gas_conduct * 2.0 * 2.25
    around_g = gas_conduct * (
        g[2:, 1:-1] + g[:-2, 1:-1] + g[1:-1, 2:] + g[1:-1, :-2] + 0.25 * (z_next(gc) + z_prev(gc))
    ) + flow_rate * g[1:-1, :-2]
    res_s = rs - diag * sc + c * gc + around_s
    res_g = rg - gas_diag * gc + c * sc + around_g
    return res_s, res_g


def coarse_sum(a):
    return a.reshape(a.shape[0] // 2, 2, a.shape[1] // 2, 2, a.shape[2]).sum(axis=(1, 3))


def spread(a):
    x, y, z = a.shape
    return jnp.broadcast_to(a[:, None, :, None, :], (x, 2, y, 2, z)).reshape(2 * x, 2 * y, z)


def shards(temps, right_side, exchange, coupling):
    nx, ny, nz = exchange.shape
    fields = jnp.concatenate([temps, right_side, exchange[None], coupling[None]])
    fields = widened(fields, "gx", 1, WX)
    fields = widened(fields, "gy", 2, WY)
    s, g, rs, rg, e, c = (fields[k] for k in range(6))
    mask = (inside("gx", nx, WX)[:, None] * inside("gy", ny, WY)[None, :])[:, :, None]

    cond = (1.0 + 4.0 * e * s * s * s) * mask
    fx = 0.5 * (cond[1:] + cond[:-1])
    fy = 0.5 * (cond[:, 1:] + cond[:, :-1])
    fz_up = 0.125 * (cond + z_next(cond))
    fz_down = 0.125 * (cond + z_prev(cond))
    rs, rg, c, m = (crop(a, 1, 1) for a in (rs, rg, c, mask))
    fx, fy = fx[:, 1:-1], fy[1:-1]
    fz = crop(fz_up, 1, 1)
    diag = solid_cap + c + fx[1:] + fx[:-1] + fy[:, 1:] + fy[:, :-1] + fz + crop(fz_down, 1, 1)
    gas_diag = gas_cap + c + flow_rate + gas_conduct * 2.0 * 2.25
    inv = m * relaxation / (diag * gas_diag - c * c)
    a_ss, a_sg, a_gg = inv * gas_diag, inv * c, inv * diag

    def parts(dx, dy):
        fxk = fx[dx : fx.shape[0] - dx, dy : fx.shape[1] - dy]
        fyk = fy[dx : fy.shape[0] - dx, dy : fy.shape[1] - dy]
        return [crop(rs, dx, dy), crop(rg, dx, dy), crop(c, dx, dy), fxk, fyk, crop(fz, dx, dy), crop(diag, dx, dy)]

    def sweep(s, g, dx, dy):
        res_s, res_g = residual(s, g, *parts(dx, dy))
        ss, sg, gg = (crop(a, dx, dy) for a in (a_ss, a_sg, a_gg))
        return s[1:-1, 1:-1] + ss * res_s + sg * res_g, g[1:-1, 1:-1] + sg * res_s + gg * res_g

    s, g = sweep(s, g, 0, 0)
    s, g = sweep(s, g, 1, 1)
    hx, hy = WX - 3, WY - 3
    res_s, res_g = residual(s, g, *parts(2, 2))
    res_s, res_g = (crop(a, 0, hy) for a in (res_s, res_g))
    mk = crop(mask, WX - 2, WY)
    res_s, res_g = coarse_sum(res_s * mk), coarse_sum(res_g * mk)
    c_sum = coarse_sum(crop(c, WX - 3, WY - 1))
    k_sum = coarse_sum(crop(cond, WX - 2, WY))
    solid_coarse = 4.0 * solid_cap + c_sum + lump_factor * k_sum
    gas_coarse = 4.0 * gas_cap + c_sum + 2.0 * flow_rate
    lead, ratio = res_s / solid_coarse, c_sum / solid_coarse
    denominator = gas_coarse - c_sum * ratio
    slope = 2.0 * flow_rate / denominator
    offset = (res_g + c_sum * lead) / denominator

    rows = ny // 2
    slopes, offsets = [slope[:, 0]], [offset[:, 0]]
    for j in range(1, rows):
        slopes.append(slope[:, j] * slopes[-1])
        offsets.append(slope[:, j] * offsets[-1] + offset[:, j])

    count, me = lax.axis_size("gy"), lax.axis_index("gy")
    onward = jnp.stack([slopes[-1], offsets[-1], lead[:, -1], ratio[:, -1]])
    back = jnp.stack([slope[:, 0], offset[:, 0], lead[:, 0], ratio[:, 0]])
    to = jnp.arange(count)[:, None, None, None]
    sent = jnp.where(to > me, onward[None], back[None])
    got = lax.all_to_all(sent, "gy", 0, 0)
    gas_in = jnp.zeros_like(slopes[0])
    for d in range(count - 1):
        gas_in = jnp.where(d < me, got[d, 0] * gas_in + got[d, 1], gas_in)
    before = lax.dynamic_index_in_dim(got, jnp.maximum(me - 1, 0), 0, False)
    after = lax.dynamic_index_in_dim(got, jnp.minimum(me + 1, count - 1), 0, False)
    gas_err = [gas_in] + [slopes[j] * gas_in + offsets[j] for j in range(rows)]
    gas_err.append(after[0] * gas_err[-1] + after[1])
    gas_err = jnp.stack(gas_err, axis=1)
    lead = jnp.concatenate([before[2][:, None], lead, after[2][:, None]], axis=1)
    ratio = jnp.concatenate([before[3][:, None], ratio, after[3][:, None]], axis=1)
    solid_err = lead + ratio * gas_err
    mk = crop(mask, WX - 2, WY - 2)
    s = crop(s, 1, 0) + mk * spread(solid_err)
    g = crop(g, 1, 0) + mk * spread(gas_err)
    s, g = sweep(s, g, WX - 2, WY - 2)
    s, g = sweep(s, g, WX - 1, WY - 1)
    return jnp.stack([s, g])


def solution(mesh):
    return jax.shard_map(
        shards,
        mesh=mesh,
        in_specs=(
            P(None, "gx", "gy", None),
            P(None, "gx", "gy", None),
            P("gx", "gy", None),
            P("gx", "gy", None),
        ),
        out_specs=P(None, "gx", "gy", None),
        check_vma=False,
    )
```

```python
import functools

import jax
import jax.numpy as jnp
from jax import lax
from jax.experimental import pallas as pl
from jax.experimental.pallas import tpu as pltpu
from jax.sharding import PartitionSpec as P

SOLID_CAP, GAS_CAP, FLOW, CONDUCT, RELAX, LUMP = 0.5, 0.02, 40.0, 0.05, 0.8, 0.25
GAS_SELF = GAS_CAP + 4.5 * CONDUCT

PAD = 8
WX = 5
CROP = 4
(SA, GA, SB, GB, K, C, RS, RG, FX, FZ, H, FY, ASS, ASG, AGG) = range(15)
PLANES = 15
(M_S, M_G, M_K, M_C, M_FY, M_C2, M_D2, M_1S, M_1G, M_2S, M_2G, M_3S, M_3G) = range(13)
MESSAGE = 13

VMEM = pl.BlockSpec(memory_space=pltpu.VMEM)
PARAMS = pltpu.CompilerParams(vmem_limit_bytes=40 * 1024 * 1024)


def up_x(v):
    return pltpu.roll(v, v.shape[0] - 1, 0)


def down_x(v):
    return pltpu.roll(v, 1, 0)


def up_z(v):
    return pltpu.roll(v, v.shape[1] - 1, 1)


def down_z(v):
    return pltpu.roll(v, 1, 1)


def lanes(shape):
    return lax.broadcasted_iota(jnp.int32, shape, 1)


def x_mask(shape, nx):
    row = lax.broadcasted_iota(jnp.int32, shape, 0)
    place, count = lax.axis_index("gx"), lax.axis_size("gx")
    low = jnp.where(place == 0, PAD, PAD - WX)
    high = jnp.where(place == count - 1, PAD + nx, PAD + nx + WX)
    return jnp.where((row >= low) & (row < high), 1.0, 0.0).astype(jnp.float32)


def pack_kernel(temps, right, exchange, coupling, one, two):
    even = lax.axis_index("gx") % 2 == 0
    top = exchange.shape[1]
    parts = [(temps, 0, WX), (temps, 1, WX), (exchange, None, WX)]
    parts += [(right, 0, WX - 1), (right, 1, WX - 1), (coupling, None, WX - 1)]

    def row(y, carry):
        at = 0
        for ref, plane, width in parts:
            lead = (y,) if plane is None else (plane, y)
            low = ref[lead + (slice(0, width),)]
            high = ref[lead + (slice(top - width, top),)]
            one[y, at : at + width] = jnp.where(even, high, low)
            two[y, at : at + width] = jnp.where(even, low, high)
            at += width
        return carry

    lax.fori_loop(0, one.shape[0], row, 0)


def inner(s, g, c, h, fx, fz, edge):
    t = c * (s - g)
    flux_x = fx * (up_x(s) - s)
    flux_z = fz * (up_z(s) - s)
    part_s = (flux_x - down_x(flux_x)) + (flux_z - down_z(flux_z)) - h * s - t
    part_g = (
        t
        - GAS_SELF * g
        + CONDUCT * (up_x(g) + down_x(g))
        + edge[0] * up_z(g)
        + edge[1] * down_z(g)
    )
    return part_s, part_g


def edge_weights(shape):
    lane = lanes(shape)
    weight = jnp.float32(0.25 * CONDUCT)
    return jnp.where(lane == shape[1] - 1, 0.0, weight), jnp.where(lane == 0, 0.0, weight)


def row_inner(st, i, s_at, edge):
    return inner(st[s_at, i], st[s_at + 1, i], st[C, i], st[H, i], st[FX, i], st[FZ, i], edge)


def row_residual(st, i, s_at, edge):
    part_s, part_g = row_inner(st, i, s_at, edge)
    s, g, before = st[s_at, i], st[s_at + 1, i], st[s_at + 1, i - 1]
    part_s += st[FY, i] * (st[s_at, i + 1] - s) + st[FY, i - 1] * (st[s_at, i - 1] - s)
    part_g += CONDUCT * (st[s_at + 1, i + 1] + before) - FLOW * (g - before)
    return st[RS, i] + part_s, st[RG, i] + part_g


def relaxed(st, i, s_at, res_s, res_g):
    s = st[s_at, i] + st[ASS, i] * res_s + st[ASG, i] * res_g
    g = st[s_at + 1, i] + st[ASG, i] * res_s + st[AGG, i] * res_g
    return s, g


def faces(st, i):
    k = st[K, i]
    lane = lanes(k.shape)
    end = k.shape[1] - 1
    fx = 0.5 * (k + up_x(k))
    fz = jnp.where(lane == end, 0.0, 0.125 * (k + up_z(k)))
    h = SOLID_CAP + jnp.where((lane == 0) | (lane == end), 0.125 * k, 0.0)
    st[FX, i] = fx
    st[FZ, i] = fz
    st[H, i] = h
    return h + (fx + down_x(fx)) + (fz + down_z(fz))


def inverse(diag, c, mask):
    gas_diag = (GAS_SELF + FLOW) + c
    inv = (RELAX * mask) / (diag * gas_diag - c * c)
    return inv * gas_diag, inv * c, inv * diag


def store_inverse(st, i, diag, mask):
    st[ASS, i], st[ASG, i], st[AGG, i] = inverse(diag, st[C, i], mask)


def first_kernel(temps, right, exchange, coupling, one, two, st, out_one, out_two):
    ny, nx, nz = exchange.shape
    ext = nx + 2 * PAD
    even = lax.axis_index("gx") % 2 == 0
    shape = (ext, nz)
    mask = x_mask(shape, nx)
    edge = edge_weights(shape)
    zeros = jnp.zeros((PAD, nz), jnp.float32)

    def build(y, carry):
        i = y + 1
        at = 0
        for plane, own, width in (
            (SA, temps[0, y], WX),
            (GA, temps[1, y], WX),
            (K, exchange[y], WX),
            (RS, right[0, y], WX - 1),
            (RG, right[1, y], WX - 1),
            (C, coupling[y], WX - 1),
        ):
            a, b = one[y, at : at + width], two[y, at : at + width]
            st[plane, i, :PAD] = zeros
            st[plane, i, PAD + nx :] = zeros
            st[plane, i, PAD - width : PAD] = jnp.where(even, b, a)
            st[plane, i, PAD + nx : PAD + nx + width] = jnp.where(even, a, b)
            st[plane, i, PAD : PAD + nx] = own
            at += width
        return carry

    lax.fori_loop(0, ny, build, 0)

    def conduct(y, carry):
        s = st[SA, y + 1]
        st[K, y + 1] = (1.0 + 4.0 * st[K, y + 1] * s * s * s) * mask
        return carry

    lax.fori_loop(0, ny, conduct, 0)

    def row_diag(i):
        diag = faces(st, i) + st[C, i]
        st[FY, i] = 0.5 * (st[K, i] + st[K, i + 1])
        return diag + st[FY, i] + st[FY, i - 1]

    faces(st, 1)
    faces(st, ny)
    st[FY, 1] = 0.5 * (st[K, 1] + st[K, 2])

    def sweep(i, carry):
        store_inverse(st, i, row_diag(i), mask)
        st[SB, i], st[GB, i] = relaxed(st, i, SA, *row_residual(st, i, SA, edge))
        return carry

    lax.fori_loop(2, ny, sweep, 0)

    def diag_of(i):
        fx, fz = st[FX, i], st[FZ, i]
        return st[H, i] + (fx + down_x(fx)) + (fz + down_z(fz)) + st[C, i] + st[FY, i] + st[FY, i - 1]

    e, d = ny, ny - 1
    s, g, fy = st[SA, e], st[GA, e], st[FY, d]
    part_s, part_g = row_inner(st, e, SA, edge)
    m1s = st[RS, e] + part_s + fy * (st[SA, d] - s)
    m1g = st[RG, e] + part_g + CONDUCT * st[GA, d] - FLOW * (g - st[GA, d])
    s1, g1 = st[SB, d], st[GB, d]
    m2s = st[RS, e] + fy * s1
    m2g = st[RG, e] + (CONDUCT + FLOW) * g1
    part_s, part_g = row_inner(st, d, SB, edge)
    m3s = st[RS, d] + part_s - fy * s1 + st[FY, d - 1] * (st[SB, d - 1] - s1)
    m3g = st[RG, d] + part_g + CONDUCT * st[GB, d - 1] - FLOW * (g1 - st[GB, d - 1])
    onward = [s, g, st[K, e], st[C, e], fy, st[C, d], diag_of(d), m1s, m1g, m2s, m2g, m3s, m3g]

    e, d = 1, 2
    s, g, fy = st[SA, e], st[GA, e], st[FY, e]
    part_s, part_g = row_inner(st, e, SA, edge)
    m1s = st[RS, e] + part_s + fy * (st[SA, d] - s)
    m1g = st[RG, e] + part_g + CONDUCT * st[GA, d] - FLOW * g
    s1, g1 = st[SB, d], st[GB, d]
    m2s = st[RS, e] + fy * s1
    m2g = st[RG, e] + CONDUCT * g1
    part_s, part_g = row_inner(st, d, SB, edge)
    m3s = st[RS, d] + part_s - fy * s1 + st[FY, d] * (st[SB, d + 1] - s1)
    m3g = st[RG, d] + part_g + CONDUCT * st[GB, d + 1] - FLOW * g1
    back = [s, g, st[K, e], st[C, e], fy, st[C, d], diag_of(d), m1s, m1g, m2s, m2g, m3s, m3g]

    even_y = lax.axis_index("gy") % 2 == 0
    for plane, (a, b) in enumerate(zip(onward, back)):
        a, b = a[CROP : ext - CROP], b[CROP : ext - CROP]
        out_one[plane] = jnp.where(even_y, a, b)
        out_two[plane] = jnp.where(even_y, b, a)


def outer_residual(st, i, s_at, rs, rg, fy_out, edge, after):
    part_s, part_g = row_inner(st, i, s_at, edge)
    s, g = st[s_at, i], st[s_at + 1, i]
    if after:
        part_s += st[FY, i - 1] * (st[s_at, i - 1] - s)
        part_g += (CONDUCT + FLOW) * st[s_at + 1, i - 1]
    else:
        part_s += st[FY, i] * (st[s_at, i + 1] - s)
        part_g += CONDUCT * st[s_at + 1, i + 1]
    return rs + part_s - fy_out * s, rg + part_g - FLOW * g


def pair_x(v):
    row = lax.broadcasted_iota(jnp.int32, v.shape, 0)
    return v + jnp.where(row % 2 == 0, up_x(v), down_x(v))


def second_kernel(st_in, one, two, st, extra, coarse, sides, message, before, after, squeeze):
    del st_in
    planes, rows, ext, nz = st.shape
    ny, nx = rows - 2, ext - 2 * PAD
    shape = (ext, nz)
    me, count = lax.axis_index("gy"), lax.axis_size("gy")
    even = me % 2 == 0
    mask = x_mask(shape, nx)
    low = jnp.where(me == 0, 0.0, mask)
    high = jnp.where(me == count - 1, 0.0, mask)
    edge = edge_weights(shape)
    zeros = jnp.zeros((PAD, nz), jnp.float32)

    def unpack(plane, carry):
        a, b = one[plane], two[plane]
        for ref, v in ((before, jnp.where(even, b, a)), (after, jnp.where(even, a, b))):
            ref[plane, :PAD] = zeros
            ref[plane, ext - PAD :] = zeros
            ref[plane, CROP : ext - CROP] = v
        return carry

    lax.fori_loop(0, MESSAGE, unpack, 0)

    last = ny + 1
    for i, ref in ((0, before), (last, after)):
        st[SA, i], st[GA, i], st[K, i], st[C, i] = ref[M_S], ref[M_G], ref[M_K], ref[M_C]
    st[FY, 0] = 0.5 * (st[K, 0] + st[K, 1])
    st[FY, ny] = 0.5 * (st[K, ny] + st[K, last])

    def diag_of(i):
        fx, fz = st[FX, i], st[FZ, i]
        return st[H, i] + (fx + down_x(fx)) + (fz + down_z(fz)) + st[C, i]

    store_inverse(st, 1, diag_of(1) + st[FY, 0] + st[FY, 1], mask)
    store_inverse(st, ny, diag_of(ny) + st[FY, ny - 1] + st[FY, ny], mask)
    store_inverse(st, 0, faces(st, 0) + st[C, 0] + before[M_FY] + st[FY, 0], low)
    store_inverse(st, last, faces(st, last) + st[C, last] + after[M_FY] + st[FY, ny], high)

    res_s = before[M_1S] + st[FY, 0] * (st[SA, 1] - st[SA, 0])
    res_g = before[M_1G] + CONDUCT * st[GA, 1]
    st[SB, 0], st[GB, 0] = relaxed(st, 0, SA, res_s, res_g)
    res_s = after[M_1S] + st[FY, ny] * (st[SA, ny] - st[SA, last])
    res_g = after[M_1G] + (CONDUCT + FLOW) * st[GA, ny]
    st[SB, last], st[GB, last] = relaxed(st, last, SA, res_s, res_g)
    for i in (1, ny):
        st[SB, i], st[GB, i] = relaxed(st, i, SA, *row_residual(st, i, SA, edge))

    for i, ref, is_after, inside in ((0, before, False, low), (last, after, True, high)):
        res = outer_residual(st, i, SB, ref[M_2S], ref[M_2G], ref[M_FY], edge, is_after)
        st[SA, i], st[GA, i] = relaxed(st, i, SB, *res)
        ss, sg, gg = inverse(jnp.maximum(ref[M_D2], SOLID_CAP), ref[M_C2], inside)
        to, back = (CONDUCT + FLOW, CONDUCT) if is_after else (CONDUCT, CONDUCT + FLOW)
        res_s = ref[M_3S] + ref[M_FY] * st[SB, i]
        res_g = ref[M_3G] + to * st[GB, i]
        side = 3 if is_after else 0
        extra[side] = ref[M_2S] + ref[M_FY] * (ss * res_s + sg * res_g)
        extra[side + 1] = ref[M_2G] + back * (sg * res_s + gg * res_g)
        extra[side + 2] = ref[M_FY]

    def sweep(i, carry):
        st[SA, i], st[GA, i] = relaxed(st, i, SB, *row_residual(st, i, SB, edge))
        return carry

    lax.fori_loop(1, ny + 1, sweep, 0)

    def coefficients(c_sum, k_sum):
        solid = 4.0 * SOLID_CAP + c_sum + LUMP * k_sum
        ratio = c_sum / solid
        denominator = (4.0 * GAS_CAP + 2.0 * FLOW) + c_sum - c_sum * ratio
        return solid, ratio, denominator

    def coarse_row(j, carry):
        slopes, offsets = carry
        i = 2 * j + 1
        res_s, res_g = row_residual(st, i, SA, edge)
        more_s, more_g = row_residual(st, i + 1, SA, edge)
        res_s, res_g = pair_x((res_s + more_s) * mask), pair_x((res_g + more_g) * mask)
        c_sum = pair_x(st[C, i] + st[C, i + 1])
        solid, ratio, denominator = coefficients(c_sum, pair_x(st[K, i] + st[K, i + 1]))
        lead = res_s / solid
        slope = (2.0 * FLOW) / denominator
        offset = (res_g + c_sum * lead) / denominator
        slopes, offsets = slope * slopes, slope * offsets + offset
        coarse[0, j], coarse[1, j], coarse[2, j], coarse[3, j] = lead, ratio, slopes, offsets
        return slopes, offsets

    blocks = ny // 2
    slopes, offsets = lax.fori_loop(0, blocks, coarse_row, (jnp.ones(shape, jnp.float32), jnp.zeros(shape, jnp.float32)))

    for side, (i, ref) in enumerate(((0, before), (last, after))):
        k2 = 2.0 * ref[M_FY] - ref[M_K]
        solid, ratio, denominator = coefficients(pair_x(ref[M_C] + ref[M_C2]), pair_x(ref[M_K] + k2))
        sides[side] = ratio
        if side:
            sides[2] = (2.0 * FLOW) / denominator

    squeeze[0], squeeze[1], squeeze[2] = slopes, offsets, coarse[0, blocks - 1]
    squeeze[3], squeeze[4] = coarse[0, 0], coarse[3, 0]
    span = nx // 2 + 2
    pick = pl.ds(PAD - 2, span, 2)
    thin = [squeeze[k, pick, :] for k in range(5)]
    blank = jnp.zeros_like(thin[0])

    def fill(d, carry):
        onward = d > me
        for k, (a, b) in enumerate(zip(thin[:3], thin[3:] + [blank])):
            message[d, k * span : (k + 1) * span] = jnp.where(onward, a, b)
        return carry

    lax.fori_loop(0, count, fill, 0)


def third_kernel(st, extra, coarse, sides, got, out, sc, wide):
    planes, rows, ext, nz = st.shape
    ny, nx = rows - 2, ext - 2 * PAD
    shape = (ext, nz)
    me, count = lax.axis_index("gy"), lax.axis_size("gy")
    edge = edge_weights(shape)
    span = nx // 2 + 2
    blocks = ny // 2

    def fold(d, gas):
        return got[d, :span] * gas + got[d, span : 2 * span]

    gas_in = lax.fori_loop(0, me, fold, jnp.zeros((span, nz), jnp.float32))
    inside_low, inside_high = me > 0, me < count - 1
    prev, following = jnp.maximum(me - 1, 0), jnp.minimum(me + 1, count - 1)
    lead_low = jnp.where(inside_low, got[prev, 2 * span : 3 * span], 0.0)
    lead_high = jnp.where(inside_high, got[following, :span], 0.0)
    offset_high = jnp.where(inside_high, got[following, span : 2 * span], 0.0)
    for k, v in enumerate((gas_in, lead_low, lead_high, offset_high)):
        wide[k, : PAD - 2] = jnp.zeros((PAD - 2, nz), jnp.float32)
        wide[k, ext - PAD + 2 :] = jnp.zeros((PAD - 2, nz), jnp.float32)
        wide[k, pl.ds(PAD - 2, span, 2), :] = v
        wide[k, pl.ds(PAD - 1, span, 2), :] = v

    gas_in = wide[0]
    last = ny + 1
    solid_low = wide[1] + sides[0] * gas_in
    sc[0, 0] = st[SA, 0] + solid_low
    sc[1, 0] = st[GA, 0] + gas_in

    def correct(j, carry):
        gas = coarse[2, j] * gas_in + coarse[3, j]
        solid = coarse[0, j] + coarse[1, j] * gas
        for i in (2 * j + 1, 2 * j + 2):
            sc[0, i] = st[SA, i] + solid
            sc[1, i] = st[GA, i] + gas
        return carry

    lax.fori_loop(0, blocks, correct, 0)
    gas = coarse[2, blocks - 1] * gas_in + coarse[3, blocks - 1]
    gas_high = jnp.where(inside_high, sides[2] * gas + wide[3], 0.0)
    solid_high = wide[2] + sides[1] * gas_high
    sc[0, last] = st[SA, last] + solid_high
    sc[1, last] = st[GA, last] + gas_high

    view = Fields(st, sc)
    for i, is_after, solid, gas in ((0, False, solid_low, gas_in), (last, True, solid_high, gas_high)):
        side = 3 if is_after else 0
        fy = extra[side + 2]
        rs = extra[side] + fy * solid
        rg = extra[side + 1] + (CONDUCT if is_after else CONDUCT + FLOW) * gas
        res = outer_residual(view, i, SA, rs, rg, fy, edge, is_after)
        sc[2, i], sc[3, i] = relaxed(view, i, SA, *res)

    def sweep(i, carry):
        sc[2, i], sc[3, i] = relaxed(view, i, SA, *row_residual(view, i, SA, edge))
        return carry

    lax.fori_loop(1, ny + 1, sweep, 0)

    def final(i, carry):
        s, g = relaxed(view, i, SB, *row_residual(view, i, SB, edge))
        out[0, i - 1] = s[PAD : PAD + nx]
        out[1, i - 1] = g[PAD : PAD + nx]
        return carry

    lax.fori_loop(1, ny + 1, final, 0)


class Fields:
    def __init__(self, st, sc):
        self.st, self.sc = st, sc

    def __getitem__(self, at):
        return (self.sc if at[0] <= GB else self.st)[at]


def swap(one, two, axis):
    def pairs(first):
        out = []
        for i in range(first, lax.axis_size(axis) - 1, 2):
            out += [(i, i + 1), (i + 1, i)]
        return out

    return lax.ppermute(one, axis, pairs(0)), lax.ppermute(two, axis, pairs(1))


def shards(temps, right_side, exchange, coupling):
    temps, right_side = (jnp.transpose(a, (0, 2, 1, 3)) for a in (temps, right_side))
    exchange, coupling = (jnp.transpose(a, (1, 0, 2)) for a in (exchange, coupling))
    ny, nx, nz = exchange.shape
    ext = nx + 2 * PAD
    f32 = functools.partial(jax.ShapeDtypeStruct, dtype=jnp.float32)

    strip = f32((ny, 32, nz))
    one, two = pl.pallas_call(
        pack_kernel,
        out_shape=(strip, strip),
        in_specs=[VMEM] * 4,
        out_specs=(VMEM, VMEM),
        compiler_params=PARAMS,
        name="pack_x",
    )(temps, right_side, exchange, coupling)
    one, two = swap(one, two, "gx")

    state = f32((PLANES, ny + 2, ext, nz))
    letter = f32((MESSAGE, ext - 2 * CROP, nz))
    st, one, two = pl.pallas_call(
        first_kernel,
        out_shape=(state, letter, letter),
        in_specs=[VMEM] * 6,
        out_specs=(VMEM,) * 3,
        compiler_params=PARAMS,
        name="first",
    )(temps, right_side, exchange, coupling, one, two)
    one, two = swap(one, two, "gy")

    count = lax.axis_size("gy")
    span = nx // 2 + 2
    height = (3 * span + 7) // 8 * 8
    st, extra, coarse, sides, message = pl.pallas_call(
        second_kernel,
        out_shape=(state, f32((6, ext, nz)), f32((4, ny // 2, ext, nz)), f32((3, ext, nz)), f32((count, height, nz))),
        in_specs=[VMEM] * 3,
        out_specs=(VMEM,) * 5,
        scratch_shapes=[pltpu.VMEM((MESSAGE, ext, nz), jnp.float32)] * 2 + [pltpu.VMEM((5, ext, nz), jnp.float32)],
        input_output_aliases={0: 0},
        compiler_params=PARAMS,
        name="second",
    )(st, one, two)
    got = lax.all_to_all(message, "gy", 0, 0)

    out = pl.pallas_call(
        third_kernel,
        out_shape=f32((2, ny, nx, nz)),
        in_specs=[VMEM] * 5,
        out_specs=VMEM,
        scratch_shapes=[pltpu.VMEM((4, ny + 2, ext, nz), jnp.float32), pltpu.VMEM((4, ext, nz), jnp.float32)],
        compiler_params=PARAMS,
        name="third",
    )(st, extra, coarse, sides, got)
    return jnp.transpose(out, (0, 2, 1, 3))


def solution(mesh):
    return jax.shard_map(
        shards,
        mesh=mesh,
        in_specs=(
            P(None, "gx", "gy", None),
            P(None, "gx", "gy", None),
            P("gx", "gy", None),
            P("gx", "gy", None),
        ),
        out_specs=P(None, "gx", "gy", None),
        check_vma=False,
    )
```

```python
import functools

import jax
import jax.numpy as jnp
from jax import lax
from jax.experimental import pallas as pl
from jax.experimental.pallas import tpu as pltpu
from jax.sharding import PartitionSpec as P

SOLID_CAP, GAS_CAP, FLOW, CONDUCT, RELAX, LUMP = 0.5, 0.02, 40.0, 0.05, 0.8, 0.25
GAS_SELF = GAS_CAP + 4.5 * CONDUCT

PAD = 8
WX = 5
CROP = 4
(SA, GA, SB, GB, K, C, RS, RG, FX, FZ, H, FY, ASS, ASG, AGG) = range(15)
PLANES = 15
(M_S, M_G, M_K, M_C, M_FY, M_C2, M_D2, M_1S, M_1G, M_2S, M_2G, M_3S, M_3G) = range(13)
MESSAGE = 13

GROUP = 3

VMEM = pl.BlockSpec(memory_space=pltpu.VMEM)
HBM = pl.BlockSpec(memory_space=pltpu.HBM)
PARAMS = pltpu.CompilerParams(vmem_limit_bytes=40 * 1024 * 1024)


def up_x(v):
    return pltpu.roll(v, v.shape[0] - 1, 0)


def down_x(v):
    return pltpu.roll(v, 1, 0)


def up_z(v):
    return pltpu.roll(v, v.shape[1] - 1, 1)


def down_z(v):
    return pltpu.roll(v, 1, 1)


def lanes(shape):
    return lax.broadcasted_iota(jnp.int32, shape, 1)


def x_mask(shape, nx):
    row = lax.broadcasted_iota(jnp.int32, shape, 0)
    place, count = lax.axis_index("gx"), lax.axis_size("gx")
    low = jnp.where(place == 0, PAD, PAD - WX)
    high = jnp.where(place == count - 1, PAD + nx, PAD + nx + WX)
    return jnp.where((row >= low) & (row < high), 1.0, 0.0).astype(jnp.float32)


STRIP = ((SA, WX), (GA, WX), (K, WX), (RS, WX - 1), (RG, WX - 1), (C, WX - 1))
STRIP_ROWS = sum(width for plane, width in STRIP)


def pack_kernel(temps, right, exchange, coupling, one, two, pair_low, pair_high, single_low, single_high, sems):
    even = lax.axis_index("gx") % 2 == 0
    ny, nx, nz = exchange.shape
    copies = []
    for k, ref in enumerate((temps, right, exchange, coupling)):
        low, high, at = (pair_low, pair_high, k) if k < 2 else (single_low, single_high, k - 2)
        lead = (slice(None),) * (ref.ndim - 2)
        copies.append(pltpu.make_async_copy(ref.at[lead + (slice(0, 8),)], low.at[at], sems.at[2 * k]))
        copies.append(pltpu.make_async_copy(ref.at[lead + (slice(nx - 8, nx),)], high.at[at], sems.at[2 * k + 1]))
    for copy in copies:
        copy.start()
    for copy in copies:
        copy.wait()
    parts = [(pair_low, pair_high, (0, 0)), (pair_low, pair_high, (0, 1)), (single_low, single_high, (0,))]
    parts += [(pair_low, pair_high, (1, 0)), (pair_low, pair_high, (1, 1)), (single_low, single_high, (1,))]
    at = 0
    for y in range(ny):
        for (first, last, where), (plane, width) in zip(parts, STRIP):
            low = first[where + (y, slice(0, width))]
            high = last[where + (y, slice(8 - width, 8))]
            one[at : at + width] = jnp.where(even, high, low)
            two[at : at + width] = jnp.where(even, low, high)
            at += width


def load_kernel(temps, right, exchange, coupling, st, sems):
    ny, nx, nz = exchange.shape
    planes, rows, ext, nz = st.shape
    copies = []
    for k, (plane, ref) in enumerate(
        ((SA, temps.at[0]), (K, exchange), (GA, temps.at[1]), (RS, right.at[0]), (RG, right.at[1]), (C, coupling))
    ):
        to = st.at[plane, pl.ds(1, ny), pl.ds(PAD, nx)]
        copies.append(pltpu.make_async_copy(ref, to, sems.at[k]))
    for copy in copies:
        copy.start()
    zeros = jnp.zeros((PAD, nz), jnp.float32)

    def clear(i, carry):
        for plane, width in STRIP:
            st[plane, i, :PAD] = zeros
            st[plane, i, PAD + nx :] = zeros
        return carry

    lax.fori_loop(1, ny + 1, clear, 0)
    for copy in copies:
        copy.wait()

    def conduct(i, carry):
        s = st[SA, i, PAD : PAD + nx]
        st[K, i, PAD : PAD + nx] = 1.0 + 4.0 * st[K, i, PAD : PAD + nx] * s * s * s
        return carry

    lax.fori_loop(1, ny + 1, conduct, 0)


def place_halo(st, one, two, y, nx, mask):
    even = lax.axis_index("gx") % 2 == 0
    at, i = y * STRIP_ROWS, y + 1
    for plane, width in STRIP:
        a, b = one[at : at + width], two[at : at + width]
        st[plane, i, PAD - width : PAD] = jnp.where(even, b, a)
        st[plane, i, PAD + nx : PAD + nx + width] = jnp.where(even, a, b)
        at += width
    for part in (slice(0, PAD), slice(PAD + nx, 2 * PAD + nx)):
        s = st[SA, i, part]
        st[K, i, part] = (1.0 + 4.0 * st[K, i, part] * s * s * s) * mask[part]


def inner(s, g, c, h, fx, fz, edge):
    t = c * (s - g)
    flux_x = fx * (up_x(s) - s)
    flux_z = fz * (up_z(s) - s)
    part_s = (flux_x - down_x(flux_x)) + (flux_z - down_z(flux_z)) - h * s - t
    part_g = (
        t
        - GAS_SELF * g
        + CONDUCT * (up_x(g) + down_x(g))
        + edge[0] * up_z(g)
        + edge[1] * down_z(g)
    )
    return part_s, part_g


def edge_weights(shape):
    lane = lanes(shape)
    weight = jnp.float32(0.25 * CONDUCT)
    return jnp.where(lane == shape[1] - 1, 0.0, weight), jnp.where(lane == 0, 0.0, weight)


def row_inner(st, i, s_at, edge):
    return inner(st[s_at, i], st[s_at + 1, i], st[C, i], st[H, i], st[FX, i], st[FZ, i], edge)


def row_residual(st, i, s_at, edge):
    part_s, part_g = row_inner(st, i, s_at, edge)
    s, g, before = st[s_at, i], st[s_at + 1, i], st[s_at + 1, i - 1]
    part_s += st[FY, i] * (st[s_at, i + 1] - s) + st[FY, i - 1] * (st[s_at, i - 1] - s)
    part_g += CONDUCT * (st[s_at + 1, i + 1] + before) - FLOW * (g - before)
    return st[RS, i] + part_s, st[RG, i] + part_g


def relaxed(st, i, s_at, res_s, res_g):
    s = st[s_at, i] + st[ASS, i] * res_s + st[ASG, i] * res_g
    g = st[s_at + 1, i] + st[ASG, i] * res_s + st[AGG, i] * res_g
    return s, g


def faces(k):
    lane = lanes(k.shape)
    end = k.shape[1] - 1
    fx = 0.5 * (k + up_x(k))
    fz = jnp.where(lane == end, 0.0, 0.125 * (k + up_z(k)))
    h = SOLID_CAP + jnp.where((lane == 0) | (lane == end), 0.125 * k, 0.0)
    return fx, fz, h, h + (fx + down_x(fx)) + (fz + down_z(fz))


def inverse(diag, c, mask):
    gas_diag = (GAS_SELF + FLOW) + c
    inv = (RELAX * mask) / (diag * gas_diag - c * c)
    return inv * gas_diag, inv * c, inv * diag


def grouped(rows, work):
    for start in range(0, len(rows), GROUP):
        stores = []
        for i in rows[start : start + GROUP]:
            stores += work(i)
        for ref, at, value in stores:
            ref[at] = value


def row_coefficients(st, i, mask):
    fx, fz, h, diag = faces(st[K, i])
    fy = 0.5 * (st[K, i] + st[K, i + 1])
    before = 0.5 * (st[K, i] + st[K, i - 1])
    ss, sg, gg = inverse(diag + st[C, i] + fy + before, st[C, i], mask)
    values = ((FX, fx), (FZ, fz), (H, h), (FY, fy), (ASS, ss), (ASG, sg), (AGG, gg))
    return [(st, (plane, i), v) for plane, v in values]


def row_sweep(st, i, source, target, edge):
    s, g = relaxed(st, i, source, *row_residual(st, i, source, edge))
    return [(st, (target, i), s), (st, (target + 1, i), g)]


def first_kernel(st_in, one, two, st, out_one, out_two):
    del st_in
    planes, rows, ext, nz = st.shape
    ny, nx = rows - 2, ext - 2 * PAD
    shape = (ext, nz)
    mask = x_mask(shape, nx)
    edge = edge_weights(shape)

    for y in list(range(4)) + list(range(ny - 4, ny)):
        place_halo(st, one, two, y, nx, mask)
    for i in (1, ny):
        fx, fz, h, diag = faces(st[K, i])
        st[FX, i], st[FZ, i], st[H, i] = fx, fz, h
    st[FY, 1] = 0.5 * (st[K, 1] + st[K, 2])
    st[FY, ny - 3] = 0.5 * (st[K, ny - 3] + st[K, ny - 2])
    ends = [2, 3, ny - 2, ny - 1]
    grouped(ends, lambda i: row_coefficients(st, i, mask))
    grouped(ends, lambda i: row_sweep(st, i, SA, SB, edge))

    def diag_of(i):
        fx, fz = st[FX, i], st[FZ, i]
        return st[H, i] + (fx + down_x(fx)) + (fz + down_z(fz)) + st[C, i] + st[FY, i] + st[FY, i - 1]

    e, d = ny, ny - 1
    s, g, fy = st[SA, e], st[GA, e], st[FY, d]
    part_s, part_g = row_inner(st, e, SA, edge)
    m1s = st[RS, e] + part_s + fy * (st[SA, d] - s)
    m1g = st[RG, e] + part_g + CONDUCT * st[GA, d] - FLOW * (g - st[GA, d])
    s1, g1 = st[SB, d], st[GB, d]
    m2s = st[RS, e] + fy * s1
    m2g = st[RG, e] + (CONDUCT + FLOW) * g1
    part_s, part_g = row_inner(st, d, SB, edge)
    m3s = st[RS, d] + part_s - fy * s1 + st[FY, d - 1] * (st[SB, d - 1] - s1)
    m3g = st[RG, d] + part_g + CONDUCT * st[GB, d - 1] - FLOW * (g1 - st[GB, d - 1])
    onward = [s, g, st[K, e], st[C, e], fy, st[C, d], diag_of(d), m1s, m1g, m2s, m2g, m3s, m3g]

    e, d = 1, 2
    s, g, fy = st[SA, e], st[GA, e], st[FY, e]
    part_s, part_g = row_inner(st, e, SA, edge)
    m1s = st[RS, e] + part_s + fy * (st[SA, d] - s)
    m1g = st[RG, e] + part_g + CONDUCT * st[GA, d] - FLOW * g
    s1, g1 = st[SB, d], st[GB, d]
    m2s = st[RS, e] + fy * s1
    m2g = st[RG, e] + CONDUCT * g1
    part_s, part_g = row_inner(st, d, SB, edge)
    m3s = st[RS, d] + part_s - fy * s1 + st[FY, d] * (st[SB, d + 1] - s1)
    m3g = st[RG, d] + part_g + CONDUCT * st[GB, d + 1] - FLOW * g1
    back = [s, g, st[K, e], st[C, e], fy, st[C, d], diag_of(d), m1s, m1g, m2s, m2g, m3s, m3g]

    even_y = lax.axis_index("gy") % 2 == 0
    for plane, (a, b) in enumerate(zip(onward, back)):
        a, b = a[CROP : ext - CROP], b[CROP : ext - CROP]
        out_one[plane] = jnp.where(even_y, a, b)
        out_two[plane] = jnp.where(even_y, b, a)


def outer_residual(st, i, s_at, rs, rg, fy_out, edge, after):
    part_s, part_g = row_inner(st, i, s_at, edge)
    s, g = st[s_at, i], st[s_at + 1, i]
    if after:
        part_s += st[FY, i - 1] * (st[s_at, i - 1] - s)
        part_g += (CONDUCT + FLOW) * st[s_at + 1, i - 1]
    else:
        part_s += st[FY, i] * (st[s_at, i + 1] - s)
        part_g += CONDUCT * st[s_at + 1, i + 1]
    return rs + part_s - fy_out * s, rg + part_g - FLOW * g


def pair_x(v):
    row = lax.broadcasted_iota(jnp.int32, v.shape, 0)
    return v + jnp.where(row % 2 == 0, up_x(v), down_x(v))


def coarse_coefficients(c_sum, k_sum):
    solid = 4.0 * SOLID_CAP + c_sum + LUMP * k_sum
    ratio = c_sum / solid
    denominator = (4.0 * GAS_CAP + 2.0 * FLOW) + c_sum - c_sum * ratio
    return solid, ratio, denominator


def coarse_row(st, coarse, j, mask, edge):
    i = 2 * j + 1
    res_s, res_g = row_residual(st, i, SA, edge)
    more_s, more_g = row_residual(st, i + 1, SA, edge)
    res_s, res_g = pair_x((res_s + more_s) * mask), pair_x((res_g + more_g) * mask)
    c_sum = pair_x(st[C, i] + st[C, i + 1])
    solid, ratio, denominator = coarse_coefficients(c_sum, pair_x(st[K, i] + st[K, i + 1]))
    lead = res_s / solid
    values = (lead, ratio, (2.0 * FLOW) / denominator, (res_g + c_sum * lead) / denominator)
    return [(coarse, (k, j), v) for k, v in enumerate(values)]


def inner_kernel(st_in, one, two, st, coarse):
    del st_in
    planes, rows, ext, nz = st.shape
    ny, nx = rows - 2, ext - 2 * PAD
    shape = (ext, nz)
    mask = x_mask(shape, nx)
    edge = edge_weights(shape)
    for y in range(4, ny - 4):
        place_halo(st, one, two, y, nx, mask)
    grouped(list(range(4, ny - 2)), lambda i: row_coefficients(st, i, mask))
    grouped(list(range(4, ny - 2)), lambda i: row_sweep(st, i, SA, SB, edge))
    grouped(list(range(3, ny - 1)), lambda i: row_sweep(st, i, SB, SA, edge))
    for j in range(2, ny // 2 - 2):
        for ref, at, value in coarse_row(st, coarse, j, mask, edge):
            ref[at] = value


def second_kernel(st_in, coarse_in, one, two, st, coarse, extra, sides, message, before, after, squeeze):
    del st_in, coarse_in
    planes, rows, ext, nz = st.shape
    ny, nx = rows - 2, ext - 2 * PAD
    shape = (ext, nz)
    me, count = lax.axis_index("gy"), lax.axis_size("gy")
    even = me % 2 == 0
    mask = x_mask(shape, nx)
    low = jnp.where(me == 0, 0.0, mask)
    high = jnp.where(me == count - 1, 0.0, mask)
    edge = edge_weights(shape)
    zeros = jnp.zeros((PAD, nz), jnp.float32)

    for plane in range(MESSAGE):
        a, b = one[plane], two[plane]
        for ref, v in ((before, jnp.where(even, b, a)), (after, jnp.where(even, a, b))):
            ref[plane, :PAD] = zeros
            ref[plane, ext - PAD :] = zeros
            ref[plane, CROP : ext - CROP] = v

    last = ny + 1
    ends = ((0, before, low), (last, after, high))
    for i, ref, inside in ends:
        st[SA, i], st[GA, i], st[K, i], st[C, i] = ref[M_S], ref[M_G], ref[M_K], ref[M_C]
    st[FY, 0] = 0.5 * (st[K, 0] + st[K, 1])
    st[FY, ny] = 0.5 * (st[K, ny] + st[K, last])
    for i in (1, ny):
        fx, fz = st[FX, i], st[FZ, i]
        diag = st[H, i] + (fx + down_x(fx)) + (fz + down_z(fz)) + st[C, i] + st[FY, i - 1] + st[FY, i]
        st[ASS, i], st[ASG, i], st[AGG, i] = inverse(diag, st[C, i], mask)
    for i, ref, inside in ends:
        fx, fz, h, diag = faces(st[K, i])
        st[FX, i], st[FZ, i], st[H, i] = fx, fz, h
        diag += st[C, i] + ref[M_FY] + st[FY, min(i, ny)]
        st[ASS, i], st[ASG, i], st[AGG, i] = inverse(diag, st[C, i], inside)

    res = before[M_1S] + st[FY, 0] * (st[SA, 1] - st[SA, 0]), before[M_1G] + CONDUCT * st[GA, 1]
    new_low = relaxed(st, 0, SA, *res)
    res = after[M_1S] + st[FY, ny] * (st[SA, ny] - st[SA, last]), after[M_1G] + (CONDUCT + FLOW) * st[GA, ny]
    new_high = relaxed(st, last, SA, *res)
    stores = row_sweep(st, 1, SA, SB, edge) + row_sweep(st, ny, SA, SB, edge)
    st[SB, 0], st[GB, 0] = new_low
    st[SB, last], st[GB, last] = new_high
    for ref, at, value in stores:
        ref[at] = value

    for i, ref, inside in ends:
        is_after = i > 0
        res = outer_residual(st, i, SB, ref[M_2S], ref[M_2G], ref[M_FY], edge, is_after)
        st[SA, i], st[GA, i] = relaxed(st, i, SB, *res)
        ss, sg, gg = inverse(jnp.maximum(ref[M_D2], SOLID_CAP), ref[M_C2], inside)
        to, back = (CONDUCT + FLOW, CONDUCT) if is_after else (CONDUCT, CONDUCT + FLOW)
        res_s = ref[M_3S] + ref[M_FY] * st[SB, i]
        res_g = ref[M_3G] + to * st[GB, i]
        side = 3 if is_after else 0
        extra[side] = ref[M_2S] + ref[M_FY] * (ss * res_s + sg * res_g)
        extra[side + 1] = ref[M_2G] + back * (sg * res_s + gg * res_g)
        extra[side + 2] = ref[M_FY]
    grouped([1, 2, ny - 1, ny], lambda i: row_sweep(st, i, SB, SA, edge))

    blocks = ny // 2
    for j in (0, 1, blocks - 2, blocks - 1):
        for ref, at, value in coarse_row(st, coarse, j, mask, edge):
            ref[at] = value
    first_offset = coarse[3, 0]
    slopes, offsets = coarse[2, 0], first_offset
    for j in range(1, blocks):
        slope = coarse[2, j]
        slopes, offsets = slope * slopes, slope * offsets + coarse[3, j]
        coarse[2, j], coarse[3, j] = slopes, offsets

    for side, (i, ref, inside) in enumerate(ends):
        k2 = 2.0 * ref[M_FY] - ref[M_K]
        solid, ratio, denominator = coarse_coefficients(pair_x(ref[M_C] + ref[M_C2]), pair_x(ref[M_K] + k2))
        sides[side] = ratio
        if side:
            sides[2] = (2.0 * FLOW) / denominator

    squeeze[0], squeeze[1], squeeze[2] = slopes, offsets, coarse[0, blocks - 1]
    squeeze[3], squeeze[4] = coarse[0, 0], first_offset
    span = nx // 2 + 2
    pick = pl.ds(PAD - 2, span, 2)
    thin = [squeeze[k, pick, :] for k in range(5)]
    blank = jnp.zeros_like(thin[0])

    def fill(d, carry):
        onward = d > me
        for k, (a, b) in enumerate(zip(thin[:3], thin[3:] + [blank])):
            message[d, k * span : (k + 1) * span] = jnp.where(onward, a, b)
        return carry

    lax.fori_loop(0, count, fill, 0)


def third_kernel(st, extra, coarse, sides, got, out, sc, wide, done, sems):
    planes, rows, ext, nz = st.shape
    ny, nx = rows - 2, ext - 2 * PAD
    shape = (ext, nz)
    me, count = lax.axis_index("gy"), lax.axis_size("gy")
    edge = edge_weights(shape)
    span = nx // 2 + 2
    blocks = ny // 2

    def fold(d, gas):
        return got[d, :span] * gas + got[d, span : 2 * span]

    gas_in = lax.fori_loop(0, me, fold, jnp.zeros((span, nz), jnp.float32))
    inside_low, inside_high = me > 0, me < count - 1
    prev, following = jnp.maximum(me - 1, 0), jnp.minimum(me + 1, count - 1)
    lead_low = jnp.where(inside_low, got[prev, 2 * span : 3 * span], 0.0)
    lead_high = jnp.where(inside_high, got[following, :span], 0.0)
    offset_high = jnp.where(inside_high, got[following, span : 2 * span], 0.0)
    for k, v in enumerate((gas_in, lead_low, lead_high, offset_high)):
        wide[k, : PAD - 2] = jnp.zeros((PAD - 2, nz), jnp.float32)
        wide[k, ext - PAD + 2 :] = jnp.zeros((PAD - 2, nz), jnp.float32)
        wide[k, pl.ds(PAD - 2, span, 2), :] = v
        wide[k, pl.ds(PAD - 1, span, 2), :] = v

    gas_in = wide[0]
    last = ny + 1
    solid_low = wide[1] + sides[0] * gas_in
    sc[0, 0] = st[SA, 0] + solid_low
    sc[1, 0] = st[GA, 0] + gas_in

    def correct(j, carry):
        gas = coarse[2, j] * gas_in + coarse[3, j]
        solid = coarse[0, j] + coarse[1, j] * gas
        for i in (2 * j + 1, 2 * j + 2):
            sc[0, i] = st[SA, i] + solid
            sc[1, i] = st[GA, i] + gas
        return carry

    lax.fori_loop(0, blocks, correct, 0)
    gas = coarse[2, blocks - 1] * gas_in + coarse[3, blocks - 1]
    gas_high = jnp.where(inside_high, sides[2] * gas + wide[3], 0.0)
    solid_high = wide[2] + sides[1] * gas_high
    sc[0, last] = st[SA, last] + solid_high
    sc[1, last] = st[GA, last] + gas_high

    view = Fields(st, sc)
    for i, is_after, solid, gas in ((0, False, solid_low, gas_in), (last, True, solid_high, gas_high)):
        side = 3 if is_after else 0
        fy = extra[side + 2]
        rs = extra[side] + fy * solid
        rg = extra[side + 1] + (CONDUCT if is_after else CONDUCT + FLOW) * gas
        res = outer_residual(view, i, SA, rs, rg, fy, edge, is_after)
        sc[2, i], sc[3, i] = relaxed(view, i, SA, *res)

    def sweep(k, carry):
        stores = []
        for r in range(GROUP):
            i = GROUP * k + 1 + r
            new_s, new_g = relaxed(view, i, SA, *row_residual(view, i, SA, edge))
            stores += [((2, i), new_s), ((3, i), new_g)]
        for at, value in stores:
            sc[at] = value
        return carry

    lax.fori_loop(0, ny // GROUP, sweep, 0)

    def leaving(k):
        part = pl.ds(GROUP * k, GROUP)
        return pltpu.make_async_copy(done.at[:, part], out.at[:, part], sems.at[k])

    def final(k, carry):
        stores = []
        for r in range(GROUP):
            i = GROUP * k + 1 + r
            new_s, new_g = relaxed(view, i, SB, *row_residual(view, i, SB, edge))
            stores += [((0, i - 1), new_s), ((1, i - 1), new_g)]
        for at, value in stores:
            done[at] = value[PAD : PAD + nx]
        leaving(k).start()
        return carry

    lax.fori_loop(0, ny // GROUP, final, 0)
    for k in range(ny // GROUP):
        leaving(k).wait()


class Fields:
    def __init__(self, st, sc):
        self.st, self.sc = st, sc

    def __getitem__(self, at):
        return (self.sc if at[0] <= GB else self.st)[at]


def swap(one, two, axis, second_first=False):
    def pairs(first):
        out = []
        for i in range(first, lax.axis_size(axis) - 1, 2):
            out += [(i, i + 1), (i + 1, i)]
        return out

    if second_first:
        two = lax.ppermute(two, axis, pairs(1))
        return lax.ppermute(one, axis, pairs(0)), two
    return lax.ppermute(one, axis, pairs(0)), lax.ppermute(two, axis, pairs(1))


def shards(temps, right_side, exchange, coupling):
    temps, right_side = (jnp.transpose(a, (0, 2, 1, 3)) for a in (temps, right_side))
    exchange, coupling = (jnp.transpose(a, (1, 0, 2)) for a in (exchange, coupling))
    temps, right_side, exchange, coupling = (
        pltpu.with_memory_space_constraint(a, pltpu.HBM) for a in (temps, right_side, exchange, coupling)
    )
    ny, nx, nz = exchange.shape
    ext = nx + 2 * PAD
    f32 = functools.partial(jax.ShapeDtypeStruct, dtype=jnp.float32)

    strip = f32(((ny * STRIP_ROWS + 7) // 8 * 8, nz))
    edges = [pltpu.VMEM((2, 2, ny, 8, nz), jnp.float32)] * 2 + [pltpu.VMEM((2, ny, 8, nz), jnp.float32)] * 2
    one, two = pl.pallas_call(
        pack_kernel,
        out_shape=(strip, strip),
        in_specs=[HBM] * 4,
        out_specs=(VMEM, VMEM),
        scratch_shapes=edges + [pltpu.SemaphoreType.DMA((8,))],
        compiler_params=PARAMS,
        name="pack_x",
    )(temps, right_side, exchange, coupling)
    one, two = swap(one, two, "gx")

    state = f32((PLANES, ny + 2, ext, nz))
    letter = f32((MESSAGE, ext - 2 * CROP, nz))
    st = pl.pallas_call(
        load_kernel,
        out_shape=state,
        in_specs=[HBM] * 4,
        out_specs=VMEM,
        scratch_shapes=[pltpu.SemaphoreType.DMA((6,))],
        compiler_params=PARAMS,
        name="load",
    )(temps, right_side, exchange, coupling)
    st, out_one, out_two = pl.pallas_call(
        first_kernel,
        out_shape=(state, letter, letter),
        in_specs=[VMEM] * 3,
        out_specs=(VMEM,) * 3,
        input_output_aliases={0: 0},
        compiler_params=PARAMS,
        name="first",
    )(st, one, two)
    y_one, y_two = swap(out_one, out_two, "gy", True)

    rows = f32((4, ny // 2, ext, nz))
    st, coarse = pl.pallas_call(
        inner_kernel,
        out_shape=(state, rows),
        in_specs=[VMEM] * 3,
        out_specs=(VMEM,) * 2,
        input_output_aliases={0: 0},
        compiler_params=PARAMS,
        name="inner",
    )(st, one, two)

    count = lax.axis_size("gy")
    span = nx // 2 + 2
    height = (3 * span + 7) // 8 * 8
    st, coarse, extra, sides, message = pl.pallas_call(
        second_kernel,
        out_shape=(state, rows, f32((6, ext, nz)), f32((3, ext, nz)), f32((count, height, nz))),
        in_specs=[VMEM] * 4,
        out_specs=(VMEM,) * 5,
        scratch_shapes=[pltpu.VMEM((MESSAGE, ext, nz), jnp.float32)] * 2 + [pltpu.VMEM((5, ext, nz), jnp.float32)],
        input_output_aliases={0: 0, 1: 1},
        compiler_params=PARAMS,
        name="second",
    )(st, coarse, y_one, y_two)
    got = lax.all_to_all(message, "gy", 0, 0)

    out = pl.pallas_call(
        third_kernel,
        out_shape=f32((2, ny, nx, nz)),
        in_specs=[VMEM] * 5,
        out_specs=HBM,
        scratch_shapes=[
            pltpu.VMEM((4, ny + 2, ext, nz), jnp.float32),
            pltpu.VMEM((4, ext, nz), jnp.float32),
            pltpu.VMEM((2, ny, nx, nz), jnp.float32),
            pltpu.SemaphoreType.DMA((ny // GROUP,)),
        ],
        compiler_params=PARAMS,
        name="third",
    )(st, extra, coarse, sides, got)
    return jnp.transpose(out, (0, 2, 1, 3))


def solution(mesh):
    return jax.shard_map(
        shards,
        mesh=mesh,
        in_specs=(
            P(None, "gx", "gy", None),
            P(None, "gx", "gy", None),
            P("gx", "gy", None),
            P("gx", "gy", None),
        ),
        out_specs=P(None, "gx", "gy", None),
        check_vma=False,
    )
```

```python
import functools

import jax
import jax.numpy as jnp
from jax import lax
from jax.experimental import pallas as pl
from jax.experimental.pallas import tpu as pltpu
from jax.sharding import PartitionSpec as P

SOLID_CAP, GAS_CAP, FLOW, CONDUCT, RELAX, LUMP = 0.5, 0.02, 40.0, 0.05, 0.8, 0.25
GAS_SELF = GAS_CAP + 4.5 * CONDUCT

PAD = 8
WX = 5
CROP = 4
(SA, GA, SB, GB, K, C, RS, RG, FX, FZ, H, FY, ASS, ASG, AGG) = range(15)
PLANES = 15
(M_S, M_G, M_K, M_C, M_FY, M_1S, M_1G, M_2S, M_2G, M_C2, M_D2, M_3S, M_3G) = range(13)
MESSAGE, SOON = 13, 9
(R_SLOPE, R_OFFSET, R_LAST, R_FIRST, R_FIRST_OFFSET) = range(5)

GROUP = 3

VMEM = pl.BlockSpec(memory_space=pltpu.VMEM)
HBM = pl.BlockSpec(memory_space=pltpu.HBM)
PARAMS = pltpu.CompilerParams(vmem_limit_bytes=40 * 1024 * 1024)


def up_x(v):
    return pltpu.roll(v, v.shape[0] - 1, 0)


def down_x(v):
    return pltpu.roll(v, 1, 0)


def up_z(v):
    return pltpu.roll(v, v.shape[1] - 1, 1)


def down_z(v):
    return pltpu.roll(v, 1, 1)


def lanes(shape):
    return lax.broadcasted_iota(jnp.int32, shape, 1)


def x_mask(shape, nx):
    row = lax.broadcasted_iota(jnp.int32, shape, 0)
    place, count = lax.axis_index("gx"), lax.axis_size("gx")
    low = jnp.where(place == 0, PAD, PAD - WX)
    high = jnp.where(place == count - 1, PAD + nx, PAD + nx + WX)
    return jnp.where((row >= low) & (row < high), 1.0, 0.0).astype(jnp.float32)


STRIP = ((SA, WX), (GA, WX), (K, WX), (RS, WX - 1), (RG, WX - 1), (C, WX - 1))
STRIP_ROWS = sum(width for plane, width in STRIP)


def pack_kernel(temps, right, exchange, coupling, one, two, pair_low, pair_high, single_low, single_high, sems):
    even = lax.axis_index("gx") % 2 == 0
    ny, nx, nz = exchange.shape
    copies = []
    for k, ref in enumerate((temps, right, exchange, coupling)):
        low, high, at = (pair_low, pair_high, k) if k < 2 else (single_low, single_high, k - 2)
        lead = (slice(None),) * (ref.ndim - 2)
        copies.append(pltpu.make_async_copy(ref.at[lead + (slice(0, 8),)], low.at[at], sems.at[2 * k]))
        copies.append(pltpu.make_async_copy(ref.at[lead + (slice(nx - 8, nx),)], high.at[at], sems.at[2 * k + 1]))
    for copy in copies:
        copy.start()
    for copy in copies:
        copy.wait()
    parts = [(pair_low, pair_high, (0, 0)), (pair_low, pair_high, (0, 1)), (single_low, single_high, (0,))]
    parts += [(pair_low, pair_high, (1, 0)), (pair_low, pair_high, (1, 1)), (single_low, single_high, (1,))]
    at = 0
    for y in range(ny):
        for (first, last, where), (plane, width) in zip(parts, STRIP):
            low = first[where + (y, slice(0, width))]
            high = last[where + (y, slice(8 - width, 8))]
            one[at : at + width] = jnp.where(even, high, low)
            two[at : at + width] = jnp.where(even, low, high)
            at += width


def load_kernel(temps, right, exchange, coupling, st, sems):
    ny, nx, nz = exchange.shape
    planes, rows, ext, nz = st.shape
    copies = []
    for k, (plane, ref) in enumerate(
        ((SA, temps.at[0]), (K, exchange), (GA, temps.at[1]), (RS, right.at[0]), (RG, right.at[1]), (C, coupling))
    ):
        to = st.at[plane, pl.ds(1, ny), pl.ds(PAD, nx)]
        copies.append(pltpu.make_async_copy(ref, to, sems.at[k]))
    for copy in copies:
        copy.start()
    zeros = jnp.zeros((PAD, nz), jnp.float32)

    def clear(i, carry):
        for plane, width in STRIP:
            st[plane, i, :PAD] = zeros
            st[plane, i, PAD + nx :] = zeros
        return carry

    lax.fori_loop(1, ny + 1, clear, 0)
    for copy in copies:
        copy.wait()

    def conduct(i, carry):
        s = st[SA, i, PAD : PAD + nx]
        st[K, i, PAD : PAD + nx] = 1.0 + 4.0 * st[K, i, PAD : PAD + nx] * s * s * s
        return carry

    lax.fori_loop(1, ny + 1, conduct, 0)


def place_halo(st, one, two, y, nx, mask):
    even = lax.axis_index("gx") % 2 == 0
    at, i = y * STRIP_ROWS, y + 1
    for plane, width in STRIP:
        a, b = one[at : at + width], two[at : at + width]
        st[plane, i, PAD - width : PAD] = jnp.where(even, b, a)
        st[plane, i, PAD + nx : PAD + nx + width] = jnp.where(even, a, b)
        at += width
    for part in (slice(0, PAD), slice(PAD + nx, 2 * PAD + nx)):
        s = st[SA, i, part]
        st[K, i, part] = (1.0 + 4.0 * st[K, i, part] * s * s * s) * mask[part]


def inner(s, g, c, h, fx, fz, edge):
    t = c * (s - g)
    flux_x = fx * (up_x(s) - s)
    flux_z = fz * (up_z(s) - s)
    part_s = (flux_x - down_x(flux_x)) + (flux_z - down_z(flux_z)) - h * s - t
    part_g = (
        t
        - GAS_SELF * g
        + CONDUCT * (up_x(g) + down_x(g))
        + edge[0] * up_z(g)
        + edge[1] * down_z(g)
    )
    return part_s, part_g


def edge_weights(shape):
    lane = lanes(shape)
    weight = jnp.float32(0.25 * CONDUCT)
    return jnp.where(lane == shape[1] - 1, 0.0, weight), jnp.where(lane == 0, 0.0, weight)


def row_inner(st, i, s_at, edge):
    return inner(st[s_at, i], st[s_at + 1, i], st[C, i], st[H, i], st[FX, i], st[FZ, i], edge)


def row_residual(st, i, s_at, edge):
    part_s, part_g = row_inner(st, i, s_at, edge)
    s, g, before = st[s_at, i], st[s_at + 1, i], st[s_at + 1, i - 1]
    part_s += st[FY, i] * (st[s_at, i + 1] - s) + st[FY, i - 1] * (st[s_at, i - 1] - s)
    part_g += CONDUCT * (st[s_at + 1, i + 1] + before) - FLOW * (g - before)
    return st[RS, i] + part_s, st[RG, i] + part_g


def relaxed(st, i, s_at, res_s, res_g):
    s = st[s_at, i] + st[ASS, i] * res_s + st[ASG, i] * res_g
    g = st[s_at + 1, i] + st[ASG, i] * res_s + st[AGG, i] * res_g
    return s, g


def faces(k):
    lane = lanes(k.shape)
    end = k.shape[1] - 1
    fx = 0.5 * (k + up_x(k))
    fz = jnp.where(lane == end, 0.0, 0.125 * (k + up_z(k)))
    h = SOLID_CAP + jnp.where((lane == 0) | (lane == end), 0.125 * k, 0.0)
    return fx, fz, h, h + (fx + down_x(fx)) + (fz + down_z(fz))


def inverse(diag, c, mask):
    gas_diag = (GAS_SELF + FLOW) + c
    inv = (RELAX * mask) / (diag * gas_diag - c * c)
    return inv * gas_diag, inv * c, inv * diag


def grouped(rows, work):
    for start in range(0, len(rows), GROUP):
        stores = []
        for i in rows[start : start + GROUP]:
            stores += work(i)
        for ref, at, value in stores:
            ref[at] = value


def row_coefficients(st, i, mask):
    fx, fz, h, diag = faces(st[K, i])
    fy = 0.5 * (st[K, i] + st[K, i + 1])
    before = 0.5 * (st[K, i] + st[K, i - 1])
    ss, sg, gg = inverse(diag + st[C, i] + fy + before, st[C, i], mask)
    values = ((FX, fx), (FZ, fz), (H, h), (FY, fy), (ASS, ss), (ASG, sg), (AGG, gg))
    return [(st, (plane, i), v) for plane, v in values]


def row_sweep(st, i, source, target, edge):
    s, g = relaxed(st, i, source, *row_residual(st, i, source, edge))
    return [(st, (target, i), s), (st, (target + 1, i), g)]


def send_planes(st, onward, planes, edge):
    ny, ext = st.shape[1] - 2, st.shape[2]
    e, d, f, way = (ny, ny - 1, ny - 2, -1) if onward else (1, 2, 3, 1)
    near, far = (d, f) if onward else (e, d)
    from_d = CONDUCT + FLOW if onward else CONDUCT
    fy = st[FY, near]
    out = {M_FY: fy}
    if M_S in planes:
        s, g = st[SA, e], st[GA, e]
        part_s, part_g = row_inner(st, e, SA, edge)
        out.update({M_S: s, M_G: g, M_K: st[K, e], M_C: st[C, e]})
        out[M_1S] = st[RS, e] + part_s + fy * (st[SA, d] - s)
        if onward:
            out[M_1G] = st[RG, e] + part_g + CONDUCT * st[GA, d] - FLOW * (g - st[GA, d])
        else:
            out[M_1G] = st[RG, e] + part_g + CONDUCT * st[GA, d] - FLOW * g
        out[M_2S] = st[RS, e] + fy * st[SB, d]
        out[M_2G] = st[RG, e] + from_d * st[GB, d]
    if M_C2 in planes:
        s, g = st[SB, d], st[GB, d]
        part_s, part_g = row_inner(st, d, SB, edge)
        out[M_3S] = st[RS, d] + part_s - fy * s + st[FY, far] * (st[SB, f] - s)
        if onward:
            out[M_3G] = st[RG, d] + part_g + CONDUCT * st[GB, f] - FLOW * (g - st[GB, f])
        else:
            out[M_3G] = st[RG, d] + part_g + CONDUCT * st[GB, f] - FLOW * g
        fx, fz = st[FX, d], st[FZ, d]
        diag = st[H, d] + (fx + down_x(fx)) + (fz + down_z(fz)) + st[C, d] + fy + st[FY, far]
        out.update({M_C2: st[C, d], M_D2: diag})
    return [out[plane][CROP : ext - CROP] for plane in planes]


def write_message(ref, st, onward, planes, edge):
    for go in (True, False):

        @pl.when(onward == go)
        def _():
            for k, value in enumerate(send_planes(st, go, planes, edge)):
                ref[k] = value


def first_kernel(st_in, one, two, st, across):
    del st_in
    planes, rows, ext, nz = st.shape
    ny, nx = rows - 2, ext - 2 * PAD
    shape = (ext, nz)
    mask = x_mask(shape, nx)
    edge = edge_weights(shape)

    for y in list(range(4)) + list(range(ny - 4, ny)):
        place_halo(st, one, two, y, nx, mask)
    for i in (1, ny):
        fx, fz, h, diag = faces(st[K, i])
        st[FX, i], st[FZ, i], st[H, i] = fx, fz, h
    st[FY, 1] = 0.5 * (st[K, 1] + st[K, 2])
    st[FY, ny - 3] = 0.5 * (st[K, ny - 3] + st[K, ny - 2])
    ends = [2, 3, ny - 2, ny - 1]
    grouped(ends, lambda i: row_coefficients(st, i, mask))
    grouped(ends, lambda i: row_sweep(st, i, SA, SB, edge))
    write_message(across, st, lax.axis_index("gy") % 2 == 1, range(SOON), edge)


def outer_residual(st, i, s_at, rs, rg, fy_out, edge, after):
    part_s, part_g = row_inner(st, i, s_at, edge)
    s, g = st[s_at, i], st[s_at + 1, i]
    if after:
        part_s += st[FY, i - 1] * (st[s_at, i - 1] - s)
        part_g += (CONDUCT + FLOW) * st[s_at + 1, i - 1]
    else:
        part_s += st[FY, i] * (st[s_at, i + 1] - s)
        part_g += CONDUCT * st[s_at + 1, i + 1]
    return rs + part_s - fy_out * s, rg + part_g - FLOW * g


def pair_x(v):
    row = lax.broadcasted_iota(jnp.int32, v.shape, 0)
    return v + jnp.where(row % 2 == 0, up_x(v), down_x(v))


def coarse_coefficients(c_sum, k_sum):
    solid = 4.0 * SOLID_CAP + c_sum + LUMP * k_sum
    ratio = c_sum / solid
    denominator = (4.0 * GAS_CAP + 2.0 * FLOW) + c_sum - c_sum * ratio
    return solid, ratio, denominator


def coarse_row(st, coarse, j, mask, edge):
    i = 2 * j + 1
    res_s, res_g = row_residual(st, i, SA, edge)
    more_s, more_g = row_residual(st, i + 1, SA, edge)
    res_s, res_g = pair_x((res_s + more_s) * mask), pair_x((res_g + more_g) * mask)
    c_sum = pair_x(st[C, i] + st[C, i + 1])
    solid, ratio, denominator = coarse_coefficients(c_sum, pair_x(st[K, i] + st[K, i + 1]))
    lead = res_s / solid
    values = (lead, ratio, (2.0 * FLOW) / denominator, (res_g + c_sum * lead) / denominator)
    return [(coarse, (k, j), v) for k, v in enumerate(values)]


def inner_kernel(st_in, one, two, st, coarse, across, beside_late, beside):
    del st_in
    planes, rows, ext, nz = st.shape
    ny, nx = rows - 2, ext - 2 * PAD
    shape = (ext, nz)
    mask = x_mask(shape, nx)
    edge = edge_weights(shape)
    for y in range(4, ny - 4):
        place_halo(st, one, two, y, nx, mask)
    grouped(list(range(4, ny - 2)), lambda i: row_coefficients(st, i, mask))
    grouped(list(range(4, ny - 2)), lambda i: row_sweep(st, i, SA, SB, edge))
    grouped(list(range(3, ny - 1)), lambda i: row_sweep(st, i, SB, SA, edge))
    for j in range(2, ny // 2 - 2):
        for ref, at, value in coarse_row(st, coarse, j, mask, edge):
            ref[at] = value
    odd = lax.axis_index("gy") % 2 == 1
    write_message(across, st, odd, range(SOON, MESSAGE), edge)
    write_message(beside_late, st, ~odd, range(SOON, MESSAGE), edge)
    write_message(beside, st, ~odd, range(SOON), edge)


def unpack(across, beside, planes, before, after, first=0):
    even = lax.axis_index("gy") % 2 == 0
    ext, nz = before.shape[1:]
    zeros = jnp.zeros((PAD, nz), jnp.float32)
    for plane in planes:
        a, b = beside[plane - first], across[plane - first]
        for ref, v in ((before, jnp.where(even, b, a)), (after, jnp.where(even, a, b))):
            ref[plane, :PAD] = zeros
            ref[plane, ext - PAD :] = zeros
            ref[plane, CROP : ext - CROP] = v


def second_kernel(st_in, coarse_in, across, beside, st, coarse, message, before, after, squeeze):
    del st_in, coarse_in
    planes, rows, ext, nz = st.shape
    ny, nx = rows - 2, ext - 2 * PAD
    shape = (ext, nz)
    me, count = lax.axis_index("gy"), lax.axis_size("gy")
    mask = x_mask(shape, nx)
    low = jnp.where(me == 0, 0.0, mask)
    high = jnp.where(me == count - 1, 0.0, mask)
    edge = edge_weights(shape)
    unpack(across, beside, range(SOON), before, after)

    last = ny + 1
    ends = ((0, before, low), (last, after, high))
    for i, ref, inside in ends:
        st[SA, i], st[GA, i], st[K, i], st[C, i] = ref[M_S], ref[M_G], ref[M_K], ref[M_C]
    st[FY, 0] = 0.5 * (st[K, 0] + st[K, 1])
    st[FY, ny] = 0.5 * (st[K, ny] + st[K, last])
    for i in (1, ny):
        fx, fz = st[FX, i], st[FZ, i]
        diag = st[H, i] + (fx + down_x(fx)) + (fz + down_z(fz)) + st[C, i] + st[FY, i - 1] + st[FY, i]
        st[ASS, i], st[ASG, i], st[AGG, i] = inverse(diag, st[C, i], mask)
    for i, ref, inside in ends:
        fx, fz, h, diag = faces(st[K, i])
        st[FX, i], st[FZ, i], st[H, i] = fx, fz, h
        diag += st[C, i] + ref[M_FY] + st[FY, min(i, ny)]
        st[ASS, i], st[ASG, i], st[AGG, i] = inverse(diag, st[C, i], inside)

    res = before[M_1S] + st[FY, 0] * (st[SA, 1] - st[SA, 0]), before[M_1G] + CONDUCT * st[GA, 1]
    new_low = relaxed(st, 0, SA, *res)
    res = after[M_1S] + st[FY, ny] * (st[SA, ny] - st[SA, last]), after[M_1G] + (CONDUCT + FLOW) * st[GA, ny]
    new_high = relaxed(st, last, SA, *res)
    stores = row_sweep(st, 1, SA, SB, edge) + row_sweep(st, ny, SA, SB, edge)
    st[SB, 0], st[GB, 0] = new_low
    st[SB, last], st[GB, last] = new_high
    for ref, at, value in stores:
        ref[at] = value

    for i, ref, inside in ends:
        is_after = i > 0
        res = outer_residual(st, i, SB, ref[M_2S], ref[M_2G], ref[M_FY], edge, is_after)
        st[SA, i], st[GA, i] = relaxed(st, i, SB, *res)
    grouped([1, 2, ny - 1, ny], lambda i: row_sweep(st, i, SB, SA, edge))

    blocks = ny // 2
    for j in (0, 1, blocks - 2, blocks - 1):
        for ref, at, value in coarse_row(st, coarse, j, mask, edge):
            ref[at] = value
    first_offset = coarse[3, 0]
    slopes, offsets = coarse[2, 0], first_offset
    for j in range(1, blocks):
        slope = coarse[2, j]
        slopes, offsets = slope * slopes, slope * offsets + coarse[3, j]
        coarse[2, j], coarse[3, j] = slopes, offsets

    squeeze[R_SLOPE], squeeze[R_OFFSET], squeeze[R_LAST] = slopes, offsets, coarse[0, blocks - 1]
    squeeze[R_FIRST], squeeze[R_FIRST_OFFSET] = coarse[0, 0], first_offset
    span = nx // 2 + 2
    for k in range(5):
        message[k * span : (k + 1) * span] = squeeze[k, pl.ds(PAD - 2, span, 2), :]


def outer_kernel(st, across, beside, across_late, beside_late, extra, sides, before, after):
    planes, rows, ext, nz = st.shape
    ny, nx = rows - 2, ext - 2 * PAD
    me, count = lax.axis_index("gy"), lax.axis_size("gy")
    mask = x_mask((ext, nz), nx)
    unpack(across, beside, (M_K, M_C, M_FY, M_2S, M_2G), before, after)
    unpack(across_late, beside_late, range(SOON, MESSAGE), before, after, SOON)
    low = jnp.where(me == 0, 0.0, mask)
    high = jnp.where(me == count - 1, 0.0, mask)
    for i, ref, inside in ((0, before, low), (ny + 1, after, high)):
        is_after = i > 0
        ss, sg, gg = inverse(jnp.maximum(ref[M_D2], SOLID_CAP), ref[M_C2], inside)
        to, back = (CONDUCT + FLOW, CONDUCT) if is_after else (CONDUCT, CONDUCT + FLOW)
        res_s = ref[M_3S] + ref[M_FY] * st[SB, i]
        res_g = ref[M_3G] + to * st[GB, i]
        side = 3 if is_after else 0
        extra[side] = ref[M_2S] + ref[M_FY] * (ss * res_s + sg * res_g)
        extra[side + 1] = ref[M_2G] + back * (sg * res_s + gg * res_g)
        extra[side + 2] = ref[M_FY]
        k2 = 2.0 * ref[M_FY] - ref[M_K]
        solid, ratio, denominator = coarse_coefficients(pair_x(ref[M_C] + ref[M_C2]), pair_x(ref[M_K] + k2))
        sides[int(is_after)] = ratio
        if is_after:
            sides[2] = (2.0 * FLOW) / denominator


class Group:
    def __init__(self, radix, stride, own, others, span):
        self.radix, self.own, self.others, self.span = radix, own, others, span
        me = lax.axis_index("gy")
        self.at = lax.rem(lax.div(me, stride), radix)
        low = lax.rem(me, stride)
        self.lowest, self.highest = low == 0, low == stride - 1

    def plane(self, ref, plane):
        return ref[plane * self.span : (plane + 1) * self.span]

    def member(self, place, plane):
        value = None if self.own is None else self.plane(self.own, plane)
        for k, ref in enumerate(self.others, 1):
            got = self.plane(ref, plane)
            value = got if value is None else jnp.where(source(self.at, k, self.radix) == place, got, value)
        return value

    def lower(self, slope, offset):
        ahead = (jnp.ones_like(slope), jnp.zeros_like(slope))
        for place in range(self.radix - 1):
            a, b = self.member(place, R_SLOPE), self.member(place, R_OFFSET)
            below = place < self.at
            ahead = tuple(jnp.where(below, new, old) for new, old in zip((a * ahead[0], a * ahead[1] + b), ahead))
        return slope * ahead[0], slope * ahead[1] + offset

    def beside(self, leads, first, first_offset):
        last_low, lead_high, offset_high = leads
        for place in range(self.radix):
            low, high = self.lowest & (self.at == place + 1), self.highest & (self.at == place - 1)
            last_low = jnp.where(low, self.member(place, R_LAST), last_low)
            lead_high = jnp.where(high, self.member(place, first), lead_high)
            offset_high = jnp.where(high, self.member(place, first_offset), offset_high)
        return last_low, lead_high, offset_high


def source(at, k, radix):
    if radix & (radix - 1) == 0:
        return at ^ k
    return (at + radix - k) % radix


def stages(count):
    out, rest = [2], count // 2
    if count % 2:
        return [1, count]
    while rest > 1:
        radix = next((r for r in (8, 4, 2) if rest % r == 0), rest)
        out.append(radix)
        rest //= radix
    return out if len(out) > 1 else out + [1]


def exchange_stage(messages, radix, stride):
    count, got = lax.axis_size("gy"), []
    for k, message in enumerate(messages, 1):
        pairs = []
        for me in range(count):
            at = me // stride % radix
            pairs.append((me + (source(at, k, radix) - at) * stride, me))
        got.append(lax.ppermute(message, "gy", pairs))
    return got


def join_kernel(radix, stride, final, span, *refs):
    own, near_in, others, (near, outs) = refs[0], refs[1], refs[2 : 1 + radix + 1], (refs[radix + 1], refs[radix + 2 :])
    group = Group(radix, stride, own, others, span)
    old = [group.plane(near_in, k) for k in range(5)]
    ahead = group.lower(old[0], old[1])
    leads = group.beside(old[2:], R_FIRST, R_FIRST_OFFSET)
    for k, value in enumerate(ahead + leads):
        near[k * span : (k + 1) * span] = value
    slope, offset = group.member(0, R_SLOPE), group.member(0, R_OFFSET)
    for place in range(1, radix):
        a = group.member(place, R_SLOPE)
        slope, offset = a * slope, a * offset + group.member(place, R_OFFSET)
    total = [slope, offset, group.member(radix - 1, R_LAST), group.member(0, R_FIRST), group.member(0, R_FIRST_OFFSET)]
    if final == 0:
        for k, value in enumerate(total):
            outs[0][k * span : (k + 1) * span] = value
        return
    at = lax.axis_index("gy") // (stride * radix)
    for k, out in enumerate(outs, 1):
        onward = (at ^ k) > at if final & (final - 1) == 0 else (at + k) % final > at
        for plane, (a, b) in enumerate(zip(total[:3], total[3:] + [jnp.zeros_like(slope)])):
            out[plane * span : (plane + 1) * span] = jnp.where(onward, a, b)


def third_kernel(radix, stride, *refs):
    st, extra, coarse, sides, near = refs[:5]
    others, (out, sc, wide, done, sems) = refs[5 : 4 + radix], refs[4 + radix :]
    planes, rows, ext, nz = st.shape
    ny, nx = rows - 2, ext - 2 * PAD
    me, count = lax.axis_index("gy"), lax.axis_size("gy")
    edge = edge_weights((ext, nz))
    span = nx // 2 + 2
    blocks = ny // 2

    group = Group(radix, stride, None, others, span)
    leads = [group.plane(near, k) for k in range(2, 5)]
    gas_in = group.plane(near, 1)
    if radix > 1:
        gas_in = group.lower(group.plane(near, 0), gas_in)[1]
        leads = group.beside(leads, 0, 1)
    inside_high = me < count - 1
    lead_low, lead_high, offset_high = leads
    for k, v in enumerate((gas_in, lead_low, lead_high, offset_high)):
        wide[k, : PAD - 2] = jnp.zeros((PAD - 2, nz), jnp.float32)
        wide[k, ext - PAD + 2 :] = jnp.zeros((PAD - 2, nz), jnp.float32)
        wide[k, pl.ds(PAD - 2, span, 2), :] = v
        wide[k, pl.ds(PAD - 1, span, 2), :] = v

    gas_in = wide[0]
    last = ny + 1
    solid_low = wide[1] + sides[0] * gas_in
    sc[0, 0] = st[SA, 0] + solid_low
    sc[1, 0] = st[GA, 0] + gas_in

    def correct(j, carry):
        gas = coarse[2, j] * gas_in + coarse[3, j]
        solid = coarse[0, j] + coarse[1, j] * gas
        for i in (2 * j + 1, 2 * j + 2):
            sc[0, i] = st[SA, i] + solid
            sc[1, i] = st[GA, i] + gas
        return carry

    lax.fori_loop(0, blocks, correct, 0)
    gas = coarse[2, blocks - 1] * gas_in + coarse[3, blocks - 1]
    gas_high = jnp.where(inside_high, sides[2] * gas + wide[3], 0.0)
    solid_high = wide[2] + sides[1] * gas_high
    sc[0, last] = st[SA, last] + solid_high
    sc[1, last] = st[GA, last] + gas_high

    view = Fields(st, sc)
    for i, is_after, solid, gas in ((0, False, solid_low, gas_in), (last, True, solid_high, gas_high)):
        side = 3 if is_after else 0
        fy = extra[side + 2]
        rs = extra[side] + fy * solid
        rg = extra[side + 1] + (CONDUCT if is_after else CONDUCT + FLOW) * gas
        res = outer_residual(view, i, SA, rs, rg, fy, edge, is_after)
        sc[2, i], sc[3, i] = relaxed(view, i, SA, *res)

    def sweep(k, carry):
        stores = []
        for r in range(GROUP):
            i = GROUP * k + 1 + r
            new_s, new_g = relaxed(view, i, SA, *row_residual(view, i, SA, edge))
            stores += [((2, i), new_s), ((3, i), new_g)]
        for at, value in stores:
            sc[at] = value
        return carry

    lax.fori_loop(0, ny // GROUP, sweep, 0)

    def leaving(k):
        part = pl.ds(GROUP * k, GROUP)
        return pltpu.make_async_copy(done.at[:, part], out.at[:, part], sems.at[k])

    def final(k, carry):
        stores = []
        for r in range(GROUP):
            i = GROUP * k + 1 + r
            new_s, new_g = relaxed(view, i, SB, *row_residual(view, i, SB, edge))
            stores += [((0, i - 1), new_s), ((1, i - 1), new_g)]
        for at, value in stores:
            done[at] = value[PAD : PAD + nx]
        leaving(k).start()
        return carry

    lax.fori_loop(0, ny // GROUP, final, 0)
    for k in range(ny // GROUP):
        leaving(k).wait()


class Fields:
    def __init__(self, st, sc):
        self.st, self.sc = st, sc

    def __getitem__(self, at):
        return (self.sc if at[0] <= GB else self.st)[at]


def cost(rows, cells):
    return pl.CostEstimate(flops=50 * rows * cells, bytes_accessed=16 * 4 * rows * cells, transcendentals=0)


def swap(x, axis, first):
    pairs = []
    for i in range(first, lax.axis_size(axis) - 1, 2):
        pairs += [(i, i + 1), (i + 1, i)]
    return lax.ppermute(x, axis, pairs)


def shards(temps, right_side, exchange, coupling):
    temps, right_side = (jnp.transpose(a, (0, 2, 1, 3)) for a in (temps, right_side))
    exchange, coupling = (jnp.transpose(a, (1, 0, 2)) for a in (exchange, coupling))
    temps, right_side, exchange, coupling = (
        pltpu.with_memory_space_constraint(a, pltpu.HBM) for a in (temps, right_side, exchange, coupling)
    )
    ny, nx, nz = exchange.shape
    ext = nx + 2 * PAD
    f32 = functools.partial(jax.ShapeDtypeStruct, dtype=jnp.float32)

    strip = f32(((ny * STRIP_ROWS + 7) // 8 * 8, nz))
    edges = [pltpu.VMEM((2, 2, ny, 8, nz), jnp.float32)] * 2 + [pltpu.VMEM((2, ny, 8, nz), jnp.float32)] * 2
    one, two = pl.pallas_call(
        pack_kernel,
        out_shape=(strip, strip),
        in_specs=[HBM] * 4,
        out_specs=(VMEM, VMEM),
        scratch_shapes=edges + [pltpu.SemaphoreType.DMA((8,))],
        compiler_params=PARAMS,
        name="pack_x",
    )(temps, right_side, exchange, coupling)
    one, two = swap(one, "gx", 0), swap(two, "gx", 1)

    state = f32((PLANES, ny + 2, ext, nz))

    def letter(planes):
        return f32((planes, ext - 2 * CROP, nz))

    st = pl.pallas_call(
        load_kernel,
        out_shape=state,
        in_specs=[HBM] * 4,
        out_specs=VMEM,
        scratch_shapes=[pltpu.SemaphoreType.DMA((6,))],
        compiler_params=PARAMS,
        cost_estimate=cost(2 * ny, ext * nz),
        name="load",
    )(temps, right_side, exchange, coupling)
    st, across = pl.pallas_call(
        first_kernel,
        out_shape=(state, letter(SOON)),
        in_specs=[VMEM] * 3,
        out_specs=(VMEM,) * 2,
        input_output_aliases={0: 0},
        compiler_params=PARAMS,
        name="first",
    )(st, one, two)
    across = swap(across, "gy", 1)

    rows = f32((4, ny // 2, ext, nz))
    st, coarse, late, beside_late, beside = pl.pallas_call(
        inner_kernel,
        out_shape=(state, rows, letter(MESSAGE - SOON), letter(MESSAGE - SOON), letter(SOON)),
        in_specs=[VMEM] * 3,
        out_specs=(VMEM,) * 5,
        input_output_aliases={0: 0},
        compiler_params=PARAMS,
        cost_estimate=cost(4 * ny, ext * nz),
        name="inner",
    )(st, one, two)

    beside = swap(beside, "gy", 0)
    late, beside_late = swap(late, "gy", 1), swap(beside_late, "gy", 0)

    span = nx // 2 + 2
    five, three = (f32(((k * span + 7) // 8 * 8, nz)) for k in (5, 3))
    letters = [pltpu.VMEM((MESSAGE, ext, nz), jnp.float32)] * 2
    st, coarse, total = pl.pallas_call(
        second_kernel,
        out_shape=(state, rows, five),
        in_specs=[VMEM] * 4,
        out_specs=(VMEM,) * 3,
        scratch_shapes=letters + [pltpu.VMEM((5, ext, nz), jnp.float32)],
        input_output_aliases={0: 0, 1: 1},
        compiler_params=PARAMS,
        name="second",
    )(st, coarse, across, beside)
    extra, sides = pl.pallas_call(
        outer_kernel,
        out_shape=(f32((6, ext, nz)), f32((3, ext, nz))),
        in_specs=[VMEM] * 5,
        out_specs=(VMEM,) * 2,
        scratch_shapes=letters,
        compiler_params=PARAMS,
        name="outer",
    )(st, across, beside, late, beside_late)

    near = jnp.concatenate([jnp.ones((span, nz), jnp.float32), jnp.zeros((five.shape[0] - span, nz), jnp.float32)])
    radices, stride = stages(lax.axis_size("gy")), 1
    for place, radix in enumerate(radices[:-1]):
        others = exchange_stage([total] * (radix - 1), radix, stride)
        final = radices[-1] if place == len(radices) - 2 else 0
        outs = (three,) * (final - 1) if final else (five,)
        near, *messages = pl.pallas_call(
            functools.partial(join_kernel, radix, stride, final, span),
            out_shape=(five,) + outs,
            in_specs=[VMEM] * (1 + radix),
            out_specs=(VMEM,) * (1 + len(outs)),
            compiler_params=PARAMS,
            name="join",
        )(total, near, *others)
        total = messages[0] if messages else total
        stride *= radix
    got = exchange_stage(messages, radices[-1], stride)

    out = pl.pallas_call(
        functools.partial(third_kernel, radices[-1], stride),
        out_shape=f32((2, ny, nx, nz)),
        in_specs=[VMEM] * (5 + len(got)),
        out_specs=HBM,
        scratch_shapes=[
            pltpu.VMEM((4, ny + 2, ext, nz), jnp.float32),
            pltpu.VMEM((4, ext, nz), jnp.float32),
            pltpu.VMEM((2, ny, nx, nz), jnp.float32),
            pltpu.SemaphoreType.DMA((ny // GROUP,)),
        ],
        compiler_params=PARAMS,
        name="third",
    )(st, extra, coarse, sides, near, *got)
    return jnp.transpose(out, (0, 2, 1, 3))


def solution(mesh):
    return jax.shard_map(
        shards,
        mesh=mesh,
        in_specs=(
            P(None, "gx", "gy", None),
            P(None, "gx", "gy", None),
            P("gx", "gy", None),
            P("gx", "gy", None),
        ),
        out_specs=P(None, "gx", "gy", None),
        check_vma=False,
    )
```

```python
import functools

import jax
import jax.numpy as jnp
from jax import lax
from jax.experimental import pallas as pl
from jax.experimental.pallas import tpu as pltpu
from jax.sharding import PartitionSpec as P

SOLID_CAP, GAS_CAP, FLOW, CONDUCT, RELAX, LUMP = 0.5, 0.02, 40.0, 0.05, 0.8, 0.25
GAS_SELF = GAS_CAP + 4.5 * CONDUCT

PAD = 8
WX = 5
CROP = 4
(SA, GA, SB, GB, K, C, RS, RG, FX, FZ, H, FY, ASS, ASG, AGG) = range(15)
PLANES = 15
(M_S, M_G, M_K, M_C, M_FY, M_1S, M_1G, M_2S, M_2G) = range(9)
MESSAGE, EARLY = 9, 5

GROUP = 3

VMEM = pl.BlockSpec(memory_space=pltpu.VMEM)
HBM = pl.BlockSpec(memory_space=pltpu.HBM)
PARAMS = pltpu.CompilerParams(vmem_limit_bytes=40 * 1024 * 1024)


def up_x(v):
    return pltpu.roll(v, v.shape[0] - 1, 0)


def down_x(v):
    return pltpu.roll(v, 1, 0)


def up_z(v):
    return pltpu.roll(v, v.shape[1] - 1, 1)


def down_z(v):
    return pltpu.roll(v, 1, 1)


def lanes(shape):
    return lax.broadcasted_iota(jnp.int32, shape, 1)


def x_mask(shape, nx):
    row = lax.broadcasted_iota(jnp.int32, shape, 0)
    place, count = lax.axis_index("gx"), lax.axis_size("gx")
    low = jnp.where(place == 0, PAD, PAD - WX)
    high = jnp.where(place == count - 1, PAD + nx, PAD + nx + WX)
    return jnp.where((row >= low) & (row < high), 1.0, 0.0).astype(jnp.float32)


STRIP = ((SA, WX - 1), (GA, WX - 1), (K, WX), (RS, WX - 1), (RG, WX - 1), (C, WX - 1))
STRIP_ROWS = sum(width for plane, width in STRIP)


def conductivity_of(s, exchange):
    return 1.0 + 4.0 * exchange * s * s * s


def strip_values(s, g, k, rs, rg, c, low):
    out, inn = (WX - 1, WX - 2) if low else (8 - WX, 9 - WX)
    four = slice(0, WX - 1) if low else slice(9 - WX, 8)
    five = slice(0, WX) if low else slice(8 - WX, 8)
    row = lax.broadcasted_iota(jnp.int32, s.shape, 0)
    rs = rs + jnp.where(row == inn, 0.5 * (k[inn : inn + 1] + k[out : out + 1]) * s[out : out + 1], 0.0)
    rg = rg + jnp.where(row == inn, CONDUCT * g[out : out + 1], 0.0)
    return [s[four], g[four], k[five], rs[four], rg[four], c[four]]


def pack_kernel(temps, right, exchange, coupling, one, two, early, *scratch):
    pair_low, pair_high, single_low, single_high, rows_t, rows_e, rows_c, sems = scratch
    even = lax.axis_index("gx") % 2 == 0
    odd = lax.axis_index("gy") % 2 == 1
    ny, nx, nz = exchange.shape
    copies = []
    for k, ref in enumerate((temps, right, exchange, coupling)):
        low, high, at = (pair_low, pair_high, k) if k < 2 else (single_low, single_high, k - 2)
        lead = (slice(None),) * (ref.ndim - 2)
        copies.append(pltpu.make_async_copy(ref.at[lead + (slice(0, 8),)], low.at[at], sems.at[2 * k]))
        copies.append(pltpu.make_async_copy(ref.at[lead + (slice(nx - 8, nx),)], high.at[at], sems.at[2 * k + 1]))
    ends = pl.ds(jnp.where(odd, ny - 2, 0), 2)
    copies.append(pltpu.make_async_copy(temps.at[:, ends], rows_t, sems.at[8]))
    copies.append(pltpu.make_async_copy(exchange.at[ends], rows_e, sems.at[9]))
    copies.append(pltpu.make_async_copy(coupling.at[ends], rows_c, sems.at[10]))
    for copy in copies:
        copy.start()
    for copy in copies:
        copy.wait()
    at = 0
    for y in range(ny):
        sides = []
        for pair, single, is_low in ((pair_low, single_low, True), (pair_high, single_high, False)):
            s, g, rs, rg = (pair[i, j, y] for i in range(2) for j in range(2))
            sides.append(strip_values(s, g, conductivity_of(s, single[0, y]), rs, rg, single[1, y], is_low))
        for low, high, (plane, width) in zip(*sides, STRIP):
            one[at : at + width] = jnp.where(even, high, low)
            two[at : at + width] = jnp.where(even, low, high)
            at += width
    k = [conductivity_of(rows_t[0, i], rows_e[i]) for i in range(2)]
    pick = lambda pair: jnp.where(odd, pair[1], pair[0])
    early[M_S], early[M_G] = pick([rows_t[0, i] for i in range(2)]), pick([rows_t[1, i] for i in range(2)])
    early[M_K], early[M_C], early[M_FY] = pick(k), pick([rows_c[i] for i in range(2)]), 0.5 * (k[0] + k[1])


def load_kernel(temps, right, exchange, coupling, st, sems):
    ny, nx, nz = exchange.shape
    planes, rows, ext, nz = st.shape
    copies = []
    for k, (plane, ref) in enumerate(
        ((SA, temps.at[0]), (K, exchange), (GA, temps.at[1]), (RS, right.at[0]), (RG, right.at[1]), (C, coupling))
    ):
        to = st.at[plane, pl.ds(1, ny), pl.ds(PAD, nx)]
        copies.append(pltpu.make_async_copy(ref, to, sems.at[k]))
    for copy in copies:
        copy.start()
    zeros = jnp.zeros((PAD, nz), jnp.float32)

    def clear(i, carry):
        for plane, width in STRIP:
            st[plane, i, :PAD] = zeros
            st[plane, i, PAD + nx :] = zeros
        return carry

    lax.fori_loop(1, ny + 1, clear, 0)
    for copy in copies:
        copy.wait()

    def conduct(i, carry):
        s = st[SA, i, PAD : PAD + nx]
        st[K, i, PAD : PAD + nx] = conductivity_of(s, st[K, i, PAD : PAD + nx])
        return carry

    lax.fori_loop(1, ny + 1, conduct, 0)


def place_halo(st, one, two, y, nx):
    even = lax.axis_index("gx") % 2 == 0
    at, i = y * STRIP_ROWS, y + 1
    for plane, width in STRIP:
        a, b = one[at : at + width], two[at : at + width]
        st[plane, i, PAD - width : PAD] = jnp.where(even, b, a)
        st[plane, i, PAD + nx : PAD + nx + width] = jnp.where(even, a, b)
        at += width


def inner(s, g, c, h, fx, fz, edge):
    t = c * (s - g)
    flux_x = fx * (up_x(s) - s)
    flux_z = fz * (up_z(s) - s)
    part_s = (flux_x - down_x(flux_x)) + (flux_z - down_z(flux_z)) - h * s - t
    part_g = (
        t
        - GAS_SELF * g
        + CONDUCT * (up_x(g) + down_x(g))
        + edge[0] * up_z(g)
        + edge[1] * down_z(g)
    )
    return part_s, part_g


def edge_weights(shape):
    lane = lanes(shape)
    weight = jnp.float32(0.25 * CONDUCT)
    return jnp.where(lane == shape[1] - 1, 0.0, weight), jnp.where(lane == 0, 0.0, weight)


def row_inner(st, i, s_at, edge):
    return inner(st[s_at, i], st[s_at + 1, i], st[C, i], st[H, i], st[FX, i], st[FZ, i], edge)


def row_residual(st, i, s_at, edge):
    part_s, part_g = row_inner(st, i, s_at, edge)
    s, g, before = st[s_at, i], st[s_at + 1, i], st[s_at + 1, i - 1]
    part_s += st[FY, i] * (st[s_at, i + 1] - s) + st[FY, i - 1] * (st[s_at, i - 1] - s)
    part_g += CONDUCT * (st[s_at + 1, i + 1] + before) - FLOW * (g - before)
    return st[RS, i] + part_s, st[RG, i] + part_g


def relaxed(st, i, s_at, res_s, res_g):
    s = st[s_at, i] + st[ASS, i] * res_s + st[ASG, i] * res_g
    g = st[s_at + 1, i] + st[ASG, i] * res_s + st[AGG, i] * res_g
    return s, g


def faces(k):
    lane = lanes(k.shape)
    end = k.shape[1] - 1
    fx = 0.5 * (k + up_x(k))
    fz = jnp.where(lane == end, 0.0, 0.125 * (k + up_z(k)))
    h = SOLID_CAP + jnp.where((lane == 0) | (lane == end), 0.125 * k, 0.0)
    return fx, fz, h, h + (fx + down_x(fx)) + (fz + down_z(fz))


def inverse(diag, c, mask):
    gas_diag = (GAS_SELF + FLOW) + c
    inv = (RELAX * mask) / (diag * gas_diag - c * c)
    return inv * gas_diag, inv * c, inv * diag


def last_relaxed(st, i, s_at, edge, own):
    full_s, full_g = st[s_at, i], st[s_at + 1, i]
    s, g = full_s[own], full_g[own]
    flux_x = st[FX, i] * (up_x(full_s) - full_s)
    flux_z = st[FZ, i, own] * (up_z(s) - s)
    c, before = st[C, i, own], st[s_at + 1, i - 1, own]
    t = c * (s - g)
    res_s = st[RS, i, own] + (flux_x[own] - down_x(flux_x)[own]) + (flux_z - down_z(flux_z)) - st[H, i, own] * s - t
    res_s += st[FY, i, own] * (st[s_at, i + 1, own] - s) + st[FY, i - 1, own] * (st[s_at, i - 1, own] - s)
    res_g = st[RG, i, own] + t - GAS_SELF * g + edge[0][own] * up_z(g) + edge[1][own] * down_z(g)
    res_g += CONDUCT * (up_x(full_g)[own] + down_x(full_g)[own] + st[s_at + 1, i + 1, own] + before) - FLOW * (g - before)
    ss, sg, gg = st[ASS, i, own], st[ASG, i, own], st[AGG, i, own]
    return s + ss * res_s + sg * res_g, g + sg * res_s + gg * res_g


def grouped(rows, work):
    for start in range(0, len(rows), GROUP):
        stores = []
        for i in rows[start : start + GROUP]:
            stores += work(i)
        for ref, at, value in stores:
            ref[at] = value


def row_coefficients(st, i, mask):
    fx, fz, h, diag = faces(st[K, i])
    fy = 0.5 * (st[K, i] + st[K, i + 1])
    before = 0.5 * (st[K, i] + st[K, i - 1])
    ss, sg, gg = inverse(diag + st[C, i] + fy + before, st[C, i], mask)
    values = ((FX, fx), (FZ, fz), (H, h), (FY, fy), (ASS, ss), (ASG, sg), (AGG, gg))
    return [(st, (plane, i), v) for plane, v in values]


def row_sweep(st, i, source, target, edge):
    s, g = relaxed(st, i, source, *row_residual(st, i, source, edge))
    return [(st, (target, i), s), (st, (target + 1, i), g)]


def send_planes(st, onward, edge):
    ny = st.shape[1] - 2
    e, d, near = (ny, ny - 1, ny - 1) if onward else (1, 2, 1)
    fy, s, g, g_d = st[FY, near], st[SA, e], st[GA, e], st[GA, d]
    part_s, part_g = row_inner(st, e, SA, edge)
    m_1s = st[RS, e] + part_s + fy * (st[SA, d] - s)
    m_1g = st[RG, e] + part_g + CONDUCT * g_d - FLOW * (g - g_d if onward else g)
    m_2s = st[RS, e] + fy * st[SB, d]
    m_2g = st[RG, e] + (CONDUCT + FLOW if onward else CONDUCT) * st[GB, d]
    return [s, g, st[K, e], st[C, e], fy, m_1s, m_1g, m_2s, m_2g]


def write_across(ref, st, onward, edge):
    ext = st.shape[2]
    for k, value in enumerate(send_planes(st, onward, edge)):
        if k >= EARLY:
            ref[k - EARLY] = value[CROP : ext - CROP]
        else:
            ref[MESSAGE - EARLY, 8 * k : 8 * k + 4] = value[CROP:PAD]
            ref[MESSAGE - EARLY, 8 * k + 4 : 8 * k + 8] = value[ext - PAD : ext - CROP]


def write_beside(refs, st, onward, edge):
    ext = st.shape[2]
    for k, value in enumerate(send_planes(st, onward, edge)):
        ref, at = (refs[0], k) if k < EARLY else (refs[1], k - EARLY)
        ref[at] = value[CROP : ext - CROP]


def write_message(write, ref, st, onward, edge):
    for go in (True, False):

        @pl.when(onward == go)
        def _():
            write(ref, st, go, edge)


def first_kernel(st_in, one, two, early, st, across):
    del st_in, early
    planes, rows, ext, nz = st.shape
    ny, nx = rows - 2, ext - 2 * PAD
    shape = (ext, nz)
    mask = x_mask(shape, nx)
    edge = edge_weights(shape)

    for y in list(range(4)) + list(range(ny - 4, ny)):
        place_halo(st, one, two, y, nx)
    for i in (1, ny):
        fx, fz, h, diag = faces(st[K, i])
        st[FX, i], st[FZ, i], st[H, i] = fx, fz, h
    st[FY, 1] = 0.5 * (st[K, 1] + st[K, 2])
    st[FY, ny - 3] = 0.5 * (st[K, ny - 3] + st[K, ny - 2])
    ends = [2, 3, ny - 2, ny - 1]
    grouped(ends, lambda i: row_coefficients(st, i, mask))
    grouped(ends, lambda i: row_sweep(st, i, SA, SB, edge))
    write_message(write_across, across, st, lax.axis_index("gy") % 2 == 1, edge)


def outer_residual(st, i, s_at, rs, rg, fy_out, edge, after):
    part_s, part_g = row_inner(st, i, s_at, edge)
    s, g = st[s_at, i], st[s_at + 1, i]
    if after:
        part_s += st[FY, i - 1] * (st[s_at, i - 1] - s)
        part_g += (CONDUCT + FLOW) * st[s_at + 1, i - 1]
    else:
        part_s += st[FY, i] * (st[s_at, i + 1] - s)
        part_g += CONDUCT * st[s_at + 1, i + 1]
    return rs + part_s - fy_out * s, rg + part_g - FLOW * g


def pair_x(v):
    row = lax.broadcasted_iota(jnp.int32, v.shape, 0)
    return v + jnp.where(row % 2 == 0, up_x(v), down_x(v))


def coarse_coefficients(c_sum, k_sum):
    solid = 4.0 * SOLID_CAP + c_sum + LUMP * k_sum
    ratio = c_sum / solid
    denominator = (4.0 * GAS_CAP + 2.0 * FLOW) + c_sum - c_sum * ratio
    return solid, ratio, denominator


def coarse_row(st, coarse, j, mask, edge):
    i = 2 * j + 1
    res_s, res_g = row_residual(st, i, SA, edge)
    more_s, more_g = row_residual(st, i + 1, SA, edge)
    res_s, res_g = pair_x((res_s + more_s) * mask), pair_x((res_g + more_g) * mask)
    c_sum = pair_x(st[C, i] + st[C, i + 1])
    solid, ratio, denominator = coarse_coefficients(c_sum, pair_x(st[K, i] + st[K, i + 1]))
    lead = res_s / solid
    values = (lead, ratio, (2.0 * FLOW) / denominator, (res_g + c_sum * lead) / denominator)
    return [(coarse, (k, j), v) for k, v in enumerate(values)]


def inner_kernel(st_in, one, two, st, coarse, beside_a, beside_b):
    del st_in
    planes, rows, ext, nz = st.shape
    ny, nx = rows - 2, ext - 2 * PAD
    shape = (ext, nz)
    mask = x_mask(shape, nx)
    edge = edge_weights(shape)
    for y in range(4, ny - 4):
        place_halo(st, one, two, y, nx)
    grouped(list(range(4, ny - 2)), lambda i: row_coefficients(st, i, mask))
    grouped(list(range(4, ny - 2)), lambda i: row_sweep(st, i, SA, SB, edge))
    grouped(list(range(3, ny - 1)), lambda i: row_sweep(st, i, SB, SA, edge))
    for j in range(2, ny // 2 - 2):
        for ref, at, value in coarse_row(st, coarse, j, mask, edge):
            ref[at] = value
    write_message(write_beside, (beside_a, beside_b), st, lax.axis_index("gy") % 2 == 0, edge)


def unpack(early, across, beside_a, beside_b, before, after):
    even = lax.axis_index("gy") % 2 == 0
    ext, nz = before.shape[1:]
    zeros = jnp.zeros((PAD, nz), jnp.float32)

    def fill(far, near):
        for k in range(MESSAGE):
            for ref in (far, near):
                ref[k, :PAD] = zeros
                ref[k, ext - PAD :] = zeros
            near[k, CROP : ext - CROP] = beside_a[k] if k < EARLY else beside_b[k - EARLY]
            if k >= EARLY:
                far[k, CROP : ext - CROP] = across[k - EARLY]
            else:
                far[k, PAD : ext - PAD] = early[k]
                far[k, CROP:PAD] = across[MESSAGE - EARLY, 8 * k : 8 * k + 4]
                far[k, ext - PAD : ext - CROP] = across[MESSAGE - EARLY, 8 * k + 4 : 8 * k + 8]

    for is_even, far, near in ((True, before, after), (False, after, before)):

        @pl.when(even == is_even)
        def _():
            fill(far, near)


def second_kernel(st_in, coarse_in, early, across, beside_a, beside_b, st, coarse, extra, total, last_info, first_info, message, before, after, squeeze):
    del st_in, coarse_in
    planes, rows, ext, nz = st.shape
    ny, nx = rows - 2, ext - 2 * PAD
    shape = (ext, nz)
    me, count = lax.axis_index("gy"), lax.axis_size("gy")
    mask = x_mask(shape, nx)
    low = jnp.where(me == 0, 0.0, mask)
    high = jnp.where(me == count - 1, 0.0, mask)
    edge = edge_weights(shape)
    unpack(early, across, beside_a, beside_b, before, after)

    last = ny + 1
    ends = ((0, before, low), (last, after, high))
    for i, ref, inside in ends:
        st[SA, i], st[GA, i], st[K, i], st[C, i] = ref[M_S], ref[M_G], ref[M_K], ref[M_C]
    st[FY, 0] = 0.5 * (st[K, 0] + st[K, 1])
    st[FY, ny] = 0.5 * (st[K, ny] + st[K, last])
    for i in (1, ny):
        fx, fz = st[FX, i], st[FZ, i]
        diag = st[H, i] + (fx + down_x(fx)) + (fz + down_z(fz)) + st[C, i] + st[FY, i - 1] + st[FY, i]
        st[ASS, i], st[ASG, i], st[AGG, i] = inverse(diag, st[C, i], mask)
    for i, ref, inside in ends:
        fx, fz, h, diag = faces(st[K, i])
        st[FX, i], st[FZ, i], st[H, i] = fx, fz, h
        diag += st[C, i] + ref[M_FY] + st[FY, min(i, ny)]
        st[ASS, i], st[ASG, i], st[AGG, i] = inverse(diag, st[C, i], inside)

    res = before[M_1S] + st[FY, 0] * (st[SA, 1] - st[SA, 0]), before[M_1G] + CONDUCT * st[GA, 1]
    new_low = relaxed(st, 0, SA, *res)
    res = after[M_1S] + st[FY, ny] * (st[SA, ny] - st[SA, last]), after[M_1G] + (CONDUCT + FLOW) * st[GA, ny]
    new_high = relaxed(st, last, SA, *res)
    stores = row_sweep(st, 1, SA, SB, edge) + row_sweep(st, ny, SA, SB, edge)
    st[SB, 0], st[GB, 0] = new_low
    st[SB, last], st[GB, last] = new_high
    for ref, at, value in stores:
        ref[at] = value

    for i, ref, inside in ends:
        is_after = i > 0
        res = outer_residual(st, i, SB, ref[M_2S], ref[M_2G], ref[M_FY], edge, is_after)
        st[SA, i], st[GA, i] = relaxed(st, i, SB, *res)
    grouped([1, 2, ny - 1, ny], lambda i: row_sweep(st, i, SB, SA, edge))

    for i, ref, inside in ends:
        for k, plane in enumerate((M_2S, M_2G, M_FY)):
            extra[(3 if i else 0) + k] = ref[plane]

    blocks = ny // 2
    for j in (0, 1, blocks - 2, blocks - 1):
        for ref, at, value in coarse_row(st, coarse, j, mask, edge):
            ref[at] = value
    for k in range(4):
        squeeze[k] = coarse[k, 0]
    slopes, offsets = coarse[2, 0], coarse[3, 0]
    for j in range(1, blocks):
        slope = coarse[2, j]
        slopes, offsets = slope * slopes, slope * offsets + coarse[3, j]
        coarse[2, j], coarse[3, j] = slopes, offsets
    squeeze[4], squeeze[5], squeeze[6], squeeze[7] = slopes, offsets, coarse[0, blocks - 1], coarse[1, blocks - 1]

    span = nx // 2 + 2
    lead, ratio, slope, offset, slopes, offsets, lead_last, ratio_last = (
        squeeze[k, pl.ds(PAD - 2, span, 2), :] for k in range(8)
    )
    part = slice(PAD - 1, PAD + nx + 1)

    def increments(d, face, gas):
        return [(st[FY, face] * (st[SA, d] - st[SB, d]))[part], (gas * (st[GA, d] - st[GB, d]))[part]]

    onward = [lead_last, ratio_last] + increments(ny - 1, ny - 1, CONDUCT + FLOW)
    back = [lead, offset] + increments(2, 1, CONDUCT) + [slope, ratio]
    write_rows(total, [slopes, offsets])
    write_rows(last_info, onward)
    write_rows(first_info, back)
    for go, info in ((True, onward), (False, back)):

        @pl.when((me % 2 == 0) == go)
        def _():
            write_rows(message, [slopes, offsets] + info)


def write_rows(ref, values):
    at = 0
    for value in values:
        ref[at : at + value.shape[0]] = value
        at += value.shape[0]


class Rows:
    def __init__(self, nx):
        self.span = nx // 2 + 2
        self.map = 2 * self.span
        self.info = self.map + 2 * (nx + 2)
        self.rest = self.map
        self.final = self.map + self.info
        self.full = self.final + self.rest
        self.low = self.map
        self.high = self.low + self.info
        self.near = self.high + self.info + self.rest


def source(at, k, radix):
    if radix & (radix - 1) == 0:
        return at ^ k
    return (at + radix - k) % radix


def target(at, k, radix):
    return at ^ k if radix & (radix - 1) == 0 else (at + k) % radix


def order(radix):
    out = [(k, any(abs(source(at, k, radix) - at) == 1 for at in range(radix))) for k in range(1, radix)]
    return sorted(out, key=lambda item: (not item[1], -item[0]))


def stages(count):
    if count % 2:
        return [1, count]
    out, rest = [2], count // 2
    while rest > 1:
        radix = next((r for r in (8, 4, 2) if rest % r == 0), rest)
        out.append(radix)
        rest //= radix
    return out if len(out) > 1 else out + [1]


def exchange_stage(messages, radix, stride):
    count, got = lax.axis_size("gy"), []
    for (k, near), message in zip(order(radix), messages):
        pairs = []
        for me in range(count):
            at, low = me // stride % radix, me % stride
            sender = me - low + (source(at, k, radix) - at) * stride + (stride - 1 - low)
            pairs.append((sender, me))
        got.append(lax.ppermute(message, "gy", pairs))
    return got


class Group:
    def __init__(self, radix, stride, others, nx):
        self.radix, self.others, self.nx = radix, others, nx
        me = lax.axis_index("gy")
        self.at = lax.rem(lax.div(me, stride), radix)
        low = lax.rem(me, stride)
        self.lowest, self.highest = low == 0, low == stride - 1

    def map_of(self, place, own):
        rows = Rows(self.nx)
        out = own
        for (k, near), ref in zip(order(self.radix), self.others):
            here = source(self.at, k, self.radix) == place
            got = [ref[i * rows.span : (i + 1) * rows.span] for i in range(2)]
            out = got if out is None else [jnp.where(here, new, old) for new, old in zip(got, out)]
        return out

    def ahead(self, slope, offset):
        a, b = jnp.ones_like(slope), jnp.zeros_like(slope)
        for place in range(self.radix - 1):
            new_a, new_b = self.map_of(place, None)
            below = place < self.at
            a, b = jnp.where(below, new_a * a, a), jnp.where(below, new_a * b + new_b, b)
        return slope * a, slope * b + offset

    def total(self, own):
        a, b = self.map_of(0, own)
        for place in range(1, self.radix):
            new_a, new_b = self.map_of(place, own)
            a, b = new_a * a, new_a * b + new_b
        return a, b

    def collect(self, near, final):
        rows = Rows(self.nx)
        for (k, adjacent), ref in zip(order(self.radix), self.others):
            if not adjacent:
                continue
            place = source(self.at, k, self.radix)

            @pl.when(self.lowest & (place == self.at - 1))
            def _():
                near[rows.low : rows.low + rows.info] = ref[rows.map : rows.final]

            @pl.when(self.highest & (place == self.at + 1))
            def _():
                near[rows.high : rows.high + rows.info] = ref[rows.map : rows.final]
                rest = slice(0, rows.map) if final else slice(rows.final, rows.full)
                near[rows.high + rows.info : rows.near] = ref[rest]


def start_near(near, nx, nz):
    rows = Rows(nx)
    near[: rows.span] = jnp.ones((rows.span, nz), jnp.float32)
    near[rows.span :] = jnp.zeros((near.shape[0] - rows.span, nz), jnp.float32)


def join_kernel(radix, stride, final, nx, is_first, *refs):
    rows = Rows(nx)
    total, last_info, first_info, near_in = refs[:4]
    others, near, outs = refs[4 : 3 + radix], refs[3 + radix], refs[4 + radix :]
    nz = near.shape[1]
    if is_first:
        start_near(near, nx, nz)
    else:
        near[...] = near_in[...]
    group = Group(radix, stride, others, nx)
    own = [total[i * rows.span : (i + 1) * rows.span] for i in range(2)]
    ahead = group.ahead(near[: rows.span], near[rows.span : rows.map])
    write_rows(near, ahead)
    group.collect(near, False)
    whole = group.total(own)
    at = lax.div(lax.axis_index("gy"), stride * radix)
    if final == 0:
        write_rows(outs[0], whole)
        return
    at = lax.rem(at, final)
    for (k, adjacent), out in zip(order(final), outs):
        up = target(at, k, final) > at
        if not adjacent:
            write_rows(out, whole)
            continue

        @pl.when(up)
        def _():
            write_rows(out, whole)
            out[rows.map : rows.final] = last_info[: rows.info]

        @pl.when(jnp.logical_not(up))
        def _():
            out[: rows.map] = first_info[rows.info : rows.info + rows.rest]
            out[rows.map : rows.final] = first_info[: rows.info]


def full_message(nx, stride, radix, total, last_info, first_info, k):
    rows = Rows(nx)
    at = lax.axis_index("gy") // stride % radix
    onward = jnp.concatenate([total[: rows.map], last_info[: rows.info], first_info[rows.info : rows.info + rows.rest]])
    back = jnp.concatenate([total[: rows.map], first_info[: rows.info + rows.rest]])
    message = jnp.where(target(at, k, radix) > at, onward, back)
    return jnp.pad(message, ((0, -rows.full % 8), (0, 0)))


def third_kernel(radix, stride, *refs):
    st, extra, coarse, near_in = refs[:4]
    others, (out, sc, wide, near, done, sems) = refs[4 : 3 + radix], refs[3 + radix :]
    planes, rows, ext, nz = st.shape
    ny, nx = rows - 2, ext - 2 * PAD
    edge = edge_weights((ext, nz))
    blocks = ny // 2

    lay = Rows(nx)
    span = lay.span
    near[...] = near_in[...]
    group = Group(radix, stride, others, nx)
    if radix > 1:
        group.collect(near, True)
    gas_in = group.ahead(near[:span], near[span : lay.map])[1]
    at_high = lay.high + lay.info
    starts = [lay.low, lay.low + span, lay.high, lay.high + span, at_high, at_high + span]
    for k, v in enumerate([gas_in] + [near[start : start + span] for start in starts]):
        wide[k, : PAD - 2] = jnp.zeros((PAD - 2, nz), jnp.float32)
        wide[k, ext - PAD + 2 :] = jnp.zeros((PAD - 2, nz), jnp.float32)
        wide[k, pl.ds(PAD - 2, span, 2), :] = v
        wide[k, pl.ds(PAD - 1, span, 2), :] = v
    for k, start in enumerate((lay.low, lay.low + nx + 2, lay.high, lay.high + nx + 2)):
        start += lay.map
        wide[7 + k, :PAD] = jnp.zeros((PAD, nz), jnp.float32)
        wide[7 + k, ext - PAD :] = jnp.zeros((PAD, nz), jnp.float32)
        wide[7 + k, PAD - 1 : PAD + nx + 1] = near[start : start + nx + 2]

    gas_in = wide[0]
    last = ny + 1
    solid_low = wide[1] + wide[2] * gas_in
    sc[0, 0] = st[SA, 0] + solid_low
    sc[1, 0] = st[GA, 0] + gas_in

    def correct(j, carry):
        gas = coarse[2, j] * gas_in + coarse[3, j]
        solid = coarse[0, j] + coarse[1, j] * gas
        for i in (2 * j + 1, 2 * j + 2):
            sc[0, i] = st[SA, i] + solid
            sc[1, i] = st[GA, i] + gas
        return carry

    lax.fori_loop(0, blocks, correct, 0)
    gas = coarse[2, blocks - 1] * gas_in + coarse[3, blocks - 1]
    gas_high = wide[5] * gas + wide[4]
    solid_high = wide[3] + wide[6] * gas_high
    sc[0, last] = st[SA, last] + solid_high
    sc[1, last] = st[GA, last] + gas_high

    view = Fields(st, sc)
    for i, is_after, solid, gas in ((0, False, solid_low, gas_in), (last, True, solid_high, gas_high)):
        side = 3 if is_after else 0
        fy = extra[side + 2]
        to = 9 if is_after else 7
        rs = extra[side] + wide[to] + fy * solid
        rg = extra[side + 1] + wide[to + 1] + (CONDUCT if is_after else CONDUCT + FLOW) * gas
        res = outer_residual(view, i, SA, rs, rg, fy, edge, is_after)
        sc[2, i], sc[3, i] = relaxed(view, i, SA, *res)

    def sweep(k, carry):
        stores = []
        for r in range(GROUP):
            i = GROUP * k + 1 + r
            new_s, new_g = relaxed(view, i, SA, *row_residual(view, i, SA, edge))
            stores += [((2, i), new_s), ((3, i), new_g)]
        for at, value in stores:
            sc[at] = value
        return carry

    lax.fori_loop(0, ny // GROUP, sweep, 0)

    def leaving(k):
        part = pl.ds(GROUP * k, GROUP)
        return pltpu.make_async_copy(done.at[:, part], out.at[:, part], sems.at[k])

    def final(k, carry):
        stores = []
        for r in range(GROUP):
            i = GROUP * k + 1 + r
            new_s, new_g = last_relaxed(view, i, SB, edge, slice(PAD, PAD + nx))
            stores += [((0, i - 1), new_s), ((1, i - 1), new_g)]
        for at, value in stores:
            done[at] = value
        leaving(k).start()
        return carry

    lax.fori_loop(0, ny // GROUP, final, 0)
    for k in range(ny // GROUP):
        leaving(k).wait()


class Fields:
    def __init__(self, st, sc):
        self.st, self.sc = st, sc

    def __getitem__(self, at):
        return (self.sc if at[0] <= GB else self.st)[at]


def cost(rows, cells):
    return pl.CostEstimate(flops=50 * rows * cells, bytes_accessed=16 * 4 * rows * cells, transcendentals=0)


def swap(x, axis, first):
    pairs = []
    for i in range(first, lax.axis_size(axis) - 1, 2):
        pairs += [(i, i + 1), (i + 1, i)]
    return lax.ppermute(x, axis, pairs)


def shards(temps, right_side, exchange, coupling):
    temps, right_side = (jnp.transpose(a, (0, 2, 1, 3)) for a in (temps, right_side))
    exchange, coupling = (jnp.transpose(a, (1, 0, 2)) for a in (exchange, coupling))
    temps, right_side, exchange, coupling = (
        pltpu.with_memory_space_constraint(a, pltpu.HBM) for a in (temps, right_side, exchange, coupling)
    )
    ny, nx, nz = exchange.shape
    ext = nx + 2 * PAD
    f32 = functools.partial(jax.ShapeDtypeStruct, dtype=jnp.float32)

    strip = f32(((ny * STRIP_ROWS + 7) // 8 * 8, nz))
    scratch = [(2, 2, ny, 8, nz)] * 2 + [(2, ny, 8, nz)] * 2 + [(2, 2, nx, nz), (2, nx, nz), (2, nx, nz)]
    one, two, early = pl.pallas_call(
        pack_kernel,
        out_shape=(strip, strip, f32((EARLY, nx, nz))),
        in_specs=[HBM] * 4,
        out_specs=(VMEM,) * 3,
        scratch_shapes=[pltpu.VMEM(shape, jnp.float32) for shape in scratch] + [pltpu.SemaphoreType.DMA((11,))],
        compiler_params=PARAMS,
        name="pack_x",
    )(temps, right_side, exchange, coupling)
    one, two = swap(one, "gx", 0), swap(two, "gx", 1)
    early = swap(early, "gy", 1)

    state = f32((PLANES, ny + 2, ext, nz))

    def letter(planes):
        return f32((planes, ext - 2 * CROP, nz))

    st = pl.pallas_call(
        load_kernel,
        out_shape=state,
        in_specs=[HBM] * 4,
        out_specs=VMEM,
        scratch_shapes=[pltpu.SemaphoreType.DMA((6,))],
        compiler_params=PARAMS,
        cost_estimate=cost(2 * ny, ext * nz),
        name="load",
    )(temps, right_side, exchange, coupling)
    st, across = pl.pallas_call(
        first_kernel,
        out_shape=(state, letter(MESSAGE - EARLY + 1)),
        in_specs=[VMEM] * 4,
        out_specs=(VMEM,) * 2,
        input_output_aliases={0: 0},
        compiler_params=PARAMS,
        name="first",
    )(st, one, two, early)
    across = swap(across, "gy", 1)

    rows = f32((4, ny // 2, ext, nz))
    st, coarse, beside_a, beside_b = pl.pallas_call(
        inner_kernel,
        out_shape=(state, rows, letter(EARLY), letter(MESSAGE - EARLY)),
        in_specs=[VMEM] * 3,
        out_specs=(VMEM,) * 4,
        input_output_aliases={0: 0},
        compiler_params=PARAMS,
        cost_estimate=cost(4 * ny, ext * nz),
        name="inner",
    )(st, one, two)

    beside_a, beside_b = swap(beside_a, "gy", 0), swap(beside_b, "gy", 0)

    lay = Rows(nx)

    def tall(height):
        return f32(((height + 7) // 8 * 8, nz))

    letters = [pltpu.VMEM((MESSAGE, ext, nz), jnp.float32)] * 2
    st, coarse, extra, total, last_info, first_info, message = pl.pallas_call(
        second_kernel,
        out_shape=(
            state,
            rows,
            f32((6, ext, nz)),
            tall(lay.map),
            tall(lay.info),
            tall(lay.info + lay.rest),
            tall(lay.full),
        ),
        in_specs=[VMEM] * 6,
        out_specs=(VMEM,) * 7,
        scratch_shapes=letters + [pltpu.VMEM((8, ext, nz), jnp.float32)],
        input_output_aliases={0: 0, 1: 1},
        compiler_params=PARAMS,
        name="second",
    )(st, coarse, early, across, beside_a, beside_b)

    near, messages = total, [message]
    radices, stride = stages(lax.axis_size("gy")), 1
    for place, radix in enumerate(radices[:-1]):
        if place:
            messages = [full_message(nx, stride, radix, total, last_info, first_info, k) for k, _ in order(radix)]
        others = exchange_stage(messages, radix, stride)
        final = radices[-1] if place == len(radices) - 2 else 0
        outs = [tall(lay.final if adjacent else lay.map) for _, adjacent in order(final)] if final else [tall(lay.map)]
        near, *messages = pl.pallas_call(
            functools.partial(join_kernel, radix, stride, final, nx, place == 0),
            out_shape=(tall(lay.near), *outs),
            in_specs=[VMEM] * (3 + radix),
            out_specs=(VMEM,) * (1 + len(outs)),
            compiler_params=PARAMS,
            name="join",
        )(total, last_info, first_info, near, *others)
        total = total if final else messages[0]
        stride *= radix
    got = exchange_stage(messages, radices[-1], stride)

    out = pl.pallas_call(
        functools.partial(third_kernel, radices[-1], stride),
        out_shape=f32((2, ny, nx, nz)),
        in_specs=[VMEM] * (4 + len(got)),
        out_specs=HBM,
        scratch_shapes=[
            pltpu.VMEM((4, ny + 2, ext, nz), jnp.float32),
            pltpu.VMEM((11, ext, nz), jnp.float32),
            pltpu.VMEM(tall(lay.near).shape, jnp.float32),
            pltpu.VMEM((2, ny, nx, nz), jnp.float32),
            pltpu.SemaphoreType.DMA((ny // GROUP,)),
        ],
        compiler_params=PARAMS,
        name="third",
    )(st, extra, coarse, near, *got)
    return jnp.transpose(out, (0, 2, 1, 3))


def solution(mesh):
    return jax.shard_map(
        shards,
        mesh=mesh,
        in_specs=(
            P(None, "gx", "gy", None),
            P(None, "gx", "gy", None),
            P("gx", "gy", None),
            P("gx", "gy", None),
        ),
        out_specs=P(None, "gx", "gy", None),
        check_vma=False,
    )
```

```python
import functools

import jax
import jax.numpy as jnp
from jax import lax
from jax.experimental import pallas as pl
from jax.experimental.pallas import tpu as pltpu
from jax.sharding import PartitionSpec as P

SOLID_CAP, GAS_CAP, FLOW, CONDUCT, RELAX, LUMP = 0.5, 0.02, 40.0, 0.05, 0.8, 0.25
GAS_SELF = GAS_CAP + 4.5 * CONDUCT

PAD = 8
WX = 5
CROP = 4
(SA, GA, SB, GB, K, C, RS, RG, FX, FZ, H, FY, ASS, ASG, AGG) = range(15)
PLANES = 15
(M_S, M_G, M_K, M_C, M_FY, M_1S, M_1G, M_2S, M_2G) = range(9)
MESSAGE = 9

GROUP = 3

VMEM = pl.BlockSpec(memory_space=pltpu.VMEM)
HBM = pl.BlockSpec(memory_space=pltpu.HBM)
PARAMS = pltpu.CompilerParams(vmem_limit_bytes=40 * 1024 * 1024)


def up_x(v):
    return pltpu.roll(v, v.shape[0] - 1, 0)


def down_x(v):
    return pltpu.roll(v, 1, 0)


def up_z(v):
    return pltpu.roll(v, v.shape[1] - 1, 1)


def down_z(v):
    return pltpu.roll(v, 1, 1)


def lanes(shape):
    return lax.broadcasted_iota(jnp.int32, shape, 1)


def x_mask(shape, nx):
    row = lax.broadcasted_iota(jnp.int32, shape, 0)
    place, count = lax.axis_index("gx"), lax.axis_size("gx")
    low = jnp.where(place == 0, PAD, PAD - WX)
    high = jnp.where(place == count - 1, PAD + nx, PAD + nx + WX)
    return jnp.where((row >= low) & (row < high), 1.0, 0.0).astype(jnp.float32)


STRIP = ((SA, WX - 1), (GA, WX - 1), (K, WX), (RS, WX - 1), (RG, WX - 1), (C, WX - 1))
STRIP_ROWS = sum(width for plane, width in STRIP)


def conductivity_of(s, exchange):
    return 1.0 + 4.0 * exchange * s * s * s


def strip_values(s, g, k, rs, rg, c, low):
    out, inn = (WX - 1, WX - 2) if low else (8 - WX, 9 - WX)
    four = slice(0, WX - 1) if low else slice(9 - WX, 8)
    five = slice(0, WX) if low else slice(8 - WX, 8)
    row = lax.broadcasted_iota(jnp.int32, s.shape, 0)
    rs = rs + jnp.where(row == inn, 0.5 * (k[inn : inn + 1] + k[out : out + 1]) * s[out : out + 1], 0.0)
    rg = rg + jnp.where(row == inn, CONDUCT * g[out : out + 1], 0.0)
    return [s[four], g[four], k[five], rs[four], rg[four], c[four]]


def pack_kernel(temps, right, exchange, coupling, one, two, pair_low, pair_high, single_low, single_high, sems):
    even = lax.axis_index("gx") % 2 == 0
    ny, nx, nz = exchange.shape
    copies = []
    for k, ref in enumerate((temps, right, exchange, coupling)):
        low, high, at = (pair_low, pair_high, k) if k < 2 else (single_low, single_high, k - 2)
        lead = (slice(None),) * (ref.ndim - 2)
        copies.append(pltpu.make_async_copy(ref.at[lead + (slice(0, 8),)], low.at[at], sems.at[2 * k]))
        copies.append(pltpu.make_async_copy(ref.at[lead + (slice(nx - 8, nx),)], high.at[at], sems.at[2 * k + 1]))
    for copy in copies:
        copy.start()
    for copy in copies:
        copy.wait()
    at = 0
    for y in range(ny):
        sides = []
        for pair, single, is_low in ((pair_low, single_low, True), (pair_high, single_high, False)):
            s, g, rs, rg = (pair[i, j, y] for i in range(2) for j in range(2))
            sides.append(strip_values(s, g, conductivity_of(s, single[0, y]), rs, rg, single[1, y], is_low))
        for low, high, (plane, width) in zip(*sides, STRIP):
            one[at : at + width] = jnp.where(even, high, low)
            two[at : at + width] = jnp.where(even, low, high)
            at += width
    two[one.shape[0] :] = jnp.zeros((8, nz), jnp.float32)


def load_kernel(temps, right, exchange, coupling, st, sems):
    ny, nx, nz = exchange.shape
    planes, rows, ext, nz = st.shape
    copies = []
    for k, (plane, ref) in enumerate(
        ((SA, temps.at[0]), (K, exchange), (GA, temps.at[1]), (RS, right.at[0]), (RG, right.at[1]), (C, coupling))
    ):
        to = st.at[plane, pl.ds(1, ny), pl.ds(PAD, nx)]
        copies.append(pltpu.make_async_copy(ref, to, sems.at[k]))
    for copy in copies:
        copy.start()
    zeros = jnp.zeros((PAD, nz), jnp.float32)

    def clear(i, carry):
        for plane, width in STRIP:
            st[plane, i, :PAD] = zeros
            st[plane, i, PAD + nx :] = zeros
        return carry

    lax.fori_loop(1, ny + 1, clear, 0)
    for copy in copies:
        copy.wait()

    def conduct(i, carry):
        s = st[SA, i, PAD : PAD + nx]
        st[K, i, PAD : PAD + nx] = conductivity_of(s, st[K, i, PAD : PAD + nx])
        return carry

    lax.fori_loop(1, ny + 1, conduct, 0)


def place_halo(st, one, two, y, nx):
    even = lax.axis_index("gx") % 2 == 0
    at, i = y * STRIP_ROWS, y + 1
    for plane, width in STRIP:
        a, b = one[at : at + width], two[at : at + width]
        st[plane, i, PAD - width : PAD] = jnp.where(even, b, a)
        st[plane, i, PAD + nx : PAD + nx + width] = jnp.where(even, a, b)
        at += width


def inner(s, g, c, h, fx, fz, edge):
    t = c * (s - g)
    flux_x = fx * (up_x(s) - s)
    flux_z = fz * (up_z(s) - s)
    part_s = (flux_x - down_x(flux_x)) + (flux_z - down_z(flux_z)) - h * s - t
    part_g = (
        t
        - GAS_SELF * g
        + CONDUCT * (up_x(g) + down_x(g))
        + edge[0] * up_z(g)
        + edge[1] * down_z(g)
    )
    return part_s, part_g


def edge_weights(shape):
    lane = lanes(shape)
    weight = jnp.float32(0.25 * CONDUCT)
    return jnp.where(lane == shape[1] - 1, 0.0, weight), jnp.where(lane == 0, 0.0, weight)


def row_inner(st, i, s_at, edge):
    return inner(st[s_at, i], st[s_at + 1, i], st[C, i], st[H, i], st[FX, i], st[FZ, i], edge)


def row_residual(st, i, s_at, edge):
    part_s, part_g = row_inner(st, i, s_at, edge)
    s, g, before = st[s_at, i], st[s_at + 1, i], st[s_at + 1, i - 1]
    part_s += st[FY, i] * (st[s_at, i + 1] - s) + st[FY, i - 1] * (st[s_at, i - 1] - s)
    part_g += CONDUCT * (st[s_at + 1, i + 1] + before) - FLOW * (g - before)
    return st[RS, i] + part_s, st[RG, i] + part_g


def relaxed(st, i, s_at, res_s, res_g):
    s = st[s_at, i] + st[ASS, i] * res_s + st[ASG, i] * res_g
    g = st[s_at + 1, i] + st[ASG, i] * res_s + st[AGG, i] * res_g
    return s, g


def faces(k):
    lane = lanes(k.shape)
    end = k.shape[1] - 1
    fx = 0.5 * (k + up_x(k))
    fz = jnp.where(lane == end, 0.0, 0.125 * (k + up_z(k)))
    h = SOLID_CAP + jnp.where((lane == 0) | (lane == end), 0.125 * k, 0.0)
    return fx, fz, h, h + (fx + down_x(fx)) + (fz + down_z(fz))


def inverse(diag, c, mask):
    gas_diag = (GAS_SELF + FLOW) + c
    inv = (RELAX * mask) / (diag * gas_diag - c * c)
    return inv * gas_diag, inv * c, inv * diag


def last_relaxed(st, i, s_at, edge, own):
    full_s, full_g = st[s_at, i], st[s_at + 1, i]
    s, g = full_s[own], full_g[own]
    flux_x = st[FX, i] * (up_x(full_s) - full_s)
    flux_z = st[FZ, i, own] * (up_z(s) - s)
    c, before = st[C, i, own], st[s_at + 1, i - 1, own]
    t = c * (s - g)
    res_s = st[RS, i, own] + (flux_x[own] - down_x(flux_x)[own]) + (flux_z - down_z(flux_z)) - st[H, i, own] * s - t
    res_s += st[FY, i, own] * (st[s_at, i + 1, own] - s) + st[FY, i - 1, own] * (st[s_at, i - 1, own] - s)
    res_g = st[RG, i, own] + t - GAS_SELF * g + edge[0][own] * up_z(g) + edge[1][own] * down_z(g)
    res_g += CONDUCT * (up_x(full_g)[own] + down_x(full_g)[own] + st[s_at + 1, i + 1, own] + before) - FLOW * (g - before)
    ss, sg, gg = st[ASS, i, own], st[ASG, i, own], st[AGG, i, own]
    return s + ss * res_s + sg * res_g, g + sg * res_s + gg * res_g


def grouped(rows, work):
    for start in range(0, len(rows), GROUP):
        stores = []
        for i in rows[start : start + GROUP]:
            stores += work(i)
        for ref, at, value in stores:
            ref[at] = value


def row_coefficients(st, i, mask):
    fx, fz, h, diag = faces(st[K, i])
    fy = 0.5 * (st[K, i] + st[K, i + 1])
    before = 0.5 * (st[K, i] + st[K, i - 1])
    ss, sg, gg = inverse(diag + st[C, i] + fy + before, st[C, i], mask)
    values = ((FX, fx), (FZ, fz), (H, h), (FY, fy), (ASS, ss), (ASG, sg), (AGG, gg))
    return [(st, (plane, i), v) for plane, v in values]


def row_sweep(st, i, source, target, edge):
    s, g = relaxed(st, i, source, *row_residual(st, i, source, edge))
    return [(st, (target, i), s), (st, (target + 1, i), g)]


def send_planes(st, onward, edge):
    ny = st.shape[1] - 2
    e, d, near = (ny, ny - 1, ny - 1) if onward else (1, 2, 1)
    fy, s, g, g_d = st[FY, near], st[SA, e], st[GA, e], st[GA, d]
    part_s, part_g = row_inner(st, e, SA, edge)
    m_1s = st[RS, e] + part_s + fy * (st[SA, d] - s)
    m_1g = st[RG, e] + part_g + CONDUCT * g_d - FLOW * (g - g_d if onward else g)
    m_2s = st[RS, e] + fy * st[SB, d]
    m_2g = st[RG, e] + (CONDUCT + FLOW if onward else CONDUCT) * st[GB, d]
    return [s, g, st[K, e], st[C, e], fy, m_1s, m_1g, m_2s, m_2g]


def write_message(ref, st, onward, edge):
    ext = st.shape[2]
    for go in (True, False):

        @pl.when(onward == go)
        def _():
            for k, value in enumerate(send_planes(st, go, edge)):
                ref[k] = value[CROP : ext - CROP]


def first_kernel(st_in, one, two, st, across):
    del st_in
    planes, rows, ext, nz = st.shape
    ny, nx = rows - 2, ext - 2 * PAD
    shape = (ext, nz)
    mask = x_mask(shape, nx)
    edge = edge_weights(shape)

    for y in list(range(4)) + list(range(ny - 4, ny)):
        place_halo(st, one, two, y, nx)
    for i in (1, ny):
        fx, fz, h, diag = faces(st[K, i])
        st[FX, i], st[FZ, i], st[H, i] = fx, fz, h
    st[FY, 1] = 0.5 * (st[K, 1] + st[K, 2])
    st[FY, ny - 3] = 0.5 * (st[K, ny - 3] + st[K, ny - 2])
    ends = [2, 3, ny - 2, ny - 1]
    grouped(ends, lambda i: row_coefficients(st, i, mask))
    grouped(ends, lambda i: row_sweep(st, i, SA, SB, edge))
    write_message(across, st, lax.axis_index("gy") % 2 == 1, edge)


def outer_residual(st, i, s_at, rs, rg, fy_out, edge, after):
    part_s, part_g = row_inner(st, i, s_at, edge)
    s, g = st[s_at, i], st[s_at + 1, i]
    if after:
        part_s += st[FY, i - 1] * (st[s_at, i - 1] - s)
        part_g += (CONDUCT + FLOW) * st[s_at + 1, i - 1]
    else:
        part_s += st[FY, i] * (st[s_at, i + 1] - s)
        part_g += CONDUCT * st[s_at + 1, i + 1]
    return rs + part_s - fy_out * s, rg + part_g - FLOW * g


def pair_x(v):
    row = lax.broadcasted_iota(jnp.int32, v.shape, 0)
    return v + jnp.where(row % 2 == 0, up_x(v), down_x(v))


def coarse_coefficients(c_sum, k_sum):
    solid = 4.0 * SOLID_CAP + c_sum + LUMP * k_sum
    ratio = c_sum / solid
    denominator = (4.0 * GAS_CAP + 2.0 * FLOW) + c_sum - c_sum * ratio
    return solid, ratio, denominator


def coarse_row(st, coarse, j, mask, edge):
    i = 2 * j + 1
    res_s, res_g = row_residual(st, i, SA, edge)
    more_s, more_g = row_residual(st, i + 1, SA, edge)
    res_s, res_g = pair_x((res_s + more_s) * mask), pair_x((res_g + more_g) * mask)
    c_sum = pair_x(st[C, i] + st[C, i + 1])
    solid, ratio, denominator = coarse_coefficients(c_sum, pair_x(st[K, i] + st[K, i + 1]))
    lead = res_s / solid
    values = (lead, ratio, (2.0 * FLOW) / denominator, (res_g + c_sum * lead) / denominator)
    return [(coarse, (k, j), v) for k, v in enumerate(values)]


def inner_kernel(st_in, one, two, st, coarse, beside):
    del st_in
    planes, rows, ext, nz = st.shape
    ny, nx = rows - 2, ext - 2 * PAD
    shape = (ext, nz)
    mask = x_mask(shape, nx)
    edge = edge_weights(shape)
    for y in range(4, ny - 4):
        place_halo(st, one, two, y, nx)
    grouped(list(range(4, ny - 2)), lambda i: row_coefficients(st, i, mask))
    grouped(list(range(4, ny - 2)), lambda i: row_sweep(st, i, SA, SB, edge))
    grouped(list(range(3, ny - 1)), lambda i: row_sweep(st, i, SB, SA, edge))
    for j in range(2, ny // 2 - 2):
        for ref, at, value in coarse_row(st, coarse, j, mask, edge):
            ref[at] = value
    write_message(beside, st, lax.axis_index("gy") % 2 == 0, edge)


def unpack(across, beside, before, after):
    even = lax.axis_index("gy") % 2 == 0
    ext, nz = before.shape[1:]
    zeros = jnp.zeros((PAD, nz), jnp.float32)
    for is_even, far, near in ((True, before, after), (False, after, before)):

        @pl.when(even == is_even)
        def _():
            for k in range(MESSAGE):
                for ref, got in ((far, across), (near, beside)):
                    ref[k, :PAD] = zeros
                    ref[k, ext - PAD :] = zeros
                    ref[k, CROP : ext - CROP] = got[k]


def second_kernel(st_in, coarse_in, across, beside, st, coarse, extra, total, last_info, first_info, message, before, after, squeeze):
    del st_in, coarse_in
    planes, rows, ext, nz = st.shape
    ny, nx = rows - 2, ext - 2 * PAD
    shape = (ext, nz)
    me, count = lax.axis_index("gy"), lax.axis_size("gy")
    mask = x_mask(shape, nx)
    low = jnp.where(me == 0, 0.0, mask)
    high = jnp.where(me == count - 1, 0.0, mask)
    edge = edge_weights(shape)
    unpack(across, beside, before, after)

    last = ny + 1
    ends = ((0, before, low), (last, after, high))
    for i, ref, inside in ends:
        st[SA, i], st[GA, i], st[K, i], st[C, i] = ref[M_S], ref[M_G], ref[M_K], ref[M_C]
    st[FY, 0] = 0.5 * (st[K, 0] + st[K, 1])
    st[FY, ny] = 0.5 * (st[K, ny] + st[K, last])
    for i in (1, ny):
        fx, fz = st[FX, i], st[FZ, i]
        diag = st[H, i] + (fx + down_x(fx)) + (fz + down_z(fz)) + st[C, i] + st[FY, i - 1] + st[FY, i]
        st[ASS, i], st[ASG, i], st[AGG, i] = inverse(diag, st[C, i], mask)
    for i, ref, inside in ends:
        fx, fz, h, diag = faces(st[K, i])
        st[FX, i], st[FZ, i], st[H, i] = fx, fz, h
        diag += st[C, i] + ref[M_FY] + st[FY, min(i, ny)]
        st[ASS, i], st[ASG, i], st[AGG, i] = inverse(diag, st[C, i], inside)

    res = before[M_1S] + st[FY, 0] * (st[SA, 1] - st[SA, 0]), before[M_1G] + CONDUCT * st[GA, 1]
    new_low = relaxed(st, 0, SA, *res)
    res = after[M_1S] + st[FY, ny] * (st[SA, ny] - st[SA, last]), after[M_1G] + (CONDUCT + FLOW) * st[GA, ny]
    new_high = relaxed(st, last, SA, *res)
    stores = row_sweep(st, 1, SA, SB, edge) + row_sweep(st, ny, SA, SB, edge)
    st[SB, 0], st[GB, 0] = new_low
    st[SB, last], st[GB, last] = new_high
    for ref, at, value in stores:
        ref[at] = value

    for i, ref, inside in ends:
        is_after = i > 0
        res = outer_residual(st, i, SB, ref[M_2S], ref[M_2G], ref[M_FY], edge, is_after)
        st[SA, i], st[GA, i] = relaxed(st, i, SB, *res)
    grouped([1, 2, ny - 1, ny], lambda i: row_sweep(st, i, SB, SA, edge))

    for i, ref, inside in ends:
        for k, plane in enumerate((M_2S, M_2G, M_FY)):
            extra[(3 if i else 0) + k] = ref[plane]

    blocks = ny // 2
    for j in (0, 1, blocks - 2, blocks - 1):
        for ref, at, value in coarse_row(st, coarse, j, mask, edge):
            ref[at] = value
    for k in range(4):
        squeeze[k] = coarse[k, 0]
    slopes, offsets = coarse[2, 0], coarse[3, 0]
    for j in range(1, blocks):
        slope = coarse[2, j]
        slopes, offsets = slope * slopes, slope * offsets + coarse[3, j]
        coarse[2, j], coarse[3, j] = slopes, offsets
    squeeze[4], squeeze[5], squeeze[6], squeeze[7] = slopes, offsets, coarse[0, blocks - 1], coarse[1, blocks - 1]

    span = nx // 2 + 2
    lead, ratio, slope, offset, slopes, offsets, lead_last, ratio_last = (
        squeeze[k, pl.ds(PAD - 2, span, 2), :] for k in range(8)
    )
    part = slice(PAD - 1, PAD + nx + 1)

    def increments(d, face, gas):
        return [(st[FY, face] * (st[SA, d] - st[SB, d]))[part], (gas * (st[GA, d] - st[GB, d]))[part]]

    onward = [lead_last, ratio_last] + increments(ny - 1, ny - 1, CONDUCT + FLOW)
    back = [lead, offset] + increments(2, 1, CONDUCT) + [slope, ratio]
    write_rows(total, [slopes, offsets])
    write_rows(last_info, onward)
    write_rows(first_info, back)
    for go, info in ((True, onward), (False, back)):

        @pl.when((me % 2 == 0) == go)
        def _():
            write_rows(message, [slopes, offsets] + info)


def write_rows(ref, values):
    at = 0
    for value in values:
        ref[at : at + value.shape[0]] = value
        at += value.shape[0]


class Rows:
    def __init__(self, nx):
        self.span = nx // 2 + 2
        self.map = 2 * self.span
        self.info = self.map + 2 * (nx + 2)
        self.rest = self.map
        self.final = self.map + self.info
        self.full = self.final + self.rest
        self.low = self.map
        self.high = self.low + self.info
        self.near = self.high + self.info + self.rest


def source(at, k, radix):
    if radix & (radix - 1) == 0:
        return at ^ k
    return (at + radix - k) % radix


def target(at, k, radix):
    return at ^ k if radix & (radix - 1) == 0 else (at + k) % radix


def order(radix):
    out = [(k, any(abs(source(at, k, radix) - at) == 1 for at in range(radix))) for k in range(1, radix)]
    return sorted(out, key=lambda item: (not item[1], -item[0]))


def stages(count):
    if count % 2:
        return [1, count]
    out, rest = [2], count // 2
    while rest > 1:
        radix = next((r for r in (8, 4, 2) if rest % r == 0), rest)
        out.append(radix)
        rest //= radix
    return out if len(out) > 1 else out + [1]


def exchange_stage(messages, radix, stride):
    count, got = lax.axis_size("gy"), []
    for (k, near), message in zip(order(radix), messages):
        pairs = []
        for me in range(count):
            at, low = me // stride % radix, me % stride
            sender = me - low + (source(at, k, radix) - at) * stride + (stride - 1 - low)
            pairs.append((sender, me))
        got.append(lax.ppermute(message, "gy", pairs))
    return got


class Group:
    def __init__(self, radix, stride, others, nx):
        self.radix, self.others, self.nx = radix, others, nx
        me = lax.axis_index("gy")
        self.at = lax.rem(lax.div(me, stride), radix)
        low = lax.rem(me, stride)
        self.lowest, self.highest = low == 0, low == stride - 1

    def map_of(self, place, own):
        rows = Rows(self.nx)
        out = own
        for (k, near), ref in zip(order(self.radix), self.others):
            here = source(self.at, k, self.radix) == place
            got = [ref[i * rows.span : (i + 1) * rows.span] for i in range(2)]
            out = got if out is None else [jnp.where(here, new, old) for new, old in zip(got, out)]
        return out

    def ahead(self, slope, offset):
        a, b = jnp.ones_like(slope), jnp.zeros_like(slope)
        for place in range(self.radix - 1):
            new_a, new_b = self.map_of(place, None)
            below = place < self.at
            a, b = jnp.where(below, new_a * a, a), jnp.where(below, new_a * b + new_b, b)
        return slope * a, slope * b + offset

    def total(self, own):
        a, b = self.map_of(0, own)
        for place in range(1, self.radix):
            new_a, new_b = self.map_of(place, own)
            a, b = new_a * a, new_a * b + new_b
        return a, b

    def collect(self, near, final):
        rows = Rows(self.nx)
        for (k, adjacent), ref in zip(order(self.radix), self.others):
            if not adjacent:
                continue
            place = source(self.at, k, self.radix)

            @pl.when(self.lowest & (place == self.at - 1))
            def _():
                near[rows.low : rows.low + rows.info] = ref[rows.map : rows.final]

            @pl.when(self.highest & (place == self.at + 1))
            def _():
                near[rows.high : rows.high + rows.info] = ref[rows.map : rows.final]
                rest = slice(0, rows.map) if final else slice(rows.final, rows.full)
                near[rows.high + rows.info : rows.near] = ref[rest]


def start_near(near, nx, nz):
    rows = Rows(nx)
    near[: rows.span] = jnp.ones((rows.span, nz), jnp.float32)
    near[rows.span :] = jnp.zeros((near.shape[0] - rows.span, nz), jnp.float32)


def join_kernel(radix, stride, final, nx, is_first, *refs):
    rows = Rows(nx)
    total, last_info, first_info, near_in = refs[:4]
    others, near, outs = refs[4 : 3 + radix], refs[3 + radix], refs[4 + radix :]
    nz = near.shape[1]
    if is_first:
        start_near(near, nx, nz)
    else:
        near[...] = near_in[...]
    group = Group(radix, stride, others, nx)
    own = [total[i * rows.span : (i + 1) * rows.span] for i in range(2)]
    ahead = group.ahead(near[: rows.span], near[rows.span : rows.map])
    write_rows(near, ahead)
    group.collect(near, False)
    whole = group.total(own)
    at = lax.div(lax.axis_index("gy"), stride * radix)
    if final == 0:
        write_rows(outs[0], whole)
        return
    at = lax.rem(at, final)
    for (k, adjacent), out in zip(order(final), outs):
        up = target(at, k, final) > at
        if not adjacent:
            write_rows(out, whole)
            continue

        @pl.when(up)
        def _():
            write_rows(out, whole)
            out[rows.map : rows.final] = last_info[: rows.info]

        @pl.when(jnp.logical_not(up))
        def _():
            out[: rows.map] = first_info[rows.info : rows.info + rows.rest]
            out[rows.map : rows.final] = first_info[: rows.info]


def full_message(nx, stride, radix, total, last_info, first_info, k):
    rows = Rows(nx)
    at = lax.axis_index("gy") // stride % radix
    onward = jnp.concatenate([total[: rows.map], last_info[: rows.info], first_info[rows.info : rows.info + rows.rest]])
    back = jnp.concatenate([total[: rows.map], first_info[: rows.info + rows.rest]])
    message = jnp.where(target(at, k, radix) > at, onward, back)
    return jnp.pad(message, ((0, -rows.full % 8), (0, 0)))


def third_kernel(radix, stride, *refs):
    st, extra, coarse, near_in = refs[:4]
    others, (out, sc, wide, near, done, sems) = refs[4 : 3 + radix], refs[3 + radix :]
    planes, rows, ext, nz = st.shape
    ny, nx = rows - 2, ext - 2 * PAD
    edge = edge_weights((ext, nz))
    blocks = ny // 2

    lay = Rows(nx)
    span = lay.span
    near[...] = near_in[...]
    group = Group(radix, stride, others, nx)
    if radix > 1:
        group.collect(near, True)
    gas_in = group.ahead(near[:span], near[span : lay.map])[1]
    at_high = lay.high + lay.info
    starts = [lay.low, lay.low + span, lay.high, lay.high + span, at_high, at_high + span]
    for k, v in enumerate([gas_in] + [near[start : start + span] for start in starts]):
        wide[k, : PAD - 2] = jnp.zeros((PAD - 2, nz), jnp.float32)
        wide[k, ext - PAD + 2 :] = jnp.zeros((PAD - 2, nz), jnp.float32)
        wide[k, pl.ds(PAD - 2, span, 2), :] = v
        wide[k, pl.ds(PAD - 1, span, 2), :] = v
    for k, start in enumerate((lay.low, lay.low + nx + 2, lay.high, lay.high + nx + 2)):
        start += lay.map
        wide[7 + k, :PAD] = jnp.zeros((PAD, nz), jnp.float32)
        wide[7 + k, ext - PAD :] = jnp.zeros((PAD, nz), jnp.float32)
        wide[7 + k, PAD - 1 : PAD + nx + 1] = near[start : start + nx + 2]

    gas_in = wide[0]
    last = ny + 1
    solid_low = wide[1] + wide[2] * gas_in
    sc[0, 0] = st[SA, 0] + solid_low
    sc[1, 0] = st[GA, 0] + gas_in

    def correct(j, carry):
        gas = coarse[2, j] * gas_in + coarse[3, j]
        solid = coarse[0, j] + coarse[1, j] * gas
        for i in (2 * j + 1, 2 * j + 2):
            sc[0, i] = st[SA, i] + solid
            sc[1, i] = st[GA, i] + gas
        return carry

    lax.fori_loop(0, blocks, correct, 0)
    gas = coarse[2, blocks - 1] * gas_in + coarse[3, blocks - 1]
    gas_high = wide[5] * gas + wide[4]
    solid_high = wide[3] + wide[6] * gas_high
    sc[0, last] = st[SA, last] + solid_high
    sc[1, last] = st[GA, last] + gas_high

    view = Fields(st, sc)
    for i, is_after, solid, gas in ((0, False, solid_low, gas_in), (last, True, solid_high, gas_high)):
        side = 3 if is_after else 0
        fy = extra[side + 2]
        to = 9 if is_after else 7
        rs = extra[side] + wide[to] + fy * solid
        rg = extra[side + 1] + wide[to + 1] + (CONDUCT if is_after else CONDUCT + FLOW) * gas
        res = outer_residual(view, i, SA, rs, rg, fy, edge, is_after)
        sc[2, i], sc[3, i] = relaxed(view, i, SA, *res)

    def sweep(k, carry):
        stores = []
        for r in range(GROUP):
            i = GROUP * k + 1 + r
            new_s, new_g = relaxed(view, i, SA, *row_residual(view, i, SA, edge))
            stores += [((2, i), new_s), ((3, i), new_g)]
        for at, value in stores:
            sc[at] = value
        return carry

    lax.fori_loop(0, ny // GROUP, sweep, 0)

    def leaving(k):
        part = pl.ds(GROUP * k, GROUP)
        return pltpu.make_async_copy(done.at[:, part], out.at[:, part], sems.at[k])

    def final(k, carry):
        stores = []
        for r in range(GROUP):
            i = GROUP * k + 1 + r
            new_s, new_g = last_relaxed(view, i, SB, edge, slice(PAD, PAD + nx))
            stores += [((0, i - 1), new_s), ((1, i - 1), new_g)]
        for at, value in stores:
            done[at] = value
        leaving(k).start()
        return carry

    lax.fori_loop(0, ny // GROUP, final, 0)
    for k in range(ny // GROUP):
        leaving(k).wait()


class Fields:
    def __init__(self, st, sc):
        self.st, self.sc = st, sc

    def __getitem__(self, at):
        return (self.sc if at[0] <= GB else self.st)[at]


def cost(rows, cells):
    return pl.CostEstimate(flops=50 * rows * cells, bytes_accessed=16 * 4 * rows * cells, transcendentals=0)


def swap(x, axis, first):
    pairs = []
    for i in range(first, lax.axis_size(axis) - 1, 2):
        pairs += [(i, i + 1), (i + 1, i)]
    return lax.ppermute(x, axis, pairs)


def shards(temps, right_side, exchange, coupling):
    temps, right_side = (jnp.transpose(a, (0, 2, 1, 3)) for a in (temps, right_side))
    exchange, coupling = (jnp.transpose(a, (1, 0, 2)) for a in (exchange, coupling))
    temps, right_side, exchange, coupling = (
        pltpu.with_memory_space_constraint(a, pltpu.HBM) for a in (temps, right_side, exchange, coupling)
    )
    ny, nx, nz = exchange.shape
    ext = nx + 2 * PAD
    f32 = functools.partial(jax.ShapeDtypeStruct, dtype=jnp.float32)

    height = (ny * STRIP_ROWS + 7) // 8 * 8
    strips = f32((height, nz)), f32((height + 8, nz))
    scratch = [(2, 2, ny, 8, nz)] * 2 + [(2, ny, 8, nz)] * 2
    one, two = pl.pallas_call(
        pack_kernel,
        out_shape=strips,
        in_specs=[HBM] * 4,
        out_specs=(VMEM,) * 2,
        scratch_shapes=[pltpu.VMEM(shape, jnp.float32) for shape in scratch] + [pltpu.SemaphoreType.DMA((8,))],
        compiler_params=PARAMS,
        name="pack_x",
    )(temps, right_side, exchange, coupling)
    two = swap(two, "gx", 1)
    one = swap(one, "gx", 0)

    state = f32((PLANES, ny + 2, ext, nz))

    def letter(planes):
        return f32((planes, ext - 2 * CROP, nz))

    st = pl.pallas_call(
        load_kernel,
        out_shape=state,
        in_specs=[HBM] * 4,
        out_specs=VMEM,
        scratch_shapes=[pltpu.SemaphoreType.DMA((6,))],
        compiler_params=PARAMS,
        cost_estimate=cost(2 * ny, ext * nz),
        name="load",
    )(temps, right_side, exchange, coupling)
    st, across = pl.pallas_call(
        first_kernel,
        out_shape=(state, letter(MESSAGE)),
        in_specs=[VMEM] * 3,
        out_specs=(VMEM,) * 2,
        input_output_aliases={0: 0},
        compiler_params=PARAMS,
        name="first",
    )(st, one, two)
    across = swap(across, "gy", 1)

    rows = f32((4, ny // 2, ext, nz))
    st, coarse, beside = pl.pallas_call(
        inner_kernel,
        out_shape=(state, rows, letter(MESSAGE)),
        in_specs=[VMEM] * 3,
        out_specs=(VMEM,) * 3,
        input_output_aliases={0: 0},
        compiler_params=PARAMS,
        cost_estimate=cost(4 * ny, ext * nz),
        name="inner",
    )(st, one, two)

    beside = swap(beside, "gy", 0)

    lay = Rows(nx)

    def tall(height):
        return f32(((height + 7) // 8 * 8, nz))

    letters = [pltpu.VMEM((MESSAGE, ext, nz), jnp.float32)] * 2
    st, coarse, extra, total, last_info, first_info, message = pl.pallas_call(
        second_kernel,
        out_shape=(
            state,
            rows,
            f32((6, ext, nz)),
            tall(lay.map),
            tall(lay.info),
            tall(lay.info + lay.rest),
            tall(lay.full),
        ),
        in_specs=[VMEM] * 4,
        out_specs=(VMEM,) * 7,
        scratch_shapes=letters + [pltpu.VMEM((8, ext, nz), jnp.float32)],
        input_output_aliases={0: 0, 1: 1},
        compiler_params=PARAMS,
        name="second",
    )(st, coarse, across, beside)

    near, messages = total, [message]
    radices, stride = stages(lax.axis_size("gy")), 1
    for place, radix in enumerate(radices[:-1]):
        if place:
            messages = [full_message(nx, stride, radix, total, last_info, first_info, k) for k, _ in order(radix)]
        others = exchange_stage(messages, radix, stride)
        final = radices[-1] if place == len(radices) - 2 else 0
        outs = [tall(lay.final if adjacent else lay.map) for _, adjacent in order(final)] if final else [tall(lay.map)]
        near, *messages = pl.pallas_call(
            functools.partial(join_kernel, radix, stride, final, nx, place == 0),
            out_shape=(tall(lay.near), *outs),
            in_specs=[VMEM] * (3 + radix),
            out_specs=(VMEM,) * (1 + len(outs)),
            compiler_params=PARAMS,
            name="join",
        )(total, last_info, first_info, near, *others)
        total = total if final else messages[0]
        stride *= radix
    got = exchange_stage(messages, radices[-1], stride)

    out = pl.pallas_call(
        functools.partial(third_kernel, radices[-1], stride),
        out_shape=f32((2, ny, nx, nz)),
        in_specs=[VMEM] * (4 + len(got)),
        out_specs=HBM,
        scratch_shapes=[
            pltpu.VMEM((4, ny + 2, ext, nz), jnp.float32),
            pltpu.VMEM((11, ext, nz), jnp.float32),
            pltpu.VMEM(tall(lay.near).shape, jnp.float32),
            pltpu.VMEM((2, ny, nx, nz), jnp.float32),
            pltpu.SemaphoreType.DMA((ny // GROUP,)),
        ],
        compiler_params=PARAMS,
        name="third",
    )(st, extra, coarse, near, *got)
    return jnp.transpose(out, (0, 2, 1, 3))


def solution(mesh):
    return jax.shard_map(
        shards,
        mesh=mesh,
        in_specs=(
            P(None, "gx", "gy", None),
            P(None, "gx", "gy", None),
            P("gx", "gy", None),
            P("gx", "gy", None),
        ),
        out_specs=P(None, "gx", "gy", None),
        check_vma=False,
    )
```

```python
import functools

import jax
import jax.numpy as jnp
from jax import lax
from jax.experimental import pallas as pl
from jax.experimental.pallas import tpu as pltpu
from jax.sharding import PartitionSpec as P

SOLID_CAP, GAS_CAP, FLOW, CONDUCT, RELAX, LUMP = 0.5, 0.02, 40.0, 0.05, 0.8, 0.25
GAS_SELF = GAS_CAP + 4.5 * CONDUCT

PAD = 8
WX = 5
CROP = 4
(SA, GA, SB, GB, K, C, RS, RG, FX, FZ, H, FY, ASS, ASG, AGG) = range(15)
PLANES = 15
(M_S, M_G, M_K, M_C, M_FY, M_1S, M_1G, M_2S, M_2G) = range(9)
MESSAGE, HALF = 9, 5

GROUP = 3

VMEM = pl.BlockSpec(memory_space=pltpu.VMEM)
HBM = pl.BlockSpec(memory_space=pltpu.HBM)
PARAMS = pltpu.CompilerParams(vmem_limit_bytes=40 * 1024 * 1024)


def up_x(v):
    return pltpu.roll(v, v.shape[0] - 1, 0)


def down_x(v):
    return pltpu.roll(v, 1, 0)


def up_z(v):
    return pltpu.roll(v, v.shape[1] - 1, 1)


def down_z(v):
    return pltpu.roll(v, 1, 1)


def lanes(shape):
    return lax.broadcasted_iota(jnp.int32, shape, 1)


def x_mask(shape, nx):
    row = lax.broadcasted_iota(jnp.int32, shape, 0)
    place, count = lax.axis_index("gx"), lax.axis_size("gx")
    low = jnp.where(place == 0, PAD, PAD - WX)
    high = jnp.where(place == count - 1, PAD + nx, PAD + nx + WX)
    return jnp.where((row >= low) & (row < high), 1.0, 0.0).astype(jnp.float32)


STRIP = ((SA, WX - 1), (GA, WX - 1), (K, WX), (RS, WX - 1), (RG, WX - 1), (C, WX - 1))
STRIP_ROWS = sum(width for plane, width in STRIP)


def conductivity_of(s, exchange):
    return 1.0 + 4.0 * exchange * s * s * s


def strip_values(s, g, k, rs, rg, c, low):
    out, inn = (WX - 1, WX - 2) if low else (8 - WX, 9 - WX)
    four = slice(0, WX - 1) if low else slice(9 - WX, 8)
    five = slice(0, WX) if low else slice(8 - WX, 8)
    row = lax.broadcasted_iota(jnp.int32, s.shape, 0)
    rs = rs + jnp.where(row == inn, 0.5 * (k[inn : inn + 1] + k[out : out + 1]) * s[out : out + 1], 0.0)
    rg = rg + jnp.where(row == inn, CONDUCT * g[out : out + 1], 0.0)
    return [s[four], g[four], k[five], rs[four], rg[four], c[four]]


def pack_kernel(temps, right, exchange, coupling, one, two, pair_low, pair_high, single_low, single_high, sems):
    even = lax.axis_index("gx") % 2 == 0
    ny, nx, nz = exchange.shape
    copies = []
    for k, ref in enumerate((temps, right, exchange, coupling)):
        low, high, at = (pair_low, pair_high, k) if k < 2 else (single_low, single_high, k - 2)
        lead = (slice(None),) * (ref.ndim - 2)
        copies.append(pltpu.make_async_copy(ref.at[lead + (slice(0, 8),)], low.at[at], sems.at[2 * k]))
        copies.append(pltpu.make_async_copy(ref.at[lead + (slice(nx - 8, nx),)], high.at[at], sems.at[2 * k + 1]))
    for copy in copies:
        copy.start()
    for copy in copies:
        copy.wait()
    at = 0
    for y in range(ny):
        sides = []
        for pair, single, is_low in ((pair_low, single_low, True), (pair_high, single_high, False)):
            s, g, rs, rg = (pair[i, j, y] for i in range(2) for j in range(2))
            sides.append(strip_values(s, g, conductivity_of(s, single[0, y]), rs, rg, single[1, y], is_low))
        for low, high, (plane, width) in zip(*sides, STRIP):
            one[at : at + width] = jnp.where(even, high, low)
            two[at : at + width] = jnp.where(even, low, high)
            at += width


def load_kernel(temps, right, exchange, coupling, st, sems):
    ny, nx, nz = exchange.shape
    planes, rows, ext, nz = st.shape
    copies = []
    for k, (plane, ref) in enumerate(
        ((SA, temps.at[0]), (K, exchange), (GA, temps.at[1]), (RS, right.at[0]), (RG, right.at[1]), (C, coupling))
    ):
        to = st.at[plane, pl.ds(1, ny), pl.ds(PAD, nx)]
        copies.append(pltpu.make_async_copy(ref, to, sems.at[k]))
    for copy in copies:
        copy.start()
    zeros = jnp.zeros((PAD, nz), jnp.float32)

    def clear(i, carry):
        for plane, width in STRIP:
            st[plane, i, :PAD] = zeros
            st[plane, i, PAD + nx :] = zeros
        return carry

    lax.fori_loop(1, ny + 1, clear, 0)
    for copy in copies:
        copy.wait()

    def conduct(i, carry):
        s = st[SA, i, PAD : PAD + nx]
        st[K, i, PAD : PAD + nx] = conductivity_of(s, st[K, i, PAD : PAD + nx])
        return carry

    lax.fori_loop(1, ny + 1, conduct, 0)


def place_halo(st, one, two, y, nx):
    even = lax.axis_index("gx") % 2 == 0
    at, i = y * STRIP_ROWS, y + 1
    for plane, width in STRIP:
        a, b = one[at : at + width], two[at : at + width]
        st[plane, i, PAD - width : PAD] = jnp.where(even, b, a)
        st[plane, i, PAD + nx : PAD + nx + width] = jnp.where(even, a, b)
        at += width


def inner(s, g, c, h, fx, fz, edge):
    t = c * (s - g)
    flux_x = fx * (up_x(s) - s)
    flux_z = fz * (up_z(s) - s)
    part_s = (flux_x - down_x(flux_x)) + (flux_z - down_z(flux_z)) - h * s - t
    part_g = (
        t
        - GAS_SELF * g
        + CONDUCT * (up_x(g) + down_x(g))
        + edge[0] * up_z(g)
        + edge[1] * down_z(g)
    )
    return part_s, part_g


def edge_weights(shape):
    lane = lanes(shape)
    weight = jnp.float32(0.25 * CONDUCT)
    return jnp.where(lane == shape[1] - 1, 0.0, weight), jnp.where(lane == 0, 0.0, weight)


def row_inner(st, i, s_at, edge):
    return inner(st[s_at, i], st[s_at + 1, i], st[C, i], st[H, i], st[FX, i], st[FZ, i], edge)


def row_residual(st, i, s_at, edge):
    part_s, part_g = row_inner(st, i, s_at, edge)
    s, g, before = st[s_at, i], st[s_at + 1, i], st[s_at + 1, i - 1]
    part_s += st[FY, i] * (st[s_at, i + 1] - s) + st[FY, i - 1] * (st[s_at, i - 1] - s)
    part_g += CONDUCT * (st[s_at + 1, i + 1] + before) - FLOW * (g - before)
    return st[RS, i] + part_s, st[RG, i] + part_g


def relaxed(st, i, s_at, res_s, res_g):
    s = st[s_at, i] + st[ASS, i] * res_s + st[ASG, i] * res_g
    g = st[s_at + 1, i] + st[ASG, i] * res_s + st[AGG, i] * res_g
    return s, g


def faces(k):
    lane = lanes(k.shape)
    end = k.shape[1] - 1
    fx = 0.5 * (k + up_x(k))
    fz = jnp.where(lane == end, 0.0, 0.125 * (k + up_z(k)))
    h = SOLID_CAP + jnp.where((lane == 0) | (lane == end), 0.125 * k, 0.0)
    return fx, fz, h, h + (fx + down_x(fx)) + (fz + down_z(fz))


def inverse(diag, c, mask):
    gas_diag = (GAS_SELF + FLOW) + c
    inv = (RELAX * mask) / (diag * gas_diag - c * c)
    return inv * gas_diag, inv * c, inv * diag


def last_relaxed(st, i, s_at, edge, own):
    full_s, full_g = st[s_at, i], st[s_at + 1, i]
    s, g = full_s[own], full_g[own]
    flux_x = st[FX, i] * (up_x(full_s) - full_s)
    flux_z = st[FZ, i, own] * (up_z(s) - s)
    c, before = st[C, i, own], st[s_at + 1, i - 1, own]
    t = c * (s - g)
    res_s = st[RS, i, own] + (flux_x[own] - down_x(flux_x)[own]) + (flux_z - down_z(flux_z)) - st[H, i, own] * s - t
    res_s += st[FY, i, own] * (st[s_at, i + 1, own] - s) + st[FY, i - 1, own] * (st[s_at, i - 1, own] - s)
    res_g = st[RG, i, own] + t - GAS_SELF * g + edge[0][own] * up_z(g) + edge[1][own] * down_z(g)
    res_g += CONDUCT * (up_x(full_g)[own] + down_x(full_g)[own] + st[s_at + 1, i + 1, own] + before) - FLOW * (g - before)
    ss, sg, gg = st[ASS, i, own], st[ASG, i, own], st[AGG, i, own]
    return s + ss * res_s + sg * res_g, g + sg * res_s + gg * res_g


def grouped(rows, work):
    for start in range(0, len(rows), GROUP):
        stores = []
        for i in rows[start : start + GROUP]:
            stores += work(i)
        for ref, at, value in stores:
            ref[at] = value


def row_coefficients(st, i, mask):
    fx, fz, h, diag = faces(st[K, i])
    fy = 0.5 * (st[K, i] + st[K, i + 1])
    before = 0.5 * (st[K, i] + st[K, i - 1])
    ss, sg, gg = inverse(diag + st[C, i] + fy + before, st[C, i], mask)
    values = ((FX, fx), (FZ, fz), (H, h), (FY, fy), (ASS, ss), (ASG, sg), (AGG, gg))
    return [(st, (plane, i), v) for plane, v in values]


def row_sweep(st, i, source, target, edge):
    s, g = relaxed(st, i, source, *row_residual(st, i, source, edge))
    return [(st, (target, i), s), (st, (target + 1, i), g)]


def send_planes(st, onward, edge):
    ny = st.shape[1] - 2
    e, d, near = (ny, ny - 1, ny - 1) if onward else (1, 2, 1)
    fy, s, g, g_d = st[FY, near], st[SA, e], st[GA, e], st[GA, d]
    part_s, part_g = row_inner(st, e, SA, edge)
    m_1s = st[RS, e] + part_s + fy * (st[SA, d] - s)
    m_1g = st[RG, e] + part_g + CONDUCT * g_d - FLOW * (g - g_d if onward else g)
    m_2s = st[RS, e] + fy * st[SB, d]
    m_2g = st[RG, e] + (CONDUCT + FLOW if onward else CONDUCT) * st[GB, d]
    return [s, g, st[K, e], st[C, e], fy, m_1s, m_1g, m_2s, m_2g]


def write_message(refs, st, onward, edge):
    ext = st.shape[2]
    for go in (True, False):

        @pl.when(onward == go)
        def _():
            for k, value in enumerate(send_planes(st, go, edge)):
                ref, at = message_plane(refs, k)
                ref[at] = value[CROP : ext - CROP]


def message_plane(refs, plane):
    return (refs[0], plane) if len(refs) == 1 or plane < HALF else (refs[1], plane - HALF)


def first_kernel(st_in, one, two, st, across):
    del st_in
    planes, rows, ext, nz = st.shape
    ny, nx = rows - 2, ext - 2 * PAD
    shape = (ext, nz)
    mask = x_mask(shape, nx)
    edge = edge_weights(shape)

    for y in list(range(4)) + list(range(ny - 4, ny)):
        place_halo(st, one, two, y, nx)
    for i in (1, ny):
        fx, fz, h, diag = faces(st[K, i])
        st[FX, i], st[FZ, i], st[H, i] = fx, fz, h
    st[FY, 1] = 0.5 * (st[K, 1] + st[K, 2])
    st[FY, ny - 3] = 0.5 * (st[K, ny - 3] + st[K, ny - 2])
    ends = [2, 3, ny - 2, ny - 1]
    grouped(ends, lambda i: row_coefficients(st, i, mask))
    grouped(ends, lambda i: row_sweep(st, i, SA, SB, edge))
    write_message([across], st, lax.axis_index("gy") % 2 == 1, edge)


def outer_residual(st, i, s_at, rs, rg, fy_out, edge, after):
    part_s, part_g = row_inner(st, i, s_at, edge)
    s, g = st[s_at, i], st[s_at + 1, i]
    if after:
        part_s += st[FY, i - 1] * (st[s_at, i - 1] - s)
        part_g += (CONDUCT + FLOW) * st[s_at + 1, i - 1]
    else:
        part_s += st[FY, i] * (st[s_at, i + 1] - s)
        part_g += CONDUCT * st[s_at + 1, i + 1]
    return rs + part_s - fy_out * s, rg + part_g - FLOW * g


def pair_x(v):
    row = lax.broadcasted_iota(jnp.int32, v.shape, 0)
    return v + jnp.where(row % 2 == 0, up_x(v), down_x(v))


def coarse_coefficients(c_sum, k_sum):
    solid = 4.0 * SOLID_CAP + c_sum + LUMP * k_sum
    ratio = c_sum / solid
    denominator = (4.0 * GAS_CAP + 2.0 * FLOW) + c_sum - c_sum * ratio
    return solid, ratio, denominator


def coarse_row(st, coarse, j, mask, edge):
    i = 2 * j + 1
    res_s, res_g = row_residual(st, i, SA, edge)
    more_s, more_g = row_residual(st, i + 1, SA, edge)
    res_s, res_g = pair_x((res_s + more_s) * mask), pair_x((res_g + more_g) * mask)
    c_sum = pair_x(st[C, i] + st[C, i + 1])
    solid, ratio, denominator = coarse_coefficients(c_sum, pair_x(st[K, i] + st[K, i + 1]))
    lead = res_s / solid
    values = (lead, ratio, (2.0 * FLOW) / denominator, (res_g + c_sum * lead) / denominator)
    return [(coarse, (k, j), v) for k, v in enumerate(values)]


def inner_kernel(st_in, one, two, st, coarse, beside_a, beside_b):
    del st_in
    planes, rows, ext, nz = st.shape
    ny, nx = rows - 2, ext - 2 * PAD
    shape = (ext, nz)
    mask = x_mask(shape, nx)
    edge = edge_weights(shape)
    for y in range(4, ny - 4):
        place_halo(st, one, two, y, nx)
    grouped(list(range(4, ny - 2)), lambda i: row_coefficients(st, i, mask))
    grouped(list(range(4, ny - 2)), lambda i: row_sweep(st, i, SA, SB, edge))
    grouped(list(range(3, ny - 1)), lambda i: row_sweep(st, i, SB, SA, edge))
    for j in range(2, ny // 2 - 2):
        for ref, at, value in coarse_row(st, coarse, j, mask, edge):
            ref[at] = value
    write_message([beside_a, beside_b], st, lax.axis_index("gy") % 2 == 0, edge)


def end_work(st, coarse, extra, got, outer, is_after):
    planes, rows, ext, nz = st.shape
    ny, nx = rows - 2, ext - 2 * PAD
    me, count = lax.axis_index("gy"), lax.axis_size("gy")
    mask = x_mask((ext, nz), nx)
    inside = jnp.where(me == (count - 1 if is_after else 0), 0.0, mask)
    edge = edge_weights((ext, nz))
    zeros = jnp.zeros((PAD, nz), jnp.float32)
    for k in range(MESSAGE):
        outer[k, :PAD] = zeros
        outer[k, ext - PAD :] = zeros
        ref, at = message_plane(got, k)
        outer[k, CROP : ext - CROP] = ref[at]

    o, e, near = (ny + 1, ny, ny) if is_after else (0, 1, 0)
    to_o = CONDUCT + FLOW if is_after else CONDUCT
    s_o, g_o, k_o, c_o, fy_out = (outer[plane] for plane in (M_S, M_G, M_K, M_C, M_FY))
    fy = 0.5 * (k_o + st[K, e])
    fx, fz, h, diag = faces(k_o)
    inv_o = inverse(diag + c_o + fy_out + fy, c_o, inside)
    fx_e, fz_e = st[FX, e], st[FZ, e]
    diag = st[H, e] + (fx_e + down_x(fx_e)) + (fz_e + down_z(fz_e)) + st[C, e] + fy
    inv_e = inverse(diag + st[FY, near - 1 if is_after else near + 1], st[C, e], mask)
    for plane, value in ((SA, s_o), (GA, g_o), (K, k_o), (C, c_o), (FX, fx), (FZ, fz), (H, h)):
        st[plane, o] = value
    st[FY, near] = fy
    for k in range(3):
        st[ASS + k, o], st[ASS + k, e] = inv_o[k], inv_e[k]

    res = outer[M_1S] + fy * (st[SA, e] - s_o), outer[M_1G] + to_o * st[GA, e]
    new_o = relaxed(st, o, SA, *res)
    stores = row_sweep(st, e, SA, SB, edge)
    st[SB, o], st[GB, o] = new_o
    for ref, at, value in stores:
        ref[at] = value
    res = outer_residual(st, o, SB, outer[M_2S], outer[M_2G], fy_out, edge, is_after)
    new_o = relaxed(st, o, SB, *res)
    ends = [e - 1, e] if is_after else [e, e + 1]
    grouped(ends, lambda i: row_sweep(st, i, SB, SA, edge))
    st[SA, o], st[GA, o] = new_o
    for k, plane in enumerate((M_2S, M_2G, M_FY)):
        extra[(3 if is_after else 0) + k] = outer[plane]
    blocks = ny // 2
    stores = []
    for j in (blocks - 2, blocks - 1) if is_after else (0, 1):
        stores += coarse_row(st, coarse, j, mask, edge)
    for ref, at, value in stores:
        ref[at] = value


def either_end(after, st, coarse, extra, got, outer):
    for is_after in (True, False):

        @pl.when(after == is_after)
        def _():
            end_work(st, coarse, extra, got, outer, is_after)


def near_kernel(st_in, coarse_in, beside_a, beside_b, st, coarse, extra, outer):
    del st_in, coarse_in
    either_end(lax.axis_index("gy") % 2 == 0, st, coarse, extra, [beside_a, beside_b], outer)


def second_kernel(st_in, coarse_in, extra_in, across, *refs):
    st, coarse, extra, total, last_info, first_info, message, outer, squeeze = refs
    del st_in, coarse_in, extra_in
    planes, rows, ext, nz = st.shape
    ny, nx = rows - 2, ext - 2 * PAD
    me = lax.axis_index("gy")
    either_end(me % 2 == 1, st, coarse, extra, [across], outer)

    blocks = ny // 2
    for k in range(4):
        squeeze[k] = coarse[k, 0]
    slopes, offsets = coarse[2, 0], coarse[3, 0]
    for j in range(1, blocks):
        slope = coarse[2, j]
        slopes, offsets = slope * slopes, slope * offsets + coarse[3, j]
        coarse[2, j], coarse[3, j] = slopes, offsets
    squeeze[4], squeeze[5], squeeze[6], squeeze[7] = slopes, offsets, coarse[0, blocks - 1], coarse[1, blocks - 1]

    span = nx // 2 + 2
    lead, ratio, slope, offset, slopes, offsets, lead_last, ratio_last = (
        squeeze[k, pl.ds(PAD - 2, span, 2), :] for k in range(8)
    )
    part = slice(PAD - 1, PAD + nx + 1)

    def increments(d, face, gas):
        return [(st[FY, face] * (st[SA, d] - st[SB, d]))[part], (gas * (st[GA, d] - st[GB, d]))[part]]

    onward = [lead_last, ratio_last] + increments(ny - 1, ny - 1, CONDUCT + FLOW)
    back = [lead, offset] + increments(2, 1, CONDUCT) + [slope, ratio]
    write_rows(total, [slopes, offsets])
    write_rows(last_info, onward)
    write_rows(first_info, back)
    for go, info in ((True, onward), (False, back)):

        @pl.when((me % 2 == 0) == go)
        def _():
            write_rows(message, [slopes, offsets] + info)


def write_rows(ref, values):
    at = 0
    for value in values:
        ref[at : at + value.shape[0]] = value
        at += value.shape[0]


class Rows:
    def __init__(self, nx):
        self.span = nx // 2 + 2
        self.map = 2 * self.span
        self.info = self.map + 2 * (nx + 2)
        self.rest = self.map
        self.final = self.map + self.info
        self.full = self.final + self.rest
        self.low = self.map
        self.high = self.low + self.info
        self.near = self.high + self.info + self.rest


def source(at, k, radix):
    if radix & (radix - 1) == 0:
        return at ^ k
    return (at + radix - k) % radix


def target(at, k, radix):
    return at ^ k if radix & (radix - 1) == 0 else (at + k) % radix


def order(radix):
    out = [(k, any(abs(source(at, k, radix) - at) == 1 for at in range(radix))) for k in range(1, radix)]
    return sorted(out, key=lambda item: (not item[1], -item[0]))


def stages(count):
    if count % 2:
        return [1, count]
    out, rest = [2], count // 2
    while rest > 1:
        radix = next((r for r in (8, 4, 2) if rest % r == 0), rest)
        out.append(radix)
        rest //= radix
    return out if len(out) > 1 else out + [1]


def exchange_stage(messages, radix, stride):
    count, got = lax.axis_size("gy"), []
    for (k, near), message in zip(order(radix), messages):
        pairs = []
        for me in range(count):
            at, low = me // stride % radix, me % stride
            sender = me - low + (source(at, k, radix) - at) * stride + (stride - 1 - low)
            pairs.append((sender, me))
        got.append(lax.ppermute(message, "gy", pairs))
    return got


class Group:
    def __init__(self, radix, stride, others, nx):
        self.radix, self.others, self.nx = radix, others, nx
        me = lax.axis_index("gy")
        self.at = lax.rem(lax.div(me, stride), radix)
        low = lax.rem(me, stride)
        self.lowest, self.highest = low == 0, low == stride - 1

    def map_of(self, place, own):
        rows = Rows(self.nx)
        out = own
        for (k, near), ref in zip(order(self.radix), self.others):
            here = source(self.at, k, self.radix) == place
            got = [ref[i * rows.span : (i + 1) * rows.span] for i in range(2)]
            out = got if out is None else [jnp.where(here, new, old) for new, old in zip(got, out)]
        return out

    def ahead(self, slope, offset):
        a, b = jnp.ones_like(slope), jnp.zeros_like(slope)
        for place in range(self.radix - 1):
            new_a, new_b = self.map_of(place, None)
            below = place < self.at
            a, b = jnp.where(below, new_a * a, a), jnp.where(below, new_a * b + new_b, b)
        return slope * a, slope * b + offset

    def total(self, own):
        a, b = self.map_of(0, own)
        for place in range(1, self.radix):
            new_a, new_b = self.map_of(place, own)
            a, b = new_a * a, new_a * b + new_b
        return a, b

    def collect(self, near, final):
        rows = Rows(self.nx)
        for (k, adjacent), ref in zip(order(self.radix), self.others):
            if not adjacent:
                continue
            place = source(self.at, k, self.radix)

            @pl.when(self.lowest & (place == self.at - 1))
            def _():
                near[rows.low : rows.low + rows.info] = ref[rows.map : rows.final]

            @pl.when(self.highest & (place == self.at + 1))
            def _():
                near[rows.high : rows.high + rows.info] = ref[rows.map : rows.final]
                rest = slice(0, rows.map) if final else slice(rows.final, rows.full)
                near[rows.high + rows.info : rows.near] = ref[rest]


def start_near(near, nx, nz):
    rows = Rows(nx)
    near[: rows.span] = jnp.ones((rows.span, nz), jnp.float32)
    near[rows.span :] = jnp.zeros((near.shape[0] - rows.span, nz), jnp.float32)


def join_kernel(radix, stride, final, nx, is_first, *refs):
    rows = Rows(nx)
    total, last_info, first_info, near_in = refs[:4]
    others, near, outs = refs[4 : 3 + radix], refs[3 + radix], refs[4 + radix :]
    nz = near.shape[1]
    if is_first:
        start_near(near, nx, nz)
    else:
        near[...] = near_in[...]
    group = Group(radix, stride, others, nx)
    own = [total[i * rows.span : (i + 1) * rows.span] for i in range(2)]
    ahead = group.ahead(near[: rows.span], near[rows.span : rows.map])
    write_rows(near, ahead)
    group.collect(near, False)
    whole = group.total(own)
    at = lax.div(lax.axis_index("gy"), stride * radix)
    if final == 0:
        write_rows(outs[0], whole)
        return
    at = lax.rem(at, final)
    for (k, adjacent), out in zip(order(final), outs):
        up = target(at, k, final) > at
        if not adjacent:
            write_rows(out, whole)
            continue

        @pl.when(up)
        def _():
            write_rows(out, whole)
            out[rows.map : rows.final] = last_info[: rows.info]

        @pl.when(jnp.logical_not(up))
        def _():
            out[: rows.map] = first_info[rows.info : rows.info + rows.rest]
            out[rows.map : rows.final] = first_info[: rows.info]


def full_message(nx, stride, radix, total, last_info, first_info, k):
    rows = Rows(nx)
    at = lax.axis_index("gy") // stride % radix
    onward = jnp.concatenate([total[: rows.map], last_info[: rows.info], first_info[rows.info : rows.info + rows.rest]])
    back = jnp.concatenate([total[: rows.map], first_info[: rows.info + rows.rest]])
    message = jnp.where(target(at, k, radix) > at, onward, back)
    return jnp.pad(message, ((0, -rows.full % 8), (0, 0)))


def third_kernel(radix, stride, *refs):
    st, extra, coarse, near_in = refs[:4]
    others, (out, sc, wide, near, done, sems) = refs[4 : 3 + radix], refs[3 + radix :]
    planes, rows, ext, nz = st.shape
    ny, nx = rows - 2, ext - 2 * PAD
    edge = edge_weights((ext, nz))
    blocks = ny // 2

    lay = Rows(nx)
    span = lay.span
    near[...] = near_in[...]
    group = Group(radix, stride, others, nx)
    if radix > 1:
        group.collect(near, True)
    gas_in = group.ahead(near[:span], near[span : lay.map])[1]
    at_high = lay.high + lay.info
    starts = [lay.low, lay.low + span, lay.high, lay.high + span, at_high, at_high + span]
    for k, v in enumerate([gas_in] + [near[start : start + span] for start in starts]):
        wide[k, : PAD - 2] = jnp.zeros((PAD - 2, nz), jnp.float32)
        wide[k, ext - PAD + 2 :] = jnp.zeros((PAD - 2, nz), jnp.float32)
        wide[k, pl.ds(PAD - 2, span, 2), :] = v
        wide[k, pl.ds(PAD - 1, span, 2), :] = v
    for k, start in enumerate((lay.low, lay.low + nx + 2, lay.high, lay.high + nx + 2)):
        start += lay.map
        wide[7 + k, :PAD] = jnp.zeros((PAD, nz), jnp.float32)
        wide[7 + k, ext - PAD :] = jnp.zeros((PAD, nz), jnp.float32)
        wide[7 + k, PAD - 1 : PAD + nx + 1] = near[start : start + nx + 2]

    gas_in = wide[0]
    last = ny + 1
    solid_low = wide[1] + wide[2] * gas_in
    sc[0, 0] = st[SA, 0] + solid_low
    sc[1, 0] = st[GA, 0] + gas_in

    def correct(j, carry):
        gas = coarse[2, j] * gas_in + coarse[3, j]
        solid = coarse[0, j] + coarse[1, j] * gas
        for i in (2 * j + 1, 2 * j + 2):
            sc[0, i] = st[SA, i] + solid
            sc[1, i] = st[GA, i] + gas
        return carry

    lax.fori_loop(0, blocks, correct, 0)
    gas = coarse[2, blocks - 1] * gas_in + coarse[3, blocks - 1]
    gas_high = wide[5] * gas + wide[4]
    solid_high = wide[3] + wide[6] * gas_high
    sc[0, last] = st[SA, last] + solid_high
    sc[1, last] = st[GA, last] + gas_high

    view = Fields(st, sc)
    for i, is_after, solid, gas in ((0, False, solid_low, gas_in), (last, True, solid_high, gas_high)):
        side = 3 if is_after else 0
        fy = extra[side + 2]
        to = 9 if is_after else 7
        rs = extra[side] + wide[to] + fy * solid
        rg = extra[side + 1] + wide[to + 1] + (CONDUCT if is_after else CONDUCT + FLOW) * gas
        res = outer_residual(view, i, SA, rs, rg, fy, edge, is_after)
        sc[2, i], sc[3, i] = relaxed(view, i, SA, *res)

    def sweep(k, carry):
        stores = []
        for r in range(GROUP):
            i = GROUP * k + 1 + r
            new_s, new_g = relaxed(view, i, SA, *row_residual(view, i, SA, edge))
            stores += [((2, i), new_s), ((3, i), new_g)]
        for at, value in stores:
            sc[at] = value
        return carry

    lax.fori_loop(0, ny // GROUP, sweep, 0)

    def leaving(k):
        part = pl.ds(GROUP * k, GROUP)
        return pltpu.make_async_copy(done.at[:, part], out.at[:, part], sems.at[k])

    def final(k, carry):
        stores = []
        for r in range(GROUP):
            i = GROUP * k + 1 + r
            new_s, new_g = last_relaxed(view, i, SB, edge, slice(PAD, PAD + nx))
            stores += [((0, i - 1), new_s), ((1, i - 1), new_g)]
        for at, value in stores:
            done[at] = value
        leaving(k).start()
        return carry

    lax.fori_loop(0, ny // GROUP, final, 0)
    for k in range(ny // GROUP):
        leaving(k).wait()


class Fields:
    def __init__(self, st, sc):
        self.st, self.sc = st, sc

    def __getitem__(self, at):
        return (self.sc if at[0] <= GB else self.st)[at]


def cost(rows, cells):
    return pl.CostEstimate(flops=50 * rows * cells, bytes_accessed=16 * 4 * rows * cells, transcendentals=0)


def swap(x, axis, first):
    pairs = []
    for i in range(first, lax.axis_size(axis) - 1, 2):
        pairs += [(i, i + 1), (i + 1, i)]
    return lax.ppermute(x, axis, pairs)


def shards(temps, right_side, exchange, coupling):
    temps, right_side = (jnp.transpose(a, (0, 2, 1, 3)) for a in (temps, right_side))
    exchange, coupling = (jnp.transpose(a, (1, 0, 2)) for a in (exchange, coupling))
    temps, right_side, exchange, coupling = (
        pltpu.with_memory_space_constraint(a, pltpu.HBM) for a in (temps, right_side, exchange, coupling)
    )
    ny, nx, nz = exchange.shape
    ext = nx + 2 * PAD
    f32 = functools.partial(jax.ShapeDtypeStruct, dtype=jnp.float32)

    height = (ny * STRIP_ROWS + 7) // 8 * 8
    strips = f32((height, nz)), f32((height, nz))
    scratch = [(2, 2, ny, 8, nz)] * 2 + [(2, ny, 8, nz)] * 2
    one, two = pl.pallas_call(
        pack_kernel,
        out_shape=strips,
        in_specs=[HBM] * 4,
        out_specs=(VMEM,) * 2,
        scratch_shapes=[pltpu.VMEM(shape, jnp.float32) for shape in scratch] + [pltpu.SemaphoreType.DMA((8,))],
        compiler_params=PARAMS,
        name="pack_x",
    )(temps, right_side, exchange, coupling)
    one, two = swap(one, "gx", 0), swap(two, "gx", 1)

    state = f32((PLANES, ny + 2, ext, nz))

    def letter(planes):
        return f32((planes, ext - 2 * CROP, nz))

    st = pl.pallas_call(
        load_kernel,
        out_shape=state,
        in_specs=[HBM] * 4,
        out_specs=VMEM,
        scratch_shapes=[pltpu.SemaphoreType.DMA((6,))],
        compiler_params=PARAMS,
        cost_estimate=cost(2 * ny, ext * nz),
        name="load",
    )(temps, right_side, exchange, coupling)
    st, across = pl.pallas_call(
        first_kernel,
        out_shape=(state, letter(MESSAGE)),
        in_specs=[VMEM] * 3,
        out_specs=(VMEM,) * 2,
        input_output_aliases={0: 0},
        compiler_params=PARAMS,
        name="first",
    )(st, one, two)
    across = swap(across, "gy", 1)

    rows = f32((4, ny // 2, ext, nz))
    st, coarse, beside_a, beside_b = pl.pallas_call(
        inner_kernel,
        out_shape=(state, rows, letter(HALF), letter(MESSAGE - HALF)),
        in_specs=[VMEM] * 3,
        out_specs=(VMEM,) * 4,
        input_output_aliases={0: 0},
        compiler_params=PARAMS,
        cost_estimate=cost(4 * ny, ext * nz),
        name="inner",
    )(st, one, two)

    beside_a, beside_b = swap(beside_a, "gy", 0), swap(beside_b, "gy", 0)

    lay = Rows(nx)

    def tall(height):
        return f32(((height + 7) // 8 * 8, nz))

    letter_room = pltpu.VMEM((MESSAGE, ext, nz), jnp.float32)
    more = f32((6, ext, nz))
    st, coarse, extra = pl.pallas_call(
        near_kernel,
        out_shape=(state, rows, more),
        in_specs=[VMEM] * 4,
        out_specs=(VMEM,) * 3,
        scratch_shapes=[letter_room],
        input_output_aliases={0: 0, 1: 1},
        compiler_params=PARAMS,
        name="near",
    )(st, coarse, beside_a, beside_b)
    st, coarse, extra, total, last_info, first_info, message = pl.pallas_call(
        second_kernel,
        out_shape=(state, rows, more, tall(lay.map), tall(lay.info), tall(lay.info + lay.rest), tall(lay.full)),
        in_specs=[VMEM] * 4,
        out_specs=(VMEM,) * 7,
        scratch_shapes=[letter_room, pltpu.VMEM((8, ext, nz), jnp.float32)],
        input_output_aliases={0: 0, 1: 1, 2: 2},
        compiler_params=PARAMS,
        name="second",
    )(st, coarse, extra, across)

    near, messages = total, [message]
    radices, stride = stages(lax.axis_size("gy")), 1
    for place, radix in enumerate(radices[:-1]):
        if place:
            messages = [full_message(nx, stride, radix, total, last_info, first_info, k) for k, _ in order(radix)]
        others = exchange_stage(messages, radix, stride)
        final = radices[-1] if place == len(radices) - 2 else 0
        outs = [tall(lay.final if adjacent else lay.map) for _, adjacent in order(final)] if final else [tall(lay.map)]
        near, *messages = pl.pallas_call(
            functools.partial(join_kernel, radix, stride, final, nx, place == 0),
            out_shape=(tall(lay.near), *outs),
            in_specs=[VMEM] * (3 + radix),
            out_specs=(VMEM,) * (1 + len(outs)),
            compiler_params=PARAMS,
            name="join",
        )(total, last_info, first_info, near, *others)
        total = total if final else messages[0]
        stride *= radix
    got = exchange_stage(messages, radices[-1], stride)

    out = pl.pallas_call(
        functools.partial(third_kernel, radices[-1], stride),
        out_shape=f32((2, ny, nx, nz)),
        in_specs=[VMEM] * (4 + len(got)),
        out_specs=HBM,
        scratch_shapes=[
            pltpu.VMEM((4, ny + 2, ext, nz), jnp.float32),
            pltpu.VMEM((11, ext, nz), jnp.float32),
            pltpu.VMEM(tall(lay.near).shape, jnp.float32),
            pltpu.VMEM((2, ny, nx, nz), jnp.float32),
            pltpu.SemaphoreType.DMA((ny // GROUP,)),
        ],
        compiler_params=PARAMS,
        name="third",
    )(st, extra, coarse, near, *got)
    return jnp.transpose(out, (0, 2, 1, 3))


def solution(mesh):
    return jax.shard_map(
        shards,
        mesh=mesh,
        in_specs=(
            P(None, "gx", "gy", None),
            P(None, "gx", "gy", None),
            P("gx", "gy", None),
            P("gx", "gy", None),
        ),
        out_specs=P(None, "gx", "gy", None),
        check_vma=False,
    )
```

```python
import functools

import jax
import jax.numpy as jnp
from jax import lax
from jax.experimental import pallas as pl
from jax.experimental.pallas import tpu as pltpu
from jax.sharding import PartitionSpec as P

SOLID_CAP, GAS_CAP, FLOW, CONDUCT, RELAX, LUMP = 0.5, 0.02, 40.0, 0.05, 0.8, 0.25
GAS_SELF = GAS_CAP + 4.5 * CONDUCT

PAD = 8
WX = 5
CROP = 4
(SA, GA, SB, GB, K, C, RS, RG, FX, FZ, H, FY, ASS, ASG, AGG) = range(15)
PLANES = 15
(M_S, M_G, M_K, M_C, M_FY, M_1S, M_1G, M_2S, M_2G) = range(9)
MESSAGE, EARLY, THIRD = 9, 5, 3

GROUP = 3

VMEM = pl.BlockSpec(memory_space=pltpu.VMEM)
HBM = pl.BlockSpec(memory_space=pltpu.HBM)
PARAMS = pltpu.CompilerParams(vmem_limit_bytes=40 * 1024 * 1024)


def up_x(v):
    return pltpu.roll(v, v.shape[0] - 1, 0)


def down_x(v):
    return pltpu.roll(v, 1, 0)


def up_z(v):
    return pltpu.roll(v, v.shape[1] - 1, 1)


def down_z(v):
    return pltpu.roll(v, 1, 1)


def lanes(shape):
    return lax.broadcasted_iota(jnp.int32, shape, 1)


def x_mask(shape, nx):
    row = lax.broadcasted_iota(jnp.int32, shape, 0)
    place, count = lax.axis_index("gx"), lax.axis_size("gx")
    low = jnp.where(place == 0, PAD, PAD - WX)
    high = jnp.where(place == count - 1, PAD + nx, PAD + nx + WX)
    return jnp.where((row >= low) & (row < high), 1.0, 0.0).astype(jnp.float32)


STRIP = ((SA, WX - 1), (GA, WX - 1), (K, WX), (RS, WX - 1), (RG, WX - 1), (C, WX - 1))
STRIP_ROWS = sum(width for plane, width in STRIP)


def conductivity_of(s, exchange):
    return 1.0 + 4.0 * exchange * s * s * s


def strip_values(s, g, k, rs, rg, c, low):
    out, inn = (WX - 1, WX - 2) if low else (8 - WX, 9 - WX)
    four = slice(0, WX - 1) if low else slice(9 - WX, 8)
    five = slice(0, WX) if low else slice(8 - WX, 8)
    row = lax.broadcasted_iota(jnp.int32, s.shape, 0)
    rs = rs + jnp.where(row == inn, 0.5 * (k[inn : inn + 1] + k[out : out + 1]) * s[out : out + 1], 0.0)
    rg = rg + jnp.where(row == inn, CONDUCT * g[out : out + 1], 0.0)
    return [s[four], g[four], k[five], rs[four], rg[four], c[four]]


def pack_kernel(temps, right, exchange, coupling, one, two, early, *scratch):
    pair_low, pair_high, single_low, single_high, rows_t, rows_e, rows_c, sems = scratch
    even = lax.axis_index("gx") % 2 == 0
    odd = lax.axis_index("gy") % 2 == 1
    ny, nx, nz = exchange.shape
    copies = []
    for k, ref in enumerate((temps, right, exchange, coupling)):
        low, high, at = (pair_low, pair_high, k) if k < 2 else (single_low, single_high, k - 2)
        lead = (slice(None),) * (ref.ndim - 2)
        copies.append(pltpu.make_async_copy(ref.at[lead + (slice(0, 8),)], low.at[at], sems.at[2 * k]))
        copies.append(pltpu.make_async_copy(ref.at[lead + (slice(nx - 8, nx),)], high.at[at], sems.at[2 * k + 1]))
    ends = pl.ds(jnp.where(odd, ny - 2, 0), 2)
    copies.append(pltpu.make_async_copy(temps.at[:, ends], rows_t, sems.at[8]))
    copies.append(pltpu.make_async_copy(exchange.at[ends], rows_e, sems.at[9]))
    copies.append(pltpu.make_async_copy(coupling.at[ends], rows_c, sems.at[10]))
    for copy in copies:
        copy.start()
    for copy in copies:
        copy.wait()
    at = 0
    for y in range(ny):
        sides = []
        for pair, single, is_low in ((pair_low, single_low, True), (pair_high, single_high, False)):
            s, g, rs, rg = (pair[i, j, y] for i in range(2) for j in range(2))
            sides.append(strip_values(s, g, conductivity_of(s, single[0, y]), rs, rg, single[1, y], is_low))
        for low, high, (plane, width) in zip(*sides, STRIP):
            one[at : at + width] = jnp.where(even, high, low)
            two[at : at + width] = jnp.where(even, low, high)
            at += width
    k = [conductivity_of(rows_t[0, i], rows_e[i]) for i in range(2)]
    pick = lambda pair: jnp.where(odd, pair[1], pair[0])
    early[M_S], early[M_G] = pick([rows_t[0, i] for i in range(2)]), pick([rows_t[1, i] for i in range(2)])
    early[M_K], early[M_C], early[M_FY] = pick(k), pick([rows_c[i] for i in range(2)]), 0.5 * (k[0] + k[1])


def load_kernel(temps, right, exchange, coupling, st, sems):
    ny, nx, nz = exchange.shape
    planes, rows, ext, nz = st.shape
    copies = []
    for k, (plane, ref) in enumerate(
        ((SA, temps.at[0]), (K, exchange), (GA, temps.at[1]), (RS, right.at[0]), (RG, right.at[1]), (C, coupling))
    ):
        to = st.at[plane, pl.ds(1, ny), pl.ds(PAD, nx)]
        copies.append(pltpu.make_async_copy(ref, to, sems.at[k]))
    for copy in copies:
        copy.start()
    zeros = jnp.zeros((PAD, nz), jnp.float32)

    def clear(i, carry):
        for plane, width in STRIP:
            st[plane, i, :PAD] = zeros
            st[plane, i, PAD + nx :] = zeros
        return carry

    lax.fori_loop(1, ny + 1, clear, 0)
    for copy in copies:
        copy.wait()

    def conduct(i, carry):
        s = st[SA, i, PAD : PAD + nx]
        st[K, i, PAD : PAD + nx] = conductivity_of(s, st[K, i, PAD : PAD + nx])
        return carry

    lax.fori_loop(1, ny + 1, conduct, 0)


def place_halo(st, one, two, y, nx):
    even = lax.axis_index("gx") % 2 == 0
    at, i = y * STRIP_ROWS, y + 1
    for plane, width in STRIP:
        a, b = one[at : at + width], two[at : at + width]
        st[plane, i, PAD - width : PAD] = jnp.where(even, b, a)
        st[plane, i, PAD + nx : PAD + nx + width] = jnp.where(even, a, b)
        at += width


def inner(s, g, c, h, fx, fz, edge):
    t = c * (s - g)
    flux_x = fx * (up_x(s) - s)
    flux_z = fz * (up_z(s) - s)
    part_s = (flux_x - down_x(flux_x)) + (flux_z - down_z(flux_z)) - h * s - t
    part_g = (
        t
        - GAS_SELF * g
        + CONDUCT * (up_x(g) + down_x(g))
        + edge[0] * up_z(g)
        + edge[1] * down_z(g)
    )
    return part_s, part_g


def edge_weights(shape):
    lane = lanes(shape)
    weight = jnp.float32(0.25 * CONDUCT)
    return jnp.where(lane == shape[1] - 1, 0.0, weight), jnp.where(lane == 0, 0.0, weight)


def row_inner(st, i, s_at, edge):
    return inner(st[s_at, i], st[s_at + 1, i], st[C, i], st[H, i], st[FX, i], st[FZ, i], edge)


def row_residual(st, i, s_at, edge):
    part_s, part_g = row_inner(st, i, s_at, edge)
    s, g, before = st[s_at, i], st[s_at + 1, i], st[s_at + 1, i - 1]
    part_s += st[FY, i] * (st[s_at, i + 1] - s) + st[FY, i - 1] * (st[s_at, i - 1] - s)
    part_g += CONDUCT * (st[s_at + 1, i + 1] + before) - FLOW * (g - before)
    return st[RS, i] + part_s, st[RG, i] + part_g


def relaxed(st, i, s_at, res_s, res_g):
    s = st[s_at, i] + st[ASS, i] * res_s + st[ASG, i] * res_g
    g = st[s_at + 1, i] + st[ASG, i] * res_s + st[AGG, i] * res_g
    return s, g


def faces(k):
    lane = lanes(k.shape)
    end = k.shape[1] - 1
    fx = 0.5 * (k + up_x(k))
    fz = jnp.where(lane == end, 0.0, 0.125 * (k + up_z(k)))
    h = SOLID_CAP + jnp.where((lane == 0) | (lane == end), 0.125 * k, 0.0)
    return fx, fz, h, h + (fx + down_x(fx)) + (fz + down_z(fz))


def inverse(diag, c, mask):
    gas_diag = (GAS_SELF + FLOW) + c
    inv = (RELAX * mask) / (diag * gas_diag - c * c)
    return inv * gas_diag, inv * c, inv * diag


def last_relaxed(st, i, s_at, edge, own):
    full_s, full_g = st[s_at, i], st[s_at + 1, i]
    s, g = full_s[own], full_g[own]
    flux_x = st[FX, i] * (up_x(full_s) - full_s)
    flux_z = st[FZ, i, own] * (up_z(s) - s)
    c, before = st[C, i, own], st[s_at + 1, i - 1, own]
    t = c * (s - g)
    res_s = st[RS, i, own] + (flux_x[own] - down_x(flux_x)[own]) + (flux_z - down_z(flux_z)) - st[H, i, own] * s - t
    res_s += st[FY, i, own] * (st[s_at, i + 1, own] - s) + st[FY, i - 1, own] * (st[s_at, i - 1, own] - s)
    res_g = st[RG, i, own] + t - GAS_SELF * g + edge[0][own] * up_z(g) + edge[1][own] * down_z(g)
    res_g += CONDUCT * (up_x(full_g)[own] + down_x(full_g)[own] + st[s_at + 1, i + 1, own] + before) - FLOW * (g - before)
    ss, sg, gg = st[ASS, i, own], st[ASG, i, own], st[AGG, i, own]
    return s + ss * res_s + sg * res_g, g + sg * res_s + gg * res_g


def grouped(rows, work):
    for start in range(0, len(rows), GROUP):
        stores = []
        for i in rows[start : start + GROUP]:
            stores += work(i)
        for ref, at, value in stores:
            ref[at] = value


def row_coefficients(st, i, mask):
    fx, fz, h, diag = faces(st[K, i])
    fy = 0.5 * (st[K, i] + st[K, i + 1])
    before = 0.5 * (st[K, i] + st[K, i - 1])
    ss, sg, gg = inverse(diag + st[C, i] + fy + before, st[C, i], mask)
    values = ((FX, fx), (FZ, fz), (H, h), (FY, fy), (ASS, ss), (ASG, sg), (AGG, gg))
    return [(st, (plane, i), v) for plane, v in values]


def row_sweep(st, i, source, target, edge):
    s, g = relaxed(st, i, source, *row_residual(st, i, source, edge))
    return [(st, (target, i), s), (st, (target + 1, i), g)]


def send_planes(st, onward, edge):
    ny = st.shape[1] - 2
    e, d, near = (ny, ny - 1, ny - 1) if onward else (1, 2, 1)
    fy, s, g, g_d = st[FY, near], st[SA, e], st[GA, e], st[GA, d]
    part_s, part_g = row_inner(st, e, SA, edge)
    m_1s = st[RS, e] + part_s + fy * (st[SA, d] - s)
    m_1g = st[RG, e] + part_g + CONDUCT * g_d - FLOW * (g - g_d if onward else g)
    m_2s = st[RS, e] + fy * st[SB, d]
    m_2g = st[RG, e] + (CONDUCT + FLOW if onward else CONDUCT) * st[GB, d]
    return [s, g, st[K, e], st[C, e], fy, m_1s, m_1g, m_2s, m_2g]


def write_across(ref, k, value):
    ext = value.shape[0]
    if k >= EARLY:
        ref[k - EARLY] = value[CROP : ext - CROP]
    else:
        ref[MESSAGE - EARLY, 8 * k : 8 * k + 4] = value[CROP:PAD]
        ref[MESSAGE - EARLY, 8 * k + 4 : 8 * k + 8] = value[ext - PAD : ext - CROP]


def read_across(early, across, outer, k):
    ext = outer.shape[1]
    if k >= EARLY:
        outer[k, CROP : ext - CROP] = across[k - EARLY]
    else:
        outer[k, PAD : ext - PAD] = early[k]
        outer[k, CROP:PAD] = across[MESSAGE - EARLY, 8 * k : 8 * k + 4]
        outer[k, ext - PAD : ext - CROP] = across[MESSAGE - EARLY, 8 * k + 4 : 8 * k + 8]


def write_beside(refs, k, value):
    refs[k // THIRD][k % THIRD] = value[CROP : value.shape[0] - CROP]


def read_beside(refs, outer, k):
    outer[k, CROP : outer.shape[1] - CROP] = refs[k // THIRD][k % THIRD]


def write_message(write, st, onward, edge):
    for go in (True, False):

        @pl.when(onward == go)
        def _():
            for k, value in enumerate(send_planes(st, go, edge)):
                write(k, value)


def first_kernel(st_in, one, two, st, across):
    del st_in
    planes, rows, ext, nz = st.shape
    ny, nx = rows - 2, ext - 2 * PAD
    shape = (ext, nz)
    mask = x_mask(shape, nx)
    edge = edge_weights(shape)

    for y in list(range(4)) + list(range(ny - 4, ny)):
        place_halo(st, one, two, y, nx)
    for i in (1, ny):
        fx, fz, h, diag = faces(st[K, i])
        st[FX, i], st[FZ, i], st[H, i] = fx, fz, h
    st[FY, 1] = 0.5 * (st[K, 1] + st[K, 2])
    st[FY, ny - 3] = 0.5 * (st[K, ny - 3] + st[K, ny - 2])
    ends = [2, 3, ny - 2, ny - 1]
    grouped(ends, lambda i: row_coefficients(st, i, mask))
    grouped(ends, lambda i: row_sweep(st, i, SA, SB, edge))
    write_message(functools.partial(write_across, across), st, lax.axis_index("gy") % 2 == 1, edge)


def outer_residual(st, i, s_at, rs, rg, fy_out, edge, after):
    part_s, part_g = row_inner(st, i, s_at, edge)
    s, g = st[s_at, i], st[s_at + 1, i]
    if after:
        part_s += st[FY, i - 1] * (st[s_at, i - 1] - s)
        part_g += (CONDUCT + FLOW) * st[s_at + 1, i - 1]
    else:
        part_s += st[FY, i] * (st[s_at, i + 1] - s)
        part_g += CONDUCT * st[s_at + 1, i + 1]
    return rs + part_s - fy_out * s, rg + part_g - FLOW * g


def pair_x(v):
    row = lax.broadcasted_iota(jnp.int32, v.shape, 0)
    return v + jnp.where(row % 2 == 0, up_x(v), down_x(v))


def coarse_coefficients(c_sum, k_sum):
    solid = 4.0 * SOLID_CAP + c_sum + LUMP * k_sum
    ratio = c_sum / solid
    denominator = (4.0 * GAS_CAP + 2.0 * FLOW) + c_sum - c_sum * ratio
    return solid, ratio, denominator


def coarse_row(st, coarse, j, mask, edge):
    i = 2 * j + 1
    res_s, res_g = row_residual(st, i, SA, edge)
    more_s, more_g = row_residual(st, i + 1, SA, edge)
    res_s, res_g = pair_x((res_s + more_s) * mask), pair_x((res_g + more_g) * mask)
    c_sum = pair_x(st[C, i] + st[C, i + 1])
    solid, ratio, denominator = coarse_coefficients(c_sum, pair_x(st[K, i] + st[K, i + 1]))
    lead = res_s / solid
    values = (lead, ratio, (2.0 * FLOW) / denominator, (res_g + c_sum * lead) / denominator)
    return [(coarse, (k, j), v) for k, v in enumerate(values)]


def inner_kernel(st_in, one, two, early, st, coarse, *beside):
    del st_in, early
    planes, rows, ext, nz = st.shape
    ny, nx = rows - 2, ext - 2 * PAD
    shape = (ext, nz)
    mask = x_mask(shape, nx)
    edge = edge_weights(shape)
    for y in range(4, ny - 4):
        place_halo(st, one, two, y, nx)
    grouped(list(range(4, ny - 2)), lambda i: row_coefficients(st, i, mask))
    grouped(list(range(4, ny - 2)), lambda i: row_sweep(st, i, SA, SB, edge))
    grouped(list(range(3, ny - 1)), lambda i: row_sweep(st, i, SB, SA, edge))
    for j in range(2, ny // 2 - 2):
        for ref, at, value in coarse_row(st, coarse, j, mask, edge):
            ref[at] = value
    write_message(functools.partial(write_beside, beside), st, lax.axis_index("gy") % 2 == 0, edge)


def end_work(st, coarse, extra, read, outer, is_after):
    planes, rows, ext, nz = st.shape
    ny, nx = rows - 2, ext - 2 * PAD
    me, count = lax.axis_index("gy"), lax.axis_size("gy")
    mask = x_mask((ext, nz), nx)
    inside = jnp.where(me == (count - 1 if is_after else 0), 0.0, mask)
    edge = edge_weights((ext, nz))
    zeros = jnp.zeros((PAD, nz), jnp.float32)
    for k in range(MESSAGE):
        outer[k, :PAD] = zeros
        outer[k, ext - PAD :] = zeros
        read(outer, k)

    o, e, near = (ny + 1, ny, ny) if is_after else (0, 1, 0)
    to_o = CONDUCT + FLOW if is_after else CONDUCT
    s_o, g_o, k_o, c_o, fy_out = (outer[plane] for plane in (M_S, M_G, M_K, M_C, M_FY))
    fy = 0.5 * (k_o + st[K, e])
    fx, fz, h, diag = faces(k_o)
    inv_o = inverse(diag + c_o + fy_out + fy, c_o, inside)
    fx_e, fz_e = st[FX, e], st[FZ, e]
    diag = st[H, e] + (fx_e + down_x(fx_e)) + (fz_e + down_z(fz_e)) + st[C, e] + fy
    inv_e = inverse(diag + st[FY, near - 1 if is_after else near + 1], st[C, e], mask)
    for plane, value in ((SA, s_o), (GA, g_o), (K, k_o), (C, c_o), (FX, fx), (FZ, fz), (H, h)):
        st[plane, o] = value
    st[FY, near] = fy
    for k in range(3):
        st[ASS + k, o], st[ASS + k, e] = inv_o[k], inv_e[k]

    res = outer[M_1S] + fy * (st[SA, e] - s_o), outer[M_1G] + to_o * st[GA, e]
    new_o = relaxed(st, o, SA, *res)
    stores = row_sweep(st, e, SA, SB, edge)
    st[SB, o], st[GB, o] = new_o
    for ref, at, value in stores:
        ref[at] = value
    res = outer_residual(st, o, SB, outer[M_2S], outer[M_2G], fy_out, edge, is_after)
    new_o = relaxed(st, o, SB, *res)
    ends = [e - 1, e] if is_after else [e, e + 1]
    grouped(ends, lambda i: row_sweep(st, i, SB, SA, edge))
    st[SA, o], st[GA, o] = new_o
    for k, plane in enumerate((M_2S, M_2G, M_FY)):
        extra[(3 if is_after else 0) + k] = outer[plane]
    blocks = ny // 2
    stores = []
    for j in (blocks - 2, blocks - 1) if is_after else (0, 1):
        stores += coarse_row(st, coarse, j, mask, edge)
    for ref, at, value in stores:
        ref[at] = value


def either_end(after, st, coarse, extra, read, outer):
    for is_after in (True, False):

        @pl.when(after == is_after)
        def _():
            end_work(st, coarse, extra, read, outer, is_after)


def near_kernel(st_in, coarse_in, *refs):
    beside, (st, coarse, extra, outer) = refs[:-4], refs[-4:]
    del st_in, coarse_in
    either_end(lax.axis_index("gy") % 2 == 0, st, coarse, extra, functools.partial(read_beside, beside), outer)


def second_kernel(st_in, coarse_in, extra_in, early, across, *refs):
    st, coarse, extra, total, last_info, first_info, message, outer, squeeze = refs
    del st_in, coarse_in, extra_in
    planes, rows, ext, nz = st.shape
    ny, nx = rows - 2, ext - 2 * PAD
    me = lax.axis_index("gy")
    either_end(me % 2 == 1, st, coarse, extra, functools.partial(read_across, early, across), outer)

    blocks = ny // 2
    for k in range(4):
        squeeze[k] = coarse[k, 0]
    slopes, offsets = coarse[2, 0], coarse[3, 0]
    for j in range(1, blocks):
        slope = coarse[2, j]
        slopes, offsets = slope * slopes, slope * offsets + coarse[3, j]
        coarse[2, j], coarse[3, j] = slopes, offsets
    squeeze[4], squeeze[5], squeeze[6], squeeze[7] = slopes, offsets, coarse[0, blocks - 1], coarse[1, blocks - 1]

    span = nx // 2 + 2
    lead, ratio, slope, offset, slopes, offsets, lead_last, ratio_last = (
        squeeze[k, pl.ds(PAD - 2, span, 2), :] for k in range(8)
    )
    part = slice(PAD - 1, PAD + nx + 1)

    def increments(d, face, gas):
        return [(st[FY, face] * (st[SA, d] - st[SB, d]))[part], (gas * (st[GA, d] - st[GB, d]))[part]]

    onward = [lead_last, ratio_last] + increments(ny - 1, ny - 1, CONDUCT + FLOW)
    back = [lead, offset] + increments(2, 1, CONDUCT) + [slope, ratio]
    write_rows(total, [slopes, offsets])
    write_rows(last_info, onward)
    write_rows(first_info, back)
    for go, info in ((True, onward), (False, back)):

        @pl.when((me % 2 == 0) == go)
        def _():
            write_rows(message, [slopes, offsets] + info)


def write_rows(ref, values):
    at = 0
    for value in values:
        ref[at : at + value.shape[0]] = value
        at += value.shape[0]


class Rows:
    def __init__(self, nx):
        self.span = nx // 2 + 2
        self.map = 2 * self.span
        self.info = self.map + 2 * (nx + 2)
        self.rest = self.map
        self.final = self.map + self.info
        self.full = self.final + self.rest
        self.low = self.map
        self.high = self.low + self.info
        self.near = self.high + self.info + self.rest


def source(at, k, radix):
    if radix & (radix - 1) == 0:
        return at ^ k
    return (at + radix - k) % radix


def target(at, k, radix):
    return at ^ k if radix & (radix - 1) == 0 else (at + k) % radix


def order(radix):
    out = [(k, any(abs(source(at, k, radix) - at) == 1 for at in range(radix))) for k in range(1, radix)]
    return sorted(out, key=lambda item: (not item[1], -item[0]))


def stages(count):
    if count % 2:
        return [1, count]
    out, rest = [2], count // 2
    while rest > 1:
        radix = next((r for r in (8, 4, 2) if rest % r == 0), rest)
        out.append(radix)
        rest //= radix
    return out if len(out) > 1 else out + [1]


def exchange_stage(messages, radix, stride):
    count, got = lax.axis_size("gy"), []
    for (k, near), message in zip(order(radix), messages):
        pairs = []
        for me in range(count):
            at, low = me // stride % radix, me % stride
            sender = me - low + (source(at, k, radix) - at) * stride + (stride - 1 - low)
            pairs.append((sender, me))
        got.append(lax.ppermute(message, "gy", pairs))
    return got


class Group:
    def __init__(self, radix, stride, others, nx):
        self.radix, self.others, self.nx = radix, others, nx
        me = lax.axis_index("gy")
        self.at = lax.rem(lax.div(me, stride), radix)
        low = lax.rem(me, stride)
        self.lowest, self.highest = low == 0, low == stride - 1

    def map_of(self, place, own):
        rows = Rows(self.nx)
        out = own
        for (k, near), ref in zip(order(self.radix), self.others):
            here = source(self.at, k, self.radix) == place
            got = [ref[i * rows.span : (i + 1) * rows.span] for i in range(2)]
            out = got if out is None else [jnp.where(here, new, old) for new, old in zip(got, out)]
        return out

    def ahead(self, slope, offset):
        a, b = jnp.ones_like(slope), jnp.zeros_like(slope)
        for place in range(self.radix - 1):
            new_a, new_b = self.map_of(place, None)
            below = place < self.at
            a, b = jnp.where(below, new_a * a, a), jnp.where(below, new_a * b + new_b, b)
        return slope * a, slope * b + offset

    def total(self, own):
        a, b = self.map_of(0, own)
        for place in range(1, self.radix):
            new_a, new_b = self.map_of(place, own)
            a, b = new_a * a, new_a * b + new_b
        return a, b

    def collect(self, near, final):
        rows = Rows(self.nx)
        for (k, adjacent), ref in zip(order(self.radix), self.others):
            if not adjacent:
                continue
            place = source(self.at, k, self.radix)

            @pl.when(self.lowest & (place == self.at - 1))
            def _():
                near[rows.low : rows.low + rows.info] = ref[rows.map : rows.final]

            @pl.when(self.highest & (place == self.at + 1))
            def _():
                near[rows.high : rows.high + rows.info] = ref[rows.map : rows.final]
                rest = slice(0, rows.map) if final else slice(rows.final, rows.full)
                near[rows.high + rows.info : rows.near] = ref[rest]


def start_near(near, nx, nz):
    rows = Rows(nx)
    near[: rows.span] = jnp.ones((rows.span, nz), jnp.float32)
    near[rows.span :] = jnp.zeros((near.shape[0] - rows.span, nz), jnp.float32)


def join_kernel(radix, stride, final, nx, is_first, *refs):
    rows = Rows(nx)
    total, last_info, first_info, near_in = refs[:4]
    others, near, outs = refs[4 : 3 + radix], refs[3 + radix], refs[4 + radix :]
    nz = near.shape[1]
    if is_first:
        start_near(near, nx, nz)
    else:
        near[...] = near_in[...]
    group = Group(radix, stride, others, nx)
    own = [total[i * rows.span : (i + 1) * rows.span] for i in range(2)]
    ahead = group.ahead(near[: rows.span], near[rows.span : rows.map])
    write_rows(near, ahead)
    group.collect(near, False)
    whole = group.total(own)
    at = lax.div(lax.axis_index("gy"), stride * radix)
    if final == 0:
        write_rows(outs[0], whole)
        return
    at = lax.rem(at, final)
    for (k, adjacent), out in zip(order(final), outs):
        up = target(at, k, final) > at
        if not adjacent:
            write_rows(out, whole)
            continue

        @pl.when(up)
        def _():
            write_rows(out, whole)
            out[rows.map : rows.final] = last_info[: rows.info]

        @pl.when(jnp.logical_not(up))
        def _():
            out[: rows.map] = first_info[rows.info : rows.info + rows.rest]
            out[rows.map : rows.final] = first_info[: rows.info]


def full_message(nx, stride, radix, total, last_info, first_info, k):
    rows = Rows(nx)
    at = lax.axis_index("gy") // stride % radix
    onward = jnp.concatenate([total[: rows.map], last_info[: rows.info], first_info[rows.info : rows.info + rows.rest]])
    back = jnp.concatenate([total[: rows.map], first_info[: rows.info + rows.rest]])
    message = jnp.where(target(at, k, radix) > at, onward, back)
    return jnp.pad(message, ((0, -rows.full % 8), (0, 0)))


def third_kernel(radix, stride, *refs):
    st, extra, coarse, near_in = refs[:4]
    others, (out, sc, wide, near, done, sems) = refs[4 : 3 + radix], refs[3 + radix :]
    planes, rows, ext, nz = st.shape
    ny, nx = rows - 2, ext - 2 * PAD
    edge = edge_weights((ext, nz))
    blocks = ny // 2

    lay = Rows(nx)
    span = lay.span
    near[...] = near_in[...]
    group = Group(radix, stride, others, nx)
    if radix > 1:
        group.collect(near, True)
    gas_in = group.ahead(near[:span], near[span : lay.map])[1]
    at_high = lay.high + lay.info
    starts = [lay.low, lay.low + span, lay.high, lay.high + span, at_high, at_high + span]
    for k, v in enumerate([gas_in] + [near[start : start + span] for start in starts]):
        wide[k, : PAD - 2] = jnp.zeros((PAD - 2, nz), jnp.float32)
        wide[k, ext - PAD + 2 :] = jnp.zeros((PAD - 2, nz), jnp.float32)
        wide[k, pl.ds(PAD - 2, span, 2), :] = v
        wide[k, pl.ds(PAD - 1, span, 2), :] = v
    for k, start in enumerate((lay.low, lay.low + nx + 2, lay.high, lay.high + nx + 2)):
        start += lay.map
        wide[7 + k, :PAD] = jnp.zeros((PAD, nz), jnp.float32)
        wide[7 + k, ext - PAD :] = jnp.zeros((PAD, nz), jnp.float32)
        wide[7 + k, PAD - 1 : PAD + nx + 1] = near[start : start + nx + 2]

    gas_in = wide[0]
    last = ny + 1
    solid_low = wide[1] + wide[2] * gas_in
    sc[0, 0] = st[SA, 0] + solid_low
    sc[1, 0] = st[GA, 0] + gas_in

    def correct(j, carry):
        gas = coarse[2, j] * gas_in + coarse[3, j]
        solid = coarse[0, j] + coarse[1, j] * gas
        for i in (2 * j + 1, 2 * j + 2):
            sc[0, i] = st[SA, i] + solid
            sc[1, i] = st[GA, i] + gas
        return carry

    lax.fori_loop(0, blocks, correct, 0)
    gas = coarse[2, blocks - 1] * gas_in + coarse[3, blocks - 1]
    gas_high = wide[5] * gas + wide[4]
    solid_high = wide[3] + wide[6] * gas_high
    sc[0, last] = st[SA, last] + solid_high
    sc[1, last] = st[GA, last] + gas_high

    view = Fields(st, sc)
    for i, is_after, solid, gas in ((0, False, solid_low, gas_in), (last, True, solid_high, gas_high)):
        side = 3 if is_after else 0
        fy = extra[side + 2]
        to = 9 if is_after else 7
        rs = extra[side] + wide[to] + fy * solid
        rg = extra[side + 1] + wide[to + 1] + (CONDUCT if is_after else CONDUCT + FLOW) * gas
        res = outer_residual(view, i, SA, rs, rg, fy, edge, is_after)
        sc[2, i], sc[3, i] = relaxed(view, i, SA, *res)

    def sweep(k, carry):
        stores = []
        for r in range(GROUP):
            i = GROUP * k + 1 + r
            new_s, new_g = relaxed(view, i, SA, *row_residual(view, i, SA, edge))
            stores += [((2, i), new_s), ((3, i), new_g)]
        for at, value in stores:
            sc[at] = value
        return carry

    lax.fori_loop(0, ny // GROUP, sweep, 0)

    def leaving(k):
        part = pl.ds(GROUP * k, GROUP)
        return pltpu.make_async_copy(done.at[:, part], out.at[:, part], sems.at[k])

    def final(k, carry):
        stores = []
        for r in range(GROUP):
            i = GROUP * k + 1 + r
            new_s, new_g = last_relaxed(view, i, SB, edge, slice(PAD, PAD + nx))
            stores += [((0, i - 1), new_s), ((1, i - 1), new_g)]
        for at, value in stores:
            done[at] = value
        leaving(k).start()
        return carry

    lax.fori_loop(0, ny // GROUP, final, 0)
    for k in range(ny // GROUP):
        leaving(k).wait()


class Fields:
    def __init__(self, st, sc):
        self.st, self.sc = st, sc

    def __getitem__(self, at):
        return (self.sc if at[0] <= GB else self.st)[at]


def cost(rows, cells):
    return pl.CostEstimate(flops=50 * rows * cells, bytes_accessed=16 * 4 * rows * cells, transcendentals=0)


def swap(x, axis, first):
    pairs = []
    for i in range(first, lax.axis_size(axis) - 1, 2):
        pairs += [(i, i + 1), (i + 1, i)]
    return lax.ppermute(x, axis, pairs)


def shards(temps, right_side, exchange, coupling):
    temps, right_side = (jnp.transpose(a, (0, 2, 1, 3)) for a in (temps, right_side))
    exchange, coupling = (jnp.transpose(a, (1, 0, 2)) for a in (exchange, coupling))
    temps, right_side, exchange, coupling = (
        pltpu.with_memory_space_constraint(a, pltpu.HBM) for a in (temps, right_side, exchange, coupling)
    )
    ny, nx, nz = exchange.shape
    ext = nx + 2 * PAD
    f32 = functools.partial(jax.ShapeDtypeStruct, dtype=jnp.float32)

    strip = f32(((ny * STRIP_ROWS + 7) // 8 * 8, nz))
    scratch = [(2, 2, ny, 8, nz)] * 2 + [(2, ny, 8, nz)] * 2 + [(2, 2, nx, nz), (2, nx, nz), (2, nx, nz)]
    one, two, early = pl.pallas_call(
        pack_kernel,
        out_shape=(strip, strip, f32((EARLY, nx, nz))),
        in_specs=[HBM] * 4,
        out_specs=(VMEM,) * 3,
        scratch_shapes=[pltpu.VMEM(shape, jnp.float32) for shape in scratch] + [pltpu.SemaphoreType.DMA((11,))],
        compiler_params=PARAMS,
        name="pack_x",
    )(temps, right_side, exchange, coupling)
    one, two = swap(one, "gx", 0), swap(two, "gx", 1)
    early = swap(early, "gy", 1)

    state = f32((PLANES, ny + 2, ext, nz))

    def letter(planes):
        return f32((planes, ext - 2 * CROP, nz))

    st = pl.pallas_call(
        load_kernel,
        out_shape=state,
        in_specs=[HBM] * 4,
        out_specs=VMEM,
        scratch_shapes=[pltpu.SemaphoreType.DMA((6,))],
        compiler_params=PARAMS,
        cost_estimate=cost(2 * ny, ext * nz),
        name="load",
    )(temps, right_side, exchange, coupling)
    st, across = pl.pallas_call(
        first_kernel,
        out_shape=(state, letter(MESSAGE - EARLY + 1)),
        in_specs=[VMEM] * 3,
        out_specs=(VMEM,) * 2,
        input_output_aliases={0: 0},
        compiler_params=PARAMS,
        name="first",
    )(st, one, two)
    across = swap(across, "gy", 1)

    rows = f32((4, ny // 2, ext, nz))
    st, coarse, *beside = pl.pallas_call(
        inner_kernel,
        out_shape=(state, rows) + (letter(THIRD),) * (MESSAGE // THIRD),
        in_specs=[VMEM] * 4,
        out_specs=(VMEM,) * (2 + MESSAGE // THIRD),
        input_output_aliases={0: 0},
        compiler_params=PARAMS,
        cost_estimate=cost(4 * ny, ext * nz),
        name="inner",
    )(st, one, two, early)

    beside = [swap(part, "gy", 0) for part in beside]

    lay = Rows(nx)

    def tall(height):
        return f32(((height + 7) // 8 * 8, nz))

    letter_room = pltpu.VMEM((MESSAGE, ext, nz), jnp.float32)
    more = f32((6, ext, nz))
    st, coarse, extra = pl.pallas_call(
        near_kernel,
        out_shape=(state, rows, more),
        in_specs=[VMEM] * (2 + len(beside)),
        out_specs=(VMEM,) * 3,
        scratch_shapes=[letter_room],
        input_output_aliases={0: 0, 1: 1},
        compiler_params=PARAMS,
        name="near",
    )(st, coarse, *beside)
    st, coarse, extra, total, last_info, first_info, message = pl.pallas_call(
        second_kernel,
        out_shape=(state, rows, more, tall(lay.map), tall(lay.info), tall(lay.info + lay.rest), tall(lay.full)),
        in_specs=[VMEM] * 5,
        out_specs=(VMEM,) * 7,
        scratch_shapes=[letter_room, pltpu.VMEM((8, ext, nz), jnp.float32)],
        input_output_aliases={0: 0, 1: 1, 2: 2},
        compiler_params=PARAMS,
        name="second",
    )(st, coarse, extra, early, across)

    near, messages = total, [message]
    radices, stride = stages(lax.axis_size("gy")), 1
    for place, radix in enumerate(radices[:-1]):
        if place:
            messages = [full_message(nx, stride, radix, total, last_info, first_info, k) for k, _ in order(radix)]
        others = exchange_stage(messages, radix, stride)
        final = radices[-1] if place == len(radices) - 2 else 0
        outs = [tall(lay.final if adjacent else lay.map) for _, adjacent in order(final)] if final else [tall(lay.map)]
        near, *messages = pl.pallas_call(
            functools.partial(join_kernel, radix, stride, final, nx, place == 0),
            out_shape=(tall(lay.near), *outs),
            in_specs=[VMEM] * (3 + radix),
            out_specs=(VMEM,) * (1 + len(outs)),
            compiler_params=PARAMS,
            name="join",
        )(total, last_info, first_info, near, *others)
        total = total if final else messages[0]
        stride *= radix
    got = exchange_stage(messages, radices[-1], stride)

    out = pl.pallas_call(
        functools.partial(third_kernel, radices[-1], stride),
        out_shape=f32((2, ny, nx, nz)),
        in_specs=[VMEM] * (4 + len(got)),
        out_specs=HBM,
        scratch_shapes=[
            pltpu.VMEM((4, ny + 2, ext, nz), jnp.float32),
            pltpu.VMEM((11, ext, nz), jnp.float32),
            pltpu.VMEM(tall(lay.near).shape, jnp.float32),
            pltpu.VMEM((2, ny, nx, nz), jnp.float32),
            pltpu.SemaphoreType.DMA((ny // GROUP,)),
        ],
        compiler_params=PARAMS,
        name="third",
    )(st, extra, coarse, near, *got)
    return jnp.transpose(out, (0, 2, 1, 3))


def solution(mesh):
    return jax.shard_map(
        shards,
        mesh=mesh,
        in_specs=(
            P(None, "gx", "gy", None),
            P(None, "gx", "gy", None),
            P("gx", "gy", None),
            P("gx", "gy", None),
        ),
        out_specs=P(None, "gx", "gy", None),
        check_vma=False,
    )
```

```python
import functools

import jax
import jax.numpy as jnp
from jax import lax
from jax.experimental import pallas as pl
from jax.experimental.pallas import tpu as pltpu
from jax.sharding import PartitionSpec as P

SOLID_CAP, GAS_CAP, FLOW, CONDUCT, RELAX, LUMP = 0.5, 0.02, 40.0, 0.05, 0.8, 0.25
GAS_SELF = GAS_CAP + 4.5 * CONDUCT

PAD = 8
WX = 5
CROP = 4
(SA, GA, SB, GB, K, C, RS, RG, FX, FZ, H, FY, ASS, ASG, AGG) = range(15)
PLANES = 15
(M_S, M_G, M_K, M_C, M_FY, M_1S, M_1G, M_2S, M_2G) = range(9)
MESSAGE, EARLY, THIRD = 9, 5, 3

GROUP = 4

VMEM = pl.BlockSpec(memory_space=pltpu.VMEM)
HBM = pl.BlockSpec(memory_space=pltpu.HBM)
PARAMS = pltpu.CompilerParams(vmem_limit_bytes=40 * 1024 * 1024)


def up_x(v):
    return pltpu.roll(v, v.shape[0] - 1, 0)


def down_x(v):
    return pltpu.roll(v, 1, 0)


def up_z(v):
    return pltpu.roll(v, v.shape[1] - 1, 1)


def down_z(v):
    return pltpu.roll(v, 1, 1)


def lanes(shape):
    return lax.broadcasted_iota(jnp.int32, shape, 1)


def x_mask(shape, nx):
    row = lax.broadcasted_iota(jnp.int32, shape, 0)
    place, count = lax.axis_index("gx"), lax.axis_size("gx")
    low = jnp.where(place == 0, PAD, PAD - WX)
    high = jnp.where(place == count - 1, PAD + nx, PAD + nx + WX)
    return jnp.where((row >= low) & (row < high), 1.0, 0.0).astype(jnp.float32)


STRIP = ((SA, WX - 1), (GA, WX - 1), (K, WX), (RS, WX - 1), (RG, WX - 1), (C, WX - 1))
STRIP_ROWS = sum(width for plane, width in STRIP)


def conductivity_of(s, exchange):
    return 1.0 + 4.0 * exchange * s * s * s


def strip_values(s, g, k, rs, rg, c, low):
    out, inn = (WX - 1, WX - 2) if low else (8 - WX, 9 - WX)
    four = slice(0, WX - 1) if low else slice(9 - WX, 8)
    five = slice(0, WX) if low else slice(8 - WX, 8)
    row = lax.broadcasted_iota(jnp.int32, s.shape, 0)
    rs = rs + jnp.where(row == inn, 0.5 * (k[inn : inn + 1] + k[out : out + 1]) * s[out : out + 1], 0.0)
    rg = rg + jnp.where(row == inn, CONDUCT * g[out : out + 1], 0.0)
    return [s[four], g[four], k[five], rs[four], rg[four], c[four]]


def pack_kernel(temps, right, exchange, coupling, one, two, early, st, *scratch):
    pair_low, pair_high, single_low, single_high, rows_t, rows_e, rows_c, sems = scratch
    even = lax.axis_index("gx") % 2 == 0
    odd = lax.axis_index("gy") % 2 == 1
    ny, nx, nz = exchange.shape
    copies = []
    for k, ref in enumerate((temps, right, exchange, coupling)):
        low, high, at = (pair_low, pair_high, k) if k < 2 else (single_low, single_high, k - 2)
        lead = (slice(None),) * (ref.ndim - 2)
        copies.append(pltpu.make_async_copy(ref.at[lead + (slice(0, 8),)], low.at[at], sems.at[2 * k]))
        copies.append(pltpu.make_async_copy(ref.at[lead + (slice(nx - 8, nx),)], high.at[at], sems.at[2 * k + 1]))
    ends = pl.ds(jnp.where(odd, ny - 2, 0), 2)
    copies.append(pltpu.make_async_copy(temps.at[:, ends], rows_t, sems.at[8]))
    copies.append(pltpu.make_async_copy(exchange.at[ends], rows_e, sems.at[9]))
    copies.append(pltpu.make_async_copy(coupling.at[ends], rows_c, sems.at[10]))
    loads = []
    for k, (plane, ref) in enumerate(
        ((SA, temps.at[0]), (K, exchange), (GA, temps.at[1]), (RS, right.at[0]), (RG, right.at[1]), (C, coupling))
    ):
        to = st.at[plane, pl.ds(1, ny), pl.ds(PAD, nx)]
        loads.append(pltpu.make_async_copy(ref, to, sems.at[11 + k]))
    for copy in copies + loads:
        copy.start()
    for copy in copies:
        copy.wait()
    at = 0
    for y in range(ny):
        sides = []
        for pair, single, is_low in ((pair_low, single_low, True), (pair_high, single_high, False)):
            s, g, rs, rg = (pair[i, j, y] for i in range(2) for j in range(2))
            sides.append(strip_values(s, g, conductivity_of(s, single[0, y]), rs, rg, single[1, y], is_low))
        for low, high, (plane, width) in zip(*sides, STRIP):
            one[at : at + width] = jnp.where(even, high, low)
            two[at : at + width] = jnp.where(even, low, high)
            at += width
    k = [conductivity_of(rows_t[0, i], rows_e[i]) for i in range(2)]
    pick = lambda pair: jnp.where(odd, pair[1], pair[0])
    early[M_S], early[M_G] = pick([rows_t[0, i] for i in range(2)]), pick([rows_t[1, i] for i in range(2)])
    early[M_K], early[M_C], early[M_FY] = pick(k), pick([rows_c[i] for i in range(2)]), 0.5 * (k[0] + k[1])
    for copy in loads:
        copy.wait()


def conduct_kernel(st_in, st):
    del st_in
    planes, rows, ext, nz = st.shape
    own = slice(PAD, ext - PAD)
    zeros = jnp.zeros((PAD, nz), jnp.float32)
    for i in range(1, rows - 1):
        st[K, i, own] = conductivity_of(st[SA, i, own], st[K, i, own])
        for plane, width in STRIP:
            st[plane, i, :PAD] = zeros
            st[plane, i, ext - PAD :] = zeros


def place_halo(st, one, two, y, nx):
    even = lax.axis_index("gx") % 2 == 0
    at, i = y * STRIP_ROWS, y + 1
    for plane, width in STRIP:
        a, b = one[at : at + width], two[at : at + width]
        st[plane, i, PAD - width : PAD] = jnp.where(even, b, a)
        st[plane, i, PAD + nx : PAD + nx + width] = jnp.where(even, a, b)
        at += width


def inner(s, g, c, h, fx, fz, edge):
    t = c * (s - g)
    flux_x = fx * (up_x(s) - s)
    flux_z = fz * (up_z(s) - s)
    part_s = (flux_x - down_x(flux_x)) + (flux_z - down_z(flux_z)) - h * s - t
    part_g = (
        t
        - GAS_SELF * g
        + CONDUCT * (up_x(g) + down_x(g))
        + edge[0] * up_z(g)
        + edge[1] * down_z(g)
    )
    return part_s, part_g


def edge_weights(shape):
    lane = lanes(shape)
    weight = jnp.float32(0.25 * CONDUCT)
    return jnp.where(lane == shape[1] - 1, 0.0, weight), jnp.where(lane == 0, 0.0, weight)


def row_inner(st, i, s_at, edge):
    return inner(st[s_at, i], st[s_at + 1, i], st[C, i], st[H, i], st[FX, i], st[FZ, i], edge)


def row_residual(st, i, s_at, edge):
    part_s, part_g = row_inner(st, i, s_at, edge)
    s, g, before = st[s_at, i], st[s_at + 1, i], st[s_at + 1, i - 1]
    part_s += st[FY, i] * (st[s_at, i + 1] - s) + st[FY, i - 1] * (st[s_at, i - 1] - s)
    part_g += CONDUCT * (st[s_at + 1, i + 1] + before) - FLOW * (g - before)
    return st[RS, i] + part_s, st[RG, i] + part_g


def relaxed(st, i, s_at, res_s, res_g):
    s = st[s_at, i] + st[ASS, i] * res_s + st[ASG, i] * res_g
    g = st[s_at + 1, i] + st[ASG, i] * res_s + st[AGG, i] * res_g
    return s, g


def faces(k):
    lane = lanes(k.shape)
    end = k.shape[1] - 1
    fx = 0.5 * (k + up_x(k))
    fz = jnp.where(lane == end, 0.0, 0.125 * (k + up_z(k)))
    h = SOLID_CAP + jnp.where((lane == 0) | (lane == end), 0.125 * k, 0.0)
    return fx, fz, h, h + (fx + down_x(fx)) + (fz + down_z(fz))


def inverse(diag, c, mask):
    gas_diag = (GAS_SELF + FLOW) + c
    inv = (RELAX * mask) / (diag * gas_diag - c * c)
    return inv * gas_diag, inv * c, inv * diag


def last_relaxed(st, i, s_at, edge, own):
    full_s, full_g = st[s_at, i], st[s_at + 1, i]
    s, g = full_s[own], full_g[own]
    flux_x = st[FX, i] * (up_x(full_s) - full_s)
    flux_z = st[FZ, i, own] * (up_z(s) - s)
    c, before = st[C, i, own], st[s_at + 1, i - 1, own]
    t = c * (s - g)
    res_s = st[RS, i, own] + (flux_x[own] - down_x(flux_x)[own]) + (flux_z - down_z(flux_z)) - st[H, i, own] * s - t
    res_s += st[FY, i, own] * (st[s_at, i + 1, own] - s) + st[FY, i - 1, own] * (st[s_at, i - 1, own] - s)
    res_g = st[RG, i, own] + t - GAS_SELF * g + edge[0][own] * up_z(g) + edge[1][own] * down_z(g)
    res_g += CONDUCT * (up_x(full_g)[own] + down_x(full_g)[own] + st[s_at + 1, i + 1, own] + before) - FLOW * (g - before)
    ss, sg, gg = st[ASS, i, own], st[ASG, i, own], st[AGG, i, own]
    return s + ss * res_s + sg * res_g, g + sg * res_s + gg * res_g


def grouped(rows, work):
    for start in range(0, len(rows), GROUP):
        stores = []
        for i in rows[start : start + GROUP]:
            stores += work(i)
        for ref, at, value in stores:
            ref[at] = value


def row_coefficients(st, i, mask):
    fx, fz, h, diag = faces(st[K, i])
    fy = 0.5 * (st[K, i] + st[K, i + 1])
    before = 0.5 * (st[K, i] + st[K, i - 1])
    ss, sg, gg = inverse(diag + st[C, i] + fy + before, st[C, i], mask)
    values = ((FX, fx), (FZ, fz), (H, h), (FY, fy), (ASS, ss), (ASG, sg), (AGG, gg))
    return [(st, (plane, i), v) for plane, v in values]


def row_sweep(st, i, source, target, edge):
    s, g = relaxed(st, i, source, *row_residual(st, i, source, edge))
    return [(st, (target, i), s), (st, (target + 1, i), g)]


def send_planes(st, onward, edge):
    ny = st.shape[1] - 2
    e, d, near = (ny, ny - 1, ny - 1) if onward else (1, 2, 1)
    fy, s, g, g_d = st[FY, near], st[SA, e], st[GA, e], st[GA, d]
    part_s, part_g = row_inner(st, e, SA, edge)
    m_1s = st[RS, e] + part_s + fy * (st[SA, d] - s)
    m_1g = st[RG, e] + part_g + CONDUCT * g_d - FLOW * (g - g_d if onward else g)
    m_2s = st[RS, e] + fy * st[SB, d]
    m_2g = st[RG, e] + (CONDUCT + FLOW if onward else CONDUCT) * st[GB, d]
    return [s, g, st[K, e], st[C, e], fy, m_1s, m_1g, m_2s, m_2g]


def write_across(ref, k, value):
    ext = value.shape[0]
    if k >= EARLY:
        ref[k - EARLY] = value[CROP : ext - CROP]
    else:
        ref[MESSAGE - EARLY, 8 * k : 8 * k + 4] = value[CROP:PAD]
        ref[MESSAGE - EARLY, 8 * k + 4 : 8 * k + 8] = value[ext - PAD : ext - CROP]


def read_across(early, across, outer, k):
    ext = outer.shape[1]
    if k >= EARLY:
        outer[k, CROP : ext - CROP] = across[k - EARLY]
    else:
        outer[k, PAD : ext - PAD] = early[k]
        outer[k, CROP:PAD] = across[MESSAGE - EARLY, 8 * k : 8 * k + 4]
        outer[k, ext - PAD : ext - CROP] = across[MESSAGE - EARLY, 8 * k + 4 : 8 * k + 8]


def write_beside(refs, k, value):
    refs[k // THIRD][k % THIRD] = value[CROP : value.shape[0] - CROP]


def read_beside(refs, outer, k):
    outer[k, CROP : outer.shape[1] - CROP] = refs[k // THIRD][k % THIRD]


def write_message(write, st, onward, edge):
    for go in (True, False):

        @pl.when(onward == go)
        def _():
            for k, value in enumerate(send_planes(st, go, edge)):
                write(k, value)


def first_kernel(st_in, one, two, st, across):
    del st_in
    planes, rows, ext, nz = st.shape
    ny, nx = rows - 2, ext - 2 * PAD
    shape = (ext, nz)
    mask = x_mask(shape, nx)
    edge = edge_weights(shape)

    for y in list(range(4)) + list(range(ny - 4, ny)):
        place_halo(st, one, two, y, nx)
    for i in (1, ny):
        fx, fz, h, diag = faces(st[K, i])
        st[FX, i], st[FZ, i], st[H, i] = fx, fz, h
    st[FY, 1] = 0.5 * (st[K, 1] + st[K, 2])
    st[FY, ny - 3] = 0.5 * (st[K, ny - 3] + st[K, ny - 2])
    ends = [2, 3, ny - 2, ny - 1]
    grouped(ends, lambda i: row_coefficients(st, i, mask))
    grouped(ends, lambda i: row_sweep(st, i, SA, SB, edge))
    write_message(functools.partial(write_across, across), st, lax.axis_index("gy") % 2 == 1, edge)


def outer_residual(st, i, s_at, rs, rg, fy_out, edge, after):
    part_s, part_g = row_inner(st, i, s_at, edge)
    s, g = st[s_at, i], st[s_at + 1, i]
    if after:
        part_s += st[FY, i - 1] * (st[s_at, i - 1] - s)
        part_g += (CONDUCT + FLOW) * st[s_at + 1, i - 1]
    else:
        part_s += st[FY, i] * (st[s_at, i + 1] - s)
        part_g += CONDUCT * st[s_at + 1, i + 1]
    return rs + part_s - fy_out * s, rg + part_g - FLOW * g


def pair_x(v):
    row = lax.broadcasted_iota(jnp.int32, v.shape, 0)
    return v + jnp.where(row % 2 == 0, up_x(v), down_x(v))


def coarse_coefficients(c_sum, k_sum):
    solid = 4.0 * SOLID_CAP + c_sum + LUMP * k_sum
    ratio = c_sum / solid
    denominator = (4.0 * GAS_CAP + 2.0 * FLOW) + c_sum - c_sum * ratio
    return solid, ratio, denominator


def coarse_row(st, coarse, j, mask, edge):
    i = 2 * j + 1
    res_s, res_g = row_residual(st, i, SA, edge)
    more_s, more_g = row_residual(st, i + 1, SA, edge)
    res_s, res_g = pair_x((res_s + more_s) * mask), pair_x((res_g + more_g) * mask)
    c_sum = pair_x(st[C, i] + st[C, i + 1])
    solid, ratio, denominator = coarse_coefficients(c_sum, pair_x(st[K, i] + st[K, i + 1]))
    lead = res_s / solid
    values = (lead, ratio, (2.0 * FLOW) / denominator, (res_g + c_sum * lead) / denominator)
    return [(coarse, (k, j), v) for k, v in enumerate(values)]


def inner_kernel(st_in, one, two, early, st, coarse, *beside):
    del st_in, early
    planes, rows, ext, nz = st.shape
    ny, nx = rows - 2, ext - 2 * PAD
    shape = (ext, nz)
    mask = x_mask(shape, nx)
    edge = edge_weights(shape)
    for y in range(4, ny - 4):
        place_halo(st, one, two, y, nx)
    grouped(list(range(4, ny - 2)), lambda i: row_coefficients(st, i, mask))
    grouped(list(range(4, ny - 2)), lambda i: row_sweep(st, i, SA, SB, edge))
    grouped(list(range(3, ny - 1)), lambda i: row_sweep(st, i, SB, SA, edge))
    for j in range(2, ny // 2 - 2):
        for ref, at, value in coarse_row(st, coarse, j, mask, edge):
            ref[at] = value
    write_message(functools.partial(write_beside, beside), st, lax.axis_index("gy") % 2 == 0, edge)


def end_work(st, coarse, extra, read, outer, is_after):
    planes, rows, ext, nz = st.shape
    ny, nx = rows - 2, ext - 2 * PAD
    me, count = lax.axis_index("gy"), lax.axis_size("gy")
    mask = x_mask((ext, nz), nx)
    inside = jnp.where(me == (count - 1 if is_after else 0), 0.0, mask)
    edge = edge_weights((ext, nz))
    zeros = jnp.zeros((PAD, nz), jnp.float32)
    for k in range(MESSAGE):
        outer[k, :PAD] = zeros
        outer[k, ext - PAD :] = zeros
        read(outer, k)

    o, e, near = (ny + 1, ny, ny) if is_after else (0, 1, 0)
    to_o = CONDUCT + FLOW if is_after else CONDUCT
    s_o, g_o, k_o, c_o, fy_out = (outer[plane] for plane in (M_S, M_G, M_K, M_C, M_FY))
    fy = 0.5 * (k_o + st[K, e])
    fx, fz, h, diag = faces(k_o)
    inv_o = inverse(diag + c_o + fy_out + fy, c_o, inside)
    fx_e, fz_e = st[FX, e], st[FZ, e]
    diag = st[H, e] + (fx_e + down_x(fx_e)) + (fz_e + down_z(fz_e)) + st[C, e] + fy
    inv_e = inverse(diag + st[FY, near - 1 if is_after else near + 1], st[C, e], mask)
    for plane, value in ((SA, s_o), (GA, g_o), (K, k_o), (C, c_o), (FX, fx), (FZ, fz), (H, h)):
        st[plane, o] = value
    st[FY, near] = fy
    for k in range(3):
        st[ASS + k, o], st[ASS + k, e] = inv_o[k], inv_e[k]

    res = outer[M_1S] + fy * (st[SA, e] - s_o), outer[M_1G] + to_o * st[GA, e]
    new_o = relaxed(st, o, SA, *res)
    stores = row_sweep(st, e, SA, SB, edge)
    st[SB, o], st[GB, o] = new_o
    for ref, at, value in stores:
        ref[at] = value
    res = outer_residual(st, o, SB, outer[M_2S], outer[M_2G], fy_out, edge, is_after)
    new_o = relaxed(st, o, SB, *res)
    ends = [e - 1, e] if is_after else [e, e + 1]
    grouped(ends, lambda i: row_sweep(st, i, SB, SA, edge))
    st[SA, o], st[GA, o] = new_o
    for k, plane in enumerate((M_2S, M_2G, M_FY)):
        extra[(3 if is_after else 0) + k] = outer[plane]
    blocks = ny // 2
    stores = []
    for j in (blocks - 2, blocks - 1) if is_after else (0, 1):
        stores += coarse_row(st, coarse, j, mask, edge)
    for ref, at, value in stores:
        ref[at] = value


def either_end(after, st, coarse, extra, read, outer):
    for is_after in (True, False):

        @pl.when(after == is_after)
        def _():
            end_work(st, coarse, extra, read, outer, is_after)


def near_kernel(st_in, coarse_in, *refs):
    beside, (st, coarse, extra, outer) = refs[:-4], refs[-4:]
    del st_in, coarse_in
    either_end(lax.axis_index("gy") % 2 == 0, st, coarse, extra, functools.partial(read_beside, beside), outer)


def second_kernel(st_in, coarse_in, extra_in, early, across, *refs):
    st, coarse, extra, total, last_info, first_info, message, outer, squeeze = refs
    del st_in, coarse_in, extra_in
    planes, rows, ext, nz = st.shape
    ny, nx = rows - 2, ext - 2 * PAD
    me = lax.axis_index("gy")
    either_end(me % 2 == 1, st, coarse, extra, functools.partial(read_across, early, across), outer)

    blocks = ny // 2
    for k in range(4):
        squeeze[k] = coarse[k, 0]
    slopes, offsets = coarse[2, 0], coarse[3, 0]
    for j in range(1, blocks):
        slope = coarse[2, j]
        slopes, offsets = slope * slopes, slope * offsets + coarse[3, j]
        coarse[2, j], coarse[3, j] = slopes, offsets
    squeeze[4], squeeze[5], squeeze[6], squeeze[7] = slopes, offsets, coarse[0, blocks - 1], coarse[1, blocks - 1]

    span = nx // 2 + 2
    lead, ratio, slope, offset, slopes, offsets, lead_last, ratio_last = (
        squeeze[k, pl.ds(PAD - 2, span, 2), :] for k in range(8)
    )
    part = slice(PAD - 1, PAD + nx + 1)

    def increments(d, face, gas):
        return [(st[FY, face] * (st[SA, d] - st[SB, d]))[part], (gas * (st[GA, d] - st[GB, d]))[part]]

    onward = [lead_last, ratio_last] + increments(ny - 1, ny - 1, CONDUCT + FLOW)
    back = [lead, offset] + increments(2, 1, CONDUCT) + [slope, ratio]
    write_rows(total, [slopes, offsets])
    write_rows(last_info, onward)
    write_rows(first_info, back)
    for go, info in ((True, onward), (False, back)):

        @pl.when((me % 2 == 0) == go)
        def _():
            write_rows(message, [slopes, offsets] + info)


def write_rows(ref, values):
    at = 0
    for value in values:
        ref[at : at + value.shape[0]] = value
        at += value.shape[0]


class Rows:
    def __init__(self, nx):
        self.span = nx // 2 + 2
        self.map = 2 * self.span
        self.info = self.map + 2 * (nx + 2)
        self.rest = self.map
        self.final = self.map + self.info
        self.full = self.final + self.rest
        self.low = self.map
        self.high = self.low + self.info
        self.near = self.high + self.info + self.rest


def source(at, k, radix):
    if radix & (radix - 1) == 0:
        return at ^ k
    return (at + radix - k) % radix


def target(at, k, radix):
    return at ^ k if radix & (radix - 1) == 0 else (at + k) % radix


def order(radix):
    out = [(k, any(abs(source(at, k, radix) - at) == 1 for at in range(radix))) for k in range(1, radix)]
    return sorted(out, key=lambda item: (not item[1], -item[0]))


def stages(count):
    if count % 2:
        return [1, count]
    out, rest = [2], count // 2
    while rest > 1:
        radix = next((r for r in (8, 4, 2) if rest % r == 0), rest)
        out.append(radix)
        rest //= radix
    return out if len(out) > 1 else out + [1]


def exchange_stage(messages, radix, stride):
    count, got = lax.axis_size("gy"), []
    for (k, near), message in zip(order(radix), messages):
        pairs = []
        for me in range(count):
            at, low = me // stride % radix, me % stride
            sender = me - low + (source(at, k, radix) - at) * stride + (stride - 1 - low)
            pairs.append((sender, me))
        got.append(lax.ppermute(message, "gy", pairs))
    return got


class Group:
    def __init__(self, radix, stride, others, nx):
        self.radix, self.others, self.nx = radix, others, nx
        me = lax.axis_index("gy")
        self.at = lax.rem(lax.div(me, stride), radix)
        low = lax.rem(me, stride)
        self.lowest, self.highest = low == 0, low == stride - 1

    def map_of(self, place, own):
        rows = Rows(self.nx)
        out = own
        for (k, near), ref in zip(order(self.radix), self.others):
            here = source(self.at, k, self.radix) == place
            got = [ref[i * rows.span : (i + 1) * rows.span] for i in range(2)]
            out = got if out is None else [jnp.where(here, new, old) for new, old in zip(got, out)]
        return out

    def ahead(self, slope, offset):
        a, b = jnp.ones_like(slope), jnp.zeros_like(slope)
        for place in range(self.radix - 1):
            new_a, new_b = self.map_of(place, None)
            below = place < self.at
            a, b = jnp.where(below, new_a * a, a), jnp.where(below, new_a * b + new_b, b)
        return slope * a, slope * b + offset

    def total(self, own):
        a, b = self.map_of(0, own)
        for place in range(1, self.radix):
            new_a, new_b = self.map_of(place, own)
            a, b = new_a * a, new_a * b + new_b
        return a, b

    def collect(self, near, final):
        rows = Rows(self.nx)
        for (k, adjacent), ref in zip(order(self.radix), self.others):
            if not adjacent:
                continue
            place = source(self.at, k, self.radix)

            @pl.when(self.lowest & (place == self.at - 1))
            def _():
                near[rows.low : rows.low + rows.info] = ref[rows.map : rows.final]

            @pl.when(self.highest & (place == self.at + 1))
            def _():
                near[rows.high : rows.high + rows.info] = ref[rows.map : rows.final]
                rest = slice(0, rows.map) if final else slice(rows.final, rows.full)
                near[rows.high + rows.info : rows.near] = ref[rest]


def start_near(near, nx, nz):
    rows = Rows(nx)
    near[: rows.span] = jnp.ones((rows.span, nz), jnp.float32)
    near[rows.span :] = jnp.zeros((near.shape[0] - rows.span, nz), jnp.float32)


def join_kernel(radix, stride, final, nx, is_first, *refs):
    rows = Rows(nx)
    total, last_info, first_info, near_in = refs[:4]
    others, near, outs = refs[4 : 3 + radix], refs[3 + radix], refs[4 + radix :]
    nz = near.shape[1]
    if is_first:
        start_near(near, nx, nz)
    else:
        near[...] = near_in[...]
    group = Group(radix, stride, others, nx)
    own = [total[i * rows.span : (i + 1) * rows.span] for i in range(2)]
    ahead = group.ahead(near[: rows.span], near[rows.span : rows.map])
    write_rows(near, ahead)
    group.collect(near, False)
    whole = group.total(own)
    at = lax.div(lax.axis_index("gy"), stride * radix)
    if final == 0:
        write_rows(outs[0], whole)
        return
    at = lax.rem(at, final)
    for (k, adjacent), out in zip(order(final), outs):
        up = target(at, k, final) > at
        if not adjacent:
            write_rows(out, whole)
            continue

        @pl.when(up)
        def _():
            write_rows(out, whole)
            out[rows.map : rows.final] = last_info[: rows.info]

        @pl.when(jnp.logical_not(up))
        def _():
            out[: rows.map] = first_info[rows.info : rows.info + rows.rest]
            out[rows.map : rows.final] = first_info[: rows.info]


def full_message(nx, stride, radix, total, last_info, first_info, k):
    rows = Rows(nx)
    at = lax.axis_index("gy") // stride % radix
    onward = jnp.concatenate([total[: rows.map], last_info[: rows.info], first_info[rows.info : rows.info + rows.rest]])
    back = jnp.concatenate([total[: rows.map], first_info[: rows.info + rows.rest]])
    message = jnp.where(target(at, k, radix) > at, onward, back)
    return jnp.pad(message, ((0, -rows.full % 8), (0, 0)))


def third_kernel(radix, stride, *refs):
    st, extra, coarse, near_in = refs[:4]
    others, (out, sc, wide, near, done, sems) = refs[4 : 3 + radix], refs[3 + radix :]
    planes, rows, ext, nz = st.shape
    ny, nx = rows - 2, ext - 2 * PAD
    edge = edge_weights((ext, nz))
    blocks = ny // 2

    lay = Rows(nx)
    span = lay.span
    near[...] = near_in[...]
    group = Group(radix, stride, others, nx)
    if radix > 1:
        group.collect(near, True)
    gas_in = group.ahead(near[:span], near[span : lay.map])[1]
    at_high = lay.high + lay.info
    starts = [lay.low, lay.low + span, lay.high, lay.high + span, at_high, at_high + span]
    for k, v in enumerate([gas_in] + [near[start : start + span] for start in starts]):
        wide[k, : PAD - 2] = jnp.zeros((PAD - 2, nz), jnp.float32)
        wide[k, ext - PAD + 2 :] = jnp.zeros((PAD - 2, nz), jnp.float32)
        wide[k, pl.ds(PAD - 2, span, 2), :] = v
        wide[k, pl.ds(PAD - 1, span, 2), :] = v
    for k, start in enumerate((lay.low, lay.low + nx + 2, lay.high, lay.high + nx + 2)):
        start += lay.map
        wide[7 + k, :PAD] = jnp.zeros((PAD, nz), jnp.float32)
        wide[7 + k, ext - PAD :] = jnp.zeros((PAD, nz), jnp.float32)
        wide[7 + k, PAD - 1 : PAD + nx + 1] = near[start : start + nx + 2]

    gas_in = wide[0]
    last = ny + 1
    solid_low = wide[1] + wide[2] * gas_in
    sc[0, 0] = st[SA, 0] + solid_low
    sc[1, 0] = st[GA, 0] + gas_in

    def correct(j, carry):
        gas = coarse[2, j] * gas_in + coarse[3, j]
        solid = coarse[0, j] + coarse[1, j] * gas
        for i in (2 * j + 1, 2 * j + 2):
            sc[0, i] = st[SA, i] + solid
            sc[1, i] = st[GA, i] + gas
        return carry

    lax.fori_loop(0, blocks, correct, 0)
    gas = coarse[2, blocks - 1] * gas_in + coarse[3, blocks - 1]
    gas_high = wide[5] * gas + wide[4]
    solid_high = wide[3] + wide[6] * gas_high
    sc[0, last] = st[SA, last] + solid_high
    sc[1, last] = st[GA, last] + gas_high

    view = Fields(st, sc)
    for i, is_after, solid, gas in ((0, False, solid_low, gas_in), (last, True, solid_high, gas_high)):
        side = 3 if is_after else 0
        fy = extra[side + 2]
        to = 9 if is_after else 7
        rs = extra[side] + wide[to] + fy * solid
        rg = extra[side + 1] + wide[to + 1] + (CONDUCT if is_after else CONDUCT + FLOW) * gas
        res = outer_residual(view, i, SA, rs, rg, fy, edge, is_after)
        sc[2, i], sc[3, i] = relaxed(view, i, SA, *res)

    def sweep(k, carry):
        stores = []
        for r in range(GROUP):
            i = GROUP * k + 1 + r
            new_s, new_g = relaxed(view, i, SA, *row_residual(view, i, SA, edge))
            stores += [((2, i), new_s), ((3, i), new_g)]
        for at, value in stores:
            sc[at] = value
        return carry

    lax.fori_loop(0, ny // GROUP, sweep, 0)

    def leaving(k):
        part = pl.ds(GROUP * k, GROUP)
        return pltpu.make_async_copy(done.at[:, part], out.at[:, part], sems.at[k])

    def final(k, carry):
        stores = []
        for r in range(GROUP):
            i = GROUP * k + 1 + r
            new_s, new_g = last_relaxed(view, i, SB, edge, slice(PAD, PAD + nx))
            stores += [((0, i - 1), new_s), ((1, i - 1), new_g)]
        for at, value in stores:
            done[at] = value
        leaving(k).start()
        return carry

    lax.fori_loop(0, ny // GROUP, final, 0)
    for k in range(ny // GROUP):
        leaving(k).wait()


class Fields:
    def __init__(self, st, sc):
        self.st, self.sc = st, sc

    def __getitem__(self, at):
        return (self.sc if at[0] <= GB else self.st)[at]


def cost(rows, cells):
    return pl.CostEstimate(flops=50 * rows * cells, bytes_accessed=16 * 4 * rows * cells, transcendentals=0)


def swap(x, axis, first):
    pairs = []
    for i in range(first, lax.axis_size(axis) - 1, 2):
        pairs += [(i, i + 1), (i + 1, i)]
    return lax.ppermute(x, axis, pairs)


def shards(temps, right_side, exchange, coupling):
    temps, right_side = (jnp.transpose(a, (0, 2, 1, 3)) for a in (temps, right_side))
    exchange, coupling = (jnp.transpose(a, (1, 0, 2)) for a in (exchange, coupling))
    temps, right_side, exchange, coupling = (
        pltpu.with_memory_space_constraint(a, pltpu.HBM) for a in (temps, right_side, exchange, coupling)
    )
    ny, nx, nz = exchange.shape
    ext = nx + 2 * PAD
    f32 = functools.partial(jax.ShapeDtypeStruct, dtype=jnp.float32)

    strip = f32(((ny * STRIP_ROWS + 7) // 8 * 8, nz))
    scratch = [(2, 2, ny, 8, nz)] * 2 + [(2, ny, 8, nz)] * 2 + [(2, 2, nx, nz), (2, nx, nz), (2, nx, nz)]
    state = f32((PLANES, ny + 2, ext, nz))
    one, two, early, st = pl.pallas_call(
        pack_kernel,
        out_shape=(strip, strip, f32((EARLY, nx, nz)), state),
        in_specs=[HBM] * 4,
        out_specs=(VMEM,) * 4,
        scratch_shapes=[pltpu.VMEM(shape, jnp.float32) for shape in scratch] + [pltpu.SemaphoreType.DMA((17,))],
        compiler_params=PARAMS,
        name="pack_x",
    )(temps, right_side, exchange, coupling)
    one, two = swap(one, "gx", 0), swap(two, "gx", 1)
    early = swap(early, "gy", 1)

    def letter(planes):
        return f32((planes, ext - 2 * CROP, nz))

    st = pl.pallas_call(
        conduct_kernel,
        out_shape=state,
        in_specs=[VMEM],
        out_specs=VMEM,
        input_output_aliases={0: 0},
        compiler_params=PARAMS,
        cost_estimate=cost(2 * ny, ext * nz),
        name="conduct",
    )(st)
    st, across = pl.pallas_call(
        first_kernel,
        out_shape=(state, letter(MESSAGE - EARLY + 1)),
        in_specs=[VMEM] * 3,
        out_specs=(VMEM,) * 2,
        input_output_aliases={0: 0},
        compiler_params=PARAMS,
        name="first",
    )(st, one, two)
    across = swap(across, "gy", 1)

    rows = f32((4, ny // 2, ext, nz))
    st, coarse, *beside = pl.pallas_call(
        inner_kernel,
        out_shape=(state, rows) + (letter(THIRD),) * (MESSAGE // THIRD),
        in_specs=[VMEM] * 4,
        out_specs=(VMEM,) * (2 + MESSAGE // THIRD),
        input_output_aliases={0: 0},
        compiler_params=PARAMS,
        cost_estimate=cost(4 * ny, ext * nz),
        name="inner",
    )(st, one, two, early)

    beside = [swap(part, "gy", 0) for part in beside]

    lay = Rows(nx)

    def tall(height):
        return f32(((height + 7) // 8 * 8, nz))

    letter_room = pltpu.VMEM((MESSAGE, ext, nz), jnp.float32)
    more = f32((6, ext, nz))
    st, coarse, extra = pl.pallas_call(
        near_kernel,
        out_shape=(state, rows, more),
        in_specs=[VMEM] * (2 + len(beside)),
        out_specs=(VMEM,) * 3,
        scratch_shapes=[letter_room],
        input_output_aliases={0: 0, 1: 1},
        compiler_params=PARAMS,
        name="near",
    )(st, coarse, *beside)
    st, coarse, extra, total, last_info, first_info, message = pl.pallas_call(
        second_kernel,
        out_shape=(state, rows, more, tall(lay.map), tall(lay.info), tall(lay.info + lay.rest), tall(lay.full)),
        in_specs=[VMEM] * 5,
        out_specs=(VMEM,) * 7,
        scratch_shapes=[letter_room, pltpu.VMEM((8, ext, nz), jnp.float32)],
        input_output_aliases={0: 0, 1: 1, 2: 2},
        compiler_params=PARAMS,
        name="second",
    )(st, coarse, extra, early, across)

    near, messages = total, [message]
    radices, stride = stages(lax.axis_size("gy")), 1
    for place, radix in enumerate(radices[:-1]):
        if place:
            messages = [full_message(nx, stride, radix, total, last_info, first_info, k) for k, _ in order(radix)]
        others = exchange_stage(messages, radix, stride)
        final = radices[-1] if place == len(radices) - 2 else 0
        outs = [tall(lay.final if adjacent else lay.map) for _, adjacent in order(final)] if final else [tall(lay.map)]
        near, *messages = pl.pallas_call(
            functools.partial(join_kernel, radix, stride, final, nx, place == 0),
            out_shape=(tall(lay.near), *outs),
            in_specs=[VMEM] * (3 + radix),
            out_specs=(VMEM,) * (1 + len(outs)),
            compiler_params=PARAMS,
            name="join",
        )(total, last_info, first_info, near, *others)
        total = total if final else messages[0]
        stride *= radix
    got = exchange_stage(messages, radices[-1], stride)

    out = pl.pallas_call(
        functools.partial(third_kernel, radices[-1], stride),
        out_shape=f32((2, ny, nx, nz)),
        in_specs=[VMEM] * (4 + len(got)),
        out_specs=HBM,
        scratch_shapes=[
            pltpu.VMEM((4, ny + 2, ext, nz), jnp.float32),
            pltpu.VMEM((11, ext, nz), jnp.float32),
            pltpu.VMEM(tall(lay.near).shape, jnp.float32),
            pltpu.VMEM((2, ny, nx, nz), jnp.float32),
            pltpu.SemaphoreType.DMA((ny // GROUP,)),
        ],
        compiler_params=PARAMS,
        name="third",
    )(st, extra, coarse, near, *got)
    return jnp.transpose(out, (0, 2, 1, 3))


def solution(mesh):
    return jax.shard_map(
        shards,
        mesh=mesh,
        in_specs=(
            P(None, "gx", "gy", None),
            P(None, "gx", "gy", None),
            P("gx", "gy", None),
            P("gx", "gy", None),
        ),
        out_specs=P(None, "gx", "gy", None),
        check_vma=False,
    )
```

```python
import functools

import jax
import jax.numpy as jnp
from jax import lax
from jax.experimental import pallas as pl
from jax.experimental.pallas import tpu as pltpu
from jax.sharding import PartitionSpec as P

SOLID_CAP, GAS_CAP, FLOW, CONDUCT, RELAX, LUMP = 0.5, 0.02, 40.0, 0.05, 0.8, 0.25
GAS_SELF = GAS_CAP + 4.5 * CONDUCT

PAD = 8
WX = 5
CROP = 4
(SA, GA, SB, GB, K, C, RS, RG, FX, FZ, H, FY, ASS, ASG, AGG) = range(15)
PLANES = 15
(M_S, M_G, M_K, M_C, M_FY, M_1S, M_1G, M_2S, M_2G) = range(9)
MESSAGE, EARLY, THIRD = 9, 7, 3

GROUP = 4

VMEM = pl.BlockSpec(memory_space=pltpu.VMEM)
HBM = pl.BlockSpec(memory_space=pltpu.HBM)
PARAMS = pltpu.CompilerParams(vmem_limit_bytes=40 * 1024 * 1024)


def up_x(v):
    return pltpu.roll(v, v.shape[0] - 1, 0)


def down_x(v):
    return pltpu.roll(v, 1, 0)


def up_z(v):
    return pltpu.roll(v, v.shape[1] - 1, 1)


def down_z(v):
    return pltpu.roll(v, 1, 1)


def lanes(shape):
    return lax.broadcasted_iota(jnp.int32, shape, 1)


def x_mask(shape, nx):
    row = lax.broadcasted_iota(jnp.int32, shape, 0)
    place, count = lax.axis_index("gx"), lax.axis_size("gx")
    low = jnp.where(place == 0, PAD, PAD - WX)
    high = jnp.where(place == count - 1, PAD + nx, PAD + nx + WX)
    return jnp.where((row >= low) & (row < high), 1.0, 0.0).astype(jnp.float32)


STRIP = ((SA, WX - 1), (GA, WX - 1), (K, WX), (RS, WX - 1), (RG, WX - 1), (C, WX - 1))
STRIP_ROWS = sum(width for plane, width in STRIP)


def conductivity_of(s, exchange):
    return 1.0 + 4.0 * exchange * s * s * s


def strip_values(s, g, k, rs, rg, c, low):
    out, inn = (WX - 1, WX - 2) if low else (8 - WX, 9 - WX)
    four = slice(0, WX - 1) if low else slice(9 - WX, 8)
    five = slice(0, WX) if low else slice(8 - WX, 8)
    row = lax.broadcasted_iota(jnp.int32, s.shape, 0)
    rs = rs + jnp.where(row == inn, 0.5 * (k[inn : inn + 1] + k[out : out + 1]) * s[out : out + 1], 0.0)
    rg = rg + jnp.where(row == inn, CONDUCT * g[out : out + 1], 0.0)
    return [s[four], g[four], k[five], rs[four], rg[four], c[four]]


def pack_kernel(temps, right, exchange, coupling, one, two, early, st, sems):
    even = lax.axis_index("gx") % 2 == 0
    odd = lax.axis_index("gy") % 2 == 1
    ny, nx, nz = exchange.shape
    copies = []
    for k, (plane, ref) in enumerate(
        ((SA, temps.at[0]), (K, exchange), (GA, temps.at[1]), (C, coupling), (RS, right.at[0]), (RG, right.at[1]))
    ):
        to = st.at[plane, pl.ds(1, ny), pl.ds(PAD, nx)]
        copies.append(pltpu.make_async_copy(ref, to, sems.at[k]))
    for copy in copies:
        copy.start()
    for copy in copies:
        copy.wait()
    at = 0
    for i in range(1, ny + 1):
        sides = []
        for start in (PAD, PAD + nx - 8):
            s, g, e, rs, rg, c = (st[plane, i, start : start + 8] for plane in (SA, GA, K, RS, RG, C))
            sides.append(strip_values(s, g, conductivity_of(s, e), rs, rg, c, start == PAD))
        for low, high, (plane, width) in zip(*sides, STRIP):
            one[at : at + width] = jnp.where(even, high, low)
            two[at : at + width] = jnp.where(even, low, high)
            at += width
    own = slice(PAD, PAD + nx)
    for is_odd, e, d in ((True, ny, ny - 1), (False, 1, 2)):

        @pl.when(odd == is_odd)
        def _():
            s, s_d, g, g_d = st[SA, e, own], st[SA, d, own], st[GA, e, own], st[GA, d, own]
            c, k, k_d = st[C, e, own], conductivity_of(s, st[K, e, own]), conductivity_of(s_d, st[K, d, own])
            fx, fz, h, _ = faces(k)
            fy = 0.5 * (k + k_d)
            part_s, part_g = inner(s, g, c, h, fx, fz, edge_weights((nx, nz)))
            m_1s, m_1g = first_partial(st[RS, e, own] + part_s, st[RG, e, own] + part_g, s, s_d, g, g_d, fy, is_odd)
            for plane, value in enumerate((s, g, k, c, fy, m_1s, m_1g)):
                early[plane] = value


def conduct_kernel(st_in, st):
    del st_in
    planes, rows, ext, nz = st.shape
    own = slice(PAD, ext - PAD)
    zeros = jnp.zeros((PAD, nz), jnp.float32)
    for i in range(1, rows - 1):
        st[K, i, own] = conductivity_of(st[SA, i, own], st[K, i, own])
        for plane, width in STRIP:
            st[plane, i, :PAD] = zeros
            st[plane, i, ext - PAD :] = zeros


def place_halo(st, one, two, y, nx):
    even = lax.axis_index("gx") % 2 == 0
    at, i = y * STRIP_ROWS, y + 1
    for plane, width in STRIP:
        a, b = one[at : at + width], two[at : at + width]
        st[plane, i, PAD - width : PAD] = jnp.where(even, b, a)
        st[plane, i, PAD + nx : PAD + nx + width] = jnp.where(even, a, b)
        at += width


def inner(s, g, c, h, fx, fz, edge):
    t = c * (s - g)
    flux_x = fx * (up_x(s) - s)
    flux_z = fz * (up_z(s) - s)
    part_s = (flux_x - down_x(flux_x)) + (flux_z - down_z(flux_z)) - h * s - t
    part_g = (
        t
        - GAS_SELF * g
        + CONDUCT * (up_x(g) + down_x(g))
        + edge[0] * up_z(g)
        + edge[1] * down_z(g)
    )
    return part_s, part_g


def edge_weights(shape):
    lane = lanes(shape)
    weight = jnp.float32(0.25 * CONDUCT)
    return jnp.where(lane == shape[1] - 1, 0.0, weight), jnp.where(lane == 0, 0.0, weight)


def row_inner(st, i, s_at, edge):
    return inner(st[s_at, i], st[s_at + 1, i], st[C, i], st[H, i], st[FX, i], st[FZ, i], edge)


def row_residual(st, i, s_at, edge):
    part_s, part_g = row_inner(st, i, s_at, edge)
    s, g, before = st[s_at, i], st[s_at + 1, i], st[s_at + 1, i - 1]
    part_s += st[FY, i] * (st[s_at, i + 1] - s) + st[FY, i - 1] * (st[s_at, i - 1] - s)
    part_g += CONDUCT * (st[s_at + 1, i + 1] + before) - FLOW * (g - before)
    return st[RS, i] + part_s, st[RG, i] + part_g


def relaxed(st, i, s_at, res_s, res_g):
    s = st[s_at, i] + st[ASS, i] * res_s + st[ASG, i] * res_g
    g = st[s_at + 1, i] + st[ASG, i] * res_s + st[AGG, i] * res_g
    return s, g


def faces(k):
    lane = lanes(k.shape)
    end = k.shape[1] - 1
    fx = 0.5 * (k + up_x(k))
    fz = jnp.where(lane == end, 0.0, 0.125 * (k + up_z(k)))
    h = SOLID_CAP + jnp.where((lane == 0) | (lane == end), 0.125 * k, 0.0)
    return fx, fz, h, h + (fx + down_x(fx)) + (fz + down_z(fz))


def inverse(diag, c, mask):
    gas_diag = (GAS_SELF + FLOW) + c
    inv = (RELAX * mask) / (diag * gas_diag - c * c)
    return inv * gas_diag, inv * c, inv * diag


def last_relaxed(st, i, s_at, edge, own):
    full_s, full_g = st[s_at, i], st[s_at + 1, i]
    s, g = full_s[own], full_g[own]
    flux_x = st[FX, i] * (up_x(full_s) - full_s)
    flux_z = st[FZ, i, own] * (up_z(s) - s)
    c, before = st[C, i, own], st[s_at + 1, i - 1, own]
    t = c * (s - g)
    res_s = st[RS, i, own] + (flux_x[own] - down_x(flux_x)[own]) + (flux_z - down_z(flux_z)) - st[H, i, own] * s - t
    res_s += st[FY, i, own] * (st[s_at, i + 1, own] - s) + st[FY, i - 1, own] * (st[s_at, i - 1, own] - s)
    res_g = st[RG, i, own] + t - GAS_SELF * g + edge[0][own] * up_z(g) + edge[1][own] * down_z(g)
    res_g += CONDUCT * (up_x(full_g)[own] + down_x(full_g)[own] + st[s_at + 1, i + 1, own] + before) - FLOW * (g - before)
    ss, sg, gg = st[ASS, i, own], st[ASG, i, own], st[AGG, i, own]
    return s + ss * res_s + sg * res_g, g + sg * res_s + gg * res_g


def grouped(rows, work):
    for start in range(0, len(rows), GROUP):
        stores = []
        for i in rows[start : start + GROUP]:
            stores += work(i)
        for ref, at, value in stores:
            ref[at] = value


def row_coefficients(st, i, mask):
    fx, fz, h, diag = faces(st[K, i])
    fy = 0.5 * (st[K, i] + st[K, i + 1])
    before = 0.5 * (st[K, i] + st[K, i - 1])
    ss, sg, gg = inverse(diag + st[C, i] + fy + before, st[C, i], mask)
    values = ((FX, fx), (FZ, fz), (H, h), (FY, fy), (ASS, ss), (ASG, sg), (AGG, gg))
    return [(st, (plane, i), v) for plane, v in values]


def row_sweep(st, i, source, target, edge):
    s, g = relaxed(st, i, source, *row_residual(st, i, source, edge))
    return [(st, (target, i), s), (st, (target + 1, i), g)]


def first_partial(res_s, res_g, s, s_d, g, g_d, fy, onward):
    return res_s + fy * (s_d - s), res_g + CONDUCT * g_d - FLOW * (g - g_d if onward else g)


def send_planes(st, onward, edge):
    ny = st.shape[1] - 2
    e, d, near = (ny, ny - 1, ny - 1) if onward else (1, 2, 1)
    fy, s, g, g_d = st[FY, near], st[SA, e], st[GA, e], st[GA, d]
    part_s, part_g = row_inner(st, e, SA, edge)
    m_1s, m_1g = first_partial(st[RS, e] + part_s, st[RG, e] + part_g, s, st[SA, d], g, g_d, fy, onward)
    m_2s = st[RS, e] + fy * st[SB, d]
    m_2g = st[RG, e] + (CONDUCT + FLOW if onward else CONDUCT) * st[GB, d]
    return [s, g, st[K, e], st[C, e], fy, m_1s, m_1g, m_2s, m_2g]


def across_parts(ext):
    parts, at = [], 0
    for k in range(EARLY, MESSAGE):
        parts.append((k, CROP, ext - CROP, at))
        at += ext - 2 * CROP
    for k in range(EARLY):
        more = 1 if k in (M_1S, M_1G) else 0
        for low, high in ((CROP, PAD + more), (ext - PAD - more, ext - CROP)):
            parts.append((k, low, high, at))
            at += high - low
    return parts, (at + 7) // 8 * 8


def write_across(ref, k, value):
    for plane, low, high, at in across_parts(value.shape[0])[0]:
        if plane == k:
            ref[at : at + high - low] = value[low:high]


def read_across(early, across, outer, k):
    ext = outer.shape[1]
    if k < EARLY:
        outer[k, PAD : ext - PAD] = early[k]
    for plane, low, high, at in across_parts(ext)[0]:
        if plane == k:
            outer[k, low:high] = across[at : at + high - low]


def write_beside(refs, k, value):
    refs[k // THIRD][k % THIRD] = value[CROP : value.shape[0] - CROP]


def read_beside(refs, outer, k):
    outer[k, CROP : outer.shape[1] - CROP] = refs[k // THIRD][k % THIRD]


def write_message(write, st, onward, edge):
    for go in (True, False):

        @pl.when(onward == go)
        def _():
            for k, value in enumerate(send_planes(st, go, edge)):
                write(k, value)


def first_kernel(st_in, one, two, st, across, *beside):
    del st_in
    planes, rows, ext, nz = st.shape
    ny, nx = rows - 2, ext - 2 * PAD
    shape = (ext, nz)
    mask = x_mask(shape, nx)
    edge = edge_weights(shape)

    for y in list(range(4)) + list(range(ny - 4, ny)):
        place_halo(st, one, two, y, nx)
    for i in (1, ny):
        fx, fz, h, diag = faces(st[K, i])
        st[FX, i], st[FZ, i], st[H, i] = fx, fz, h
    st[FY, 1] = 0.5 * (st[K, 1] + st[K, 2])
    st[FY, ny - 3] = 0.5 * (st[K, ny - 3] + st[K, ny - 2])
    ends = [2, 3, ny - 2, ny - 1]
    grouped(ends, lambda i: row_coefficients(st, i, mask))
    grouped(ends, lambda i: row_sweep(st, i, SA, SB, edge))
    odd = lax.axis_index("gy") % 2 == 1
    write_message(functools.partial(write_across, across), st, odd, edge)
    write_message(functools.partial(write_beside, beside), st, jnp.logical_not(odd), edge)


def outer_residual(st, i, s_at, rs, rg, fy_out, edge, after):
    part_s, part_g = row_inner(st, i, s_at, edge)
    s, g = st[s_at, i], st[s_at + 1, i]
    if after:
        part_s += st[FY, i - 1] * (st[s_at, i - 1] - s)
        part_g += (CONDUCT + FLOW) * st[s_at + 1, i - 1]
    else:
        part_s += st[FY, i] * (st[s_at, i + 1] - s)
        part_g += CONDUCT * st[s_at + 1, i + 1]
    return rs + part_s - fy_out * s, rg + part_g - FLOW * g


def pair_x(v):
    row = lax.broadcasted_iota(jnp.int32, v.shape, 0)
    return v + jnp.where(row % 2 == 0, up_x(v), down_x(v))


def coarse_coefficients(c_sum, k_sum):
    solid = 4.0 * SOLID_CAP + c_sum + LUMP * k_sum
    ratio = c_sum / solid
    denominator = (4.0 * GAS_CAP + 2.0 * FLOW) + c_sum - c_sum * ratio
    return solid, ratio, denominator


def coarse_row(st, coarse, j, mask, edge):
    i = 2 * j + 1
    res_s, res_g = row_residual(st, i, SA, edge)
    more_s, more_g = row_residual(st, i + 1, SA, edge)
    res_s, res_g = pair_x((res_s + more_s) * mask), pair_x((res_g + more_g) * mask)
    c_sum = pair_x(st[C, i] + st[C, i + 1])
    solid, ratio, denominator = coarse_coefficients(c_sum, pair_x(st[K, i] + st[K, i + 1]))
    lead = res_s / solid
    values = (lead, ratio, (2.0 * FLOW) / denominator, (res_g + c_sum * lead) / denominator)
    return [(coarse, (k, j), v) for k, v in enumerate(values)]


def inner_kernel(st_in, one, two, early, st, coarse):
    del st_in, early
    planes, rows, ext, nz = st.shape
    ny, nx = rows - 2, ext - 2 * PAD
    shape = (ext, nz)
    mask = x_mask(shape, nx)
    edge = edge_weights(shape)
    for y in range(4, ny - 4):
        place_halo(st, one, two, y, nx)
    grouped(list(range(4, ny - 2)), lambda i: row_coefficients(st, i, mask))
    grouped(list(range(4, ny - 2)), lambda i: row_sweep(st, i, SA, SB, edge))
    grouped(list(range(3, ny - 1)), lambda i: row_sweep(st, i, SB, SA, edge))
    for j in range(2, ny // 2 - 2):
        for ref, at, value in coarse_row(st, coarse, j, mask, edge):
            ref[at] = value


def end_work(st, coarse, extra, read, outer, is_after):
    planes, rows, ext, nz = st.shape
    ny, nx = rows - 2, ext - 2 * PAD
    me, count = lax.axis_index("gy"), lax.axis_size("gy")
    mask = x_mask((ext, nz), nx)
    inside = jnp.where(me == (count - 1 if is_after else 0), 0.0, mask)
    edge = edge_weights((ext, nz))
    zeros = jnp.zeros((PAD, nz), jnp.float32)
    for k in range(MESSAGE):
        outer[k, :PAD] = zeros
        outer[k, ext - PAD :] = zeros
        read(outer, k)

    o, e, near = (ny + 1, ny, ny) if is_after else (0, 1, 0)
    to_o = CONDUCT + FLOW if is_after else CONDUCT
    s_o, g_o, k_o, c_o, fy_out = (outer[plane] for plane in (M_S, M_G, M_K, M_C, M_FY))
    fy = 0.5 * (k_o + st[K, e])
    fx, fz, h, diag = faces(k_o)
    inv_o = inverse(diag + c_o + fy_out + fy, c_o, inside)
    fx_e, fz_e = st[FX, e], st[FZ, e]
    diag = st[H, e] + (fx_e + down_x(fx_e)) + (fz_e + down_z(fz_e)) + st[C, e] + fy
    inv_e = inverse(diag + st[FY, near - 1 if is_after else near + 1], st[C, e], mask)
    for plane, value in ((SA, s_o), (GA, g_o), (K, k_o), (C, c_o), (FX, fx), (FZ, fz), (H, h)):
        st[plane, o] = value
    st[FY, near] = fy
    for k in range(3):
        st[ASS + k, o], st[ASS + k, e] = inv_o[k], inv_e[k]

    res = outer[M_1S] + fy * (st[SA, e] - s_o), outer[M_1G] + to_o * st[GA, e]
    new_o = relaxed(st, o, SA, *res)
    stores = row_sweep(st, e, SA, SB, edge)
    st[SB, o], st[GB, o] = new_o
    for ref, at, value in stores:
        ref[at] = value
    res = outer_residual(st, o, SB, outer[M_2S], outer[M_2G], fy_out, edge, is_after)
    new_o = relaxed(st, o, SB, *res)
    ends = [e - 1, e] if is_after else [e, e + 1]
    grouped(ends, lambda i: row_sweep(st, i, SB, SA, edge))
    st[SA, o], st[GA, o] = new_o
    for k, plane in enumerate((M_2S, M_2G, M_FY)):
        extra[(3 if is_after else 0) + k] = outer[plane]
    blocks = ny // 2
    stores = []
    for j in (blocks - 2, blocks - 1) if is_after else (0, 1):
        stores += coarse_row(st, coarse, j, mask, edge)
    for ref, at, value in stores:
        ref[at] = value


def either_end(after, st, coarse, extra, read, outer):
    for is_after in (True, False):

        @pl.when(after == is_after)
        def _():
            end_work(st, coarse, extra, read, outer, is_after)


def near_kernel(st_in, coarse_in, *refs):
    beside, (st, coarse, extra, outer) = refs[:-4], refs[-4:]
    del st_in, coarse_in
    either_end(lax.axis_index("gy") % 2 == 0, st, coarse, extra, functools.partial(read_beside, beside), outer)


def second_kernel(st_in, coarse_in, extra_in, early, across, *refs):
    st, coarse, extra, total, last_info, first_info, message, outer, squeeze = refs
    del st_in, coarse_in, extra_in
    planes, rows, ext, nz = st.shape
    ny, nx = rows - 2, ext - 2 * PAD
    me = lax.axis_index("gy")
    either_end(me % 2 == 1, st, coarse, extra, functools.partial(read_across, early, across), outer)

    blocks = ny // 2
    for k in range(4):
        squeeze[k] = coarse[k, 0]
    slopes, offsets = coarse[2, 0], coarse[3, 0]
    for j in range(1, blocks):
        slope = coarse[2, j]
        slopes, offsets = slope * slopes, slope * offsets + coarse[3, j]
        coarse[2, j], coarse[3, j] = slopes, offsets
    squeeze[4], squeeze[5], squeeze[6], squeeze[7] = slopes, offsets, coarse[0, blocks - 1], coarse[1, blocks - 1]

    span = nx // 2 + 2
    lead, ratio, slope, offset, slopes, offsets, lead_last, ratio_last = (
        squeeze[k, pl.ds(PAD - 2, span, 2), :] for k in range(8)
    )
    part = slice(PAD - 1, PAD + nx + 1)

    def increments(d, face, gas):
        return [(st[FY, face] * (st[SA, d] - st[SB, d]))[part], (gas * (st[GA, d] - st[GB, d]))[part]]

    onward = [lead_last, ratio_last] + increments(ny - 1, ny - 1, CONDUCT + FLOW)
    back = [lead, offset] + increments(2, 1, CONDUCT) + [slope, ratio]
    write_rows(total, [slopes, offsets])
    write_rows(last_info, onward)
    write_rows(first_info, back)
    for go, info in ((True, onward), (False, back)):

        @pl.when((me % 2 == 0) == go)
        def _():
            write_rows(message, [slopes, offsets] + info)


def write_rows(ref, values):
    at = 0
    for value in values:
        ref[at : at + value.shape[0]] = value
        at += value.shape[0]


class Rows:
    def __init__(self, nx):
        self.span = nx // 2 + 2
        self.map = 2 * self.span
        self.info = self.map + 2 * (nx + 2)
        self.rest = self.map
        self.final = self.map + self.info
        self.full = self.final + self.rest
        self.low = self.map
        self.high = self.low + self.info
        self.near = self.high + self.info + self.rest


def source(at, k, radix):
    if radix & (radix - 1) == 0:
        return at ^ k
    return (at + radix - k) % radix


def target(at, k, radix):
    return at ^ k if radix & (radix - 1) == 0 else (at + k) % radix


def order(radix):
    out = [(k, any(abs(source(at, k, radix) - at) == 1 for at in range(radix))) for k in range(1, radix)]
    return sorted(out, key=lambda item: (not item[1], -item[0]))


def stages(count):
    if count % 2:
        return [1, count]
    out, rest = [2], count // 2
    while rest > 1:
        radix = next((r for r in (8, 4, 2) if rest % r == 0), rest)
        out.append(radix)
        rest //= radix
    return out if len(out) > 1 else out + [1]


def exchange_stage(messages, radix, stride):
    count, got = lax.axis_size("gy"), []
    for (k, near), message in zip(order(radix), messages):
        pairs = []
        for me in range(count):
            at, low = me // stride % radix, me % stride
            sender = me - low + (source(at, k, radix) - at) * stride + (stride - 1 - low)
            pairs.append((sender, me))
        got.append(lax.ppermute(message, "gy", pairs))
    return got


class Group:
    def __init__(self, radix, stride, others, nx):
        self.radix, self.others, self.nx = radix, others, nx
        me = lax.axis_index("gy")
        self.at = lax.rem(lax.div(me, stride), radix)
        low = lax.rem(me, stride)
        self.lowest, self.highest = low == 0, low == stride - 1

    def map_of(self, place, own):
        rows = Rows(self.nx)
        out = own
        for (k, near), ref in zip(order(self.radix), self.others):
            here = source(self.at, k, self.radix) == place
            got = [ref[i * rows.span : (i + 1) * rows.span] for i in range(2)]
            out = got if out is None else [jnp.where(here, new, old) for new, old in zip(got, out)]
        return out

    def ahead(self, slope, offset):
        a, b = jnp.ones_like(slope), jnp.zeros_like(slope)
        for place in range(self.radix - 1):
            new_a, new_b = self.map_of(place, None)
            below = place < self.at
            a, b = jnp.where(below, new_a * a, a), jnp.where(below, new_a * b + new_b, b)
        return slope * a, slope * b + offset

    def total(self, own):
        a, b = self.map_of(0, own)
        for place in range(1, self.radix):
            new_a, new_b = self.map_of(place, own)
            a, b = new_a * a, new_a * b + new_b
        return a, b

    def collect(self, near, final):
        rows = Rows(self.nx)
        for (k, adjacent), ref in zip(order(self.radix), self.others):
            if not adjacent:
                continue
            place = source(self.at, k, self.radix)

            @pl.when(self.lowest & (place == self.at - 1))
            def _():
                near[rows.low : rows.low + rows.info] = ref[rows.map : rows.final]

            @pl.when(self.highest & (place == self.at + 1))
            def _():
                near[rows.high : rows.high + rows.info] = ref[rows.map : rows.final]
                rest = slice(0, rows.map) if final else slice(rows.final, rows.full)
                near[rows.high + rows.info : rows.near] = ref[rest]


def start_near(near, nx, nz):
    rows = Rows(nx)
    near[: rows.span] = jnp.ones((rows.span, nz), jnp.float32)
    near[rows.span :] = jnp.zeros((near.shape[0] - rows.span, nz), jnp.float32)


def join_kernel(radix, stride, final, nx, is_first, *refs):
    rows = Rows(nx)
    total, last_info, first_info, near_in = refs[:4]
    others, near, outs = refs[4 : 3 + radix], refs[3 + radix], refs[4 + radix :]
    nz = near.shape[1]
    if is_first:
        start_near(near, nx, nz)
    else:
        near[...] = near_in[...]
    group = Group(radix, stride, others, nx)
    own = [total[i * rows.span : (i + 1) * rows.span] for i in range(2)]
    ahead = group.ahead(near[: rows.span], near[rows.span : rows.map])
    write_rows(near, ahead)
    group.collect(near, False)
    whole = group.total(own)
    at = lax.div(lax.axis_index("gy"), stride * radix)
    if final == 0:
        write_rows(outs[0], whole)
        return
    at = lax.rem(at, final)
    for (k, adjacent), out in zip(order(final), outs):
        up = target(at, k, final) > at
        if not adjacent:
            write_rows(out, whole)
            continue

        @pl.when(up)
        def _():
            write_rows(out, whole)
            out[rows.map : rows.final] = last_info[: rows.info]

        @pl.when(jnp.logical_not(up))
        def _():
            out[: rows.map] = first_info[rows.info : rows.info + rows.rest]
            out[rows.map : rows.final] = first_info[: rows.info]


def full_message(nx, stride, radix, total, last_info, first_info, k):
    rows = Rows(nx)
    at = lax.axis_index("gy") // stride % radix
    onward = jnp.concatenate([total[: rows.map], last_info[: rows.info], first_info[rows.info : rows.info + rows.rest]])
    back = jnp.concatenate([total[: rows.map], first_info[: rows.info + rows.rest]])
    message = jnp.where(target(at, k, radix) > at, onward, back)
    return jnp.pad(message, ((0, -rows.full % 8), (0, 0)))


def third_kernel(radix, stride, *refs):
    st, extra, coarse, near_in = refs[:4]
    others, (out, sc, wide, near, done, sems) = refs[4 : 3 + radix], refs[3 + radix :]
    planes, rows, ext, nz = st.shape
    ny, nx = rows - 2, ext - 2 * PAD
    edge = edge_weights((ext, nz))
    blocks = ny // 2

    lay = Rows(nx)
    span = lay.span
    near[...] = near_in[...]
    group = Group(radix, stride, others, nx)
    if radix > 1:
        group.collect(near, True)
    gas_in = group.ahead(near[:span], near[span : lay.map])[1]
    at_high = lay.high + lay.info
    starts = [lay.low, lay.low + span, lay.high, lay.high + span, at_high, at_high + span]
    for k, v in enumerate([gas_in] + [near[start : start + span] for start in starts]):
        wide[k, : PAD - 2] = jnp.zeros((PAD - 2, nz), jnp.float32)
        wide[k, ext - PAD + 2 :] = jnp.zeros((PAD - 2, nz), jnp.float32)
        wide[k, pl.ds(PAD - 2, span, 2), :] = v
        wide[k, pl.ds(PAD - 1, span, 2), :] = v
    for k, start in enumerate((lay.low, lay.low + nx + 2, lay.high, lay.high + nx + 2)):
        start += lay.map
        wide[7 + k, :PAD] = jnp.zeros((PAD, nz), jnp.float32)
        wide[7 + k, ext - PAD :] = jnp.zeros((PAD, nz), jnp.float32)
        wide[7 + k, PAD - 1 : PAD + nx + 1] = near[start : start + nx + 2]

    gas_in = wide[0]
    last = ny + 1
    solid_low = wide[1] + wide[2] * gas_in
    sc[0, 0] = st[SA, 0] + solid_low
    sc[1, 0] = st[GA, 0] + gas_in

    def correct(j, carry):
        gas = coarse[2, j] * gas_in + coarse[3, j]
        solid = coarse[0, j] + coarse[1, j] * gas
        for i in (2 * j + 1, 2 * j + 2):
            sc[0, i] = st[SA, i] + solid
            sc[1, i] = st[GA, i] + gas
        return carry

    lax.fori_loop(0, blocks, correct, 0)
    gas = coarse[2, blocks - 1] * gas_in + coarse[3, blocks - 1]
    gas_high = wide[5] * gas + wide[4]
    solid_high = wide[3] + wide[6] * gas_high
    sc[0, last] = st[SA, last] + solid_high
    sc[1, last] = st[GA, last] + gas_high

    view = Fields(st, sc)
    for i, is_after, solid, gas in ((0, False, solid_low, gas_in), (last, True, solid_high, gas_high)):
        side = 3 if is_after else 0
        fy = extra[side + 2]
        to = 9 if is_after else 7
        rs = extra[side] + wide[to] + fy * solid
        rg = extra[side + 1] + wide[to + 1] + (CONDUCT if is_after else CONDUCT + FLOW) * gas
        res = outer_residual(view, i, SA, rs, rg, fy, edge, is_after)
        sc[2, i], sc[3, i] = relaxed(view, i, SA, *res)

    def sweep(k, carry):
        stores = []
        for r in range(GROUP):
            i = GROUP * k + 1 + r
            new_s, new_g = relaxed(view, i, SA, *row_residual(view, i, SA, edge))
            stores += [((2, i), new_s), ((3, i), new_g)]
        for at, value in stores:
            sc[at] = value
        return carry

    lax.fori_loop(0, ny // GROUP, sweep, 0)

    def leaving(k):
        part = pl.ds(GROUP * k, GROUP)
        return pltpu.make_async_copy(done.at[:, part], out.at[:, part], sems.at[k])

    def final(k, carry):
        stores = []
        for r in range(GROUP):
            i = GROUP * k + 1 + r
            new_s, new_g = last_relaxed(view, i, SB, edge, slice(PAD, PAD + nx))
            stores += [((0, i - 1), new_s), ((1, i - 1), new_g)]
        for at, value in stores:
            done[at] = value
        leaving(k).start()
        return carry

    lax.fori_loop(0, ny // GROUP, final, 0)
    for k in range(ny // GROUP):
        leaving(k).wait()


class Fields:
    def __init__(self, st, sc):
        self.st, self.sc = st, sc

    def __getitem__(self, at):
        return (self.sc if at[0] <= GB else self.st)[at]


def cost(rows, cells):
    return pl.CostEstimate(flops=50 * rows * cells, bytes_accessed=16 * 4 * rows * cells, transcendentals=0)


def swap(x, axis, first):
    pairs = []
    for i in range(first, lax.axis_size(axis) - 1, 2):
        pairs += [(i, i + 1), (i + 1, i)]
    return lax.ppermute(x, axis, pairs)


def shards(temps, right_side, exchange, coupling):
    temps, right_side = (jnp.transpose(a, (0, 2, 1, 3)) for a in (temps, right_side))
    exchange, coupling = (jnp.transpose(a, (1, 0, 2)) for a in (exchange, coupling))
    temps, right_side, exchange, coupling = (
        pltpu.with_memory_space_constraint(a, pltpu.HBM) for a in (temps, right_side, exchange, coupling)
    )
    ny, nx, nz = exchange.shape
    ext = nx + 2 * PAD
    f32 = functools.partial(jax.ShapeDtypeStruct, dtype=jnp.float32)

    strip = f32(((ny * STRIP_ROWS + 7) // 8 * 8, nz))
    state = f32((PLANES, ny + 2, ext, nz))
    one, two, early, st = pl.pallas_call(
        pack_kernel,
        out_shape=(strip, strip, f32((EARLY, nx, nz)), state),
        in_specs=[HBM] * 4,
        out_specs=(VMEM,) * 4,
        scratch_shapes=[pltpu.SemaphoreType.DMA((6,))],
        compiler_params=PARAMS,
        name="pack_x",
    )(temps, right_side, exchange, coupling)
    one, two = swap(one, "gx", 0), swap(two, "gx", 1)
    early = swap(early, "gy", 1)

    def letter(planes):
        return f32((planes, ext - 2 * CROP, nz))

    st = pl.pallas_call(
        conduct_kernel,
        out_shape=state,
        in_specs=[VMEM],
        out_specs=VMEM,
        input_output_aliases={0: 0},
        compiler_params=PARAMS,
        cost_estimate=cost(2 * ny, ext * nz),
        name="conduct",
    )(st)
    st, across, *beside = pl.pallas_call(
        first_kernel,
        out_shape=(state, f32((across_parts(ext)[1], nz))) + (letter(THIRD),) * (MESSAGE // THIRD),
        in_specs=[VMEM] * 3,
        out_specs=(VMEM,) * (2 + MESSAGE // THIRD),
        input_output_aliases={0: 0},
        compiler_params=PARAMS,
        name="first",
    )(st, one, two)
    across = swap(across, "gy", 1)

    rows = f32((4, ny // 2, ext, nz))
    st, coarse = pl.pallas_call(
        inner_kernel,
        out_shape=(state, rows),
        in_specs=[VMEM] * 4,
        out_specs=(VMEM,) * 2,
        input_output_aliases={0: 0},
        compiler_params=PARAMS,
        cost_estimate=cost(4 * ny, ext * nz),
        name="inner",
    )(st, one, two, early)

    beside = [swap(part, "gy", 0) for part in beside]

    lay = Rows(nx)

    def tall(height):
        return f32(((height + 7) // 8 * 8, nz))

    letter_room = pltpu.VMEM((MESSAGE, ext, nz), jnp.float32)
    more = f32((6, ext, nz))
    st, coarse, extra = pl.pallas_call(
        near_kernel,
        out_shape=(state, rows, more),
        in_specs=[VMEM] * (2 + len(beside)),
        out_specs=(VMEM,) * 3,
        scratch_shapes=[letter_room],
        input_output_aliases={0: 0, 1: 1},
        compiler_params=PARAMS,
        name="near",
    )(st, coarse, *beside)
    st, coarse, extra, total, last_info, first_info, message = pl.pallas_call(
        second_kernel,
        out_shape=(state, rows, more, tall(lay.map), tall(lay.info), tall(lay.info + lay.rest), tall(lay.full)),
        in_specs=[VMEM] * 5,
        out_specs=(VMEM,) * 7,
        scratch_shapes=[letter_room, pltpu.VMEM((8, ext, nz), jnp.float32)],
        input_output_aliases={0: 0, 1: 1, 2: 2},
        compiler_params=PARAMS,
        name="second",
    )(st, coarse, extra, early, across)

    near, messages = total, [message]
    radices, stride = stages(lax.axis_size("gy")), 1
    for place, radix in enumerate(radices[:-1]):
        if place:
            messages = [full_message(nx, stride, radix, total, last_info, first_info, k) for k, _ in order(radix)]
        others = exchange_stage(messages, radix, stride)
        final = radices[-1] if place == len(radices) - 2 else 0
        outs = [tall(lay.final if adjacent else lay.map) for _, adjacent in order(final)] if final else [tall(lay.map)]
        near, *messages = pl.pallas_call(
            functools.partial(join_kernel, radix, stride, final, nx, place == 0),
            out_shape=(tall(lay.near), *outs),
            in_specs=[VMEM] * (3 + radix),
            out_specs=(VMEM,) * (1 + len(outs)),
            compiler_params=PARAMS,
            name="join",
        )(total, last_info, first_info, near, *others)
        total = total if final else messages[0]
        stride *= radix
    got = exchange_stage(messages, radices[-1], stride)

    out = pl.pallas_call(
        functools.partial(third_kernel, radices[-1], stride),
        out_shape=f32((2, ny, nx, nz)),
        in_specs=[VMEM] * (4 + len(got)),
        out_specs=HBM,
        scratch_shapes=[
            pltpu.VMEM((4, ny + 2, ext, nz), jnp.float32),
            pltpu.VMEM((11, ext, nz), jnp.float32),
            pltpu.VMEM(tall(lay.near).shape, jnp.float32),
            pltpu.VMEM((2, ny, nx, nz), jnp.float32),
            pltpu.SemaphoreType.DMA((ny // GROUP,)),
        ],
        compiler_params=PARAMS,
        name="third",
    )(st, extra, coarse, near, *got)
    return jnp.transpose(out, (0, 2, 1, 3))


def solution(mesh):
    return jax.shard_map(
        shards,
        mesh=mesh,
        in_specs=(
            P(None, "gx", "gy", None),
            P(None, "gx", "gy", None),
            P("gx", "gy", None),
            P("gx", "gy", None),
        ),
        out_specs=P(None, "gx", "gy", None),
        check_vma=False,
    )
```

```python
import functools

import jax
import jax.numpy as jnp
from jax import lax
from jax.experimental import pallas as pl
from jax.experimental.pallas import tpu as pltpu
from jax.sharding import PartitionSpec as P

SOLID_CAP, GAS_CAP, FLOW, CONDUCT, RELAX, LUMP = 0.5, 0.02, 40.0, 0.05, 0.8, 0.25
GAS_SELF = GAS_CAP + 4.5 * CONDUCT

PAD = 8
WX = 5
CROP = 4
(SA, GA, SB, GB, K, C, RS, RG, FX, FZ, H, FY, ASS, ASG, AGG) = range(15)
PLANES = 15
(M_S, M_G, M_K, M_C, M_FY, M_1S, M_1G, M_2S, M_2G) = range(9)
MESSAGE, EARLY, THIRD = 9, 7, 3

GROUP = 4

VMEM = pl.BlockSpec(memory_space=pltpu.VMEM)
HBM = pl.BlockSpec(memory_space=pltpu.HBM)
PARAMS = pltpu.CompilerParams(vmem_limit_bytes=40 * 1024 * 1024)


def up_x(v):
    return pltpu.roll(v, v.shape[0] - 1, 0)


def down_x(v):
    return pltpu.roll(v, 1, 0)


def up_z(v):
    return pltpu.roll(v, v.shape[1] - 1, 1)


def down_z(v):
    return pltpu.roll(v, 1, 1)


def lanes(shape):
    return lax.broadcasted_iota(jnp.int32, shape, 1)


def x_mask(shape, nx):
    row = lax.broadcasted_iota(jnp.int32, shape, 0)
    place, count = lax.axis_index("gx"), lax.axis_size("gx")
    low = jnp.where(place == 0, PAD, PAD - WX)
    high = jnp.where(place == count - 1, PAD + nx, PAD + nx + WX)
    return jnp.where((row >= low) & (row < high), 1.0, 0.0).astype(jnp.float32)


STRIP = ((SA, WX - 1), (GA, WX - 1), (K, WX), (RS, WX - 1), (RG, WX - 1), (C, WX - 1))
STRIP_ROWS = sum(width for plane, width in STRIP)


def conductivity_of(s, exchange):
    return 1.0 + 4.0 * exchange * s * s * s


def strip_values(s, g, k, rs, rg, c, low):
    out, inn = (WX - 1, WX - 2) if low else (8 - WX, 9 - WX)
    four = slice(0, WX - 1) if low else slice(9 - WX, 8)
    five = slice(0, WX) if low else slice(8 - WX, 8)
    row = lax.broadcasted_iota(jnp.int32, s.shape, 0)
    rs = rs + jnp.where(row == inn, 0.5 * (k[inn : inn + 1] + k[out : out + 1]) * s[out : out + 1], 0.0)
    rg = rg + jnp.where(row == inn, CONDUCT * g[out : out + 1], 0.0)
    return [s[four], g[four], k[five], rs[four], rg[four], c[four]]


def pack_kernel(temps, right, exchange, coupling, one, two, early, st, sems):
    even = lax.axis_index("gx") % 2 == 0
    odd = lax.axis_index("gy") % 2 == 1
    ny, nx, nz = exchange.shape
    copies = []
    for k, (plane, ref) in enumerate(
        ((SA, temps.at[0]), (K, exchange), (GA, temps.at[1]), (C, coupling), (RS, right.at[0]), (RG, right.at[1]))
    ):
        to = st.at[plane, pl.ds(1, ny), pl.ds(PAD, nx)]
        copies.append(pltpu.make_async_copy(ref, to, sems.at[k]))
    for copy in copies:
        copy.start()
    for copy in copies:
        copy.wait()
    at = 0
    for i in range(1, ny + 1):
        sides = []
        for start in (PAD, PAD + nx - 8):
            s, g, e, rs, rg, c = (st[plane, i, start : start + 8] for plane in (SA, GA, K, RS, RG, C))
            sides.append(strip_values(s, g, conductivity_of(s, e), rs, rg, c, start == PAD))
        for low, high, (plane, width) in zip(*sides, STRIP):
            one[at : at + width] = jnp.where(even, high, low)
            two[at : at + width] = jnp.where(even, low, high)
            at += width
    own = slice(PAD, PAD + nx)
    for is_odd, e, d in ((True, ny, ny - 1), (False, 1, 2)):

        @pl.when(odd == is_odd)
        def _():
            s, s_d, g, g_d = st[SA, e, own], st[SA, d, own], st[GA, e, own], st[GA, d, own]
            c, k, k_d = st[C, e, own], conductivity_of(s, st[K, e, own]), conductivity_of(s_d, st[K, d, own])
            fx, fz, h, _ = faces(k)
            fy = 0.5 * (k + k_d)
            part_s, part_g = inner(s, g, c, h, fx, fz, edge_weights((nx, nz)))
            m_1s, m_1g = first_partial(st[RS, e, own] + part_s, st[RG, e, own] + part_g, s, s_d, g, g_d, fy, is_odd)
            for plane, value in enumerate((s, g, k, c, fy, m_1s, m_1g)):
                early[plane] = value


def conduct_kernel(st_in, st):
    del st_in
    planes, rows, ext, nz = st.shape
    own = slice(PAD, ext - PAD)
    zeros = jnp.zeros((PAD, nz), jnp.float32)
    for i in range(1, rows - 1):
        st[K, i, own] = conductivity_of(st[SA, i, own], st[K, i, own])
        for plane, width in STRIP:
            st[plane, i, :PAD] = zeros
            st[plane, i, ext - PAD :] = zeros


def place_halo(st, one, two, y, nx):
    even = lax.axis_index("gx") % 2 == 0
    at, i = y * STRIP_ROWS, y + 1
    for plane, width in STRIP:
        a, b = one[at : at + width], two[at : at + width]
        st[plane, i, PAD - width : PAD] = jnp.where(even, b, a)
        st[plane, i, PAD + nx : PAD + nx + width] = jnp.where(even, a, b)
        at += width


def inner(s, g, c, h, fx, fz, edge):
    t = c * (s - g)
    flux_x = fx * (up_x(s) - s)
    flux_z = fz * (up_z(s) - s)
    part_s = (flux_x - down_x(flux_x)) + (flux_z - down_z(flux_z)) - h * s - t
    part_g = (
        t
        - GAS_SELF * g
        + CONDUCT * (up_x(g) + down_x(g))
        + edge[0] * up_z(g)
        + edge[1] * down_z(g)
    )
    return part_s, part_g


def edge_weights(shape):
    lane = lanes(shape)
    weight = jnp.float32(0.25 * CONDUCT)
    return jnp.where(lane == shape[1] - 1, 0.0, weight), jnp.where(lane == 0, 0.0, weight)


def row_inner(st, i, s_at, edge):
    return inner(st[s_at, i], st[s_at + 1, i], st[C, i], st[H, i], st[FX, i], st[FZ, i], edge)


def row_residual(st, i, s_at, edge):
    part_s, part_g = row_inner(st, i, s_at, edge)
    s, g, before = st[s_at, i], st[s_at + 1, i], st[s_at + 1, i - 1]
    part_s += st[FY, i] * (st[s_at, i + 1] - s) + st[FY, i - 1] * (st[s_at, i - 1] - s)
    part_g += CONDUCT * (st[s_at + 1, i + 1] + before) - FLOW * (g - before)
    return st[RS, i] + part_s, st[RG, i] + part_g


def relaxed(st, i, s_at, res_s, res_g):
    s = st[s_at, i] + st[ASS, i] * res_s + st[ASG, i] * res_g
    g = st[s_at + 1, i] + st[ASG, i] * res_s + st[AGG, i] * res_g
    return s, g


def faces(k):
    lane = lanes(k.shape)
    end = k.shape[1] - 1
    fx = 0.5 * (k + up_x(k))
    fz = jnp.where(lane == end, 0.0, 0.125 * (k + up_z(k)))
    h = SOLID_CAP + jnp.where((lane == 0) | (lane == end), 0.125 * k, 0.0)
    return fx, fz, h, h + (fx + down_x(fx)) + (fz + down_z(fz))


def inverse(diag, c, mask):
    gas_diag = (GAS_SELF + FLOW) + c
    inv = (RELAX * mask) / (diag * gas_diag - c * c)
    return inv * gas_diag, inv * c, inv * diag


def last_relaxed(st, i, s_at, edge, own):
    full_s, full_g = st[s_at, i], st[s_at + 1, i]
    s, g = full_s[own], full_g[own]
    flux_x = st[FX, i] * (up_x(full_s) - full_s)
    flux_z = st[FZ, i, own] * (up_z(s) - s)
    c, before = st[C, i, own], st[s_at + 1, i - 1, own]
    t = c * (s - g)
    res_s = st[RS, i, own] + (flux_x[own] - down_x(flux_x)[own]) + (flux_z - down_z(flux_z)) - st[H, i, own] * s - t
    res_s += st[FY, i, own] * (st[s_at, i + 1, own] - s) + st[FY, i - 1, own] * (st[s_at, i - 1, own] - s)
    res_g = st[RG, i, own] + t - GAS_SELF * g + edge[0][own] * up_z(g) + edge[1][own] * down_z(g)
    res_g += CONDUCT * (up_x(full_g)[own] + down_x(full_g)[own] + st[s_at + 1, i + 1, own] + before) - FLOW * (g - before)
    ss, sg, gg = st[ASS, i, own], st[ASG, i, own], st[AGG, i, own]
    return s + ss * res_s + sg * res_g, g + sg * res_s + gg * res_g


def grouped(rows, work):
    for start in range(0, len(rows), GROUP):
        stores = []
        for i in rows[start : start + GROUP]:
            stores += work(i)
        for ref, at, value in stores:
            ref[at] = value


def row_coefficients(st, i, mask):
    fx, fz, h, diag = faces(st[K, i])
    fy = 0.5 * (st[K, i] + st[K, i + 1])
    before = 0.5 * (st[K, i] + st[K, i - 1])
    ss, sg, gg = inverse(diag + st[C, i] + fy + before, st[C, i], mask)
    values = ((FX, fx), (FZ, fz), (H, h), (FY, fy), (ASS, ss), (ASG, sg), (AGG, gg))
    return [(st, (plane, i), v) for plane, v in values]


def row_sweep(st, i, source, target, edge):
    s, g = relaxed(st, i, source, *row_residual(st, i, source, edge))
    return [(st, (target, i), s), (st, (target + 1, i), g)]


def first_partial(res_s, res_g, s, s_d, g, g_d, fy, onward):
    return res_s + fy * (s_d - s), res_g + CONDUCT * g_d - FLOW * (g - g_d if onward else g)


def send_planes(st, onward, edge):
    ny = st.shape[1] - 2
    e, d, near = (ny, ny - 1, ny - 1) if onward else (1, 2, 1)
    fy, s, g, g_d = st[FY, near], st[SA, e], st[GA, e], st[GA, d]
    part_s, part_g = row_inner(st, e, SA, edge)
    m_1s, m_1g = first_partial(st[RS, e] + part_s, st[RG, e] + part_g, s, st[SA, d], g, g_d, fy, onward)
    m_2s = st[RS, e] + fy * st[SB, d]
    m_2g = st[RG, e] + (CONDUCT + FLOW if onward else CONDUCT) * st[GB, d]
    return [s, g, st[K, e], st[C, e], fy, m_1s, m_1g, m_2s, m_2g]


def across_parts(ext):
    parts, at = [], 0
    for k in range(EARLY, MESSAGE):
        parts.append((k, CROP, ext - CROP, at))
        at += ext - 2 * CROP
    for k in range(EARLY):
        more = 1 if k in (M_1S, M_1G) else 0
        for low, high in ((CROP, PAD + more), (ext - PAD - more, ext - CROP)):
            parts.append((k, low, high, at))
            at += high - low
    return parts, (at + 7) // 8 * 8


def write_across(ref, k, value):
    for plane, low, high, at in across_parts(value.shape[0])[0]:
        if plane == k:
            ref[at : at + high - low] = value[low:high]


def read_across(early, across, outer, k):
    ext = outer.shape[1]
    if k < EARLY:
        outer[k, PAD : ext - PAD] = early[k]
    for plane, low, high, at in across_parts(ext)[0]:
        if plane == k:
            outer[k, low:high] = across[at : at + high - low]


def write_beside(refs, k, value):
    refs[k // THIRD][k % THIRD] = value[CROP : value.shape[0] - CROP]


def read_beside(refs, outer, k):
    outer[k, CROP : outer.shape[1] - CROP] = refs[k // THIRD][k % THIRD]


def write_message(write, st, onward, edge):
    for go in (True, False):

        @pl.when(onward == go)
        def _():
            for k, value in enumerate(send_planes(st, go, edge)):
                write(k, value)


def first_kernel(st_in, one, two, st, across, *beside):
    del st_in
    planes, rows, ext, nz = st.shape
    ny, nx = rows - 2, ext - 2 * PAD
    shape = (ext, nz)
    mask = x_mask(shape, nx)
    edge = edge_weights(shape)

    for y in list(range(4)) + list(range(ny - 4, ny)):
        place_halo(st, one, two, y, nx)
    for i in (1, ny):
        fx, fz, h, diag = faces(st[K, i])
        st[FX, i], st[FZ, i], st[H, i] = fx, fz, h
    st[FY, 1] = 0.5 * (st[K, 1] + st[K, 2])
    st[FY, ny - 3] = 0.5 * (st[K, ny - 3] + st[K, ny - 2])
    ends = [2, 3, ny - 2, ny - 1]
    grouped(ends, lambda i: row_coefficients(st, i, mask))
    grouped(ends, lambda i: row_sweep(st, i, SA, SB, edge))
    odd = lax.axis_index("gy") % 2 == 1
    write_message(functools.partial(write_across, across), st, odd, edge)
    write_message(functools.partial(write_beside, beside), st, jnp.logical_not(odd), edge)


def outer_residual(st, i, s_at, rs, rg, fy_out, edge, after):
    part_s, part_g = row_inner(st, i, s_at, edge)
    s, g = st[s_at, i], st[s_at + 1, i]
    if after:
        part_s += st[FY, i - 1] * (st[s_at, i - 1] - s)
        part_g += (CONDUCT + FLOW) * st[s_at + 1, i - 1]
    else:
        part_s += st[FY, i] * (st[s_at, i + 1] - s)
        part_g += CONDUCT * st[s_at + 1, i + 1]
    return rs + part_s - fy_out * s, rg + part_g - FLOW * g


def pair_x(v):
    row = lax.broadcasted_iota(jnp.int32, v.shape, 0)
    return v + jnp.where(row % 2 == 0, up_x(v), down_x(v))


def coarse_coefficients(c_sum, k_sum):
    solid = 4.0 * SOLID_CAP + c_sum + LUMP * k_sum
    ratio = c_sum / solid
    denominator = (4.0 * GAS_CAP + 2.0 * FLOW) + c_sum - c_sum * ratio
    return solid, ratio, denominator


def coarse_row(st, coarse, j, mask, edge):
    i = 2 * j + 1
    res_s, res_g = row_residual(st, i, SA, edge)
    more_s, more_g = row_residual(st, i + 1, SA, edge)
    res_s, res_g = pair_x((res_s + more_s) * mask), pair_x((res_g + more_g) * mask)
    c_sum = pair_x(st[C, i] + st[C, i + 1])
    solid, ratio, denominator = coarse_coefficients(c_sum, pair_x(st[K, i] + st[K, i + 1]))
    lead = res_s / solid
    values = (lead, ratio, (2.0 * FLOW) / denominator, (res_g + c_sum * lead) / denominator)
    return [(coarse, (k, j), v) for k, v in enumerate(values)]


def inner_kernel(st_in, one, two, early, st, coarse):
    del st_in, early
    planes, rows, ext, nz = st.shape
    ny, nx = rows - 2, ext - 2 * PAD
    shape = (ext, nz)
    mask = x_mask(shape, nx)
    edge = edge_weights(shape)
    for y in range(4, ny - 4):
        place_halo(st, one, two, y, nx)
    grouped(list(range(4, ny - 2)), lambda i: row_coefficients(st, i, mask))
    grouped(list(range(4, ny - 2)), lambda i: row_sweep(st, i, SA, SB, edge))
    grouped(list(range(3, ny - 1)), lambda i: row_sweep(st, i, SB, SA, edge))
    for j in range(2, ny // 2 - 2):
        for ref, at, value in coarse_row(st, coarse, j, mask, edge):
            ref[at] = value


def end_work(st, coarse, extra, read, outer, is_after):
    planes, rows, ext, nz = st.shape
    ny, nx = rows - 2, ext - 2 * PAD
    me, count = lax.axis_index("gy"), lax.axis_size("gy")
    mask = x_mask((ext, nz), nx)
    inside = jnp.where(me == (count - 1 if is_after else 0), 0.0, mask)
    edge = edge_weights((ext, nz))
    zeros = jnp.zeros((PAD, nz), jnp.float32)
    for k in range(MESSAGE):
        outer[k, :PAD] = zeros
        outer[k, ext - PAD :] = zeros
        read(outer, k)

    o, e, near = (ny + 1, ny, ny) if is_after else (0, 1, 0)
    to_o = CONDUCT + FLOW if is_after else CONDUCT
    s_o, g_o, k_o, c_o, fy_out = (outer[plane] for plane in (M_S, M_G, M_K, M_C, M_FY))
    fy = 0.5 * (k_o + st[K, e])
    fx, fz, h, diag = faces(k_o)
    inv_o = inverse(diag + c_o + fy_out + fy, c_o, inside)
    fx_e, fz_e = st[FX, e], st[FZ, e]
    diag = st[H, e] + (fx_e + down_x(fx_e)) + (fz_e + down_z(fz_e)) + st[C, e] + fy
    inv_e = inverse(diag + st[FY, near - 1 if is_after else near + 1], st[C, e], mask)
    for plane, value in ((SA, s_o), (GA, g_o), (K, k_o), (C, c_o), (FX, fx), (FZ, fz), (H, h)):
        st[plane, o] = value
    st[FY, near] = fy
    for k in range(3):
        st[ASS + k, o], st[ASS + k, e] = inv_o[k], inv_e[k]

    res = outer[M_1S] + fy * (st[SA, e] - s_o), outer[M_1G] + to_o * st[GA, e]
    new_o = relaxed(st, o, SA, *res)
    stores = row_sweep(st, e, SA, SB, edge)
    st[SB, o], st[GB, o] = new_o
    for ref, at, value in stores:
        ref[at] = value
    res = outer_residual(st, o, SB, outer[M_2S], outer[M_2G], fy_out, edge, is_after)
    new_o = relaxed(st, o, SB, *res)
    ends = [e - 1, e] if is_after else [e, e + 1]
    grouped(ends, lambda i: row_sweep(st, i, SB, SA, edge))
    st[SA, o], st[GA, o] = new_o
    for k, plane in enumerate((M_2S, M_2G, M_FY)):
        extra[(3 if is_after else 0) + k] = outer[plane]
    blocks = ny // 2
    stores = []
    for j in (blocks - 2, blocks - 1) if is_after else (0, 1):
        stores += coarse_row(st, coarse, j, mask, edge)
    for ref, at, value in stores:
        ref[at] = value


def either_end(after, st, coarse, extra, read, outer):
    for is_after in (True, False):

        @pl.when(after == is_after)
        def _():
            end_work(st, coarse, extra, read, outer, is_after)


def near_kernel(st_in, coarse_in, *refs):
    beside, (st, coarse, extra, outer) = refs[:-4], refs[-4:]
    del st_in, coarse_in
    either_end(lax.axis_index("gy") % 2 == 0, st, coarse, extra, functools.partial(read_beside, beside), outer)


def second_kernel(st_in, coarse_in, extra_in, early, across, *refs):
    st, coarse, extra, total, info_far, info_near, outer, squeeze = refs
    del st_in, coarse_in, extra_in
    planes, rows, ext, nz = st.shape
    ny, nx = rows - 2, ext - 2 * PAD
    me = lax.axis_index("gy")
    either_end(me % 2 == 1, st, coarse, extra, functools.partial(read_across, early, across), outer)

    blocks = ny // 2
    for k in range(4):
        squeeze[k] = coarse[k, 0]
    slopes, offsets = coarse[2, 0], coarse[3, 0]
    for j in range(1, blocks):
        slope = coarse[2, j]
        slopes, offsets = slope * slopes, slope * offsets + coarse[3, j]
        coarse[2, j], coarse[3, j] = slopes, offsets
    squeeze[4], squeeze[5], squeeze[6], squeeze[7] = slopes, offsets, coarse[0, blocks - 1], coarse[1, blocks - 1]

    span = nx // 2 + 2
    lead, ratio, slope, offset, slopes, offsets, lead_last, ratio_last = (
        squeeze[k, pl.ds(PAD - 2, span, 2), :] for k in range(8)
    )
    part = slice(PAD - 1, PAD + nx + 1)

    def increments(d, face, gas):
        return [(st[FY, face] * (st[SA, d] - st[SB, d]))[part], (gas * (st[GA, d] - st[GB, d]))[part]]

    onward = [lead_last, ratio_last] + increments(ny - 1, ny - 1, CONDUCT + FLOW)
    back = [lead, offset] + increments(2, 1, CONDUCT) + [slope, ratio]
    write_rows(total, [slopes, offsets])
    for odd in (True, False):

        @pl.when((me % 2 == 1) == odd)
        def _():
            write_rows(info_far, onward if odd else back)
            write_rows(info_near, back if odd else onward)


def write_rows(ref, values):
    at = 0
    for value in values:
        ref[at : at + value.shape[0]] = value
        at += value.shape[0]


class Info:
    def __init__(self, nx):
        span = self.span = nx // 2 + 2
        self.lead, self.second = 0, span
        self.solid, self.gas = 2 * span, 2 * span + nx + 2
        self.slope = 2 * span + 2 * (nx + 2)
        self.ratio = self.slope + span
        self.height = (self.ratio + span + 7) // 8 * 8


def source(at, k, radix):
    if radix & (radix - 1) == 0:
        return at ^ k
    return (at + radix - k) % radix


def stages(count):
    if count % 2:
        return [1, count]
    out, rest = [2], count // 2
    while rest > 1:
        radix = next((r for r in (8, 4, 2) if rest % r == 0), rest)
        out.append(radix)
        rest //= radix
    return out if len(out) > 1 else out + [1]


def exchange_stage(message, radix, stride):
    count, got = lax.axis_size("gy"), []
    for k in range(1, radix):
        pairs = []
        for me in range(count):
            at = me // stride % radix
            pairs.append((me + (source(at, k, radix) - at) * stride, me))
        got.append(lax.ppermute(message, "gy", pairs))
    return got


class Group:
    def __init__(self, radix, stride, others, span):
        self.radix, self.others, self.span = radix, others, span
        self.at = lax.rem(lax.div(lax.axis_index("gy"), stride), radix)

    def map_of(self, place, own):
        out = own
        for k, ref in enumerate(self.others, 1):
            here = source(self.at, k, self.radix) == place
            got = read_map(ref, self.span)
            out = got if out is None else [jnp.where(here, new, old) for new, old in zip(got, out)]
        return out

    def ahead(self, slope, offset):
        a, b = jnp.ones_like(slope), jnp.zeros_like(slope)
        for place in range(self.radix - 1):
            new_a, new_b = self.map_of(place, None)
            below = place < self.at
            a, b = jnp.where(below, new_a * a, a), jnp.where(below, new_a * b + new_b, b)
        return slope * a, slope * b + offset

    def total(self, own):
        a, b = self.map_of(0, own)
        for place in range(1, self.radix):
            new_a, new_b = self.map_of(place, own)
            a, b = new_a * a, new_a * b + new_b
        return a, b


def read_map(ref, span):
    return [ref[i * span : (i + 1) * span] for i in range(2)]


def join_kernel(radix, stride, span, is_first, *refs):
    total, ahead_in, info_far, info_near = refs[:4]
    others, (ahead, whole, far_out, near_out) = refs[4 : 3 + radix], refs[3 + radix :]
    own = read_map(total, span)
    before = (jnp.ones_like(own[0]), jnp.zeros_like(own[0])) if is_first else read_map(ahead_in, span)
    group = Group(radix, stride, others, span)
    write_rows(ahead, group.ahead(*before))
    write_rows(whole, group.total(own))
    far_out[...] = info_far[...]
    near_out[...] = info_near[...]


def third_kernel(radix, stride, *refs):
    st, extra, coarse, ahead, info_far, info_near = refs[:6]
    others, (out, sc, wide, done, sems) = refs[6 : 5 + radix], refs[5 + radix :]
    planes, rows, ext, nz = st.shape
    ny, nx = rows - 2, ext - 2 * PAD
    edge = edge_weights((ext, nz))
    blocks = ny // 2

    info = Info(nx)
    span = info.span
    gas_in = Group(radix, stride, others, span).ahead(*read_map(ahead, span))[1]
    odd = lax.axis_index("gy") % 2 == 1

    def from_beside(after, start, height):
        part = slice(start, start + height)
        return jnp.where(odd, info_far[part], info_near[part]) if after else jnp.where(odd, info_near[part], info_far[part])

    starts = ((False, info.lead), (False, info.second), (True, info.lead), (True, info.second), (True, info.slope), (True, info.ratio))
    for k, v in enumerate([gas_in] + [from_beside(after, start, span) for after, start in starts]):
        wide[k, : PAD - 2] = jnp.zeros((PAD - 2, nz), jnp.float32)
        wide[k, ext - PAD + 2 :] = jnp.zeros((PAD - 2, nz), jnp.float32)
        wide[k, pl.ds(PAD - 2, span, 2), :] = v
        wide[k, pl.ds(PAD - 1, span, 2), :] = v
    for k, (after, start) in enumerate(((False, info.solid), (False, info.gas), (True, info.solid), (True, info.gas))):
        wide[7 + k, :PAD] = jnp.zeros((PAD, nz), jnp.float32)
        wide[7 + k, ext - PAD :] = jnp.zeros((PAD, nz), jnp.float32)
        wide[7 + k, PAD - 1 : PAD + nx + 1] = from_beside(after, start, nx + 2)

    gas_in = wide[0]
    last = ny + 1
    solid_low = wide[1] + wide[2] * gas_in
    sc[0, 0] = st[SA, 0] + solid_low
    sc[1, 0] = st[GA, 0] + gas_in

    def correct(j, carry):
        gas = coarse[2, j] * gas_in + coarse[3, j]
        solid = coarse[0, j] + coarse[1, j] * gas
        for i in (2 * j + 1, 2 * j + 2):
            sc[0, i] = st[SA, i] + solid
            sc[1, i] = st[GA, i] + gas
        return carry

    lax.fori_loop(0, blocks, correct, 0)
    gas = coarse[2, blocks - 1] * gas_in + coarse[3, blocks - 1]
    gas_high = wide[5] * gas + wide[4]
    solid_high = wide[3] + wide[6] * gas_high
    sc[0, last] = st[SA, last] + solid_high
    sc[1, last] = st[GA, last] + gas_high

    view = Fields(st, sc)
    for i, is_after, solid, gas in ((0, False, solid_low, gas_in), (last, True, solid_high, gas_high)):
        side = 3 if is_after else 0
        fy = extra[side + 2]
        to = 9 if is_after else 7
        rs = extra[side] + wide[to] + fy * solid
        rg = extra[side + 1] + wide[to + 1] + (CONDUCT if is_after else CONDUCT + FLOW) * gas
        res = outer_residual(view, i, SA, rs, rg, fy, edge, is_after)
        sc[2, i], sc[3, i] = relaxed(view, i, SA, *res)

    def sweep(k, carry):
        stores = []
        for r in range(GROUP):
            i = GROUP * k + 1 + r
            new_s, new_g = relaxed(view, i, SA, *row_residual(view, i, SA, edge))
            stores += [((2, i), new_s), ((3, i), new_g)]
        for at, value in stores:
            sc[at] = value
        return carry

    lax.fori_loop(0, ny // GROUP, sweep, 0)

    def leaving(k):
        part = pl.ds(GROUP * k, GROUP)
        return pltpu.make_async_copy(done.at[:, part], out.at[:, part], sems.at[k])

    def final(k, carry):
        stores = []
        for r in range(GROUP):
            i = GROUP * k + 1 + r
            new_s, new_g = last_relaxed(view, i, SB, edge, slice(PAD, PAD + nx))
            stores += [((0, i - 1), new_s), ((1, i - 1), new_g)]
        for at, value in stores:
            done[at] = value
        leaving(k).start()
        return carry

    lax.fori_loop(0, ny // GROUP, final, 0)
    for k in range(ny // GROUP):
        leaving(k).wait()


class Fields:
    def __init__(self, st, sc):
        self.st, self.sc = st, sc

    def __getitem__(self, at):
        return (self.sc if at[0] <= GB else self.st)[at]


def cost(rows, cells):
    return pl.CostEstimate(flops=50 * rows * cells, bytes_accessed=16 * 4 * rows * cells, transcendentals=0)


def swap(x, axis, first):
    pairs = []
    for i in range(first, lax.axis_size(axis) - 1, 2):
        pairs += [(i, i + 1), (i + 1, i)]
    return lax.ppermute(x, axis, pairs)


def shards(temps, right_side, exchange, coupling):
    temps, right_side = (jnp.transpose(a, (0, 2, 1, 3)) for a in (temps, right_side))
    exchange, coupling = (jnp.transpose(a, (1, 0, 2)) for a in (exchange, coupling))
    temps, right_side, exchange, coupling = (
        pltpu.with_memory_space_constraint(a, pltpu.HBM) for a in (temps, right_side, exchange, coupling)
    )
    ny, nx, nz = exchange.shape
    ext = nx + 2 * PAD
    f32 = functools.partial(jax.ShapeDtypeStruct, dtype=jnp.float32)

    strip = f32(((ny * STRIP_ROWS + 7) // 8 * 8, nz))
    state = f32((PLANES, ny + 2, ext, nz))
    one, two, early, st = pl.pallas_call(
        pack_kernel,
        out_shape=(strip, strip, f32((EARLY, nx, nz)), state),
        in_specs=[HBM] * 4,
        out_specs=(VMEM,) * 4,
        scratch_shapes=[pltpu.SemaphoreType.DMA((6,))],
        compiler_params=PARAMS,
        name="pack_x",
    )(temps, right_side, exchange, coupling)
    one, two = swap(one, "gx", 0), swap(two, "gx", 1)
    early = swap(early, "gy", 1)

    def letter(planes):
        return f32((planes, ext - 2 * CROP, nz))

    st = pl.pallas_call(
        conduct_kernel,
        out_shape=state,
        in_specs=[VMEM],
        out_specs=VMEM,
        input_output_aliases={0: 0},
        compiler_params=PARAMS,
        cost_estimate=cost(2 * ny, ext * nz),
        name="conduct",
    )(st)
    st, across, *beside = pl.pallas_call(
        first_kernel,
        out_shape=(state, f32((across_parts(ext)[1], nz))) + (letter(THIRD),) * (MESSAGE // THIRD),
        in_specs=[VMEM] * 3,
        out_specs=(VMEM,) * (2 + MESSAGE // THIRD),
        input_output_aliases={0: 0},
        compiler_params=PARAMS,
        name="first",
    )(st, one, two)
    across = swap(across, "gy", 1)

    rows = f32((4, ny // 2, ext, nz))
    st, coarse = pl.pallas_call(
        inner_kernel,
        out_shape=(state, rows),
        in_specs=[VMEM] * 4,
        out_specs=(VMEM,) * 2,
        input_output_aliases={0: 0},
        compiler_params=PARAMS,
        cost_estimate=cost(4 * ny, ext * nz),
        name="inner",
    )(st, one, two, early)

    beside = [swap(part, "gy", 0) for part in beside]

    info = f32((Info(nx).height, nz))
    span = Info(nx).span
    map_shape = f32(((2 * span + 7) // 8 * 8, nz))
    letter_room = pltpu.VMEM((MESSAGE, ext, nz), jnp.float32)
    more = f32((6, ext, nz))
    st, coarse, extra = pl.pallas_call(
        near_kernel,
        out_shape=(state, rows, more),
        in_specs=[VMEM] * (2 + len(beside)),
        out_specs=(VMEM,) * 3,
        scratch_shapes=[letter_room],
        input_output_aliases={0: 0, 1: 1},
        compiler_params=PARAMS,
        name="near",
    )(st, coarse, *beside)
    st, coarse, extra, total, info_far, info_near = pl.pallas_call(
        second_kernel,
        out_shape=(state, rows, more, map_shape, info, info),
        in_specs=[VMEM] * 5,
        out_specs=(VMEM,) * 6,
        scratch_shapes=[letter_room, pltpu.VMEM((8, ext, nz), jnp.float32)],
        input_output_aliases={0: 0, 1: 1, 2: 2},
        compiler_params=PARAMS,
        name="second",
    )(st, coarse, extra, early, across)

    ahead, radices, stride = total, stages(lax.axis_size("gy")), 1
    for place, radix in enumerate(radices[:-1]):
        others = exchange_stage(total, radix, stride)
        ahead, total, info_far, info_near = pl.pallas_call(
            functools.partial(join_kernel, radix, stride, span, place == 0),
            out_shape=(map_shape, map_shape, info, info),
            in_specs=[VMEM] * (3 + radix),
            out_specs=(VMEM,) * 4,
            compiler_params=PARAMS,
            name="join",
        )(total, ahead, info_far, info_near, *others)
        stride *= radix
    info_far, info_near = swap(info_far, "gy", 1), swap(info_near, "gy", 0)
    got = exchange_stage(total, radices[-1], stride)

    out = pl.pallas_call(
        functools.partial(third_kernel, radices[-1], stride),
        out_shape=f32((2, ny, nx, nz)),
        in_specs=[VMEM] * (6 + len(got)),
        out_specs=HBM,
        scratch_shapes=[
            pltpu.VMEM((4, ny + 2, ext, nz), jnp.float32),
            pltpu.VMEM((11, ext, nz), jnp.float32),
            pltpu.VMEM((2, ny, nx, nz), jnp.float32),
            pltpu.SemaphoreType.DMA((ny // GROUP,)),
        ],
        compiler_params=PARAMS,
        name="third",
    )(st, extra, coarse, ahead, info_far, info_near, *got)
    return jnp.transpose(out, (0, 2, 1, 3))


def solution(mesh):
    return jax.shard_map(
        shards,
        mesh=mesh,
        in_specs=(
            P(None, "gx", "gy", None),
            P(None, "gx", "gy", None),
            P("gx", "gy", None),
            P("gx", "gy", None),
        ),
        out_specs=P(None, "gx", "gy", None),
        check_vma=False,
    )
```

```python
import functools

import jax
import jax.numpy as jnp
from jax import lax
from jax.experimental import pallas as pl
from jax.experimental.pallas import tpu as pltpu
from jax.sharding import PartitionSpec as P

SOLID_CAP, GAS_CAP, FLOW, CONDUCT, RELAX, LUMP = 0.5, 0.02, 40.0, 0.05, 0.8, 0.25
GAS_SELF = GAS_CAP + 4.5 * CONDUCT

PAD = 8
WX = 5
CROP = 4
(SA, GA, SB, GB, K, C, RS, RG, FX, FZ, H, FY, ASS, ASG, AGG) = range(15)
PLANES = 15
(M_S, M_G, M_K, M_C, M_FY, M_1S, M_1G, M_2S, M_2G) = range(9)
MESSAGE, EARLY, THIRD = 9, 7, 3

GROUP = 4

VMEM = pl.BlockSpec(memory_space=pltpu.VMEM)
HBM = pl.BlockSpec(memory_space=pltpu.HBM)
PARAMS = pltpu.CompilerParams(vmem_limit_bytes=40 * 1024 * 1024)


def up_x(v):
    return pltpu.roll(v, v.shape[0] - 1, 0)


def down_x(v):
    return pltpu.roll(v, 1, 0)


def up_z(v):
    return pltpu.roll(v, v.shape[1] - 1, 1)


def down_z(v):
    return pltpu.roll(v, 1, 1)


def lanes(shape):
    return lax.broadcasted_iota(jnp.int32, shape, 1)


def x_mask(shape, nx):
    row = lax.broadcasted_iota(jnp.int32, shape, 0)
    place, count = lax.axis_index("gx"), lax.axis_size("gx")
    low = jnp.where(place == 0, PAD, PAD - WX)
    high = jnp.where(place == count - 1, PAD + nx, PAD + nx + WX)
    return jnp.where((row >= low) & (row < high), 1.0, 0.0).astype(jnp.float32)


STRIP = ((SA, WX - 1), (GA, WX - 1), (K, WX), (RS, WX - 1), (RG, WX - 1), (C, WX - 1))
STRIP_ROWS = sum(width for plane, width in STRIP)


def conductivity_of(s, exchange):
    return 1.0 + 4.0 * exchange * s * s * s


def strip_values(s, g, k, rs, rg, c, low):
    out, inn = (WX - 1, WX - 2) if low else (8 - WX, 9 - WX)
    four = slice(0, WX - 1) if low else slice(9 - WX, 8)
    five = slice(0, WX) if low else slice(8 - WX, 8)
    row = lax.broadcasted_iota(jnp.int32, s.shape, 0)
    rs = rs + jnp.where(row == inn, 0.5 * (k[inn : inn + 1] + k[out : out + 1]) * s[out : out + 1], 0.0)
    rg = rg + jnp.where(row == inn, CONDUCT * g[out : out + 1], 0.0)
    return [s[four], g[four], k[five], rs[four], rg[four], c[four]]


def pack_kernel(temps, right, exchange, coupling, one, two, early, st, sems):
    even = lax.axis_index("gx") % 2 == 0
    odd = lax.axis_index("gy") % 2 == 1
    ny, nx, nz = exchange.shape
    copies = []
    for k, (plane, ref) in enumerate(
        ((SA, temps.at[0]), (K, exchange), (GA, temps.at[1]), (C, coupling), (RS, right.at[0]), (RG, right.at[1]))
    ):
        to = st.at[plane, pl.ds(1, ny), pl.ds(PAD, nx)]
        copies.append(pltpu.make_async_copy(ref, to, sems.at[k]))
    for copy in copies:
        copy.start()
    for copy in copies:
        copy.wait()
    at = 0
    for i in range(1, ny + 1):
        sides = []
        for start in (PAD, PAD + nx - 8):
            s, g, e, rs, rg, c = (st[plane, i, start : start + 8] for plane in (SA, GA, K, RS, RG, C))
            sides.append(strip_values(s, g, conductivity_of(s, e), rs, rg, c, start == PAD))
        for low, high, (plane, width) in zip(*sides, STRIP):
            one[at : at + width] = jnp.where(even, high, low)
            two[at : at + width] = jnp.where(even, low, high)
            at += width
    own = slice(PAD, PAD + nx)
    for is_odd, e, d in ((True, ny, ny - 1), (False, 1, 2)):

        @pl.when(odd == is_odd)
        def _():
            s, s_d, g, g_d = st[SA, e, own], st[SA, d, own], st[GA, e, own], st[GA, d, own]
            c, k, k_d = st[C, e, own], conductivity_of(s, st[K, e, own]), conductivity_of(s_d, st[K, d, own])
            fx, fz, h, _ = faces(k)
            fy = 0.5 * (k + k_d)
            part_s, part_g = inner(s, g, c, h, fx, fz, edge_weights((nx, nz)))
            m_1s, m_1g = first_partial(st[RS, e, own] + part_s, st[RG, e, own] + part_g, s, s_d, g, g_d, fy, is_odd)
            for plane, value in enumerate((s, g, k, c, fy, m_1s, m_1g)):
                early[plane] = value


def conduct_kernel(st_in, st):
    del st_in
    planes, rows, ext, nz = st.shape
    own = slice(PAD, ext - PAD)
    zeros = jnp.zeros((PAD, nz), jnp.float32)
    for i in range(1, rows - 1):
        st[K, i, own] = conductivity_of(st[SA, i, own], st[K, i, own])
        for plane, width in STRIP:
            st[plane, i, :PAD] = zeros
            st[plane, i, ext - PAD :] = zeros


def place_halo(st, one, two, y, nx):
    even = lax.axis_index("gx") % 2 == 0
    at, i = y * STRIP_ROWS, y + 1
    for plane, width in STRIP:
        a, b = one[at : at + width], two[at : at + width]
        st[plane, i, PAD - width : PAD] = jnp.where(even, b, a)
        st[plane, i, PAD + nx : PAD + nx + width] = jnp.where(even, a, b)
        at += width


def inner(s, g, c, h, fx, fz, edge):
    t = c * (s - g)
    flux_x = fx * (up_x(s) - s)
    flux_z = fz * (up_z(s) - s)
    part_s = (flux_x - down_x(flux_x)) + (flux_z - down_z(flux_z)) - h * s - t
    part_g = (
        t
        - GAS_SELF * g
        + CONDUCT * (up_x(g) + down_x(g))
        + edge[0] * up_z(g)
        + edge[1] * down_z(g)
    )
    return part_s, part_g


def edge_weights(shape):
    lane = lanes(shape)
    weight = jnp.float32(0.25 * CONDUCT)
    return jnp.where(lane == shape[1] - 1, 0.0, weight), jnp.where(lane == 0, 0.0, weight)


def row_inner(st, i, s_at, edge):
    return inner(st[s_at, i], st[s_at + 1, i], st[C, i], st[H, i], st[FX, i], st[FZ, i], edge)


def row_residual(st, i, s_at, edge):
    part_s, part_g = row_inner(st, i, s_at, edge)
    s, g, before = st[s_at, i], st[s_at + 1, i], st[s_at + 1, i - 1]
    part_s += st[FY, i] * (st[s_at, i + 1] - s) + st[FY, i - 1] * (st[s_at, i - 1] - s)
    part_g += CONDUCT * (st[s_at + 1, i + 1] + before) - FLOW * (g - before)
    return st[RS, i] + part_s, st[RG, i] + part_g


def relaxed(st, i, s_at, res_s, res_g):
    s = st[s_at, i] + st[ASS, i] * res_s + st[ASG, i] * res_g
    g = st[s_at + 1, i] + st[ASG, i] * res_s + st[AGG, i] * res_g
    return s, g


def faces(k):
    lane = lanes(k.shape)
    end = k.shape[1] - 1
    fx = 0.5 * (k + up_x(k))
    fz = jnp.where(lane == end, 0.0, 0.125 * (k + up_z(k)))
    h = SOLID_CAP + jnp.where((lane == 0) | (lane == end), 0.125 * k, 0.0)
    return fx, fz, h, h + (fx + down_x(fx)) + (fz + down_z(fz))


def inverse(diag, c, mask):
    gas_diag = (GAS_SELF + FLOW) + c
    inv = (RELAX * mask) / (diag * gas_diag - c * c)
    return inv * gas_diag, inv * c, inv * diag


def last_relaxed(st, i, s_at, edge, own):
    full_s, full_g = st[s_at, i], st[s_at + 1, i]
    s, g = full_s[own], full_g[own]
    flux_x = st[FX, i] * (up_x(full_s) - full_s)
    flux_z = st[FZ, i, own] * (up_z(s) - s)
    c, before = st[C, i, own], st[s_at + 1, i - 1, own]
    t = c * (s - g)
    res_s = st[RS, i, own] + (flux_x[own] - down_x(flux_x)[own]) + (flux_z - down_z(flux_z)) - st[H, i, own] * s - t
    res_s += st[FY, i, own] * (st[s_at, i + 1, own] - s) + st[FY, i - 1, own] * (st[s_at, i - 1, own] - s)
    res_g = st[RG, i, own] + t - GAS_SELF * g + edge[0][own] * up_z(g) + edge[1][own] * down_z(g)
    res_g += CONDUCT * (up_x(full_g)[own] + down_x(full_g)[own] + st[s_at + 1, i + 1, own] + before) - FLOW * (g - before)
    ss, sg, gg = st[ASS, i, own], st[ASG, i, own], st[AGG, i, own]
    return s + ss * res_s + sg * res_g, g + sg * res_s + gg * res_g


def grouped(rows, work):
    for start in range(0, len(rows), GROUP):
        stores = []
        for i in rows[start : start + GROUP]:
            stores += work(i)
        for ref, at, value in stores:
            ref[at] = value


def row_coefficients(st, i, mask):
    fx, fz, h, diag = faces(st[K, i])
    fy = 0.5 * (st[K, i] + st[K, i + 1])
    before = 0.5 * (st[K, i] + st[K, i - 1])
    ss, sg, gg = inverse(diag + st[C, i] + fy + before, st[C, i], mask)
    values = ((FX, fx), (FZ, fz), (H, h), (FY, fy), (ASS, ss), (ASG, sg), (AGG, gg))
    return [(st, (plane, i), v) for plane, v in values]


def row_sweep(st, i, source, target, edge):
    s, g = relaxed(st, i, source, *row_residual(st, i, source, edge))
    return [(st, (target, i), s), (st, (target + 1, i), g)]


def first_partial(res_s, res_g, s, s_d, g, g_d, fy, onward):
    return res_s + fy * (s_d - s), res_g + CONDUCT * g_d - FLOW * (g - g_d if onward else g)


def send_planes(st, onward, edge):
    ny = st.shape[1] - 2
    e, d, near = (ny, ny - 1, ny - 1) if onward else (1, 2, 1)
    fy, s, g, g_d = st[FY, near], st[SA, e], st[GA, e], st[GA, d]
    part_s, part_g = row_inner(st, e, SA, edge)
    m_1s, m_1g = first_partial(st[RS, e] + part_s, st[RG, e] + part_g, s, st[SA, d], g, g_d, fy, onward)
    m_2s = st[RS, e] + fy * st[SB, d]
    m_2g = st[RG, e] + (CONDUCT + FLOW if onward else CONDUCT) * st[GB, d]
    return [s, g, st[K, e], st[C, e], fy, m_1s, m_1g, m_2s, m_2g]


def across_parts(ext):
    parts, at = [], 0
    for k in range(EARLY, MESSAGE):
        parts.append((k, CROP, ext - CROP, at))
        at += ext - 2 * CROP
    for k in range(EARLY):
        more = 1 if k in (M_1S, M_1G) else 0
        for low, high in ((CROP, PAD + more), (ext - PAD - more, ext - CROP)):
            parts.append((k, low, high, at))
            at += high - low
    return parts, (at + 7) // 8 * 8


def write_across(ref, k, value):
    for plane, low, high, at in across_parts(value.shape[0])[0]:
        if plane == k:
            ref[at : at + high - low] = value[low:high]


def read_across(early, across, outer, k):
    ext = outer.shape[1]
    if k < EARLY:
        outer[k, PAD : ext - PAD] = early[k]
    for plane, low, high, at in across_parts(ext)[0]:
        if plane == k:
            outer[k, low:high] = across[at : at + high - low]


def write_beside(refs, k, value):
    refs[k // THIRD][k % THIRD] = value[CROP : value.shape[0] - CROP]


def read_beside(refs, outer, k):
    outer[k, CROP : outer.shape[1] - CROP] = refs[k // THIRD][k % THIRD]


def write_message(write, st, onward, edge):
    for go in (True, False):

        @pl.when(onward == go)
        def _():
            for k, value in enumerate(send_planes(st, go, edge)):
                write(k, value)


def first_kernel(st_in, one, two, st, across, *beside):
    del st_in
    planes, rows, ext, nz = st.shape
    ny, nx = rows - 2, ext - 2 * PAD
    shape = (ext, nz)
    mask = x_mask(shape, nx)
    edge = edge_weights(shape)

    for y in list(range(4)) + list(range(ny - 4, ny)):
        place_halo(st, one, two, y, nx)
    for i in (1, ny):
        fx, fz, h, diag = faces(st[K, i])
        st[FX, i], st[FZ, i], st[H, i] = fx, fz, h
    st[FY, 1] = 0.5 * (st[K, 1] + st[K, 2])
    st[FY, ny - 3] = 0.5 * (st[K, ny - 3] + st[K, ny - 2])
    ends = [2, 3, ny - 2, ny - 1]
    grouped(ends, lambda i: row_coefficients(st, i, mask))
    grouped(ends, lambda i: row_sweep(st, i, SA, SB, edge))
    odd = lax.axis_index("gy") % 2 == 1
    write_message(functools.partial(write_across, across), st, odd, edge)
    write_message(functools.partial(write_beside, beside), st, jnp.logical_not(odd), edge)


def outer_residual(st, i, s_at, rs, rg, fy_out, edge, after):
    part_s, part_g = row_inner(st, i, s_at, edge)
    s, g = st[s_at, i], st[s_at + 1, i]
    if after:
        part_s += st[FY, i - 1] * (st[s_at, i - 1] - s)
        part_g += (CONDUCT + FLOW) * st[s_at + 1, i - 1]
    else:
        part_s += st[FY, i] * (st[s_at, i + 1] - s)
        part_g += CONDUCT * st[s_at + 1, i + 1]
    return rs + part_s - fy_out * s, rg + part_g - FLOW * g


def pair_x(v):
    row = lax.broadcasted_iota(jnp.int32, v.shape, 0)
    return v + jnp.where(row % 2 == 0, up_x(v), down_x(v))


def coarse_coefficients(c_sum, k_sum):
    solid = 4.0 * SOLID_CAP + c_sum + LUMP * k_sum
    ratio = c_sum / solid
    denominator = (4.0 * GAS_CAP + 2.0 * FLOW) + c_sum - c_sum * ratio
    return solid, ratio, denominator


def coarse_row(st, coarse, j, mask, edge):
    i = 2 * j + 1
    res_s, res_g = row_residual(st, i, SA, edge)
    more_s, more_g = row_residual(st, i + 1, SA, edge)
    res_s, res_g = pair_x((res_s + more_s) * mask), pair_x((res_g + more_g) * mask)
    c_sum = pair_x(st[C, i] + st[C, i + 1])
    solid, ratio, denominator = coarse_coefficients(c_sum, pair_x(st[K, i] + st[K, i + 1]))
    lead = res_s / solid
    values = (lead, ratio, (2.0 * FLOW) / denominator, (res_g + c_sum * lead) / denominator)
    return [(coarse, (k, j), v) for k, v in enumerate(values)]


def inner_kernel(st_in, one, two, early, st, coarse):
    del st_in, early
    planes, rows, ext, nz = st.shape
    ny, nx = rows - 2, ext - 2 * PAD
    shape = (ext, nz)
    mask = x_mask(shape, nx)
    edge = edge_weights(shape)
    for y in range(4, ny - 4):
        place_halo(st, one, two, y, nx)
    grouped(list(range(4, ny - 2)), lambda i: row_coefficients(st, i, mask))
    grouped(list(range(4, ny - 2)), lambda i: row_sweep(st, i, SA, SB, edge))
    grouped(list(range(3, ny - 1)), lambda i: row_sweep(st, i, SB, SA, edge))
    for j in range(2, ny // 2 - 2):
        for ref, at, value in coarse_row(st, coarse, j, mask, edge):
            ref[at] = value


def end_work(st, coarse, extra, read, outer, is_after):
    planes, rows, ext, nz = st.shape
    ny, nx = rows - 2, ext - 2 * PAD
    me, count = lax.axis_index("gy"), lax.axis_size("gy")
    mask = x_mask((ext, nz), nx)
    inside = jnp.where(me == (count - 1 if is_after else 0), 0.0, mask)
    edge = edge_weights((ext, nz))
    zeros = jnp.zeros((PAD, nz), jnp.float32)
    for k in range(MESSAGE):
        outer[k, :PAD] = zeros
        outer[k, ext - PAD :] = zeros
        read(outer, k)

    o, e, near = (ny + 1, ny, ny) if is_after else (0, 1, 0)
    to_o = CONDUCT + FLOW if is_after else CONDUCT
    s_o, g_o, k_o, c_o, fy_out = (outer[plane] for plane in (M_S, M_G, M_K, M_C, M_FY))
    fy = 0.5 * (k_o + st[K, e])
    fx, fz, h, diag = faces(k_o)
    inv_o = inverse(diag + c_o + fy_out + fy, c_o, inside)
    fx_e, fz_e = st[FX, e], st[FZ, e]
    diag = st[H, e] + (fx_e + down_x(fx_e)) + (fz_e + down_z(fz_e)) + st[C, e] + fy
    inv_e = inverse(diag + st[FY, near - 1 if is_after else near + 1], st[C, e], mask)
    for plane, value in ((SA, s_o), (GA, g_o), (K, k_o), (C, c_o), (FX, fx), (FZ, fz), (H, h)):
        st[plane, o] = value
    st[FY, near] = fy
    for k in range(3):
        st[ASS + k, o], st[ASS + k, e] = inv_o[k], inv_e[k]

    res = outer[M_1S] + fy * (st[SA, e] - s_o), outer[M_1G] + to_o * st[GA, e]
    new_o = relaxed(st, o, SA, *res)
    stores = row_sweep(st, e, SA, SB, edge)
    st[SB, o], st[GB, o] = new_o
    for ref, at, value in stores:
        ref[at] = value
    res = outer_residual(st, o, SB, outer[M_2S], outer[M_2G], fy_out, edge, is_after)
    new_o = relaxed(st, o, SB, *res)
    ends = [e - 1, e] if is_after else [e, e + 1]
    grouped(ends, lambda i: row_sweep(st, i, SB, SA, edge))
    st[SA, o], st[GA, o] = new_o
    for k, plane in enumerate((M_2S, M_2G, M_FY)):
        extra[(3 if is_after else 0) + k] = outer[plane]
    blocks = ny // 2
    stores = []
    for j in (blocks - 2, blocks - 1) if is_after else (0, 1):
        stores += coarse_row(st, coarse, j, mask, edge)
    for ref, at, value in stores:
        ref[at] = value


def either_end(after, st, coarse, extra, read, outer):
    for is_after in (True, False):

        @pl.when(after == is_after)
        def _():
            end_work(st, coarse, extra, read, outer, is_after)


def near_kernel(st_in, coarse_in, *refs):
    beside, (st, coarse, extra, outer) = refs[:-4], refs[-4:]
    del st_in, coarse_in
    either_end(lax.axis_index("gy") % 2 == 0, st, coarse, extra, functools.partial(read_beside, beside), outer)


def second_kernel(st_in, coarse_in, extra_in, early, across, *refs):
    st, coarse, extra, total, last_info, first_info, message, outer, squeeze = refs
    del st_in, coarse_in, extra_in
    planes, rows, ext, nz = st.shape
    ny, nx = rows - 2, ext - 2 * PAD
    me = lax.axis_index("gy")
    either_end(me % 2 == 1, st, coarse, extra, functools.partial(read_across, early, across), outer)

    blocks = ny // 2
    for k in range(4):
        squeeze[k] = coarse[k, 0]
    slopes, offsets = coarse[2, 0], coarse[3, 0]
    for j in range(1, blocks):
        slope = coarse[2, j]
        slopes, offsets = slope * slopes, slope * offsets + coarse[3, j]
        coarse[2, j], coarse[3, j] = slopes, offsets
    squeeze[4], squeeze[5], squeeze[6], squeeze[7] = slopes, offsets, coarse[0, blocks - 1], coarse[1, blocks - 1]

    span = nx // 2 + 2
    lead, ratio, slope, offset, slopes, offsets, lead_last, ratio_last = (
        squeeze[k, pl.ds(PAD - 2, span, 2), :] for k in range(8)
    )
    part = slice(PAD - 1, PAD + nx + 1)

    def increments(d, face, gas):
        return [(st[FY, face] * (st[SA, d] - st[SB, d]))[part], (gas * (st[GA, d] - st[GB, d]))[part]]

    onward = [lead_last, ratio_last] + increments(ny - 1, ny - 1, CONDUCT + FLOW)
    back = [lead, offset] + increments(2, 1, CONDUCT) + [slope, ratio]
    write_rows(total, [slopes, offsets])
    write_rows(last_info, onward)
    write_rows(first_info, back)
    for go, info in ((True, onward), (False, back)):

        @pl.when((me % 2 == 0) == go)
        def _():
            write_rows(message, [slopes, offsets] + info)


def write_rows(ref, values):
    at = 0
    for value in values:
        ref[at : at + value.shape[0]] = value
        at += value.shape[0]


class Rows:
    def __init__(self, nx):
        self.span = nx // 2 + 2
        self.map = 2 * self.span
        self.info = self.map + 2 * (nx + 2)
        self.rest = self.map
        self.final = self.map + self.info
        self.full = self.final + self.rest
        self.low = self.map
        self.high = self.low + self.info
        self.near = self.high + self.info + self.rest


def source(at, k, radix):
    if radix & (radix - 1) == 0:
        return at ^ k
    return (at + radix - k) % radix


def matchings(count, radix, stride):
    if (count, radix, stride) == (8, 4, 2):
        swaps = ((1, 2), (3, 4), (5, 6), (0, 7)), ((0, 3), (1, 5), (2, 6), (4, 7)), ((0, 4), (1, 6), (2, 5), (3, 7))
        out = []
        for pairs in swaps:
            senders = [0] * count
            for a, b in pairs:
                senders[a], senders[b] = b, a
            out.append((senders, len(out) == 0))
        return out
    out = []
    for k in range(1, radix):
        senders = []
        for me in range(count):
            at, low = me // stride % radix, me % stride
            senders.append(me - low + (source(at, k, radix) - at) * stride + (stride - 1 - low))
        out.append((senders, any(abs(source(at, k, radix) - at) == 1 for at in range(radix))))
    return sorted(out, key=lambda item: not item[1])


def look_up(table):
    me, value = lax.axis_index("gy"), jnp.int32(table[0])
    for k in range(1, len(table)):
        value = jnp.where(me == k, table[k], value)
    return value


def stages(count):
    if count % 2:
        return [1, count]
    out, rest = [2], count // 2
    while rest > 1:
        radix = next((r for r in (8, 4, 2) if rest % r == 0), rest)
        out.append(radix)
        rest //= radix
    return out if len(out) > 1 else out + [1]


def exchange_stage(messages, swaps):
    return [
        lax.ppermute(message, "gy", [(sender, me) for me, sender in enumerate(senders)])
        for (senders, near), message in zip(swaps, messages)
    ]


class Group:
    def __init__(self, radix, stride, others, nx):
        self.radix, self.others, self.nx = radix, others, nx
        me = lax.axis_index("gy")
        self.swaps = [
            (look_up([sender // stride % radix for sender in senders]), near)
            for senders, near in matchings(lax.axis_size("gy"), radix, stride)
        ]
        self.at = lax.rem(lax.div(me, stride), radix)
        low = lax.rem(me, stride)
        self.lowest, self.highest = low == 0, low == stride - 1

    def map_of(self, place, own):
        rows = Rows(self.nx)
        out = own
        for (sender, near), ref in zip(self.swaps, self.others):
            here = sender == place
            got = [ref[i * rows.span : (i + 1) * rows.span] for i in range(2)]
            out = got if out is None else [jnp.where(here, new, old) for new, old in zip(got, out)]
        return out

    def ahead(self, slope, offset):
        a, b = jnp.ones_like(slope), jnp.zeros_like(slope)
        for place in range(self.radix - 1):
            new_a, new_b = self.map_of(place, None)
            below = place < self.at
            a, b = jnp.where(below, new_a * a, a), jnp.where(below, new_a * b + new_b, b)
        return slope * a, slope * b + offset

    def total(self, own):
        a, b = self.map_of(0, own)
        for place in range(1, self.radix):
            new_a, new_b = self.map_of(place, own)
            a, b = new_a * a, new_a * b + new_b
        return a, b

    def collect(self, near, final):
        rows = Rows(self.nx)
        for (place, adjacent), ref in zip(self.swaps, self.others):
            if not adjacent:
                continue

            @pl.when(self.lowest & (place == self.at - 1))
            def _():
                near[rows.low : rows.low + rows.info] = ref[rows.map : rows.final]

            @pl.when(self.highest & (place == self.at + 1))
            def _():
                near[rows.high : rows.high + rows.info] = ref[rows.map : rows.final]
                rest = slice(0, rows.map) if final else slice(rows.final, rows.full)
                near[rows.high + rows.info : rows.near] = ref[rest]


def start_near(near, nx, nz):
    rows = Rows(nx)
    near[: rows.span] = jnp.ones((rows.span, nz), jnp.float32)
    near[rows.span :] = jnp.zeros((near.shape[0] - rows.span, nz), jnp.float32)


def join_kernel(radix, stride, final, nx, is_first, *refs):
    rows = Rows(nx)
    total, last_info, first_info, near_in = refs[:4]
    others, near, outs = refs[4 : 3 + radix], refs[3 + radix], refs[4 + radix :]
    nz = near.shape[1]
    if is_first:
        start_near(near, nx, nz)
    else:
        near[...] = near_in[...]
    group = Group(radix, stride, others, nx)
    own = [total[i * rows.span : (i + 1) * rows.span] for i in range(2)]
    ahead = group.ahead(near[: rows.span], near[rows.span : rows.map])
    write_rows(near, ahead)
    group.collect(near, False)
    whole = group.total(own)
    if final == 0:
        write_rows(outs[0], whole)
        return
    me, count = lax.axis_index("gy"), lax.axis_size("gy")
    for (senders, adjacent), out in zip(matchings(count, final, stride * radix), outs):
        up = look_up(senders) > me
        if not adjacent:
            write_rows(out, whole)
            continue

        @pl.when(up)
        def _():
            write_rows(out, whole)
            out[rows.map : rows.final] = last_info[: rows.info]

        @pl.when(jnp.logical_not(up))
        def _():
            out[: rows.map] = first_info[rows.info : rows.info + rows.rest]
            out[rows.map : rows.final] = first_info[: rows.info]


def full_message(nx, total, last_info, first_info, senders):
    rows = Rows(nx)
    onward = jnp.concatenate([total[: rows.map], last_info[: rows.info], first_info[rows.info : rows.info + rows.rest]])
    back = jnp.concatenate([total[: rows.map], first_info[: rows.info + rows.rest]])
    message = jnp.where(look_up(senders) > lax.axis_index("gy"), onward, back)
    return jnp.pad(message, ((0, -rows.full % 8), (0, 0)))


def third_kernel(radix, stride, *refs):
    st, extra, coarse, near_in = refs[:4]
    others, (out, sc, wide, near, done, sems) = refs[4 : 3 + radix], refs[3 + radix :]
    planes, rows, ext, nz = st.shape
    ny, nx = rows - 2, ext - 2 * PAD
    edge = edge_weights((ext, nz))
    blocks = ny // 2

    lay = Rows(nx)
    span = lay.span
    near[...] = near_in[...]
    group = Group(radix, stride, others, nx)
    if radix > 1:
        group.collect(near, True)
    gas_in = group.ahead(near[:span], near[span : lay.map])[1]
    at_high = lay.high + lay.info
    starts = [lay.low, lay.low + span, lay.high, lay.high + span, at_high, at_high + span]
    for k, v in enumerate([gas_in] + [near[start : start + span] for start in starts]):
        wide[k, : PAD - 2] = jnp.zeros((PAD - 2, nz), jnp.float32)
        wide[k, ext - PAD + 2 :] = jnp.zeros((PAD - 2, nz), jnp.float32)
        wide[k, pl.ds(PAD - 2, span, 2), :] = v
        wide[k, pl.ds(PAD - 1, span, 2), :] = v
    for k, start in enumerate((lay.low, lay.low + nx + 2, lay.high, lay.high + nx + 2)):
        start += lay.map
        wide[7 + k, :PAD] = jnp.zeros((PAD, nz), jnp.float32)
        wide[7 + k, ext - PAD :] = jnp.zeros((PAD, nz), jnp.float32)
        wide[7 + k, PAD - 1 : PAD + nx + 1] = near[start : start + nx + 2]

    gas_in = wide[0]
    last = ny + 1
    solid_low = wide[1] + wide[2] * gas_in
    sc[0, 0] = st[SA, 0] + solid_low
    sc[1, 0] = st[GA, 0] + gas_in

    def correct(j, carry):
        gas = coarse[2, j] * gas_in + coarse[3, j]
        solid = coarse[0, j] + coarse[1, j] * gas
        for i in (2 * j + 1, 2 * j + 2):
            sc[0, i] = st[SA, i] + solid
            sc[1, i] = st[GA, i] + gas
        return carry

    lax.fori_loop(0, blocks, correct, 0)
    gas = coarse[2, blocks - 1] * gas_in + coarse[3, blocks - 1]
    gas_high = wide[5] * gas + wide[4]
    solid_high = wide[3] + wide[6] * gas_high
    sc[0, last] = st[SA, last] + solid_high
    sc[1, last] = st[GA, last] + gas_high

    view = Fields(st, sc)
    for i, is_after, solid, gas in ((0, False, solid_low, gas_in), (last, True, solid_high, gas_high)):
        side = 3 if is_after else 0
        fy = extra[side + 2]
        to = 9 if is_after else 7
        rs = extra[side] + wide[to] + fy * solid
        rg = extra[side + 1] + wide[to + 1] + (CONDUCT if is_after else CONDUCT + FLOW) * gas
        res = outer_residual(view, i, SA, rs, rg, fy, edge, is_after)
        sc[2, i], sc[3, i] = relaxed(view, i, SA, *res)

    def sweep(k, carry):
        stores = []
        for r in range(GROUP):
            i = GROUP * k + 1 + r
            new_s, new_g = relaxed(view, i, SA, *row_residual(view, i, SA, edge))
            stores += [((2, i), new_s), ((3, i), new_g)]
        for at, value in stores:
            sc[at] = value
        return carry

    lax.fori_loop(0, ny // GROUP, sweep, 0)

    def leaving(k):
        part = pl.ds(GROUP * k, GROUP)
        return pltpu.make_async_copy(done.at[:, part], out.at[:, part], sems.at[k])

    def final(k, carry):
        stores = []
        for r in range(GROUP):
            i = GROUP * k + 1 + r
            new_s, new_g = last_relaxed(view, i, SB, edge, slice(PAD, PAD + nx))
            stores += [((0, i - 1), new_s), ((1, i - 1), new_g)]
        for at, value in stores:
            done[at] = value
        leaving(k).start()
        return carry

    lax.fori_loop(0, ny // GROUP, final, 0)
    for k in range(ny // GROUP):
        leaving(k).wait()


class Fields:
    def __init__(self, st, sc):
        self.st, self.sc = st, sc

    def __getitem__(self, at):
        return (self.sc if at[0] <= GB else self.st)[at]


def cost(rows, cells):
    return pl.CostEstimate(flops=50 * rows * cells, bytes_accessed=16 * 4 * rows * cells, transcendentals=0)


def swap(x, axis, first):
    pairs = []
    for i in range(first, lax.axis_size(axis) - 1, 2):
        pairs += [(i, i + 1), (i + 1, i)]
    return lax.ppermute(x, axis, pairs)


def shards(temps, right_side, exchange, coupling):
    temps, right_side = (jnp.transpose(a, (0, 2, 1, 3)) for a in (temps, right_side))
    exchange, coupling = (jnp.transpose(a, (1, 0, 2)) for a in (exchange, coupling))
    temps, right_side, exchange, coupling = (
        pltpu.with_memory_space_constraint(a, pltpu.HBM) for a in (temps, right_side, exchange, coupling)
    )
    ny, nx, nz = exchange.shape
    ext = nx + 2 * PAD
    f32 = functools.partial(jax.ShapeDtypeStruct, dtype=jnp.float32)

    strip = f32(((ny * STRIP_ROWS + 7) // 8 * 8, nz))
    state = f32((PLANES, ny + 2, ext, nz))
    one, two, early, st = pl.pallas_call(
        pack_kernel,
        out_shape=(strip, strip, f32((EARLY, nx, nz)), state),
        in_specs=[HBM] * 4,
        out_specs=(VMEM,) * 4,
        scratch_shapes=[pltpu.SemaphoreType.DMA((6,))],
        compiler_params=PARAMS,
        name="pack_x",
    )(temps, right_side, exchange, coupling)
    one, two = swap(one, "gx", 0), swap(two, "gx", 1)
    early = swap(early, "gy", 1)

    def letter(planes):
        return f32((planes, ext - 2 * CROP, nz))

    st = pl.pallas_call(
        conduct_kernel,
        out_shape=state,
        in_specs=[VMEM],
        out_specs=VMEM,
        input_output_aliases={0: 0},
        compiler_params=PARAMS,
        cost_estimate=cost(2 * ny, ext * nz),
        name="conduct",
    )(st)
    st, across, *beside = pl.pallas_call(
        first_kernel,
        out_shape=(state, f32((across_parts(ext)[1], nz))) + (letter(THIRD),) * (MESSAGE // THIRD),
        in_specs=[VMEM] * 3,
        out_specs=(VMEM,) * (2 + MESSAGE // THIRD),
        input_output_aliases={0: 0},
        compiler_params=PARAMS,
        name="first",
    )(st, one, two)
    across = swap(across, "gy", 1)

    rows = f32((4, ny // 2, ext, nz))
    st, coarse = pl.pallas_call(
        inner_kernel,
        out_shape=(state, rows),
        in_specs=[VMEM] * 4,
        out_specs=(VMEM,) * 2,
        input_output_aliases={0: 0},
        compiler_params=PARAMS,
        cost_estimate=cost(4 * ny, ext * nz),
        name="inner",
    )(st, one, two, early)

    beside = [swap(part, "gy", 0) for part in beside]

    lay = Rows(nx)

    def tall(height):
        return f32(((height + 7) // 8 * 8, nz))

    letter_room = pltpu.VMEM((MESSAGE, ext, nz), jnp.float32)
    more = f32((6, ext, nz))
    st, coarse, extra = pl.pallas_call(
        near_kernel,
        out_shape=(state, rows, more),
        in_specs=[VMEM] * (2 + len(beside)),
        out_specs=(VMEM,) * 3,
        scratch_shapes=[letter_room],
        input_output_aliases={0: 0, 1: 1},
        compiler_params=PARAMS,
        name="near",
    )(st, coarse, *beside)
    st, coarse, extra, total, last_info, first_info, message = pl.pallas_call(
        second_kernel,
        out_shape=(state, rows, more, tall(lay.map), tall(lay.info), tall(lay.info + lay.rest), tall(lay.full)),
        in_specs=[VMEM] * 5,
        out_specs=(VMEM,) * 7,
        scratch_shapes=[letter_room, pltpu.VMEM((8, ext, nz), jnp.float32)],
        input_output_aliases={0: 0, 1: 1, 2: 2},
        compiler_params=PARAMS,
        name="second",
    )(st, coarse, extra, early, across)

    near, messages = total, [message]
    count = lax.axis_size("gy")
    radices, stride = stages(count), 1
    for place, radix in enumerate(radices[:-1]):
        swaps = matchings(count, radix, stride)
        if place:
            messages = [full_message(nx, total, last_info, first_info, senders) for senders, _ in swaps]
        others = exchange_stage(messages, swaps)
        final = radices[-1] if place == len(radices) - 2 else 0
        following = matchings(count, final, stride * radix) if final else []
        outs = [tall(lay.final if adjacent else lay.map) for _, adjacent in following] if final else [tall(lay.map)]
        near, *messages = pl.pallas_call(
            functools.partial(join_kernel, radix, stride, final, nx, place == 0),
            out_shape=(tall(lay.near), *outs),
            in_specs=[VMEM] * (3 + radix),
            out_specs=(VMEM,) * (1 + len(outs)),
            compiler_params=PARAMS,
            name="join",
        )(total, last_info, first_info, near, *others)
        total = total if final else messages[0]
        stride *= radix
    got = exchange_stage(messages, matchings(count, radices[-1], stride))

    out = pl.pallas_call(
        functools.partial(third_kernel, radices[-1], stride),
        out_shape=f32((2, ny, nx, nz)),
        in_specs=[VMEM] * (4 + len(got)),
        out_specs=HBM,
        scratch_shapes=[
            pltpu.VMEM((4, ny + 2, ext, nz), jnp.float32),
            pltpu.VMEM((11, ext, nz), jnp.float32),
            pltpu.VMEM(tall(lay.near).shape, jnp.float32),
            pltpu.VMEM((2, ny, nx, nz), jnp.float32),
            pltpu.SemaphoreType.DMA((ny // GROUP,)),
        ],
        compiler_params=PARAMS,
        name="third",
    )(st, extra, coarse, near, *got)
    return jnp.transpose(out, (0, 2, 1, 3))


def solution(mesh):
    return jax.shard_map(
        shards,
        mesh=mesh,
        in_specs=(
            P(None, "gx", "gy", None),
            P(None, "gx", "gy", None),
            P("gx", "gy", None),
            P("gx", "gy", None),
        ),
        out_specs=P(None, "gx", "gy", None),
        check_vma=False,
    )
```

```python
import functools

import jax
import jax.numpy as jnp
from jax import lax
from jax.experimental import pallas as pl
from jax.experimental.pallas import tpu as pltpu
from jax.sharding import PartitionSpec as P

SOLID_CAP, GAS_CAP, FLOW, CONDUCT, RELAX, LUMP = 0.5, 0.02, 40.0, 0.05, 0.8, 0.25
GAS_SELF = GAS_CAP + 4.5 * CONDUCT

PAD = 8
WX = 5
CROP = 4
(SA, GA, SB, GB, K, C, RS, RG, FX, FZ, H, FY, ASS, ASG, AGG) = range(15)
PLANES = 15
(M_S, M_G, M_K, M_C, M_FY, M_1S, M_1G, M_2S, M_2G) = range(9)
MESSAGE, EARLY, THIRD = 9, 7, 3

GROUP = 4

VMEM = pl.BlockSpec(memory_space=pltpu.VMEM)
HBM = pl.BlockSpec(memory_space=pltpu.HBM)
PARAMS = pltpu.CompilerParams(vmem_limit_bytes=40 * 1024 * 1024)


def up_x(v):
    return pltpu.roll(v, v.shape[0] - 1, 0)


def down_x(v):
    return pltpu.roll(v, 1, 0)


def up_z(v):
    return pltpu.roll(v, v.shape[1] - 1, 1)


def down_z(v):
    return pltpu.roll(v, 1, 1)


def lanes(shape):
    return lax.broadcasted_iota(jnp.int32, shape, 1)


def x_mask(shape, nx):
    row = lax.broadcasted_iota(jnp.int32, shape, 0)
    place, count = lax.axis_index("gx"), lax.axis_size("gx")
    low = jnp.where(place == 0, PAD, PAD - WX)
    high = jnp.where(place == count - 1, PAD + nx, PAD + nx + WX)
    return jnp.where((row >= low) & (row < high), 1.0, 0.0).astype(jnp.float32)


STRIP = ((SA, WX - 1), (GA, WX - 1), (K, WX), (RS, WX - 1), (RG, WX - 1), (C, WX - 1))
STRIP_ROWS = sum(width for plane, width in STRIP)


def conductivity_of(s, exchange):
    return 1.0 + 4.0 * exchange * s * s * s


def strip_values(s, g, k, rs, rg, c, low):
    out, inn = (WX - 1, WX - 2) if low else (8 - WX, 9 - WX)
    four = slice(0, WX - 1) if low else slice(9 - WX, 8)
    five = slice(0, WX) if low else slice(8 - WX, 8)
    row = lax.broadcasted_iota(jnp.int32, s.shape, 0)
    rs = rs + jnp.where(row == inn, 0.5 * (k[inn : inn + 1] + k[out : out + 1]) * s[out : out + 1], 0.0)
    rg = rg + jnp.where(row == inn, CONDUCT * g[out : out + 1], 0.0)
    return [s[four], g[four], k[five], rs[four], rg[four], c[four]]


def x_order():
    return (lax.axis_index("gx") % 2 == 0) == (lax.axis_index("gy") % 2 == 1)


def pack_kernel(temps, right, exchange, coupling, one, two, early, st, sems):
    high_first = x_order()
    odd = lax.axis_index("gy") % 2 == 1
    ny, nx, nz = exchange.shape
    copies = []
    for k, (plane, ref) in enumerate(
        ((SA, temps.at[0]), (K, exchange), (GA, temps.at[1]), (C, coupling), (RS, right.at[0]), (RG, right.at[1]))
    ):
        to = st.at[plane, pl.ds(1, ny), pl.ds(PAD, nx)]
        copies.append(pltpu.make_async_copy(ref, to, sems.at[k]))
    for copy in copies:
        copy.start()
    for copy in copies:
        copy.wait()
    at = 0
    for i in range(1, ny + 1):
        sides = []
        for start in (PAD, PAD + nx - 8):
            s, g, e, rs, rg, c = (st[plane, i, start : start + 8] for plane in (SA, GA, K, RS, RG, C))
            sides.append(strip_values(s, g, conductivity_of(s, e), rs, rg, c, start == PAD))
        for low, high, (plane, width) in zip(*sides, STRIP):
            one[at : at + width] = jnp.where(high_first, high, low)
            two[at : at + width] = jnp.where(high_first, low, high)
            at += width
    own = slice(PAD, PAD + nx)
    for is_odd, e, d in ((True, ny, ny - 1), (False, 1, 2)):

        @pl.when(odd == is_odd)
        def _():
            s, s_d, g, g_d = st[SA, e, own], st[SA, d, own], st[GA, e, own], st[GA, d, own]
            c, k, k_d = st[C, e, own], conductivity_of(s, st[K, e, own]), conductivity_of(s_d, st[K, d, own])
            fx, fz, h, _ = faces(k)
            fy = 0.5 * (k + k_d)
            part_s, part_g = inner(s, g, c, h, fx, fz, edge_weights((nx, nz)))
            m_1s, m_1g = first_partial(st[RS, e, own] + part_s, st[RG, e, own] + part_g, s, s_d, g, g_d, fy, is_odd)
            for plane, value in enumerate((s, g, k, c, fy, m_1s, m_1g)):
                early[plane] = value


def conduct_kernel(st_in, st):
    del st_in
    planes, rows, ext, nz = st.shape
    own = slice(PAD, ext - PAD)
    zeros = jnp.zeros((PAD, nz), jnp.float32)
    for i in range(1, rows - 1):
        st[K, i, own] = conductivity_of(st[SA, i, own], st[K, i, own])
        for plane, width in STRIP:
            st[plane, i, :PAD] = zeros
            st[plane, i, ext - PAD :] = zeros


def place_halo(st, one, two, y, nx):
    high_first = x_order()
    at, i = y * STRIP_ROWS, y + 1
    for plane, width in STRIP:
        a, b = one[at : at + width], two[at : at + width]
        st[plane, i, PAD - width : PAD] = jnp.where(high_first, b, a)
        st[plane, i, PAD + nx : PAD + nx + width] = jnp.where(high_first, a, b)
        at += width


def inner(s, g, c, h, fx, fz, edge):
    t = c * (s - g)
    flux_x = fx * (up_x(s) - s)
    flux_z = fz * (up_z(s) - s)
    part_s = (flux_x - down_x(flux_x)) + (flux_z - down_z(flux_z)) - h * s - t
    part_g = (
        t
        - GAS_SELF * g
        + CONDUCT * (up_x(g) + down_x(g))
        + edge[0] * up_z(g)
        + edge[1] * down_z(g)
    )
    return part_s, part_g


def edge_weights(shape):
    lane = lanes(shape)
    weight = jnp.float32(0.25 * CONDUCT)
    return jnp.where(lane == shape[1] - 1, 0.0, weight), jnp.where(lane == 0, 0.0, weight)


def row_inner(st, i, s_at, edge):
    return inner(st[s_at, i], st[s_at + 1, i], st[C, i], st[H, i], st[FX, i], st[FZ, i], edge)


def row_residual(st, i, s_at, edge):
    part_s, part_g = row_inner(st, i, s_at, edge)
    s, g, before = st[s_at, i], st[s_at + 1, i], st[s_at + 1, i - 1]
    part_s += st[FY, i] * (st[s_at, i + 1] - s) + st[FY, i - 1] * (st[s_at, i - 1] - s)
    part_g += CONDUCT * (st[s_at + 1, i + 1] + before) - FLOW * (g - before)
    return st[RS, i] + part_s, st[RG, i] + part_g


def relaxed(st, i, s_at, res_s, res_g):
    s = st[s_at, i] + st[ASS, i] * res_s + st[ASG, i] * res_g
    g = st[s_at + 1, i] + st[ASG, i] * res_s + st[AGG, i] * res_g
    return s, g


def faces(k):
    lane = lanes(k.shape)
    end = k.shape[1] - 1
    fx = 0.5 * (k + up_x(k))
    fz = jnp.where(lane == end, 0.0, 0.125 * (k + up_z(k)))
    h = SOLID_CAP + jnp.where((lane == 0) | (lane == end), 0.125 * k, 0.0)
    return fx, fz, h, h + (fx + down_x(fx)) + (fz + down_z(fz))


def inverse(diag, c, mask):
    gas_diag = (GAS_SELF + FLOW) + c
    inv = (RELAX * mask) / (diag * gas_diag - c * c)
    return inv * gas_diag, inv * c, inv * diag


def last_relaxed(st, i, s_at, edge, own):
    full_s, full_g = st[s_at, i], st[s_at + 1, i]
    s, g = full_s[own], full_g[own]
    flux_x = st[FX, i] * (up_x(full_s) - full_s)
    flux_z = st[FZ, i, own] * (up_z(s) - s)
    c, before = st[C, i, own], st[s_at + 1, i - 1, own]
    t = c * (s - g)
    res_s = st[RS, i, own] + (flux_x[own] - down_x(flux_x)[own]) + (flux_z - down_z(flux_z)) - st[H, i, own] * s - t
    res_s += st[FY, i, own] * (st[s_at, i + 1, own] - s) + st[FY, i - 1, own] * (st[s_at, i - 1, own] - s)
    res_g = st[RG, i, own] + t - GAS_SELF * g + edge[0][own] * up_z(g) + edge[1][own] * down_z(g)
    res_g += CONDUCT * (up_x(full_g)[own] + down_x(full_g)[own] + st[s_at + 1, i + 1, own] + before) - FLOW * (g - before)
    ss, sg, gg = st[ASS, i, own], st[ASG, i, own], st[AGG, i, own]
    return s + ss * res_s + sg * res_g, g + sg * res_s + gg * res_g


def grouped(rows, work):
    for start in range(0, len(rows), GROUP):
        stores = []
        for i in rows[start : start + GROUP]:
            stores += work(i)
        for ref, at, value in stores:
            ref[at] = value


def row_coefficients(st, i, mask):
    fx, fz, h, diag = faces(st[K, i])
    fy = 0.5 * (st[K, i] + st[K, i + 1])
    before = 0.5 * (st[K, i] + st[K, i - 1])
    ss, sg, gg = inverse(diag + st[C, i] + fy + before, st[C, i], mask)
    values = ((FX, fx), (FZ, fz), (H, h), (FY, fy), (ASS, ss), (ASG, sg), (AGG, gg))
    return [(st, (plane, i), v) for plane, v in values]


def row_sweep(st, i, source, target, edge):
    s, g = relaxed(st, i, source, *row_residual(st, i, source, edge))
    return [(st, (target, i), s), (st, (target + 1, i), g)]


def first_partial(res_s, res_g, s, s_d, g, g_d, fy, onward):
    return res_s + fy * (s_d - s), res_g + CONDUCT * g_d - FLOW * (g - g_d if onward else g)


def send_planes(st, onward, edge):
    ny = st.shape[1] - 2
    e, d, near = (ny, ny - 1, ny - 1) if onward else (1, 2, 1)
    fy, s, g, g_d = st[FY, near], st[SA, e], st[GA, e], st[GA, d]
    part_s, part_g = row_inner(st, e, SA, edge)
    m_1s, m_1g = first_partial(st[RS, e] + part_s, st[RG, e] + part_g, s, st[SA, d], g, g_d, fy, onward)
    m_2s = st[RS, e] + fy * st[SB, d]
    m_2g = st[RG, e] + (CONDUCT + FLOW if onward else CONDUCT) * st[GB, d]
    return [s, g, st[K, e], st[C, e], fy, m_1s, m_1g, m_2s, m_2g]


def across_parts(ext):
    parts, at = [], 0
    for k in range(EARLY, MESSAGE):
        parts.append((k, CROP, ext - CROP, at))
        at += ext - 2 * CROP
    for k in range(EARLY):
        more = 1 if k in (M_1S, M_1G) else 0
        for low, high in ((CROP, PAD + more), (ext - PAD - more, ext - CROP)):
            parts.append((k, low, high, at))
            at += high - low
    return parts, (at + 7) // 8 * 8


def write_across(ref, k, value):
    for plane, low, high, at in across_parts(value.shape[0])[0]:
        if plane == k:
            ref[at : at + high - low] = value[low:high]


def read_across(early, across, outer, k):
    ext = outer.shape[1]
    if k < EARLY:
        outer[k, PAD : ext - PAD] = early[k]
    for plane, low, high, at in across_parts(ext)[0]:
        if plane == k:
            outer[k, low:high] = across[at : at + high - low]


def write_beside(refs, k, value):
    refs[k // THIRD][k % THIRD] = value[CROP : value.shape[0] - CROP]


def read_beside(refs, outer, k):
    outer[k, CROP : outer.shape[1] - CROP] = refs[k // THIRD][k % THIRD]


def write_message(write, st, onward, edge):
    for go in (True, False):

        @pl.when(onward == go)
        def _():
            for k, value in enumerate(send_planes(st, go, edge)):
                write(k, value)


def first_kernel(st_in, one, two, st, across, *beside):
    del st_in
    planes, rows, ext, nz = st.shape
    ny, nx = rows - 2, ext - 2 * PAD
    shape = (ext, nz)
    mask = x_mask(shape, nx)
    edge = edge_weights(shape)

    for y in list(range(4)) + list(range(ny - 4, ny)):
        place_halo(st, one, two, y, nx)
    for i in (1, ny):
        fx, fz, h, diag = faces(st[K, i])
        st[FX, i], st[FZ, i], st[H, i] = fx, fz, h
    st[FY, 1] = 0.5 * (st[K, 1] + st[K, 2])
    st[FY, ny - 3] = 0.5 * (st[K, ny - 3] + st[K, ny - 2])
    ends = [2, 3, ny - 2, ny - 1]
    grouped(ends, lambda i: row_coefficients(st, i, mask))
    grouped(ends, lambda i: row_sweep(st, i, SA, SB, edge))
    odd = lax.axis_index("gy") % 2 == 1
    write_message(functools.partial(write_across, across), st, odd, edge)
    write_message(functools.partial(write_beside, beside), st, jnp.logical_not(odd), edge)


def outer_residual(st, i, s_at, rs, rg, fy_out, edge, after):
    part_s, part_g = row_inner(st, i, s_at, edge)
    s, g = st[s_at, i], st[s_at + 1, i]
    if after:
        part_s += st[FY, i - 1] * (st[s_at, i - 1] - s)
        part_g += (CONDUCT + FLOW) * st[s_at + 1, i - 1]
    else:
        part_s += st[FY, i] * (st[s_at, i + 1] - s)
        part_g += CONDUCT * st[s_at + 1, i + 1]
    return rs + part_s - fy_out * s, rg + part_g - FLOW * g


def pair_x(v):
    row = lax.broadcasted_iota(jnp.int32, v.shape, 0)
    return v + jnp.where(row % 2 == 0, up_x(v), down_x(v))


def coarse_coefficients(c_sum, k_sum):
    solid = 4.0 * SOLID_CAP + c_sum + LUMP * k_sum
    ratio = c_sum / solid
    denominator = (4.0 * GAS_CAP + 2.0 * FLOW) + c_sum - c_sum * ratio
    return solid, ratio, denominator


def coarse_row(st, coarse, j, mask, edge):
    i = 2 * j + 1
    res_s, res_g = row_residual(st, i, SA, edge)
    more_s, more_g = row_residual(st, i + 1, SA, edge)
    res_s, res_g = pair_x((res_s + more_s) * mask), pair_x((res_g + more_g) * mask)
    c_sum = pair_x(st[C, i] + st[C, i + 1])
    solid, ratio, denominator = coarse_coefficients(c_sum, pair_x(st[K, i] + st[K, i + 1]))
    lead = res_s / solid
    values = (lead, ratio, (2.0 * FLOW) / denominator, (res_g + c_sum * lead) / denominator)
    return [(coarse, (k, j), v) for k, v in enumerate(values)]


def inner_kernel(st_in, one, two, early, st, coarse):
    del st_in, early
    planes, rows, ext, nz = st.shape
    ny, nx = rows - 2, ext - 2 * PAD
    shape = (ext, nz)
    mask = x_mask(shape, nx)
    edge = edge_weights(shape)
    for y in range(4, ny - 4):
        place_halo(st, one, two, y, nx)
    grouped(list(range(4, ny - 2)), lambda i: row_coefficients(st, i, mask))
    grouped(list(range(4, ny - 2)), lambda i: row_sweep(st, i, SA, SB, edge))
    grouped(list(range(3, ny - 1)), lambda i: row_sweep(st, i, SB, SA, edge))
    for j in range(2, ny // 2 - 2):
        for ref, at, value in coarse_row(st, coarse, j, mask, edge):
            ref[at] = value


def end_work(st, coarse, extra, read, outer, is_after):
    planes, rows, ext, nz = st.shape
    ny, nx = rows - 2, ext - 2 * PAD
    me, count = lax.axis_index("gy"), lax.axis_size("gy")
    mask = x_mask((ext, nz), nx)
    inside = jnp.where(me == (count - 1 if is_after else 0), 0.0, mask)
    edge = edge_weights((ext, nz))
    zeros = jnp.zeros((PAD, nz), jnp.float32)
    for k in range(MESSAGE):
        outer[k, :PAD] = zeros
        outer[k, ext - PAD :] = zeros
        read(outer, k)

    o, e, near = (ny + 1, ny, ny) if is_after else (0, 1, 0)
    to_o = CONDUCT + FLOW if is_after else CONDUCT
    s_o, g_o, k_o, c_o, fy_out = (outer[plane] for plane in (M_S, M_G, M_K, M_C, M_FY))
    fy = 0.5 * (k_o + st[K, e])
    fx, fz, h, diag = faces(k_o)
    inv_o = inverse(diag + c_o + fy_out + fy, c_o, inside)
    fx_e, fz_e = st[FX, e], st[FZ, e]
    diag = st[H, e] + (fx_e + down_x(fx_e)) + (fz_e + down_z(fz_e)) + st[C, e] + fy
    inv_e = inverse(diag + st[FY, near - 1 if is_after else near + 1], st[C, e], mask)
    for plane, value in ((SA, s_o), (GA, g_o), (K, k_o), (C, c_o), (FX, fx), (FZ, fz), (H, h)):
        st[plane, o] = value
    st[FY, near] = fy
    for k in range(3):
        st[ASS + k, o], st[ASS + k, e] = inv_o[k], inv_e[k]

    res = outer[M_1S] + fy * (st[SA, e] - s_o), outer[M_1G] + to_o * st[GA, e]
    new_o = relaxed(st, o, SA, *res)
    stores = row_sweep(st, e, SA, SB, edge)
    st[SB, o], st[GB, o] = new_o
    for ref, at, value in stores:
        ref[at] = value
    res = outer_residual(st, o, SB, outer[M_2S], outer[M_2G], fy_out, edge, is_after)
    new_o = relaxed(st, o, SB, *res)
    ends = [e - 1, e] if is_after else [e, e + 1]
    grouped(ends, lambda i: row_sweep(st, i, SB, SA, edge))
    st[SA, o], st[GA, o] = new_o
    for k, plane in enumerate((M_2S, M_2G, M_FY)):
        extra[(3 if is_after else 0) + k] = outer[plane]
    blocks = ny // 2
    stores = []
    for j in (blocks - 2, blocks - 1) if is_after else (0, 1):
        stores += coarse_row(st, coarse, j, mask, edge)
    for ref, at, value in stores:
        ref[at] = value


def either_end(after, st, coarse, extra, read, outer):
    for is_after in (True, False):

        @pl.when(after == is_after)
        def _():
            end_work(st, coarse, extra, read, outer, is_after)


def near_kernel(st_in, coarse_in, *refs):
    beside, (st, coarse, extra, outer) = refs[:-4], refs[-4:]
    del st_in, coarse_in
    either_end(lax.axis_index("gy") % 2 == 0, st, coarse, extra, functools.partial(read_beside, beside), outer)


def second_kernel(st_in, coarse_in, extra_in, early, across, *refs):
    st, coarse, extra, total, last_info, first_info, message, outer, squeeze = refs
    del st_in, coarse_in, extra_in
    planes, rows, ext, nz = st.shape
    ny, nx = rows - 2, ext - 2 * PAD
    me = lax.axis_index("gy")
    either_end(me % 2 == 1, st, coarse, extra, functools.partial(read_across, early, across), outer)

    blocks = ny // 2
    for k in range(4):
        squeeze[k] = coarse[k, 0]
    slopes, offsets = coarse[2, 0], coarse[3, 0]
    for j in range(1, blocks):
        slope = coarse[2, j]
        slopes, offsets = slope * slopes, slope * offsets + coarse[3, j]
        coarse[2, j], coarse[3, j] = slopes, offsets
    squeeze[4], squeeze[5], squeeze[6], squeeze[7] = slopes, offsets, coarse[0, blocks - 1], coarse[1, blocks - 1]

    span = nx // 2 + 2
    lead, ratio, slope, offset, slopes, offsets, lead_last, ratio_last = (
        squeeze[k, pl.ds(PAD - 2, span, 2), :] for k in range(8)
    )
    part = slice(PAD - 1, PAD + nx + 1)

    def increments(d, face, gas):
        return [(st[FY, face] * (st[SA, d] - st[SB, d]))[part], (gas * (st[GA, d] - st[GB, d]))[part]]

    onward = [lead_last, ratio_last] + increments(ny - 1, ny - 1, CONDUCT + FLOW)
    back = [lead, offset] + increments(2, 1, CONDUCT) + [slope, ratio]
    write_rows(total, [slopes, offsets])
    write_rows(last_info, onward)
    write_rows(first_info, back)
    for go, info in ((True, onward), (False, back)):

        @pl.when((me % 2 == 0) == go)
        def _():
            write_rows(message, [slopes, offsets] + info)


def write_rows(ref, values):
    at = 0
    for value in values:
        ref[at : at + value.shape[0]] = value
        at += value.shape[0]


class Rows:
    def __init__(self, nx):
        self.span = nx // 2 + 2
        self.map = 2 * self.span
        self.info = self.map + 2 * (nx + 2)
        self.rest = self.map
        self.final = self.map + self.info
        self.full = self.final + self.rest
        self.low = self.map
        self.high = self.low + self.info
        self.near = self.high + self.info + self.rest


def source(at, k, radix):
    if radix & (radix - 1) == 0:
        return at ^ k
    return (at + radix - k) % radix


def matchings(count, radix, stride):
    if (count, radix, stride) == (8, 4, 2):
        swaps = ((1, 2), (3, 4), (5, 6), (0, 7)), ((0, 3), (1, 5), (2, 6), (4, 7)), ((0, 4), (1, 6), (2, 5), (3, 7))
        out = []
        for pairs in swaps:
            senders = [0] * count
            for a, b in pairs:
                senders[a], senders[b] = b, a
            out.append((senders, len(out) == 0))
        return out
    out = []
    for k in range(1, radix):
        senders = []
        for me in range(count):
            at, low = me // stride % radix, me % stride
            senders.append(me - low + (source(at, k, radix) - at) * stride + (stride - 1 - low))
        out.append((senders, any(abs(source(at, k, radix) - at) == 1 for at in range(radix))))
    return sorted(out, key=lambda item: not item[1])


def look_up(table):
    me, value = lax.axis_index("gy"), jnp.int32(table[0])
    for k in range(1, len(table)):
        value = jnp.where(me == k, table[k], value)
    return value


def stages(count):
    if count % 2:
        return [1, count]
    out, rest = [2], count // 2
    while rest > 1:
        radix = next((r for r in (8, 4, 2) if rest % r == 0), rest)
        out.append(radix)
        rest //= radix
    return out if len(out) > 1 else out + [1]


def exchange_stage(messages, swaps):
    return [
        lax.ppermute(message, "gy", [(sender, me) for me, sender in enumerate(senders)])
        for (senders, near), message in zip(swaps, messages)
    ]


class Group:
    def __init__(self, radix, stride, others, nx):
        self.radix, self.others, self.nx = radix, others, nx
        me = lax.axis_index("gy")
        self.swaps = [
            (look_up([sender // stride % radix for sender in senders]), near)
            for senders, near in matchings(lax.axis_size("gy"), radix, stride)
        ]
        self.at = lax.rem(lax.div(me, stride), radix)
        low = lax.rem(me, stride)
        self.lowest, self.highest = low == 0, low == stride - 1

    def map_of(self, place, own):
        rows = Rows(self.nx)
        out = own
        for (sender, near), ref in zip(self.swaps, self.others):
            here = sender == place
            got = [ref[i * rows.span : (i + 1) * rows.span] for i in range(2)]
            out = got if out is None else [jnp.where(here, new, old) for new, old in zip(got, out)]
        return out

    def ahead(self, slope, offset):
        a, b = jnp.ones_like(slope), jnp.zeros_like(slope)
        for place in range(self.radix - 1):
            new_a, new_b = self.map_of(place, None)
            below = place < self.at
            a, b = jnp.where(below, new_a * a, a), jnp.where(below, new_a * b + new_b, b)
        return slope * a, slope * b + offset

    def total(self, own):
        a, b = self.map_of(0, own)
        for place in range(1, self.radix):
            new_a, new_b = self.map_of(place, own)
            a, b = new_a * a, new_a * b + new_b
        return a, b

    def collect(self, near, final):
        rows = Rows(self.nx)
        for (place, adjacent), ref in zip(self.swaps, self.others):
            if not adjacent:
                continue

            @pl.when(self.lowest & (place == self.at - 1))
            def _():
                near[rows.low : rows.low + rows.info] = ref[rows.map : rows.final]

            @pl.when(self.highest & (place == self.at + 1))
            def _():
                near[rows.high : rows.high + rows.info] = ref[rows.map : rows.final]
                rest = slice(0, rows.map) if final else slice(rows.final, rows.full)
                near[rows.high + rows.info : rows.near] = ref[rest]


def start_near(near, nx, nz):
    rows = Rows(nx)
    near[: rows.span] = jnp.ones((rows.span, nz), jnp.float32)
    near[rows.span :] = jnp.zeros((near.shape[0] - rows.span, nz), jnp.float32)


def join_kernel(radix, stride, final, nx, is_first, *refs):
    rows = Rows(nx)
    total, last_info, first_info, near_in = refs[:4]
    others, near, outs = refs[4 : 3 + radix], refs[3 + radix], refs[4 + radix :]
    nz = near.shape[1]
    if is_first:
        start_near(near, nx, nz)
    else:
        near[...] = near_in[...]
    group = Group(radix, stride, others, nx)
    own = [total[i * rows.span : (i + 1) * rows.span] for i in range(2)]
    ahead = group.ahead(near[: rows.span], near[rows.span : rows.map])
    write_rows(near, ahead)
    group.collect(near, False)
    whole = group.total(own)
    if final == 0:
        write_rows(outs[0], whole)
        return
    me, count = lax.axis_index("gy"), lax.axis_size("gy")
    for (senders, adjacent), out in zip(matchings(count, final, stride * radix), outs):
        up = look_up(senders) > me
        if not adjacent:
            write_rows(out, whole)
            continue

        @pl.when(up)
        def _():
            write_rows(out, whole)
            out[rows.map : rows.final] = last_info[: rows.info]

        @pl.when(jnp.logical_not(up))
        def _():
            out[: rows.map] = first_info[rows.info : rows.info + rows.rest]
            out[rows.map : rows.final] = first_info[: rows.info]


def full_message(nx, total, last_info, first_info, senders):
    rows = Rows(nx)
    onward = jnp.concatenate([total[: rows.map], last_info[: rows.info], first_info[rows.info : rows.info + rows.rest]])
    back = jnp.concatenate([total[: rows.map], first_info[: rows.info + rows.rest]])
    message = jnp.where(look_up(senders) > lax.axis_index("gy"), onward, back)
    return jnp.pad(message, ((0, -rows.full % 8), (0, 0)))


def third_kernel(radix, stride, *refs):
    st, extra, coarse, near_in = refs[:4]
    others, (out, sc, wide, near, done, sems) = refs[4 : 3 + radix], refs[3 + radix :]
    planes, rows, ext, nz = st.shape
    ny, nx = rows - 2, ext - 2 * PAD
    edge = edge_weights((ext, nz))
    blocks = ny // 2

    lay = Rows(nx)
    span = lay.span
    near[...] = near_in[...]
    group = Group(radix, stride, others, nx)
    if radix > 1:
        group.collect(near, True)
    gas_in = group.ahead(near[:span], near[span : lay.map])[1]
    at_high = lay.high + lay.info
    starts = [lay.low, lay.low + span, lay.high, lay.high + span, at_high, at_high + span]
    for k, v in enumerate([gas_in] + [near[start : start + span] for start in starts]):
        wide[k, : PAD - 2] = jnp.zeros((PAD - 2, nz), jnp.float32)
        wide[k, ext - PAD + 2 :] = jnp.zeros((PAD - 2, nz), jnp.float32)
        wide[k, pl.ds(PAD - 2, span, 2), :] = v
        wide[k, pl.ds(PAD - 1, span, 2), :] = v
    for k, start in enumerate((lay.low, lay.low + nx + 2, lay.high, lay.high + nx + 2)):
        start += lay.map
        wide[7 + k, :PAD] = jnp.zeros((PAD, nz), jnp.float32)
        wide[7 + k, ext - PAD :] = jnp.zeros((PAD, nz), jnp.float32)
        wide[7 + k, PAD - 1 : PAD + nx + 1] = near[start : start + nx + 2]

    gas_in = wide[0]
    last = ny + 1
    solid_low = wide[1] + wide[2] * gas_in
    sc[0, 0] = st[SA, 0] + solid_low
    sc[1, 0] = st[GA, 0] + gas_in

    def correct(j, carry):
        gas = coarse[2, j] * gas_in + coarse[3, j]
        solid = coarse[0, j] + coarse[1, j] * gas
        for i in (2 * j + 1, 2 * j + 2):
            sc[0, i] = st[SA, i] + solid
            sc[1, i] = st[GA, i] + gas
        return carry

    lax.fori_loop(0, blocks, correct, 0)
    gas = coarse[2, blocks - 1] * gas_in + coarse[3, blocks - 1]
    gas_high = wide[5] * gas + wide[4]
    solid_high = wide[3] + wide[6] * gas_high
    sc[0, last] = st[SA, last] + solid_high
    sc[1, last] = st[GA, last] + gas_high

    view = Fields(st, sc)
    for i, is_after, solid, gas in ((0, False, solid_low, gas_in), (last, True, solid_high, gas_high)):
        side = 3 if is_after else 0
        fy = extra[side + 2]
        to = 9 if is_after else 7
        rs = extra[side] + wide[to] + fy * solid
        rg = extra[side + 1] + wide[to + 1] + (CONDUCT if is_after else CONDUCT + FLOW) * gas
        res = outer_residual(view, i, SA, rs, rg, fy, edge, is_after)
        sc[2, i], sc[3, i] = relaxed(view, i, SA, *res)

    def sweep(k, carry):
        stores = []
        for r in range(GROUP):
            i = GROUP * k + 1 + r
            new_s, new_g = relaxed(view, i, SA, *row_residual(view, i, SA, edge))
            stores += [((2, i), new_s), ((3, i), new_g)]
        for at, value in stores:
            sc[at] = value
        return carry

    lax.fori_loop(0, ny // GROUP, sweep, 0)

    def leaving(k):
        part = pl.ds(GROUP * k, GROUP)
        return pltpu.make_async_copy(done.at[:, part], out.at[:, part], sems.at[k])

    def final(k, carry):
        stores = []
        for r in range(GROUP):
            i = GROUP * k + 1 + r
            new_s, new_g = last_relaxed(view, i, SB, edge, slice(PAD, PAD + nx))
            stores += [((0, i - 1), new_s), ((1, i - 1), new_g)]
        for at, value in stores:
            done[at] = value
        leaving(k).start()
        return carry

    lax.fori_loop(0, ny // GROUP, final, 0)
    for k in range(ny // GROUP):
        leaving(k).wait()


class Fields:
    def __init__(self, st, sc):
        self.st, self.sc = st, sc

    def __getitem__(self, at):
        return (self.sc if at[0] <= GB else self.st)[at]


def cost(rows, cells):
    return pl.CostEstimate(flops=50 * rows * cells, bytes_accessed=16 * 4 * rows * cells, transcendentals=0)


def swap(x, axis, first):
    pairs = []
    for i in range(first, lax.axis_size(axis) - 1, 2):
        pairs += [(i, i + 1), (i + 1, i)]
    return lax.ppermute(x, axis, pairs)


def swap_x(x, place):
    columns = lax.axis_size("gy")
    pairs = []
    for column in range(columns):
        for i in range((column + 1 + place) % 2, lax.axis_size("gx") - 1, 2):
            a, b = i * columns + column, (i + 1) * columns + column
            pairs += [(a, b), (b, a)]
    return lax.ppermute(x, ("gx", "gy"), pairs)


def shards(temps, right_side, exchange, coupling):
    temps, right_side = (jnp.transpose(a, (0, 2, 1, 3)) for a in (temps, right_side))
    exchange, coupling = (jnp.transpose(a, (1, 0, 2)) for a in (exchange, coupling))
    temps, right_side, exchange, coupling = (
        pltpu.with_memory_space_constraint(a, pltpu.HBM) for a in (temps, right_side, exchange, coupling)
    )
    ny, nx, nz = exchange.shape
    ext = nx + 2 * PAD
    f32 = functools.partial(jax.ShapeDtypeStruct, dtype=jnp.float32)

    strip = f32(((ny * STRIP_ROWS + 7) // 8 * 8, nz))
    state = f32((PLANES, ny + 2, ext, nz))
    one, two, early, st = pl.pallas_call(
        pack_kernel,
        out_shape=(strip, strip, f32((EARLY, nx, nz)), state),
        in_specs=[HBM] * 4,
        out_specs=(VMEM,) * 4,
        scratch_shapes=[pltpu.SemaphoreType.DMA((6,))],
        compiler_params=PARAMS,
        name="pack_x",
    )(temps, right_side, exchange, coupling)
    one, two = swap_x(one, 0), swap_x(two, 1)
    early = swap(early, "gy", 1)

    def letter(planes):
        return f32((planes, ext - 2 * CROP, nz))

    st = pl.pallas_call(
        conduct_kernel,
        out_shape=state,
        in_specs=[VMEM],
        out_specs=VMEM,
        input_output_aliases={0: 0},
        compiler_params=PARAMS,
        cost_estimate=cost(2 * ny, ext * nz),
        name="conduct",
    )(st)
    st, across, *beside = pl.pallas_call(
        first_kernel,
        out_shape=(state, f32((across_parts(ext)[1], nz))) + (letter(THIRD),) * (MESSAGE // THIRD),
        in_specs=[VMEM] * 3,
        out_specs=(VMEM,) * (2 + MESSAGE // THIRD),
        input_output_aliases={0: 0},
        compiler_params=PARAMS,
        name="first",
    )(st, one, two)
    across = swap(across, "gy", 1)

    rows = f32((4, ny // 2, ext, nz))
    st, coarse = pl.pallas_call(
        inner_kernel,
        out_shape=(state, rows),
        in_specs=[VMEM] * 4,
        out_specs=(VMEM,) * 2,
        input_output_aliases={0: 0},
        compiler_params=PARAMS,
        cost_estimate=cost(4 * ny, ext * nz),
        name="inner",
    )(st, one, two, early)

    beside = [swap(part, "gy", 0) for part in beside]

    lay = Rows(nx)

    def tall(height):
        return f32(((height + 7) // 8 * 8, nz))

    letter_room = pltpu.VMEM((MESSAGE, ext, nz), jnp.float32)
    more = f32((6, ext, nz))
    st, coarse, extra = pl.pallas_call(
        near_kernel,
        out_shape=(state, rows, more),
        in_specs=[VMEM] * (2 + len(beside)),
        out_specs=(VMEM,) * 3,
        scratch_shapes=[letter_room],
        input_output_aliases={0: 0, 1: 1},
        compiler_params=PARAMS,
        name="near",
    )(st, coarse, *beside)
    st, coarse, extra, total, last_info, first_info, message = pl.pallas_call(
        second_kernel,
        out_shape=(state, rows, more, tall(lay.map), tall(lay.info), tall(lay.info + lay.rest), tall(lay.full)),
        in_specs=[VMEM] * 5,
        out_specs=(VMEM,) * 7,
        scratch_shapes=[letter_room, pltpu.VMEM((8, ext, nz), jnp.float32)],
        input_output_aliases={0: 0, 1: 1, 2: 2},
        compiler_params=PARAMS,
        name="second",
    )(st, coarse, extra, early, across)

    near, messages = total, [message]
    count = lax.axis_size("gy")
    radices, stride = stages(count), 1
    for place, radix in enumerate(radices[:-1]):
        swaps = matchings(count, radix, stride)
        if place:
            messages = [full_message(nx, total, last_info, first_info, senders) for senders, _ in swaps]
        others = exchange_stage(messages, swaps)
        final = radices[-1] if place == len(radices) - 2 else 0
        following = matchings(count, final, stride * radix) if final else []
        outs = [tall(lay.final if adjacent else lay.map) for _, adjacent in following] if final else [tall(lay.map)]
        near, *messages = pl.pallas_call(
            functools.partial(join_kernel, radix, stride, final, nx, place == 0),
            out_shape=(tall(lay.near), *outs),
            in_specs=[VMEM] * (3 + radix),
            out_specs=(VMEM,) * (1 + len(outs)),
            compiler_params=PARAMS,
            name="join",
        )(total, last_info, first_info, near, *others)
        total = total if final else messages[0]
        stride *= radix
    got = exchange_stage(messages, matchings(count, radices[-1], stride))

    out = pl.pallas_call(
        functools.partial(third_kernel, radices[-1], stride),
        out_shape=f32((2, ny, nx, nz)),
        in_specs=[VMEM] * (4 + len(got)),
        out_specs=HBM,
        scratch_shapes=[
            pltpu.VMEM((4, ny + 2, ext, nz), jnp.float32),
            pltpu.VMEM((11, ext, nz), jnp.float32),
            pltpu.VMEM(tall(lay.near).shape, jnp.float32),
            pltpu.VMEM((2, ny, nx, nz), jnp.float32),
            pltpu.SemaphoreType.DMA((ny // GROUP,)),
        ],
        compiler_params=PARAMS,
        name="third",
    )(st, extra, coarse, near, *got)
    return jnp.transpose(out, (0, 2, 1, 3))


def solution(mesh):
    return jax.shard_map(
        shards,
        mesh=mesh,
        in_specs=(
            P(None, "gx", "gy", None),
            P(None, "gx", "gy", None),
            P("gx", "gy", None),
            P("gx", "gy", None),
        ),
        out_specs=P(None, "gx", "gy", None),
        check_vma=False,
    )
```

```python
import functools

import jax
import jax.numpy as jnp
from jax import lax
from jax.experimental import pallas as pl
from jax.experimental.pallas import tpu as pltpu
from jax.sharding import PartitionSpec as P

SOLID_CAP, GAS_CAP, FLOW, CONDUCT, RELAX, LUMP = 0.5, 0.02, 40.0, 0.05, 0.8, 0.25
GAS_SELF = GAS_CAP + 4.5 * CONDUCT

PAD = 8
WX = 5
CROP = 4
(SA, GA, SB, GB, K, C, RS, RG, FX, FZ, H, FY, ASS, ASG, AGG) = range(15)
PLANES = 15
(M_S, M_G, M_K, M_C, M_FY, M_1S, M_1G, M_2S, M_2G) = range(9)
MESSAGE, EARLY, THIRD = 9, 7, 3

GROUP = 6

VMEM = pl.BlockSpec(memory_space=pltpu.VMEM)
HBM = pl.BlockSpec(memory_space=pltpu.HBM)
PARAMS = pltpu.CompilerParams(vmem_limit_bytes=40 * 1024 * 1024)


def up_x(v):
    return pltpu.roll(v, v.shape[0] - 1, 0)


def down_x(v):
    return pltpu.roll(v, 1, 0)


def up_z(v):
    return pltpu.roll(v, v.shape[1] - 1, 1)


def down_z(v):
    return pltpu.roll(v, 1, 1)


def lanes(shape):
    return lax.broadcasted_iota(jnp.int32, shape, 1)


def x_mask(shape, nx):
    row = lax.broadcasted_iota(jnp.int32, shape, 0)
    place, count = lax.axis_index("gx"), lax.axis_size("gx")
    low = jnp.where(place == 0, PAD, PAD - WX)
    high = jnp.where(place == count - 1, PAD + nx, PAD + nx + WX)
    return jnp.where((row >= low) & (row < high), 1.0, 0.0).astype(jnp.float32)


STRIP = ((SA, WX - 1), (GA, WX - 1), (K, WX), (C, WX - 1), (RS, WX - 1), (RG, WX - 1))
STRIP_ROWS = sum(width for plane, width in STRIP)


def conductivity_of(s, exchange):
    return 1.0 + 4.0 * exchange * s * s * s


def strip_rows(low):
    if low:
        return WX - 1, WX - 2, slice(0, WX - 1), slice(0, WX)
    return 8 - WX, 9 - WX, slice(9 - WX, 8), slice(8 - WX, 8)


def strip_values(s, g, k, c, low):
    _, _, four, five = strip_rows(low)
    return [s[four], g[four], k[five], c[four]]


def strip_sides(s, g, k, rs, rg, low):
    out, inn, four, _ = strip_rows(low)
    row = lax.broadcasted_iota(jnp.int32, s.shape, 0)
    rs = rs + jnp.where(row == inn, 0.5 * (k[inn : inn + 1] + k[out : out + 1]) * s[out : out + 1], 0.0)
    rg = rg + jnp.where(row == inn, CONDUCT * g[out : out + 1], 0.0)
    return [rs[four], rg[four]]


def pack_kernel(temps, right, exchange, coupling, one, two, early, st, sems):
    even = lax.axis_index("gx") % 2 == 0
    odd = lax.axis_index("gy") % 2 == 1
    ny, nx, nz = exchange.shape
    copies = []
    for k, (plane, ref) in enumerate(
        ((SA, temps.at[0]), (K, exchange), (GA, temps.at[1]), (C, coupling), (RS, right.at[0]), (RG, right.at[1]))
    ):
        to = st.at[plane, pl.ds(1, ny), pl.ds(PAD, nx)]
        copies.append(pltpu.make_async_copy(ref, to, sems.at[k]))
    for copy in copies:
        copy.start()
    def put(i, at, sides):
        at += (i - 1) * STRIP_ROWS
        for low, high in zip(*sides):
            one[at : at + low.shape[0]] = jnp.where(even, high, low)
            two[at : at + low.shape[0]] = jnp.where(even, low, high)
            at += low.shape[0]

    for copy in copies[:4]:
        copy.wait()
    for i in range(1, ny + 1):
        sides = []
        for start in (PAD, PAD + nx - 8):
            s, g, e, c = (st[plane, i, start : start + 8] for plane in (SA, GA, K, C))
            sides.append(strip_values(s, g, conductivity_of(s, e), c, start == PAD))
        put(i, 0, sides)
    for copy in copies[4:]:
        copy.wait()
    for i in range(1, ny + 1):
        sides = []
        for start in (PAD, PAD + nx - 8):
            s, g, e, rs, rg = (st[plane, i, start : start + 8] for plane in (SA, GA, K, RS, RG))
            sides.append(strip_sides(s, g, conductivity_of(s, e), rs, rg, start == PAD))
        put(i, STRIP_ROWS - 2 * (WX - 1), sides)
    own = slice(PAD, PAD + nx)
    for is_odd, e, d in ((True, ny, ny - 1), (False, 1, 2)):

        @pl.when(odd == is_odd)
        def _():
            s, s_d, g, g_d = st[SA, e, own], st[SA, d, own], st[GA, e, own], st[GA, d, own]
            c, k, k_d = st[C, e, own], conductivity_of(s, st[K, e, own]), conductivity_of(s_d, st[K, d, own])
            fx, fz, h, _ = faces(k)
            fy = 0.5 * (k + k_d)
            part_s, part_g = inner(s, g, c, h, fx, fz, edge_weights((nx, nz)))
            m_1s, m_1g = first_partial(st[RS, e, own] + part_s, st[RG, e, own] + part_g, s, s_d, g, g_d, fy, is_odd)
            for plane, value in enumerate((s, g, k, c, fy, m_1s, m_1g)):
                early[plane] = value


def conduct_kernel(st_in, st):
    del st_in
    planes, rows, ext, nz = st.shape
    own = slice(PAD, ext - PAD)
    zeros = jnp.zeros((PAD, nz), jnp.float32)
    for i in range(1, rows - 1):
        st[K, i, own] = conductivity_of(st[SA, i, own], st[K, i, own])
        for plane, width in STRIP:
            st[plane, i, :PAD] = zeros
            st[plane, i, ext - PAD :] = zeros


def place_halo(st, one, two, y, nx):
    even = lax.axis_index("gx") % 2 == 0
    at, i = y * STRIP_ROWS, y + 1
    for plane, width in STRIP:
        a, b = one[at : at + width], two[at : at + width]
        st[plane, i, PAD - width : PAD] = jnp.where(even, b, a)
        st[plane, i, PAD + nx : PAD + nx + width] = jnp.where(even, a, b)
        at += width


def inner(s, g, c, h, fx, fz, edge):
    t = c * (s - g)
    flux_x = fx * (up_x(s) - s)
    flux_z = fz * (up_z(s) - s)
    part_s = (flux_x - down_x(flux_x)) + (flux_z - down_z(flux_z)) - h * s - t
    part_g = (
        t
        - GAS_SELF * g
        + CONDUCT * (up_x(g) + down_x(g))
        + edge[0] * up_z(g)
        + edge[1] * down_z(g)
    )
    return part_s, part_g


def edge_weights(shape):
    lane = lanes(shape)
    weight = jnp.float32(0.25 * CONDUCT)
    return jnp.where(lane == shape[1] - 1, 0.0, weight), jnp.where(lane == 0, 0.0, weight)


def row_inner(st, i, s_at, edge):
    return inner(st[s_at, i], st[s_at + 1, i], st[C, i], st[H, i], st[FX, i], st[FZ, i], edge)


def row_residual(st, i, s_at, edge):
    part_s, part_g = row_inner(st, i, s_at, edge)
    s, g, before = st[s_at, i], st[s_at + 1, i], st[s_at + 1, i - 1]
    part_s += st[FY, i] * (st[s_at, i + 1] - s) + st[FY, i - 1] * (st[s_at, i - 1] - s)
    part_g += CONDUCT * (st[s_at + 1, i + 1] + before) - FLOW * (g - before)
    return st[RS, i] + part_s, st[RG, i] + part_g


def relaxed(st, i, s_at, res_s, res_g):
    s = st[s_at, i] + st[ASS, i] * res_s + st[ASG, i] * res_g
    g = st[s_at + 1, i] + st[ASG, i] * res_s + st[AGG, i] * res_g
    return s, g


def faces(k):
    lane = lanes(k.shape)
    end = k.shape[1] - 1
    fx = 0.5 * (k + up_x(k))
    fz = jnp.where(lane == end, 0.0, 0.125 * (k + up_z(k)))
    h = SOLID_CAP + jnp.where((lane == 0) | (lane == end), 0.125 * k, 0.0)
    return fx, fz, h, h + (fx + down_x(fx)) + (fz + down_z(fz))


def inverse(diag, c, mask):
    gas_diag = (GAS_SELF + FLOW) + c
    inv = (RELAX * mask) / (diag * gas_diag - c * c)
    return inv * gas_diag, inv * c, inv * diag


def last_relaxed(st, i, s_at, edge, own):
    full_s, full_g = st[s_at, i], st[s_at + 1, i]
    s, g = full_s[own], full_g[own]
    flux_x = st[FX, i] * (up_x(full_s) - full_s)
    flux_z = st[FZ, i, own] * (up_z(s) - s)
    c, before = st[C, i, own], st[s_at + 1, i - 1, own]
    t = c * (s - g)
    res_s = st[RS, i, own] + (flux_x[own] - down_x(flux_x)[own]) + (flux_z - down_z(flux_z)) - st[H, i, own] * s - t
    res_s += st[FY, i, own] * (st[s_at, i + 1, own] - s) + st[FY, i - 1, own] * (st[s_at, i - 1, own] - s)
    res_g = st[RG, i, own] + t - GAS_SELF * g + edge[0][own] * up_z(g) + edge[1][own] * down_z(g)
    res_g += CONDUCT * (up_x(full_g)[own] + down_x(full_g)[own] + st[s_at + 1, i + 1, own] + before) - FLOW * (g - before)
    ss, sg, gg = st[ASS, i, own], st[ASG, i, own], st[AGG, i, own]
    return s + ss * res_s + sg * res_g, g + sg * res_s + gg * res_g


def grouped(rows, work):
    for start in range(0, len(rows), GROUP):
        stores = []
        for i in rows[start : start + GROUP]:
            stores += work(i)
        for ref, at, value in stores:
            ref[at] = value


def row_coefficients(st, i, mask):
    fx, fz, h, diag = faces(st[K, i])
    fy = 0.5 * (st[K, i] + st[K, i + 1])
    before = 0.5 * (st[K, i] + st[K, i - 1])
    ss, sg, gg = inverse(diag + st[C, i] + fy + before, st[C, i], mask)
    values = ((FX, fx), (FZ, fz), (H, h), (FY, fy), (ASS, ss), (ASG, sg), (AGG, gg))
    return [(st, (plane, i), v) for plane, v in values]


def row_sweep(st, i, source, target, edge):
    s, g = relaxed(st, i, source, *row_residual(st, i, source, edge))
    return [(st, (target, i), s), (st, (target + 1, i), g)]


def first_partial(res_s, res_g, s, s_d, g, g_d, fy, onward):
    return res_s + fy * (s_d - s), res_g + CONDUCT * g_d - FLOW * (g - g_d if onward else g)


def send_planes(st, onward, edge):
    ny = st.shape[1] - 2
    e, d, near = (ny, ny - 1, ny - 1) if onward else (1, 2, 1)
    fy, s, g, g_d = st[FY, near], st[SA, e], st[GA, e], st[GA, d]
    part_s, part_g = row_inner(st, e, SA, edge)
    m_1s, m_1g = first_partial(st[RS, e] + part_s, st[RG, e] + part_g, s, st[SA, d], g, g_d, fy, onward)
    m_2s = st[RS, e] + fy * st[SB, d]
    m_2g = st[RG, e] + (CONDUCT + FLOW if onward else CONDUCT) * st[GB, d]
    return [s, g, st[K, e], st[C, e], fy, m_1s, m_1g, m_2s, m_2g]


def across_parts(ext):
    parts, at = [], 0
    for k in range(EARLY, MESSAGE):
        parts.append((k, CROP, ext - CROP, at))
        at += ext - 2 * CROP
    for k in range(EARLY):
        more = 1 if k in (M_1S, M_1G) else 0
        for low, high in ((CROP, PAD + more), (ext - PAD - more, ext - CROP)):
            parts.append((k, low, high, at))
            at += high - low
    return parts, (at + 7) // 8 * 8


def write_across(ref, k, value):
    for plane, low, high, at in across_parts(value.shape[0])[0]:
        if plane == k:
            ref[at : at + high - low] = value[low:high]


def read_across(early, across, outer, k):
    ext = outer.shape[1]
    if k < EARLY:
        outer[k, PAD : ext - PAD] = early[k]
    for plane, low, high, at in across_parts(ext)[0]:
        if plane == k:
            outer[k, low:high] = across[at : at + high - low]


def write_beside(refs, k, value):
    refs[k // THIRD][k % THIRD] = value[CROP : value.shape[0] - CROP]


def read_beside(refs, outer, k):
    outer[k, CROP : outer.shape[1] - CROP] = refs[k // THIRD][k % THIRD]


def first_end(st, one, two, after, write):
    planes, rows, ext, nz = st.shape
    ny, nx = rows - 2, ext - 2 * PAD
    mask = x_mask((ext, nz), nx)
    edge = edge_weights((ext, nz))
    e, d, f = (ny, ny - 1, ny - 2) if after else (1, 2, 3)
    for i in (e, d, f):
        place_halo(st, one, two, i - 1, nx)
    fx, fz, h, diag = faces(st[K, e])
    st[FX, e], st[FZ, e], st[H, e] = fx, fz, h
    st[FY, min(e, d)] = 0.5 * (st[K, e] + st[K, d])
    st[FY, min(d, f)] = 0.5 * (st[K, d] + st[K, f])
    grouped([d], lambda i: row_coefficients(st, i, mask))
    grouped([d], lambda i: row_sweep(st, i, SA, SB, edge))
    for k, value in enumerate(send_planes(st, after, edge)):
        write(k, value)


def either_first(st, one, two, after, write):
    for is_after in (True, False):

        @pl.when(after == is_after)
        def _():
            first_end(st, one, two, is_after, write)


def first_kernel(st_in, one, two, st, across):
    del st_in
    either_first(st, one, two, lax.axis_index("gy") % 2 == 1, functools.partial(write_across, across))


def other_kernel(st_in, one, two, st, *beside):
    del st_in
    either_first(st, one, two, lax.axis_index("gy") % 2 == 0, functools.partial(write_beside, beside))


def outer_residual(st, i, s_at, rs, rg, fy_out, edge, after):
    part_s, part_g = row_inner(st, i, s_at, edge)
    s, g = st[s_at, i], st[s_at + 1, i]
    if after:
        part_s += st[FY, i - 1] * (st[s_at, i - 1] - s)
        part_g += (CONDUCT + FLOW) * st[s_at + 1, i - 1]
    else:
        part_s += st[FY, i] * (st[s_at, i + 1] - s)
        part_g += CONDUCT * st[s_at + 1, i + 1]
    return rs + part_s - fy_out * s, rg + part_g - FLOW * g


def pair_x(v):
    row = lax.broadcasted_iota(jnp.int32, v.shape, 0)
    return v + jnp.where(row % 2 == 0, up_x(v), down_x(v))


def coarse_coefficients(c_sum, k_sum):
    solid = 4.0 * SOLID_CAP + c_sum + LUMP * k_sum
    ratio = c_sum / solid
    denominator = (4.0 * GAS_CAP + 2.0 * FLOW) + c_sum - c_sum * ratio
    return solid, ratio, denominator


def coarse_row(st, coarse, j, mask, edge):
    i = 2 * j + 1
    res_s, res_g = row_residual(st, i, SA, edge)
    more_s, more_g = row_residual(st, i + 1, SA, edge)
    res_s, res_g = pair_x((res_s + more_s) * mask), pair_x((res_g + more_g) * mask)
    c_sum = pair_x(st[C, i] + st[C, i + 1])
    solid, ratio, denominator = coarse_coefficients(c_sum, pair_x(st[K, i] + st[K, i + 1]))
    lead = res_s / solid
    values = (lead, ratio, (2.0 * FLOW) / denominator, (res_g + c_sum * lead) / denominator)
    return [(coarse, (k, j), v) for k, v in enumerate(values)]


def inner_kernel(st_in, one, two, early, st, coarse):
    del st_in, early
    planes, rows, ext, nz = st.shape
    ny, nx = rows - 2, ext - 2 * PAD
    shape = (ext, nz)
    mask = x_mask(shape, nx)
    edge = edge_weights(shape)
    for y in range(3, ny - 3):
        place_halo(st, one, two, y, nx)
    grouped(list(range(3, ny - 1)), lambda i: row_coefficients(st, i, mask))
    grouped(list(range(3, ny - 1)), lambda i: row_sweep(st, i, SA, SB, edge))
    grouped(list(range(3, ny - 1)), lambda i: row_sweep(st, i, SB, SA, edge))
    for j in range(2, ny // 2 - 2):
        for ref, at, value in coarse_row(st, coarse, j, mask, edge):
            ref[at] = value


def end_work(st, coarse, extra, read, outer, is_after):
    planes, rows, ext, nz = st.shape
    ny, nx = rows - 2, ext - 2 * PAD
    me, count = lax.axis_index("gy"), lax.axis_size("gy")
    mask = x_mask((ext, nz), nx)
    inside = jnp.where(me == (count - 1 if is_after else 0), 0.0, mask)
    edge = edge_weights((ext, nz))
    zeros = jnp.zeros((PAD, nz), jnp.float32)
    for k in range(MESSAGE):
        outer[k, :PAD] = zeros
        outer[k, ext - PAD :] = zeros
        read(outer, k)

    o, e, near = (ny + 1, ny, ny) if is_after else (0, 1, 0)
    to_o = CONDUCT + FLOW if is_after else CONDUCT
    s_o, g_o, k_o, c_o, fy_out = (outer[plane] for plane in (M_S, M_G, M_K, M_C, M_FY))
    fy = 0.5 * (k_o + st[K, e])
    fx, fz, h, diag = faces(k_o)
    inv_o = inverse(diag + c_o + fy_out + fy, c_o, inside)
    fx_e, fz_e = st[FX, e], st[FZ, e]
    diag = st[H, e] + (fx_e + down_x(fx_e)) + (fz_e + down_z(fz_e)) + st[C, e] + fy
    inv_e = inverse(diag + st[FY, near - 1 if is_after else near + 1], st[C, e], mask)
    for plane, value in ((SA, s_o), (GA, g_o), (K, k_o), (C, c_o), (FX, fx), (FZ, fz), (H, h)):
        st[plane, o] = value
    st[FY, near] = fy
    for k in range(3):
        st[ASS + k, o], st[ASS + k, e] = inv_o[k], inv_e[k]

    res = outer[M_1S] + fy * (st[SA, e] - s_o), outer[M_1G] + to_o * st[GA, e]
    new_o = relaxed(st, o, SA, *res)
    stores = row_sweep(st, e, SA, SB, edge)
    st[SB, o], st[GB, o] = new_o
    for ref, at, value in stores:
        ref[at] = value
    res = outer_residual(st, o, SB, outer[M_2S], outer[M_2G], fy_out, edge, is_after)
    new_o = relaxed(st, o, SB, *res)
    ends = [e - 1, e] if is_after else [e, e + 1]
    grouped(ends, lambda i: row_sweep(st, i, SB, SA, edge))
    st[SA, o], st[GA, o] = new_o
    for k, plane in enumerate((M_2S, M_2G, M_FY)):
        extra[(3 if is_after else 0) + k] = outer[plane]
    blocks = ny // 2
    stores = []
    for j in (blocks - 2, blocks - 1) if is_after else (0, 1):
        stores += coarse_row(st, coarse, j, mask, edge)
    for ref, at, value in stores:
        ref[at] = value


def either_end(after, st, coarse, extra, read, outer):
    for is_after in (True, False):

        @pl.when(after == is_after)
        def _():
            end_work(st, coarse, extra, read, outer, is_after)


def near_kernel(st_in, coarse_in, *refs):
    beside, (st, coarse, extra, outer) = refs[:-4], refs[-4:]
    del st_in, coarse_in
    either_end(lax.axis_index("gy") % 2 == 0, st, coarse, extra, functools.partial(read_beside, beside), outer)


def second_kernel(st_in, coarse_in, extra_in, early, across, *refs):
    st, coarse, extra, total, last_info, first_info, message, outer, squeeze = refs
    del st_in, coarse_in, extra_in
    planes, rows, ext, nz = st.shape
    ny, nx = rows - 2, ext - 2 * PAD
    me = lax.axis_index("gy")
    either_end(me % 2 == 1, st, coarse, extra, functools.partial(read_across, early, across), outer)

    blocks = ny // 2
    for k in range(4):
        squeeze[k] = coarse[k, 0]
    slopes, offsets = coarse[2, 0], coarse[3, 0]
    for j in range(1, blocks):
        slope = coarse[2, j]
        slopes, offsets = slope * slopes, slope * offsets + coarse[3, j]
        coarse[2, j], coarse[3, j] = slopes, offsets
    squeeze[4], squeeze[5], squeeze[6], squeeze[7] = slopes, offsets, coarse[0, blocks - 1], coarse[1, blocks - 1]

    span = nx // 2 + 2
    lead, ratio, slope, offset, slopes, offsets, lead_last, ratio_last = (
        squeeze[k, pl.ds(PAD - 2, span, 2), :] for k in range(8)
    )
    part = slice(PAD - 1, PAD + nx + 1)

    def increments(d, face, gas):
        return [(st[FY, face] * (st[SA, d] - st[SB, d]))[part], (gas * (st[GA, d] - st[GB, d]))[part]]

    onward = [lead_last, ratio_last] + increments(ny - 1, ny - 1, CONDUCT + FLOW)
    back = [lead, offset] + increments(2, 1, CONDUCT) + [slope, ratio]
    write_rows(total, [slopes, offsets])
    write_rows(last_info, onward)
    write_rows(first_info, back)
    for go, info in ((True, onward), (False, back)):

        @pl.when((me % 2 == 0) == go)
        def _():
            write_rows(message, [slopes, offsets] + info)


def write_rows(ref, values):
    at = 0
    for value in values:
        ref[at : at + value.shape[0]] = value
        at += value.shape[0]


class Rows:
    def __init__(self, nx):
        self.span = nx // 2 + 2
        self.map = 2 * self.span
        self.info = self.map + 2 * (nx + 2)
        self.rest = self.map
        self.final = self.map + self.info
        self.full = self.final + self.rest
        self.low = self.map
        self.high = self.low + self.info
        self.near = self.high + self.info + self.rest


def source(at, k, radix):
    if radix & (radix - 1) == 0:
        return at ^ k
    return (at + radix - k) % radix


def matchings(count, radix, stride):
    if (count, radix, stride) == (8, 4, 2):
        swaps = ((1, 2), (3, 4), (5, 6), (0, 7)), ((0, 3), (1, 5), (2, 6), (4, 7)), ((0, 4), (1, 6), (2, 5), (3, 7))
        out = []
        for pairs in swaps:
            senders = [0] * count
            for a, b in pairs:
                senders[a], senders[b] = b, a
            out.append((senders, len(out) == 0))
        return out
    out = []
    for k in range(1, radix):
        senders = []
        for me in range(count):
            at, low = me // stride % radix, me % stride
            senders.append(me - low + (source(at, k, radix) - at) * stride + (stride - 1 - low))
        out.append((senders, any(abs(source(at, k, radix) - at) == 1 for at in range(radix))))
    return sorted(out, key=lambda item: not item[1])


def look_up(table):
    me, value = lax.axis_index("gy"), jnp.int32(table[0])
    for k in range(1, len(table)):
        value = jnp.where(me == k, table[k], value)
    return value


def stages(count):
    if count % 2:
        return [1, count]
    out, rest = [2], count // 2
    while rest > 1:
        radix = next((r for r in (8, 4, 2) if rest % r == 0), rest)
        out.append(radix)
        rest //= radix
    return out if len(out) > 1 else out + [1]


def exchange_stage(messages, swaps):
    return [
        lax.ppermute(message, "gy", [(sender, me) for me, sender in enumerate(senders)])
        for (senders, near), message in zip(swaps, messages)
    ]


class Group:
    def __init__(self, radix, stride, others, nx):
        self.radix, self.others, self.nx = radix, others, nx
        me = lax.axis_index("gy")
        self.swaps = [
            (look_up([sender // stride % radix for sender in senders]), near)
            for senders, near in matchings(lax.axis_size("gy"), radix, stride)
        ]
        self.at = lax.rem(lax.div(me, stride), radix)
        low = lax.rem(me, stride)
        self.lowest, self.highest = low == 0, low == stride - 1

    def map_of(self, place, own):
        rows = Rows(self.nx)
        out = own
        for (sender, near), ref in zip(self.swaps, self.others):
            here = sender == place
            got = [ref[i * rows.span : (i + 1) * rows.span] for i in range(2)]
            out = got if out is None else [jnp.where(here, new, old) for new, old in zip(got, out)]
        return out

    def ahead(self, slope, offset):
        a, b = jnp.ones_like(slope), jnp.zeros_like(slope)
        for place in range(self.radix - 1):
            new_a, new_b = self.map_of(place, None)
            below = place < self.at
            a, b = jnp.where(below, new_a * a, a), jnp.where(below, new_a * b + new_b, b)
        return slope * a, slope * b + offset

    def total(self, own):
        a, b = self.map_of(0, own)
        for place in range(1, self.radix):
            new_a, new_b = self.map_of(place, own)
            a, b = new_a * a, new_a * b + new_b
        return a, b

    def collect(self, near, final):
        rows = Rows(self.nx)
        for (place, adjacent), ref in zip(self.swaps, self.others):
            if not adjacent:
                continue

            @pl.when(self.lowest & (place == self.at - 1))
            def _():
                near[rows.low : rows.low + rows.info] = ref[rows.map : rows.final]

            @pl.when(self.highest & (place == self.at + 1))
            def _():
                near[rows.high : rows.high + rows.info] = ref[rows.map : rows.final]
                rest = slice(0, rows.map) if final else slice(rows.final, rows.full)
                near[rows.high + rows.info : rows.near] = ref[rest]


def start_near(near, nx, nz):
    rows = Rows(nx)
    near[: rows.span] = jnp.ones((rows.span, nz), jnp.float32)
    near[rows.span :] = jnp.zeros((near.shape[0] - rows.span, nz), jnp.float32)


def join_kernel(radix, stride, final, nx, is_first, *refs):
    rows = Rows(nx)
    total, last_info, first_info, near_in = refs[:4]
    others, near, outs = refs[4 : 3 + radix], refs[3 + radix], refs[4 + radix :]
    nz = near.shape[1]
    if is_first:
        start_near(near, nx, nz)
    else:
        near[...] = near_in[...]
    group = Group(radix, stride, others, nx)
    own = [total[i * rows.span : (i + 1) * rows.span] for i in range(2)]
    ahead = group.ahead(near[: rows.span], near[rows.span : rows.map])
    write_rows(near, ahead)
    group.collect(near, False)
    whole = group.total(own)
    if final == 0:
        write_rows(outs[0], whole)
        return
    me, count = lax.axis_index("gy"), lax.axis_size("gy")
    for (senders, adjacent), out in zip(matchings(count, final, stride * radix), outs):
        up = look_up(senders) > me
        if not adjacent:
            write_rows(out, whole)
            continue

        @pl.when(up)
        def _():
            write_rows(out, whole)
            out[rows.map : rows.final] = last_info[: rows.info]

        @pl.when(jnp.logical_not(up))
        def _():
            out[: rows.map] = first_info[rows.info : rows.info + rows.rest]
            out[rows.map : rows.final] = first_info[: rows.info]


def full_message(nx, total, last_info, first_info, senders):
    rows = Rows(nx)
    onward = jnp.concatenate([total[: rows.map], last_info[: rows.info], first_info[rows.info : rows.info + rows.rest]])
    back = jnp.concatenate([total[: rows.map], first_info[: rows.info + rows.rest]])
    message = jnp.where(look_up(senders) > lax.axis_index("gy"), onward, back)
    return jnp.pad(message, ((0, -rows.full % 8), (0, 0)))


def third_kernel(radix, stride, *refs):
    st, extra, coarse, near_in = refs[:4]
    others, (out, sc, wide, near, done, sems) = refs[4 : 3 + radix], refs[3 + radix :]
    planes, rows, ext, nz = st.shape
    ny, nx = rows - 2, ext - 2 * PAD
    edge = edge_weights((ext, nz))
    blocks = ny // 2

    lay = Rows(nx)
    span = lay.span
    near[...] = near_in[...]
    group = Group(radix, stride, others, nx)
    if radix > 1:
        group.collect(near, True)
    gas_in = group.ahead(near[:span], near[span : lay.map])[1]
    at_high = lay.high + lay.info
    starts = [lay.low, lay.low + span, lay.high, lay.high + span, at_high, at_high + span]
    for k, v in enumerate([gas_in] + [near[start : start + span] for start in starts]):
        wide[k, : PAD - 2] = jnp.zeros((PAD - 2, nz), jnp.float32)
        wide[k, ext - PAD + 2 :] = jnp.zeros((PAD - 2, nz), jnp.float32)
        wide[k, pl.ds(PAD - 2, span, 2), :] = v
        wide[k, pl.ds(PAD - 1, span, 2), :] = v
    for k, start in enumerate((lay.low, lay.low + nx + 2, lay.high, lay.high + nx + 2)):
        start += lay.map
        wide[7 + k, :PAD] = jnp.zeros((PAD, nz), jnp.float32)
        wide[7 + k, ext - PAD :] = jnp.zeros((PAD, nz), jnp.float32)
        wide[7 + k, PAD - 1 : PAD + nx + 1] = near[start : start + nx + 2]

    gas_in = wide[0]
    last = ny + 1
    solid_low = wide[1] + wide[2] * gas_in
    sc[0, 0] = st[SA, 0] + solid_low
    sc[1, 0] = st[GA, 0] + gas_in

    def correct(j, carry):
        gas = coarse[2, j] * gas_in + coarse[3, j]
        solid = coarse[0, j] + coarse[1, j] * gas
        for i in (2 * j + 1, 2 * j + 2):
            sc[0, i] = st[SA, i] + solid
            sc[1, i] = st[GA, i] + gas
        return carry

    lax.fori_loop(0, blocks, correct, 0)
    gas = coarse[2, blocks - 1] * gas_in + coarse[3, blocks - 1]
    gas_high = wide[5] * gas + wide[4]
    solid_high = wide[3] + wide[6] * gas_high
    sc[0, last] = st[SA, last] + solid_high
    sc[1, last] = st[GA, last] + gas_high

    view = Fields(st, sc)
    for i, is_after, solid, gas in ((0, False, solid_low, gas_in), (last, True, solid_high, gas_high)):
        side = 3 if is_after else 0
        fy = extra[side + 2]
        to = 9 if is_after else 7
        rs = extra[side] + wide[to] + fy * solid
        rg = extra[side + 1] + wide[to + 1] + (CONDUCT if is_after else CONDUCT + FLOW) * gas
        res = outer_residual(view, i, SA, rs, rg, fy, edge, is_after)
        sc[2, i], sc[3, i] = relaxed(view, i, SA, *res)

    def sweep(k, carry):
        stores = []
        for r in range(GROUP):
            i = GROUP * k + 1 + r
            new_s, new_g = relaxed(view, i, SA, *row_residual(view, i, SA, edge))
            stores += [((2, i), new_s), ((3, i), new_g)]
        for at, value in stores:
            sc[at] = value
        return carry

    lax.fori_loop(0, ny // GROUP, sweep, 0)

    def leaving(k):
        part = pl.ds(GROUP * k, GROUP)
        return pltpu.make_async_copy(done.at[:, part], out.at[:, part], sems.at[k])

    def final(k, carry):
        stores = []
        for r in range(GROUP):
            i = GROUP * k + 1 + r
            new_s, new_g = last_relaxed(view, i, SB, edge, slice(PAD, PAD + nx))
            stores += [((0, i - 1), new_s), ((1, i - 1), new_g)]
        for at, value in stores:
            done[at] = value
        leaving(k).start()
        return carry

    lax.fori_loop(0, ny // GROUP, final, 0)
    for k in range(ny // GROUP):
        leaving(k).wait()


class Fields:
    def __init__(self, st, sc):
        self.st, self.sc = st, sc

    def __getitem__(self, at):
        return (self.sc if at[0] <= GB else self.st)[at]


def cost(rows, cells):
    return pl.CostEstimate(flops=50 * rows * cells, bytes_accessed=16 * 4 * rows * cells, transcendentals=0)


def swap(x, axis, first):
    pairs = []
    for i in range(first, lax.axis_size(axis) - 1, 2):
        pairs += [(i, i + 1), (i + 1, i)]
    return lax.ppermute(x, axis, pairs)


def shards(temps, right_side, exchange, coupling):
    temps, right_side = (jnp.transpose(a, (0, 2, 1, 3)) for a in (temps, right_side))
    exchange, coupling = (jnp.transpose(a, (1, 0, 2)) for a in (exchange, coupling))
    temps, right_side, exchange, coupling = (
        pltpu.with_memory_space_constraint(a, pltpu.HBM) for a in (temps, right_side, exchange, coupling)
    )
    ny, nx, nz = exchange.shape
    ext = nx + 2 * PAD
    f32 = functools.partial(jax.ShapeDtypeStruct, dtype=jnp.float32)

    strip = f32(((ny * STRIP_ROWS + 7) // 8 * 8, nz))
    state = f32((PLANES, ny + 2, ext, nz))
    one, two, early, st = pl.pallas_call(
        pack_kernel,
        out_shape=(strip, strip, f32((EARLY, nx, nz)), state),
        in_specs=[HBM] * 4,
        out_specs=(VMEM,) * 4,
        scratch_shapes=[pltpu.SemaphoreType.DMA((6,))],
        compiler_params=PARAMS,
        name="pack_x",
    )(temps, right_side, exchange, coupling)
    one, two = swap(one, "gx", 0), swap(two, "gx", 1)
    early = swap(early, "gy", 1)

    def letter(planes):
        return f32((planes, ext - 2 * CROP, nz))

    st = pl.pallas_call(
        conduct_kernel,
        out_shape=state,
        in_specs=[VMEM],
        out_specs=VMEM,
        input_output_aliases={0: 0},
        compiler_params=PARAMS,
        cost_estimate=cost(2 * ny, ext * nz),
        name="conduct",
    )(st)
    st, across = pl.pallas_call(
        first_kernel,
        out_shape=(state, f32((across_parts(ext)[1], nz))),
        in_specs=[VMEM] * 3,
        out_specs=(VMEM,) * 2,
        input_output_aliases={0: 0},
        compiler_params=PARAMS,
        name="first",
    )(st, one, two)
    st, *beside = pl.pallas_call(
        other_kernel,
        out_shape=(state,) + (letter(THIRD),) * (MESSAGE // THIRD),
        in_specs=[VMEM] * 3,
        out_specs=(VMEM,) * (1 + MESSAGE // THIRD),
        input_output_aliases={0: 0},
        compiler_params=PARAMS,
        name="other",
    )(st, one, two)
    across = swap(across, "gy", 1)

    rows = f32((4, ny // 2, ext, nz))
    st, coarse = pl.pallas_call(
        inner_kernel,
        out_shape=(state, rows),
        in_specs=[VMEM] * 4,
        out_specs=(VMEM,) * 2,
        input_output_aliases={0: 0},
        compiler_params=PARAMS,
        cost_estimate=cost(4 * ny, ext * nz),
        name="inner",
    )(st, one, two, early)

    beside = [swap(part, "gy", 0) for part in beside]

    lay = Rows(nx)

    def tall(height):
        return f32(((height + 7) // 8 * 8, nz))

    letter_room = pltpu.VMEM((MESSAGE, ext, nz), jnp.float32)
    more = f32((6, ext, nz))
    st, coarse, extra = pl.pallas_call(
        near_kernel,
        out_shape=(state, rows, more),
        in_specs=[VMEM] * (2 + len(beside)),
        out_specs=(VMEM,) * 3,
        scratch_shapes=[letter_room],
        input_output_aliases={0: 0, 1: 1},
        compiler_params=PARAMS,
        name="near",
    )(st, coarse, *beside)
    st, coarse, extra, total, last_info, first_info, message = pl.pallas_call(
        second_kernel,
        out_shape=(state, rows, more, tall(lay.map), tall(lay.info), tall(lay.info + lay.rest), tall(lay.full)),
        in_specs=[VMEM] * 5,
        out_specs=(VMEM,) * 7,
        scratch_shapes=[letter_room, pltpu.VMEM((8, ext, nz), jnp.float32)],
        input_output_aliases={0: 0, 1: 1, 2: 2},
        compiler_params=PARAMS,
        name="second",
    )(st, coarse, extra, early, across)

    near, messages = total, [message]
    count = lax.axis_size("gy")
    radices, stride = stages(count), 1
    for place, radix in enumerate(radices[:-1]):
        swaps = matchings(count, radix, stride)
        if place:
            messages = [full_message(nx, total, last_info, first_info, senders) for senders, _ in swaps]
        others = exchange_stage(messages, swaps)
        final = radices[-1] if place == len(radices) - 2 else 0
        following = matchings(count, final, stride * radix) if final else []
        outs = [tall(lay.final if adjacent else lay.map) for _, adjacent in following] if final else [tall(lay.map)]
        near, *messages = pl.pallas_call(
            functools.partial(join_kernel, radix, stride, final, nx, place == 0),
            out_shape=(tall(lay.near), *outs),
            in_specs=[VMEM] * (3 + radix),
            out_specs=(VMEM,) * (1 + len(outs)),
            compiler_params=PARAMS,
            name="join",
        )(total, last_info, first_info, near, *others)
        total = total if final else messages[0]
        stride *= radix
    got = exchange_stage(messages, matchings(count, radices[-1], stride))

    out = pl.pallas_call(
        functools.partial(third_kernel, radices[-1], stride),
        out_shape=f32((2, ny, nx, nz)),
        in_specs=[VMEM] * (4 + len(got)),
        out_specs=HBM,
        scratch_shapes=[
            pltpu.VMEM((4, ny + 2, ext, nz), jnp.float32),
            pltpu.VMEM((11, ext, nz), jnp.float32),
            pltpu.VMEM(tall(lay.near).shape, jnp.float32),
            pltpu.VMEM((2, ny, nx, nz), jnp.float32),
            pltpu.SemaphoreType.DMA((ny // GROUP,)),
        ],
        compiler_params=PARAMS,
        name="third",
    )(st, extra, coarse, near, *got)
    return jnp.transpose(out, (0, 2, 1, 3))


def solution(mesh):
    return jax.shard_map(
        shards,
        mesh=mesh,
        in_specs=(
            P(None, "gx", "gy", None),
            P(None, "gx", "gy", None),
            P("gx", "gy", None),
            P("gx", "gy", None),
        ),
        out_specs=P(None, "gx", "gy", None),
        check_vma=False,
    )
```

```python
import functools

import jax
import jax.numpy as jnp
from jax import lax
from jax.experimental import pallas as pl
from jax.experimental.pallas import tpu as pltpu
from jax.sharding import PartitionSpec as P

SOLID_CAP, GAS_CAP, FLOW, CONDUCT, RELAX, LUMP = 0.5, 0.02, 40.0, 0.05, 0.8, 0.25
GAS_SELF = GAS_CAP + 4.5 * CONDUCT

PAD = 8
WX = 5
CROP = 4
(SA, GA, SB, GB, K, C, RS, RG, FX, FZ, H, FY, ASS, ASG, AGG) = range(15)
PLANES = 15
(M_S, M_G, M_K, M_C, M_FY, M_1S, M_1G, M_2S, M_2G) = range(9)
MESSAGE, EARLY, THIRD = 9, 7, 3

GROUP = 6

VMEM = pl.BlockSpec(memory_space=pltpu.VMEM)
HBM = pl.BlockSpec(memory_space=pltpu.HBM)
PARAMS = pltpu.CompilerParams(vmem_limit_bytes=40 * 1024 * 1024)


def up_x(v):
    return pltpu.roll(v, v.shape[0] - 1, 0)


def down_x(v):
    return pltpu.roll(v, 1, 0)


def up_z(v):
    return pltpu.roll(v, v.shape[1] - 1, 1)


def down_z(v):
    return pltpu.roll(v, 1, 1)


def lanes(shape):
    return lax.broadcasted_iota(jnp.int32, shape, 1)


def x_mask(shape, nx):
    row = lax.broadcasted_iota(jnp.int32, shape, 0)
    place, count = lax.axis_index("gx"), lax.axis_size("gx")
    low = jnp.where(place == 0, PAD, PAD - WX)
    high = jnp.where(place == count - 1, PAD + nx, PAD + nx + WX)
    return jnp.where((row >= low) & (row < high), 1.0, 0.0).astype(jnp.float32)


PAIRS = ((SA, GA), (C, RS), (RG, K))
STRIP_ROWS = 8 * len(PAIRS)


def strip_height(ny):
    return ny * STRIP_ROWS + (ny + 7) // 8 * 8


def sublanes(nz):
    return lax.broadcasted_iota(jnp.int32, (8, nz), 0)


def conductivity_of(s, exchange):
    return 1.0 + 4.0 * exchange * s * s * s


def strip_side(s, g, k, rs, rg, c, low):
    row = sublanes(s.shape[1])
    inn, shift = (3, 7) if low else (4, 1)
    k_out, s_out, g_out = (pltpu.roll(v, shift, 0) for v in (k, s, g))
    rs = rs + jnp.where(row == inn, 0.5 * (k + k_out) * s_out, 0.0)
    rg = rg + jnp.where(row == inn, CONDUCT * g_out, 0.0)
    values = {SA: s, GA: g, K: k, RS: rs, RG: rg, C: c}
    tiles = []
    for a, b in PAIRS:
        a, b = values[a], values[b]
        a, b = (a, pltpu.roll(b, 4, 0)) if low else (pltpu.roll(a, 4, 0), b)
        tiles.append(jnp.where(row < 4, a, b))
    return tiles, (k[4:5] if low else k[3:4])


def pack_kernel(temps, right, exchange, coupling, one, two, early, st, sems):
    even = lax.axis_index("gx") % 2 == 0
    odd = lax.axis_index("gy") % 2 == 1
    ny, nx, nz = exchange.shape
    copies = []
    for k, (plane, ref) in enumerate(
        ((SA, temps.at[0]), (K, exchange), (GA, temps.at[1]), (C, coupling), (RS, right.at[0]), (RG, right.at[1]))
    ):
        to = st.at[plane, pl.ds(1, ny), pl.ds(PAD, nx)]
        copies.append(pltpu.make_async_copy(ref, to, sems.at[k]))
    for copy in copies:
        copy.start()
    for copy in copies:
        copy.wait()
    for i in range(1, ny + 1):
        sides = []
        for start in (PAD, PAD + nx - 8):
            s, g, e, rs, rg, c = (st[plane, i, start : start + 8] for plane in (SA, GA, K, RS, RG, C))
            sides.append(strip_side(s, g, conductivity_of(s, e), rs, rg, c, start == PAD))
        (low, low_k), (high, high_k) = sides
        for p in range(len(PAIRS)):
            part = slice((i - 1) * STRIP_ROWS + 8 * p, (i - 1) * STRIP_ROWS + 8 * p + 8)
            one[part] = jnp.where(even, high[p], low[p])
            two[part] = jnp.where(even, low[p], high[p])
        part = slice(ny * STRIP_ROWS + i - 1, ny * STRIP_ROWS + i)
        one[part] = jnp.where(even, high_k, low_k)
        two[part] = jnp.where(even, low_k, high_k)
    own = slice(PAD, PAD + nx)
    for is_odd, e, d in ((True, ny, ny - 1), (False, 1, 2)):

        @pl.when(odd == is_odd)
        def _():
            s, s_d, g, g_d = st[SA, e, own], st[SA, d, own], st[GA, e, own], st[GA, d, own]
            c, k, k_d = st[C, e, own], conductivity_of(s, st[K, e, own]), conductivity_of(s_d, st[K, d, own])
            fx, fz, h, _ = faces(k)
            fy = 0.5 * (k + k_d)
            part_s, part_g = inner(s, g, c, h, fx, fz, edge_weights((nx, nz)))
            m_1s, m_1g = first_partial(st[RS, e, own] + part_s, st[RG, e, own] + part_g, s, s_d, g, g_d, fy, is_odd)
            for plane, value in enumerate((s, g, k, c, fy, m_1s, m_1g)):
                early[plane] = value


def conduct_kernel(st_in, st):
    del st_in
    planes, rows, ext, nz = st.shape
    own = slice(PAD, ext - PAD)
    for i in range(1, rows - 1):
        st[K, i, own] = conductivity_of(st[SA, i, own], st[K, i, own])


def place_halo(st, one, two, y, nx):
    even = lax.axis_index("gx") % 2 == 0
    ny, row = st.shape[1] - 2, sublanes(st.shape[3])
    i = y + 1

    def received(part):
        a, b = one[part], two[part]
        return jnp.where(even, b, a), jnp.where(even, a, b)

    for p, (plane_a, plane_b) in enumerate(PAIRS):
        before, after = received(slice(y * STRIP_ROWS + 8 * p, y * STRIP_ROWS + 8 * p + 8))
        before = {plane_a: pltpu.roll(before, 4, 0), plane_b: before}
        after = {plane_a: after, plane_b: pltpu.roll(after, 4, 0)}
        for plane in (plane_a, plane_b):
            low, high = jnp.where(row >= 4, before[plane], 0.0), jnp.where(row < 4, after[plane], 0.0)
            if plane == K:
                k_low, k_high = received(slice(ny * STRIP_ROWS + y, ny * STRIP_ROWS + y + 1))
                low, high = jnp.where(row == 3, k_low, low), jnp.where(row == 4, k_high, high)
            st[plane, i, :PAD] = low
            st[plane, i, PAD + nx :] = high


def inner(s, g, c, h, fx, fz, edge):
    t = c * (s - g)
    flux_x = fx * (up_x(s) - s)
    flux_z = fz * (up_z(s) - s)
    part_s = (flux_x - down_x(flux_x)) + (flux_z - down_z(flux_z)) - h * s - t
    part_g = (
        t
        - GAS_SELF * g
        + CONDUCT * (up_x(g) + down_x(g))
        + edge[0] * up_z(g)
        + edge[1] * down_z(g)
    )
    return part_s, part_g


def edge_weights(shape):
    lane = lanes(shape)
    weight = jnp.float32(0.25 * CONDUCT)
    return jnp.where(lane == shape[1] - 1, 0.0, weight), jnp.where(lane == 0, 0.0, weight)


def row_inner(st, i, s_at, edge):
    return inner(st[s_at, i], st[s_at + 1, i], st[C, i], st[H, i], st[FX, i], st[FZ, i], edge)


def row_residual(st, i, s_at, edge):
    part_s, part_g = row_inner(st, i, s_at, edge)
    s, g, before = st[s_at, i], st[s_at + 1, i], st[s_at + 1, i - 1]
    part_s += st[FY, i] * (st[s_at, i + 1] - s) + st[FY, i - 1] * (st[s_at, i - 1] - s)
    part_g += CONDUCT * (st[s_at + 1, i + 1] + before) - FLOW * (g - before)
    return st[RS, i] + part_s, st[RG, i] + part_g


def relaxed(st, i, s_at, res_s, res_g):
    s = st[s_at, i] + st[ASS, i] * res_s + st[ASG, i] * res_g
    g = st[s_at + 1, i] + st[ASG, i] * res_s + st[AGG, i] * res_g
    return s, g


def faces(k):
    lane = lanes(k.shape)
    end = k.shape[1] - 1
    fx = 0.5 * (k + up_x(k))
    fz = jnp.where(lane == end, 0.0, 0.125 * (k + up_z(k)))
    h = SOLID_CAP + jnp.where((lane == 0) | (lane == end), 0.125 * k, 0.0)
    return fx, fz, h, h + (fx + down_x(fx)) + (fz + down_z(fz))


def inverse(diag, c, mask):
    gas_diag = (GAS_SELF + FLOW) + c
    inv = (RELAX * mask) / (diag * gas_diag - c * c)
    return inv * gas_diag, inv * c, inv * diag


def last_relaxed(st, i, s_at, edge, own):
    full_s, full_g = st[s_at, i], st[s_at + 1, i]
    s, g = full_s[own], full_g[own]
    flux_x = st[FX, i] * (up_x(full_s) - full_s)
    flux_z = st[FZ, i, own] * (up_z(s) - s)
    c, before = st[C, i, own], st[s_at + 1, i - 1, own]
    t = c * (s - g)
    res_s = st[RS, i, own] + (flux_x[own] - down_x(flux_x)[own]) + (flux_z - down_z(flux_z)) - st[H, i, own] * s - t
    res_s += st[FY, i, own] * (st[s_at, i + 1, own] - s) + st[FY, i - 1, own] * (st[s_at, i - 1, own] - s)
    res_g = st[RG, i, own] + t - GAS_SELF * g + edge[0][own] * up_z(g) + edge[1][own] * down_z(g)
    res_g += CONDUCT * (up_x(full_g)[own] + down_x(full_g)[own] + st[s_at + 1, i + 1, own] + before) - FLOW * (g - before)
    ss, sg, gg = st[ASS, i, own], st[ASG, i, own], st[AGG, i, own]
    return s + ss * res_s + sg * res_g, g + sg * res_s + gg * res_g


def grouped(rows, work):
    for start in range(0, len(rows), GROUP):
        stores = []
        for i in rows[start : start + GROUP]:
            stores += work(i)
        for ref, at, value in stores:
            ref[at] = value


def row_coefficients(st, i, mask):
    fx, fz, h, diag = faces(st[K, i])
    fy = 0.5 * (st[K, i] + st[K, i + 1])
    before = 0.5 * (st[K, i] + st[K, i - 1])
    ss, sg, gg = inverse(diag + st[C, i] + fy + before, st[C, i], mask)
    values = ((FX, fx), (FZ, fz), (H, h), (FY, fy), (ASS, ss), (ASG, sg), (AGG, gg))
    return [(st, (plane, i), v) for plane, v in values]


def row_sweep(st, i, source, target, edge):
    s, g = relaxed(st, i, source, *row_residual(st, i, source, edge))
    return [(st, (target, i), s), (st, (target + 1, i), g)]


def first_partial(res_s, res_g, s, s_d, g, g_d, fy, onward):
    return res_s + fy * (s_d - s), res_g + CONDUCT * g_d - FLOW * (g - g_d if onward else g)


def send_planes(st, onward, edge):
    ny = st.shape[1] - 2
    e, d, near = (ny, ny - 1, ny - 1) if onward else (1, 2, 1)
    fy, s, g, g_d = st[FY, near], st[SA, e], st[GA, e], st[GA, d]
    part_s, part_g = row_inner(st, e, SA, edge)
    m_1s, m_1g = first_partial(st[RS, e] + part_s, st[RG, e] + part_g, s, st[SA, d], g, g_d, fy, onward)
    m_2s = st[RS, e] + fy * st[SB, d]
    m_2g = st[RG, e] + (CONDUCT + FLOW if onward else CONDUCT) * st[GB, d]
    return [s, g, st[K, e], st[C, e], fy, m_1s, m_1g, m_2s, m_2g]


def across_parts(ext):
    parts, at = [], 0
    for k in range(EARLY, MESSAGE):
        parts.append((k, CROP, ext - CROP, at))
        at += ext - 2 * CROP
    for k in range(EARLY):
        more = 1 if k in (M_1S, M_1G) else 0
        for low, high in ((CROP, PAD + more), (ext - PAD - more, ext - CROP)):
            parts.append((k, low, high, at))
            at += high - low
    return parts, (at + 7) // 8 * 8


def write_across(ref, k, value):
    for plane, low, high, at in across_parts(value.shape[0])[0]:
        if plane == k:
            ref[at : at + high - low] = value[low:high]


def read_across(early, across, outer, k):
    ext = outer.shape[1]
    if k < EARLY:
        outer[k, PAD : ext - PAD] = early[k]
    for plane, low, high, at in across_parts(ext)[0]:
        if plane == k:
            outer[k, low:high] = across[at : at + high - low]


def write_beside(refs, k, value):
    refs[k // THIRD][k % THIRD] = value[CROP : value.shape[0] - CROP]


def read_beside(refs, outer, k):
    outer[k, CROP : outer.shape[1] - CROP] = refs[k // THIRD][k % THIRD]


def first_end(st, one, two, after, write):
    planes, rows, ext, nz = st.shape
    ny, nx = rows - 2, ext - 2 * PAD
    mask = x_mask((ext, nz), nx)
    edge = edge_weights((ext, nz))
    e, d, f = (ny, ny - 1, ny - 2) if after else (1, 2, 3)
    for i in (e, d, f):
        place_halo(st, one, two, i - 1, nx)
    fx, fz, h, diag = faces(st[K, e])
    st[FX, e], st[FZ, e], st[H, e] = fx, fz, h
    st[FY, min(e, d)] = 0.5 * (st[K, e] + st[K, d])
    st[FY, min(d, f)] = 0.5 * (st[K, d] + st[K, f])
    grouped([d], lambda i: row_coefficients(st, i, mask))
    grouped([d], lambda i: row_sweep(st, i, SA, SB, edge))
    for k, value in enumerate(send_planes(st, after, edge)):
        write(k, value)


def either_first(st, one, two, after, write):
    for is_after in (True, False):

        @pl.when(after == is_after)
        def _():
            first_end(st, one, two, is_after, write)


def first_kernel(st_in, one, two, st, across):
    del st_in
    either_first(st, one, two, lax.axis_index("gy") % 2 == 1, functools.partial(write_across, across))


def other_kernel(st_in, one, two, st, *beside):
    del st_in
    either_first(st, one, two, lax.axis_index("gy") % 2 == 0, functools.partial(write_beside, beside))
    planes, rows, ext, nz = st.shape
    ny, nx = rows - 2, ext - 2 * PAD
    mask = x_mask((ext, nz), nx)
    for y in range(3, ny - 3):
        place_halo(st, one, two, y, nx)
    grouped(list(range(3, ny - 1)), lambda i: row_coefficients(st, i, mask))


def outer_residual(st, i, s_at, rs, rg, fy_out, edge, after):
    part_s, part_g = row_inner(st, i, s_at, edge)
    s, g = st[s_at, i], st[s_at + 1, i]
    if after:
        part_s += st[FY, i - 1] * (st[s_at, i - 1] - s)
        part_g += (CONDUCT + FLOW) * st[s_at + 1, i - 1]
    else:
        part_s += st[FY, i] * (st[s_at, i + 1] - s)
        part_g += CONDUCT * st[s_at + 1, i + 1]
    return rs + part_s - fy_out * s, rg + part_g - FLOW * g


def pair_x(v):
    row = lax.broadcasted_iota(jnp.int32, v.shape, 0)
    return v + jnp.where(row % 2 == 0, up_x(v), down_x(v))


def coarse_coefficients(c_sum, k_sum):
    per_solid = 1.0 / (4.0 * SOLID_CAP + c_sum + LUMP * k_sum)
    ratio = c_sum * per_solid
    return per_solid, ratio, 1.0 / ((4.0 * GAS_CAP + 2.0 * FLOW) + c_sum - c_sum * ratio)


def coarse_row(st, coarse, j, mask, edge):
    i = 2 * j + 1
    res_s, res_g = row_residual(st, i, SA, edge)
    more_s, more_g = row_residual(st, i + 1, SA, edge)
    res_s, res_g = pair_x((res_s + more_s) * mask), pair_x((res_g + more_g) * mask)
    c_sum = pair_x(st[C, i] + st[C, i + 1])
    per_solid, ratio, per_gas = coarse_coefficients(c_sum, pair_x(st[K, i] + st[K, i + 1]))
    lead = res_s * per_solid
    values = (lead, ratio, (2.0 * FLOW) * per_gas, (res_g + c_sum * lead) * per_gas)
    return [(coarse, (k, j), v) for k, v in enumerate(values)]


def inner_kernel(st_in, early, st, coarse):
    del st_in, early
    planes, rows, ext, nz = st.shape
    ny, nx = rows - 2, ext - 2 * PAD
    shape = (ext, nz)
    mask = x_mask(shape, nx)
    edge = edge_weights(shape)
    grouped(list(range(3, ny - 1)), lambda i: row_sweep(st, i, SA, SB, edge))
    grouped(list(range(3, ny - 1)), lambda i: row_sweep(st, i, SB, SA, edge))
    for j in range(2, ny // 2 - 2):
        for ref, at, value in coarse_row(st, coarse, j, mask, edge):
            ref[at] = value


def end_work(st, coarse, extra, read, outer, is_after):
    planes, rows, ext, nz = st.shape
    ny, nx = rows - 2, ext - 2 * PAD
    me, count = lax.axis_index("gy"), lax.axis_size("gy")
    mask = x_mask((ext, nz), nx)
    inside = jnp.where(me == (count - 1 if is_after else 0), 0.0, mask)
    edge = edge_weights((ext, nz))
    zeros = jnp.zeros((PAD, nz), jnp.float32)
    for k in range(MESSAGE):
        outer[k, :PAD] = zeros
        outer[k, ext - PAD :] = zeros
        read(outer, k)

    o, e, near = (ny + 1, ny, ny) if is_after else (0, 1, 0)
    to_o = CONDUCT + FLOW if is_after else CONDUCT
    s_o, g_o, k_o, c_o, fy_out = (outer[plane] for plane in (M_S, M_G, M_K, M_C, M_FY))
    fy = 0.5 * (k_o + st[K, e])
    fx, fz, h, diag = faces(k_o)
    inv_o = inverse(diag + c_o + fy_out + fy, c_o, inside)
    fx_e, fz_e = st[FX, e], st[FZ, e]
    diag = st[H, e] + (fx_e + down_x(fx_e)) + (fz_e + down_z(fz_e)) + st[C, e] + fy
    inv_e = inverse(diag + st[FY, near - 1 if is_after else near + 1], st[C, e], mask)
    for plane, value in ((SA, s_o), (GA, g_o), (K, k_o), (C, c_o), (FX, fx), (FZ, fz), (H, h)):
        st[plane, o] = value
    st[FY, near] = fy
    for k in range(3):
        st[ASS + k, o], st[ASS + k, e] = inv_o[k], inv_e[k]

    res = outer[M_1S] + fy * (st[SA, e] - s_o), outer[M_1G] + to_o * st[GA, e]
    new_o = relaxed(st, o, SA, *res)
    stores = row_sweep(st, e, SA, SB, edge)
    st[SB, o], st[GB, o] = new_o
    for ref, at, value in stores:
        ref[at] = value
    res = outer_residual(st, o, SB, outer[M_2S], outer[M_2G], fy_out, edge, is_after)
    new_o = relaxed(st, o, SB, *res)
    ends = [e - 1, e] if is_after else [e, e + 1]
    grouped(ends, lambda i: row_sweep(st, i, SB, SA, edge))
    st[SA, o], st[GA, o] = new_o
    for k, plane in enumerate((M_2S, M_2G, M_FY)):
        extra[(3 if is_after else 0) + k] = outer[plane]
    blocks = ny // 2
    stores = []
    for j in (blocks - 2, blocks - 1) if is_after else (0, 1):
        stores += coarse_row(st, coarse, j, mask, edge)
    for ref, at, value in stores:
        ref[at] = value


def either_end(after, st, coarse, extra, read, outer):
    for is_after in (True, False):

        @pl.when(after == is_after)
        def _():
            end_work(st, coarse, extra, read, outer, is_after)


def near_kernel(st_in, coarse_in, *refs):
    beside, (st, coarse, extra, outer) = refs[:-4], refs[-4:]
    del st_in, coarse_in
    either_end(lax.axis_index("gy") % 2 == 0, st, coarse, extra, functools.partial(read_beside, beside), outer)


def second_kernel(st_in, coarse_in, extra_in, early, across, *refs):
    st, coarse, extra, total, last_info, first_info, message, outer, squeeze = refs
    del st_in, coarse_in, extra_in
    planes, rows, ext, nz = st.shape
    ny, nx = rows - 2, ext - 2 * PAD
    me = lax.axis_index("gy")
    either_end(me % 2 == 1, st, coarse, extra, functools.partial(read_across, early, across), outer)

    blocks = ny // 2
    for k in range(4):
        squeeze[k] = coarse[k, 0]
    slopes, offsets = coarse[2, 0], coarse[3, 0]
    for j in range(1, blocks):
        slope = coarse[2, j]
        slopes, offsets = slope * slopes, slope * offsets + coarse[3, j]
        coarse[2, j], coarse[3, j] = slopes, offsets
    squeeze[4], squeeze[5], squeeze[6], squeeze[7] = slopes, offsets, coarse[0, blocks - 1], coarse[1, blocks - 1]

    span = nx // 2 + 2
    lead, ratio, slope, offset, slopes, offsets, lead_last, ratio_last = (
        squeeze[k, pl.ds(PAD - 2, span, 2), :] for k in range(8)
    )
    part = slice(PAD - 1, PAD + nx + 1)

    def increments(d, face, gas):
        return [(st[FY, face] * (st[SA, d] - st[SB, d]))[part], (gas * (st[GA, d] - st[GB, d]))[part]]

    onward = [lead_last, ratio_last] + increments(ny - 1, ny - 1, CONDUCT + FLOW)
    back = [lead, offset] + increments(2, 1, CONDUCT) + [slope, ratio]
    write_rows(total, [slopes, offsets])
    write_rows(last_info, onward)
    write_rows(first_info, back)
    for go, info in ((True, onward), (False, back)):

        @pl.when((me % 2 == 0) == go)
        def _():
            write_rows(message, [slopes, offsets] + info)


def write_rows(ref, values):
    at = 0
    for value in values:
        ref[at : at + value.shape[0]] = value
        at += value.shape[0]


class Rows:
    def __init__(self, nx):
        self.span = nx // 2 + 2
        self.map = 2 * self.span
        self.info = self.map + 2 * (nx + 2)
        self.rest = self.map
        self.final = self.map + self.info
        self.full = self.final + self.rest
        self.low = self.map
        self.high = self.low + self.info
        self.near = self.high + self.info + self.rest


def source(at, k, radix):
    if radix & (radix - 1) == 0:
        return at ^ k
    return (at + radix - k) % radix


def matchings(count, radix, stride):
    if (count, radix, stride) == (8, 4, 2):
        swaps = ((1, 2), (3, 4), (5, 6), (0, 7)), ((0, 3), (1, 5), (2, 6), (4, 7)), ((0, 4), (1, 6), (2, 5), (3, 7))
        out = []
        for pairs in swaps:
            senders = [0] * count
            for a, b in pairs:
                senders[a], senders[b] = b, a
            out.append((senders, len(out) == 0))
        return out
    out = []
    for k in range(1, radix):
        senders = []
        for me in range(count):
            at, low = me // stride % radix, me % stride
            senders.append(me - low + (source(at, k, radix) - at) * stride + (stride - 1 - low))
        out.append((senders, any(abs(source(at, k, radix) - at) == 1 for at in range(radix))))
    return sorted(out, key=lambda item: not item[1])


def look_up(table):
    me, value = lax.axis_index("gy"), jnp.int32(table[0])
    for k in range(1, len(table)):
        value = jnp.where(me == k, table[k], value)
    return value


def stages(count):
    if count % 2:
        return [1, count]
    out, rest = [2], count // 2
    while rest > 1:
        radix = next((r for r in (8, 4, 2) if rest % r == 0), rest)
        out.append(radix)
        rest //= radix
    return out if len(out) > 1 else out + [1]


def exchange_stage(messages, swaps):
    return [
        lax.ppermute(message, "gy", [(sender, me) for me, sender in enumerate(senders)])
        for (senders, near), message in zip(swaps, messages)
    ]


class Group:
    def __init__(self, radix, stride, others, nx):
        self.radix, self.others, self.nx = radix, others, nx
        me = lax.axis_index("gy")
        self.swaps = [
            (look_up([sender // stride % radix for sender in senders]), near)
            for senders, near in matchings(lax.axis_size("gy"), radix, stride)
        ]
        self.at = lax.rem(lax.div(me, stride), radix)
        low = lax.rem(me, stride)
        self.lowest, self.highest = low == 0, low == stride - 1

    def map_of(self, place, own):
        rows = Rows(self.nx)
        out = own
        for (sender, near), ref in zip(self.swaps, self.others):
            here = sender == place
            got = [ref[i * rows.span : (i + 1) * rows.span] for i in range(2)]
            out = got if out is None else [jnp.where(here, new, old) for new, old in zip(got, out)]
        return out

    def ahead(self, slope, offset):
        a, b = jnp.ones_like(slope), jnp.zeros_like(slope)
        for place in range(self.radix - 1):
            new_a, new_b = self.map_of(place, None)
            below = place < self.at
            a, b = jnp.where(below, new_a * a, a), jnp.where(below, new_a * b + new_b, b)
        return slope * a, slope * b + offset

    def total(self, own):
        a, b = self.map_of(0, own)
        for place in range(1, self.radix):
            new_a, new_b = self.map_of(place, own)
            a, b = new_a * a, new_a * b + new_b
        return a, b

    def collect(self, near, final):
        rows = Rows(self.nx)
        for (place, adjacent), ref in zip(self.swaps, self.others):
            if not adjacent:
                continue

            @pl.when(self.lowest & (place == self.at - 1))
            def _():
                near[rows.low : rows.low + rows.info] = ref[rows.map : rows.final]

            @pl.when(self.highest & (place == self.at + 1))
            def _():
                near[rows.high : rows.high + rows.info] = ref[rows.map : rows.final]
                rest = slice(0, rows.map) if final else slice(rows.final, rows.full)
                near[rows.high + rows.info : rows.near] = ref[rest]


def start_near(near, nx, nz):
    rows = Rows(nx)
    near[: rows.span] = jnp.ones((rows.span, nz), jnp.float32)
    near[rows.span :] = jnp.zeros((near.shape[0] - rows.span, nz), jnp.float32)


def join_kernel(radix, stride, final, nx, is_first, *refs):
    rows = Rows(nx)
    total, last_info, first_info, near_in = refs[:4]
    others, near, outs = refs[4 : 3 + radix], refs[3 + radix], refs[4 + radix :]
    nz = near.shape[1]
    if is_first:
        start_near(near, nx, nz)
    else:
        near[...] = near_in[...]
    group = Group(radix, stride, others, nx)
    own = [total[i * rows.span : (i + 1) * rows.span] for i in range(2)]
    ahead = group.ahead(near[: rows.span], near[rows.span : rows.map])
    write_rows(near, ahead)
    group.collect(near, False)
    whole = group.total(own)
    if final == 0:
        write_rows(outs[0], whole)
        return
    me, count = lax.axis_index("gy"), lax.axis_size("gy")
    for (senders, adjacent), out in zip(matchings(count, final, stride * radix), outs):
        up = look_up(senders) > me
        if not adjacent:
            write_rows(out, whole)
            continue

        @pl.when(up)
        def _():
            write_rows(out, whole)
            out[rows.map : rows.final] = last_info[: rows.info]

        @pl.when(jnp.logical_not(up))
        def _():
            out[: rows.map] = first_info[rows.info : rows.info + rows.rest]
            out[rows.map : rows.final] = first_info[: rows.info]


def full_message(nx, total, last_info, first_info, senders):
    rows = Rows(nx)
    onward = jnp.concatenate([total[: rows.map], last_info[: rows.info], first_info[rows.info : rows.info + rows.rest]])
    back = jnp.concatenate([total[: rows.map], first_info[: rows.info + rows.rest]])
    message = jnp.where(look_up(senders) > lax.axis_index("gy"), onward, back)
    return jnp.pad(message, ((0, -rows.full % 8), (0, 0)))


def third_kernel(radix, stride, *refs):
    st, extra, coarse, near_in = refs[:4]
    others, (out, sc, wide, near, done, sems) = refs[4 : 3 + radix], refs[3 + radix :]
    planes, rows, ext, nz = st.shape
    ny, nx = rows - 2, ext - 2 * PAD
    edge = edge_weights((ext, nz))
    blocks = ny // 2

    lay = Rows(nx)
    span = lay.span
    near[...] = near_in[...]
    group = Group(radix, stride, others, nx)
    if radix > 1:
        group.collect(near, True)
    gas_in = group.ahead(near[:span], near[span : lay.map])[1]
    at_high = lay.high + lay.info
    starts = [lay.low, lay.low + span, lay.high, lay.high + span, at_high, at_high + span]
    for k, v in enumerate([gas_in] + [near[start : start + span] for start in starts]):
        wide[k, : PAD - 2] = jnp.zeros((PAD - 2, nz), jnp.float32)
        wide[k, ext - PAD + 2 :] = jnp.zeros((PAD - 2, nz), jnp.float32)
        wide[k, pl.ds(PAD - 2, span, 2), :] = v
        wide[k, pl.ds(PAD - 1, span, 2), :] = v
    for k, start in enumerate((lay.low, lay.low + nx + 2, lay.high, lay.high + nx + 2)):
        start += lay.map
        wide[7 + k, :PAD] = jnp.zeros((PAD, nz), jnp.float32)
        wide[7 + k, ext - PAD :] = jnp.zeros((PAD, nz), jnp.float32)
        wide[7 + k, PAD - 1 : PAD + nx + 1] = near[start : start + nx + 2]

    gas_in = wide[0]
    last = ny + 1
    solid_low = wide[1] + wide[2] * gas_in
    sc[0, 0] = st[SA, 0] + solid_low
    sc[1, 0] = st[GA, 0] + gas_in

    def correct(j, carry):
        gas = coarse[2, j] * gas_in + coarse[3, j]
        solid = coarse[0, j] + coarse[1, j] * gas
        for i in (2 * j + 1, 2 * j + 2):
            sc[0, i] = st[SA, i] + solid
            sc[1, i] = st[GA, i] + gas
        return carry

    lax.fori_loop(0, blocks, correct, 0)
    gas = coarse[2, blocks - 1] * gas_in + coarse[3, blocks - 1]
    gas_high = wide[5] * gas + wide[4]
    solid_high = wide[3] + wide[6] * gas_high
    sc[0, last] = st[SA, last] + solid_high
    sc[1, last] = st[GA, last] + gas_high

    view = Fields(st, sc)
    for i, is_after, solid, gas in ((0, False, solid_low, gas_in), (last, True, solid_high, gas_high)):
        side = 3 if is_after else 0
        fy = extra[side + 2]
        to = 9 if is_after else 7
        rs = extra[side] + wide[to] + fy * solid
        rg = extra[side + 1] + wide[to + 1] + (CONDUCT if is_after else CONDUCT + FLOW) * gas
        res = outer_residual(view, i, SA, rs, rg, fy, edge, is_after)
        sc[2, i], sc[3, i] = relaxed(view, i, SA, *res)

    def sweep(k, carry):
        stores = []
        for r in range(GROUP):
            i = GROUP * k + 1 + r
            new_s, new_g = relaxed(view, i, SA, *row_residual(view, i, SA, edge))
            stores += [((2, i), new_s), ((3, i), new_g)]
        for at, value in stores:
            sc[at] = value
        return carry

    lax.fori_loop(0, ny // GROUP, sweep, 0)

    def leaving(k):
        part = pl.ds(GROUP * k, GROUP)
        return pltpu.make_async_copy(done.at[:, part], out.at[:, part], sems.at[k])

    def final(k, carry):
        stores = []
        for r in range(GROUP):
            i = GROUP * k + 1 + r
            new_s, new_g = last_relaxed(view, i, SB, edge, slice(PAD, PAD + nx))
            stores += [((0, i - 1), new_s), ((1, i - 1), new_g)]
        for at, value in stores:
            done[at] = value
        leaving(k).start()
        return carry

    lax.fori_loop(0, ny // GROUP, final, 0)
    for k in range(ny // GROUP):
        leaving(k).wait()


class Fields:
    def __init__(self, st, sc):
        self.st, self.sc = st, sc

    def __getitem__(self, at):
        return (self.sc if at[0] <= GB else self.st)[at]


def cost(rows, cells):
    return pl.CostEstimate(flops=50 * rows * cells, bytes_accessed=16 * 4 * rows * cells, transcendentals=0)


def swap(x, axis, first):
    pairs = []
    for i in range(first, lax.axis_size(axis) - 1, 2):
        pairs += [(i, i + 1), (i + 1, i)]
    return lax.ppermute(x, axis, pairs)


def shards(temps, right_side, exchange, coupling):
    temps, right_side = (jnp.transpose(a, (0, 2, 1, 3)) for a in (temps, right_side))
    exchange, coupling = (jnp.transpose(a, (1, 0, 2)) for a in (exchange, coupling))
    temps, right_side, exchange, coupling = (
        pltpu.with_memory_space_constraint(a, pltpu.HBM) for a in (temps, right_side, exchange, coupling)
    )
    ny, nx, nz = exchange.shape
    ext = nx + 2 * PAD
    f32 = functools.partial(jax.ShapeDtypeStruct, dtype=jnp.float32)

    strip = f32((strip_height(ny), nz))
    state = f32((PLANES, ny + 2, ext, nz))
    one, two, early, st = pl.pallas_call(
        pack_kernel,
        out_shape=(strip, strip, f32((EARLY, nx, nz)), state),
        in_specs=[HBM] * 4,
        out_specs=(VMEM,) * 4,
        scratch_shapes=[pltpu.SemaphoreType.DMA((6,))],
        compiler_params=PARAMS,
        name="pack_x",
    )(temps, right_side, exchange, coupling)
    one, two = swap(one, "gx", 0), swap(two, "gx", 1)
    early = swap(early, "gy", 1)

    def letter(planes):
        return f32((planes, ext - 2 * CROP, nz))

    st = pl.pallas_call(
        conduct_kernel,
        out_shape=state,
        in_specs=[VMEM],
        out_specs=VMEM,
        input_output_aliases={0: 0},
        compiler_params=PARAMS,
        cost_estimate=cost(2 * ny, ext * nz),
        name="conduct",
    )(st)
    st, across = pl.pallas_call(
        first_kernel,
        out_shape=(state, f32((across_parts(ext)[1], nz))),
        in_specs=[VMEM] * 3,
        out_specs=(VMEM,) * 2,
        input_output_aliases={0: 0},
        compiler_params=PARAMS,
        name="first",
    )(st, one, two)
    st, *beside = pl.pallas_call(
        other_kernel,
        out_shape=(state,) + (letter(THIRD),) * (MESSAGE // THIRD),
        in_specs=[VMEM] * 3,
        out_specs=(VMEM,) * (1 + MESSAGE // THIRD),
        input_output_aliases={0: 0},
        compiler_params=PARAMS,
        name="other",
    )(st, one, two)
    across = swap(across, "gy", 1)

    rows = f32((4, ny // 2, ext, nz))
    st, coarse = pl.pallas_call(
        inner_kernel,
        out_shape=(state, rows),
        in_specs=[VMEM] * 2,
        out_specs=(VMEM,) * 2,
        input_output_aliases={0: 0},
        compiler_params=PARAMS,
        cost_estimate=cost(4 * ny, ext * nz),
        name="inner",
    )(st, early)

    beside = [swap(part, "gy", 0) for part in beside]

    lay = Rows(nx)

    def tall(height):
        return f32(((height + 7) // 8 * 8, nz))

    letter_room = pltpu.VMEM((MESSAGE, ext, nz), jnp.float32)
    more = f32((6, ext, nz))
    st, coarse, extra = pl.pallas_call(
        near_kernel,
        out_shape=(state, rows, more),
        in_specs=[VMEM] * (2 + len(beside)),
        out_specs=(VMEM,) * 3,
        scratch_shapes=[letter_room],
        input_output_aliases={0: 0, 1: 1},
        compiler_params=PARAMS,
        name="near",
    )(st, coarse, *beside)
    st, coarse, extra, total, last_info, first_info, message = pl.pallas_call(
        second_kernel,
        out_shape=(state, rows, more, tall(lay.map), tall(lay.info), tall(lay.info + lay.rest), tall(lay.full)),
        in_specs=[VMEM] * 5,
        out_specs=(VMEM,) * 7,
        scratch_shapes=[letter_room, pltpu.VMEM((8, ext, nz), jnp.float32)],
        input_output_aliases={0: 0, 1: 1, 2: 2},
        compiler_params=PARAMS,
        name="second",
    )(st, coarse, extra, early, across)

    near, messages = total, [message]
    count = lax.axis_size("gy")
    radices, stride = stages(count), 1
    for place, radix in enumerate(radices[:-1]):
        swaps = matchings(count, radix, stride)
        if place:
            messages = [full_message(nx, total, last_info, first_info, senders) for senders, _ in swaps]
        others = exchange_stage(messages, swaps)
        final = radices[-1] if place == len(radices) - 2 else 0
        following = matchings(count, final, stride * radix) if final else []
        outs = [tall(lay.final if adjacent else lay.map) for _, adjacent in following] if final else [tall(lay.map)]
        near, *messages = pl.pallas_call(
            functools.partial(join_kernel, radix, stride, final, nx, place == 0),
            out_shape=(tall(lay.near), *outs),
            in_specs=[VMEM] * (3 + radix),
            out_specs=(VMEM,) * (1 + len(outs)),
            compiler_params=PARAMS,
            name="join",
        )(total, last_info, first_info, near, *others)
        total = total if final else messages[0]
        stride *= radix
    got = exchange_stage(messages, matchings(count, radices[-1], stride))

    out = pl.pallas_call(
        functools.partial(third_kernel, radices[-1], stride),
        out_shape=f32((2, ny, nx, nz)),
        in_specs=[VMEM] * (4 + len(got)),
        out_specs=HBM,
        scratch_shapes=[
            pltpu.VMEM((4, ny + 2, ext, nz), jnp.float32),
            pltpu.VMEM((11, ext, nz), jnp.float32),
            pltpu.VMEM(tall(lay.near).shape, jnp.float32),
            pltpu.VMEM((2, ny, nx, nz), jnp.float32),
            pltpu.SemaphoreType.DMA((ny // GROUP,)),
        ],
        compiler_params=PARAMS,
        name="third",
    )(st, extra, coarse, near, *got)
    return jnp.transpose(out, (0, 2, 1, 3))


def solution(mesh):
    return jax.shard_map(
        shards,
        mesh=mesh,
        in_specs=(
            P(None, "gx", "gy", None),
            P(None, "gx", "gy", None),
            P("gx", "gy", None),
            P("gx", "gy", None),
        ),
        out_specs=P(None, "gx", "gy", None),
        check_vma=False,
    )
```

```python
import functools

import jax
import jax.numpy as jnp
from jax import lax
from jax.experimental import pallas as pl
from jax.experimental.pallas import tpu as pltpu
from jax.sharding import PartitionSpec as P

SOLID_CAP, GAS_CAP, FLOW, CONDUCT, RELAX, LUMP = 0.5, 0.02, 40.0, 0.05, 0.8, 0.25
GAS_SELF = GAS_CAP + 4.5 * CONDUCT

PAD = 8
WX = 5
CROP = 4
(SA, GA, SB, GB, K, C, RS, RG, FX, FZ, H, FY, ASS, ASG, AGG) = range(15)
PLANES = 15
(M_S, M_G, M_K, M_C, M_FY, M_1S, M_1G, M_2S, M_2G) = range(9)
MESSAGE, EARLY, THIRD = 9, 7, 3

GROUP = 6

VMEM = pl.BlockSpec(memory_space=pltpu.VMEM)
HBM = pl.BlockSpec(memory_space=pltpu.HBM)
PARAMS = pltpu.CompilerParams(vmem_limit_bytes=40 * 1024 * 1024)


def up_x(v):
    return pltpu.roll(v, v.shape[0] - 1, 0)


def down_x(v):
    return pltpu.roll(v, 1, 0)


def up_z(v):
    return pltpu.roll(v, v.shape[1] - 1, 1)


def down_z(v):
    return pltpu.roll(v, 1, 1)


def lanes(shape):
    return lax.broadcasted_iota(jnp.int32, shape, 1)


def x_mask(shape, nx):
    row = lax.broadcasted_iota(jnp.int32, shape, 0)
    place, count = lax.axis_index("gx"), lax.axis_size("gx")
    low = jnp.where(place == 0, PAD, PAD - WX)
    high = jnp.where(place == count - 1, PAD + nx, PAD + nx + WX)
    return jnp.where((row >= low) & (row < high), 1.0, 0.0).astype(jnp.float32)


PAIRS = ((SA, GA), (C, RS), (RG, K))
STRIP_ROWS = 8 * len(PAIRS)


def strip_height(ny):
    return ny * STRIP_ROWS + (ny + 7) // 8 * 8


def sublanes(nz):
    return lax.broadcasted_iota(jnp.int32, (8, nz), 0)


def conductivity_of(s, exchange):
    return 1.0 + 4.0 * exchange * s * s * s


def strip_side(s, g, k, rs, rg, c, low):
    row = sublanes(s.shape[1])
    inn, shift = (3, 7) if low else (4, 1)
    k_out, s_out, g_out = (pltpu.roll(v, shift, 0) for v in (k, s, g))
    rs = rs + jnp.where(row == inn, 0.5 * (k + k_out) * s_out, 0.0)
    rg = rg + jnp.where(row == inn, CONDUCT * g_out, 0.0)
    values = {SA: s, GA: g, K: k, RS: rs, RG: rg, C: c}
    tiles = []
    for a, b in PAIRS:
        a, b = values[a], values[b]
        a, b = (a, pltpu.roll(b, 4, 0)) if low else (pltpu.roll(a, 4, 0), b)
        tiles.append(jnp.where(row < 4, a, b))
    return tiles, (k[4:5] if low else k[3:4])


def pack_kernel(temps, right, exchange, coupling, one, two, early, st, sems):
    even = lax.axis_index("gx") % 2 == 0
    odd = lax.axis_index("gy") % 2 == 1
    ny, nx, nz = exchange.shape
    copies = []
    for k, (plane, ref) in enumerate(
        ((SA, temps.at[0]), (K, exchange), (GA, temps.at[1]), (C, coupling), (RS, right.at[0]), (RG, right.at[1]))
    ):
        to = st.at[plane, pl.ds(1, ny), pl.ds(PAD, nx)]
        copies.append(pltpu.make_async_copy(ref, to, sems.at[k]))
    for copy in copies:
        copy.start()
    for copy in copies:
        copy.wait()
    for i in range(1, ny + 1):
        sides = []
        for start in (PAD, PAD + nx - 8):
            s, g, e, rs, rg, c = (st[plane, i, start : start + 8] for plane in (SA, GA, K, RS, RG, C))
            sides.append(strip_side(s, g, conductivity_of(s, e), rs, rg, c, start == PAD))
        (low, low_k), (high, high_k) = sides
        for p in range(len(PAIRS)):
            part = slice((i - 1) * STRIP_ROWS + 8 * p, (i - 1) * STRIP_ROWS + 8 * p + 8)
            one[part] = jnp.where(even, high[p], low[p])
            two[part] = jnp.where(even, low[p], high[p])
        part = slice(ny * STRIP_ROWS + i - 1, ny * STRIP_ROWS + i)
        one[part] = jnp.where(even, high_k, low_k)
        two[part] = jnp.where(even, low_k, high_k)
    own = slice(PAD, PAD + nx)
    for is_odd, e, d in ((True, ny, ny - 1), (False, 1, 2)):

        @pl.when(odd == is_odd)
        def _():
            s, s_d, g, g_d = st[SA, e, own], st[SA, d, own], st[GA, e, own], st[GA, d, own]
            c, k, k_d = st[C, e, own], conductivity_of(s, st[K, e, own]), conductivity_of(s_d, st[K, d, own])
            fx, fz, h, _ = faces(k)
            fy = 0.5 * (k + k_d)
            part_s, part_g = inner(s, g, c, h, fx, fz, edge_weights((nx, nz)))
            m_1s, m_1g = first_partial(st[RS, e, own] + part_s, st[RG, e, own] + part_g, s, s_d, g, g_d, fy, is_odd)
            for plane, value in enumerate((s, g, k, c, fy, m_1s, m_1g)):
                early[plane] = value


def conduct_kernel(st_in, st):
    del st_in
    planes, rows, ext, nz = st.shape
    own = slice(PAD, ext - PAD)
    for i in range(1, rows - 1):
        st[K, i, own] = conductivity_of(st[SA, i, own], st[K, i, own])


def place_halo(st, one, two, y, nx):
    even = lax.axis_index("gx") % 2 == 0
    ny, row = st.shape[1] - 2, sublanes(st.shape[3])
    i = y + 1

    def received(part):
        a, b = one[part], two[part]
        return jnp.where(even, b, a), jnp.where(even, a, b)

    for p, (plane_a, plane_b) in enumerate(PAIRS):
        before, after = received(slice(y * STRIP_ROWS + 8 * p, y * STRIP_ROWS + 8 * p + 8))
        before = {plane_a: pltpu.roll(before, 4, 0), plane_b: before}
        after = {plane_a: after, plane_b: pltpu.roll(after, 4, 0)}
        for plane in (plane_a, plane_b):
            low, high = jnp.where(row >= 4, before[plane], 0.0), jnp.where(row < 4, after[plane], 0.0)
            if plane == K:
                k_low, k_high = received(slice(ny * STRIP_ROWS + y, ny * STRIP_ROWS + y + 1))
                low, high = jnp.where(row == 3, k_low, low), jnp.where(row == 4, k_high, high)
            st[plane, i, :PAD] = low
            st[plane, i, PAD + nx :] = high


def inner(s, g, c, h, fx, fz, edge):
    t = c * (s - g)
    flux_x = fx * (up_x(s) - s)
    flux_z = fz * (up_z(s) - s)
    part_s = (flux_x - down_x(flux_x)) + (flux_z - down_z(flux_z)) - h * s - t
    part_g = (
        t
        - GAS_SELF * g
        + CONDUCT * (up_x(g) + down_x(g))
        + edge[0] * up_z(g)
        + edge[1] * down_z(g)
    )
    return part_s, part_g


def edge_weights(shape):
    lane = lanes(shape)
    weight = jnp.float32(0.25 * CONDUCT)
    return jnp.where(lane == shape[1] - 1, 0.0, weight), jnp.where(lane == 0, 0.0, weight)


def row_inner(st, i, s_at, edge):
    return inner(st[s_at, i], st[s_at + 1, i], st[C, i], st[H, i], st[FX, i], st[FZ, i], edge)


def row_residual(st, i, s_at, edge):
    part_s, part_g = row_inner(st, i, s_at, edge)
    s, g, before = st[s_at, i], st[s_at + 1, i], st[s_at + 1, i - 1]
    part_s += st[FY, i] * (st[s_at, i + 1] - s) + st[FY, i - 1] * (st[s_at, i - 1] - s)
    part_g += CONDUCT * (st[s_at + 1, i + 1] + before) - FLOW * (g - before)
    return st[RS, i] + part_s, st[RG, i] + part_g


def relaxed(st, i, s_at, res_s, res_g):
    s = st[s_at, i] + st[ASS, i] * res_s + st[ASG, i] * res_g
    g = st[s_at + 1, i] + st[ASG, i] * res_s + st[AGG, i] * res_g
    return s, g


def faces(k):
    lane = lanes(k.shape)
    end = k.shape[1] - 1
    fx = 0.5 * (k + up_x(k))
    fz = jnp.where(lane == end, 0.0, 0.125 * (k + up_z(k)))
    h = SOLID_CAP + jnp.where((lane == 0) | (lane == end), 0.125 * k, 0.0)
    return fx, fz, h, h + (fx + down_x(fx)) + (fz + down_z(fz))


def inverse(diag, c, mask):
    gas_diag = (GAS_SELF + FLOW) + c
    inv = (RELAX * mask) / (diag * gas_diag - c * c)
    return inv * gas_diag, inv * c, inv * diag


def last_relaxed(st, i, s_at, edge, own):
    full_s, full_g = st[s_at, i], st[s_at + 1, i]
    s, g = full_s[own], full_g[own]
    flux_x = st[FX, i] * (up_x(full_s) - full_s)
    flux_z = st[FZ, i, own] * (up_z(s) - s)
    c, before = st[C, i, own], st[s_at + 1, i - 1, own]
    t = c * (s - g)
    res_s = st[RS, i, own] + (flux_x[own] - down_x(flux_x)[own]) + (flux_z - down_z(flux_z)) - st[H, i, own] * s - t
    res_s += st[FY, i, own] * (st[s_at, i + 1, own] - s) + st[FY, i - 1, own] * (st[s_at, i - 1, own] - s)
    res_g = st[RG, i, own] + t - GAS_SELF * g + edge[0][own] * up_z(g) + edge[1][own] * down_z(g)
    res_g += CONDUCT * (up_x(full_g)[own] + down_x(full_g)[own] + st[s_at + 1, i + 1, own] + before) - FLOW * (g - before)
    ss, sg, gg = st[ASS, i, own], st[ASG, i, own], st[AGG, i, own]
    return s + ss * res_s + sg * res_g, g + sg * res_s + gg * res_g


def grouped(rows, work, size=8):
    for start in range(0, len(rows), size):
        stores = []
        for i in rows[start : start + size]:
            stores += work(i)
        for ref, at, value in stores:
            ref[at] = value


def row_coefficients(st, i, mask):
    fx, fz, h, diag = faces(st[K, i])
    fy = 0.5 * (st[K, i] + st[K, i + 1])
    before = 0.5 * (st[K, i] + st[K, i - 1])
    ss, sg, gg = inverse(diag + st[C, i] + fy + before, st[C, i], mask)
    values = ((FX, fx), (FZ, fz), (H, h), (FY, fy), (ASS, ss), (ASG, sg), (AGG, gg))
    return [(st, (plane, i), v) for plane, v in values]


def row_sweep(st, i, source, target, edge):
    s, g = relaxed(st, i, source, *row_residual(st, i, source, edge))
    return [(st, (target, i), s), (st, (target + 1, i), g)]


def first_partial(res_s, res_g, s, s_d, g, g_d, fy, onward):
    return res_s + fy * (s_d - s), res_g + CONDUCT * g_d - FLOW * (g - g_d if onward else g)


def send_planes(st, onward, edge):
    ny = st.shape[1] - 2
    e, d, near = (ny, ny - 1, ny - 1) if onward else (1, 2, 1)
    fy, s, g, g_d = st[FY, near], st[SA, e], st[GA, e], st[GA, d]
    part_s, part_g = row_inner(st, e, SA, edge)
    m_1s, m_1g = first_partial(st[RS, e] + part_s, st[RG, e] + part_g, s, st[SA, d], g, g_d, fy, onward)
    m_2s = st[RS, e] + fy * st[SB, d]
    m_2g = st[RG, e] + (CONDUCT + FLOW if onward else CONDUCT) * st[GB, d]
    return [s, g, st[K, e], st[C, e], fy, m_1s, m_1g, m_2s, m_2g]


def across_parts(ext):
    parts, at = [], 0
    for k in range(EARLY, MESSAGE):
        parts.append((k, CROP, ext - CROP, at))
        at += ext - 2 * CROP
    for k in range(EARLY):
        more = 1 if k in (M_1S, M_1G) else 0
        for low, high in ((CROP, PAD + more), (ext - PAD - more, ext - CROP)):
            parts.append((k, low, high, at))
            at += high - low
    return parts, (at + 7) // 8 * 8


def write_across(ref, k, value):
    for plane, low, high, at in across_parts(value.shape[0])[0]:
        if plane == k:
            ref[at : at + high - low] = value[low:high]


def read_across(early, across, outer, k):
    ext = outer.shape[1]
    if k < EARLY:
        outer[k, PAD : ext - PAD] = early[k]
    for plane, low, high, at in across_parts(ext)[0]:
        if plane == k:
            outer[k, low:high] = across[at : at + high - low]


def write_beside(refs, k, value):
    refs[k // THIRD][k % THIRD] = value[CROP : value.shape[0] - CROP]


def read_beside(refs, outer, k):
    outer[k, CROP : outer.shape[1] - CROP] = refs[k // THIRD][k % THIRD]


def first_end(st, one, two, after, write):
    planes, rows, ext, nz = st.shape
    ny, nx = rows - 2, ext - 2 * PAD
    mask = x_mask((ext, nz), nx)
    edge = edge_weights((ext, nz))
    e, d, f = (ny, ny - 1, ny - 2) if after else (1, 2, 3)
    for i in (e, d, f):
        place_halo(st, one, two, i - 1, nx)
    fx, fz, h, diag = faces(st[K, e])
    st[FX, e], st[FZ, e], st[H, e] = fx, fz, h
    st[FY, min(e, d)] = 0.5 * (st[K, e] + st[K, d])
    st[FY, min(d, f)] = 0.5 * (st[K, d] + st[K, f])
    grouped([d], lambda i: row_coefficients(st, i, mask))
    grouped([d], lambda i: row_sweep(st, i, SA, SB, edge))
    for k, value in enumerate(send_planes(st, after, edge)):
        write(k, value)


def either_first(st, one, two, after, write):
    for is_after in (True, False):

        @pl.when(after == is_after)
        def _():
            first_end(st, one, two, is_after, write)


def first_kernel(st_in, one, two, st, across):
    del st_in
    either_first(st, one, two, lax.axis_index("gy") % 2 == 1, functools.partial(write_across, across))


def other_kernel(st_in, one, two, st, *beside):
    del st_in
    either_first(st, one, two, lax.axis_index("gy") % 2 == 0, functools.partial(write_beside, beside))
    planes, rows, ext, nz = st.shape
    ny, nx = rows - 2, ext - 2 * PAD
    mask = x_mask((ext, nz), nx)
    for y in range(3, ny - 3):
        place_halo(st, one, two, y, nx)
    grouped(list(range(3, ny - 1)), lambda i: row_coefficients(st, i, mask))


def outer_residual(st, i, s_at, rs, rg, fy_out, edge, after):
    part_s, part_g = row_inner(st, i, s_at, edge)
    s, g = st[s_at, i], st[s_at + 1, i]
    if after:
        part_s += st[FY, i - 1] * (st[s_at, i - 1] - s)
        part_g += (CONDUCT + FLOW) * st[s_at + 1, i - 1]
    else:
        part_s += st[FY, i] * (st[s_at, i + 1] - s)
        part_g += CONDUCT * st[s_at + 1, i + 1]
    return rs + part_s - fy_out * s, rg + part_g - FLOW * g


def pair_x(v):
    row = lax.broadcasted_iota(jnp.int32, v.shape, 0)
    return v + jnp.where(row % 2 == 0, up_x(v), down_x(v))


def coarse_coefficients(c_sum, k_sum):
    per_solid = 1.0 / (4.0 * SOLID_CAP + c_sum + LUMP * k_sum)
    ratio = c_sum * per_solid
    return per_solid, ratio, 1.0 / ((4.0 * GAS_CAP + 2.0 * FLOW) + c_sum - c_sum * ratio)


def coarse_row(st, coarse, j, mask, edge):
    i = 2 * j + 1
    res_s, res_g = row_residual(st, i, SA, edge)
    more_s, more_g = row_residual(st, i + 1, SA, edge)
    res_s, res_g = pair_x((res_s + more_s) * mask), pair_x((res_g + more_g) * mask)
    c_sum = pair_x(st[C, i] + st[C, i + 1])
    per_solid, ratio, per_gas = coarse_coefficients(c_sum, pair_x(st[K, i] + st[K, i + 1]))
    lead = res_s * per_solid
    values = (lead, ratio, (2.0 * FLOW) * per_gas, (res_g + c_sum * lead) * per_gas)
    return [(coarse, (k, j), v) for k, v in enumerate(values)]


def inner_kernel(st_in, early, st, coarse):
    del st_in, early
    planes, rows, ext, nz = st.shape
    ny, nx = rows - 2, ext - 2 * PAD
    shape = (ext, nz)
    mask = x_mask(shape, nx)
    edge = edge_weights(shape)
    grouped(list(range(3, ny - 1)), lambda i: row_sweep(st, i, SA, SB, edge))
    grouped(list(range(3, ny - 1)), lambda i: row_sweep(st, i, SB, SA, edge))
    grouped(list(range(2, ny // 2 - 2)), lambda j: coarse_row(st, coarse, j, mask, edge))


def end_work(st, coarse, extra, read, outer, is_after):
    planes, rows, ext, nz = st.shape
    ny, nx = rows - 2, ext - 2 * PAD
    me, count = lax.axis_index("gy"), lax.axis_size("gy")
    mask = x_mask((ext, nz), nx)
    inside = jnp.where(me == (count - 1 if is_after else 0), 0.0, mask)
    edge = edge_weights((ext, nz))
    zeros = jnp.zeros((PAD, nz), jnp.float32)
    for k in range(MESSAGE):
        outer[k, :PAD] = zeros
        outer[k, ext - PAD :] = zeros
        read(outer, k)

    o, e, near = (ny + 1, ny, ny) if is_after else (0, 1, 0)
    to_o = CONDUCT + FLOW if is_after else CONDUCT
    s_o, g_o, k_o, c_o, fy_out = (outer[plane] for plane in (M_S, M_G, M_K, M_C, M_FY))
    fy = 0.5 * (k_o + st[K, e])
    fx, fz, h, diag = faces(k_o)
    inv_o = inverse(diag + c_o + fy_out + fy, c_o, inside)
    fx_e, fz_e = st[FX, e], st[FZ, e]
    diag = st[H, e] + (fx_e + down_x(fx_e)) + (fz_e + down_z(fz_e)) + st[C, e] + fy
    inv_e = inverse(diag + st[FY, near - 1 if is_after else near + 1], st[C, e], mask)
    for plane, value in ((SA, s_o), (GA, g_o), (K, k_o), (C, c_o), (FX, fx), (FZ, fz), (H, h)):
        st[plane, o] = value
    st[FY, near] = fy
    for k in range(3):
        st[ASS + k, o], st[ASS + k, e] = inv_o[k], inv_e[k]

    res = outer[M_1S] + fy * (st[SA, e] - s_o), outer[M_1G] + to_o * st[GA, e]
    new_o = relaxed(st, o, SA, *res)
    stores = row_sweep(st, e, SA, SB, edge)
    st[SB, o], st[GB, o] = new_o
    for ref, at, value in stores:
        ref[at] = value
    res = outer_residual(st, o, SB, outer[M_2S], outer[M_2G], fy_out, edge, is_after)
    new_o = relaxed(st, o, SB, *res)
    ends = [e - 1, e] if is_after else [e, e + 1]
    grouped(ends, lambda i: row_sweep(st, i, SB, SA, edge))
    st[SA, o], st[GA, o] = new_o
    for k, plane in enumerate((M_2S, M_2G, M_FY)):
        extra[(3 if is_after else 0) + k] = outer[plane]
    blocks = ny // 2
    stores = []
    for j in (blocks - 2, blocks - 1) if is_after else (0, 1):
        stores += coarse_row(st, coarse, j, mask, edge)
    for ref, at, value in stores:
        ref[at] = value


def either_end(after, st, coarse, extra, read, outer):
    for is_after in (True, False):

        @pl.when(after == is_after)
        def _():
            end_work(st, coarse, extra, read, outer, is_after)


def near_kernel(st_in, coarse_in, *refs):
    beside, (st, coarse, extra, outer) = refs[:-4], refs[-4:]
    del st_in, coarse_in
    either_end(lax.axis_index("gy") % 2 == 0, st, coarse, extra, functools.partial(read_beside, beside), outer)


def second_kernel(st_in, coarse_in, extra_in, early, across, *refs):
    st, coarse, extra, total, last_info, first_info, message, outer, squeeze = refs
    del st_in, coarse_in, extra_in
    planes, rows, ext, nz = st.shape
    ny, nx = rows - 2, ext - 2 * PAD
    me = lax.axis_index("gy")
    either_end(me % 2 == 1, st, coarse, extra, functools.partial(read_across, early, across), outer)

    blocks = ny // 2
    for k in range(4):
        squeeze[k] = coarse[k, 0]
    slopes, offsets = coarse[2, 0], coarse[3, 0]
    for j in range(1, blocks):
        slope = coarse[2, j]
        slopes, offsets = slope * slopes, slope * offsets + coarse[3, j]
        coarse[2, j], coarse[3, j] = slopes, offsets
    squeeze[4], squeeze[5], squeeze[6], squeeze[7] = slopes, offsets, coarse[0, blocks - 1], coarse[1, blocks - 1]

    span = nx // 2 + 2
    lead, ratio, slope, offset, slopes, offsets, lead_last, ratio_last = (
        squeeze[k, pl.ds(PAD - 2, span, 2), :] for k in range(8)
    )
    part = slice(PAD - 1, PAD + nx + 1)

    def increments(d, face, gas):
        return [(st[FY, face] * (st[SA, d] - st[SB, d]))[part], (gas * (st[GA, d] - st[GB, d]))[part]]

    onward = [lead_last, ratio_last] + increments(ny - 1, ny - 1, CONDUCT + FLOW)
    back = [lead, offset] + increments(2, 1, CONDUCT) + [slope, ratio]
    write_rows(total, [slopes, offsets])
    write_rows(last_info, onward)
    write_rows(first_info, back)
    for go, info in ((True, onward), (False, back)):

        @pl.when((me % 2 == 0) == go)
        def _():
            write_rows(message, [slopes, offsets] + info)


def write_rows(ref, values):
    at = 0
    for value in values:
        ref[at : at + value.shape[0]] = value
        at += value.shape[0]


class Rows:
    def __init__(self, nx):
        self.span = nx // 2 + 2
        self.map = 2 * self.span
        self.info = self.map + 2 * (nx + 2)
        self.rest = self.map
        self.final = self.map + self.info
        self.full = self.final + self.rest
        self.low = self.map
        self.high = self.low + self.info
        self.near = self.high + self.info + self.rest


def source(at, k, radix):
    if radix & (radix - 1) == 0:
        return at ^ k
    return (at + radix - k) % radix


def matchings(count, radix, stride):
    if (count, radix, stride) == (8, 4, 2):
        swaps = ((1, 2), (3, 4), (5, 6), (0, 7)), ((0, 3), (1, 5), (2, 6), (4, 7)), ((0, 4), (1, 6), (2, 5), (3, 7))
        out = []
        for pairs in swaps:
            senders = [0] * count
            for a, b in pairs:
                senders[a], senders[b] = b, a
            out.append((senders, len(out) == 0))
        return out
    out = []
    for k in range(1, radix):
        senders = []
        for me in range(count):
            at, low = me // stride % radix, me % stride
            senders.append(me - low + (source(at, k, radix) - at) * stride + (stride - 1 - low))
        out.append((senders, any(abs(source(at, k, radix) - at) == 1 for at in range(radix))))
    return sorted(out, key=lambda item: not item[1])


def look_up(table):
    me, value = lax.axis_index("gy"), jnp.int32(table[0])
    for k in range(1, len(table)):
        value = jnp.where(me == k, table[k], value)
    return value


def stages(count):
    if count % 2:
        return [1, count]
    out, rest = [2], count // 2
    while rest > 1:
        radix = next((r for r in (8, 4, 2) if rest % r == 0), rest)
        out.append(radix)
        rest //= radix
    return out if len(out) > 1 else out + [1]


def exchange_stage(messages, swaps):
    return [
        lax.ppermute(message, "gy", [(sender, me) for me, sender in enumerate(senders)])
        for (senders, near), message in zip(swaps, messages)
    ]


class Group:
    def __init__(self, radix, stride, others, nx):
        self.radix, self.others, self.nx = radix, others, nx
        me = lax.axis_index("gy")
        self.swaps = [
            (look_up([sender // stride % radix for sender in senders]), near)
            for senders, near in matchings(lax.axis_size("gy"), radix, stride)
        ]
        self.at = lax.rem(lax.div(me, stride), radix)
        low = lax.rem(me, stride)
        self.lowest, self.highest = low == 0, low == stride - 1

    def map_of(self, place, own):
        rows = Rows(self.nx)
        out = own
        for (sender, near), ref in zip(self.swaps, self.others):
            here = sender == place
            got = [ref[i * rows.span : (i + 1) * rows.span] for i in range(2)]
            out = got if out is None else [jnp.where(here, new, old) for new, old in zip(got, out)]
        return out

    def ahead(self, slope, offset):
        a, b = jnp.ones_like(slope), jnp.zeros_like(slope)
        for place in range(self.radix - 1):
            new_a, new_b = self.map_of(place, None)
            below = place < self.at
            a, b = jnp.where(below, new_a * a, a), jnp.where(below, new_a * b + new_b, b)
        return slope * a, slope * b + offset

    def total(self, own):
        a, b = self.map_of(0, own)
        for place in range(1, self.radix):
            new_a, new_b = self.map_of(place, own)
            a, b = new_a * a, new_a * b + new_b
        return a, b

    def collect(self, near, final):
        rows = Rows(self.nx)
        for (place, adjacent), ref in zip(self.swaps, self.others):
            if not adjacent:
                continue

            @pl.when(self.lowest & (place == self.at - 1))
            def _():
                near[rows.low : rows.low + rows.info] = ref[rows.map : rows.final]

            @pl.when(self.highest & (place == self.at + 1))
            def _():
                near[rows.high : rows.high + rows.info] = ref[rows.map : rows.final]
                rest = slice(0, rows.map) if final else slice(rows.final, rows.full)
                near[rows.high + rows.info : rows.near] = ref[rest]


def start_near(near, nx, nz):
    rows = Rows(nx)
    near[: rows.span] = jnp.ones((rows.span, nz), jnp.float32)
    near[rows.span :] = jnp.zeros((near.shape[0] - rows.span, nz), jnp.float32)


def join_kernel(radix, stride, final, nx, is_first, *refs):
    rows = Rows(nx)
    total, last_info, first_info, near_in = refs[:4]
    others, near, outs = refs[4 : 3 + radix], refs[3 + radix], refs[4 + radix :]
    nz = near.shape[1]
    if is_first:
        start_near(near, nx, nz)
    else:
        near[...] = near_in[...]
    group = Group(radix, stride, others, nx)
    own = [total[i * rows.span : (i + 1) * rows.span] for i in range(2)]
    ahead = group.ahead(near[: rows.span], near[rows.span : rows.map])
    write_rows(near, ahead)
    group.collect(near, False)
    whole = group.total(own)
    if final == 0:
        write_rows(outs[0], whole)
        return
    me, count = lax.axis_index("gy"), lax.axis_size("gy")
    for (senders, adjacent), out in zip(matchings(count, final, stride * radix), outs):
        up = look_up(senders) > me
        if not adjacent:
            write_rows(out, whole)
            continue

        @pl.when(up)
        def _():
            write_rows(out, whole)
            out[rows.map : rows.final] = last_info[: rows.info]

        @pl.when(jnp.logical_not(up))
        def _():
            out[: rows.map] = first_info[rows.info : rows.info + rows.rest]
            out[rows.map : rows.final] = first_info[: rows.info]


def full_message(nx, total, last_info, first_info, senders):
    rows = Rows(nx)
    onward = jnp.concatenate([total[: rows.map], last_info[: rows.info], first_info[rows.info : rows.info + rows.rest]])
    back = jnp.concatenate([total[: rows.map], first_info[: rows.info + rows.rest]])
    message = jnp.where(look_up(senders) > lax.axis_index("gy"), onward, back)
    return jnp.pad(message, ((0, -rows.full % 8), (0, 0)))


def third_kernel(radix, stride, *refs):
    st, extra, coarse, near_in = refs[:4]
    others, (out, sc, sc_b, wide, near, done, sems) = refs[4 : 3 + radix], refs[3 + radix :]
    planes, rows, ext, nz = st.shape
    ny, nx = rows - 2, ext - 2 * PAD
    edge = edge_weights((ext, nz))
    blocks = ny // 2

    lay = Rows(nx)
    span = lay.span
    near[...] = near_in[...]
    group = Group(radix, stride, others, nx)
    if radix > 1:
        group.collect(near, True)
    gas_in = group.ahead(near[:span], near[span : lay.map])[1]
    at_high = lay.high + lay.info
    starts = [lay.low, lay.low + span, lay.high, lay.high + span, at_high, at_high + span]
    for k, v in enumerate([gas_in] + [near[start : start + span] for start in starts]):
        wide[k, : PAD - 2] = jnp.zeros((PAD - 2, nz), jnp.float32)
        wide[k, ext - PAD + 2 :] = jnp.zeros((PAD - 2, nz), jnp.float32)
        wide[k, pl.ds(PAD - 2, span, 2), :] = v
        wide[k, pl.ds(PAD - 1, span, 2), :] = v
    for k, start in enumerate((lay.low, lay.low + nx + 2, lay.high, lay.high + nx + 2)):
        start += lay.map
        wide[7 + k, :PAD] = jnp.zeros((PAD, nz), jnp.float32)
        wide[7 + k, ext - PAD :] = jnp.zeros((PAD, nz), jnp.float32)
        wide[7 + k, PAD - 1 : PAD + nx + 1] = near[start : start + nx + 2]

    gas_in = wide[0]
    last = ny + 1
    solid_low = wide[1] + wide[2] * gas_in
    sc[0, 0] = st[SA, 0] + solid_low
    sc[1, 0] = st[GA, 0] + gas_in

    def correct(j, carry):
        gas = coarse[2, j] * gas_in + coarse[3, j]
        solid = coarse[0, j] + coarse[1, j] * gas
        for i in (2 * j + 1, 2 * j + 2):
            sc[0, i] = st[SA, i] + solid
            sc[1, i] = st[GA, i] + gas
        return carry

    lax.fori_loop(0, blocks, correct, 0)
    gas = coarse[2, blocks - 1] * gas_in + coarse[3, blocks - 1]
    gas_high = wide[5] * gas + wide[4]
    solid_high = wide[3] + wide[6] * gas_high
    sc[0, last] = st[SA, last] + solid_high
    sc[1, last] = st[GA, last] + gas_high

    view = Fields(st, sc, sc_b)
    for i, is_after, solid, gas in ((0, False, solid_low, gas_in), (last, True, solid_high, gas_high)):
        side = 3 if is_after else 0
        fy = extra[side + 2]
        to = 9 if is_after else 7
        rs = extra[side] + wide[to] + fy * solid
        rg = extra[side + 1] + wide[to + 1] + (CONDUCT if is_after else CONDUCT + FLOW) * gas
        res = outer_residual(view, i, SA, rs, rg, fy, edge, is_after)
        sc_b[0, i], sc_b[1, i] = relaxed(view, i, SA, *res)

    def sweep(i):
        new_s, new_g = relaxed(view, i, SA, *row_residual(view, i, SA, edge))
        return [(sc_b, (0, i), new_s), (sc_b, (1, i), new_g)]

    def final(i):
        new_s, new_g = last_relaxed(view, i, SB, edge, slice(PAD, PAD + nx))
        return [(done, (0, i - 1), new_s), (done, (1, i - 1), new_g)]

    def leaving(k):
        part = pl.ds(GROUP * k, GROUP)
        return pltpu.make_async_copy(done.at[:, part], out.at[:, part], sems.at[k])

    grouped(list(range(1, ny + 1)), sweep, GROUP)
    for k in range(ny // GROUP):
        grouped(list(range(GROUP * k + 1, GROUP * k + GROUP + 1)), final, GROUP)
        leaving(k).start()
    for k in range(ny // GROUP):
        leaving(k).wait()


class Fields:
    def __init__(self, st, first, second):
        self.st, self.first, self.second = st, first, second

    def __getitem__(self, at):
        if at[0] > GB:
            return self.st[at]
        return self.first[at] if at[0] <= GA else self.second[(at[0] - SB,) + at[1:]]


def cost(rows, cells):
    return pl.CostEstimate(flops=50 * rows * cells, bytes_accessed=16 * 4 * rows * cells, transcendentals=0)


def swap(x, axis, first):
    pairs = []
    for i in range(first, lax.axis_size(axis) - 1, 2):
        pairs += [(i, i + 1), (i + 1, i)]
    return lax.ppermute(x, axis, pairs)


def shards(temps, right_side, exchange, coupling):
    temps, right_side = (jnp.transpose(a, (0, 2, 1, 3)) for a in (temps, right_side))
    exchange, coupling = (jnp.transpose(a, (1, 0, 2)) for a in (exchange, coupling))
    temps, right_side, exchange, coupling = (
        pltpu.with_memory_space_constraint(a, pltpu.HBM) for a in (temps, right_side, exchange, coupling)
    )
    ny, nx, nz = exchange.shape
    ext = nx + 2 * PAD
    f32 = functools.partial(jax.ShapeDtypeStruct, dtype=jnp.float32)

    strip = f32((strip_height(ny), nz))
    state = f32((PLANES, ny + 2, ext, nz))
    one, two, early, st = pl.pallas_call(
        pack_kernel,
        out_shape=(strip, strip, f32((EARLY, nx, nz)), state),
        in_specs=[HBM] * 4,
        out_specs=(VMEM,) * 4,
        scratch_shapes=[pltpu.SemaphoreType.DMA((6,))],
        compiler_params=PARAMS,
        name="pack_x",
    )(temps, right_side, exchange, coupling)
    one, two = swap(one, "gx", 0), swap(two, "gx", 1)
    early = swap(early, "gy", 1)

    def letter(planes):
        return f32((planes, ext - 2 * CROP, nz))

    st = pl.pallas_call(
        conduct_kernel,
        out_shape=state,
        in_specs=[VMEM],
        out_specs=VMEM,
        input_output_aliases={0: 0},
        compiler_params=PARAMS,
        cost_estimate=cost(2 * ny, ext * nz),
        name="conduct",
    )(st)
    st, across = pl.pallas_call(
        first_kernel,
        out_shape=(state, f32((across_parts(ext)[1], nz))),
        in_specs=[VMEM] * 3,
        out_specs=(VMEM,) * 2,
        input_output_aliases={0: 0},
        compiler_params=PARAMS,
        name="first",
    )(st, one, two)
    st, *beside = pl.pallas_call(
        other_kernel,
        out_shape=(state,) + (letter(THIRD),) * (MESSAGE // THIRD),
        in_specs=[VMEM] * 3,
        out_specs=(VMEM,) * (1 + MESSAGE // THIRD),
        input_output_aliases={0: 0},
        compiler_params=PARAMS,
        name="other",
    )(st, one, two)
    across = swap(across, "gy", 1)

    rows = f32((4, ny // 2, ext, nz))
    st, coarse = pl.pallas_call(
        inner_kernel,
        out_shape=(state, rows),
        in_specs=[VMEM] * 2,
        out_specs=(VMEM,) * 2,
        input_output_aliases={0: 0},
        compiler_params=PARAMS,
        cost_estimate=cost(4 * ny, ext * nz),
        name="inner",
    )(st, early)

    beside = [swap(part, "gy", 0) for part in beside]

    lay = Rows(nx)

    def tall(height):
        return f32(((height + 7) // 8 * 8, nz))

    letter_room = pltpu.VMEM((MESSAGE, ext, nz), jnp.float32)
    more = f32((6, ext, nz))
    st, coarse, extra = pl.pallas_call(
        near_kernel,
        out_shape=(state, rows, more),
        in_specs=[VMEM] * (2 + len(beside)),
        out_specs=(VMEM,) * 3,
        scratch_shapes=[letter_room],
        input_output_aliases={0: 0, 1: 1},
        compiler_params=PARAMS,
        name="near",
    )(st, coarse, *beside)
    st, coarse, extra, total, last_info, first_info, message = pl.pallas_call(
        second_kernel,
        out_shape=(state, rows, more, tall(lay.map), tall(lay.info), tall(lay.info + lay.rest), tall(lay.full)),
        in_specs=[VMEM] * 5,
        out_specs=(VMEM,) * 7,
        scratch_shapes=[letter_room, pltpu.VMEM((8, ext, nz), jnp.float32)],
        input_output_aliases={0: 0, 1: 1, 2: 2},
        compiler_params=PARAMS,
        name="second",
    )(st, coarse, extra, early, across)

    near, messages = total, [message]
    count = lax.axis_size("gy")
    radices, stride = stages(count), 1
    for place, radix in enumerate(radices[:-1]):
        swaps = matchings(count, radix, stride)
        if place:
            messages = [full_message(nx, total, last_info, first_info, senders) for senders, _ in swaps]
        others = exchange_stage(messages, swaps)
        final = radices[-1] if place == len(radices) - 2 else 0
        following = matchings(count, final, stride * radix) if final else []
        outs = [tall(lay.final if adjacent else lay.map) for _, adjacent in following] if final else [tall(lay.map)]
        near, *messages = pl.pallas_call(
            functools.partial(join_kernel, radix, stride, final, nx, place == 0),
            out_shape=(tall(lay.near), *outs),
            in_specs=[VMEM] * (3 + radix),
            out_specs=(VMEM,) * (1 + len(outs)),
            compiler_params=PARAMS,
            name="join",
        )(total, last_info, first_info, near, *others)
        total = total if final else messages[0]
        stride *= radix
    got = exchange_stage(messages, matchings(count, radices[-1], stride))

    out = pl.pallas_call(
        functools.partial(third_kernel, radices[-1], stride),
        out_shape=f32((2, ny, nx, nz)),
        in_specs=[VMEM] * (4 + len(got)),
        out_specs=HBM,
        scratch_shapes=[
            pltpu.VMEM((2, ny + 2, ext, nz), jnp.float32),
            pltpu.VMEM((2, ny + 2, ext, nz), jnp.float32),
            pltpu.VMEM((11, ext, nz), jnp.float32),
            pltpu.VMEM(tall(lay.near).shape, jnp.float32),
            pltpu.VMEM((2, ny, nx, nz), jnp.float32),
            pltpu.SemaphoreType.DMA((ny // GROUP,)),
        ],
        compiler_params=PARAMS,
        name="third",
    )(st, extra, coarse, near, *got)
    return jnp.transpose(out, (0, 2, 1, 3))


def solution(mesh):
    return jax.shard_map(
        shards,
        mesh=mesh,
        in_specs=(
            P(None, "gx", "gy", None),
            P(None, "gx", "gy", None),
            P("gx", "gy", None),
            P("gx", "gy", None),
        ),
        out_specs=P(None, "gx", "gy", None),
        check_vma=False,
    )
```

```python
import functools

import jax
import jax.numpy as jnp
from jax import lax
from jax.experimental import pallas as pl
from jax.experimental.pallas import tpu as pltpu
from jax.sharding import PartitionSpec as P

SOLID_CAP, GAS_CAP, FLOW, CONDUCT, RELAX, LUMP = 0.5, 0.02, 40.0, 0.05, 0.8, 0.25
GAS_SELF = GAS_CAP + 4.5 * CONDUCT

PAD = 8
WX = 5
CROP = 4
(SA, GA, SB, GB, K, C, RS, RG, FX, FZ, H, FY, ASS, ASG, AGG) = range(15)
PLANES = 15
(M_S, M_G, M_K, M_C, M_FY, M_1S, M_1G, M_2S, M_2G) = range(9)
MESSAGE, EARLY, THIRD = 9, 7, 3

GROUP = 6

VMEM = pl.BlockSpec(memory_space=pltpu.VMEM)
HBM = pl.BlockSpec(memory_space=pltpu.HBM)
PARAMS = pltpu.CompilerParams(vmem_limit_bytes=40 * 1024 * 1024)


def up_x(v):
    return pltpu.roll(v, v.shape[0] - 1, 0)


def down_x(v):
    return pltpu.roll(v, 1, 0)


def up_z(v):
    return pltpu.roll(v, v.shape[1] - 1, 1)


def down_z(v):
    return pltpu.roll(v, 1, 1)


def lanes(shape):
    return lax.broadcasted_iota(jnp.int32, shape, 1)


def x_mask(shape, nx):
    row = lax.broadcasted_iota(jnp.int32, shape, 0)
    place, count = lax.axis_index("gx"), lax.axis_size("gx")
    low = jnp.where(place == 0, PAD, PAD - WX)
    high = jnp.where(place == count - 1, PAD + nx, PAD + nx + WX)
    return jnp.where((row >= low) & (row < high), 1.0, 0.0).astype(jnp.float32)


PAIRS = ((SA, GA), (C, RS), (RG, K))
STRIP_ROWS = 8 * len(PAIRS)


def strip_height(ny):
    return ny * STRIP_ROWS + (ny + 7) // 8 * 8


def strip_tile(y, p):
    return pl.ds(pl.multiple_of(y * STRIP_ROWS + 8 * p, 8), 8)


def sublanes(nz):
    return lax.broadcasted_iota(jnp.int32, (8, nz), 0)


def conductivity_of(s, exchange):
    return 1.0 + 4.0 * exchange * s * s * s


def strip_side(s, g, k, rs, rg, c, low):
    row = sublanes(s.shape[1])
    inn, shift = (3, 7) if low else (4, 1)
    k_out, s_out, g_out = (pltpu.roll(v, shift, 0) for v in (k, s, g))
    rs = rs + jnp.where(row == inn, 0.5 * (k + k_out) * s_out, 0.0)
    rg = rg + jnp.where(row == inn, CONDUCT * g_out, 0.0)
    values = {SA: s, GA: g, K: k, RS: rs, RG: rg, C: c}
    tiles = []
    for a, b in PAIRS:
        a, b = values[a], values[b]
        a, b = (a, pltpu.roll(b, 4, 0)) if low else (pltpu.roll(a, 4, 0), b)
        tiles.append(jnp.where(row < 4, a, b))
    return tiles, (k[4:5] if low else k[3:4])


def pack_kernel(temps, right, exchange, coupling, one, two, early, st, sems):
    even = lax.axis_index("gx") % 2 == 0
    odd = lax.axis_index("gy") % 2 == 1
    ny, nx, nz = exchange.shape
    copies = []
    for k, (plane, ref) in enumerate(
        ((SA, temps.at[0]), (K, exchange), (GA, temps.at[1]), (C, coupling), (RS, right.at[0]), (RG, right.at[1]))
    ):
        to = st.at[plane, pl.ds(1, ny), pl.ds(PAD, nx)]
        copies.append(pltpu.make_async_copy(ref, to, sems.at[k]))
    for copy in copies:
        copy.start()
    for copy in copies:
        copy.wait()

    def row(y, carry):
        sides = []
        for start in (PAD, PAD + nx - 8):
            s, g, e, rs, rg, c = (st[plane, y + 1, start : start + 8] for plane in (SA, GA, K, RS, RG, C))
            sides.append(strip_side(s, g, conductivity_of(s, e), rs, rg, c, start == PAD))
        (low, low_k), (high, high_k) = sides
        for p in range(len(PAIRS)):
            part = strip_tile(y, p)
            one[part] = jnp.where(even, high[p], low[p])
            two[part] = jnp.where(even, low[p], high[p])
        part = pl.ds(ny * STRIP_ROWS + y, 1)
        one[part] = jnp.where(even, high_k, low_k)
        two[part] = jnp.where(even, low_k, high_k)
        return carry

    lax.fori_loop(0, ny, row, 0, unroll=2)
    own = slice(PAD, PAD + nx)
    for is_odd, e, d in ((True, ny, ny - 1), (False, 1, 2)):

        @pl.when(odd == is_odd)
        def _():
            s, s_d, g, g_d = st[SA, e, own], st[SA, d, own], st[GA, e, own], st[GA, d, own]
            c, k, k_d = st[C, e, own], conductivity_of(s, st[K, e, own]), conductivity_of(s_d, st[K, d, own])
            fx, fz, h, _ = faces(k)
            fy = 0.5 * (k + k_d)
            part_s, part_g = inner(s, g, c, h, fx, fz, edge_weights((nx, nz)))
            m_1s, m_1g = first_partial(st[RS, e, own] + part_s, st[RG, e, own] + part_g, s, s_d, g, g_d, fy, is_odd)
            for plane, value in enumerate((s, g, k, c, fy, m_1s, m_1g)):
                early[plane] = value


def conduct_kernel(st_in, st):
    del st_in
    planes, rows, ext, nz = st.shape
    own = slice(PAD, ext - PAD)
    for i in range(1, rows - 1):
        st[K, i, own] = conductivity_of(st[SA, i, own], st[K, i, own])


def place_halo(st, one, two, y, nx):
    even = lax.axis_index("gx") % 2 == 0
    ny, row = st.shape[1] - 2, sublanes(st.shape[3])
    i = y + 1

    def received(part):
        a, b = one[part], two[part]
        return jnp.where(even, b, a), jnp.where(even, a, b)

    for p, (plane_a, plane_b) in enumerate(PAIRS):
        before, after = received(strip_tile(y, p))
        before = {plane_a: pltpu.roll(before, 4, 0), plane_b: before}
        after = {plane_a: after, plane_b: pltpu.roll(after, 4, 0)}
        for plane in (plane_a, plane_b):
            low, high = jnp.where(row >= 4, before[plane], 0.0), jnp.where(row < 4, after[plane], 0.0)
            if plane == K:
                k_low, k_high = received(pl.ds(ny * STRIP_ROWS + y, 1))
                low, high = jnp.where(row == 3, k_low, low), jnp.where(row == 4, k_high, high)
            st[plane, i, :PAD] = low
            st[plane, i, PAD + nx :] = high


def inner(s, g, c, h, fx, fz, edge):
    t = c * (s - g)
    flux_x = fx * (up_x(s) - s)
    flux_z = fz * (up_z(s) - s)
    part_s = (flux_x - down_x(flux_x)) + (flux_z - down_z(flux_z)) - h * s - t
    part_g = (
        t
        - GAS_SELF * g
        + CONDUCT * (up_x(g) + down_x(g))
        + edge[0] * up_z(g)
        + edge[1] * down_z(g)
    )
    return part_s, part_g


def edge_weights(shape):
    lane = lanes(shape)
    weight = jnp.float32(0.25 * CONDUCT)
    return jnp.where(lane == shape[1] - 1, 0.0, weight), jnp.where(lane == 0, 0.0, weight)


def row_inner(st, i, s_at, edge):
    return inner(st[s_at, i], st[s_at + 1, i], st[C, i], st[H, i], st[FX, i], st[FZ, i], edge)


def row_residual(st, i, s_at, edge):
    part_s, part_g = row_inner(st, i, s_at, edge)
    s, g, before = st[s_at, i], st[s_at + 1, i], st[s_at + 1, i - 1]
    part_s += st[FY, i] * (st[s_at, i + 1] - s) + st[FY, i - 1] * (st[s_at, i - 1] - s)
    part_g += CONDUCT * (st[s_at + 1, i + 1] + before) - FLOW * (g - before)
    return st[RS, i] + part_s, st[RG, i] + part_g


def relaxed(st, i, s_at, res_s, res_g):
    s = st[s_at, i] + st[ASS, i] * res_s + st[ASG, i] * res_g
    g = st[s_at + 1, i] + st[ASG, i] * res_s + st[AGG, i] * res_g
    return s, g


def faces(k):
    lane = lanes(k.shape)
    end = k.shape[1] - 1
    fx = 0.5 * (k + up_x(k))
    fz = jnp.where(lane == end, 0.0, 0.125 * (k + up_z(k)))
    h = SOLID_CAP + jnp.where((lane == 0) | (lane == end), 0.125 * k, 0.0)
    return fx, fz, h, h + (fx + down_x(fx)) + (fz + down_z(fz))


def inverse(diag, c, mask):
    gas_diag = (GAS_SELF + FLOW) + c
    inv = (RELAX * mask) / (diag * gas_diag - c * c)
    return inv * gas_diag, inv * c, inv * diag


def last_relaxed(st, i, s_at, edge, own):
    full_s, full_g = st[s_at, i], st[s_at + 1, i]
    s, g = full_s[own], full_g[own]
    flux_x = st[FX, i] * (up_x(full_s) - full_s)
    flux_z = st[FZ, i, own] * (up_z(s) - s)
    c, before = st[C, i, own], st[s_at + 1, i - 1, own]
    t = c * (s - g)
    res_s = st[RS, i, own] + (flux_x[own] - down_x(flux_x)[own]) + (flux_z - down_z(flux_z)) - st[H, i, own] * s - t
    res_s += st[FY, i, own] * (st[s_at, i + 1, own] - s) + st[FY, i - 1, own] * (st[s_at, i - 1, own] - s)
    res_g = st[RG, i, own] + t - GAS_SELF * g + edge[0][own] * up_z(g) + edge[1][own] * down_z(g)
    res_g += CONDUCT * (up_x(full_g)[own] + down_x(full_g)[own] + st[s_at + 1, i + 1, own] + before) - FLOW * (g - before)
    ss, sg, gg = st[ASS, i, own], st[ASG, i, own], st[AGG, i, own]
    return s + ss * res_s + sg * res_g, g + sg * res_s + gg * res_g


def grouped(rows, work):
    for start in range(0, len(rows), GROUP):
        stores = []
        for i in rows[start : start + GROUP]:
            stores += work(i)
        for ref, at, value in stores:
            ref[at] = value


def looped(first, last, size, work):
    def group(k, carry):
        grouped([first + size * k + r for r in range(size)], work)
        return carry

    lax.fori_loop(0, (last - first) // size, group, 0)
    grouped(list(range(last - (last - first) % size, last)), work)


def row_coefficients(st, i, mask):
    fx, fz, h, diag = faces(st[K, i])
    fy = 0.5 * (st[K, i] + st[K, i + 1])
    before = 0.5 * (st[K, i] + st[K, i - 1])
    ss, sg, gg = inverse(diag + st[C, i] + fy + before, st[C, i], mask)
    values = ((FX, fx), (FZ, fz), (H, h), (FY, fy), (ASS, ss), (ASG, sg), (AGG, gg))
    return [(st, (plane, i), v) for plane, v in values]


def row_sweep(st, i, source, target, edge):
    s, g = relaxed(st, i, source, *row_residual(st, i, source, edge))
    return [(st, (target, i), s), (st, (target + 1, i), g)]


def first_partial(res_s, res_g, s, s_d, g, g_d, fy, onward):
    return res_s + fy * (s_d - s), res_g + CONDUCT * g_d - FLOW * (g - g_d if onward else g)


def send_planes(st, onward, edge):
    ny = st.shape[1] - 2
    e, d, near = (ny, ny - 1, ny - 1) if onward else (1, 2, 1)
    fy, s, g, g_d = st[FY, near], st[SA, e], st[GA, e], st[GA, d]
    part_s, part_g = row_inner(st, e, SA, edge)
    m_1s, m_1g = first_partial(st[RS, e] + part_s, st[RG, e] + part_g, s, st[SA, d], g, g_d, fy, onward)
    m_2s = st[RS, e] + fy * st[SB, d]
    m_2g = st[RG, e] + (CONDUCT + FLOW if onward else CONDUCT) * st[GB, d]
    return [s, g, st[K, e], st[C, e], fy, m_1s, m_1g, m_2s, m_2g]


def across_parts(ext):
    parts, at = [], 0
    for k in range(EARLY, MESSAGE):
        parts.append((k, CROP, ext - CROP, at))
        at += ext - 2 * CROP
    for k in range(EARLY):
        more = 1 if k in (M_1S, M_1G) else 0
        for low, high in ((CROP, PAD + more), (ext - PAD - more, ext - CROP)):
            parts.append((k, low, high, at))
            at += high - low
    return parts, (at + 7) // 8 * 8


def write_across(ref, k, value):
    for plane, low, high, at in across_parts(value.shape[0])[0]:
        if plane == k:
            ref[at : at + high - low] = value[low:high]


def read_across(early, across, outer, k):
    ext = outer.shape[1]
    if k < EARLY:
        outer[k, PAD : ext - PAD] = early[k]
    for plane, low, high, at in across_parts(ext)[0]:
        if plane == k:
            outer[k, low:high] = across[at : at + high - low]


def write_beside(refs, k, value):
    refs[k // THIRD][k % THIRD] = value[CROP : value.shape[0] - CROP]


def read_beside(refs, outer, k):
    outer[k, CROP : outer.shape[1] - CROP] = refs[k // THIRD][k % THIRD]


def first_end(st, one, two, after, write):
    planes, rows, ext, nz = st.shape
    ny, nx = rows - 2, ext - 2 * PAD
    mask = x_mask((ext, nz), nx)
    edge = edge_weights((ext, nz))
    e, d, f = (ny, ny - 1, ny - 2) if after else (1, 2, 3)
    for i in (e, d, f):
        place_halo(st, one, two, i - 1, nx)
    fx, fz, h, diag = faces(st[K, e])
    st[FX, e], st[FZ, e], st[H, e] = fx, fz, h
    st[FY, min(e, d)] = 0.5 * (st[K, e] + st[K, d])
    st[FY, min(d, f)] = 0.5 * (st[K, d] + st[K, f])
    grouped([d], lambda i: row_coefficients(st, i, mask))
    grouped([d], lambda i: row_sweep(st, i, SA, SB, edge))
    for k, value in enumerate(send_planes(st, after, edge)):
        write(k, value)


def either_first(st, one, two, after, write):
    for is_after in (True, False):

        @pl.when(after == is_after)
        def _():
            first_end(st, one, two, is_after, write)


def first_kernel(st_in, one, two, st, across):
    del st_in
    either_first(st, one, two, lax.axis_index("gy") % 2 == 1, functools.partial(write_across, across))


def other_kernel(st_in, one, two, st, *beside):
    del st_in
    either_first(st, one, two, lax.axis_index("gy") % 2 == 0, functools.partial(write_beside, beside))
    planes, rows, ext, nz = st.shape
    ny, nx = rows - 2, ext - 2 * PAD
    mask = x_mask((ext, nz), nx)

    def halo(y, carry):
        place_halo(st, one, two, y, nx)
        return carry

    lax.fori_loop(3, ny - 3, halo, 0, unroll=2)
    looped(3, ny - 1, 4, lambda i: row_coefficients(st, i, mask))


def outer_residual(st, i, s_at, rs, rg, fy_out, edge, after):
    part_s, part_g = row_inner(st, i, s_at, edge)
    s, g = st[s_at, i], st[s_at + 1, i]
    if after:
        part_s += st[FY, i - 1] * (st[s_at, i - 1] - s)
        part_g += (CONDUCT + FLOW) * st[s_at + 1, i - 1]
    else:
        part_s += st[FY, i] * (st[s_at, i + 1] - s)
        part_g += CONDUCT * st[s_at + 1, i + 1]
    return rs + part_s - fy_out * s, rg + part_g - FLOW * g


def pair_x(v):
    row = lax.broadcasted_iota(jnp.int32, v.shape, 0)
    return v + jnp.where(row % 2 == 0, up_x(v), down_x(v))


def coarse_coefficients(c_sum, k_sum):
    per_solid = 1.0 / (4.0 * SOLID_CAP + c_sum + LUMP * k_sum)
    ratio = c_sum * per_solid
    return per_solid, ratio, 1.0 / ((4.0 * GAS_CAP + 2.0 * FLOW) + c_sum - c_sum * ratio)


def coarse_row(st, coarse, j, mask, edge):
    i = 2 * j + 1
    res_s, res_g = row_residual(st, i, SA, edge)
    more_s, more_g = row_residual(st, i + 1, SA, edge)
    res_s, res_g = pair_x((res_s + more_s) * mask), pair_x((res_g + more_g) * mask)
    c_sum = pair_x(st[C, i] + st[C, i + 1])
    per_solid, ratio, per_gas = coarse_coefficients(c_sum, pair_x(st[K, i] + st[K, i + 1]))
    lead = res_s * per_solid
    values = (lead, ratio, (2.0 * FLOW) * per_gas, (res_g + c_sum * lead) * per_gas)
    return [(coarse, (k, j), v) for k, v in enumerate(values)]


def inner_kernel(st_in, early, st, coarse):
    del st_in, early
    planes, rows, ext, nz = st.shape
    ny, nx = rows - 2, ext - 2 * PAD
    shape = (ext, nz)
    mask = x_mask(shape, nx)
    edge = edge_weights(shape)
    looped(3, ny - 1, 4, lambda i: row_sweep(st, i, SA, SB, edge))
    looped(3, ny - 1, 4, lambda i: row_sweep(st, i, SB, SA, edge))
    looped(2, ny // 2 - 2, 1, lambda j: coarse_row(st, coarse, j, mask, edge))


def end_work(st, coarse, extra, read, outer, is_after):
    planes, rows, ext, nz = st.shape
    ny, nx = rows - 2, ext - 2 * PAD
    me, count = lax.axis_index("gy"), lax.axis_size("gy")
    mask = x_mask((ext, nz), nx)
    inside = jnp.where(me == (count - 1 if is_after else 0), 0.0, mask)
    edge = edge_weights((ext, nz))
    zeros = jnp.zeros((PAD, nz), jnp.float32)
    for k in range(MESSAGE):
        outer[k, :PAD] = zeros
        outer[k, ext - PAD :] = zeros
        read(outer, k)

    o, e, near = (ny + 1, ny, ny) if is_after else (0, 1, 0)
    to_o = CONDUCT + FLOW if is_after else CONDUCT
    s_o, g_o, k_o, c_o, fy_out = (outer[plane] for plane in (M_S, M_G, M_K, M_C, M_FY))
    fy = 0.5 * (k_o + st[K, e])
    fx, fz, h, diag = faces(k_o)
    inv_o = inverse(diag + c_o + fy_out + fy, c_o, inside)
    fx_e, fz_e = st[FX, e], st[FZ, e]
    diag = st[H, e] + (fx_e + down_x(fx_e)) + (fz_e + down_z(fz_e)) + st[C, e] + fy
    inv_e = inverse(diag + st[FY, near - 1 if is_after else near + 1], st[C, e], mask)
    for plane, value in ((SA, s_o), (GA, g_o), (K, k_o), (C, c_o), (FX, fx), (FZ, fz), (H, h)):
        st[plane, o] = value
    st[FY, near] = fy
    for k in range(3):
        st[ASS + k, o], st[ASS + k, e] = inv_o[k], inv_e[k]

    res = outer[M_1S] + fy * (st[SA, e] - s_o), outer[M_1G] + to_o * st[GA, e]
    new_o = relaxed(st, o, SA, *res)
    stores = row_sweep(st, e, SA, SB, edge)
    st[SB, o], st[GB, o] = new_o
    for ref, at, value in stores:
        ref[at] = value
    res = outer_residual(st, o, SB, outer[M_2S], outer[M_2G], fy_out, edge, is_after)
    new_o = relaxed(st, o, SB, *res)
    ends = [e - 1, e] if is_after else [e, e + 1]
    grouped(ends, lambda i: row_sweep(st, i, SB, SA, edge))
    st[SA, o], st[GA, o] = new_o
    for k, plane in enumerate((M_2S, M_2G, M_FY)):
        extra[(3 if is_after else 0) + k] = outer[plane]
    blocks = ny // 2
    at = blocks - 2 if is_after else 0
    looped(at, at + 2, 1, lambda j: coarse_row(st, coarse, j, mask, edge))


def either_end(after, st, coarse, extra, read, outer):
    for is_after in (True, False):

        @pl.when(after == is_after)
        def _():
            end_work(st, coarse, extra, read, outer, is_after)


def near_kernel(st_in, coarse_in, *refs):
    beside, (st, coarse, extra, outer) = refs[:-4], refs[-4:]
    del st_in, coarse_in
    either_end(lax.axis_index("gy") % 2 == 0, st, coarse, extra, functools.partial(read_beside, beside), outer)


def second_kernel(st_in, coarse_in, extra_in, early, across, *refs):
    st, coarse, extra, total, last_info, first_info, message, outer, squeeze = refs
    del st_in, coarse_in, extra_in
    planes, rows, ext, nz = st.shape
    ny, nx = rows - 2, ext - 2 * PAD
    me = lax.axis_index("gy")
    either_end(me % 2 == 1, st, coarse, extra, functools.partial(read_across, early, across), outer)

    blocks = ny // 2
    for k in range(4):
        squeeze[k] = coarse[k, 0]
    slopes, offsets = coarse[2, 0], coarse[3, 0]
    for j in range(1, blocks):
        slope = coarse[2, j]
        slopes, offsets = slope * slopes, slope * offsets + coarse[3, j]
        coarse[2, j], coarse[3, j] = slopes, offsets
    squeeze[4], squeeze[5], squeeze[6], squeeze[7] = slopes, offsets, coarse[0, blocks - 1], coarse[1, blocks - 1]

    span = nx // 2 + 2
    lead, ratio, slope, offset, slopes, offsets, lead_last, ratio_last = (
        squeeze[k, pl.ds(PAD - 2, span, 2), :] for k in range(8)
    )
    part = slice(PAD - 1, PAD + nx + 1)

    def increments(d, face, gas):
        return [(st[FY, face] * (st[SA, d] - st[SB, d]))[part], (gas * (st[GA, d] - st[GB, d]))[part]]

    onward = [lead_last, ratio_last] + increments(ny - 1, ny - 1, CONDUCT + FLOW)
    back = [lead, offset] + increments(2, 1, CONDUCT) + [slope, ratio]
    write_rows(total, [slopes, offsets])
    write_rows(last_info, onward)
    write_rows(first_info, back)
    for go, info in ((True, onward), (False, back)):

        @pl.when((me % 2 == 0) == go)
        def _():
            write_rows(message, [slopes, offsets] + info)


def write_rows(ref, values):
    at = 0
    for value in values:
        ref[at : at + value.shape[0]] = value
        at += value.shape[0]


class Rows:
    def __init__(self, nx):
        self.span = nx // 2 + 2
        self.map = 2 * self.span
        self.info = self.map + 2 * (nx + 2)
        self.rest = self.map
        self.final = self.map + self.info
        self.full = self.final + self.rest
        self.low = self.map
        self.high = self.low + self.info
        self.near = self.high + self.info + self.rest


def source(at, k, radix):
    if radix & (radix - 1) == 0:
        return at ^ k
    return (at + radix - k) % radix


def matchings(count, radix, stride):
    if (count, radix, stride) == (8, 4, 2):
        swaps = ((1, 2), (3, 4), (5, 6), (0, 7)), ((0, 3), (1, 5), (2, 6), (4, 7)), ((0, 4), (1, 6), (2, 5), (3, 7))
        out = []
        for pairs in swaps:
            senders = [0] * count
            for a, b in pairs:
                senders[a], senders[b] = b, a
            out.append((senders, len(out) == 0))
        return out
    out = []
    for k in range(1, radix):
        senders = []
        for me in range(count):
            at, low = me // stride % radix, me % stride
            senders.append(me - low + (source(at, k, radix) - at) * stride + (stride - 1 - low))
        out.append((senders, any(abs(source(at, k, radix) - at) == 1 for at in range(radix))))
    return sorted(out, key=lambda item: not item[1])


def look_up(table):
    me, value = lax.axis_index("gy"), jnp.int32(table[0])
    for k in range(1, len(table)):
        value = jnp.where(me == k, table[k], value)
    return value


def stages(count):
    if count % 2:
        return [1, count]
    out, rest = [2], count // 2
    while rest > 1:
        radix = next((r for r in (8, 4, 2) if rest % r == 0), rest)
        out.append(radix)
        rest //= radix
    return out if len(out) > 1 else out + [1]


def exchange_stage(messages, swaps):
    return [
        lax.ppermute(message, "gy", [(sender, me) for me, sender in enumerate(senders)])
        for (senders, near), message in zip(swaps, messages)
    ]


class Group:
    def __init__(self, radix, stride, others, nx):
        self.radix, self.others, self.nx = radix, others, nx
        me = lax.axis_index("gy")
        self.swaps = [
            (look_up([sender // stride % radix for sender in senders]), near)
            for senders, near in matchings(lax.axis_size("gy"), radix, stride)
        ]
        self.at = lax.rem(lax.div(me, stride), radix)
        low = lax.rem(me, stride)
        self.lowest, self.highest = low == 0, low == stride - 1

    def map_of(self, place, own):
        rows = Rows(self.nx)
        out = own
        for (sender, near), ref in zip(self.swaps, self.others):
            here = sender == place
            got = [ref[i * rows.span : (i + 1) * rows.span] for i in range(2)]
            out = got if out is None else [jnp.where(here, new, old) for new, old in zip(got, out)]
        return out

    def ahead(self, slope, offset):
        a, b = jnp.ones_like(slope), jnp.zeros_like(slope)
        for place in range(self.radix - 1):
            new_a, new_b = self.map_of(place, None)
            below = place < self.at
            a, b = jnp.where(below, new_a * a, a), jnp.where(below, new_a * b + new_b, b)
        return slope * a, slope * b + offset

    def total(self, own):
        a, b = self.map_of(0, own)
        for place in range(1, self.radix):
            new_a, new_b = self.map_of(place, own)
            a, b = new_a * a, new_a * b + new_b
        return a, b

    def collect(self, near, final):
        rows = Rows(self.nx)
        for (place, adjacent), ref in zip(self.swaps, self.others):
            if not adjacent:
                continue

            @pl.when(self.lowest & (place == self.at - 1))
            def _():
                near[rows.low : rows.low + rows.info] = ref[rows.map : rows.final]

            @pl.when(self.highest & (place == self.at + 1))
            def _():
                near[rows.high : rows.high + rows.info] = ref[rows.map : rows.final]
                rest = slice(0, rows.map) if final else slice(rows.final, rows.full)
                near[rows.high + rows.info : rows.near] = ref[rest]


def start_near(near, nx, nz):
    rows = Rows(nx)
    near[: rows.span] = jnp.ones((rows.span, nz), jnp.float32)
    near[rows.span :] = jnp.zeros((near.shape[0] - rows.span, nz), jnp.float32)


def join_kernel(radix, stride, final, nx, is_first, *refs):
    rows = Rows(nx)
    total, last_info, first_info, near_in = refs[:4]
    others, near, outs = refs[4 : 3 + radix], refs[3 + radix], refs[4 + radix :]
    nz = near.shape[1]
    if is_first:
        start_near(near, nx, nz)
    else:
        near[...] = near_in[...]
    group = Group(radix, stride, others, nx)
    own = [total[i * rows.span : (i + 1) * rows.span] for i in range(2)]
    ahead = group.ahead(near[: rows.span], near[rows.span : rows.map])
    write_rows(near, ahead)
    group.collect(near, False)
    whole = group.total(own)
    if final == 0:
        write_rows(outs[0], whole)
        return
    me, count = lax.axis_index("gy"), lax.axis_size("gy")
    for (senders, adjacent), out in zip(matchings(count, final, stride * radix), outs):
        up = look_up(senders) > me
        if not adjacent:
            write_rows(out, whole)
            continue

        @pl.when(up)
        def _():
            write_rows(out, whole)
            out[rows.map : rows.final] = last_info[: rows.info]

        @pl.when(jnp.logical_not(up))
        def _():
            out[: rows.map] = first_info[rows.info : rows.info + rows.rest]
            out[rows.map : rows.final] = first_info[: rows.info]


def full_message(nx, total, last_info, first_info, senders):
    rows = Rows(nx)
    onward = jnp.concatenate([total[: rows.map], last_info[: rows.info], first_info[rows.info : rows.info + rows.rest]])
    back = jnp.concatenate([total[: rows.map], first_info[: rows.info + rows.rest]])
    message = jnp.where(look_up(senders) > lax.axis_index("gy"), onward, back)
    return jnp.pad(message, ((0, -rows.full % 8), (0, 0)))


def third_kernel(radix, stride, *refs):
    st, extra, coarse, near_in = refs[:4]
    others, (out, sc, wide, near, done, sems) = refs[4 : 3 + radix], refs[3 + radix :]
    planes, rows, ext, nz = st.shape
    ny, nx = rows - 2, ext - 2 * PAD
    edge = edge_weights((ext, nz))
    blocks = ny // 2

    lay = Rows(nx)
    span = lay.span
    near[...] = near_in[...]
    group = Group(radix, stride, others, nx)
    if radix > 1:
        group.collect(near, True)
    gas_in = group.ahead(near[:span], near[span : lay.map])[1]
    at_high = lay.high + lay.info
    starts = [lay.low, lay.low + span, lay.high, lay.high + span, at_high, at_high + span]
    for k, v in enumerate([gas_in] + [near[start : start + span] for start in starts]):
        wide[k, : PAD - 2] = jnp.zeros((PAD - 2, nz), jnp.float32)
        wide[k, ext - PAD + 2 :] = jnp.zeros((PAD - 2, nz), jnp.float32)
        wide[k, pl.ds(PAD - 2, span, 2), :] = v
        wide[k, pl.ds(PAD - 1, span, 2), :] = v
    for k, start in enumerate((lay.low, lay.low + nx + 2, lay.high, lay.high + nx + 2)):
        start += lay.map
        wide[7 + k, :PAD] = jnp.zeros((PAD, nz), jnp.float32)
        wide[7 + k, ext - PAD :] = jnp.zeros((PAD, nz), jnp.float32)
        wide[7 + k, PAD - 1 : PAD + nx + 1] = near[start : start + nx + 2]

    gas_in = wide[0]
    last = ny + 1
    solid_low = wide[1] + wide[2] * gas_in
    sc[0, 0] = st[SA, 0] + solid_low
    sc[1, 0] = st[GA, 0] + gas_in

    def correct(j, carry):
        gas = coarse[2, j] * gas_in + coarse[3, j]
        solid = coarse[0, j] + coarse[1, j] * gas
        for i in (2 * j + 1, 2 * j + 2):
            sc[0, i] = st[SA, i] + solid
            sc[1, i] = st[GA, i] + gas
        return carry

    lax.fori_loop(0, blocks, correct, 0)
    gas = coarse[2, blocks - 1] * gas_in + coarse[3, blocks - 1]
    gas_high = wide[5] * gas + wide[4]
    solid_high = wide[3] + wide[6] * gas_high
    sc[0, last] = st[SA, last] + solid_high
    sc[1, last] = st[GA, last] + gas_high

    view = Fields(st, sc)
    for i, is_after, solid, gas in ((0, False, solid_low, gas_in), (last, True, solid_high, gas_high)):
        side = 3 if is_after else 0
        fy = extra[side + 2]
        to = 9 if is_after else 7
        rs = extra[side] + wide[to] + fy * solid
        rg = extra[side + 1] + wide[to + 1] + (CONDUCT if is_after else CONDUCT + FLOW) * gas
        res = outer_residual(view, i, SA, rs, rg, fy, edge, is_after)
        sc[2, i], sc[3, i] = relaxed(view, i, SA, *res)

    def sweep(k, carry):
        stores = []
        for r in range(GROUP):
            i = GROUP * k + 1 + r
            new_s, new_g = relaxed(view, i, SA, *row_residual(view, i, SA, edge))
            stores += [((2, i), new_s), ((3, i), new_g)]
        for at, value in stores:
            sc[at] = value
        return carry

    lax.fori_loop(0, ny // GROUP, sweep, 0)

    def leaving(k):
        part = pl.ds(GROUP * k, GROUP)
        return pltpu.make_async_copy(done.at[:, part], out.at[:, part], sems.at[k])

    def final(k, carry):
        stores = []
        for r in range(GROUP):
            i = GROUP * k + 1 + r
            new_s, new_g = last_relaxed(view, i, SB, edge, slice(PAD, PAD + nx))
            stores += [((0, i - 1), new_s), ((1, i - 1), new_g)]
        for at, value in stores:
            done[at] = value
        leaving(k).start()
        return carry

    lax.fori_loop(0, ny // GROUP, final, 0)
    for k in range(ny // GROUP):
        leaving(k).wait()


class Fields:
    def __init__(self, st, sc):
        self.st, self.sc = st, sc

    def __getitem__(self, at):
        return (self.sc if at[0] <= GB else self.st)[at]


def cost(rows, cells):
    return pl.CostEstimate(flops=50 * rows * cells, bytes_accessed=16 * 4 * rows * cells, transcendentals=0)


def swap(x, axis, first):
    pairs = []
    for i in range(first, lax.axis_size(axis) - 1, 2):
        pairs += [(i, i + 1), (i + 1, i)]
    return lax.ppermute(x, axis, pairs)


def shards(temps, right_side, exchange, coupling):
    temps, right_side = (jnp.transpose(a, (0, 2, 1, 3)) for a in (temps, right_side))
    exchange, coupling = (jnp.transpose(a, (1, 0, 2)) for a in (exchange, coupling))
    temps, right_side, exchange, coupling = (
        pltpu.with_memory_space_constraint(a, pltpu.HBM) for a in (temps, right_side, exchange, coupling)
    )
    ny, nx, nz = exchange.shape
    ext = nx + 2 * PAD
    f32 = functools.partial(jax.ShapeDtypeStruct, dtype=jnp.float32)

    strip = f32((strip_height(ny), nz))
    state = f32((PLANES, ny + 2, ext, nz))
    one, two, early, st = pl.pallas_call(
        pack_kernel,
        out_shape=(strip, strip, f32((EARLY, nx, nz)), state),
        in_specs=[HBM] * 4,
        out_specs=(VMEM,) * 4,
        scratch_shapes=[pltpu.SemaphoreType.DMA((6,))],
        compiler_params=PARAMS,
        name="pack_x",
    )(temps, right_side, exchange, coupling)
    one, two = swap(one, "gx", 0), swap(two, "gx", 1)
    early = swap(early, "gy", 1)

    def letter(planes):
        return f32((planes, ext - 2 * CROP, nz))

    st = pl.pallas_call(
        conduct_kernel,
        out_shape=state,
        in_specs=[VMEM],
        out_specs=VMEM,
        input_output_aliases={0: 0},
        compiler_params=PARAMS,
        cost_estimate=cost(2 * ny, ext * nz),
        name="conduct",
    )(st)
    st, across = pl.pallas_call(
        first_kernel,
        out_shape=(state, f32((across_parts(ext)[1], nz))),
        in_specs=[VMEM] * 3,
        out_specs=(VMEM,) * 2,
        input_output_aliases={0: 0},
        compiler_params=PARAMS,
        name="first",
    )(st, one, two)
    st, *beside = pl.pallas_call(
        other_kernel,
        out_shape=(state,) + (letter(THIRD),) * (MESSAGE // THIRD),
        in_specs=[VMEM] * 3,
        out_specs=(VMEM,) * (1 + MESSAGE // THIRD),
        input_output_aliases={0: 0},
        compiler_params=PARAMS,
        name="other",
    )(st, one, two)
    across = swap(across, "gy", 1)

    rows = f32((4, ny // 2, ext, nz))
    st, coarse = pl.pallas_call(
        inner_kernel,
        out_shape=(state, rows),
        in_specs=[VMEM] * 2,
        out_specs=(VMEM,) * 2,
        input_output_aliases={0: 0},
        compiler_params=PARAMS,
        cost_estimate=cost(4 * ny, ext * nz),
        name="inner",
    )(st, early)

    beside = [swap(part, "gy", 0) for part in beside]

    lay = Rows(nx)

    def tall(height):
        return f32(((height + 7) // 8 * 8, nz))

    letter_room = pltpu.VMEM((MESSAGE, ext, nz), jnp.float32)
    more = f32((6, ext, nz))
    st, coarse, extra = pl.pallas_call(
        near_kernel,
        out_shape=(state, rows, more),
        in_specs=[VMEM] * (2 + len(beside)),
        out_specs=(VMEM,) * 3,
        scratch_shapes=[letter_room],
        input_output_aliases={0: 0, 1: 1},
        compiler_params=PARAMS,
        name="near",
    )(st, coarse, *beside)
    st, coarse, extra, total, last_info, first_info, message = pl.pallas_call(
        second_kernel,
        out_shape=(state, rows, more, tall(lay.map), tall(lay.info), tall(lay.info + lay.rest), tall(lay.full)),
        in_specs=[VMEM] * 5,
        out_specs=(VMEM,) * 7,
        scratch_shapes=[letter_room, pltpu.VMEM((8, ext, nz), jnp.float32)],
        input_output_aliases={0: 0, 1: 1, 2: 2},
        compiler_params=PARAMS,
        name="second",
    )(st, coarse, extra, early, across)

    near, messages = total, [message]
    count = lax.axis_size("gy")
    radices, stride = stages(count), 1
    for place, radix in enumerate(radices[:-1]):
        swaps = matchings(count, radix, stride)
        if place:
            messages = [full_message(nx, total, last_info, first_info, senders) for senders, _ in swaps]
        others = exchange_stage(messages, swaps)
        final = radices[-1] if place == len(radices) - 2 else 0
        following = matchings(count, final, stride * radix) if final else []
        outs = [tall(lay.final if adjacent else lay.map) for _, adjacent in following] if final else [tall(lay.map)]
        near, *messages = pl.pallas_call(
            functools.partial(join_kernel, radix, stride, final, nx, place == 0),
            out_shape=(tall(lay.near), *outs),
            in_specs=[VMEM] * (3 + radix),
            out_specs=(VMEM,) * (1 + len(outs)),
            compiler_params=PARAMS,
            name="join",
        )(total, last_info, first_info, near, *others)
        total = total if final else messages[0]
        stride *= radix
    got = exchange_stage(messages, matchings(count, radices[-1], stride))

    out = pl.pallas_call(
        functools.partial(third_kernel, radices[-1], stride),
        out_shape=f32((2, ny, nx, nz)),
        in_specs=[VMEM] * (4 + len(got)),
        out_specs=HBM,
        scratch_shapes=[
            pltpu.VMEM((4, ny + 2, ext, nz), jnp.float32),
            pltpu.VMEM((11, ext, nz), jnp.float32),
            pltpu.VMEM(tall(lay.near).shape, jnp.float32),
            pltpu.VMEM((2, ny, nx, nz), jnp.float32),
            pltpu.SemaphoreType.DMA((ny // GROUP,)),
        ],
        compiler_params=PARAMS,
        name="third",
    )(st, extra, coarse, near, *got)
    return jnp.transpose(out, (0, 2, 1, 3))


def solution(mesh):
    return jax.shard_map(
        shards,
        mesh=mesh,
        in_specs=(
            P(None, "gx", "gy", None),
            P(None, "gx", "gy", None),
            P("gx", "gy", None),
            P("gx", "gy", None),
        ),
        out_specs=P(None, "gx", "gy", None),
        check_vma=False,
    )
```

```python
import functools

import jax
import jax.numpy as jnp
from jax import lax
from jax.experimental import pallas as pl
from jax.experimental.pallas import tpu as pltpu
from jax.sharding import PartitionSpec as P

SOLID_CAP, GAS_CAP, FLOW, CONDUCT, RELAX, LUMP = 0.5, 0.02, 40.0, 0.05, 0.8, 0.25
GAS_SELF = GAS_CAP + 4.5 * CONDUCT

PAD = 8
WX = 5
CROP = 4
(SA, GA, SB, GB, K, C, RS, RG, FX, FZ, H, FY, ASS, ASG, AGG) = range(15)
PLANES = 15
(M_S, M_G, M_K, M_C, M_FY, M_1S, M_1G, M_2S, M_2G) = range(9)
MESSAGE, EARLY, THIRD = 9, 7, 3

GROUP = 6

VMEM = pl.BlockSpec(memory_space=pltpu.VMEM)
HBM = pl.BlockSpec(memory_space=pltpu.HBM)
PARAMS = pltpu.CompilerParams(vmem_limit_bytes=40 * 1024 * 1024)


def up_x(v):
    return pltpu.roll(v, v.shape[0] - 1, 0)


def down_x(v):
    return pltpu.roll(v, 1, 0)


def up_z(v):
    return pltpu.roll(v, v.shape[1] - 1, 1)


def down_z(v):
    return pltpu.roll(v, 1, 1)


def lanes(shape):
    return lax.broadcasted_iota(jnp.int32, shape, 1)


def x_mask(shape, nx):
    row = lax.broadcasted_iota(jnp.int32, shape, 0)
    place, count = lax.axis_index("gx"), lax.axis_size("gx")
    low = jnp.where(place == 0, PAD, PAD - WX)
    high = jnp.where(place == count - 1, PAD + nx, PAD + nx + WX)
    return jnp.where((row >= low) & (row < high), 1.0, 0.0).astype(jnp.float32)


PAIRS = ((SA, GA), (C, RS), (RG, K))
STRIP_ROWS = 8 * len(PAIRS)


def strip_height(ny):
    return ny * STRIP_ROWS + (ny + 7) // 8 * 8


def sublanes(nz):
    return lax.broadcasted_iota(jnp.int32, (8, nz), 0)


def conductivity_of(s, exchange):
    return 1.0 + 4.0 * exchange * s * s * s


def strip_side(s, g, k, rs, rg, c, low):
    row = sublanes(s.shape[1])
    inn, shift = (3, 7) if low else (4, 1)
    k_out, s_out, g_out = (pltpu.roll(v, shift, 0) for v in (k, s, g))
    rs = rs + jnp.where(row == inn, 0.5 * (k + k_out) * s_out, 0.0)
    rg = rg + jnp.where(row == inn, CONDUCT * g_out, 0.0)
    values = {SA: s, GA: g, K: k, RS: rs, RG: rg, C: c}
    tiles = []
    for a, b in PAIRS:
        a, b = values[a], values[b]
        a, b = (a, pltpu.roll(b, 4, 0)) if low else (pltpu.roll(a, 4, 0), b)
        tiles.append(jnp.where(row < 4, a, b))
    return tiles, (k[4:5] if low else k[3:4])


def pack_kernel(temps, right, exchange, coupling, one, two, early, st, sems):
    even = lax.axis_index("gx") % 2 == 0
    odd = lax.axis_index("gy") % 2 == 1
    ny, nx, nz = exchange.shape
    copies = []
    for k, (plane, ref) in enumerate(
        ((SA, temps.at[0]), (K, exchange), (GA, temps.at[1]), (C, coupling), (RS, right.at[0]), (RG, right.at[1]))
    ):
        to = st.at[plane, pl.ds(1, ny), pl.ds(PAD, nx)]
        copies.append(pltpu.make_async_copy(ref, to, sems.at[k]))
    for copy in copies:
        copy.start()
    for copy in copies:
        copy.wait()
    for i in range(1, ny + 1):
        sides = []
        for start in (PAD, PAD + nx - 8):
            s, g, e, rs, rg, c = (st[plane, i, start : start + 8] for plane in (SA, GA, K, RS, RG, C))
            sides.append(strip_side(s, g, conductivity_of(s, e), rs, rg, c, start == PAD))
        (low, low_k), (high, high_k) = sides
        for p in range(len(PAIRS)):
            part = slice((i - 1) * STRIP_ROWS + 8 * p, (i - 1) * STRIP_ROWS + 8 * p + 8)
            one[part] = jnp.where(even, high[p], low[p])
            two[part] = jnp.where(even, low[p], high[p])
        part = slice(ny * STRIP_ROWS + i - 1, ny * STRIP_ROWS + i)
        one[part] = jnp.where(even, high_k, low_k)
        two[part] = jnp.where(even, low_k, high_k)
    own = slice(PAD, PAD + nx)
    for is_odd, e, d in ((True, ny, ny - 1), (False, 1, 2)):

        @pl.when(odd == is_odd)
        def _():
            s, s_d, g, g_d = st[SA, e, own], st[SA, d, own], st[GA, e, own], st[GA, d, own]
            c, k, k_d = st[C, e, own], conductivity_of(s, st[K, e, own]), conductivity_of(s_d, st[K, d, own])
            fx, fz, h, _ = faces(k)
            fy = 0.5 * (k + k_d)
            part_s, part_g = inner(s, g, c, h, fx, fz, edge_weights((nx, nz)))
            m_1s, m_1g = first_partial(st[RS, e, own] + part_s, st[RG, e, own] + part_g, s, s_d, g, g_d, fy, is_odd)
            for plane, value in enumerate((s, g, k, c, fy, m_1s, m_1g)):
                early[plane] = value


def conduct_kernel(st_in, st):
    del st_in
    planes, rows, ext, nz = st.shape
    own = slice(PAD, ext - PAD)
    for i in range(1, rows - 1):
        st[K, i, own] = conductivity_of(st[SA, i, own], st[K, i, own])


def place_halo(st, one, two, y, nx):
    even = lax.axis_index("gx") % 2 == 0
    ny, row = st.shape[1] - 2, sublanes(st.shape[3])
    i = y + 1

    def received(part):
        a, b = one[part], two[part]
        return jnp.where(even, b, a), jnp.where(even, a, b)

    for p, (plane_a, plane_b) in enumerate(PAIRS):
        before, after = received(slice(y * STRIP_ROWS + 8 * p, y * STRIP_ROWS + 8 * p + 8))
        before = {plane_a: pltpu.roll(before, 4, 0), plane_b: before}
        after = {plane_a: after, plane_b: pltpu.roll(after, 4, 0)}
        for plane in (plane_a, plane_b):
            low, high = jnp.where(row >= 4, before[plane], 0.0), jnp.where(row < 4, after[plane], 0.0)
            if plane == K:
                k_low, k_high = received(slice(ny * STRIP_ROWS + y, ny * STRIP_ROWS + y + 1))
                low, high = jnp.where(row == 3, k_low, low), jnp.where(row == 4, k_high, high)
            st[plane, i, :PAD] = low
            st[plane, i, PAD + nx :] = high


def inner(s, g, c, h, fx, fz, edge):
    t = c * (s - g)
    flux_x = fx * (up_x(s) - s)
    flux_z = fz * (up_z(s) - s)
    part_s = (flux_x - down_x(flux_x)) + (flux_z - down_z(flux_z)) - h * s - t
    part_g = (
        t
        - GAS_SELF * g
        + CONDUCT * (up_x(g) + down_x(g))
        + edge[0] * up_z(g)
        + edge[1] * down_z(g)
    )
    return part_s, part_g


def edge_weights(shape):
    lane = lanes(shape)
    weight = jnp.float32(0.25 * CONDUCT)
    return jnp.where(lane == shape[1] - 1, 0.0, weight), jnp.where(lane == 0, 0.0, weight)


def row_inner(st, i, s_at, edge):
    return inner(st[s_at, i], st[s_at + 1, i], st[C, i], st[H, i], st[FX, i], st[FZ, i], edge)


def row_residual(st, i, s_at, edge):
    part_s, part_g = row_inner(st, i, s_at, edge)
    s, g, before = st[s_at, i], st[s_at + 1, i], st[s_at + 1, i - 1]
    part_s += st[FY, i] * (st[s_at, i + 1] - s) + st[FY, i - 1] * (st[s_at, i - 1] - s)
    part_g += CONDUCT * (st[s_at + 1, i + 1] + before) - FLOW * (g - before)
    return st[RS, i] + part_s, st[RG, i] + part_g


def relaxed(st, i, s_at, res_s, res_g):
    s = st[s_at, i] + st[ASS, i] * res_s + st[ASG, i] * res_g
    g = st[s_at + 1, i] + st[ASG, i] * res_s + st[AGG, i] * res_g
    return s, g


def faces(k):
    lane = lanes(k.shape)
    end = k.shape[1] - 1
    fx = 0.5 * (k + up_x(k))
    fz = jnp.where(lane == end, 0.0, 0.125 * (k + up_z(k)))
    h = SOLID_CAP + jnp.where((lane == 0) | (lane == end), 0.125 * k, 0.0)
    return fx, fz, h, h + (fx + down_x(fx)) + (fz + down_z(fz))


def inverse(diag, c, mask):
    gas_diag = (GAS_SELF + FLOW) + c
    inv = (RELAX * mask) / (diag * gas_diag - c * c)
    return inv * gas_diag, inv * c, inv * diag


def last_relaxed(st, i, s_at, edge, own):
    full_s, full_g = st[s_at, i], st[s_at + 1, i]
    s, g = full_s[own], full_g[own]
    flux_x = st[FX, i] * (up_x(full_s) - full_s)
    flux_z = st[FZ, i, own] * (up_z(s) - s)
    c, before = st[C, i, own], st[s_at + 1, i - 1, own]
    t = c * (s - g)
    res_s = st[RS, i, own] + (flux_x[own] - down_x(flux_x)[own]) + (flux_z - down_z(flux_z)) - st[H, i, own] * s - t
    res_s += st[FY, i, own] * (st[s_at, i + 1, own] - s) + st[FY, i - 1, own] * (st[s_at, i - 1, own] - s)
    res_g = st[RG, i, own] + t - GAS_SELF * g + edge[0][own] * up_z(g) + edge[1][own] * down_z(g)
    res_g += CONDUCT * (up_x(full_g)[own] + down_x(full_g)[own] + st[s_at + 1, i + 1, own] + before) - FLOW * (g - before)
    ss, sg, gg = st[ASS, i, own], st[ASG, i, own], st[AGG, i, own]
    return s + ss * res_s + sg * res_g, g + sg * res_s + gg * res_g


def grouped(rows, work):
    for start in range(0, len(rows), GROUP):
        stores = []
        for i in rows[start : start + GROUP]:
            stores += work(i)
        for ref, at, value in stores:
            ref[at] = value


def looped(first, last, size, work):
    def group(k, carry):
        grouped([first + size * k + r for r in range(size)], work)
        return carry

    lax.fori_loop(0, (last - first) // size, group, 0)
    grouped(list(range(last - (last - first) % size, last)), work)


def row_coefficients(st, i, mask):
    fx, fz, h, diag = faces(st[K, i])
    fy = 0.5 * (st[K, i] + st[K, i + 1])
    before = 0.5 * (st[K, i] + st[K, i - 1])
    ss, sg, gg = inverse(diag + st[C, i] + fy + before, st[C, i], mask)
    values = ((FX, fx), (FZ, fz), (H, h), (FY, fy), (ASS, ss), (ASG, sg), (AGG, gg))
    return [(st, (plane, i), v) for plane, v in values]


def row_sweep(st, i, source, target, edge):
    s, g = relaxed(st, i, source, *row_residual(st, i, source, edge))
    return [(st, (target, i), s), (st, (target + 1, i), g)]


def first_partial(res_s, res_g, s, s_d, g, g_d, fy, onward):
    return res_s + fy * (s_d - s), res_g + CONDUCT * g_d - FLOW * (g - g_d if onward else g)


def send_planes(st, onward, edge):
    ny = st.shape[1] - 2
    e, d, near = (ny, ny - 1, ny - 1) if onward else (1, 2, 1)
    fy, s, g, g_d = st[FY, near], st[SA, e], st[GA, e], st[GA, d]
    part_s, part_g = row_inner(st, e, SA, edge)
    m_1s, m_1g = first_partial(st[RS, e] + part_s, st[RG, e] + part_g, s, st[SA, d], g, g_d, fy, onward)
    m_2s = st[RS, e] + fy * st[SB, d]
    m_2g = st[RG, e] + (CONDUCT + FLOW if onward else CONDUCT) * st[GB, d]
    return [s, g, st[K, e], st[C, e], fy, m_1s, m_1g, m_2s, m_2g]


def across_parts(ext):
    parts, at = [], 0
    for k in range(EARLY, MESSAGE):
        parts.append((k, CROP, ext - CROP, at))
        at += ext - 2 * CROP
    for k in range(EARLY):
        more = 1 if k in (M_1S, M_1G) else 0
        for low, high in ((CROP, PAD + more), (ext - PAD - more, ext - CROP)):
            parts.append((k, low, high, at))
            at += high - low
    return parts, (at + 7) // 8 * 8


def write_across(ref, k, value):
    for plane, low, high, at in across_parts(value.shape[0])[0]:
        if plane == k:
            ref[at : at + high - low] = value[low:high]


def read_across(early, across, outer, k):
    ext = outer.shape[1]
    if k < EARLY:
        outer[k, PAD : ext - PAD] = early[k]
    for plane, low, high, at in across_parts(ext)[0]:
        if plane == k:
            outer[k, low:high] = across[at : at + high - low]


def write_beside(refs, k, value):
    refs[k // THIRD][k % THIRD] = value[CROP : value.shape[0] - CROP]


def read_beside(refs, outer, k):
    outer[k, CROP : outer.shape[1] - CROP] = refs[k // THIRD][k % THIRD]


def first_end(st, one, two, after, write):
    planes, rows, ext, nz = st.shape
    ny, nx = rows - 2, ext - 2 * PAD
    mask = x_mask((ext, nz), nx)
    edge = edge_weights((ext, nz))
    e, d, f = (ny, ny - 1, ny - 2) if after else (1, 2, 3)
    for i in (e, d, f):
        place_halo(st, one, two, i - 1, nx)
    fx, fz, h, diag = faces(st[K, e])
    st[FX, e], st[FZ, e], st[H, e] = fx, fz, h
    st[FY, min(e, d)] = 0.5 * (st[K, e] + st[K, d])
    st[FY, min(d, f)] = 0.5 * (st[K, d] + st[K, f])
    grouped([d], lambda i: row_coefficients(st, i, mask))
    grouped([d], lambda i: row_sweep(st, i, SA, SB, edge))
    for k, value in enumerate(send_planes(st, after, edge)):
        write(k, value)


def either_first(st, one, two, after, write):
    for is_after in (True, False):

        @pl.when(after == is_after)
        def _():
            first_end(st, one, two, is_after, write)


def first_kernel(st_in, one, two, st, across):
    del st_in
    either_first(st, one, two, lax.axis_index("gy") % 2 == 1, functools.partial(write_across, across))


def other_kernel(st_in, one, two, st, *beside):
    del st_in
    either_first(st, one, two, lax.axis_index("gy") % 2 == 0, functools.partial(write_beside, beside))
    planes, rows, ext, nz = st.shape
    ny, nx = rows - 2, ext - 2 * PAD
    mask = x_mask((ext, nz), nx)
    for y in range(3, ny - 3):
        place_halo(st, one, two, y, nx)
    grouped(list(range(3, ny - 1)), lambda i: row_coefficients(st, i, mask))


def outer_residual(st, i, s_at, rs, rg, fy_out, edge, after):
    part_s, part_g = row_inner(st, i, s_at, edge)
    s, g = st[s_at, i], st[s_at + 1, i]
    if after:
        part_s += st[FY, i - 1] * (st[s_at, i - 1] - s)
        part_g += (CONDUCT + FLOW) * st[s_at + 1, i - 1]
    else:
        part_s += st[FY, i] * (st[s_at, i + 1] - s)
        part_g += CONDUCT * st[s_at + 1, i + 1]
    return rs + part_s - fy_out * s, rg + part_g - FLOW * g


def pair_x(v):
    row = lax.broadcasted_iota(jnp.int32, v.shape, 0)
    return v + jnp.where(row % 2 == 0, up_x(v), down_x(v))


def coarse_coefficients(c_sum, k_sum):
    per_solid = 1.0 / (4.0 * SOLID_CAP + c_sum + LUMP * k_sum)
    ratio = c_sum * per_solid
    return per_solid, ratio, 1.0 / ((4.0 * GAS_CAP + 2.0 * FLOW) + c_sum - c_sum * ratio)


def coarse_row(st, coarse, j, mask, edge):
    i = 2 * j + 1
    res_s, res_g = row_residual(st, i, SA, edge)
    more_s, more_g = row_residual(st, i + 1, SA, edge)
    res_s, res_g = pair_x((res_s + more_s) * mask), pair_x((res_g + more_g) * mask)
    c_sum = pair_x(st[C, i] + st[C, i + 1])
    per_solid, ratio, per_gas = coarse_coefficients(c_sum, pair_x(st[K, i] + st[K, i + 1]))
    lead = res_s * per_solid
    values = (lead, ratio, (2.0 * FLOW) * per_gas, (res_g + c_sum * lead) * per_gas)
    return [(coarse, (k, j), v) for k, v in enumerate(values)]


def inner_kernel(st_in, early, st, coarse):
    del st_in, early
    planes, rows, ext, nz = st.shape
    ny, nx = rows - 2, ext - 2 * PAD
    shape = (ext, nz)
    mask = x_mask(shape, nx)
    edge = edge_weights(shape)
    looped(3, ny - 1, 4, lambda i: row_sweep(st, i, SA, SB, edge))
    looped(3, ny - 1, 4, lambda i: row_sweep(st, i, SB, SA, edge))
    grouped(list(range(2, ny // 2 - 2)), lambda j: coarse_row(st, coarse, j, mask, edge))


def end_work(st, coarse, extra, read, outer, is_after):
    planes, rows, ext, nz = st.shape
    ny, nx = rows - 2, ext - 2 * PAD
    me, count = lax.axis_index("gy"), lax.axis_size("gy")
    mask = x_mask((ext, nz), nx)
    inside = jnp.where(me == (count - 1 if is_after else 0), 0.0, mask)
    edge = edge_weights((ext, nz))
    zeros = jnp.zeros((PAD, nz), jnp.float32)
    for k in range(MESSAGE):
        outer[k, :PAD] = zeros
        outer[k, ext - PAD :] = zeros
        read(outer, k)

    o, e, near = (ny + 1, ny, ny) if is_after else (0, 1, 0)
    to_o = CONDUCT + FLOW if is_after else CONDUCT
    s_o, g_o, k_o, c_o, fy_out = (outer[plane] for plane in (M_S, M_G, M_K, M_C, M_FY))
    fy = 0.5 * (k_o + st[K, e])
    fx, fz, h, diag = faces(k_o)
    inv_o = inverse(diag + c_o + fy_out + fy, c_o, inside)
    fx_e, fz_e = st[FX, e], st[FZ, e]
    diag = st[H, e] + (fx_e + down_x(fx_e)) + (fz_e + down_z(fz_e)) + st[C, e] + fy
    inv_e = inverse(diag + st[FY, near - 1 if is_after else near + 1], st[C, e], mask)
    for plane, value in ((SA, s_o), (GA, g_o), (K, k_o), (C, c_o), (FX, fx), (FZ, fz), (H, h)):
        st[plane, o] = value
    st[FY, near] = fy
    for k in range(3):
        st[ASS + k, o], st[ASS + k, e] = inv_o[k], inv_e[k]

    res = outer[M_1S] + fy * (st[SA, e] - s_o), outer[M_1G] + to_o * st[GA, e]
    new_o = relaxed(st, o, SA, *res)
    stores = row_sweep(st, e, SA, SB, edge)
    st[SB, o], st[GB, o] = new_o
    for ref, at, value in stores:
        ref[at] = value
    res = outer_residual(st, o, SB, outer[M_2S], outer[M_2G], fy_out, edge, is_after)
    new_o = relaxed(st, o, SB, *res)
    ends = [e - 1, e] if is_after else [e, e + 1]
    grouped(ends, lambda i: row_sweep(st, i, SB, SA, edge))
    st[SA, o], st[GA, o] = new_o
    for k, plane in enumerate((M_2S, M_2G, M_FY)):
        extra[(3 if is_after else 0) + k] = outer[plane]
    blocks = ny // 2
    stores = []
    for j in (blocks - 2, blocks - 1) if is_after else (0, 1):
        stores += coarse_row(st, coarse, j, mask, edge)
    for ref, at, value in stores:
        ref[at] = value


def either_end(after, st, coarse, extra, read, outer):
    for is_after in (True, False):

        @pl.when(after == is_after)
        def _():
            end_work(st, coarse, extra, read, outer, is_after)


def near_kernel(st_in, coarse_in, *refs):
    beside, (st, coarse, extra, outer) = refs[:-4], refs[-4:]
    del st_in, coarse_in
    either_end(lax.axis_index("gy") % 2 == 0, st, coarse, extra, functools.partial(read_beside, beside), outer)


def second_kernel(st_in, coarse_in, extra_in, early, across, *refs):
    st, coarse, extra, total, last_info, first_info, message, outer, squeeze = refs
    del st_in, coarse_in, extra_in
    planes, rows, ext, nz = st.shape
    ny, nx = rows - 2, ext - 2 * PAD
    me = lax.axis_index("gy")
    either_end(me % 2 == 1, st, coarse, extra, functools.partial(read_across, early, across), outer)

    blocks = ny // 2
    for k in range(4):
        squeeze[k] = coarse[k, 0]
    slopes, offsets = coarse[2, 0], coarse[3, 0]
    for j in range(1, blocks):
        slope = coarse[2, j]
        slopes, offsets = slope * slopes, slope * offsets + coarse[3, j]
        coarse[2, j], coarse[3, j] = slopes, offsets
    squeeze[4], squeeze[5], squeeze[6], squeeze[7] = slopes, offsets, coarse[0, blocks - 1], coarse[1, blocks - 1]

    span = nx // 2 + 2
    lead, ratio, slope, offset, slopes, offsets, lead_last, ratio_last = (
        squeeze[k, pl.ds(PAD - 2, span, 2), :] for k in range(8)
    )
    part = slice(PAD - 1, PAD + nx + 1)

    def increments(d, face, gas):
        return [(st[FY, face] * (st[SA, d] - st[SB, d]))[part], (gas * (st[GA, d] - st[GB, d]))[part]]

    onward = [lead_last, ratio_last] + increments(ny - 1, ny - 1, CONDUCT + FLOW)
    back = [lead, offset] + increments(2, 1, CONDUCT) + [slope, ratio]
    write_rows(total, [slopes, offsets])
    write_rows(last_info, onward)
    write_rows(first_info, back)
    for go, info in ((True, onward), (False, back)):

        @pl.when((me % 2 == 0) == go)
        def _():
            write_rows(message, [slopes, offsets] + info)


def write_rows(ref, values):
    at = 0
    for value in values:
        ref[at : at + value.shape[0]] = value
        at += value.shape[0]


class Rows:
    def __init__(self, nx):
        self.span = nx // 2 + 2
        self.map = 2 * self.span
        self.info = self.map + 2 * (nx + 2)
        self.rest = self.map
        self.final = self.map + self.info
        self.full = self.final + self.rest
        self.low = self.map
        self.high = self.low + self.info
        self.near = self.high + self.info + self.rest


def source(at, k, radix):
    if radix & (radix - 1) == 0:
        return at ^ k
    return (at + radix - k) % radix


def matchings(count, radix, stride):
    if (count, radix, stride) == (8, 4, 2):
        swaps = ((1, 2), (3, 4), (5, 6), (0, 7)), ((0, 3), (1, 5), (2, 6), (4, 7)), ((0, 4), (1, 6), (2, 5), (3, 7))
        out = []
        for pairs in swaps:
            senders = [0] * count
            for a, b in pairs:
                senders[a], senders[b] = b, a
            out.append((senders, len(out) == 0))
        return out
    out = []
    for k in range(1, radix):
        senders = []
        for me in range(count):
            at, low = me // stride % radix, me % stride
            senders.append(me - low + (source(at, k, radix) - at) * stride + (stride - 1 - low))
        out.append((senders, any(abs(source(at, k, radix) - at) == 1 for at in range(radix))))
    return sorted(out, key=lambda item: not item[1])


def look_up(table):
    me, value = lax.axis_index("gy"), jnp.int32(table[0])
    for k in range(1, len(table)):
        value = jnp.where(me == k, table[k], value)
    return value


def stages(count):
    if count % 2:
        return [1, count]
    out, rest = [2], count // 2
    while rest > 1:
        radix = next((r for r in (8, 4, 2) if rest % r == 0), rest)
        out.append(radix)
        rest //= radix
    return out if len(out) > 1 else out + [1]


def exchange_stage(messages, swaps):
    return [
        lax.ppermute(message, "gy", [(sender, me) for me, sender in enumerate(senders)])
        for (senders, near), message in zip(swaps, messages)
    ]


class Group:
    def __init__(self, radix, stride, others, nx):
        self.radix, self.others, self.nx = radix, others, nx
        me = lax.axis_index("gy")
        self.swaps = [
            (look_up([sender // stride % radix for sender in senders]), near)
            for senders, near in matchings(lax.axis_size("gy"), radix, stride)
        ]
        self.at = lax.rem(lax.div(me, stride), radix)
        low = lax.rem(me, stride)
        self.lowest, self.highest = low == 0, low == stride - 1

    def map_of(self, place, own):
        rows = Rows(self.nx)
        out = own
        for (sender, near), ref in zip(self.swaps, self.others):
            here = sender == place
            got = [ref[i * rows.span : (i + 1) * rows.span] for i in range(2)]
            out = got if out is None else [jnp.where(here, new, old) for new, old in zip(got, out)]
        return out

    def ahead(self, slope, offset):
        a, b = jnp.ones_like(slope), jnp.zeros_like(slope)
        for place in range(self.radix - 1):
            new_a, new_b = self.map_of(place, None)
            below = place < self.at
            a, b = jnp.where(below, new_a * a, a), jnp.where(below, new_a * b + new_b, b)
        return slope * a, slope * b + offset

    def total(self, own):
        a, b = self.map_of(0, own)
        for place in range(1, self.radix):
            new_a, new_b = self.map_of(place, own)
            a, b = new_a * a, new_a * b + new_b
        return a, b

    def collect(self, near, final):
        rows = Rows(self.nx)
        for (place, adjacent), ref in zip(self.swaps, self.others):
            if not adjacent:
                continue

            @pl.when(self.lowest & (place == self.at - 1))
            def _():
                near[rows.low : rows.low + rows.info] = ref[rows.map : rows.final]

            @pl.when(self.highest & (place == self.at + 1))
            def _():
                near[rows.high : rows.high + rows.info] = ref[rows.map : rows.final]
                rest = slice(0, rows.map) if final else slice(rows.final, rows.full)
                near[rows.high + rows.info : rows.near] = ref[rest]


def start_near(near, nx, nz):
    rows = Rows(nx)
    near[: rows.span] = jnp.ones((rows.span, nz), jnp.float32)
    near[rows.span :] = jnp.zeros((near.shape[0] - rows.span, nz), jnp.float32)


def join_kernel(radix, stride, final, nx, is_first, *refs):
    rows = Rows(nx)
    total, last_info, first_info, near_in = refs[:4]
    others, near, outs = refs[4 : 3 + radix], refs[3 + radix], refs[4 + radix :]
    nz = near.shape[1]
    if is_first:
        start_near(near, nx, nz)
    else:
        near[...] = near_in[...]
    group = Group(radix, stride, others, nx)
    own = [total[i * rows.span : (i + 1) * rows.span] for i in range(2)]
    ahead = group.ahead(near[: rows.span], near[rows.span : rows.map])
    write_rows(near, ahead)
    group.collect(near, False)
    whole = group.total(own)
    if final == 0:
        write_rows(outs[0], whole)
        return
    me, count = lax.axis_index("gy"), lax.axis_size("gy")
    for (senders, adjacent), out in zip(matchings(count, final, stride * radix), outs):
        up = look_up(senders) > me
        if not adjacent:
            write_rows(out, whole)
            continue

        @pl.when(up)
        def _():
            write_rows(out, whole)
            out[rows.map : rows.final] = last_info[: rows.info]

        @pl.when(jnp.logical_not(up))
        def _():
            out[: rows.map] = first_info[rows.info : rows.info + rows.rest]
            out[rows.map : rows.final] = first_info[: rows.info]


def full_message(nx, total, last_info, first_info, senders):
    rows = Rows(nx)
    onward = jnp.concatenate([total[: rows.map], last_info[: rows.info], first_info[rows.info : rows.info + rows.rest]])
    back = jnp.concatenate([total[: rows.map], first_info[: rows.info + rows.rest]])
    message = jnp.where(look_up(senders) > lax.axis_index("gy"), onward, back)
    return jnp.pad(message, ((0, -rows.full % 8), (0, 0)))


def third_kernel(radix, stride, *refs):
    st, extra, coarse, near_in = refs[:4]
    others, (out, sc, wide, near, done, sems) = refs[4 : 3 + radix], refs[3 + radix :]
    planes, rows, ext, nz = st.shape
    ny, nx = rows - 2, ext - 2 * PAD
    edge = edge_weights((ext, nz))
    blocks = ny // 2

    lay = Rows(nx)
    span = lay.span
    near[...] = near_in[...]
    group = Group(radix, stride, others, nx)
    if radix > 1:
        group.collect(near, True)
    gas_in = group.ahead(near[:span], near[span : lay.map])[1]
    at_high = lay.high + lay.info
    starts = [lay.low, lay.low + span, lay.high, lay.high + span, at_high, at_high + span]
    for k, v in enumerate([gas_in] + [near[start : start + span] for start in starts]):
        wide[k, : PAD - 2] = jnp.zeros((PAD - 2, nz), jnp.float32)
        wide[k, ext - PAD + 2 :] = jnp.zeros((PAD - 2, nz), jnp.float32)
        wide[k, pl.ds(PAD - 2, span, 2), :] = v
        wide[k, pl.ds(PAD - 1, span, 2), :] = v
    for k, start in enumerate((lay.low, lay.low + nx + 2, lay.high, lay.high + nx + 2)):
        start += lay.map
        wide[7 + k, :PAD] = jnp.zeros((PAD, nz), jnp.float32)
        wide[7 + k, ext - PAD :] = jnp.zeros((PAD, nz), jnp.float32)
        wide[7 + k, PAD - 1 : PAD + nx + 1] = near[start : start + nx + 2]

    gas_in = wide[0]
    last = ny + 1
    solid_low = wide[1] + wide[2] * gas_in
    sc[0, 0] = st[SA, 0] + solid_low
    sc[1, 0] = st[GA, 0] + gas_in

    def correct(j, carry):
        gas = coarse[2, j] * gas_in + coarse[3, j]
        solid = coarse[0, j] + coarse[1, j] * gas
        for i in (2 * j + 1, 2 * j + 2):
            sc[0, i] = st[SA, i] + solid
            sc[1, i] = st[GA, i] + gas
        return carry

    lax.fori_loop(0, blocks, correct, 0)
    gas = coarse[2, blocks - 1] * gas_in + coarse[3, blocks - 1]
    gas_high = wide[5] * gas + wide[4]
    solid_high = wide[3] + wide[6] * gas_high
    sc[0, last] = st[SA, last] + solid_high
    sc[1, last] = st[GA, last] + gas_high

    view = Fields(st, sc)
    for i, is_after, solid, gas in ((0, False, solid_low, gas_in), (last, True, solid_high, gas_high)):
        side = 3 if is_after else 0
        fy = extra[side + 2]
        to = 9 if is_after else 7
        rs = extra[side] + wide[to] + fy * solid
        rg = extra[side + 1] + wide[to + 1] + (CONDUCT if is_after else CONDUCT + FLOW) * gas
        res = outer_residual(view, i, SA, rs, rg, fy, edge, is_after)
        sc[2, i], sc[3, i] = relaxed(view, i, SA, *res)

    def sweep(k, carry):
        stores = []
        for r in range(GROUP):
            i = GROUP * k + 1 + r
            new_s, new_g = relaxed(view, i, SA, *row_residual(view, i, SA, edge))
            stores += [((2, i), new_s), ((3, i), new_g)]
        for at, value in stores:
            sc[at] = value
        return carry

    lax.fori_loop(0, ny // GROUP, sweep, 0)

    def leaving(k):
        part = pl.ds(GROUP * k, GROUP)
        return pltpu.make_async_copy(done.at[:, part], out.at[:, part], sems.at[k])

    def final(k, carry):
        stores = []
        for r in range(GROUP):
            i = GROUP * k + 1 + r
            new_s, new_g = last_relaxed(view, i, SB, edge, slice(PAD, PAD + nx))
            stores += [((0, i - 1), new_s), ((1, i - 1), new_g)]
        for at, value in stores:
            done[at] = value
        leaving(k).start()
        return carry

    lax.fori_loop(0, ny // GROUP, final, 0)
    for k in range(ny // GROUP):
        leaving(k).wait()


class Fields:
    def __init__(self, st, sc):
        self.st, self.sc = st, sc

    def __getitem__(self, at):
        return (self.sc if at[0] <= GB else self.st)[at]


def cost(rows, cells):
    return pl.CostEstimate(flops=50 * rows * cells, bytes_accessed=16 * 4 * rows * cells, transcendentals=0)


def swap(x, axis, first):
    pairs = []
    for i in range(first, lax.axis_size(axis) - 1, 2):
        pairs += [(i, i + 1), (i + 1, i)]
    return lax.ppermute(x, axis, pairs)


def shards(temps, right_side, exchange, coupling):
    temps, right_side = (jnp.transpose(a, (0, 2, 1, 3)) for a in (temps, right_side))
    exchange, coupling = (jnp.transpose(a, (1, 0, 2)) for a in (exchange, coupling))
    temps, right_side, exchange, coupling = (
        pltpu.with_memory_space_constraint(a, pltpu.HBM) for a in (temps, right_side, exchange, coupling)
    )
    ny, nx, nz = exchange.shape
    ext = nx + 2 * PAD
    f32 = functools.partial(jax.ShapeDtypeStruct, dtype=jnp.float32)

    strip = f32((strip_height(ny), nz))
    state = f32((PLANES, ny + 2, ext, nz))
    one, two, early, st = pl.pallas_call(
        pack_kernel,
        out_shape=(strip, strip, f32((EARLY, nx, nz)), state),
        in_specs=[HBM] * 4,
        out_specs=(VMEM,) * 4,
        scratch_shapes=[pltpu.SemaphoreType.DMA((6,))],
        compiler_params=PARAMS,
        name="pack_x",
    )(temps, right_side, exchange, coupling)
    one, two = swap(one, "gx", 0), swap(two, "gx", 1)
    early = swap(early, "gy", 1)

    def letter(planes):
        return f32((planes, ext - 2 * CROP, nz))

    st = pl.pallas_call(
        conduct_kernel,
        out_shape=state,
        in_specs=[VMEM],
        out_specs=VMEM,
        input_output_aliases={0: 0},
        compiler_params=PARAMS,
        cost_estimate=cost(2 * ny, ext * nz),
        name="conduct",
    )(st)
    st, across = pl.pallas_call(
        first_kernel,
        out_shape=(state, f32((across_parts(ext)[1], nz))),
        in_specs=[VMEM] * 3,
        out_specs=(VMEM,) * 2,
        input_output_aliases={0: 0},
        compiler_params=PARAMS,
        name="first",
    )(st, one, two)
    st, *beside = pl.pallas_call(
        other_kernel,
        out_shape=(state,) + (letter(THIRD),) * (MESSAGE // THIRD),
        in_specs=[VMEM] * 3,
        out_specs=(VMEM,) * (1 + MESSAGE // THIRD),
        input_output_aliases={0: 0},
        compiler_params=PARAMS,
        name="other",
    )(st, one, two)
    across = swap(across, "gy", 1)

    rows = f32((4, ny // 2, ext, nz))
    st, coarse = pl.pallas_call(
        inner_kernel,
        out_shape=(state, rows),
        in_specs=[VMEM] * 2,
        out_specs=(VMEM,) * 2,
        input_output_aliases={0: 0},
        compiler_params=PARAMS,
        cost_estimate=cost(4 * ny, ext * nz),
        name="inner",
    )(st, early)

    beside = [swap(part, "gy", 0) for part in beside]

    lay = Rows(nx)

    def tall(height):
        return f32(((height + 7) // 8 * 8, nz))

    letter_room = pltpu.VMEM((MESSAGE, ext, nz), jnp.float32)
    more = f32((6, ext, nz))
    st, coarse, extra = pl.pallas_call(
        near_kernel,
        out_shape=(state, rows, more),
        in_specs=[VMEM] * (2 + len(beside)),
        out_specs=(VMEM,) * 3,
        scratch_shapes=[letter_room],
        input_output_aliases={0: 0, 1: 1},
        compiler_params=PARAMS,
        name="near",
    )(st, coarse, *beside)
    st, coarse, extra, total, last_info, first_info, message = pl.pallas_call(
        second_kernel,
        out_shape=(state, rows, more, tall(lay.map), tall(lay.info), tall(lay.info + lay.rest), tall(lay.full)),
        in_specs=[VMEM] * 5,
        out_specs=(VMEM,) * 7,
        scratch_shapes=[letter_room, pltpu.VMEM((8, ext, nz), jnp.float32)],
        input_output_aliases={0: 0, 1: 1, 2: 2},
        compiler_params=PARAMS,
        name="second",
    )(st, coarse, extra, early, across)

    near, messages = total, [message]
    count = lax.axis_size("gy")
    radices, stride = stages(count), 1
    for place, radix in enumerate(radices[:-1]):
        swaps = matchings(count, radix, stride)
        if place:
            messages = [full_message(nx, total, last_info, first_info, senders) for senders, _ in swaps]
        others = exchange_stage(messages, swaps)
        final = radices[-1] if place == len(radices) - 2 else 0
        following = matchings(count, final, stride * radix) if final else []
        outs = [tall(lay.final if adjacent else lay.map) for _, adjacent in following] if final else [tall(lay.map)]
        near, *messages = pl.pallas_call(
            functools.partial(join_kernel, radix, stride, final, nx, place == 0),
            out_shape=(tall(lay.near), *outs),
            in_specs=[VMEM] * (3 + radix),
            out_specs=(VMEM,) * (1 + len(outs)),
            compiler_params=PARAMS,
            name="join",
        )(total, last_info, first_info, near, *others)
        total = total if final else messages[0]
        stride *= radix
    got = exchange_stage(messages, matchings(count, radices[-1], stride))

    out = pl.pallas_call(
        functools.partial(third_kernel, radices[-1], stride),
        out_shape=f32((2, ny, nx, nz)),
        in_specs=[VMEM] * (4 + len(got)),
        out_specs=HBM,
        scratch_shapes=[
            pltpu.VMEM((4, ny + 2, ext, nz), jnp.float32),
            pltpu.VMEM((11, ext, nz), jnp.float32),
            pltpu.VMEM(tall(lay.near).shape, jnp.float32),
            pltpu.VMEM((2, ny, nx, nz), jnp.float32),
            pltpu.SemaphoreType.DMA((ny // GROUP,)),
        ],
        compiler_params=PARAMS,
        name="third",
    )(st, extra, coarse, near, *got)
    return jnp.transpose(out, (0, 2, 1, 3))


def solution(mesh):
    return jax.shard_map(
        shards,
        mesh=mesh,
        in_specs=(
            P(None, "gx", "gy", None),
            P(None, "gx", "gy", None),
            P("gx", "gy", None),
            P("gx", "gy", None),
        ),
        out_specs=P(None, "gx", "gy", None),
        check_vma=False,
    )
```

```python
import functools

import jax
import jax.numpy as jnp
from jax import lax
from jax.experimental import pallas as pl
from jax.experimental.pallas import tpu as pltpu
from jax.sharding import PartitionSpec as P

SOLID_CAP, GAS_CAP, FLOW, CONDUCT, RELAX, LUMP = 0.5, 0.02, 40.0, 0.05, 0.8, 0.25
GAS_SELF = GAS_CAP + 4.5 * CONDUCT

PAD = 8
WX = 5
CROP = 4
(SA, GA, SB, GB, K, C, RS, RG, FX, FZ, H, FY, ASS, ASG, AGG) = range(15)
PLANES = 15
(M_S, M_G, M_K, M_C, M_FY, M_1S, M_1G, M_2S, M_2G) = range(9)
MESSAGE, EARLY, THIRD = 9, 7, 3

GROUP = 6

VMEM = pl.BlockSpec(memory_space=pltpu.VMEM)
HBM = pl.BlockSpec(memory_space=pltpu.HBM)
PARAMS = pltpu.CompilerParams(vmem_limit_bytes=40 * 1024 * 1024)


def up_x(v):
    return pltpu.roll(v, v.shape[0] - 1, 0)


def down_x(v):
    return pltpu.roll(v, 1, 0)


def up_z(v):
    return pltpu.roll(v, v.shape[1] - 1, 1)


def down_z(v):
    return pltpu.roll(v, 1, 1)


def lanes(shape):
    return lax.broadcasted_iota(jnp.int32, shape, 1)


def x_mask(shape, nx):
    row = lax.broadcasted_iota(jnp.int32, shape, 0)
    place, count = lax.axis_index("gx"), lax.axis_size("gx")
    low = jnp.where(place == 0, PAD, PAD - WX)
    high = jnp.where(place == count - 1, PAD + nx, PAD + nx + WX)
    return jnp.where((row >= low) & (row < high), 1.0, 0.0).astype(jnp.float32)


PAIRS = ((SA, GA), (C, RS), (RG, K))
STRIP_ROWS = 8 * len(PAIRS)


def strip_height(ny):
    return ny * STRIP_ROWS + (ny + 7) // 8 * 8


def sublanes(nz):
    return lax.broadcasted_iota(jnp.int32, (8, nz), 0)


def conductivity_of(s, exchange):
    return 1.0 + 4.0 * exchange * s * s * s


def strip_side(s, g, k, rs, rg, c, low):
    row = sublanes(s.shape[1])
    inn, shift = (3, 7) if low else (4, 1)
    k_out, s_out, g_out = (pltpu.roll(v, shift, 0) for v in (k, s, g))
    rs = rs + jnp.where(row == inn, 0.5 * (k + k_out) * s_out, 0.0)
    rg = rg + jnp.where(row == inn, CONDUCT * g_out, 0.0)
    values = {SA: s, GA: g, K: k, RS: rs, RG: rg, C: c}
    tiles = []
    for a, b in PAIRS:
        a, b = values[a], values[b]
        a, b = (a, pltpu.roll(b, 4, 0)) if low else (pltpu.roll(a, 4, 0), b)
        tiles.append(jnp.where(row < 4, a, b))
    return tiles, (k[4:5] if low else k[3:4])


def pack_kernel(temps, right, exchange, coupling, one, two, early, st, sems):
    even = lax.axis_index("gx") % 2 == 0
    odd = lax.axis_index("gy") % 2 == 1
    ny, nx, nz = exchange.shape
    copies = []
    for k, (plane, ref) in enumerate(
        ((SA, temps.at[0]), (K, exchange), (GA, temps.at[1]), (C, coupling), (RS, right.at[0]), (RG, right.at[1]))
    ):
        to = st.at[plane, pl.ds(1, ny), pl.ds(PAD, nx)]
        copies.append(pltpu.make_async_copy(ref, to, sems.at[k]))
    for copy in copies:
        copy.start()
    for copy in copies:
        copy.wait()
    for i in range(1, ny + 1):
        sides = []
        for start in (PAD, PAD + nx - 8):
            s, g, e, rs, rg, c = (st[plane, i, start : start + 8] for plane in (SA, GA, K, RS, RG, C))
            sides.append(strip_side(s, g, conductivity_of(s, e), rs, rg, c, start == PAD))
        (low, low_k), (high, high_k) = sides
        for p in range(len(PAIRS)):
            part = slice((i - 1) * STRIP_ROWS + 8 * p, (i - 1) * STRIP_ROWS + 8 * p + 8)
            one[part] = jnp.where(even, high[p], low[p])
            two[part] = jnp.where(even, low[p], high[p])
        part = slice(ny * STRIP_ROWS + i - 1, ny * STRIP_ROWS + i)
        one[part] = jnp.where(even, high_k, low_k)
        two[part] = jnp.where(even, low_k, high_k)
    own = slice(PAD, PAD + nx)
    for is_odd, e, d in ((True, ny, ny - 1), (False, 1, 2)):

        @pl.when(odd == is_odd)
        def _():
            s, s_d, g, g_d = st[SA, e, own], st[SA, d, own], st[GA, e, own], st[GA, d, own]
            c, k, k_d = st[C, e, own], conductivity_of(s, st[K, e, own]), conductivity_of(s_d, st[K, d, own])
            fx, fz, h, _ = faces(k)
            fy = 0.5 * (k + k_d)
            part_s, part_g = inner(s, g, c, h, fx, fz, edge_weights((nx, nz)))
            m_1s, m_1g = first_partial(st[RS, e, own] + part_s, st[RG, e, own] + part_g, s, s_d, g, g_d, fy, is_odd)
            for plane, value in enumerate((s, g, k, c, fy, m_1s, m_1g)):
                early[plane] = value


def conduct_kernel(st_in, st):
    del st_in
    planes, rows, ext, nz = st.shape
    own = slice(PAD, ext - PAD)
    for i in range(1, rows - 1):
        st[K, i, own] = conductivity_of(st[SA, i, own], st[K, i, own])


def place_halo(st, one, two, y, nx):
    even = lax.axis_index("gx") % 2 == 0
    ny, row = st.shape[1] - 2, sublanes(st.shape[3])
    i = y + 1

    def received(part):
        a, b = one[part], two[part]
        return jnp.where(even, b, a), jnp.where(even, a, b)

    for p, (plane_a, plane_b) in enumerate(PAIRS):
        before, after = received(slice(y * STRIP_ROWS + 8 * p, y * STRIP_ROWS + 8 * p + 8))
        before = {plane_a: pltpu.roll(before, 4, 0), plane_b: before}
        after = {plane_a: after, plane_b: pltpu.roll(after, 4, 0)}
        for plane in (plane_a, plane_b):
            low, high = jnp.where(row >= 4, before[plane], 0.0), jnp.where(row < 4, after[plane], 0.0)
            if plane == K:
                k_low, k_high = received(slice(ny * STRIP_ROWS + y, ny * STRIP_ROWS + y + 1))
                low, high = jnp.where(row == 3, k_low, low), jnp.where(row == 4, k_high, high)
            st[plane, i, :PAD] = low
            st[plane, i, PAD + nx :] = high


def inner(s, g, c, h, fx, fz, edge):
    t = c * (s - g)
    flux_x = fx * (up_x(s) - s)
    flux_z = fz * (up_z(s) - s)
    part_s = (flux_x - down_x(flux_x)) + (flux_z - down_z(flux_z)) - h * s - t
    part_g = (
        t
        - GAS_SELF * g
        + CONDUCT * (up_x(g) + down_x(g))
        + edge[0] * up_z(g)
        + edge[1] * down_z(g)
    )
    return part_s, part_g


def edge_weights(shape):
    lane = lanes(shape)
    weight = jnp.float32(0.25 * CONDUCT)
    return jnp.where(lane == shape[1] - 1, 0.0, weight), jnp.where(lane == 0, 0.0, weight)


def row_inner(st, i, s_at, edge):
    return inner(st[s_at, i], st[s_at + 1, i], st[C, i], st[H, i], st[FX, i], st[FZ, i], edge)


def row_residual(st, i, s_at, edge):
    part_s, part_g = row_inner(st, i, s_at, edge)
    s, g, before = st[s_at, i], st[s_at + 1, i], st[s_at + 1, i - 1]
    part_s += st[FY, i] * (st[s_at, i + 1] - s) + st[FY, i - 1] * (st[s_at, i - 1] - s)
    part_g += CONDUCT * (st[s_at + 1, i + 1] + before) - FLOW * (g - before)
    return st[RS, i] + part_s, st[RG, i] + part_g


def relaxed(st, i, s_at, res_s, res_g):
    s = st[s_at, i] + st[ASS, i] * res_s + st[ASG, i] * res_g
    g = st[s_at + 1, i] + st[ASG, i] * res_s + st[AGG, i] * res_g
    return s, g


def faces(k):
    lane = lanes(k.shape)
    end = k.shape[1] - 1
    fx = 0.5 * (k + up_x(k))
    fz = jnp.where(lane == end, 0.0, 0.125 * (k + up_z(k)))
    h = SOLID_CAP + jnp.where((lane == 0) | (lane == end), 0.125 * k, 0.0)
    return fx, fz, h, h + (fx + down_x(fx)) + (fz + down_z(fz))


def inverse(diag, c, mask):
    gas_diag = (GAS_SELF + FLOW) + c
    inv = (RELAX * mask) / (diag * gas_diag - c * c)
    return inv * gas_diag, inv * c, inv * diag


def last_relaxed(st, i, s_at, edge, own):
    full_s, full_g = st[s_at, i], st[s_at + 1, i]
    s, g = full_s[own], full_g[own]
    flux_x = st[FX, i] * (up_x(full_s) - full_s)
    flux_z = st[FZ, i, own] * (up_z(s) - s)
    c, before = st[C, i, own], st[s_at + 1, i - 1, own]
    t = c * (s - g)
    res_s = st[RS, i, own] + (flux_x[own] - down_x(flux_x)[own]) + (flux_z - down_z(flux_z)) - st[H, i, own] * s - t
    res_s += st[FY, i, own] * (st[s_at, i + 1, own] - s) + st[FY, i - 1, own] * (st[s_at, i - 1, own] - s)
    res_g = st[RG, i, own] + t - GAS_SELF * g + edge[0][own] * up_z(g) + edge[1][own] * down_z(g)
    res_g += CONDUCT * (up_x(full_g)[own] + down_x(full_g)[own] + st[s_at + 1, i + 1, own] + before) - FLOW * (g - before)
    ss, sg, gg = st[ASS, i, own], st[ASG, i, own], st[AGG, i, own]
    return s + ss * res_s + sg * res_g, g + sg * res_s + gg * res_g


def grouped(rows, work):
    for start in range(0, len(rows), GROUP):
        stores = []
        for i in rows[start : start + GROUP]:
            stores += work(i)
        for ref, at, value in stores:
            ref[at] = value


def looped(first, last, size, work):
    def group(k, carry):
        grouped([first + size * k + r for r in range(size)], work)
        return carry

    lax.fori_loop(0, (last - first) // size, group, 0)
    grouped(list(range(last - (last - first) % size, last)), work)


def row_coefficients(st, i, mask):
    fx, fz, h, diag = faces(st[K, i])
    fy = 0.5 * (st[K, i] + st[K, i + 1])
    before = 0.5 * (st[K, i] + st[K, i - 1])
    ss, sg, gg = inverse(diag + st[C, i] + fy + before, st[C, i], mask)
    values = ((FX, fx), (FZ, fz), (H, h), (FY, fy), (ASS, ss), (ASG, sg), (AGG, gg))
    return [(st, (plane, i), v) for plane, v in values]


def row_sweep(st, i, source, target, edge):
    s, g = relaxed(st, i, source, *row_residual(st, i, source, edge))
    return [(st, (target, i), s), (st, (target + 1, i), g)]


def first_partial(res_s, res_g, s, s_d, g, g_d, fy, onward):
    return res_s + fy * (s_d - s), res_g + CONDUCT * g_d - FLOW * (g - g_d if onward else g)


def send_planes(st, onward, edge):
    ny = st.shape[1] - 2
    e, d, near = (ny, ny - 1, ny - 1) if onward else (1, 2, 1)
    fy, s, g, g_d = st[FY, near], st[SA, e], st[GA, e], st[GA, d]
    part_s, part_g = row_inner(st, e, SA, edge)
    m_1s, m_1g = first_partial(st[RS, e] + part_s, st[RG, e] + part_g, s, st[SA, d], g, g_d, fy, onward)
    m_2s = st[RS, e] + fy * st[SB, d]
    m_2g = st[RG, e] + (CONDUCT + FLOW if onward else CONDUCT) * st[GB, d]
    return [s, g, st[K, e], st[C, e], fy, m_1s, m_1g, m_2s, m_2g]


def across_parts(ext):
    parts, at = [], 0
    for k in range(EARLY, MESSAGE):
        parts.append((k, CROP, ext - CROP, at))
        at += ext - 2 * CROP
    for k in range(EARLY):
        more = 1 if k in (M_1S, M_1G) else 0
        for low, high in ((CROP, PAD + more), (ext - PAD - more, ext - CROP)):
            parts.append((k, low, high, at))
            at += high - low
    return parts, (at + 7) // 8 * 8


def write_across(ref, k, value):
    for plane, low, high, at in across_parts(value.shape[0])[0]:
        if plane == k:
            ref[at : at + high - low] = value[low:high]


def read_across(early, across, outer, k):
    ext = outer.shape[1]
    if k < EARLY:
        outer[k, PAD : ext - PAD] = early[k]
    for plane, low, high, at in across_parts(ext)[0]:
        if plane == k:
            outer[k, low:high] = across[at : at + high - low]


def write_beside(refs, k, value):
    refs[k // THIRD][k % THIRD] = value[CROP : value.shape[0] - CROP]


def read_beside(refs, outer, k):
    outer[k, CROP : outer.shape[1] - CROP] = refs[k // THIRD][k % THIRD]


def first_end(st, one, two, after, write):
    planes, rows, ext, nz = st.shape
    ny, nx = rows - 2, ext - 2 * PAD
    mask = x_mask((ext, nz), nx)
    edge = edge_weights((ext, nz))
    e, d, f = (ny, ny - 1, ny - 2) if after else (1, 2, 3)
    for i in (e, d, f):
        place_halo(st, one, two, i - 1, nx)
    fx, fz, h, diag = faces(st[K, e])
    st[FX, e], st[FZ, e], st[H, e] = fx, fz, h
    st[FY, min(e, d)] = 0.5 * (st[K, e] + st[K, d])
    st[FY, min(d, f)] = 0.5 * (st[K, d] + st[K, f])
    grouped([d], lambda i: row_coefficients(st, i, mask))
    grouped([d], lambda i: row_sweep(st, i, SA, SB, edge))
    for k, value in enumerate(send_planes(st, after, edge)):
        write(k, value)


def either_first(st, one, two, after, write):
    for is_after in (True, False):

        @pl.when(after == is_after)
        def _():
            first_end(st, one, two, is_after, write)


def first_kernel(st_in, one, two, st, across):
    del st_in
    either_first(st, one, two, lax.axis_index("gy") % 2 == 1, functools.partial(write_across, across))


def other_kernel(st_in, one, two, st, *beside):
    del st_in
    either_first(st, one, two, lax.axis_index("gy") % 2 == 0, functools.partial(write_beside, beside))
    planes, rows, ext, nz = st.shape
    ny, nx = rows - 2, ext - 2 * PAD
    mask = x_mask((ext, nz), nx)
    for y in range(3, ny - 3):
        place_halo(st, one, two, y, nx)
    grouped(list(range(3, ny - 1)), lambda i: row_coefficients(st, i, mask))


def outer_residual(st, i, s_at, rs, rg, fy_out, edge, after):
    part_s, part_g = row_inner(st, i, s_at, edge)
    s, g = st[s_at, i], st[s_at + 1, i]
    if after:
        part_s += st[FY, i - 1] * (st[s_at, i - 1] - s)
        part_g += (CONDUCT + FLOW) * st[s_at + 1, i - 1]
    else:
        part_s += st[FY, i] * (st[s_at, i + 1] - s)
        part_g += CONDUCT * st[s_at + 1, i + 1]
    return rs + part_s - fy_out * s, rg + part_g - FLOW * g


def pair_x(v):
    row = lax.broadcasted_iota(jnp.int32, v.shape, 0)
    return v + jnp.where(row % 2 == 0, up_x(v), down_x(v))


def coarse_coefficients(c_sum, k_sum):
    per_solid = 1.0 / (4.0 * SOLID_CAP + c_sum + LUMP * k_sum)
    ratio = c_sum * per_solid
    return per_solid, ratio, 1.0 / ((4.0 * GAS_CAP + 2.0 * FLOW) + c_sum - c_sum * ratio)


def coarse_row(st, coarse, j, mask, edge):
    i = 2 * j + 1
    res_s, res_g = row_residual(st, i, SA, edge)
    more_s, more_g = row_residual(st, i + 1, SA, edge)
    res_s, res_g = pair_x((res_s + more_s) * mask), pair_x((res_g + more_g) * mask)
    c_sum = pair_x(st[C, i] + st[C, i + 1])
    per_solid, ratio, per_gas = coarse_coefficients(c_sum, pair_x(st[K, i] + st[K, i + 1]))
    lead = res_s * per_solid
    values = (lead, ratio, (2.0 * FLOW) * per_gas, (res_g + c_sum * lead) * per_gas)
    return [(coarse, (k, j), v) for k, v in enumerate(values)]


def inner_kernel(st_in, early, st, coarse):
    del st_in, early
    planes, rows, ext, nz = st.shape
    ny, nx = rows - 2, ext - 2 * PAD
    shape = (ext, nz)
    mask = x_mask(shape, nx)
    edge = edge_weights(shape)
    looped(3, ny - 1, 4, lambda i: row_sweep(st, i, SA, SB, edge))
    looped(3, ny - 1, 4, lambda i: row_sweep(st, i, SB, SA, edge))
    grouped(list(range(2, ny // 2 - 2)), lambda j: coarse_row(st, coarse, j, mask, edge))


def end_work(st, coarse, extra, read, outer, is_after):
    planes, rows, ext, nz = st.shape
    ny, nx = rows - 2, ext - 2 * PAD
    me, count = lax.axis_index("gy"), lax.axis_size("gy")
    mask = x_mask((ext, nz), nx)
    inside = jnp.where(me == (count - 1 if is_after else 0), 0.0, mask)
    edge = edge_weights((ext, nz))
    zeros = jnp.zeros((PAD, nz), jnp.float32)
    for k in range(MESSAGE):
        outer[k, :PAD] = zeros
        outer[k, ext - PAD :] = zeros
        read(outer, k)

    o, e, near = (ny + 1, ny, ny) if is_after else (0, 1, 0)
    to_o = CONDUCT + FLOW if is_after else CONDUCT
    s_o, g_o, k_o, c_o, fy_out = (outer[plane] for plane in (M_S, M_G, M_K, M_C, M_FY))
    fy = 0.5 * (k_o + st[K, e])
    fx, fz, h, diag = faces(k_o)
    inv_o = inverse(diag + c_o + fy_out + fy, c_o, inside)
    fx_e, fz_e = st[FX, e], st[FZ, e]
    diag = st[H, e] + (fx_e + down_x(fx_e)) + (fz_e + down_z(fz_e)) + st[C, e] + fy
    inv_e = inverse(diag + st[FY, near - 1 if is_after else near + 1], st[C, e], mask)
    for plane, value in ((SA, s_o), (GA, g_o), (K, k_o), (C, c_o), (FX, fx), (FZ, fz), (H, h)):
        st[plane, o] = value
    st[FY, near] = fy
    for k in range(3):
        st[ASS + k, o], st[ASS + k, e] = inv_o[k], inv_e[k]

    res = outer[M_1S] + fy * (st[SA, e] - s_o), outer[M_1G] + to_o * st[GA, e]
    new_o = relaxed(st, o, SA, *res)
    stores = row_sweep(st, e, SA, SB, edge)
    st[SB, o], st[GB, o] = new_o
    for ref, at, value in stores:
        ref[at] = value
    res = outer_residual(st, o, SB, outer[M_2S], outer[M_2G], fy_out, edge, is_after)
    new_o = relaxed(st, o, SB, *res)
    ends = [e - 1, e] if is_after else [e, e + 1]
    grouped(ends, lambda i: row_sweep(st, i, SB, SA, edge))
    st[SA, o], st[GA, o] = new_o
    for k, plane in enumerate((M_2S, M_2G, M_FY)):
        extra[(3 if is_after else 0) + k] = outer[plane]
    blocks = ny // 2
    stores = []
    for j in (blocks - 2, blocks - 1) if is_after else (0, 1):
        stores += coarse_row(st, coarse, j, mask, edge)
    for ref, at, value in stores:
        ref[at] = value


def either_end(after, st, coarse, extra, read, outer):
    for is_after in (True, False):

        @pl.when(after == is_after)
        def _():
            end_work(st, coarse, extra, read, outer, is_after)


def near_kernel(st_in, coarse_in, *refs):
    beside, (st, coarse, extra, outer) = refs[:-4], refs[-4:]
    del st_in, coarse_in
    either_end(lax.axis_index("gy") % 2 == 0, st, coarse, extra, functools.partial(read_beside, beside), outer)


def second_kernel(st_in, coarse_in, extra_in, early, across, *refs):
    st, coarse, extra, total, last_info, first_info, message, outer, squeeze = refs
    del st_in, coarse_in, extra_in
    planes, rows, ext, nz = st.shape
    ny, nx = rows - 2, ext - 2 * PAD
    me = lax.axis_index("gy")
    either_end(me % 2 == 1, st, coarse, extra, functools.partial(read_across, early, across), outer)

    blocks = ny // 2
    for k in range(4):
        squeeze[k] = coarse[k, 0]
    slopes, offsets = coarse[2, 0], coarse[3, 0]
    for j in range(1, blocks):
        slope = coarse[2, j]
        slopes, offsets = slope * slopes, slope * offsets + coarse[3, j]
        coarse[2, j], coarse[3, j] = slopes, offsets
    squeeze[4], squeeze[5], squeeze[6], squeeze[7] = slopes, offsets, coarse[0, blocks - 1], coarse[1, blocks - 1]

    span = nx // 2 + 2
    lead, ratio, slope, offset, slopes, offsets, lead_last, ratio_last = (
        squeeze[k, pl.ds(PAD - 2, span, 2), :] for k in range(8)
    )
    part = slice(PAD - 1, PAD + nx + 1)

    def increments(d, face, gas):
        return [(st[FY, face] * (st[SA, d] - st[SB, d]))[part], (gas * (st[GA, d] - st[GB, d]))[part]]

    onward = [lead_last, ratio_last] + increments(ny - 1, ny - 1, CONDUCT + FLOW)
    back = [lead, offset] + increments(2, 1, CONDUCT) + [slope, ratio]
    write_rows(total, [slopes, offsets])
    write_rows(last_info, onward)
    write_rows(first_info, back)
    for go, info in ((True, onward), (False, back)):

        @pl.when((me % 2 == 0) == go)
        def _():
            write_rows(message, [slopes, offsets] + info)


def write_rows(ref, values):
    at = 0
    for value in values:
        ref[at : at + value.shape[0]] = value
        at += value.shape[0]


class Rows:
    def __init__(self, nx):
        self.span = nx // 2 + 2
        self.map = 2 * self.span
        self.info = self.map + 2 * (nx + 2)
        self.rest = self.map
        self.final = self.map + self.info
        self.full = self.final + self.rest
        self.low = self.map
        self.high = self.low + self.info
        self.near = self.high + self.info + self.rest


def source(at, k, radix):
    if radix & (radix - 1) == 0:
        return at ^ k
    return (at + radix - k) % radix


def matchings(count, radix, stride):
    if (count, radix, stride) == (8, 4, 2):
        return [
            (((1, 2), (2, 1), (3, 4), (4, 3), (5, 6), (6, 5), (0, 7)), True),
            (((0, 3), (1, 5), (2, 6), (4, 7)), False),
            (((0, 4), (1, 6), (2, 5), (3, 7)), False),
        ]
    out = []
    for k in range(1, radix):
        pairs = []
        for me in range(count):
            at, low = me // stride % radix, me % stride
            pairs.append((me - low + (source(at, k, radix) - at) * stride + (stride - 1 - low), me))
        out.append((tuple(pairs), any(abs(source(at, k, radix) - at) == 1 for at in range(radix))))
    return sorted(out, key=lambda item: not item[1])


def senders_of(pairs, count):
    found = {receiver: sender for sender, receiver in pairs}
    return [found.get(me, -1) for me in range(count)]


def receivers_of(pairs, count):
    found = dict(pairs)
    return [found.get(me, -1) for me in range(count)]


def look_up(table):
    me, value = lax.axis_index("gy"), jnp.int32(table[0])
    for k in range(1, len(table)):
        value = jnp.where(me == k, table[k], value)
    return value


def stages(count):
    if count % 2:
        return [1, count]
    out, rest = [2], count // 2
    while rest > 1:
        radix = next((r for r in (8, 4, 2) if rest % r == 0), rest)
        out.append(radix)
        rest //= radix
    return out if len(out) > 1 else out + [1]


def exchange_stage(messages, swaps):
    return [
        lax.ppermute(message, "gy", list(pairs)) for (pairs, near), message in zip(swaps, messages)
    ]


class Group:
    def __init__(self, radix, stride, others, nx):
        self.radix, self.others, self.nx = radix, others, nx
        me = lax.axis_index("gy")
        count = lax.axis_size("gy")
        self.swaps = []
        for pairs, near in matchings(count, radix, stride):
            places = [radix + 1 if sender < 0 else sender // stride % radix for sender in senders_of(pairs, count)]
            self.swaps.append((look_up(places), near))
        self.at = lax.rem(lax.div(me, stride), radix)
        low = lax.rem(me, stride)
        self.lowest, self.highest = low == 0, low == stride - 1

    def map_of(self, place, own):
        rows = Rows(self.nx)
        out = own
        for (sender, near), ref in zip(self.swaps, self.others):
            here = sender == place
            got = [ref[i * rows.span : (i + 1) * rows.span] for i in range(2)]
            out = got if out is None else [jnp.where(here, new, old) for new, old in zip(got, out)]
        return out

    def ahead(self, slope, offset):
        a, b = jnp.ones_like(slope), jnp.zeros_like(slope)
        for place in range(self.radix - 1):
            new_a, new_b = self.map_of(place, None)
            below = place < self.at
            a, b = jnp.where(below, new_a * a, a), jnp.where(below, new_a * b + new_b, b)
        return slope * a, slope * b + offset

    def total(self, own):
        a, b = self.map_of(0, own)
        for place in range(1, self.radix):
            new_a, new_b = self.map_of(place, own)
            a, b = new_a * a, new_a * b + new_b
        return a, b

    def collect(self, near, final):
        rows = Rows(self.nx)
        for (place, adjacent), ref in zip(self.swaps, self.others):
            if not adjacent:
                continue

            @pl.when(self.lowest & (place == self.at - 1))
            def _():
                near[rows.low : rows.low + rows.info] = ref[rows.map : rows.final]

            @pl.when(self.highest & (place == self.at + 1))
            def _():
                near[rows.high : rows.high + rows.info] = ref[rows.map : rows.final]
                rest = slice(0, rows.map) if final else slice(rows.final, rows.full)
                near[rows.high + rows.info : rows.near] = ref[rest]


def start_near(near, nx, nz):
    rows = Rows(nx)
    near[: rows.span] = jnp.ones((rows.span, nz), jnp.float32)
    near[rows.span :] = jnp.zeros((near.shape[0] - rows.span, nz), jnp.float32)


def join_kernel(radix, stride, final, nx, is_first, *refs):
    rows = Rows(nx)
    total, last_info, first_info, near_in = refs[:4]
    others, near, outs = refs[4 : 3 + radix], refs[3 + radix], refs[4 + radix :]
    nz = near.shape[1]
    if is_first:
        start_near(near, nx, nz)
    else:
        near[...] = near_in[...]
    group = Group(radix, stride, others, nx)
    own = [total[i * rows.span : (i + 1) * rows.span] for i in range(2)]
    ahead = group.ahead(near[: rows.span], near[rows.span : rows.map])
    write_rows(near, ahead)
    group.collect(near, False)
    whole = group.total(own)
    if final == 0:
        write_rows(outs[0], whole)
        return
    me, count = lax.axis_index("gy"), lax.axis_size("gy")
    for (pairs, adjacent), out in zip(matchings(count, final, stride * radix), outs):
        up = look_up(receivers_of(pairs, count)) > me
        if not adjacent:
            write_rows(out, whole)
            continue

        @pl.when(up)
        def _():
            write_rows(out, whole)
            out[rows.map : rows.final] = last_info[: rows.info]

        @pl.when(jnp.logical_not(up))
        def _():
            out[: rows.map] = first_info[rows.info : rows.info + rows.rest]
            out[rows.map : rows.final] = first_info[: rows.info]


def full_message(nx, total, last_info, first_info, receivers):
    rows = Rows(nx)
    onward = jnp.concatenate([total[: rows.map], last_info[: rows.info], first_info[rows.info : rows.info + rows.rest]])
    back = jnp.concatenate([total[: rows.map], first_info[: rows.info + rows.rest]])
    message = jnp.where(look_up(receivers) > lax.axis_index("gy"), onward, back)
    return jnp.pad(message, ((0, -rows.full % 8), (0, 0)))


def third_kernel(radix, stride, *refs):
    st, extra, coarse, near_in = refs[:4]
    others, (out, sc, wide, near, done, sems) = refs[4 : 3 + radix], refs[3 + radix :]
    planes, rows, ext, nz = st.shape
    ny, nx = rows - 2, ext - 2 * PAD
    edge = edge_weights((ext, nz))
    blocks = ny // 2

    lay = Rows(nx)
    span = lay.span
    near[...] = near_in[...]
    group = Group(radix, stride, others, nx)
    if radix > 1:
        group.collect(near, True)
    gas_in = group.ahead(near[:span], near[span : lay.map])[1]
    at_high = lay.high + lay.info
    starts = [lay.low, lay.low + span, lay.high, lay.high + span, at_high, at_high + span]
    for k, v in enumerate([gas_in] + [near[start : start + span] for start in starts]):
        wide[k, : PAD - 2] = jnp.zeros((PAD - 2, nz), jnp.float32)
        wide[k, ext - PAD + 2 :] = jnp.zeros((PAD - 2, nz), jnp.float32)
        wide[k, pl.ds(PAD - 2, span, 2), :] = v
        wide[k, pl.ds(PAD - 1, span, 2), :] = v
    for k, start in enumerate((lay.low, lay.low + nx + 2, lay.high, lay.high + nx + 2)):
        start += lay.map
        wide[7 + k, :PAD] = jnp.zeros((PAD, nz), jnp.float32)
        wide[7 + k, ext - PAD :] = jnp.zeros((PAD, nz), jnp.float32)
        wide[7 + k, PAD - 1 : PAD + nx + 1] = near[start : start + nx + 2]

    gas_in = wide[0]
    last = ny + 1
    solid_low = wide[1] + wide[2] * gas_in
    sc[0, 0] = st[SA, 0] + solid_low
    sc[1, 0] = st[GA, 0] + gas_in

    def correct(j, carry):
        gas = coarse[2, j] * gas_in + coarse[3, j]
        solid = coarse[0, j] + coarse[1, j] * gas
        for i in (2 * j + 1, 2 * j + 2):
            sc[0, i] = st[SA, i] + solid
            sc[1, i] = st[GA, i] + gas
        return carry

    lax.fori_loop(0, blocks, correct, 0)
    gas = coarse[2, blocks - 1] * gas_in + coarse[3, blocks - 1]
    gas_high = wide[5] * gas + wide[4]
    solid_high = wide[3] + wide[6] * gas_high
    sc[0, last] = st[SA, last] + solid_high
    sc[1, last] = st[GA, last] + gas_high

    view = Fields(st, sc)
    for i, is_after, solid, gas in ((0, False, solid_low, gas_in), (last, True, solid_high, gas_high)):
        side = 3 if is_after else 0
        fy = extra[side + 2]
        to = 9 if is_after else 7
        rs = extra[side] + wide[to] + fy * solid
        rg = extra[side + 1] + wide[to + 1] + (CONDUCT if is_after else CONDUCT + FLOW) * gas
        res = outer_residual(view, i, SA, rs, rg, fy, edge, is_after)
        sc[2, i], sc[3, i] = relaxed(view, i, SA, *res)

    def sweep(k, carry):
        stores = []
        for r in range(GROUP):
            i = GROUP * k + 1 + r
            new_s, new_g = relaxed(view, i, SA, *row_residual(view, i, SA, edge))
            stores += [((2, i), new_s), ((3, i), new_g)]
        for at, value in stores:
            sc[at] = value
        return carry

    lax.fori_loop(0, ny // GROUP, sweep, 0)

    def leaving(k):
        part = pl.ds(GROUP * k, GROUP)
        return pltpu.make_async_copy(done.at[:, part], out.at[:, part], sems.at[k])

    def final(k, carry):
        stores = []
        for r in range(GROUP):
            i = GROUP * k + 1 + r
            new_s, new_g = last_relaxed(view, i, SB, edge, slice(PAD, PAD + nx))
            stores += [((0, i - 1), new_s), ((1, i - 1), new_g)]
        for at, value in stores:
            done[at] = value
        leaving(k).start()
        return carry

    lax.fori_loop(0, ny // GROUP, final, 0)
    for k in range(ny // GROUP):
        leaving(k).wait()


class Fields:
    def __init__(self, st, sc):
        self.st, self.sc = st, sc

    def __getitem__(self, at):
        return (self.sc if at[0] <= GB else self.st)[at]


def cost(rows, cells):
    return pl.CostEstimate(flops=50 * rows * cells, bytes_accessed=16 * 4 * rows * cells, transcendentals=0)


def swap(x, axis, first):
    pairs = []
    for i in range(first, lax.axis_size(axis) - 1, 2):
        pairs += [(i, i + 1), (i + 1, i)]
    return lax.ppermute(x, axis, pairs)


def shards(temps, right_side, exchange, coupling):
    temps, right_side = (jnp.transpose(a, (0, 2, 1, 3)) for a in (temps, right_side))
    exchange, coupling = (jnp.transpose(a, (1, 0, 2)) for a in (exchange, coupling))
    temps, right_side, exchange, coupling = (
        pltpu.with_memory_space_constraint(a, pltpu.HBM) for a in (temps, right_side, exchange, coupling)
    )
    ny, nx, nz = exchange.shape
    ext = nx + 2 * PAD
    f32 = functools.partial(jax.ShapeDtypeStruct, dtype=jnp.float32)

    strip = f32((strip_height(ny), nz))
    state = f32((PLANES, ny + 2, ext, nz))
    one, two, early, st = pl.pallas_call(
        pack_kernel,
        out_shape=(strip, strip, f32((EARLY, nx, nz)), state),
        in_specs=[HBM] * 4,
        out_specs=(VMEM,) * 4,
        scratch_shapes=[pltpu.SemaphoreType.DMA((6,))],
        compiler_params=PARAMS,
        name="pack_x",
    )(temps, right_side, exchange, coupling)
    one, two = swap(one, "gx", 0), swap(two, "gx", 1)
    early = swap(early, "gy", 1)

    def letter(planes):
        return f32((planes, ext - 2 * CROP, nz))

    st = pl.pallas_call(
        conduct_kernel,
        out_shape=state,
        in_specs=[VMEM],
        out_specs=VMEM,
        input_output_aliases={0: 0},
        compiler_params=PARAMS,
        cost_estimate=cost(2 * ny, ext * nz),
        name="conduct",
    )(st)
    st, across = pl.pallas_call(
        first_kernel,
        out_shape=(state, f32((across_parts(ext)[1], nz))),
        in_specs=[VMEM] * 3,
        out_specs=(VMEM,) * 2,
        input_output_aliases={0: 0},
        compiler_params=PARAMS,
        name="first",
    )(st, one, two)
    st, *beside = pl.pallas_call(
        other_kernel,
        out_shape=(state,) + (letter(THIRD),) * (MESSAGE // THIRD),
        in_specs=[VMEM] * 3,
        out_specs=(VMEM,) * (1 + MESSAGE // THIRD),
        input_output_aliases={0: 0},
        compiler_params=PARAMS,
        name="other",
    )(st, one, two)
    across = swap(across, "gy", 1)

    rows = f32((4, ny // 2, ext, nz))
    st, coarse = pl.pallas_call(
        inner_kernel,
        out_shape=(state, rows),
        in_specs=[VMEM] * 2,
        out_specs=(VMEM,) * 2,
        input_output_aliases={0: 0},
        compiler_params=PARAMS,
        cost_estimate=cost(4 * ny, ext * nz),
        name="inner",
    )(st, early)

    beside = [swap(part, "gy", 0) for part in beside]

    lay = Rows(nx)

    def tall(height):
        return f32(((height + 7) // 8 * 8, nz))

    letter_room = pltpu.VMEM((MESSAGE, ext, nz), jnp.float32)
    more = f32((6, ext, nz))
    st, coarse, extra = pl.pallas_call(
        near_kernel,
        out_shape=(state, rows, more),
        in_specs=[VMEM] * (2 + len(beside)),
        out_specs=(VMEM,) * 3,
        scratch_shapes=[letter_room],
        input_output_aliases={0: 0, 1: 1},
        compiler_params=PARAMS,
        name="near",
    )(st, coarse, *beside)
    st, coarse, extra, total, last_info, first_info, message = pl.pallas_call(
        second_kernel,
        out_shape=(state, rows, more, tall(lay.map), tall(lay.info), tall(lay.info + lay.rest), tall(lay.full)),
        in_specs=[VMEM] * 5,
        out_specs=(VMEM,) * 7,
        scratch_shapes=[letter_room, pltpu.VMEM((8, ext, nz), jnp.float32)],
        input_output_aliases={0: 0, 1: 1, 2: 2},
        compiler_params=PARAMS,
        name="second",
    )(st, coarse, extra, early, across)

    near, messages = total, [message]
    count = lax.axis_size("gy")
    radices, stride = stages(count), 1
    for place, radix in enumerate(radices[:-1]):
        swaps = matchings(count, radix, stride)
        if place:
            messages = [full_message(nx, total, last_info, first_info, receivers_of(pairs, count)) for pairs, _ in swaps]
        others = exchange_stage(messages, swaps)
        final = radices[-1] if place == len(radices) - 2 else 0
        following = matchings(count, final, stride * radix) if final else []
        outs = [tall(lay.final if adjacent else lay.map) for _, adjacent in following] if final else [tall(lay.map)]
        near, *messages = pl.pallas_call(
            functools.partial(join_kernel, radix, stride, final, nx, place == 0),
            out_shape=(tall(lay.near), *outs),
            in_specs=[VMEM] * (3 + radix),
            out_specs=(VMEM,) * (1 + len(outs)),
            compiler_params=PARAMS,
            name="join",
        )(total, last_info, first_info, near, *others)
        total = total if final else messages[0]
        stride *= radix
    got = exchange_stage(messages, matchings(count, radices[-1], stride))

    out = pl.pallas_call(
        functools.partial(third_kernel, radices[-1], stride),
        out_shape=f32((2, ny, nx, nz)),
        in_specs=[VMEM] * (4 + len(got)),
        out_specs=HBM,
        scratch_shapes=[
            pltpu.VMEM((4, ny + 2, ext, nz), jnp.float32),
            pltpu.VMEM((11, ext, nz), jnp.float32),
            pltpu.VMEM(tall(lay.near).shape, jnp.float32),
            pltpu.VMEM((2, ny, nx, nz), jnp.float32),
            pltpu.SemaphoreType.DMA((ny // GROUP,)),
        ],
        compiler_params=PARAMS,
        name="third",
    )(st, extra, coarse, near, *got)
    return jnp.transpose(out, (0, 2, 1, 3))


def solution(mesh):
    return jax.shard_map(
        shards,
        mesh=mesh,
        in_specs=(
            P(None, "gx", "gy", None),
            P(None, "gx", "gy", None),
            P("gx", "gy", None),
            P("gx", "gy", None),
        ),
        out_specs=P(None, "gx", "gy", None),
        check_vma=False,
    )
```

```python
import functools

import jax
import jax.numpy as jnp
from jax import lax
from jax.experimental import pallas as pl
from jax.experimental.pallas import tpu as pltpu
from jax.sharding import PartitionSpec as P

SOLID_CAP, GAS_CAP, FLOW, CONDUCT, RELAX, LUMP = 0.5, 0.02, 40.0, 0.05, 0.8, 0.25
GAS_SELF = GAS_CAP + 4.5 * CONDUCT

PAD = 8
WX = 5
CROP = 4
(SA, GA, SB, GB, K, C, RS, RG, FX, FZ, H, FY, ASS, ASG, AGG) = range(15)
PLANES = 15
(M_S, M_G, M_K, M_C, M_FY, M_1S, M_1G, M_2S, M_2G) = range(9)
MESSAGE, EARLY, THIRD = 9, 7, 3

GROUP = 6

VMEM = pl.BlockSpec(memory_space=pltpu.VMEM)
HBM = pl.BlockSpec(memory_space=pltpu.HBM)
PARAMS = pltpu.CompilerParams(vmem_limit_bytes=40 * 1024 * 1024)


def up_x(v):
    return pltpu.roll(v, v.shape[0] - 1, 0)


def down_x(v):
    return pltpu.roll(v, 1, 0)


def up_z(v):
    return pltpu.roll(v, v.shape[1] - 1, 1)


def down_z(v):
    return pltpu.roll(v, 1, 1)


def lanes(shape):
    return lax.broadcasted_iota(jnp.int32, shape, 1)


def x_mask(shape, nx):
    row = lax.broadcasted_iota(jnp.int32, shape, 0)
    place, count = lax.axis_index("gx"), lax.axis_size("gx")
    low = jnp.where(place == 0, PAD, PAD - WX)
    high = jnp.where(place == count - 1, PAD + nx, PAD + nx + WX)
    return jnp.where((row >= low) & (row < high), 1.0, 0.0).astype(jnp.float32)


PAIRS = ((SA, GA), (C, RS), (RG, K))
STRIP_ROWS = 8 * len(PAIRS)


def strip_height(ny):
    return ny * STRIP_ROWS + (ny + 7) // 8 * 8


def sublanes(nz):
    return lax.broadcasted_iota(jnp.int32, (8, nz), 0)


def conductivity_of(s, exchange):
    return 1.0 + 4.0 * exchange * s * s * s


def strip_side(s, g, k, rs, rg, c, low):
    row = sublanes(s.shape[1])
    inn, shift = (3, 7) if low else (4, 1)
    k_out, s_out, g_out = (pltpu.roll(v, shift, 0) for v in (k, s, g))
    rs = rs + jnp.where(row == inn, 0.5 * (k + k_out) * s_out, 0.0)
    rg = rg + jnp.where(row == inn, CONDUCT * g_out, 0.0)
    values = {SA: s, GA: g, K: k, RS: rs, RG: rg, C: c}
    tiles = []
    for a, b in PAIRS:
        a, b = values[a], values[b]
        a, b = (a, pltpu.roll(b, 4, 0)) if low else (pltpu.roll(a, 4, 0), b)
        tiles.append(jnp.where(row < 4, a, b))
    return tiles, (k[4:5] if low else k[3:4])


def pack_kernel(temps, right, exchange, coupling, one, two, early, st, sems):
    even = lax.axis_index("gx") % 2 == 0
    odd = lax.axis_index("gy") % 2 == 1
    ny, nx, nz = exchange.shape
    copies = []
    for k, (plane, ref) in enumerate(
        ((SA, temps.at[0]), (K, exchange), (GA, temps.at[1]), (C, coupling), (RS, right.at[0]), (RG, right.at[1]))
    ):
        to = st.at[plane, pl.ds(1, ny), pl.ds(PAD, nx)]
        copies.append(pltpu.make_async_copy(ref, to, sems.at[k]))
    for copy in copies:
        copy.start()
    for copy in copies:
        copy.wait()
    for i in range(1, ny + 1):
        sides = []
        for start in (PAD, PAD + nx - 8):
            s, g, e, rs, rg, c = (st[plane, i, start : start + 8] for plane in (SA, GA, K, RS, RG, C))
            sides.append(strip_side(s, g, conductivity_of(s, e), rs, rg, c, start == PAD))
        (low, low_k), (high, high_k) = sides
        for p in range(len(PAIRS)):
            part = slice((i - 1) * STRIP_ROWS + 8 * p, (i - 1) * STRIP_ROWS + 8 * p + 8)
            one[part] = jnp.where(even, high[p], low[p])
            two[part] = jnp.where(even, low[p], high[p])
        part = slice(ny * STRIP_ROWS + i - 1, ny * STRIP_ROWS + i)
        one[part] = jnp.where(even, high_k, low_k)
        two[part] = jnp.where(even, low_k, high_k)
    own = slice(PAD, PAD + nx)
    for is_odd, e, d in ((True, ny, ny - 1), (False, 1, 2)):

        @pl.when(odd == is_odd)
        def _():
            s, s_d, g, g_d = st[SA, e, own], st[SA, d, own], st[GA, e, own], st[GA, d, own]
            c, k, k_d = st[C, e, own], conductivity_of(s, st[K, e, own]), conductivity_of(s_d, st[K, d, own])
            fx, fz, h, _ = faces(k)
            fy = 0.5 * (k + k_d)
            part_s, part_g = inner(s, g, c, h, fx, fz, edge_weights((nx, nz)))
            m_1s, m_1g = first_partial(st[RS, e, own] + part_s, st[RG, e, own] + part_g, s, s_d, g, g_d, fy, is_odd)
            for plane, value in enumerate((s, g, k, c, fy, m_1s, m_1g)):
                early[plane] = value


def conduct_kernel(st_in, st):
    del st_in
    planes, rows, ext, nz = st.shape
    own = slice(PAD, ext - PAD)
    for i in range(1, rows - 1):
        st[K, i, own] = conductivity_of(st[SA, i, own], st[K, i, own])


def place_halo(st, one, two, y, nx):
    even = lax.axis_index("gx") % 2 == 0
    ny, row = st.shape[1] - 2, sublanes(st.shape[3])
    i = y + 1

    def received(part):
        a, b = one[part], two[part]
        return jnp.where(even, b, a), jnp.where(even, a, b)

    for p, (plane_a, plane_b) in enumerate(PAIRS):
        before, after = received(slice(y * STRIP_ROWS + 8 * p, y * STRIP_ROWS + 8 * p + 8))
        before = {plane_a: pltpu.roll(before, 4, 0), plane_b: before}
        after = {plane_a: after, plane_b: pltpu.roll(after, 4, 0)}
        for plane in (plane_a, plane_b):
            low, high = jnp.where(row >= 4, before[plane], 0.0), jnp.where(row < 4, after[plane], 0.0)
            if plane == K:
                k_low, k_high = received(slice(ny * STRIP_ROWS + y, ny * STRIP_ROWS + y + 1))
                low, high = jnp.where(row == 3, k_low, low), jnp.where(row == 4, k_high, high)
            st[plane, i, :PAD] = low
            st[plane, i, PAD + nx :] = high


def inner(s, g, c, h, fx, fz, edge):
    t = c * (s - g)
    flux_x = fx * (up_x(s) - s)
    flux_z = fz * (up_z(s) - s)
    part_s = (flux_x - down_x(flux_x)) + (flux_z - down_z(flux_z)) - h * s - t
    part_g = (
        t
        - GAS_SELF * g
        + CONDUCT * (up_x(g) + down_x(g))
        + edge[0] * up_z(g)
        + edge[1] * down_z(g)
    )
    return part_s, part_g


def edge_weights(shape):
    lane = lanes(shape)
    weight = jnp.float32(0.25 * CONDUCT)
    return jnp.where(lane == shape[1] - 1, 0.0, weight), jnp.where(lane == 0, 0.0, weight)


def row_inner(st, i, s_at, edge):
    return inner(st[s_at, i], st[s_at + 1, i], st[C, i], st[H, i], st[FX, i], st[FZ, i], edge)


def row_residual(st, i, s_at, edge):
    part_s, part_g = row_inner(st, i, s_at, edge)
    s, g, before = st[s_at, i], st[s_at + 1, i], st[s_at + 1, i - 1]
    part_s += st[FY, i] * (st[s_at, i + 1] - s) + st[FY, i - 1] * (st[s_at, i - 1] - s)
    part_g += CONDUCT * (st[s_at + 1, i + 1] + before) - FLOW * (g - before)
    return st[RS, i] + part_s, st[RG, i] + part_g


def relaxed(st, i, s_at, res_s, res_g):
    s = st[s_at, i] + st[ASS, i] * res_s + st[ASG, i] * res_g
    g = st[s_at + 1, i] + st[ASG, i] * res_s + st[AGG, i] * res_g
    return s, g


def faces(k):
    lane = lanes(k.shape)
    end = k.shape[1] - 1
    fx = 0.5 * (k + up_x(k))
    fz = jnp.where(lane == end, 0.0, 0.125 * (k + up_z(k)))
    h = SOLID_CAP + jnp.where((lane == 0) | (lane == end), 0.125 * k, 0.0)
    return fx, fz, h, h + (fx + down_x(fx)) + (fz + down_z(fz))


def inverse(diag, c, mask):
    gas_diag = (GAS_SELF + FLOW) + c
    inv = (RELAX * mask) / (diag * gas_diag - c * c)
    return inv * gas_diag, inv * c, inv * diag


def last_relaxed(st, i, s_at, edge, own):
    full_s, full_g = st[s_at, i], st[s_at + 1, i]
    s, g = full_s[own], full_g[own]
    flux_x = st[FX, i] * (up_x(full_s) - full_s)
    flux_z = st[FZ, i, own] * (up_z(s) - s)
    c, before = st[C, i, own], st[s_at + 1, i - 1, own]
    t = c * (s - g)
    res_s = st[RS, i, own] + (flux_x[own] - down_x(flux_x)[own]) + (flux_z - down_z(flux_z)) - st[H, i, own] * s - t
    res_s += st[FY, i, own] * (st[s_at, i + 1, own] - s) + st[FY, i - 1, own] * (st[s_at, i - 1, own] - s)
    res_g = st[RG, i, own] + t - GAS_SELF * g + edge[0][own] * up_z(g) + edge[1][own] * down_z(g)
    res_g += CONDUCT * (up_x(full_g)[own] + down_x(full_g)[own] + st[s_at + 1, i + 1, own] + before) - FLOW * (g - before)
    ss, sg, gg = st[ASS, i, own], st[ASG, i, own], st[AGG, i, own]
    return s + ss * res_s + sg * res_g, g + sg * res_s + gg * res_g


def grouped(rows, work):
    for start in range(0, len(rows), GROUP):
        stores = []
        for i in rows[start : start + GROUP]:
            stores += work(i)
        for ref, at, value in stores:
            ref[at] = value


def looped(first, last, size, work):
    def group(k, carry):
        grouped([first + size * k + r for r in range(size)], work)
        return carry

    lax.fori_loop(0, (last - first) // size, group, 0)
    grouped(list(range(last - (last - first) % size, last)), work)


def row_coefficients(st, i, mask):
    fx, fz, h, diag = faces(st[K, i])
    fy = 0.5 * (st[K, i] + st[K, i + 1])
    before = 0.5 * (st[K, i] + st[K, i - 1])
    ss, sg, gg = inverse(diag + st[C, i] + fy + before, st[C, i], mask)
    values = ((FX, fx), (FZ, fz), (H, h), (FY, fy), (ASS, ss), (ASG, sg), (AGG, gg))
    return [(st, (plane, i), v) for plane, v in values]


def row_sweep(st, i, source, target, edge):
    s, g = relaxed(st, i, source, *row_residual(st, i, source, edge))
    return [(st, (target, i), s), (st, (target + 1, i), g)]


def first_partial(res_s, res_g, s, s_d, g, g_d, fy, onward):
    return res_s + fy * (s_d - s), res_g + CONDUCT * g_d - FLOW * (g - g_d if onward else g)


def send_planes(st, onward, edge):
    ny = st.shape[1] - 2
    e, d, near = (ny, ny - 1, ny - 1) if onward else (1, 2, 1)
    fy, s, g, g_d = st[FY, near], st[SA, e], st[GA, e], st[GA, d]
    part_s, part_g = row_inner(st, e, SA, edge)
    m_1s, m_1g = first_partial(st[RS, e] + part_s, st[RG, e] + part_g, s, st[SA, d], g, g_d, fy, onward)
    m_2s = st[RS, e] + fy * st[SB, d]
    m_2g = st[RG, e] + (CONDUCT + FLOW if onward else CONDUCT) * st[GB, d]
    return [s, g, st[K, e], st[C, e], fy, m_1s, m_1g, m_2s, m_2g]


def across_parts(ext):
    parts, at = [], 0
    for k in range(EARLY, MESSAGE):
        parts.append((k, CROP, ext - CROP, at))
        at += ext - 2 * CROP
    for k in range(EARLY):
        more = 1 if k in (M_1S, M_1G) else 0
        for low, high in ((CROP, PAD + more), (ext - PAD - more, ext - CROP)):
            parts.append((k, low, high, at))
            at += high - low
    return parts, (at + 7) // 8 * 8


def write_across(ref, k, value):
    for plane, low, high, at in across_parts(value.shape[0])[0]:
        if plane == k:
            ref[at : at + high - low] = value[low:high]


def read_across(early, across, outer, k):
    ext = outer.shape[1]
    if k < EARLY:
        outer[k, PAD : ext - PAD] = early[k]
    for plane, low, high, at in across_parts(ext)[0]:
        if plane == k:
            outer[k, low:high] = across[at : at + high - low]


def write_beside(refs, k, value):
    refs[k // THIRD][k % THIRD] = value[CROP : value.shape[0] - CROP]


def read_beside(refs, outer, k):
    outer[k, CROP : outer.shape[1] - CROP] = refs[k // THIRD][k % THIRD]


def first_end(st, one, two, after, write):
    planes, rows, ext, nz = st.shape
    ny, nx = rows - 2, ext - 2 * PAD
    mask = x_mask((ext, nz), nx)
    edge = edge_weights((ext, nz))
    e, d, f = (ny, ny - 1, ny - 2) if after else (1, 2, 3)
    for i in (e, d, f):
        place_halo(st, one, two, i - 1, nx)
    fx, fz, h, diag = faces(st[K, e])
    st[FX, e], st[FZ, e], st[H, e] = fx, fz, h
    st[FY, min(e, d)] = 0.5 * (st[K, e] + st[K, d])
    st[FY, min(d, f)] = 0.5 * (st[K, d] + st[K, f])
    grouped([d], lambda i: row_coefficients(st, i, mask))
    grouped([d], lambda i: row_sweep(st, i, SA, SB, edge))
    for k, value in enumerate(send_planes(st, after, edge)):
        write(k, value)


def either_first(st, one, two, after, write):
    for is_after in (True, False):

        @pl.when(after == is_after)
        def _():
            first_end(st, one, two, is_after, write)


def first_kernel(st_in, one, two, st, across):
    del st_in
    either_first(st, one, two, lax.axis_index("gy") % 2 == 1, functools.partial(write_across, across))


def other_kernel(st_in, one, two, st, *beside):
    del st_in
    either_first(st, one, two, lax.axis_index("gy") % 2 == 0, functools.partial(write_beside, beside))
    planes, rows, ext, nz = st.shape
    ny, nx = rows - 2, ext - 2 * PAD
    mask = x_mask((ext, nz), nx)
    for y in range(3, ny - 3):
        place_halo(st, one, two, y, nx)
    grouped(list(range(3, ny - 1)), lambda i: row_coefficients(st, i, mask))


def outer_residual(st, i, s_at, rs, rg, fy_out, edge, after):
    part_s, part_g = row_inner(st, i, s_at, edge)
    s, g = st[s_at, i], st[s_at + 1, i]
    if after:
        part_s += st[FY, i - 1] * (st[s_at, i - 1] - s)
        part_g += (CONDUCT + FLOW) * st[s_at + 1, i - 1]
    else:
        part_s += st[FY, i] * (st[s_at, i + 1] - s)
        part_g += CONDUCT * st[s_at + 1, i + 1]
    return rs + part_s - fy_out * s, rg + part_g - FLOW * g


def pair_x(v):
    row = lax.broadcasted_iota(jnp.int32, v.shape, 0)
    return v + jnp.where(row % 2 == 0, up_x(v), down_x(v))


def coarse_coefficients(c_sum, k_sum):
    per_solid = 1.0 / (4.0 * SOLID_CAP + c_sum + LUMP * k_sum)
    ratio = c_sum * per_solid
    return per_solid, ratio, 1.0 / ((4.0 * GAS_CAP + 2.0 * FLOW) + c_sum - c_sum * ratio)


def coarse_row(st, coarse, j, mask, edge):
    i = 2 * j + 1
    res_s, res_g = row_residual(st, i, SA, edge)
    more_s, more_g = row_residual(st, i + 1, SA, edge)
    res_s, res_g = pair_x((res_s + more_s) * mask), pair_x((res_g + more_g) * mask)
    c_sum = pair_x(st[C, i] + st[C, i + 1])
    per_solid, ratio, per_gas = coarse_coefficients(c_sum, pair_x(st[K, i] + st[K, i + 1]))
    lead = res_s * per_solid
    values = (lead, ratio, (2.0 * FLOW) * per_gas, (res_g + c_sum * lead) * per_gas)
    return [(coarse, (k, j), v) for k, v in enumerate(values)]


def inner_kernel(st_in, early, st, coarse):
    del st_in, early
    planes, rows, ext, nz = st.shape
    ny, nx = rows - 2, ext - 2 * PAD
    shape = (ext, nz)
    mask = x_mask(shape, nx)
    edge = edge_weights(shape)
    looped(3, ny - 1, 4, lambda i: row_sweep(st, i, SA, SB, edge))
    looped(3, ny - 1, 4, lambda i: row_sweep(st, i, SB, SA, edge))
    grouped(list(range(2, ny // 2 - 2)), lambda j: coarse_row(st, coarse, j, mask, edge))


def end_work(st, coarse, extra, read, outer, is_after):
    planes, rows, ext, nz = st.shape
    ny, nx = rows - 2, ext - 2 * PAD
    me, count = lax.axis_index("gy"), lax.axis_size("gy")
    mask = x_mask((ext, nz), nx)
    inside = jnp.where(me == (count - 1 if is_after else 0), 0.0, mask)
    edge = edge_weights((ext, nz))
    zeros = jnp.zeros((PAD, nz), jnp.float32)
    for k in range(MESSAGE):
        outer[k, :PAD] = zeros
        outer[k, ext - PAD :] = zeros
        read(outer, k)

    o, e, near = (ny + 1, ny, ny) if is_after else (0, 1, 0)
    to_o = CONDUCT + FLOW if is_after else CONDUCT
    s_o, g_o, k_o, c_o, fy_out = (outer[plane] for plane in (M_S, M_G, M_K, M_C, M_FY))
    fy = 0.5 * (k_o + st[K, e])
    fx, fz, h, diag = faces(k_o)
    inv_o = inverse(diag + c_o + fy_out + fy, c_o, inside)
    fx_e, fz_e = st[FX, e], st[FZ, e]
    diag = st[H, e] + (fx_e + down_x(fx_e)) + (fz_e + down_z(fz_e)) + st[C, e] + fy
    inv_e = inverse(diag + st[FY, near - 1 if is_after else near + 1], st[C, e], mask)
    for plane, value in ((SA, s_o), (GA, g_o), (K, k_o), (C, c_o), (FX, fx), (FZ, fz), (H, h)):
        st[plane, o] = value
    st[FY, near] = fy
    for k in range(3):
        st[ASS + k, o], st[ASS + k, e] = inv_o[k], inv_e[k]

    res = outer[M_1S] + fy * (st[SA, e] - s_o), outer[M_1G] + to_o * st[GA, e]
    new_o = relaxed(st, o, SA, *res)
    stores = row_sweep(st, e, SA, SB, edge)
    st[SB, o], st[GB, o] = new_o
    for ref, at, value in stores:
        ref[at] = value
    res = outer_residual(st, o, SB, outer[M_2S], outer[M_2G], fy_out, edge, is_after)
    new_o = relaxed(st, o, SB, *res)
    ends = [e - 1, e] if is_after else [e, e + 1]
    grouped(ends, lambda i: row_sweep(st, i, SB, SA, edge))
    st[SA, o], st[GA, o] = new_o
    for k, plane in enumerate((M_2S, M_2G, M_FY)):
        extra[(3 if is_after else 0) + k] = outer[plane]
    blocks = ny // 2
    stores = []
    for j in (blocks - 2, blocks - 1) if is_after else (0, 1):
        stores += coarse_row(st, coarse, j, mask, edge)
    for ref, at, value in stores:
        ref[at] = value


def either_end(after, st, coarse, extra, read, outer):
    for is_after in (True, False):

        @pl.when(after == is_after)
        def _():
            end_work(st, coarse, extra, read, outer, is_after)


def near_kernel(st_in, coarse_in, *refs):
    beside, (st, coarse, extra, outer) = refs[:-4], refs[-4:]
    del st_in, coarse_in
    either_end(lax.axis_index("gy") % 2 == 0, st, coarse, extra, functools.partial(read_beside, beside), outer)


def second_kernel(st_in, coarse_in, extra_in, early, across, *refs):
    st, coarse, extra, total, last_info, first_info, message, outer, squeeze = refs
    del st_in, coarse_in, extra_in
    planes, rows, ext, nz = st.shape
    ny, nx = rows - 2, ext - 2 * PAD
    me = lax.axis_index("gy")
    either_end(me % 2 == 1, st, coarse, extra, functools.partial(read_across, early, across), outer)

    blocks = ny // 2
    for k in range(4):
        squeeze[k] = coarse[k, 0]
    slopes, offsets = coarse[2, 0], coarse[3, 0]
    for j in range(1, blocks):
        slope = coarse[2, j]
        slopes, offsets = slope * slopes, slope * offsets + coarse[3, j]
        coarse[2, j], coarse[3, j] = slopes, offsets
    squeeze[4], squeeze[5], squeeze[6], squeeze[7] = slopes, offsets, coarse[0, blocks - 1], coarse[1, blocks - 1]

    span = nx // 2 + 2
    lead, ratio, slope, offset, slopes, offsets, lead_last, ratio_last = (
        squeeze[k, pl.ds(PAD - 2, span, 2), :] for k in range(8)
    )
    part = slice(PAD - 1, PAD + nx + 1)

    def increments(d, face, gas):
        return [(st[FY, face] * (st[SA, d] - st[SB, d]))[part], (gas * (st[GA, d] - st[GB, d]))[part]]

    onward = [lead_last, ratio_last] + increments(ny - 1, ny - 1, CONDUCT + FLOW)
    back = [lead, offset] + increments(2, 1, CONDUCT) + [slope, ratio]
    write_rows(total, [slopes, offsets])
    write_rows(last_info, onward)
    write_rows(first_info, back)
    for go, info in ((True, onward), (False, back)):

        @pl.when((me % 2 == 0) == go)
        def _():
            write_rows(message, [slopes, offsets] + info)


def write_rows(ref, values):
    at = 0
    for value in values:
        ref[at : at + value.shape[0]] = value
        at += value.shape[0]


class Rows:
    def __init__(self, nx):
        self.span = nx // 2 + 2
        self.map = 2 * self.span
        self.info = self.map + 2 * (nx + 2)
        self.rest = self.map
        self.final = self.map + self.info
        self.full = self.final + self.rest
        self.low = self.map
        self.high = self.low + self.info
        self.near = self.high + self.info + self.rest


def source(at, k, radix):
    if radix & (radix - 1) == 0:
        return at ^ k
    return (at + radix - k) % radix


def matchings(count, radix, stride):
    if (count, radix, stride) == (8, 4, 2):
        swaps = ((1, 2), (3, 4), (5, 6), (0, 7)), ((0, 3), (1, 5), (2, 6), (4, 7)), ((0, 4), (1, 6), (2, 5), (3, 7))
        out = []
        for pairs in swaps:
            senders = [0] * count
            for a, b in pairs:
                senders[a], senders[b] = b, a
            out.append((senders, len(out) == 0))
        return out
    out = []
    for k in range(1, radix):
        senders = []
        for me in range(count):
            at, low = me // stride % radix, me % stride
            senders.append(me - low + (source(at, k, radix) - at) * stride + (stride - 1 - low))
        out.append((senders, any(abs(source(at, k, radix) - at) == 1 for at in range(radix))))
    return sorted(out, key=lambda item: not item[1])


def look_up(table):
    me, value = lax.axis_index("gy"), jnp.int32(table[0])
    for k in range(1, len(table)):
        value = jnp.where(me == k, table[k], value)
    return value


def stages(count):
    if count % 2:
        return [1, count]
    out, rest = [2], count // 2
    while rest > 1:
        radix = next((r for r in (8, 4, 2) if rest % r == 0), rest)
        out.append(radix)
        rest //= radix
    return out if len(out) > 1 else out + [1]


def exchange_stage(messages, swaps):
    return [
        lax.ppermute(message, "gy", [(sender, me) for me, sender in enumerate(senders)])
        for (senders, near), message in zip(swaps, messages)
    ]


class Group:
    def __init__(self, radix, stride, others, nx):
        self.radix, self.others, self.nx = radix, others, nx
        me = lax.axis_index("gy")
        self.swaps = [
            (look_up([sender // stride % radix for sender in senders]), near)
            for senders, near in matchings(lax.axis_size("gy"), radix, stride)
        ]
        self.at = lax.rem(lax.div(me, stride), radix)
        low = lax.rem(me, stride)
        self.lowest, self.highest = low == 0, low == stride - 1

    def map_of(self, place, own):
        rows = Rows(self.nx)
        out = own
        for (sender, near), ref in zip(self.swaps, self.others):
            here = sender == place
            got = [ref[i * rows.span : (i + 1) * rows.span] for i in range(2)]
            out = got if out is None else [jnp.where(here, new, old) for new, old in zip(got, out)]
        return out

    def ahead(self, slope, offset):
        a, b = jnp.ones_like(slope), jnp.zeros_like(slope)
        for place in range(self.radix - 1):
            new_a, new_b = self.map_of(place, None)
            below = place < self.at
            a, b = jnp.where(below, new_a * a, a), jnp.where(below, new_a * b + new_b, b)
        return slope * a, slope * b + offset

    def total(self, own):
        a, b = self.map_of(0, own)
        for place in range(1, self.radix):
            new_a, new_b = self.map_of(place, own)
            a, b = new_a * a, new_a * b + new_b
        return a, b

    def collect(self, near, final):
        rows = Rows(self.nx)
        for (place, adjacent), ref in zip(self.swaps, self.others):
            if not adjacent:
                continue

            @pl.when(self.lowest & (place == self.at - 1))
            def _():
                near[rows.low : rows.low + rows.info] = ref[rows.map : rows.final]

            @pl.when(self.highest & (place == self.at + 1))
            def _():
                near[rows.high : rows.high + rows.info] = ref[rows.map : rows.final]
                rest = slice(0, rows.map) if final else slice(rows.final, rows.full)
                near[rows.high + rows.info : rows.near] = ref[rest]


def start_near(near, nx, nz):
    rows = Rows(nx)
    near[: rows.span] = jnp.ones((rows.span, nz), jnp.float32)
    near[rows.span :] = jnp.zeros((near.shape[0] - rows.span, nz), jnp.float32)


def join_kernel(radix, stride, final, nx, is_first, *refs):
    rows = Rows(nx)
    total, last_info, first_info, near_in = refs[:4]
    others, near, outs = refs[4 : 3 + radix], refs[3 + radix], refs[4 + radix :]
    nz = near.shape[1]
    if is_first:
        start_near(near, nx, nz)
    else:
        near[...] = near_in[...]
    group = Group(radix, stride, others, nx)
    own = [total[i * rows.span : (i + 1) * rows.span] for i in range(2)]
    ahead = group.ahead(near[: rows.span], near[rows.span : rows.map])
    write_rows(near, ahead)
    group.collect(near, False)
    whole = group.total(own)
    if final == 0:
        write_rows(outs[0], whole)
        return
    me, count = lax.axis_index("gy"), lax.axis_size("gy")
    for (senders, adjacent), out in zip(matchings(count, final, stride * radix), outs):
        up = look_up(senders) > me
        if not adjacent:
            write_rows(out, whole)
            continue

        @pl.when(up)
        def _():
            write_rows(out, whole)
            out[rows.map : rows.final] = last_info[: rows.info]

        @pl.when(jnp.logical_not(up))
        def _():
            out[: rows.map] = first_info[rows.info : rows.info + rows.rest]
            out[rows.map : rows.final] = first_info[: rows.info]


def full_message(nx, total, last_info, first_info, senders):
    rows = Rows(nx)
    onward = jnp.concatenate([total[: rows.map], last_info[: rows.info], first_info[rows.info : rows.info + rows.rest]])
    back = jnp.concatenate([total[: rows.map], first_info[: rows.info + rows.rest]])
    message = jnp.where(look_up(senders) > lax.axis_index("gy"), onward, back)
    return jnp.pad(message, ((0, -rows.full % 8), (0, 0)))


def spread_x(ref, k, values, span):
    ext, nz = ref.shape[1:]
    ref[k, : PAD - 2] = jnp.zeros((PAD - 2, nz), jnp.float32)
    ref[k, ext - PAD + 2 :] = jnp.zeros((PAD - 2, nz), jnp.float32)
    ref[k, pl.ds(PAD - 2, span, 2), :] = values
    ref[k, pl.ds(PAD - 1, span, 2), :] = values


def widen_kernel(radix, stride, *refs):
    near_in, others, (wide, near) = refs[0], refs[1:-2], refs[-2:]
    ext, nz = wide.shape[1:]
    nx = ext - 2 * PAD
    lay = Rows(nx)
    span = lay.span
    near[...] = near_in[...]
    if others:
        following = iter(others)
        group = Group(radix, stride, None, nx)
        group.others = [next(following) if adjacent else None for _, adjacent in group.swaps]
        group.collect(near, True)
    at_high = lay.high + lay.info
    starts = (lay.low, lay.low + span, lay.high, lay.high + span, at_high, at_high + span)
    for k, start in enumerate(starts, 1):
        spread_x(wide, k, near[start : start + span], span)
    for k, start in enumerate((lay.low, lay.low + nx + 2, lay.high, lay.high + nx + 2)):
        start += lay.map
        wide[7 + k, :PAD] = jnp.zeros((PAD, nz), jnp.float32)
        wide[7 + k, ext - PAD :] = jnp.zeros((PAD, nz), jnp.float32)
        wide[7 + k, PAD - 1 : PAD + nx + 1] = near[start : start + nx + 2]
    wide[0] = jnp.zeros((ext, nz), jnp.float32)


def third_kernel(radix, stride, *refs):
    st, extra, coarse, near, wide = refs[:5]
    others, (out, sc, entering, done, sems) = refs[5 : 4 + radix], refs[4 + radix :]
    planes, rows, ext, nz = st.shape
    ny, nx = rows - 2, ext - 2 * PAD
    edge = edge_weights((ext, nz))
    blocks = ny // 2

    lay = Rows(nx)
    span = lay.span
    group = Group(radix, stride, others, nx)
    spread_x(entering, 0, group.ahead(near[:span], near[span : lay.map])[1], span)
    gas_in = entering[0]
    last = ny + 1
    solid_low = wide[1] + wide[2] * gas_in
    sc[0, 0] = st[SA, 0] + solid_low
    sc[1, 0] = st[GA, 0] + gas_in

    def correct(j, carry):
        gas = coarse[2, j] * gas_in + coarse[3, j]
        solid = coarse[0, j] + coarse[1, j] * gas
        for i in (2 * j + 1, 2 * j + 2):
            sc[0, i] = st[SA, i] + solid
            sc[1, i] = st[GA, i] + gas
        return carry

    lax.fori_loop(0, blocks, correct, 0)
    gas = coarse[2, blocks - 1] * gas_in + coarse[3, blocks - 1]
    gas_high = wide[5] * gas + wide[4]
    solid_high = wide[3] + wide[6] * gas_high
    sc[0, last] = st[SA, last] + solid_high
    sc[1, last] = st[GA, last] + gas_high

    view = Fields(st, sc)
    for i, is_after, solid, gas in ((0, False, solid_low, gas_in), (last, True, solid_high, gas_high)):
        side = 3 if is_after else 0
        fy = extra[side + 2]
        to = 9 if is_after else 7
        rs = extra[side] + wide[to] + fy * solid
        rg = extra[side + 1] + wide[to + 1] + (CONDUCT if is_after else CONDUCT + FLOW) * gas
        res = outer_residual(view, i, SA, rs, rg, fy, edge, is_after)
        sc[2, i], sc[3, i] = relaxed(view, i, SA, *res)

    def sweep(k, carry):
        stores = []
        for r in range(GROUP):
            i = GROUP * k + 1 + r
            new_s, new_g = relaxed(view, i, SA, *row_residual(view, i, SA, edge))
            stores += [((2, i), new_s), ((3, i), new_g)]
        for at, value in stores:
            sc[at] = value
        return carry

    lax.fori_loop(0, ny // GROUP, sweep, 0)

    def leaving(k):
        part = pl.ds(GROUP * k, GROUP)
        return pltpu.make_async_copy(done.at[:, part], out.at[:, part], sems.at[k])

    def final(k, carry):
        stores = []
        for r in range(GROUP):
            i = GROUP * k + 1 + r
            new_s, new_g = last_relaxed(view, i, SB, edge, slice(PAD, PAD + nx))
            stores += [((0, i - 1), new_s), ((1, i - 1), new_g)]
        for at, value in stores:
            done[at] = value
        leaving(k).start()
        return carry

    lax.fori_loop(0, ny // GROUP, final, 0)
    for k in range(ny // GROUP):
        leaving(k).wait()


class Fields:
    def __init__(self, st, sc):
        self.st, self.sc = st, sc

    def __getitem__(self, at):
        return (self.sc if at[0] <= GB else self.st)[at]


def cost(rows, cells):
    return pl.CostEstimate(flops=50 * rows * cells, bytes_accessed=16 * 4 * rows * cells, transcendentals=0)


def swap(x, axis, first):
    pairs = []
    for i in range(first, lax.axis_size(axis) - 1, 2):
        pairs += [(i, i + 1), (i + 1, i)]
    return lax.ppermute(x, axis, pairs)


def shards(temps, right_side, exchange, coupling):
    temps, right_side = (jnp.transpose(a, (0, 2, 1, 3)) for a in (temps, right_side))
    exchange, coupling = (jnp.transpose(a, (1, 0, 2)) for a in (exchange, coupling))
    temps, right_side, exchange, coupling = (
        pltpu.with_memory_space_constraint(a, pltpu.HBM) for a in (temps, right_side, exchange, coupling)
    )
    ny, nx, nz = exchange.shape
    ext = nx + 2 * PAD
    f32 = functools.partial(jax.ShapeDtypeStruct, dtype=jnp.float32)

    strip = f32((strip_height(ny), nz))
    state = f32((PLANES, ny + 2, ext, nz))
    one, two, early, st = pl.pallas_call(
        pack_kernel,
        out_shape=(strip, strip, f32((EARLY, nx, nz)), state),
        in_specs=[HBM] * 4,
        out_specs=(VMEM,) * 4,
        scratch_shapes=[pltpu.SemaphoreType.DMA((6,))],
        compiler_params=PARAMS,
        name="pack_x",
    )(temps, right_side, exchange, coupling)
    one, two = swap(one, "gx", 0), swap(two, "gx", 1)
    early = swap(early, "gy", 1)

    def letter(planes):
        return f32((planes, ext - 2 * CROP, nz))

    st = pl.pallas_call(
        conduct_kernel,
        out_shape=state,
        in_specs=[VMEM],
        out_specs=VMEM,
        input_output_aliases={0: 0},
        compiler_params=PARAMS,
        cost_estimate=cost(2 * ny, ext * nz),
        name="conduct",
    )(st)
    st, across = pl.pallas_call(
        first_kernel,
        out_shape=(state, f32((across_parts(ext)[1], nz))),
        in_specs=[VMEM] * 3,
        out_specs=(VMEM,) * 2,
        input_output_aliases={0: 0},
        compiler_params=PARAMS,
        name="first",
    )(st, one, two)
    st, *beside = pl.pallas_call(
        other_kernel,
        out_shape=(state,) + (letter(THIRD),) * (MESSAGE // THIRD),
        in_specs=[VMEM] * 3,
        out_specs=(VMEM,) * (1 + MESSAGE // THIRD),
        input_output_aliases={0: 0},
        compiler_params=PARAMS,
        name="other",
    )(st, one, two)
    across = swap(across, "gy", 1)

    rows = f32((4, ny // 2, ext, nz))
    st, coarse = pl.pallas_call(
        inner_kernel,
        out_shape=(state, rows),
        in_specs=[VMEM] * 2,
        out_specs=(VMEM,) * 2,
        input_output_aliases={0: 0},
        compiler_params=PARAMS,
        cost_estimate=cost(4 * ny, ext * nz),
        name="inner",
    )(st, early)

    beside = [swap(part, "gy", 0) for part in beside]

    lay = Rows(nx)

    def tall(height):
        return f32(((height + 7) // 8 * 8, nz))

    letter_room = pltpu.VMEM((MESSAGE, ext, nz), jnp.float32)
    more = f32((6, ext, nz))
    st, coarse, extra = pl.pallas_call(
        near_kernel,
        out_shape=(state, rows, more),
        in_specs=[VMEM] * (2 + len(beside)),
        out_specs=(VMEM,) * 3,
        scratch_shapes=[letter_room],
        input_output_aliases={0: 0, 1: 1},
        compiler_params=PARAMS,
        name="near",
    )(st, coarse, *beside)
    st, coarse, extra, total, last_info, first_info, message = pl.pallas_call(
        second_kernel,
        out_shape=(state, rows, more, tall(lay.map), tall(lay.info), tall(lay.info + lay.rest), tall(lay.full)),
        in_specs=[VMEM] * 5,
        out_specs=(VMEM,) * 7,
        scratch_shapes=[letter_room, pltpu.VMEM((8, ext, nz), jnp.float32)],
        input_output_aliases={0: 0, 1: 1, 2: 2},
        compiler_params=PARAMS,
        name="second",
    )(st, coarse, extra, early, across)

    near, messages = total, [message]
    count = lax.axis_size("gy")
    radices, stride = stages(count), 1
    for place, radix in enumerate(radices[:-1]):
        swaps = matchings(count, radix, stride)
        if place:
            messages = [full_message(nx, total, last_info, first_info, senders) for senders, _ in swaps]
        others = exchange_stage(messages, swaps)
        final = radices[-1] if place == len(radices) - 2 else 0
        following = matchings(count, final, stride * radix) if final else []
        outs = [tall(lay.final if adjacent else lay.map) for _, adjacent in following] if final else [tall(lay.map)]
        near, *messages = pl.pallas_call(
            functools.partial(join_kernel, radix, stride, final, nx, place == 0),
            out_shape=(tall(lay.near), *outs),
            in_specs=[VMEM] * (3 + radix),
            out_specs=(VMEM,) * (1 + len(outs)),
            compiler_params=PARAMS,
            name="join",
        )(total, last_info, first_info, near, *others)
        total = total if final else messages[0]
        stride *= radix
    got = exchange_stage(messages, matchings(count, radices[-1], stride))

    last = matchings(count, radices[-1], stride)
    beside = [message for (_, adjacent), message in zip(last, got) if adjacent]
    wide = pl.pallas_call(
        functools.partial(widen_kernel, radices[-1], stride),
        out_shape=f32((11, ext, nz)),
        in_specs=[VMEM] * (1 + len(beside)),
        out_specs=VMEM,
        scratch_shapes=[pltpu.VMEM(near.shape, jnp.float32)],
        compiler_params=PARAMS,
        name="widen",
    )(near, *beside)
    out = pl.pallas_call(
        functools.partial(third_kernel, radices[-1], stride),
        out_shape=f32((2, ny, nx, nz)),
        in_specs=[VMEM] * (5 + len(got)),
        out_specs=HBM,
        scratch_shapes=[
            pltpu.VMEM((4, ny + 2, ext, nz), jnp.float32),
            pltpu.VMEM((1, ext, nz), jnp.float32),
            pltpu.VMEM((2, ny, nx, nz), jnp.float32),
            pltpu.SemaphoreType.DMA((ny // GROUP,)),
        ],
        compiler_params=PARAMS,
        name="third",
    )(st, extra, coarse, near, wide, *got)
    return jnp.transpose(out, (0, 2, 1, 3))


def solution(mesh):
    return jax.shard_map(
        shards,
        mesh=mesh,
        in_specs=(
            P(None, "gx", "gy", None),
            P(None, "gx", "gy", None),
            P("gx", "gy", None),
            P("gx", "gy", None),
        ),
        out_specs=P(None, "gx", "gy", None),
        check_vma=False,
    )
```

```python
import functools

import jax
import jax.numpy as jnp
from jax import lax
from jax.experimental import pallas as pl
from jax.experimental.pallas import tpu as pltpu
from jax.sharding import PartitionSpec as P

SOLID_CAP, GAS_CAP, FLOW, CONDUCT, RELAX, LUMP = 0.5, 0.02, 40.0, 0.05, 0.8, 0.25
GAS_SELF = GAS_CAP + 4.5 * CONDUCT

PAD = 8
WX = 5
CROP = 4
(SA, GA, SB, GB, K, C, RS, RG, FX, FZ, H, FY, ASS, ASG, AGG) = range(15)
PLANES = 15
(M_S, M_G, M_K, M_C, M_FY, M_1S, M_1G, M_2S, M_2G) = range(9)
MESSAGE, EARLY, THIRD = 9, 7, 3

GROUP = 6

VMEM = pl.BlockSpec(memory_space=pltpu.VMEM)
HBM = pl.BlockSpec(memory_space=pltpu.HBM)
PARAMS = pltpu.CompilerParams(vmem_limit_bytes=40 * 1024 * 1024)


def up_x(v):
    return pltpu.roll(v, v.shape[0] - 1, 0)


def down_x(v):
    return pltpu.roll(v, 1, 0)


def up_z(v):
    return pltpu.roll(v, v.shape[1] - 1, 1)


def down_z(v):
    return pltpu.roll(v, 1, 1)


def lanes(shape):
    return lax.broadcasted_iota(jnp.int32, shape, 1)


def x_mask(shape, nx):
    row = lax.broadcasted_iota(jnp.int32, shape, 0)
    place, count = lax.axis_index("gx"), lax.axis_size("gx")
    low = jnp.where(place == 0, PAD, PAD - WX)
    high = jnp.where(place == count - 1, PAD + nx, PAD + nx + WX)
    return jnp.where((row >= low) & (row < high), 1.0, 0.0).astype(jnp.float32)


PAIRS = ((SA, GA), (C, RS), (RG, K))
STRIP_ROWS = 8 * len(PAIRS)


def strip_height(ny):
    return ny * STRIP_ROWS + (ny + 7) // 8 * 8


def sublanes(nz):
    return lax.broadcasted_iota(jnp.int32, (8, nz), 0)


def conductivity_of(s, exchange):
    return 1.0 + 4.0 * exchange * s * s * s


def strip_side(s, g, k, rs, rg, c, low):
    row = sublanes(s.shape[1])
    inn, shift = (3, 7) if low else (4, 1)
    k_out, s_out, g_out = (pltpu.roll(v, shift, 0) for v in (k, s, g))
    rs = rs + jnp.where(row == inn, 0.5 * (k + k_out) * s_out, 0.0)
    rg = rg + jnp.where(row == inn, CONDUCT * g_out, 0.0)
    values = {SA: s, GA: g, K: k, RS: rs, RG: rg, C: c}
    tiles = []
    for a, b in PAIRS:
        a, b = values[a], values[b]
        a, b = (a, pltpu.roll(b, 4, 0)) if low else (pltpu.roll(a, 4, 0), b)
        tiles.append(jnp.where(row < 4, a, b))
    return tiles, (k[4:5] if low else k[3:4])


def pack_kernel(temps, right, exchange, coupling, one, two, st, sems):
    even = lax.axis_index("gx") % 2 == 0
    ny, nx, nz = exchange.shape
    copies = []
    for k, (plane, ref) in enumerate(
        ((SA, temps.at[0]), (K, exchange), (GA, temps.at[1]), (C, coupling), (RS, right.at[0]), (RG, right.at[1]))
    ):
        to = st.at[plane, pl.ds(1, ny), pl.ds(PAD, nx)]
        copies.append(pltpu.make_async_copy(ref, to, sems.at[k]))
    for copy in copies:
        copy.start()
    for copy in copies:
        copy.wait()
    for i in range(1, ny + 1):
        sides = []
        for start in (PAD, PAD + nx - 8):
            s, g, e, rs, rg, c = (st[plane, i, start : start + 8] for plane in (SA, GA, K, RS, RG, C))
            sides.append(strip_side(s, g, conductivity_of(s, e), rs, rg, c, start == PAD))
        (low, low_k), (high, high_k) = sides
        for p in range(len(PAIRS)):
            part = slice((i - 1) * STRIP_ROWS + 8 * p, (i - 1) * STRIP_ROWS + 8 * p + 8)
            one[part] = jnp.where(even, high[p], low[p])
            two[part] = jnp.where(even, low[p], high[p])
        part = slice(ny * STRIP_ROWS + i - 1, ny * STRIP_ROWS + i)
        one[part] = jnp.where(even, high_k, low_k)
        two[part] = jnp.where(even, low_k, high_k)


def conduct_kernel(st_in, st, early):
    del st_in
    planes, rows, ext, nz = st.shape
    ny, nx = rows - 2, ext - 2 * PAD
    odd = lax.axis_index("gy") % 2 == 1
    own = slice(PAD, PAD + nx)
    for i in range(1, ny + 1):
        st[K, i, own] = conductivity_of(st[SA, i, own], st[K, i, own])
    for is_odd, e, d in ((True, ny, ny - 1), (False, 1, 2)):

        @pl.when(odd == is_odd)
        def _():
            s, s_d, g, g_d = st[SA, e, own], st[SA, d, own], st[GA, e, own], st[GA, d, own]
            c, k, k_d = st[C, e, own], st[K, e, own], st[K, d, own]
            fx, fz, h, _ = faces(k)
            fy = 0.5 * (k + k_d)
            part_s, part_g = inner(s, g, c, h, fx, fz, edge_weights((nx, nz)))
            m_1s, m_1g = first_partial(st[RS, e, own] + part_s, st[RG, e, own] + part_g, s, s_d, g, g_d, fy, is_odd)
            for plane, value in enumerate((s, g, k, c, fy, m_1s, m_1g)):
                early[plane] = value


def place_halo(st, one, two, y, nx):
    even = lax.axis_index("gx") % 2 == 0
    ny, row = st.shape[1] - 2, sublanes(st.shape[3])
    i = y + 1

    def received(part):
        a, b = one[part], two[part]
        return jnp.where(even, b, a), jnp.where(even, a, b)

    for p, (plane_a, plane_b) in enumerate(PAIRS):
        before, after = received(slice(y * STRIP_ROWS + 8 * p, y * STRIP_ROWS + 8 * p + 8))
        before = {plane_a: pltpu.roll(before, 4, 0), plane_b: before}
        after = {plane_a: after, plane_b: pltpu.roll(after, 4, 0)}
        for plane in (plane_a, plane_b):
            low, high = jnp.where(row >= 4, before[plane], 0.0), jnp.where(row < 4, after[plane], 0.0)
            if plane == K:
                k_low, k_high = received(slice(ny * STRIP_ROWS + y, ny * STRIP_ROWS + y + 1))
                low, high = jnp.where(row == 3, k_low, low), jnp.where(row == 4, k_high, high)
            st[plane, i, :PAD] = low
            st[plane, i, PAD + nx :] = high


def inner(s, g, c, h, fx, fz, edge):
    t = c * (s - g)
    flux_x = fx * (up_x(s) - s)
    flux_z = fz * (up_z(s) - s)
    part_s = (flux_x - down_x(flux_x)) + (flux_z - down_z(flux_z)) - h * s - t
    part_g = (
        t
        - GAS_SELF * g
        + CONDUCT * (up_x(g) + down_x(g))
        + edge[0] * up_z(g)
        + edge[1] * down_z(g)
    )
    return part_s, part_g


def edge_weights(shape):
    lane = lanes(shape)
    weight = jnp.float32(0.25 * CONDUCT)
    return jnp.where(lane == shape[1] - 1, 0.0, weight), jnp.where(lane == 0, 0.0, weight)


def row_inner(st, i, s_at, edge):
    return inner(st[s_at, i], st[s_at + 1, i], st[C, i], st[H, i], st[FX, i], st[FZ, i], edge)


def row_residual(st, i, s_at, edge):
    part_s, part_g = row_inner(st, i, s_at, edge)
    s, g, before = st[s_at, i], st[s_at + 1, i], st[s_at + 1, i - 1]
    part_s += st[FY, i] * (st[s_at, i + 1] - s) + st[FY, i - 1] * (st[s_at, i - 1] - s)
    part_g += CONDUCT * (st[s_at + 1, i + 1] + before) - FLOW * (g - before)
    return st[RS, i] + part_s, st[RG, i] + part_g


def relaxed(st, i, s_at, res_s, res_g):
    s = st[s_at, i] + st[ASS, i] * res_s + st[ASG, i] * res_g
    g = st[s_at + 1, i] + st[ASG, i] * res_s + st[AGG, i] * res_g
    return s, g


def faces(k):
    lane = lanes(k.shape)
    end = k.shape[1] - 1
    fx = 0.5 * (k + up_x(k))
    fz = jnp.where(lane == end, 0.0, 0.125 * (k + up_z(k)))
    h = SOLID_CAP + jnp.where((lane == 0) | (lane == end), 0.125 * k, 0.0)
    return fx, fz, h, h + (fx + down_x(fx)) + (fz + down_z(fz))


def inverse(diag, c, mask):
    gas_diag = (GAS_SELF + FLOW) + c
    inv = (RELAX * mask) / (diag * gas_diag - c * c)
    return inv * gas_diag, inv * c, inv * diag


def last_relaxed(st, i, s_at, edge, own):
    full_s, full_g = st[s_at, i], st[s_at + 1, i]
    s, g = full_s[own], full_g[own]
    flux_x = st[FX, i] * (up_x(full_s) - full_s)
    flux_z = st[FZ, i, own] * (up_z(s) - s)
    c, before = st[C, i, own], st[s_at + 1, i - 1, own]
    t = c * (s - g)
    res_s = st[RS, i, own] + (flux_x[own] - down_x(flux_x)[own]) + (flux_z - down_z(flux_z)) - st[H, i, own] * s - t
    res_s += st[FY, i, own] * (st[s_at, i + 1, own] - s) + st[FY, i - 1, own] * (st[s_at, i - 1, own] - s)
    res_g = st[RG, i, own] + t - GAS_SELF * g + edge[0][own] * up_z(g) + edge[1][own] * down_z(g)
    res_g += CONDUCT * (up_x(full_g)[own] + down_x(full_g)[own] + st[s_at + 1, i + 1, own] + before) - FLOW * (g - before)
    ss, sg, gg = st[ASS, i, own], st[ASG, i, own], st[AGG, i, own]
    return s + ss * res_s + sg * res_g, g + sg * res_s + gg * res_g


def grouped(rows, work):
    for start in range(0, len(rows), GROUP):
        stores = []
        for i in rows[start : start + GROUP]:
            stores += work(i)
        for ref, at, value in stores:
            ref[at] = value


def looped(first, last, size, work):
    def group(k, carry):
        grouped([first + size * k + r for r in range(size)], work)
        return carry

    lax.fori_loop(0, (last - first) // size, group, 0)
    grouped(list(range(last - (last - first) % size, last)), work)


def row_coefficients(st, i, mask):
    fx, fz, h, diag = faces(st[K, i])
    fy = 0.5 * (st[K, i] + st[K, i + 1])
    before = 0.5 * (st[K, i] + st[K, i - 1])
    ss, sg, gg = inverse(diag + st[C, i] + fy + before, st[C, i], mask)
    values = ((FX, fx), (FZ, fz), (H, h), (FY, fy), (ASS, ss), (ASG, sg), (AGG, gg))
    return [(st, (plane, i), v) for plane, v in values]


def row_sweep(st, i, source, target, edge):
    s, g = relaxed(st, i, source, *row_residual(st, i, source, edge))
    return [(st, (target, i), s), (st, (target + 1, i), g)]


def first_partial(res_s, res_g, s, s_d, g, g_d, fy, onward):
    return res_s + fy * (s_d - s), res_g + CONDUCT * g_d - FLOW * (g - g_d if onward else g)


def send_planes(st, onward, edge):
    ny = st.shape[1] - 2
    e, d, near = (ny, ny - 1, ny - 1) if onward else (1, 2, 1)
    fy, s, g, g_d = st[FY, near], st[SA, e], st[GA, e], st[GA, d]
    part_s, part_g = row_inner(st, e, SA, edge)
    m_1s, m_1g = first_partial(st[RS, e] + part_s, st[RG, e] + part_g, s, st[SA, d], g, g_d, fy, onward)
    m_2s = st[RS, e] + fy * st[SB, d]
    m_2g = st[RG, e] + (CONDUCT + FLOW if onward else CONDUCT) * st[GB, d]
    return [s, g, st[K, e], st[C, e], fy, m_1s, m_1g, m_2s, m_2g]


def across_parts(ext):
    parts, at = [], 0
    for k in range(EARLY, MESSAGE):
        parts.append((k, CROP, ext - CROP, at))
        at += ext - 2 * CROP
    for k in range(EARLY):
        more = 1 if k in (M_1S, M_1G) else 0
        for low, high in ((CROP, PAD + more), (ext - PAD - more, ext - CROP)):
            parts.append((k, low, high, at))
            at += high - low
    return parts, (at + 7) // 8 * 8


def write_across(ref, k, value):
    for plane, low, high, at in across_parts(value.shape[0])[0]:
        if plane == k:
            ref[at : at + high - low] = value[low:high]


def read_across(early, across, outer, k):
    ext = outer.shape[1]
    if k < EARLY:
        outer[k, PAD : ext - PAD] = early[k]
    for plane, low, high, at in across_parts(ext)[0]:
        if plane == k:
            outer[k, low:high] = across[at : at + high - low]


def write_beside(refs, k, value):
    refs[k // THIRD][k % THIRD] = value[CROP : value.shape[0] - CROP]


def read_beside(refs, outer, k):
    outer[k, CROP : outer.shape[1] - CROP] = refs[k // THIRD][k % THIRD]


def first_end(st, one, two, after, write):
    planes, rows, ext, nz = st.shape
    ny, nx = rows - 2, ext - 2 * PAD
    mask = x_mask((ext, nz), nx)
    edge = edge_weights((ext, nz))
    e, d, f = (ny, ny - 1, ny - 2) if after else (1, 2, 3)
    for i in (e, d, f):
        place_halo(st, one, two, i - 1, nx)
    fx, fz, h, diag = faces(st[K, e])
    st[FX, e], st[FZ, e], st[H, e] = fx, fz, h
    st[FY, min(e, d)] = 0.5 * (st[K, e] + st[K, d])
    st[FY, min(d, f)] = 0.5 * (st[K, d] + st[K, f])
    grouped([d], lambda i: row_coefficients(st, i, mask))
    grouped([d], lambda i: row_sweep(st, i, SA, SB, edge))
    for k, value in enumerate(send_planes(st, after, edge)):
        write(k, value)


def either_first(st, one, two, after, write):
    for is_after in (True, False):

        @pl.when(after == is_after)
        def _():
            first_end(st, one, two, is_after, write)


def first_kernel(st_in, one, two, st, across):
    del st_in
    either_first(st, one, two, lax.axis_index("gy") % 2 == 1, functools.partial(write_across, across))


def other_kernel(st_in, one, two, st, *beside):
    del st_in
    either_first(st, one, two, lax.axis_index("gy") % 2 == 0, functools.partial(write_beside, beside))
    planes, rows, ext, nz = st.shape
    ny, nx = rows - 2, ext - 2 * PAD
    mask = x_mask((ext, nz), nx)
    for y in range(3, ny - 3):
        place_halo(st, one, two, y, nx)
    grouped(list(range(3, ny - 1)), lambda i: row_coefficients(st, i, mask))


def outer_residual(st, i, s_at, rs, rg, fy_out, edge, after):
    part_s, part_g = row_inner(st, i, s_at, edge)
    s, g = st[s_at, i], st[s_at + 1, i]
    if after:
        part_s += st[FY, i - 1] * (st[s_at, i - 1] - s)
        part_g += (CONDUCT + FLOW) * st[s_at + 1, i - 1]
    else:
        part_s += st[FY, i] * (st[s_at, i + 1] - s)
        part_g += CONDUCT * st[s_at + 1, i + 1]
    return rs + part_s - fy_out * s, rg + part_g - FLOW * g


def pair_x(v):
    row = lax.broadcasted_iota(jnp.int32, v.shape, 0)
    return v + jnp.where(row % 2 == 0, up_x(v), down_x(v))


def coarse_coefficients(c_sum, k_sum):
    per_solid = 1.0 / (4.0 * SOLID_CAP + c_sum + LUMP * k_sum)
    ratio = c_sum * per_solid
    return per_solid, ratio, 1.0 / ((4.0 * GAS_CAP + 2.0 * FLOW) + c_sum - c_sum * ratio)


def coarse_row(st, coarse, j, mask, edge):
    i = 2 * j + 1
    res_s, res_g = row_residual(st, i, SA, edge)
    more_s, more_g = row_residual(st, i + 1, SA, edge)
    res_s, res_g = pair_x((res_s + more_s) * mask), pair_x((res_g + more_g) * mask)
    c_sum = pair_x(st[C, i] + st[C, i + 1])
    per_solid, ratio, per_gas = coarse_coefficients(c_sum, pair_x(st[K, i] + st[K, i + 1]))
    lead = res_s * per_solid
    values = (lead, ratio, (2.0 * FLOW) * per_gas, (res_g + c_sum * lead) * per_gas)
    return [(coarse, (k, j), v) for k, v in enumerate(values)]


def inner_kernel(st_in, early, st, coarse):
    del st_in, early
    planes, rows, ext, nz = st.shape
    ny, nx = rows - 2, ext - 2 * PAD
    shape = (ext, nz)
    mask = x_mask(shape, nx)
    edge = edge_weights(shape)
    looped(3, ny - 1, 4, lambda i: row_sweep(st, i, SA, SB, edge))
    looped(3, ny - 1, 4, lambda i: row_sweep(st, i, SB, SA, edge))
    grouped(list(range(2, ny // 2 - 2)), lambda j: coarse_row(st, coarse, j, mask, edge))


def end_work(st, coarse, extra, read, outer, is_after):
    planes, rows, ext, nz = st.shape
    ny, nx = rows - 2, ext - 2 * PAD
    me, count = lax.axis_index("gy"), lax.axis_size("gy")
    mask = x_mask((ext, nz), nx)
    inside = jnp.where(me == (count - 1 if is_after else 0), 0.0, mask)
    edge = edge_weights((ext, nz))
    zeros = jnp.zeros((PAD, nz), jnp.float32)
    for k in range(MESSAGE):
        outer[k, :PAD] = zeros
        outer[k, ext - PAD :] = zeros
        read(outer, k)

    o, e, near = (ny + 1, ny, ny) if is_after else (0, 1, 0)
    to_o = CONDUCT + FLOW if is_after else CONDUCT
    s_o, g_o, k_o, c_o, fy_out = (outer[plane] for plane in (M_S, M_G, M_K, M_C, M_FY))
    fy = 0.5 * (k_o + st[K, e])
    fx, fz, h, diag = faces(k_o)
    inv_o = inverse(diag + c_o + fy_out + fy, c_o, inside)
    fx_e, fz_e = st[FX, e], st[FZ, e]
    diag = st[H, e] + (fx_e + down_x(fx_e)) + (fz_e + down_z(fz_e)) + st[C, e] + fy
    inv_e = inverse(diag + st[FY, near - 1 if is_after else near + 1], st[C, e], mask)
    for plane, value in ((SA, s_o), (GA, g_o), (K, k_o), (C, c_o), (FX, fx), (FZ, fz), (H, h)):
        st[plane, o] = value
    st[FY, near] = fy
    for k in range(3):
        st[ASS + k, o], st[ASS + k, e] = inv_o[k], inv_e[k]

    res = outer[M_1S] + fy * (st[SA, e] - s_o), outer[M_1G] + to_o * st[GA, e]
    new_o = relaxed(st, o, SA, *res)
    stores = row_sweep(st, e, SA, SB, edge)
    st[SB, o], st[GB, o] = new_o
    for ref, at, value in stores:
        ref[at] = value
    res = outer_residual(st, o, SB, outer[M_2S], outer[M_2G], fy_out, edge, is_after)
    new_o = relaxed(st, o, SB, *res)
    ends = [e - 1, e] if is_after else [e, e + 1]
    grouped(ends, lambda i: row_sweep(st, i, SB, SA, edge))
    st[SA, o], st[GA, o] = new_o
    for k, plane in enumerate((M_2S, M_2G, M_FY)):
        extra[(3 if is_after else 0) + k] = outer[plane]
    blocks = ny // 2
    stores = []
    for j in (blocks - 2, blocks - 1) if is_after else (0, 1):
        stores += coarse_row(st, coarse, j, mask, edge)
    for ref, at, value in stores:
        ref[at] = value


def either_end(after, st, coarse, extra, read, outer):
    for is_after in (True, False):

        @pl.when(after == is_after)
        def _():
            end_work(st, coarse, extra, read, outer, is_after)


def near_kernel(st_in, coarse_in, *refs):
    beside, (st, coarse, extra, outer) = refs[:-4], refs[-4:]
    del st_in, coarse_in
    either_end(lax.axis_index("gy") % 2 == 0, st, coarse, extra, functools.partial(read_beside, beside), outer)


def second_kernel(st_in, coarse_in, extra_in, early, across, *refs):
    st, coarse, extra, total, last_info, first_info, message, outer, squeeze = refs
    del st_in, coarse_in, extra_in
    planes, rows, ext, nz = st.shape
    ny, nx = rows - 2, ext - 2 * PAD
    me = lax.axis_index("gy")
    either_end(me % 2 == 1, st, coarse, extra, functools.partial(read_across, early, across), outer)

    blocks = ny // 2
    for k in range(4):
        squeeze[k] = coarse[k, 0]
    slopes, offsets = coarse[2, 0], coarse[3, 0]
    for j in range(1, blocks):
        slope = coarse[2, j]
        slopes, offsets = slope * slopes, slope * offsets + coarse[3, j]
        coarse[2, j], coarse[3, j] = slopes, offsets
    squeeze[4], squeeze[5], squeeze[6], squeeze[7] = slopes, offsets, coarse[0, blocks - 1], coarse[1, blocks - 1]

    span = nx // 2 + 2
    lead, ratio, slope, offset, slopes, offsets, lead_last, ratio_last = (
        squeeze[k, pl.ds(PAD - 2, span, 2), :] for k in range(8)
    )
    part = slice(PAD - 1, PAD + nx + 1)

    def increments(d, face, gas):
        return [(st[FY, face] * (st[SA, d] - st[SB, d]))[part], (gas * (st[GA, d] - st[GB, d]))[part]]

    onward = [lead_last, ratio_last] + increments(ny - 1, ny - 1, CONDUCT + FLOW)
    back = [lead, offset] + increments(2, 1, CONDUCT) + [slope, ratio]
    write_rows(total, [slopes, offsets])
    write_rows(last_info, onward)
    write_rows(first_info, back)
    for go, info in ((True, onward), (False, back)):

        @pl.when((me % 2 == 0) == go)
        def _():
            write_rows(message, [slopes, offsets] + info)


def write_rows(ref, values):
    at = 0
    for value in values:
        ref[at : at + value.shape[0]] = value
        at += value.shape[0]


class Rows:
    def __init__(self, nx):
        self.span = nx // 2 + 2
        self.map = 2 * self.span
        self.info = self.map + 2 * (nx + 2)
        self.rest = self.map
        self.final = self.map + self.info
        self.full = self.final + self.rest
        self.low = self.map
        self.high = self.low + self.info
        self.near = self.high + self.info + self.rest


def source(at, k, radix):
    if radix & (radix - 1) == 0:
        return at ^ k
    return (at + radix - k) % radix


def matchings(count, radix, stride):
    if (count, radix, stride) == (8, 4, 2):
        swaps = ((1, 2), (3, 4), (5, 6), (0, 7)), ((0, 4), (1, 6), (2, 5), (3, 7)), ((0, 3), (1, 5), (2, 6), (4, 7))
        out = []
        for pairs in swaps:
            senders = [0] * count
            for a, b in pairs:
                senders[a], senders[b] = b, a
            out.append((senders, len(out) == 0))
        return out
    out = []
    for k in range(1, radix):
        senders = []
        for me in range(count):
            at, low = me // stride % radix, me % stride
            senders.append(me - low + (source(at, k, radix) - at) * stride + (stride - 1 - low))
        out.append((senders, any(abs(source(at, k, radix) - at) == 1 for at in range(radix))))
    return sorted(out, key=lambda item: not item[1])


def look_up(table):
    me, value = lax.axis_index("gy"), jnp.int32(table[0])
    for k in range(1, len(table)):
        value = jnp.where(me == k, table[k], value)
    return value


def stages(count):
    if count % 2:
        return [1, count]
    out, rest = [2], count // 2
    while rest > 1:
        radix = next((r for r in (8, 4, 2) if rest % r == 0), rest)
        out.append(radix)
        rest //= radix
    return out if len(out) > 1 else out + [1]


def exchange_stage(messages, swaps):
    return [
        lax.ppermute(message, "gy", [(sender, me) for me, sender in enumerate(senders)])
        for (senders, near), message in zip(swaps, messages)
    ]


class Group:
    def __init__(self, radix, stride, others, nx):
        self.radix, self.others, self.nx = radix, others, nx
        me = lax.axis_index("gy")
        self.swaps = [
            (look_up([sender // stride % radix for sender in senders]), near)
            for senders, near in matchings(lax.axis_size("gy"), radix, stride)
        ]
        self.at = lax.rem(lax.div(me, stride), radix)
        low = lax.rem(me, stride)
        self.lowest, self.highest = low == 0, low == stride - 1

    def map_of(self, place, own):
        rows = Rows(self.nx)
        out = own
        for (sender, near), ref in zip(self.swaps, self.others):
            here = sender == place
            got = [ref[i * rows.span : (i + 1) * rows.span] for i in range(2)]
            out = got if out is None else [jnp.where(here, new, old) for new, old in zip(got, out)]
        return out

    def ahead(self, slope, offset):
        a, b = jnp.ones_like(slope), jnp.zeros_like(slope)
        for place in range(self.radix - 1):
            new_a, new_b = self.map_of(place, None)
            below = place < self.at
            a, b = jnp.where(below, new_a * a, a), jnp.where(below, new_a * b + new_b, b)
        return slope * a, slope * b + offset

    def total(self, own):
        a, b = self.map_of(0, own)
        for place in range(1, self.radix):
            new_a, new_b = self.map_of(place, own)
            a, b = new_a * a, new_a * b + new_b
        return a, b

    def collect(self, near, final):
        rows = Rows(self.nx)
        for (place, adjacent), ref in zip(self.swaps, self.others):
            if not adjacent:
                continue

            @pl.when(self.lowest & (place == self.at - 1))
            def _():
                near[rows.low : rows.low + rows.info] = ref[rows.map : rows.final]

            @pl.when(self.highest & (place == self.at + 1))
            def _():
                near[rows.high : rows.high + rows.info] = ref[rows.map : rows.final]
                rest = slice(0, rows.map) if final else slice(rows.final, rows.full)
                near[rows.high + rows.info : rows.near] = ref[rest]


def start_near(near, nx, nz):
    rows = Rows(nx)
    near[: rows.span] = jnp.ones((rows.span, nz), jnp.float32)
    near[rows.span :] = jnp.zeros((near.shape[0] - rows.span, nz), jnp.float32)


def join_kernel(radix, stride, final, nx, is_first, *refs):
    rows = Rows(nx)
    total, last_info, first_info, near_in = refs[:4]
    others, near, outs = refs[4 : 3 + radix], refs[3 + radix], refs[4 + radix :]
    nz = near.shape[1]
    if is_first:
        start_near(near, nx, nz)
    else:
        near[...] = near_in[...]
    group = Group(radix, stride, others, nx)
    own = [total[i * rows.span : (i + 1) * rows.span] for i in range(2)]
    ahead = group.ahead(near[: rows.span], near[rows.span : rows.map])
    write_rows(near, ahead)
    group.collect(near, False)
    whole = group.total(own)
    if final == 0:
        write_rows(outs[0], whole)
        return
    me, count = lax.axis_index("gy"), lax.axis_size("gy")
    for (senders, adjacent), out in zip(matchings(count, final, stride * radix), outs):
        up = look_up(senders) > me
        if not adjacent:
            write_rows(out, whole)
            continue

        @pl.when(up)
        def _():
            write_rows(out, whole)
            out[rows.map : rows.final] = last_info[: rows.info]

        @pl.when(jnp.logical_not(up))
        def _():
            out[: rows.map] = first_info[rows.info : rows.info + rows.rest]
            out[rows.map : rows.final] = first_info[: rows.info]


def full_message(nx, total, last_info, first_info, senders):
    rows = Rows(nx)
    onward = jnp.concatenate([total[: rows.map], last_info[: rows.info], first_info[rows.info : rows.info + rows.rest]])
    back = jnp.concatenate([total[: rows.map], first_info[: rows.info + rows.rest]])
    message = jnp.where(look_up(senders) > lax.axis_index("gy"), onward, back)
    return jnp.pad(message, ((0, -rows.full % 8), (0, 0)))


def third_kernel(radix, stride, *refs):
    st, extra, coarse, near_in = refs[:4]
    others, (out, sc, wide, near, done, sems) = refs[4 : 3 + radix], refs[3 + radix :]
    planes, rows, ext, nz = st.shape
    ny, nx = rows - 2, ext - 2 * PAD
    edge = edge_weights((ext, nz))
    blocks = ny // 2

    lay = Rows(nx)
    span = lay.span
    near[...] = near_in[...]
    group = Group(radix, stride, others, nx)
    if radix > 1:
        group.collect(near, True)
    gas_in = group.ahead(near[:span], near[span : lay.map])[1]
    at_high = lay.high + lay.info
    starts = [lay.low, lay.low + span, lay.high, lay.high + span, at_high, at_high + span]
    for k, v in enumerate([gas_in] + [near[start : start + span] for start in starts]):
        wide[k, : PAD - 2] = jnp.zeros((PAD - 2, nz), jnp.float32)
        wide[k, ext - PAD + 2 :] = jnp.zeros((PAD - 2, nz), jnp.float32)
        wide[k, pl.ds(PAD - 2, span, 2), :] = v
        wide[k, pl.ds(PAD - 1, span, 2), :] = v
    for k, start in enumerate((lay.low, lay.low + nx + 2, lay.high, lay.high + nx + 2)):
        start += lay.map
        wide[7 + k, :PAD] = jnp.zeros((PAD, nz), jnp.float32)
        wide[7 + k, ext - PAD :] = jnp.zeros((PAD, nz), jnp.float32)
        wide[7 + k, PAD - 1 : PAD + nx + 1] = near[start : start + nx + 2]

    gas_in = wide[0]
    last = ny + 1
    solid_low = wide[1] + wide[2] * gas_in
    sc[0, 0] = st[SA, 0] + solid_low
    sc[1, 0] = st[GA, 0] + gas_in

    def correct(j, carry):
        gas = coarse[2, j] * gas_in + coarse[3, j]
        solid = coarse[0, j] + coarse[1, j] * gas
        for i in (2 * j + 1, 2 * j + 2):
            sc[0, i] = st[SA, i] + solid
            sc[1, i] = st[GA, i] + gas
        return carry

    lax.fori_loop(0, blocks, correct, 0)
    gas = coarse[2, blocks - 1] * gas_in + coarse[3, blocks - 1]
    gas_high = wide[5] * gas + wide[4]
    solid_high = wide[3] + wide[6] * gas_high
    sc[0, last] = st[SA, last] + solid_high
    sc[1, last] = st[GA, last] + gas_high

    view = Fields(st, sc)
    for i, is_after, solid, gas in ((0, False, solid_low, gas_in), (last, True, solid_high, gas_high)):
        side = 3 if is_after else 0
        fy = extra[side + 2]
        to = 9 if is_after else 7
        rs = extra[side] + wide[to] + fy * solid
        rg = extra[side + 1] + wide[to + 1] + (CONDUCT if is_after else CONDUCT + FLOW) * gas
        res = outer_residual(view, i, SA, rs, rg, fy, edge, is_after)
        sc[2, i], sc[3, i] = relaxed(view, i, SA, *res)

    def sweep(k, carry):
        stores = []
        for r in range(GROUP):
            i = GROUP * k + 1 + r
            new_s, new_g = relaxed(view, i, SA, *row_residual(view, i, SA, edge))
            stores += [((2, i), new_s), ((3, i), new_g)]
        for at, value in stores:
            sc[at] = value
        return carry

    lax.fori_loop(0, ny // GROUP, sweep, 0)

    def leaving(k):
        part = pl.ds(GROUP * k, GROUP)
        return pltpu.make_async_copy(done.at[:, part], out.at[:, part], sems.at[k])

    def final(k, carry):
        stores = []
        for r in range(GROUP):
            i = GROUP * k + 1 + r
            new_s, new_g = last_relaxed(view, i, SB, edge, slice(PAD, PAD + nx))
            stores += [((0, i - 1), new_s), ((1, i - 1), new_g)]
        for at, value in stores:
            done[at] = value
        leaving(k).start()
        return carry

    lax.fori_loop(0, ny // GROUP, final, 0)
    for k in range(ny // GROUP):
        leaving(k).wait()


class Fields:
    def __init__(self, st, sc):
        self.st, self.sc = st, sc

    def __getitem__(self, at):
        return (self.sc if at[0] <= GB else self.st)[at]


def cost(rows, cells):
    return pl.CostEstimate(flops=50 * rows * cells, bytes_accessed=16 * 4 * rows * cells, transcendentals=0)


def swap(x, axis, first):
    pairs = []
    for i in range(first, lax.axis_size(axis) - 1, 2):
        pairs += [(i, i + 1), (i + 1, i)]
    return lax.ppermute(x, axis, pairs)


def shards(temps, right_side, exchange, coupling):
    temps, right_side = (jnp.transpose(a, (0, 2, 1, 3)) for a in (temps, right_side))
    exchange, coupling = (jnp.transpose(a, (1, 0, 2)) for a in (exchange, coupling))
    temps, right_side, exchange, coupling = (
        pltpu.with_memory_space_constraint(a, pltpu.HBM) for a in (temps, right_side, exchange, coupling)
    )
    ny, nx, nz = exchange.shape
    ext = nx + 2 * PAD
    f32 = functools.partial(jax.ShapeDtypeStruct, dtype=jnp.float32)

    strip = f32((strip_height(ny), nz))
    state = f32((PLANES, ny + 2, ext, nz))
    one, two, st = pl.pallas_call(
        pack_kernel,
        out_shape=(strip, strip, state),
        in_specs=[HBM] * 4,
        out_specs=(VMEM,) * 3,
        scratch_shapes=[pltpu.SemaphoreType.DMA((6,))],
        compiler_params=PARAMS,
        name="pack_x",
    )(temps, right_side, exchange, coupling)
    one, two = swap(one, "gx", 0), swap(two, "gx", 1)

    def letter(planes):
        return f32((planes, ext - 2 * CROP, nz))

    st, early = pl.pallas_call(
        conduct_kernel,
        out_shape=(state, f32((EARLY, nx, nz))),
        in_specs=[VMEM],
        out_specs=(VMEM,) * 2,
        input_output_aliases={0: 0},
        compiler_params=PARAMS,
        cost_estimate=cost(2 * ny, ext * nz),
        name="conduct",
    )(st)
    early = swap(early, "gy", 1)
    st, across = pl.pallas_call(
        first_kernel,
        out_shape=(state, f32((across_parts(ext)[1], nz))),
        in_specs=[VMEM] * 3,
        out_specs=(VMEM,) * 2,
        input_output_aliases={0: 0},
        compiler_params=PARAMS,
        name="first",
    )(st, one, two)
    st, *beside = pl.pallas_call(
        other_kernel,
        out_shape=(state,) + (letter(THIRD),) * (MESSAGE // THIRD),
        in_specs=[VMEM] * 3,
        out_specs=(VMEM,) * (1 + MESSAGE // THIRD),
        input_output_aliases={0: 0},
        compiler_params=PARAMS,
        name="other",
    )(st, one, two)
    across = swap(across, "gy", 1)

    rows = f32((4, ny // 2, ext, nz))
    st, coarse = pl.pallas_call(
        inner_kernel,
        out_shape=(state, rows),
        in_specs=[VMEM] * 2,
        out_specs=(VMEM,) * 2,
        input_output_aliases={0: 0},
        compiler_params=PARAMS,
        cost_estimate=cost(4 * ny, ext * nz),
        name="inner",
    )(st, early)

    beside = [swap(part, "gy", 0) for part in beside]

    lay = Rows(nx)

    def tall(height):
        return f32(((height + 7) // 8 * 8, nz))

    letter_room = pltpu.VMEM((MESSAGE, ext, nz), jnp.float32)
    more = f32((6, ext, nz))
    st, coarse, extra = pl.pallas_call(
        near_kernel,
        out_shape=(state, rows, more),
        in_specs=[VMEM] * (2 + len(beside)),
        out_specs=(VMEM,) * 3,
        scratch_shapes=[letter_room],
        input_output_aliases={0: 0, 1: 1},
        compiler_params=PARAMS,
        name="near",
    )(st, coarse, *beside)
    st, coarse, extra, total, last_info, first_info, message = pl.pallas_call(
        second_kernel,
        out_shape=(state, rows, more, tall(lay.map), tall(lay.info), tall(lay.info + lay.rest), tall(lay.full)),
        in_specs=[VMEM] * 5,
        out_specs=(VMEM,) * 7,
        scratch_shapes=[letter_room, pltpu.VMEM((8, ext, nz), jnp.float32)],
        input_output_aliases={0: 0, 1: 1, 2: 2},
        compiler_params=PARAMS,
        name="second",
    )(st, coarse, extra, early, across)

    near, messages = total, [message]
    count = lax.axis_size("gy")
    radices, stride = stages(count), 1
    for place, radix in enumerate(radices[:-1]):
        swaps = matchings(count, radix, stride)
        if place:
            messages = [full_message(nx, total, last_info, first_info, senders) for senders, _ in swaps]
        others = exchange_stage(messages, swaps)
        final = radices[-1] if place == len(radices) - 2 else 0
        following = matchings(count, final, stride * radix) if final else []
        outs = [tall(lay.final if adjacent else lay.map) for _, adjacent in following] if final else [tall(lay.map)]
        near, *messages = pl.pallas_call(
            functools.partial(join_kernel, radix, stride, final, nx, place == 0),
            out_shape=(tall(lay.near), *outs),
            in_specs=[VMEM] * (3 + radix),
            out_specs=(VMEM,) * (1 + len(outs)),
            compiler_params=PARAMS,
            name="join",
        )(total, last_info, first_info, near, *others)
        total = total if final else messages[0]
        stride *= radix
    got = exchange_stage(messages, matchings(count, radices[-1], stride))

    out = pl.pallas_call(
        functools.partial(third_kernel, radices[-1], stride),
        out_shape=f32((2, ny, nx, nz)),
        in_specs=[VMEM] * (4 + len(got)),
        out_specs=HBM,
        scratch_shapes=[
            pltpu.VMEM((4, ny + 2, ext, nz), jnp.float32),
            pltpu.VMEM((11, ext, nz), jnp.float32),
            pltpu.VMEM(tall(lay.near).shape, jnp.float32),
            pltpu.VMEM((2, ny, nx, nz), jnp.float32),
            pltpu.SemaphoreType.DMA((ny // GROUP,)),
        ],
        compiler_params=PARAMS,
        name="third",
    )(st, extra, coarse, near, *got)
    return jnp.transpose(out, (0, 2, 1, 3))


def solution(mesh):
    return jax.shard_map(
        shards,
        mesh=mesh,
        in_specs=(
            P(None, "gx", "gy", None),
            P(None, "gx", "gy", None),
            P("gx", "gy", None),
            P("gx", "gy", None),
        ),
        out_specs=P(None, "gx", "gy", None),
        check_vma=False,
    )
```

```python
import functools

import jax
import jax.numpy as jnp
from jax import lax
from jax.experimental import pallas as pl
from jax.experimental.pallas import tpu as pltpu
from jax.sharding import PartitionSpec as P

SOLID_CAP, GAS_CAP, FLOW, CONDUCT, RELAX, LUMP = 0.5, 0.02, 40.0, 0.05, 0.8, 0.25
GAS_SELF = GAS_CAP + 4.5 * CONDUCT

PAD = 8
WX = 5
CROP = 4
(SA, GA, SB, GB, K, C, RS, RG, FX, FZ, H, FY, ASS, ASG, AGG) = range(15)
PLANES = 15
(M_S, M_G, M_K, M_C, M_FY, M_1S, M_1G, M_2S, M_2G) = range(9)
MESSAGE, EARLY, THIRD = 9, 7, 3

GROUP = 6

VMEM = pl.BlockSpec(memory_space=pltpu.VMEM)
HBM = pl.BlockSpec(memory_space=pltpu.HBM)
PARAMS = pltpu.CompilerParams(vmem_limit_bytes=40 * 1024 * 1024)


def up_x(v):
    return pltpu.roll(v, v.shape[0] - 1, 0)


def down_x(v):
    return pltpu.roll(v, 1, 0)


def up_z(v):
    return pltpu.roll(v, v.shape[1] - 1, 1)


def down_z(v):
    return pltpu.roll(v, 1, 1)


def lanes(shape):
    return lax.broadcasted_iota(jnp.int32, shape, 1)


def x_mask(shape, nx):
    row = lax.broadcasted_iota(jnp.int32, shape, 0)
    place, count = lax.axis_index("gx"), lax.axis_size("gx")
    low = jnp.where(place == 0, PAD, PAD - WX)
    high = jnp.where(place == count - 1, PAD + nx, PAD + nx + WX)
    return jnp.where((row >= low) & (row < high), 1.0, 0.0).astype(jnp.float32)


PAIRS = ((SA, GA), (C, RS), (RG, K))
STRIP_ROWS = 8 * len(PAIRS)


def strip_height(ny):
    return ny * STRIP_ROWS + ny


def sublanes(nz):
    return lax.broadcasted_iota(jnp.int32, (8, nz), 0)


def conductivity_of(s, exchange):
    return 1.0 + 4.0 * exchange * s * s * s


def strip_side(s, g, k, rs, rg, c, low):
    row = sublanes(s.shape[1])
    inn, shift = (3, 7) if low else (4, 1)
    k_out, s_out, g_out = (pltpu.roll(v, shift, 0) for v in (k, s, g))
    rs = rs + jnp.where(row == inn, 0.5 * (k + k_out) * s_out, 0.0)
    rg = rg + jnp.where(row == inn, CONDUCT * g_out, 0.0)
    values = {SA: s, GA: g, K: k, RS: rs, RG: rg, C: c}
    tiles = []
    for a, b in PAIRS:
        a, b = values[a], values[b]
        a, b = (a, pltpu.roll(b, 4, 0)) if low else (pltpu.roll(a, 4, 0), b)
        tiles.append(jnp.where(row < 4, a, b))
    return tiles, (k[4:5] if low else k[3:4])


def pack_kernel(temps, right, exchange, coupling, one, two, late, st, sems):
    even = lax.axis_index("gx") % 2 == 0
    ny, nx, nz = exchange.shape
    copies = []
    for k, (plane, ref) in enumerate(
        ((SA, temps.at[0]), (K, exchange), (GA, temps.at[1]), (C, coupling), (RS, right.at[0]), (RG, right.at[1]))
    ):
        to = st.at[plane, pl.ds(1, ny), pl.ds(PAD, nx)]
        copies.append(pltpu.make_async_copy(ref, to, sems.at[k]))
    for copy in copies:
        copy.start()
    for copy in copies:
        copy.wait()
    for i in range(1, ny + 1):
        sides = []
        for start in (PAD, PAD + nx - 8):
            s, g, e, rs, rg, c = (st[plane, i, start : start + 8] for plane in (SA, GA, K, RS, RG, C))
            sides.append(strip_side(s, g, conductivity_of(s, e), rs, rg, c, start == PAD))
        (low, low_k), (high, high_k) = sides
        for p in range(len(PAIRS)):
            part = slice((i - 1) * STRIP_ROWS + 8 * p, (i - 1) * STRIP_ROWS + 8 * p + 8)
            one[part] = jnp.where(even, high[p], low[p])
            late[part] = jnp.where(even, high[p], low[p])
            two[part] = jnp.where(even, low[p], high[p])
        part = slice(ny * STRIP_ROWS + i - 1, ny * STRIP_ROWS + i)
        one[part] = jnp.where(even, high_k, low_k)
        late[part] = jnp.where(even, high_k, low_k)
        two[part] = jnp.where(even, low_k, high_k)


def conduct_kernel(st_in, st, early):
    del st_in
    planes, rows, ext, nz = st.shape
    ny, nx = rows - 2, ext - 2 * PAD
    odd = lax.axis_index("gy") % 2 == 1
    own = slice(PAD, PAD + nx)
    for i in range(1, ny + 1):
        st[K, i, own] = conductivity_of(st[SA, i, own], st[K, i, own])
    for is_odd, e, d in ((True, ny, ny - 1), (False, 1, 2)):

        @pl.when(odd == is_odd)
        def _():
            s, s_d, g, g_d = st[SA, e, own], st[SA, d, own], st[GA, e, own], st[GA, d, own]
            c, k, k_d = st[C, e, own], st[K, e, own], st[K, d, own]
            fx, fz, h, _ = faces(k)
            fy = 0.5 * (k + k_d)
            part_s, part_g = inner(s, g, c, h, fx, fz, edge_weights((nx, nz)))
            m_1s, m_1g = first_partial(st[RS, e, own] + part_s, st[RG, e, own] + part_g, s, s_d, g, g_d, fy, is_odd)
            for plane, value in enumerate((s, g, k, c, fy, m_1s, m_1g)):
                early[plane] = value


def place_halo(st, strips, y, nx):
    one, two, late = strips
    place = lax.axis_index("gx")
    even, soon = place % 2 == 0, place % 4 < 2
    ny, row = st.shape[1] - 2, sublanes(st.shape[3])
    i = y + 1

    def received(part):
        a, b = jnp.where(soon, one[part], late[part]), two[part]
        return jnp.where(even, b, a), jnp.where(even, a, b)

    for p, (plane_a, plane_b) in enumerate(PAIRS):
        before, after = received(slice(y * STRIP_ROWS + 8 * p, y * STRIP_ROWS + 8 * p + 8))
        before = {plane_a: pltpu.roll(before, 4, 0), plane_b: before}
        after = {plane_a: after, plane_b: pltpu.roll(after, 4, 0)}
        for plane in (plane_a, plane_b):
            low, high = jnp.where(row >= 4, before[plane], 0.0), jnp.where(row < 4, after[plane], 0.0)
            if plane == K:
                k_low, k_high = received(slice(ny * STRIP_ROWS + y, ny * STRIP_ROWS + y + 1))
                low, high = jnp.where(row == 3, k_low, low), jnp.where(row == 4, k_high, high)
            st[plane, i, :PAD] = low
            st[plane, i, PAD + nx :] = high


def inner(s, g, c, h, fx, fz, edge):
    t = c * (s - g)
    flux_x = fx * (up_x(s) - s)
    flux_z = fz * (up_z(s) - s)
    part_s = (flux_x - down_x(flux_x)) + (flux_z - down_z(flux_z)) - h * s - t
    part_g = (
        t
        - GAS_SELF * g
        + CONDUCT * (up_x(g) + down_x(g))
        + edge[0] * up_z(g)
        + edge[1] * down_z(g)
    )
    return part_s, part_g


def edge_weights(shape):
    lane = lanes(shape)
    weight = jnp.float32(0.25 * CONDUCT)
    return jnp.where(lane == shape[1] - 1, 0.0, weight), jnp.where(lane == 0, 0.0, weight)


def row_inner(st, i, s_at, edge):
    return inner(st[s_at, i], st[s_at + 1, i], st[C, i], st[H, i], st[FX, i], st[FZ, i], edge)


def row_residual(st, i, s_at, edge):
    part_s, part_g = row_inner(st, i, s_at, edge)
    s, g, before = st[s_at, i], st[s_at + 1, i], st[s_at + 1, i - 1]
    part_s += st[FY, i] * (st[s_at, i + 1] - s) + st[FY, i - 1] * (st[s_at, i - 1] - s)
    part_g += CONDUCT * (st[s_at + 1, i + 1] + before) - FLOW * (g - before)
    return st[RS, i] + part_s, st[RG, i] + part_g


def relaxed(st, i, s_at, res_s, res_g):
    s = st[s_at, i] + st[ASS, i] * res_s + st[ASG, i] * res_g
    g = st[s_at + 1, i] + st[ASG, i] * res_s + st[AGG, i] * res_g
    return s, g


def faces(k):
    lane = lanes(k.shape)
    end = k.shape[1] - 1
    fx = 0.5 * (k + up_x(k))
    fz = jnp.where(lane == end, 0.0, 0.125 * (k + up_z(k)))
    h = SOLID_CAP + jnp.where((lane == 0) | (lane == end), 0.125 * k, 0.0)
    return fx, fz, h, h + (fx + down_x(fx)) + (fz + down_z(fz))


def inverse(diag, c, mask):
    gas_diag = (GAS_SELF + FLOW) + c
    inv = (RELAX * mask) / (diag * gas_diag - c * c)
    return inv * gas_diag, inv * c, inv * diag


def last_relaxed(st, i, s_at, edge, own):
    full_s, full_g = st[s_at, i], st[s_at + 1, i]
    s, g = full_s[own], full_g[own]
    flux_x = st[FX, i] * (up_x(full_s) - full_s)
    flux_z = st[FZ, i, own] * (up_z(s) - s)
    c, before = st[C, i, own], st[s_at + 1, i - 1, own]
    t = c * (s - g)
    res_s = st[RS, i, own] + (flux_x[own] - down_x(flux_x)[own]) + (flux_z - down_z(flux_z)) - st[H, i, own] * s - t
    res_s += st[FY, i, own] * (st[s_at, i + 1, own] - s) + st[FY, i - 1, own] * (st[s_at, i - 1, own] - s)
    res_g = st[RG, i, own] + t - GAS_SELF * g + edge[0][own] * up_z(g) + edge[1][own] * down_z(g)
    res_g += CONDUCT * (up_x(full_g)[own] + down_x(full_g)[own] + st[s_at + 1, i + 1, own] + before) - FLOW * (g - before)
    ss, sg, gg = st[ASS, i, own], st[ASG, i, own], st[AGG, i, own]
    return s + ss * res_s + sg * res_g, g + sg * res_s + gg * res_g


def grouped(rows, work):
    for start in range(0, len(rows), GROUP):
        stores = []
        for i in rows[start : start + GROUP]:
            stores += work(i)
        for ref, at, value in stores:
            ref[at] = value


def looped(first, last, size, work):
    def group(k, carry):
        grouped([first + size * k + r for r in range(size)], work)
        return carry

    lax.fori_loop(0, (last - first) // size, group, 0)
    grouped(list(range(last - (last - first) % size, last)), work)


def row_coefficients(st, i, mask):
    fx, fz, h, diag = faces(st[K, i])
    fy = 0.5 * (st[K, i] + st[K, i + 1])
    before = 0.5 * (st[K, i] + st[K, i - 1])
    ss, sg, gg = inverse(diag + st[C, i] + fy + before, st[C, i], mask)
    values = ((FX, fx), (FZ, fz), (H, h), (FY, fy), (ASS, ss), (ASG, sg), (AGG, gg))
    return [(st, (plane, i), v) for plane, v in values]


def row_sweep(st, i, source, target, edge):
    s, g = relaxed(st, i, source, *row_residual(st, i, source, edge))
    return [(st, (target, i), s), (st, (target + 1, i), g)]


def first_partial(res_s, res_g, s, s_d, g, g_d, fy, onward):
    return res_s + fy * (s_d - s), res_g + CONDUCT * g_d - FLOW * (g - g_d if onward else g)


def send_planes(st, onward, edge):
    ny = st.shape[1] - 2
    e, d, near = (ny, ny - 1, ny - 1) if onward else (1, 2, 1)
    fy, s, g, g_d = st[FY, near], st[SA, e], st[GA, e], st[GA, d]
    part_s, part_g = row_inner(st, e, SA, edge)
    m_1s, m_1g = first_partial(st[RS, e] + part_s, st[RG, e] + part_g, s, st[SA, d], g, g_d, fy, onward)
    m_2s = st[RS, e] + fy * st[SB, d]
    m_2g = st[RG, e] + (CONDUCT + FLOW if onward else CONDUCT) * st[GB, d]
    return [s, g, st[K, e], st[C, e], fy, m_1s, m_1g, m_2s, m_2g]


def across_parts(ext):
    parts, at = [], 0
    for k in range(EARLY, MESSAGE):
        parts.append((k, CROP, ext - CROP, at))
        at += ext - 2 * CROP
    for k in range(EARLY):
        more = 1 if k in (M_1S, M_1G) else 0
        for low, high in ((CROP, PAD + more), (ext - PAD - more, ext - CROP)):
            parts.append((k, low, high, at))
            at += high - low
    return parts, (at + 7) // 8 * 8


def write_across(ref, k, value):
    for plane, low, high, at in across_parts(value.shape[0])[0]:
        if plane == k:
            ref[at : at + high - low] = value[low:high]


def read_across(early, across, outer, k):
    ext = outer.shape[1]
    if k < EARLY:
        outer[k, PAD : ext - PAD] = early[k]
    for plane, low, high, at in across_parts(ext)[0]:
        if plane == k:
            outer[k, low:high] = across[at : at + high - low]


def write_beside(refs, k, value):
    refs[k // THIRD][k % THIRD] = value[CROP : value.shape[0] - CROP]


def read_beside(refs, outer, k):
    outer[k, CROP : outer.shape[1] - CROP] = refs[k // THIRD][k % THIRD]


def first_end(st, strips, after, write):
    planes, rows, ext, nz = st.shape
    ny, nx = rows - 2, ext - 2 * PAD
    mask = x_mask((ext, nz), nx)
    edge = edge_weights((ext, nz))
    e, d, f = (ny, ny - 1, ny - 2) if after else (1, 2, 3)
    for i in (e, d, f):
        place_halo(st, strips, i - 1, nx)
    fx, fz, h, diag = faces(st[K, e])
    st[FX, e], st[FZ, e], st[H, e] = fx, fz, h
    st[FY, min(e, d)] = 0.5 * (st[K, e] + st[K, d])
    st[FY, min(d, f)] = 0.5 * (st[K, d] + st[K, f])
    grouped([d], lambda i: row_coefficients(st, i, mask))
    grouped([d], lambda i: row_sweep(st, i, SA, SB, edge))
    for k, value in enumerate(send_planes(st, after, edge)):
        write(k, value)


def either_first(st, strips, after, write):
    for is_after in (True, False):

        @pl.when(after == is_after)
        def _():
            first_end(st, strips, is_after, write)


def first_kernel(st_in, one, two, late, st, across):
    del st_in
    either_first(st, (one, two, late), lax.axis_index("gy") % 2 == 1, functools.partial(write_across, across))


def other_kernel(st_in, one, two, late, st, *beside):
    del st_in
    either_first(st, (one, two, late), lax.axis_index("gy") % 2 == 0, functools.partial(write_beside, beside))
    planes, rows, ext, nz = st.shape
    ny, nx = rows - 2, ext - 2 * PAD
    mask = x_mask((ext, nz), nx)
    for y in range(3, ny - 3):
        place_halo(st, (one, two, late), y, nx)
    grouped(list(range(3, ny - 1)), lambda i: row_coefficients(st, i, mask))


def outer_residual(st, i, s_at, rs, rg, fy_out, edge, after):
    part_s, part_g = row_inner(st, i, s_at, edge)
    s, g = st[s_at, i], st[s_at + 1, i]
    if after:
        part_s += st[FY, i - 1] * (st[s_at, i - 1] - s)
        part_g += (CONDUCT + FLOW) * st[s_at + 1, i - 1]
    else:
        part_s += st[FY, i] * (st[s_at, i + 1] - s)
        part_g += CONDUCT * st[s_at + 1, i + 1]
    return rs + part_s - fy_out * s, rg + part_g - FLOW * g


def pair_x(v):
    row = lax.broadcasted_iota(jnp.int32, v.shape, 0)
    return v + jnp.where(row % 2 == 0, up_x(v), down_x(v))


def coarse_coefficients(c_sum, k_sum):
    per_solid = 1.0 / (4.0 * SOLID_CAP + c_sum + LUMP * k_sum)
    ratio = c_sum * per_solid
    return per_solid, ratio, 1.0 / ((4.0 * GAS_CAP + 2.0 * FLOW) + c_sum - c_sum * ratio)


def coarse_row(st, coarse, j, mask, edge):
    i = 2 * j + 1
    res_s, res_g = row_residual(st, i, SA, edge)
    more_s, more_g = row_residual(st, i + 1, SA, edge)
    res_s, res_g = pair_x((res_s + more_s) * mask), pair_x((res_g + more_g) * mask)
    c_sum = pair_x(st[C, i] + st[C, i + 1])
    per_solid, ratio, per_gas = coarse_coefficients(c_sum, pair_x(st[K, i] + st[K, i + 1]))
    lead = res_s * per_solid
    values = (lead, ratio, (2.0 * FLOW) * per_gas, (res_g + c_sum * lead) * per_gas)
    return [(coarse, (k, j), v) for k, v in enumerate(values)]


def inner_kernel(st_in, early, st, coarse):
    del st_in, early
    planes, rows, ext, nz = st.shape
    ny, nx = rows - 2, ext - 2 * PAD
    shape = (ext, nz)
    mask = x_mask(shape, nx)
    edge = edge_weights(shape)
    looped(3, ny - 1, 4, lambda i: row_sweep(st, i, SA, SB, edge))
    looped(3, ny - 1, 4, lambda i: row_sweep(st, i, SB, SA, edge))
    grouped(list(range(2, ny // 2 - 2)), lambda j: coarse_row(st, coarse, j, mask, edge))


def end_work(st, coarse, extra, read, outer, is_after):
    planes, rows, ext, nz = st.shape
    ny, nx = rows - 2, ext - 2 * PAD
    me, count = lax.axis_index("gy"), lax.axis_size("gy")
    mask = x_mask((ext, nz), nx)
    inside = jnp.where(me == (count - 1 if is_after else 0), 0.0, mask)
    edge = edge_weights((ext, nz))
    zeros = jnp.zeros((PAD, nz), jnp.float32)
    for k in range(MESSAGE):
        outer[k, :PAD] = zeros
        outer[k, ext - PAD :] = zeros
        read(outer, k)

    o, e, near = (ny + 1, ny, ny) if is_after else (0, 1, 0)
    to_o = CONDUCT + FLOW if is_after else CONDUCT
    s_o, g_o, k_o, c_o, fy_out = (outer[plane] for plane in (M_S, M_G, M_K, M_C, M_FY))
    fy = 0.5 * (k_o + st[K, e])
    fx, fz, h, diag = faces(k_o)
    inv_o = inverse(diag + c_o + fy_out + fy, c_o, inside)
    fx_e, fz_e = st[FX, e], st[FZ, e]
    diag = st[H, e] + (fx_e + down_x(fx_e)) + (fz_e + down_z(fz_e)) + st[C, e] + fy
    inv_e = inverse(diag + st[FY, near - 1 if is_after else near + 1], st[C, e], mask)
    for plane, value in ((SA, s_o), (GA, g_o), (K, k_o), (C, c_o), (FX, fx), (FZ, fz), (H, h)):
        st[plane, o] = value
    st[FY, near] = fy
    for k in range(3):
        st[ASS + k, o], st[ASS + k, e] = inv_o[k], inv_e[k]

    res = outer[M_1S] + fy * (st[SA, e] - s_o), outer[M_1G] + to_o * st[GA, e]
    new_o = relaxed(st, o, SA, *res)
    stores = row_sweep(st, e, SA, SB, edge)
    st[SB, o], st[GB, o] = new_o
    for ref, at, value in stores:
        ref[at] = value
    res = outer_residual(st, o, SB, outer[M_2S], outer[M_2G], fy_out, edge, is_after)
    new_o = relaxed(st, o, SB, *res)
    ends = [e - 1, e] if is_after else [e, e + 1]
    grouped(ends, lambda i: row_sweep(st, i, SB, SA, edge))
    st[SA, o], st[GA, o] = new_o
    for k, plane in enumerate((M_2S, M_2G, M_FY)):
        extra[(3 if is_after else 0) + k] = outer[plane]
    blocks = ny // 2
    stores = []
    for j in (blocks - 2, blocks - 1) if is_after else (0, 1):
        stores += coarse_row(st, coarse, j, mask, edge)
    for ref, at, value in stores:
        ref[at] = value


def either_end(after, st, coarse, extra, read, outer):
    for is_after in (True, False):

        @pl.when(after == is_after)
        def _():
            end_work(st, coarse, extra, read, outer, is_after)


def near_kernel(st_in, coarse_in, *refs):
    beside, (st, coarse, extra, outer) = refs[:-4], refs[-4:]
    del st_in, coarse_in
    either_end(lax.axis_index("gy") % 2 == 0, st, coarse, extra, functools.partial(read_beside, beside), outer)


def second_kernel(st_in, coarse_in, extra_in, early, across, *refs):
    st, coarse, extra, total, last_info, first_info, message, outer, squeeze = refs
    del st_in, coarse_in, extra_in
    planes, rows, ext, nz = st.shape
    ny, nx = rows - 2, ext - 2 * PAD
    me = lax.axis_index("gy")
    either_end(me % 2 == 1, st, coarse, extra, functools.partial(read_across, early, across), outer)

    blocks = ny // 2
    for k in range(4):
        squeeze[k] = coarse[k, 0]
    slopes, offsets = coarse[2, 0], coarse[3, 0]
    for j in range(1, blocks):
        slope = coarse[2, j]
        slopes, offsets = slope * slopes, slope * offsets + coarse[3, j]
        coarse[2, j], coarse[3, j] = slopes, offsets
    squeeze[4], squeeze[5], squeeze[6], squeeze[7] = slopes, offsets, coarse[0, blocks - 1], coarse[1, blocks - 1]

    span = nx // 2 + 2
    lead, ratio, slope, offset, slopes, offsets, lead_last, ratio_last = (
        squeeze[k, pl.ds(PAD - 2, span, 2), :] for k in range(8)
    )
    part = slice(PAD - 1, PAD + nx + 1)

    def increments(d, face, gas):
        return [(st[FY, face] * (st[SA, d] - st[SB, d]))[part], (gas * (st[GA, d] - st[GB, d]))[part]]

    onward = [lead_last, ratio_last] + increments(ny - 1, ny - 1, CONDUCT + FLOW)
    back = [lead, offset] + increments(2, 1, CONDUCT) + [slope, ratio]
    write_rows(total, [slopes, offsets])
    write_rows(last_info, onward)
    write_rows(first_info, back)
    for go, info in ((True, onward), (False, back)):

        @pl.when((me % 2 == 0) == go)
        def _():
            write_rows(message, [slopes, offsets] + info)


def write_rows(ref, values):
    at = 0
    for value in values:
        ref[at : at + value.shape[0]] = value
        at += value.shape[0]


class Rows:
    def __init__(self, nx):
        self.span = nx // 2 + 2
        self.map = 2 * self.span
        self.info = self.map + 2 * (nx + 2)
        self.rest = self.map
        self.final = self.map + self.info
        self.full = self.final + self.rest
        self.low = self.map
        self.high = self.low + self.info
        self.near = self.high + self.info + self.rest


def source(at, k, radix):
    if radix & (radix - 1) == 0:
        return at ^ k
    return (at + radix - k) % radix


def matchings(count, radix, stride):
    if (count, radix, stride) == (8, 4, 2):
        swaps = ((1, 2), (3, 4), (5, 6), (0, 7)), ((0, 4), (1, 6), (2, 5), (3, 7)), ((0, 3), (1, 5), (2, 6), (4, 7))
        out = []
        for pairs in swaps:
            senders = [0] * count
            for a, b in pairs:
                senders[a], senders[b] = b, a
            out.append((senders, len(out) == 0))
        return out
    out = []
    for k in range(1, radix):
        senders = []
        for me in range(count):
            at, low = me // stride % radix, me % stride
            senders.append(me - low + (source(at, k, radix) - at) * stride + (stride - 1 - low))
        out.append((senders, any(abs(source(at, k, radix) - at) == 1 for at in range(radix))))
    return sorted(out, key=lambda item: not item[1])


def look_up(table):
    me, value = lax.axis_index("gy"), jnp.int32(table[0])
    for k in range(1, len(table)):
        value = jnp.where(me == k, table[k], value)
    return value


def stages(count):
    if count % 2:
        return [1, count]
    out, rest = [2], count // 2
    while rest > 1:
        radix = next((r for r in (8, 4, 2) if rest % r == 0), rest)
        out.append(radix)
        rest //= radix
    return out if len(out) > 1 else out + [1]


def exchange_stage(messages, swaps):
    return [
        lax.ppermute(message, "gy", [(sender, me) for me, sender in enumerate(senders)])
        for (senders, near), message in zip(swaps, messages)
    ]


class Group:
    def __init__(self, radix, stride, others, nx):
        self.radix, self.others, self.nx = radix, others, nx
        me = lax.axis_index("gy")
        self.swaps = [
            (look_up([sender // stride % radix for sender in senders]), near)
            for senders, near in matchings(lax.axis_size("gy"), radix, stride)
        ]
        self.at = lax.rem(lax.div(me, stride), radix)
        low = lax.rem(me, stride)
        self.lowest, self.highest = low == 0, low == stride - 1

    def map_of(self, place, own):
        rows = Rows(self.nx)
        out = own
        for (sender, near), ref in zip(self.swaps, self.others):
            here = sender == place
            got = [ref[i * rows.span : (i + 1) * rows.span] for i in range(2)]
            out = got if out is None else [jnp.where(here, new, old) for new, old in zip(got, out)]
        return out

    def ahead(self, slope, offset):
        a, b = jnp.ones_like(slope), jnp.zeros_like(slope)
        for place in range(self.radix - 1):
            new_a, new_b = self.map_of(place, None)
            below = place < self.at
            a, b = jnp.where(below, new_a * a, a), jnp.where(below, new_a * b + new_b, b)
        return slope * a, slope * b + offset

    def total(self, own):
        a, b = self.map_of(0, own)
        for place in range(1, self.radix):
            new_a, new_b = self.map_of(place, own)
            a, b = new_a * a, new_a * b + new_b
        return a, b

    def collect(self, near, final):
        rows = Rows(self.nx)
        for (place, adjacent), ref in zip(self.swaps, self.others):
            if not adjacent:
                continue

            @pl.when(self.lowest & (place == self.at - 1))
            def _():
                near[rows.low : rows.low + rows.info] = ref[rows.map : rows.final]

            @pl.when(self.highest & (place == self.at + 1))
            def _():
                near[rows.high : rows.high + rows.info] = ref[rows.map : rows.final]
                rest = slice(0, rows.map) if final else slice(rows.final, rows.full)
                near[rows.high + rows.info : rows.near] = ref[rest]


def start_near(near, nx, nz):
    rows = Rows(nx)
    near[: rows.span] = jnp.ones((rows.span, nz), jnp.float32)
    near[rows.span :] = jnp.zeros((near.shape[0] - rows.span, nz), jnp.float32)


def join_kernel(radix, stride, final, nx, is_first, *refs):
    rows = Rows(nx)
    total, last_info, first_info, near_in = refs[:4]
    others, near, outs = refs[4 : 3 + radix], refs[3 + radix], refs[4 + radix :]
    nz = near.shape[1]
    if is_first:
        start_near(near, nx, nz)
    else:
        near[...] = near_in[...]
    group = Group(radix, stride, others, nx)
    own = [total[i * rows.span : (i + 1) * rows.span] for i in range(2)]
    ahead = group.ahead(near[: rows.span], near[rows.span : rows.map])
    write_rows(near, ahead)
    group.collect(near, False)
    whole = group.total(own)
    if final == 0:
        write_rows(outs[0], whole)
        return
    me, count = lax.axis_index("gy"), lax.axis_size("gy")
    for (senders, adjacent), out in zip(matchings(count, final, stride * radix), outs):
        up = look_up(senders) > me
        if not adjacent:
            write_rows(out, whole)
            continue

        @pl.when(up)
        def _():
            write_rows(out, whole)
            out[rows.map : rows.final] = last_info[: rows.info]

        @pl.when(jnp.logical_not(up))
        def _():
            out[: rows.map] = first_info[rows.info : rows.info + rows.rest]
            out[rows.map : rows.final] = first_info[: rows.info]


def full_message(nx, total, last_info, first_info, senders):
    rows = Rows(nx)
    onward = jnp.concatenate([total[: rows.map], last_info[: rows.info], first_info[rows.info : rows.info + rows.rest]])
    back = jnp.concatenate([total[: rows.map], first_info[: rows.info + rows.rest]])
    message = jnp.where(look_up(senders) > lax.axis_index("gy"), onward, back)
    return jnp.pad(message, ((0, -rows.full % 8), (0, 0)))


def third_kernel(radix, stride, *refs):
    st, extra, coarse, near_in = refs[:4]
    others, (out, sc, wide, near, done, sems) = refs[4 : 3 + radix], refs[3 + radix :]
    planes, rows, ext, nz = st.shape
    ny, nx = rows - 2, ext - 2 * PAD
    edge = edge_weights((ext, nz))
    blocks = ny // 2

    lay = Rows(nx)
    span = lay.span
    near[...] = near_in[...]
    group = Group(radix, stride, others, nx)
    if radix > 1:
        group.collect(near, True)
    gas_in = group.ahead(near[:span], near[span : lay.map])[1]
    at_high = lay.high + lay.info
    starts = [lay.low, lay.low + span, lay.high, lay.high + span, at_high, at_high + span]
    for k, v in enumerate([gas_in] + [near[start : start + span] for start in starts]):
        wide[k, : PAD - 2] = jnp.zeros((PAD - 2, nz), jnp.float32)
        wide[k, ext - PAD + 2 :] = jnp.zeros((PAD - 2, nz), jnp.float32)
        wide[k, pl.ds(PAD - 2, span, 2), :] = v
        wide[k, pl.ds(PAD - 1, span, 2), :] = v
    for k, start in enumerate((lay.low, lay.low + nx + 2, lay.high, lay.high + nx + 2)):
        start += lay.map
        wide[7 + k, :PAD] = jnp.zeros((PAD, nz), jnp.float32)
        wide[7 + k, ext - PAD :] = jnp.zeros((PAD, nz), jnp.float32)
        wide[7 + k, PAD - 1 : PAD + nx + 1] = near[start : start + nx + 2]

    gas_in = wide[0]
    last = ny + 1
    solid_low = wide[1] + wide[2] * gas_in
    sc[0, 0] = st[SA, 0] + solid_low
    sc[1, 0] = st[GA, 0] + gas_in

    def correct(j, carry):
        gas = coarse[2, j] * gas_in + coarse[3, j]
        solid = coarse[0, j] + coarse[1, j] * gas
        for i in (2 * j + 1, 2 * j + 2):
            sc[0, i] = st[SA, i] + solid
            sc[1, i] = st[GA, i] + gas
        return carry

    lax.fori_loop(0, blocks, correct, 0, unroll=3)
    gas = coarse[2, blocks - 1] * gas_in + coarse[3, blocks - 1]
    gas_high = wide[5] * gas + wide[4]
    solid_high = wide[3] + wide[6] * gas_high
    sc[0, last] = st[SA, last] + solid_high
    sc[1, last] = st[GA, last] + gas_high

    view = Fields(st, sc)
    for i, is_after, solid, gas in ((0, False, solid_low, gas_in), (last, True, solid_high, gas_high)):
        side = 3 if is_after else 0
        fy = extra[side + 2]
        to = 9 if is_after else 7
        rs = extra[side] + wide[to] + fy * solid
        rg = extra[side + 1] + wide[to + 1] + (CONDUCT if is_after else CONDUCT + FLOW) * gas
        res = outer_residual(view, i, SA, rs, rg, fy, edge, is_after)
        sc[2, i], sc[3, i] = relaxed(view, i, SA, *res)

    def sweep(k, carry):
        stores = []
        for r in range(GROUP):
            i = GROUP * k + 1 + r
            new_s, new_g = relaxed(view, i, SA, *row_residual(view, i, SA, edge))
            stores += [((2, i), new_s), ((3, i), new_g)]
        for at, value in stores:
            sc[at] = value
        return carry

    lax.fori_loop(0, ny // GROUP, sweep, 0)

    def leaving(k):
        part = pl.ds(GROUP * k, GROUP)
        return pltpu.make_async_copy(done.at[:, part], out.at[:, part], sems.at[k])

    def final(k, carry):
        stores = []
        for r in range(GROUP):
            i = GROUP * k + 1 + r
            new_s, new_g = last_relaxed(view, i, SB, edge, slice(PAD, PAD + nx))
            stores += [((0, i - 1), new_s), ((1, i - 1), new_g)]
        for at, value in stores:
            done[at] = value
        leaving(k).start()
        return carry

    lax.fori_loop(0, ny // GROUP, final, 0)
    for k in range(ny // GROUP):
        leaving(k).wait()


class Fields:
    def __init__(self, st, sc):
        self.st, self.sc = st, sc

    def __getitem__(self, at):
        return (self.sc if at[0] <= GB else self.st)[at]


def cost(rows, cells):
    return pl.CostEstimate(flops=50 * rows * cells, bytes_accessed=16 * 4 * rows * cells, transcendentals=0)


def swap(x, axis, first, step=2):
    pairs = []
    for i in range(first, lax.axis_size(axis) - 1, step):
        pairs += [(i, i + 1), (i + 1, i)]
    return lax.ppermute(x, axis, pairs)


def shards(temps, right_side, exchange, coupling):
    temps, right_side = (jnp.transpose(a, (0, 2, 1, 3)) for a in (temps, right_side))
    exchange, coupling = (jnp.transpose(a, (1, 0, 2)) for a in (exchange, coupling))
    temps, right_side, exchange, coupling = (
        pltpu.with_memory_space_constraint(a, pltpu.HBM) for a in (temps, right_side, exchange, coupling)
    )
    ny, nx, nz = exchange.shape
    ext = nx + 2 * PAD
    f32 = functools.partial(jax.ShapeDtypeStruct, dtype=jnp.float32)

    strips = tuple(f32((strip_height(ny) + more, nz)) for more in (2, 1, 0))
    state = f32((PLANES, ny + 2, ext, nz))
    one, two, late, st = pl.pallas_call(
        pack_kernel,
        out_shape=strips + (state,),
        in_specs=[HBM] * 4,
        out_specs=(VMEM,) * 4,
        scratch_shapes=[pltpu.SemaphoreType.DMA((6,))],
        compiler_params=PARAMS,
        name="pack_x",
    )(temps, right_side, exchange, coupling)
    one, two, late = swap(one, "gx", 0, 4), swap(two, "gx", 1), swap(late, "gx", 2, 4)

    def letter(planes):
        return f32((planes, ext - 2 * CROP, nz))

    st, early = pl.pallas_call(
        conduct_kernel,
        out_shape=(state, f32((EARLY, nx, nz))),
        in_specs=[VMEM],
        out_specs=(VMEM,) * 2,
        input_output_aliases={0: 0},
        compiler_params=PARAMS,
        cost_estimate=cost(2 * ny, ext * nz),
        name="conduct",
    )(st)
    early = swap(early, "gy", 1)
    st, across = pl.pallas_call(
        first_kernel,
        out_shape=(state, f32((across_parts(ext)[1], nz))),
        in_specs=[VMEM] * 4,
        out_specs=(VMEM,) * 2,
        input_output_aliases={0: 0},
        compiler_params=PARAMS,
        name="first",
    )(st, one, two, late)
    st, *beside = pl.pallas_call(
        other_kernel,
        out_shape=(state,) + (letter(THIRD),) * (MESSAGE // THIRD),
        in_specs=[VMEM] * 4,
        out_specs=(VMEM,) * (1 + MESSAGE // THIRD),
        input_output_aliases={0: 0},
        compiler_params=PARAMS,
        name="other",
    )(st, one, two, late)
    across = swap(across, "gy", 1)

    rows = f32((4, ny // 2, ext, nz))
    st, coarse = pl.pallas_call(
        inner_kernel,
        out_shape=(state, rows),
        in_specs=[VMEM] * 2,
        out_specs=(VMEM,) * 2,
        input_output_aliases={0: 0},
        compiler_params=PARAMS,
        cost_estimate=cost(4 * ny, ext * nz),
        name="inner",
    )(st, early)

    beside = [swap(part, "gy", 0) for part in beside]

    lay = Rows(nx)

    def tall(height):
        return f32(((height + 7) // 8 * 8, nz))

    letter_room = pltpu.VMEM((MESSAGE, ext, nz), jnp.float32)
    more = f32((6, ext, nz))
    st, coarse, extra = pl.pallas_call(
        near_kernel,
        out_shape=(state, rows, more),
        in_specs=[VMEM] * (2 + len(beside)),
        out_specs=(VMEM,) * 3,
        scratch_shapes=[letter_room],
        input_output_aliases={0: 0, 1: 1},
        compiler_params=PARAMS,
        name="near",
    )(st, coarse, *beside)
    st, coarse, extra, total, last_info, first_info, message = pl.pallas_call(
        second_kernel,
        out_shape=(state, rows, more, tall(lay.map), tall(lay.info), tall(lay.info + lay.rest), tall(lay.full)),
        in_specs=[VMEM] * 5,
        out_specs=(VMEM,) * 7,
        scratch_shapes=[letter_room, pltpu.VMEM((8, ext, nz), jnp.float32)],
        input_output_aliases={0: 0, 1: 1, 2: 2},
        compiler_params=PARAMS,
        name="second",
    )(st, coarse, extra, early, across)

    near, messages = total, [message]
    count = lax.axis_size("gy")
    radices, stride = stages(count), 1
    for place, radix in enumerate(radices[:-1]):
        swaps = matchings(count, radix, stride)
        if place:
            messages = [full_message(nx, total, last_info, first_info, senders) for senders, _ in swaps]
        others = exchange_stage(messages, swaps)
        final = radices[-1] if place == len(radices) - 2 else 0
        following = matchings(count, final, stride * radix) if final else []
        outs = [tall(lay.final if adjacent else lay.map) for _, adjacent in following] if final else [tall(lay.map)]
        near, *messages = pl.pallas_call(
            functools.partial(join_kernel, radix, stride, final, nx, place == 0),
            out_shape=(tall(lay.near), *outs),
            in_specs=[VMEM] * (3 + radix),
            out_specs=(VMEM,) * (1 + len(outs)),
            compiler_params=PARAMS,
            name="join",
        )(total, last_info, first_info, near, *others)
        total = total if final else messages[0]
        stride *= radix
    got = exchange_stage(messages, matchings(count, radices[-1], stride))

    out = pl.pallas_call(
        functools.partial(third_kernel, radices[-1], stride),
        out_shape=f32((2, ny, nx, nz)),
        in_specs=[VMEM] * (4 + len(got)),
        out_specs=HBM,
        scratch_shapes=[
            pltpu.VMEM((4, ny + 2, ext, nz), jnp.float32),
            pltpu.VMEM((11, ext, nz), jnp.float32),
            pltpu.VMEM(tall(lay.near).shape, jnp.float32),
            pltpu.VMEM((2, ny, nx, nz), jnp.float32),
            pltpu.SemaphoreType.DMA((ny // GROUP,)),
        ],
        compiler_params=PARAMS,
        name="third",
    )(st, extra, coarse, near, *got)
    return jnp.transpose(out, (0, 2, 1, 3))


def solution(mesh):
    return jax.shard_map(
        shards,
        mesh=mesh,
        in_specs=(
            P(None, "gx", "gy", None),
            P(None, "gx", "gy", None),
            P("gx", "gy", None),
            P("gx", "gy", None),
        ),
        out_specs=P(None, "gx", "gy", None),
        check_vma=False,
    )
```

```python
import functools

import jax
import jax.numpy as jnp
from jax import lax
from jax.experimental import pallas as pl
from jax.experimental.pallas import tpu as pltpu
from jax.sharding import PartitionSpec as P

SOLID_CAP, GAS_CAP, FLOW, CONDUCT, RELAX, LUMP = 0.5, 0.02, 40.0, 0.05, 0.8, 0.25
GAS_SELF = GAS_CAP + 4.5 * CONDUCT

PAD = 8
WX = 5
CROP = 4
(SA, GA, SB, GB, K, C, RS, RG, FX, FZ, H, FY, ASS, ASG, AGG) = range(15)
PLANES = 15
(M_S, M_G, M_K, M_C, M_FY, M_1S, M_1G, M_2S, M_2G) = range(9)
MESSAGE, EARLY, THIRD = 9, 7, 3

GROUP = 6

VMEM = pl.BlockSpec(memory_space=pltpu.VMEM)
HBM = pl.BlockSpec(memory_space=pltpu.HBM)
PARAMS = pltpu.CompilerParams(vmem_limit_bytes=40 * 1024 * 1024)


def up_x(v):
    return pltpu.roll(v, v.shape[0] - 1, 0)


def down_x(v):
    return pltpu.roll(v, 1, 0)


def up_z(v):
    return pltpu.roll(v, v.shape[1] - 1, 1)


def down_z(v):
    return pltpu.roll(v, 1, 1)


def lanes(shape):
    return lax.broadcasted_iota(jnp.int32, shape, 1)


def x_mask(shape, nx):
    row = lax.broadcasted_iota(jnp.int32, shape, 0)
    place, count = lax.axis_index("gx"), lax.axis_size("gx")
    low = jnp.where(place == 0, PAD, PAD - WX)
    high = jnp.where(place == count - 1, PAD + nx, PAD + nx + WX)
    return jnp.where((row >= low) & (row < high), 1.0, 0.0).astype(jnp.float32)


PAIRS = ((SA, GA), (C, RS), (RG, K))
STRIP_ROWS = 8 * len(PAIRS)


def strip_height(ny):
    return ny * STRIP_ROWS + (ny + 7) // 8 * 8


def sublanes(nz):
    return lax.broadcasted_iota(jnp.int32, (8, nz), 0)


def conductivity_of(s, exchange):
    return 1.0 + 4.0 * exchange * s * s * s


def strip_side(s, g, k, rs, rg, c, low):
    row = sublanes(s.shape[1])
    inn, shift = (3, 7) if low else (4, 1)
    k_out, s_out, g_out = (pltpu.roll(v, shift, 0) for v in (k, s, g))
    rs = rs + jnp.where(row == inn, 0.5 * (k + k_out) * s_out, 0.0)
    rg = rg + jnp.where(row == inn, CONDUCT * g_out, 0.0)
    values = {SA: s, GA: g, K: k, RS: rs, RG: rg, C: c}
    tiles = []
    for a, b in PAIRS:
        a, b = values[a], values[b]
        a, b = (a, pltpu.roll(b, 4, 0)) if low else (pltpu.roll(a, 4, 0), b)
        tiles.append(jnp.where(row < 4, a, b))
    return tiles, (k[4:5] if low else k[3:4])


def pack_kernel(temps, right, exchange, coupling, one, two, st, sems):
    even = lax.axis_index("gx") % 2 == 0
    ny, nx, nz = exchange.shape
    halves = [(0, ny // 2), (ny // 2, ny - ny // 2)]
    copies = [[], []]
    for k, (plane, ref) in enumerate(
        ((SA, temps.at[0]), (K, exchange), (GA, temps.at[1]), (C, coupling), (RS, right.at[0]), (RG, right.at[1]))
    ):
        for h, (start, count) in enumerate(halves):
            to = st.at[plane, pl.ds(1 + start, count), pl.ds(PAD, nx)]
            copies[h].append(pltpu.make_async_copy(ref.at[pl.ds(start, count)], to, sems.at[6 * h + k]))
    for copy in copies[0] + copies[1]:
        copy.start()
    for i in range(1, ny + 1):
        for h, (start, count) in enumerate(halves):
            if i == start + 1:
                for copy in copies[h]:
                    copy.wait()
        sides = []
        for start in (PAD, PAD + nx - 8):
            s, g, e, rs, rg, c = (st[plane, i, start : start + 8] for plane in (SA, GA, K, RS, RG, C))
            sides.append(strip_side(s, g, conductivity_of(s, e), rs, rg, c, start == PAD))
        (low, low_k), (high, high_k) = sides
        for p in range(len(PAIRS)):
            part = slice((i - 1) * STRIP_ROWS + 8 * p, (i - 1) * STRIP_ROWS + 8 * p + 8)
            one[part] = jnp.where(even, high[p], low[p])
            two[part] = jnp.where(even, low[p], high[p])
        part = slice(ny * STRIP_ROWS + i - 1, ny * STRIP_ROWS + i)
        one[part] = jnp.where(even, high_k, low_k)
        two[part] = jnp.where(even, low_k, high_k)


def conduct_kernel(st_in, st, early):
    del st_in
    planes, rows, ext, nz = st.shape
    ny, nx = rows - 2, ext - 2 * PAD
    odd = lax.axis_index("gy") % 2 == 1
    own = slice(PAD, PAD + nx)
    for i in range(1, ny + 1):
        st[K, i, own] = conductivity_of(st[SA, i, own], st[K, i, own])
    for is_odd, e, d in ((True, ny, ny - 1), (False, 1, 2)):

        @pl.when(odd == is_odd)
        def _():
            s, s_d, g, g_d = st[SA, e, own], st[SA, d, own], st[GA, e, own], st[GA, d, own]
            c, k, k_d = st[C, e, own], st[K, e, own], st[K, d, own]
            fx, fz, h, _ = faces(k)
            fy = 0.5 * (k + k_d)
            part_s, part_g = inner(s, g, c, h, fx, fz, edge_weights((nx, nz)))
            m_1s, m_1g = first_partial(st[RS, e, own] + part_s, st[RG, e, own] + part_g, s, s_d, g, g_d, fy, is_odd)
            for plane, value in enumerate((s, g, k, c, fy, m_1s, m_1g)):
                early[plane] = value


def place_halo(st, one, two, y, nx):
    even = lax.axis_index("gx") % 2 == 0
    ny, row = st.shape[1] - 2, sublanes(st.shape[3])
    i = y + 1

    def received(part):
        a, b = one[part], two[part]
        return jnp.where(even, b, a), jnp.where(even, a, b)

    for p, (plane_a, plane_b) in enumerate(PAIRS):
        before, after = received(slice(y * STRIP_ROWS + 8 * p, y * STRIP_ROWS + 8 * p + 8))
        before = {plane_a: pltpu.roll(before, 4, 0), plane_b: before}
        after = {plane_a: after, plane_b: pltpu.roll(after, 4, 0)}
        for plane in (plane_a, plane_b):
            low, high = jnp.where(row >= 4, before[plane], 0.0), jnp.where(row < 4, after[plane], 0.0)
            if plane == K:
                k_low, k_high = received(slice(ny * STRIP_ROWS + y, ny * STRIP_ROWS + y + 1))
                low, high = jnp.where(row == 3, k_low, low), jnp.where(row == 4, k_high, high)
            st[plane, i, :PAD] = low
            st[plane, i, PAD + nx :] = high


def inner(s, g, c, h, fx, fz, edge):
    t = c * (s - g)
    flux_x = fx * (up_x(s) - s)
    flux_z = fz * (up_z(s) - s)
    part_s = (flux_x - down_x(flux_x)) + (flux_z - down_z(flux_z)) - h * s - t
    part_g = (
        t
        - GAS_SELF * g
        + CONDUCT * (up_x(g) + down_x(g))
        + edge[0] * up_z(g)
        + edge[1] * down_z(g)
    )
    return part_s, part_g


def edge_weights(shape):
    lane = lanes(shape)
    weight = jnp.float32(0.25 * CONDUCT)
    return jnp.where(lane == shape[1] - 1, 0.0, weight), jnp.where(lane == 0, 0.0, weight)


def row_inner(st, i, s_at, edge):
    return inner(st[s_at, i], st[s_at + 1, i], st[C, i], st[H, i], st[FX, i], st[FZ, i], edge)


def row_residual(st, i, s_at, edge):
    part_s, part_g = row_inner(st, i, s_at, edge)
    s, g, before = st[s_at, i], st[s_at + 1, i], st[s_at + 1, i - 1]
    part_s += st[FY, i] * (st[s_at, i + 1] - s) + st[FY, i - 1] * (st[s_at, i - 1] - s)
    part_g += CONDUCT * (st[s_at + 1, i + 1] + before) - FLOW * (g - before)
    return st[RS, i] + part_s, st[RG, i] + part_g


def relaxed(st, i, s_at, res_s, res_g):
    s = st[s_at, i] + st[ASS, i] * res_s + st[ASG, i] * res_g
    g = st[s_at + 1, i] + st[ASG, i] * res_s + st[AGG, i] * res_g
    return s, g


def faces(k):
    lane = lanes(k.shape)
    end = k.shape[1] - 1
    fx = 0.5 * (k + up_x(k))
    fz = jnp.where(lane == end, 0.0, 0.125 * (k + up_z(k)))
    h = SOLID_CAP + jnp.where((lane == 0) | (lane == end), 0.125 * k, 0.0)
    return fx, fz, h, h + (fx + down_x(fx)) + (fz + down_z(fz))


def inverse(diag, c, mask):
    gas_diag = (GAS_SELF + FLOW) + c
    inv = (RELAX * mask) / (diag * gas_diag - c * c)
    return inv * gas_diag, inv * c, inv * diag


def last_relaxed(st, i, s_at, edge, own):
    full_s, full_g = st[s_at, i], st[s_at + 1, i]
    s, g = full_s[own], full_g[own]
    flux_x = st[FX, i] * (up_x(full_s) - full_s)
    flux_z = st[FZ, i, own] * (up_z(s) - s)
    c, before = st[C, i, own], st[s_at + 1, i - 1, own]
    t = c * (s - g)
    res_s = st[RS, i, own] + (flux_x[own] - down_x(flux_x)[own]) + (flux_z - down_z(flux_z)) - st[H, i, own] * s - t
    res_s += st[FY, i, own] * (st[s_at, i + 1, own] - s) + st[FY, i - 1, own] * (st[s_at, i - 1, own] - s)
    res_g = st[RG, i, own] + t - GAS_SELF * g + edge[0][own] * up_z(g) + edge[1][own] * down_z(g)
    res_g += CONDUCT * (up_x(full_g)[own] + down_x(full_g)[own] + st[s_at + 1, i + 1, own] + before) - FLOW * (g - before)
    ss, sg, gg = st[ASS, i, own], st[ASG, i, own], st[AGG, i, own]
    return s + ss * res_s + sg * res_g, g + sg * res_s + gg * res_g


def grouped(rows, work):
    for start in range(0, len(rows), GROUP):
        stores = []
        for i in rows[start : start + GROUP]:
            stores += work(i)
        for ref, at, value in stores:
            ref[at] = value


def looped(first, last, size, work):
    def group(k, carry):
        grouped([first + size * k + r for r in range(size)], work)
        return carry

    lax.fori_loop(0, (last - first) // size, group, 0)
    grouped(list(range(last - (last - first) % size, last)), work)


def row_coefficients(st, i, mask):
    fx, fz, h, diag = faces(st[K, i])
    fy = 0.5 * (st[K, i] + st[K, i + 1])
    before = 0.5 * (st[K, i] + st[K, i - 1])
    ss, sg, gg = inverse(diag + st[C, i] + fy + before, st[C, i], mask)
    values = ((FX, fx), (FZ, fz), (H, h), (FY, fy), (ASS, ss), (ASG, sg), (AGG, gg))
    return [(st, (plane, i), v) for plane, v in values]


def row_sweep(st, i, source, target, edge):
    s, g = relaxed(st, i, source, *row_residual(st, i, source, edge))
    return [(st, (target, i), s), (st, (target + 1, i), g)]


def first_partial(res_s, res_g, s, s_d, g, g_d, fy, onward):
    return res_s + fy * (s_d - s), res_g + CONDUCT * g_d - FLOW * (g - g_d if onward else g)


def send_planes(st, onward, edge):
    ny = st.shape[1] - 2
    e, d, near = (ny, ny - 1, ny - 1) if onward else (1, 2, 1)
    fy, s, g, g_d = st[FY, near], st[SA, e], st[GA, e], st[GA, d]
    part_s, part_g = row_inner(st, e, SA, edge)
    m_1s, m_1g = first_partial(st[RS, e] + part_s, st[RG, e] + part_g, s, st[SA, d], g, g_d, fy, onward)
    m_2s = st[RS, e] + fy * st[SB, d]
    m_2g = st[RG, e] + (CONDUCT + FLOW if onward else CONDUCT) * st[GB, d]
    return [s, g, st[K, e], st[C, e], fy, m_1s, m_1g, m_2s, m_2g]


def across_parts(ext):
    parts, at = [], 0
    for k in range(EARLY, MESSAGE):
        parts.append((k, CROP, ext - CROP, at))
        at += ext - 2 * CROP
    for k in range(EARLY):
        more = 1 if k in (M_1S, M_1G) else 0
        for low, high in ((CROP, PAD + more), (ext - PAD - more, ext - CROP)):
            parts.append((k, low, high, at))
            at += high - low
    return parts, (at + 7) // 8 * 8


def write_across(ref, k, value):
    for plane, low, high, at in across_parts(value.shape[0])[0]:
        if plane == k:
            ref[at : at + high - low] = value[low:high]


def read_across(early, across, outer, k):
    ext = outer.shape[1]
    if k < EARLY:
        outer[k, PAD : ext - PAD] = early[k]
    for plane, low, high, at in across_parts(ext)[0]:
        if plane == k:
            outer[k, low:high] = across[at : at + high - low]


def write_beside(refs, k, value):
    refs[k // THIRD][k % THIRD] = value[CROP : value.shape[0] - CROP]


def read_beside(refs, outer, k):
    outer[k, CROP : outer.shape[1] - CROP] = refs[k // THIRD][k % THIRD]


def first_end(st, one, two, after, write):
    planes, rows, ext, nz = st.shape
    ny, nx = rows - 2, ext - 2 * PAD
    mask = x_mask((ext, nz), nx)
    edge = edge_weights((ext, nz))
    e, d, f = (ny, ny - 1, ny - 2) if after else (1, 2, 3)
    for i in (e, d, f):
        place_halo(st, one, two, i - 1, nx)
    fx, fz, h, diag = faces(st[K, e])
    st[FX, e], st[FZ, e], st[H, e] = fx, fz, h
    st[FY, min(e, d)] = 0.5 * (st[K, e] + st[K, d])
    st[FY, min(d, f)] = 0.5 * (st[K, d] + st[K, f])
    grouped([d], lambda i: row_coefficients(st, i, mask))
    grouped([d], lambda i: row_sweep(st, i, SA, SB, edge))
    for k, value in enumerate(send_planes(st, after, edge)):
        write(k, value)


def either_first(st, one, two, after, write):
    for is_after in (True, False):

        @pl.when(after == is_after)
        def _():
            first_end(st, one, two, is_after, write)


def first_kernel(st_in, one, two, st, across):
    del st_in
    either_first(st, one, two, lax.axis_index("gy") % 2 == 1, functools.partial(write_across, across))


def other_kernel(st_in, one, two, st, *beside):
    del st_in
    either_first(st, one, two, lax.axis_index("gy") % 2 == 0, functools.partial(write_beside, beside))
    planes, rows, ext, nz = st.shape
    ny, nx = rows - 2, ext - 2 * PAD
    mask = x_mask((ext, nz), nx)
    for y in range(3, ny - 3):
        place_halo(st, one, two, y, nx)
    grouped(list(range(3, ny - 1)), lambda i: row_coefficients(st, i, mask))


def outer_residual(st, i, s_at, rs, rg, fy_out, edge, after):
    part_s, part_g = row_inner(st, i, s_at, edge)
    s, g = st[s_at, i], st[s_at + 1, i]
    if after:
        part_s += st[FY, i - 1] * (st[s_at, i - 1] - s)
        part_g += (CONDUCT + FLOW) * st[s_at + 1, i - 1]
    else:
        part_s += st[FY, i] * (st[s_at, i + 1] - s)
        part_g += CONDUCT * st[s_at + 1, i + 1]
    return rs + part_s - fy_out * s, rg + part_g - FLOW * g


def pair_x(v):
    row = lax.broadcasted_iota(jnp.int32, v.shape, 0)
    return v + jnp.where(row % 2 == 0, up_x(v), down_x(v))


def coarse_coefficients(c_sum, k_sum):
    per_solid = 1.0 / (4.0 * SOLID_CAP + c_sum + LUMP * k_sum)
    ratio = c_sum * per_solid
    return per_solid, ratio, 1.0 / ((4.0 * GAS_CAP + 2.0 * FLOW) + c_sum - c_sum * ratio)


def coarse_row(st, coarse, j, mask, edge):
    i = 2 * j + 1
    res_s, res_g = row_residual(st, i, SA, edge)
    more_s, more_g = row_residual(st, i + 1, SA, edge)
    res_s, res_g = pair_x((res_s + more_s) * mask), pair_x((res_g + more_g) * mask)
    c_sum = pair_x(st[C, i] + st[C, i + 1])
    per_solid, ratio, per_gas = coarse_coefficients(c_sum, pair_x(st[K, i] + st[K, i + 1]))
    lead = res_s * per_solid
    values = (lead, ratio, (2.0 * FLOW) * per_gas, (res_g + c_sum * lead) * per_gas)
    return [(coarse, (k, j), v) for k, v in enumerate(values)]


def inner_kernel(st_in, early, st, coarse):
    del st_in, early
    planes, rows, ext, nz = st.shape
    ny, nx = rows - 2, ext - 2 * PAD
    shape = (ext, nz)
    mask = x_mask(shape, nx)
    edge = edge_weights(shape)
    looped(3, ny - 1, 4, lambda i: row_sweep(st, i, SA, SB, edge))
    looped(3, ny - 1, 4, lambda i: row_sweep(st, i, SB, SA, edge))
    grouped(list(range(2, ny // 2 - 2)), lambda j: coarse_row(st, coarse, j, mask, edge))


def end_work(st, coarse, extra, read, outer, is_after):
    planes, rows, ext, nz = st.shape
    ny, nx = rows - 2, ext - 2 * PAD
    me, count = lax.axis_index("gy"), lax.axis_size("gy")
    mask = x_mask((ext, nz), nx)
    inside = jnp.where(me == (count - 1 if is_after else 0), 0.0, mask)
    edge = edge_weights((ext, nz))
    zeros = jnp.zeros((PAD, nz), jnp.float32)
    for k in range(MESSAGE):
        outer[k, :PAD] = zeros
        outer[k, ext - PAD :] = zeros
        read(outer, k)

    o, e, near = (ny + 1, ny, ny) if is_after else (0, 1, 0)
    to_o = CONDUCT + FLOW if is_after else CONDUCT
    s_o, g_o, k_o, c_o, fy_out = (outer[plane] for plane in (M_S, M_G, M_K, M_C, M_FY))
    fy = 0.5 * (k_o + st[K, e])
    fx, fz, h, diag = faces(k_o)
    inv_o = inverse(diag + c_o + fy_out + fy, c_o, inside)
    fx_e, fz_e = st[FX, e], st[FZ, e]
    diag = st[H, e] + (fx_e + down_x(fx_e)) + (fz_e + down_z(fz_e)) + st[C, e] + fy
    inv_e = inverse(diag + st[FY, near - 1 if is_after else near + 1], st[C, e], mask)
    for plane, value in ((SA, s_o), (GA, g_o), (K, k_o), (C, c_o), (FX, fx), (FZ, fz), (H, h)):
        st[plane, o] = value
    st[FY, near] = fy
    for k in range(3):
        st[ASS + k, o], st[ASS + k, e] = inv_o[k], inv_e[k]

    res = outer[M_1S] + fy * (st[SA, e] - s_o), outer[M_1G] + to_o * st[GA, e]
    new_o = relaxed(st, o, SA, *res)
    stores = row_sweep(st, e, SA, SB, edge)
    st[SB, o], st[GB, o] = new_o
    for ref, at, value in stores:
        ref[at] = value
    res = outer_residual(st, o, SB, outer[M_2S], outer[M_2G], fy_out, edge, is_after)
    new_o = relaxed(st, o, SB, *res)
    ends = [e - 1, e] if is_after else [e, e + 1]
    grouped(ends, lambda i: row_sweep(st, i, SB, SA, edge))
    st[SA, o], st[GA, o] = new_o
    for k, plane in enumerate((M_2S, M_2G, M_FY)):
        extra[(3 if is_after else 0) + k] = outer[plane]
    blocks = ny // 2
    stores = []
    for j in (blocks - 2, blocks - 1) if is_after else (0, 1):
        stores += coarse_row(st, coarse, j, mask, edge)
    for ref, at, value in stores:
        ref[at] = value


def either_end(after, st, coarse, extra, read, outer):
    for is_after in (True, False):

        @pl.when(after == is_after)
        def _():
            end_work(st, coarse, extra, read, outer, is_after)


def near_kernel(st_in, coarse_in, *refs):
    beside, (st, coarse, extra, outer) = refs[:-4], refs[-4:]
    del st_in, coarse_in
    either_end(lax.axis_index("gy") % 2 == 0, st, coarse, extra, functools.partial(read_beside, beside), outer)


def second_kernel(st_in, coarse_in, extra_in, early, across, *refs):
    st, coarse, extra, total, last_info, first_info, message, outer, squeeze = refs
    del st_in, coarse_in, extra_in
    planes, rows, ext, nz = st.shape
    ny, nx = rows - 2, ext - 2 * PAD
    me = lax.axis_index("gy")
    either_end(me % 2 == 1, st, coarse, extra, functools.partial(read_across, early, across), outer)

    blocks = ny // 2
    for k in range(4):
        squeeze[k] = coarse[k, 0]
    slopes, offsets = coarse[2, 0], coarse[3, 0]
    for j in range(1, blocks):
        slope = coarse[2, j]
        slopes, offsets = slope * slopes, slope * offsets + coarse[3, j]
        coarse[2, j], coarse[3, j] = slopes, offsets
    squeeze[4], squeeze[5], squeeze[6], squeeze[7] = slopes, offsets, coarse[0, blocks - 1], coarse[1, blocks - 1]

    span = nx // 2 + 2
    lead, ratio, slope, offset, slopes, offsets, lead_last, ratio_last = (
        squeeze[k, pl.ds(PAD - 2, span, 2), :] for k in range(8)
    )
    part = slice(PAD - 1, PAD + nx + 1)

    def increments(d, face, gas):
        return [(st[FY, face] * (st[SA, d] - st[SB, d]))[part], (gas * (st[GA, d] - st[GB, d]))[part]]

    onward = [lead_last, ratio_last] + increments(ny - 1, ny - 1, CONDUCT + FLOW)
    back = [lead, offset] + increments(2, 1, CONDUCT) + [slope, ratio]
    write_rows(total, [slopes, offsets])
    write_rows(last_info, onward)
    write_rows(first_info, back)
    for go, info in ((True, onward), (False, back)):

        @pl.when((me % 2 == 0) == go)
        def _():
            write_rows(message, [slopes, offsets] + info)


def write_rows(ref, values):
    at = 0
    for value in values:
        ref[at : at + value.shape[0]] = value
        at += value.shape[0]


class Rows:
    def __init__(self, nx):
        self.span = nx // 2 + 2
        self.map = 2 * self.span
        self.info = self.map + 2 * (nx + 2)
        self.rest = self.map
        self.final = self.map + self.info
        self.full = self.final + self.rest
        self.low = self.map
        self.high = self.low + self.info
        self.near = self.high + self.info + self.rest


def source(at, k, radix):
    if radix & (radix - 1) == 0:
        return at ^ k
    return (at + radix - k) % radix


def matchings(count, radix, stride):
    if (count, radix, stride) == (8, 4, 2):
        swaps = ((1, 2), (3, 4), (5, 6), (0, 7)), ((0, 4), (1, 6), (2, 5), (3, 7)), ((0, 3), (1, 5), (2, 6), (4, 7))
        out = []
        for pairs in swaps:
            senders = [0] * count
            for a, b in pairs:
                senders[a], senders[b] = b, a
            out.append((senders, len(out) == 0))
        return out
    out = []
    for k in range(1, radix):
        senders = []
        for me in range(count):
            at, low = me // stride % radix, me % stride
            senders.append(me - low + (source(at, k, radix) - at) * stride + (stride - 1 - low))
        out.append((senders, any(abs(source(at, k, radix) - at) == 1 for at in range(radix))))
    return sorted(out, key=lambda item: not item[1])


def look_up(table):
    me, value = lax.axis_index("gy"), jnp.int32(table[0])
    for k in range(1, len(table)):
        value = jnp.where(me == k, table[k], value)
    return value


def stages(count):
    if count % 2:
        return [1, count]
    out, rest = [2], count // 2
    while rest > 1:
        radix = next((r for r in (8, 4, 2) if rest % r == 0), rest)
        out.append(radix)
        rest //= radix
    return out if len(out) > 1 else out + [1]


def exchange_stage(messages, swaps):
    return [
        lax.ppermute(message, "gy", [(sender, me) for me, sender in enumerate(senders)])
        for (senders, near), message in zip(swaps, messages)
    ]


class Group:
    def __init__(self, radix, stride, others, nx):
        self.radix, self.others, self.nx = radix, others, nx
        me = lax.axis_index("gy")
        self.swaps = [
            (look_up([sender // stride % radix for sender in senders]), near)
            for senders, near in matchings(lax.axis_size("gy"), radix, stride)
        ]
        self.at = lax.rem(lax.div(me, stride), radix)
        low = lax.rem(me, stride)
        self.lowest, self.highest = low == 0, low == stride - 1

    def map_of(self, place, own):
        rows = Rows(self.nx)
        out = own
        for (sender, near), ref in zip(self.swaps, self.others):
            here = sender == place
            got = [ref[i * rows.span : (i + 1) * rows.span] for i in range(2)]
            out = got if out is None else [jnp.where(here, new, old) for new, old in zip(got, out)]
        return out

    def ahead(self, slope, offset):
        a, b = jnp.ones_like(slope), jnp.zeros_like(slope)
        for place in range(self.radix - 1):
            new_a, new_b = self.map_of(place, None)
            below = place < self.at
            a, b = jnp.where(below, new_a * a, a), jnp.where(below, new_a * b + new_b, b)
        return slope * a, slope * b + offset

    def total(self, own):
        a, b = self.map_of(0, own)
        for place in range(1, self.radix):
            new_a, new_b = self.map_of(place, own)
            a, b = new_a * a, new_a * b + new_b
        return a, b

    def collect(self, near, final):
        rows = Rows(self.nx)
        for (place, adjacent), ref in zip(self.swaps, self.others):
            if not adjacent:
                continue

            @pl.when(self.lowest & (place == self.at - 1))
            def _():
                near[rows.low : rows.low + rows.info] = ref[rows.map : rows.final]

            @pl.when(self.highest & (place == self.at + 1))
            def _():
                near[rows.high : rows.high + rows.info] = ref[rows.map : rows.final]
                rest = slice(0, rows.map) if final else slice(rows.final, rows.full)
                near[rows.high + rows.info : rows.near] = ref[rest]


def start_near(near, nx, nz):
    rows = Rows(nx)
    near[: rows.span] = jnp.ones((rows.span, nz), jnp.float32)
    near[rows.span :] = jnp.zeros((near.shape[0] - rows.span, nz), jnp.float32)


def join_kernel(radix, stride, final, nx, is_first, *refs):
    rows = Rows(nx)
    total, last_info, first_info, near_in = refs[:4]
    others, near, outs = refs[4 : 3 + radix], refs[3 + radix], refs[4 + radix :]
    nz = near.shape[1]
    if is_first:
        start_near(near, nx, nz)
    else:
        near[...] = near_in[...]
    group = Group(radix, stride, others, nx)
    own = [total[i * rows.span : (i + 1) * rows.span] for i in range(2)]
    ahead = group.ahead(near[: rows.span], near[rows.span : rows.map])
    write_rows(near, ahead)
    group.collect(near, False)
    whole = group.total(own)
    if final == 0:
        write_rows(outs[0], whole)
        return
    me, count = lax.axis_index("gy"), lax.axis_size("gy")
    for (senders, adjacent), out in zip(matchings(count, final, stride * radix), outs):
        up = look_up(senders) > me
        if not adjacent:
            write_rows(out, whole)
            continue

        @pl.when(up)
        def _():
            write_rows(out, whole)
            out[rows.map : rows.final] = last_info[: rows.info]

        @pl.when(jnp.logical_not(up))
        def _():
            out[: rows.map] = first_info[rows.info : rows.info + rows.rest]
            out[rows.map : rows.final] = first_info[: rows.info]


def full_message(nx, total, last_info, first_info, senders):
    rows = Rows(nx)
    onward = jnp.concatenate([total[: rows.map], last_info[: rows.info], first_info[rows.info : rows.info + rows.rest]])
    back = jnp.concatenate([total[: rows.map], first_info[: rows.info + rows.rest]])
    message = jnp.where(look_up(senders) > lax.axis_index("gy"), onward, back)
    return jnp.pad(message, ((0, -rows.full % 8), (0, 0)))


def third_kernel(radix, stride, *refs):
    st, extra, coarse, near_in = refs[:4]
    others, (out, sc, wide, near, done, sems) = refs[4 : 3 + radix], refs[3 + radix :]
    planes, rows, ext, nz = st.shape
    ny, nx = rows - 2, ext - 2 * PAD
    edge = edge_weights((ext, nz))
    blocks = ny // 2

    lay = Rows(nx)
    span = lay.span
    near[...] = near_in[...]
    group = Group(radix, stride, others, nx)
    if radix > 1:
        group.collect(near, True)
    gas_in = group.ahead(near[:span], near[span : lay.map])[1]
    at_high = lay.high + lay.info
    starts = [lay.low, lay.low + span, lay.high, lay.high + span, at_high, at_high + span]
    for k, v in enumerate([gas_in] + [near[start : start + span] for start in starts]):
        wide[k, : PAD - 2] = jnp.zeros((PAD - 2, nz), jnp.float32)
        wide[k, ext - PAD + 2 :] = jnp.zeros((PAD - 2, nz), jnp.float32)
        wide[k, pl.ds(PAD - 2, span, 2), :] = v
        wide[k, pl.ds(PAD - 1, span, 2), :] = v
    for k, start in enumerate((lay.low, lay.low + nx + 2, lay.high, lay.high + nx + 2)):
        start += lay.map
        wide[7 + k, :PAD] = jnp.zeros((PAD, nz), jnp.float32)
        wide[7 + k, ext - PAD :] = jnp.zeros((PAD, nz), jnp.float32)
        wide[7 + k, PAD - 1 : PAD + nx + 1] = near[start : start + nx + 2]

    gas_in = wide[0]
    last = ny + 1
    solid_low = wide[1] + wide[2] * gas_in
    sc[0, 0] = st[SA, 0] + solid_low
    sc[1, 0] = st[GA, 0] + gas_in

    def correct(j, carry):
        gas = coarse[2, j] * gas_in + coarse[3, j]
        solid = coarse[0, j] + coarse[1, j] * gas
        for i in (2 * j + 1, 2 * j + 2):
            sc[0, i] = st[SA, i] + solid
            sc[1, i] = st[GA, i] + gas
        return carry

    lax.fori_loop(0, blocks, correct, 0)
    gas = coarse[2, blocks - 1] * gas_in + coarse[3, blocks - 1]
    gas_high = wide[5] * gas + wide[4]
    solid_high = wide[3] + wide[6] * gas_high
    sc[0, last] = st[SA, last] + solid_high
    sc[1, last] = st[GA, last] + gas_high

    view = Fields(st, sc)
    for i, is_after, solid, gas in ((0, False, solid_low, gas_in), (last, True, solid_high, gas_high)):
        side = 3 if is_after else 0
        fy = extra[side + 2]
        to = 9 if is_after else 7
        rs = extra[side] + wide[to] + fy * solid
        rg = extra[side + 1] + wide[to + 1] + (CONDUCT if is_after else CONDUCT + FLOW) * gas
        res = outer_residual(view, i, SA, rs, rg, fy, edge, is_after)
        sc[2, i], sc[3, i] = relaxed(view, i, SA, *res)

    def sweep(k, carry):
        stores = []
        for r in range(GROUP):
            i = GROUP * k + 1 + r
            new_s, new_g = relaxed(view, i, SA, *row_residual(view, i, SA, edge))
            stores += [((2, i), new_s), ((3, i), new_g)]
        for at, value in stores:
            sc[at] = value
        return carry

    lax.fori_loop(0, ny // GROUP, sweep, 0)

    def leaving(k):
        part = pl.ds(GROUP * k, GROUP)
        return pltpu.make_async_copy(done.at[:, part], out.at[:, part], sems.at[k])

    def final(k, carry):
        stores = []
        for r in range(GROUP):
            i = GROUP * k + 1 + r
            new_s, new_g = last_relaxed(view, i, SB, edge, slice(PAD, PAD + nx))
            stores += [((0, i - 1), new_s), ((1, i - 1), new_g)]
        for at, value in stores:
            done[at] = value
        leaving(k).start()
        return carry

    lax.fori_loop(0, ny // GROUP, final, 0)
    for k in range(ny // GROUP):
        leaving(k).wait()


class Fields:
    def __init__(self, st, sc):
        self.st, self.sc = st, sc

    def __getitem__(self, at):
        return (self.sc if at[0] <= GB else self.st)[at]


def cost(rows, cells):
    return pl.CostEstimate(flops=50 * rows * cells, bytes_accessed=16 * 4 * rows * cells, transcendentals=0)


def swap(x, axis, first):
    pairs = []
    for i in range(first, lax.axis_size(axis) - 1, 2):
        pairs += [(i, i + 1), (i + 1, i)]
    return lax.ppermute(x, axis, pairs)


def shards(temps, right_side, exchange, coupling):
    temps, right_side = (jnp.transpose(a, (0, 2, 1, 3)) for a in (temps, right_side))
    exchange, coupling = (jnp.transpose(a, (1, 0, 2)) for a in (exchange, coupling))
    temps, right_side, exchange, coupling = (
        pltpu.with_memory_space_constraint(a, pltpu.HBM) for a in (temps, right_side, exchange, coupling)
    )
    ny, nx, nz = exchange.shape
    ext = nx + 2 * PAD
    f32 = functools.partial(jax.ShapeDtypeStruct, dtype=jnp.float32)

    strip = f32((strip_height(ny), nz))
    state = f32((PLANES, ny + 2, ext, nz))
    one, two, st = pl.pallas_call(
        pack_kernel,
        out_shape=(strip, strip, state),
        in_specs=[HBM] * 4,
        out_specs=(VMEM,) * 3,
        scratch_shapes=[pltpu.SemaphoreType.DMA((12,))],
        compiler_params=PARAMS,
        name="pack_x",
    )(temps, right_side, exchange, coupling)
    one, two = swap(one, "gx", 0), swap(two, "gx", 1)

    def letter(planes):
        return f32((planes, ext - 2 * CROP, nz))

    st, early = pl.pallas_call(
        conduct_kernel,
        out_shape=(state, f32((EARLY, nx, nz))),
        in_specs=[VMEM],
        out_specs=(VMEM,) * 2,
        input_output_aliases={0: 0},
        compiler_params=PARAMS,
        cost_estimate=cost(2 * ny, ext * nz),
        name="conduct",
    )(st)
    early = swap(early, "gy", 1)
    st, across = pl.pallas_call(
        first_kernel,
        out_shape=(state, f32((across_parts(ext)[1], nz))),
        in_specs=[VMEM] * 3,
        out_specs=(VMEM,) * 2,
        input_output_aliases={0: 0},
        compiler_params=PARAMS,
        name="first",
    )(st, one, two)
    st, *beside = pl.pallas_call(
        other_kernel,
        out_shape=(state,) + (letter(THIRD),) * (MESSAGE // THIRD),
        in_specs=[VMEM] * 3,
        out_specs=(VMEM,) * (1 + MESSAGE // THIRD),
        input_output_aliases={0: 0},
        compiler_params=PARAMS,
        name="other",
    )(st, one, two)
    across = swap(across, "gy", 1)

    rows = f32((4, ny // 2, ext, nz))
    st, coarse = pl.pallas_call(
        inner_kernel,
        out_shape=(state, rows),
        in_specs=[VMEM] * 2,
        out_specs=(VMEM,) * 2,
        input_output_aliases={0: 0},
        compiler_params=PARAMS,
        cost_estimate=cost(4 * ny, ext * nz),
        name="inner",
    )(st, early)

    beside = [swap(part, "gy", 0) for part in beside]

    lay = Rows(nx)

    def tall(height):
        return f32(((height + 7) // 8 * 8, nz))

    letter_room = pltpu.VMEM((MESSAGE, ext, nz), jnp.float32)
    more = f32((6, ext, nz))
    st, coarse, extra = pl.pallas_call(
        near_kernel,
        out_shape=(state, rows, more),
        in_specs=[VMEM] * (2 + len(beside)),
        out_specs=(VMEM,) * 3,
        scratch_shapes=[letter_room],
        input_output_aliases={0: 0, 1: 1},
        compiler_params=PARAMS,
        name="near",
    )(st, coarse, *beside)
    st, coarse, extra, total, last_info, first_info, message = pl.pallas_call(
        second_kernel,
        out_shape=(state, rows, more, tall(lay.map), tall(lay.info), tall(lay.info + lay.rest), tall(lay.full)),
        in_specs=[VMEM] * 5,
        out_specs=(VMEM,) * 7,
        scratch_shapes=[letter_room, pltpu.VMEM((8, ext, nz), jnp.float32)],
        input_output_aliases={0: 0, 1: 1, 2: 2},
        compiler_params=PARAMS,
        name="second",
    )(st, coarse, extra, early, across)

    near, messages = total, [message]
    count = lax.axis_size("gy")
    radices, stride = stages(count), 1
    for place, radix in enumerate(radices[:-1]):
        swaps = matchings(count, radix, stride)
        if place:
            messages = [full_message(nx, total, last_info, first_info, senders) for senders, _ in swaps]
        others = exchange_stage(messages, swaps)
        final = radices[-1] if place == len(radices) - 2 else 0
        following = matchings(count, final, stride * radix) if final else []
        outs = [tall(lay.final if adjacent else lay.map) for _, adjacent in following] if final else [tall(lay.map)]
        near, *messages = pl.pallas_call(
            functools.partial(join_kernel, radix, stride, final, nx, place == 0),
            out_shape=(tall(lay.near), *outs),
            in_specs=[VMEM] * (3 + radix),
            out_specs=(VMEM,) * (1 + len(outs)),
            compiler_params=PARAMS,
            name="join",
        )(total, last_info, first_info, near, *others)
        total = total if final else messages[0]
        stride *= radix
    got = exchange_stage(messages, matchings(count, radices[-1], stride))

    out = pl.pallas_call(
        functools.partial(third_kernel, radices[-1], stride),
        out_shape=f32((2, ny, nx, nz)),
        in_specs=[VMEM] * (4 + len(got)),
        out_specs=HBM,
        scratch_shapes=[
            pltpu.VMEM((4, ny + 2, ext, nz), jnp.float32),
            pltpu.VMEM((11, ext, nz), jnp.float32),
            pltpu.VMEM(tall(lay.near).shape, jnp.float32),
            pltpu.VMEM((2, ny, nx, nz), jnp.float32),
            pltpu.SemaphoreType.DMA((ny // GROUP,)),
        ],
        compiler_params=PARAMS,
        name="third",
    )(st, extra, coarse, near, *got)
    return jnp.transpose(out, (0, 2, 1, 3))


def solution(mesh):
    return jax.shard_map(
        shards,
        mesh=mesh,
        in_specs=(
            P(None, "gx", "gy", None),
            P(None, "gx", "gy", None),
            P("gx", "gy", None),
            P("gx", "gy", None),
        ),
        out_specs=P(None, "gx", "gy", None),
        check_vma=False,
    )
```

```python
import functools

import jax
import jax.numpy as jnp
from jax import lax
from jax.experimental import pallas as pl
from jax.experimental.pallas import tpu as pltpu
from jax.sharding import PartitionSpec as P

SOLID_CAP, GAS_CAP, FLOW, CONDUCT, RELAX, LUMP = 0.5, 0.02, 40.0, 0.05, 0.8, 0.25
GAS_SELF = GAS_CAP + 4.5 * CONDUCT

PAD = 8
WX = 5
CROP = 4
(SA, GA, SB, GB, K, C, RS, RG, FX, FZ, H, FY, ASS, ASG, AGG) = range(15)
PLANES = 15
(M_S, M_G, M_K, M_C, M_FY, M_1S, M_1G, M_2S, M_2G) = range(9)
MESSAGE, EARLY, THIRD = 9, 7, 3

GROUP = 6

VMEM = pl.BlockSpec(memory_space=pltpu.VMEM)
HBM = pl.BlockSpec(memory_space=pltpu.HBM)
PARAMS = pltpu.CompilerParams(vmem_limit_bytes=40 * 1024 * 1024)


def up_x(v):
    return pltpu.roll(v, v.shape[0] - 1, 0)


def down_x(v):
    return pltpu.roll(v, 1, 0)


def up_z(v):
    return pltpu.roll(v, v.shape[1] - 1, 1)


def down_z(v):
    return pltpu.roll(v, 1, 1)


def lanes(shape):
    return lax.broadcasted_iota(jnp.int32, shape, 1)


def x_mask(shape, nx):
    row = lax.broadcasted_iota(jnp.int32, shape, 0)
    place, count = lax.axis_index("gx"), lax.axis_size("gx")
    low = jnp.where(place == 0, PAD, PAD - WX)
    high = jnp.where(place == count - 1, PAD + nx, PAD + nx + WX)
    return jnp.where((row >= low) & (row < high), 1.0, 0.0).astype(jnp.float32)


PAIRS = ((SA, GA), (C, RS), (RG, K))
STRIP_ROWS = 8 * len(PAIRS)


def strip_height(ny):
    return ny * STRIP_ROWS + (ny + 7) // 8 * 8


def sublanes(nz):
    return lax.broadcasted_iota(jnp.int32, (8, nz), 0)


def conductivity_of(s, exchange):
    return 1.0 + 4.0 * exchange * s * s * s


def strip_side(s, g, k, rs, rg, c, low):
    row = sublanes(s.shape[1])
    inn, shift = (3, 7) if low else (4, 1)
    k_out, s_out, g_out = (pltpu.roll(v, shift, 0) for v in (k, s, g))
    rs = rs + jnp.where(row == inn, 0.5 * (k + k_out) * s_out, 0.0)
    rg = rg + jnp.where(row == inn, CONDUCT * g_out, 0.0)
    values = {SA: s, GA: g, K: k, RS: rs, RG: rg, C: c}
    tiles = []
    for a, b in PAIRS:
        a, b = values[a], values[b]
        a, b = (a, pltpu.roll(b, 4, 0)) if low else (pltpu.roll(a, 4, 0), b)
        tiles.append(jnp.where(row < 4, a, b))
    return tiles, (k[4:5] if low else k[3:4])


def pack_kernel(temps, right, exchange, coupling, one, two, st, sems):
    even = lax.axis_index("gx") % 2 == 0
    ny, nx, nz = exchange.shape
    halves = [(0, ny // 2), (ny // 2, ny - ny // 2)]
    copies = [[], []]
    for k, (plane, ref) in enumerate(
        ((SA, temps.at[0]), (K, exchange), (GA, temps.at[1]), (C, coupling), (RS, right.at[0]), (RG, right.at[1]))
    ):
        for h, (start, count) in enumerate(halves):
            to = st.at[plane, pl.ds(1 + start, count), pl.ds(PAD, nx)]
            copies[h].append(pltpu.make_async_copy(ref.at[pl.ds(start, count)], to, sems.at[6 * h + k]))
    for copy in copies[0] + copies[1]:
        copy.start()
    for i in range(1, ny + 1):
        for h, (start, count) in enumerate(halves):
            if i == start + 1:
                for copy in copies[h]:
                    copy.wait()
        sides = []
        for start in (PAD, PAD + nx - 8):
            s, g, e, rs, rg, c = (st[plane, i, start : start + 8] for plane in (SA, GA, K, RS, RG, C))
            sides.append(strip_side(s, g, conductivity_of(s, e), rs, rg, c, start == PAD))
        (low, low_k), (high, high_k) = sides
        for p in range(len(PAIRS)):
            part = slice((i - 1) * STRIP_ROWS + 8 * p, (i - 1) * STRIP_ROWS + 8 * p + 8)
            one[part] = jnp.where(even, high[p], low[p])
            two[part] = jnp.where(even, low[p], high[p])
        part = slice(ny * STRIP_ROWS + i - 1, ny * STRIP_ROWS + i)
        one[part] = jnp.where(even, high_k, low_k)
        two[part] = jnp.where(even, low_k, high_k)


def conduct_kernel(st_in, st, early):
    del st_in
    planes, rows, ext, nz = st.shape
    ny, nx = rows - 2, ext - 2 * PAD
    odd = lax.axis_index("gy") % 2 == 1
    own = slice(PAD, PAD + nx)
    for i in range(1, ny + 1):
        st[K, i, own] = conductivity_of(st[SA, i, own], st[K, i, own])
    for is_odd, e, d in ((True, ny, ny - 1), (False, 1, 2)):

        @pl.when(odd == is_odd)
        def _():
            s, s_d, g, g_d = st[SA, e, own], st[SA, d, own], st[GA, e, own], st[GA, d, own]
            c, k, k_d = st[C, e, own], st[K, e, own], st[K, d, own]
            fx, fz, h, _ = faces(k)
            fy = 0.5 * (k + k_d)
            part_s, part_g = inner(s, g, c, h, fx, fz, edge_weights((nx, nz)))
            m_1s, m_1g = first_partial(st[RS, e, own] + part_s, st[RG, e, own] + part_g, s, s_d, g, g_d, fy, is_odd)
            for plane, value in enumerate((s, g, k, c, fy, m_1s, m_1g)):
                early[plane] = value


def place_halo(st, one, two, y, nx):
    even = lax.axis_index("gx") % 2 == 0
    ny, row = st.shape[1] - 2, sublanes(st.shape[3])
    i = y + 1

    def received(part):
        a, b = one[part], two[part]
        return jnp.where(even, b, a), jnp.where(even, a, b)

    for p, (plane_a, plane_b) in enumerate(PAIRS):
        before, after = received(slice(y * STRIP_ROWS + 8 * p, y * STRIP_ROWS + 8 * p + 8))
        before = {plane_a: pltpu.roll(before, 4, 0), plane_b: before}
        after = {plane_a: after, plane_b: pltpu.roll(after, 4, 0)}
        for plane in (plane_a, plane_b):
            low, high = jnp.where(row >= 4, before[plane], 0.0), jnp.where(row < 4, after[plane], 0.0)
            if plane == K:
                k_low, k_high = received(slice(ny * STRIP_ROWS + y, ny * STRIP_ROWS + y + 1))
                low, high = jnp.where(row == 3, k_low, low), jnp.where(row == 4, k_high, high)
            st[plane, i, :PAD] = low
            st[plane, i, PAD + nx :] = high


def inner(s, g, c, h, fx, fz, edge):
    t = c * (s - g)
    flux_x = fx * (up_x(s) - s)
    flux_z = fz * (up_z(s) - s)
    part_s = (flux_x - down_x(flux_x)) + (flux_z - down_z(flux_z)) - h * s - t
    part_g = (
        t
        - GAS_SELF * g
        + CONDUCT * (up_x(g) + down_x(g))
        + edge[0] * up_z(g)
        + edge[1] * down_z(g)
    )
    return part_s, part_g


def edge_weights(shape):
    lane = lanes(shape)
    weight = jnp.float32(0.25 * CONDUCT)
    return jnp.where(lane == shape[1] - 1, 0.0, weight), jnp.where(lane == 0, 0.0, weight)


def row_inner(st, i, s_at, edge):
    return inner(st[s_at, i], st[s_at + 1, i], st[C, i], st[H, i], st[FX, i], st[FZ, i], edge)


def row_residual(st, i, s_at, edge):
    part_s, part_g = row_inner(st, i, s_at, edge)
    s, g, before = st[s_at, i], st[s_at + 1, i], st[s_at + 1, i - 1]
    part_s += st[FY, i] * (st[s_at, i + 1] - s) + st[FY, i - 1] * (st[s_at, i - 1] - s)
    part_g += CONDUCT * (st[s_at + 1, i + 1] + before) - FLOW * (g - before)
    return st[RS, i] + part_s, st[RG, i] + part_g


def relaxed(st, i, s_at, res_s, res_g):
    s = st[s_at, i] + st[ASS, i] * res_s + st[ASG, i] * res_g
    g = st[s_at + 1, i] + st[ASG, i] * res_s + st[AGG, i] * res_g
    return s, g


def faces(k):
    lane = lanes(k.shape)
    end = k.shape[1] - 1
    fx = 0.5 * (k + up_x(k))
    fz = jnp.where(lane == end, 0.0, 0.125 * (k + up_z(k)))
    h = SOLID_CAP + jnp.where((lane == 0) | (lane == end), 0.125 * k, 0.0)
    return fx, fz, h, h + (fx + down_x(fx)) + (fz + down_z(fz))


def inverse(diag, c, mask):
    gas_diag = (GAS_SELF + FLOW) + c
    inv = (RELAX * mask) / (diag * gas_diag - c * c)
    return inv * gas_diag, inv * c, inv * diag


def last_relaxed(st, i, s_at, edge, own):
    full_s, full_g = st[s_at, i], st[s_at + 1, i]
    s, g = full_s[own], full_g[own]
    flux_x = st[FX, i] * (up_x(full_s) - full_s)
    flux_z = st[FZ, i, own] * (up_z(s) - s)
    c, before = st[C, i, own], st[s_at + 1, i - 1, own]
    t = c * (s - g)
    res_s = st[RS, i, own] + (flux_x[own] - down_x(flux_x)[own]) + (flux_z - down_z(flux_z)) - st[H, i, own] * s - t
    res_s += st[FY, i, own] * (st[s_at, i + 1, own] - s) + st[FY, i - 1, own] * (st[s_at, i - 1, own] - s)
    res_g = st[RG, i, own] + t - GAS_SELF * g + edge[0][own] * up_z(g) + edge[1][own] * down_z(g)
    res_g += CONDUCT * (up_x(full_g)[own] + down_x(full_g)[own] + st[s_at + 1, i + 1, own] + before) - FLOW * (g - before)
    ss, sg, gg = st[ASS, i, own], st[ASG, i, own], st[AGG, i, own]
    return s + ss * res_s + sg * res_g, g + sg * res_s + gg * res_g


def grouped(rows, work):
    for start in range(0, len(rows), GROUP):
        stores = []
        for i in rows[start : start + GROUP]:
            stores += work(i)
        for ref, at, value in stores:
            ref[at] = value


def looped(first, last, size, work):
    def group(k, carry):
        grouped([first + size * k + r for r in range(size)], work)
        return carry

    lax.fori_loop(0, (last - first) // size, group, 0)
    grouped(list(range(last - (last - first) % size, last)), work)


def row_coefficients(st, i, mask):
    fx, fz, h, diag = faces(st[K, i])
    fy = 0.5 * (st[K, i] + st[K, i + 1])
    before = 0.5 * (st[K, i] + st[K, i - 1])
    ss, sg, gg = inverse(diag + st[C, i] + fy + before, st[C, i], mask)
    values = ((FX, fx), (FZ, fz), (H, h), (FY, fy), (ASS, ss), (ASG, sg), (AGG, gg))
    return [(st, (plane, i), v) for plane, v in values]


def row_sweep(st, i, source, target, edge):
    s, g = relaxed(st, i, source, *row_residual(st, i, source, edge))
    return [(st, (target, i), s), (st, (target + 1, i), g)]


def first_partial(res_s, res_g, s, s_d, g, g_d, fy, onward):
    return res_s + fy * (s_d - s), res_g + CONDUCT * g_d - FLOW * (g - g_d if onward else g)


def send_planes(st, onward, edge):
    ny = st.shape[1] - 2
    e, d, near = (ny, ny - 1, ny - 1) if onward else (1, 2, 1)
    fy, s, g, g_d = st[FY, near], st[SA, e], st[GA, e], st[GA, d]
    part_s, part_g = row_inner(st, e, SA, edge)
    m_1s, m_1g = first_partial(st[RS, e] + part_s, st[RG, e] + part_g, s, st[SA, d], g, g_d, fy, onward)
    m_2s = st[RS, e] + fy * st[SB, d]
    m_2g = st[RG, e] + (CONDUCT + FLOW if onward else CONDUCT) * st[GB, d]
    return [s, g, st[K, e], st[C, e], fy, m_1s, m_1g, m_2s, m_2g]


def across_parts(ext):
    parts, at = [], 0
    for k in range(EARLY, MESSAGE):
        parts.append((k, CROP, ext - CROP, at))
        at += ext - 2 * CROP
    for k in range(EARLY):
        more = 1 if k in (M_1S, M_1G) else 0
        for low, high in ((CROP, PAD + more), (ext - PAD - more, ext - CROP)):
            parts.append((k, low, high, at))
            at += high - low
    return parts, (at + 7) // 8 * 8


def write_across(ref, k, value):
    for plane, low, high, at in across_parts(value.shape[0])[0]:
        if plane == k:
            ref[at : at + high - low] = value[low:high]


def read_across(early, across, outer, k):
    ext = outer.shape[1]
    if k < EARLY:
        outer[k, PAD : ext - PAD] = early[k]
    for plane, low, high, at in across_parts(ext)[0]:
        if plane == k:
            outer[k, low:high] = across[at : at + high - low]


def write_beside(refs, k, value):
    refs[k // THIRD][k % THIRD] = value[CROP : value.shape[0] - CROP]


def read_beside(refs, outer, k):
    outer[k, CROP : outer.shape[1] - CROP] = refs[k // THIRD][k % THIRD]


def first_end(st, one, two, after, write):
    planes, rows, ext, nz = st.shape
    ny, nx = rows - 2, ext - 2 * PAD
    mask = x_mask((ext, nz), nx)
    edge = edge_weights((ext, nz))
    e, d, f = (ny, ny - 1, ny - 2) if after else (1, 2, 3)
    for i in (e, d, f):
        place_halo(st, one, two, i - 1, nx)
    fx, fz, h, diag = faces(st[K, e])
    st[FX, e], st[FZ, e], st[H, e] = fx, fz, h
    st[FY, min(e, d)] = 0.5 * (st[K, e] + st[K, d])
    st[FY, min(d, f)] = 0.5 * (st[K, d] + st[K, f])
    grouped([d], lambda i: row_coefficients(st, i, mask))
    grouped([d], lambda i: row_sweep(st, i, SA, SB, edge))
    for k, value in enumerate(send_planes(st, after, edge)):
        write(k, value)


def either_first(st, one, two, after, write):
    for is_after in (True, False):

        @pl.when(after == is_after)
        def _():
            first_end(st, one, two, is_after, write)


def first_kernel(st_in, one, two, st, across):
    del st_in
    either_first(st, one, two, lax.axis_index("gy") % 2 == 1, functools.partial(write_across, across))


def other_kernel(st_in, one, two, st, *beside):
    del st_in
    either_first(st, one, two, lax.axis_index("gy") % 2 == 0, functools.partial(write_beside, beside))
    planes, rows, ext, nz = st.shape
    ny, nx = rows - 2, ext - 2 * PAD
    mask = x_mask((ext, nz), nx)
    for y in range(3, ny - 3):
        place_halo(st, one, two, y, nx)
    grouped(list(range(3, ny - 1)), lambda i: row_coefficients(st, i, mask))


def outer_residual(st, i, s_at, rs, rg, fy_out, edge, after):
    part_s, part_g = row_inner(st, i, s_at, edge)
    s, g = st[s_at, i], st[s_at + 1, i]
    if after:
        part_s += st[FY, i - 1] * (st[s_at, i - 1] - s)
        part_g += (CONDUCT + FLOW) * st[s_at + 1, i - 1]
    else:
        part_s += st[FY, i] * (st[s_at, i + 1] - s)
        part_g += CONDUCT * st[s_at + 1, i + 1]
    return rs + part_s - fy_out * s, rg + part_g - FLOW * g


def pair_x(v):
    row = lax.broadcasted_iota(jnp.int32, v.shape, 0)
    return v + jnp.where(row % 2 == 0, up_x(v), down_x(v))


def coarse_coefficients(c_sum, k_sum):
    per_solid = 1.0 / (4.0 * SOLID_CAP + c_sum + LUMP * k_sum)
    ratio = c_sum * per_solid
    return per_solid, ratio, 1.0 / ((4.0 * GAS_CAP + 2.0 * FLOW) + c_sum - c_sum * ratio)


def coarse_row(st, coarse, j, mask, edge):
    i = 2 * j + 1
    res_s, res_g = row_residual(st, i, SA, edge)
    more_s, more_g = row_residual(st, i + 1, SA, edge)
    res_s, res_g = pair_x((res_s + more_s) * mask), pair_x((res_g + more_g) * mask)
    c_sum = pair_x(st[C, i] + st[C, i + 1])
    per_solid, ratio, per_gas = coarse_coefficients(c_sum, pair_x(st[K, i] + st[K, i + 1]))
    lead = res_s * per_solid
    values = (lead, ratio, (2.0 * FLOW) * per_gas, (res_g + c_sum * lead) * per_gas)
    return [(coarse, (k, j), v) for k, v in enumerate(values)]


def inner_kernel(st_in, early, st, coarse):
    del st_in, early
    planes, rows, ext, nz = st.shape
    ny, nx = rows - 2, ext - 2 * PAD
    shape = (ext, nz)
    mask = x_mask(shape, nx)
    edge = edge_weights(shape)
    looped(3, ny - 1, 4, lambda i: row_sweep(st, i, SA, SB, edge))
    looped(3, ny - 1, 4, lambda i: row_sweep(st, i, SB, SA, edge))
    grouped(list(range(2, ny // 2 - 2)), lambda j: coarse_row(st, coarse, j, mask, edge))


def end_work(st, coarse, extra, read, outer, is_after):
    planes, rows, ext, nz = st.shape
    ny, nx = rows - 2, ext - 2 * PAD
    me, count = lax.axis_index("gy"), lax.axis_size("gy")
    mask = x_mask((ext, nz), nx)
    inside = jnp.where(me == (count - 1 if is_after else 0), 0.0, mask)
    edge = edge_weights((ext, nz))
    zeros = jnp.zeros((PAD, nz), jnp.float32)
    for k in range(MESSAGE):
        outer[k, :PAD] = zeros
        outer[k, ext - PAD :] = zeros
        read(outer, k)

    o, e, near = (ny + 1, ny, ny) if is_after else (0, 1, 0)
    to_o = CONDUCT + FLOW if is_after else CONDUCT
    s_o, g_o, k_o, c_o, fy_out = (outer[plane] for plane in (M_S, M_G, M_K, M_C, M_FY))
    fy = 0.5 * (k_o + st[K, e])
    fx, fz, h, diag = faces(k_o)
    inv_o = inverse(diag + c_o + fy_out + fy, c_o, inside)
    fx_e, fz_e = st[FX, e], st[FZ, e]
    diag = st[H, e] + (fx_e + down_x(fx_e)) + (fz_e + down_z(fz_e)) + st[C, e] + fy
    inv_e = inverse(diag + st[FY, near - 1 if is_after else near + 1], st[C, e], mask)
    for plane, value in ((SA, s_o), (GA, g_o), (K, k_o), (C, c_o), (FX, fx), (FZ, fz), (H, h)):
        st[plane, o] = value
    st[FY, near] = fy
    for k in range(3):
        st[ASS + k, o], st[ASS + k, e] = inv_o[k], inv_e[k]

    res = outer[M_1S] + fy * (st[SA, e] - s_o), outer[M_1G] + to_o * st[GA, e]
    new_o = relaxed(st, o, SA, *res)
    stores = row_sweep(st, e, SA, SB, edge)
    st[SB, o], st[GB, o] = new_o
    for ref, at, value in stores:
        ref[at] = value
    res = outer_residual(st, o, SB, outer[M_2S], outer[M_2G], fy_out, edge, is_after)
    new_o = relaxed(st, o, SB, *res)
    ends = [e - 1, e] if is_after else [e, e + 1]
    grouped(ends, lambda i: row_sweep(st, i, SB, SA, edge))
    st[SA, o], st[GA, o] = new_o
    for k, plane in enumerate((M_2S, M_2G, M_FY)):
        extra[(3 if is_after else 0) + k] = outer[plane]
    blocks = ny // 2
    stores = []
    for j in (blocks - 2, blocks - 1) if is_after else (0, 1):
        stores += coarse_row(st, coarse, j, mask, edge)
    for ref, at, value in stores:
        ref[at] = value


def either_end(after, st, coarse, extra, read, outer):
    for is_after in (True, False):

        @pl.when(after == is_after)
        def _():
            end_work(st, coarse, extra, read, outer, is_after)


def near_kernel(st_in, coarse_in, *refs):
    beside, (st, coarse, extra, outer) = refs[:-4], refs[-4:]
    del st_in, coarse_in
    either_end(lax.axis_index("gy") % 2 == 0, st, coarse, extra, functools.partial(read_beside, beside), outer)


def second_kernel(st_in, coarse_in, extra_in, early, across, *refs):
    st, coarse, extra, total, last_info, first_info, message, outer, squeeze = refs
    del st_in, coarse_in, extra_in
    planes, rows, ext, nz = st.shape
    ny, nx = rows - 2, ext - 2 * PAD
    me = lax.axis_index("gy")
    either_end(me % 2 == 1, st, coarse, extra, functools.partial(read_across, early, across), outer)

    blocks = ny // 2
    for k in range(4):
        squeeze[k] = coarse[k, 0]
    slopes, offsets = coarse[2, 0], coarse[3, 0]
    for j in range(1, blocks):
        slope = coarse[2, j]
        slopes, offsets = slope * slopes, slope * offsets + coarse[3, j]
        coarse[2, j], coarse[3, j] = slopes, offsets
    squeeze[4], squeeze[5], squeeze[6], squeeze[7] = slopes, offsets, coarse[0, blocks - 1], coarse[1, blocks - 1]

    span = nx // 2 + 2
    lead, ratio, slope, offset, slopes, offsets, lead_last, ratio_last = (
        squeeze[k, pl.ds(PAD - 2, span, 2), :] for k in range(8)
    )
    part = slice(PAD, PAD + nx)

    def increments(d, face, gas):
        return [(st[FY, face] * (st[SA, d] - st[SB, d]))[part], (gas * (st[GA, d] - st[GB, d]))[part]]

    onward = [lead_last, ratio_last] + increments(ny - 1, ny - 1, CONDUCT + FLOW)
    back = [lead, offset] + increments(2, 1, CONDUCT) + [slope, ratio]
    write_rows(total, [slopes, offsets])
    write_rows(last_info, onward)
    write_rows(first_info, back)
    for go, info in ((True, onward), (False, back)):

        @pl.when((me % 2 == 0) == go)
        def _():
            write_rows(message, [slopes, offsets] + info)


def write_rows(ref, values):
    at = 0
    for value in values:
        ref[at : at + value.shape[0]] = value
        at += value.shape[0]


class Rows:
    def __init__(self, nx):
        self.span = nx // 2 + 2
        self.map = 2 * self.span
        self.info = self.map + 2 * nx
        self.rest = self.map
        self.final = self.map + self.info
        self.full = self.final + self.rest
        self.low = self.map
        self.high = self.low + self.info
        self.near = self.high + self.info + self.rest


def source(at, k, radix):
    if radix & (radix - 1) == 0:
        return at ^ k
    return (at + radix - k) % radix


def matchings(count, radix, stride):
    if (count, radix, stride) == (8, 4, 2):
        swaps = ((1, 2), (3, 4), (5, 6), (0, 7)), ((0, 4), (1, 6), (2, 5), (3, 7)), ((0, 3), (1, 5), (2, 6), (4, 7))
        out = []
        for pairs in swaps:
            senders = [0] * count
            for a, b in pairs:
                senders[a], senders[b] = b, a
            out.append((senders, len(out) == 0))
        return out
    out = []
    for k in range(1, radix):
        senders = []
        for me in range(count):
            at, low = me // stride % radix, me % stride
            senders.append(me - low + (source(at, k, radix) - at) * stride + (stride - 1 - low))
        out.append((senders, any(abs(source(at, k, radix) - at) == 1 for at in range(radix))))
    return sorted(out, key=lambda item: not item[1])


def look_up(table):
    me, value = lax.axis_index("gy"), jnp.int32(table[0])
    for k in range(1, len(table)):
        value = jnp.where(me == k, table[k], value)
    return value


def stages(count):
    if count % 2:
        return [1, count]
    out, rest = [2], count // 2
    while rest > 1:
        radix = next((r for r in (8, 4, 2) if rest % r == 0), rest)
        out.append(radix)
        rest //= radix
    return out if len(out) > 1 else out + [1]


def exchange_stage(messages, swaps):
    return [
        lax.ppermute(message, "gy", [(sender, me) for me, sender in enumerate(senders)])
        for (senders, near), message in zip(swaps, messages)
    ]


class Group:
    def __init__(self, radix, stride, others, nx):
        self.radix, self.others, self.nx = radix, others, nx
        me = lax.axis_index("gy")
        self.swaps = [
            (look_up([sender // stride % radix for sender in senders]), near)
            for senders, near in matchings(lax.axis_size("gy"), radix, stride)
        ]
        self.at = lax.rem(lax.div(me, stride), radix)
        low = lax.rem(me, stride)
        self.lowest, self.highest = low == 0, low == stride - 1

    def map_of(self, place, own):
        rows = Rows(self.nx)
        out = own
        for (sender, near), ref in zip(self.swaps, self.others):
            here = sender == place
            got = [ref[i * rows.span : (i + 1) * rows.span] for i in range(2)]
            out = got if out is None else [jnp.where(here, new, old) for new, old in zip(got, out)]
        return out

    def ahead(self, slope, offset):
        a, b = jnp.ones_like(slope), jnp.zeros_like(slope)
        for place in range(self.radix - 1):
            new_a, new_b = self.map_of(place, None)
            below = place < self.at
            a, b = jnp.where(below, new_a * a, a), jnp.where(below, new_a * b + new_b, b)
        return slope * a, slope * b + offset

    def total(self, own):
        a, b = self.map_of(0, own)
        for place in range(1, self.radix):
            new_a, new_b = self.map_of(place, own)
            a, b = new_a * a, new_a * b + new_b
        return a, b

    def collect(self, near, final):
        rows = Rows(self.nx)
        for (place, adjacent), ref in zip(self.swaps, self.others):
            if not adjacent:
                continue

            @pl.when(self.lowest & (place == self.at - 1))
            def _():
                near[rows.low : rows.low + rows.info] = ref[rows.map : rows.final]

            @pl.when(self.highest & (place == self.at + 1))
            def _():
                near[rows.high : rows.high + rows.info] = ref[rows.map : rows.final]
                rest = slice(0, rows.map) if final else slice(rows.final, rows.full)
                near[rows.high + rows.info : rows.near] = ref[rest]


def start_near(near, nx, nz):
    rows = Rows(nx)
    near[: rows.span] = jnp.ones((rows.span, nz), jnp.float32)
    near[rows.span :] = jnp.zeros((near.shape[0] - rows.span, nz), jnp.float32)


def join_kernel(radix, stride, final, nx, is_first, *refs):
    rows = Rows(nx)
    total, last_info, first_info, near_in = refs[:4]
    others, near, outs = refs[4 : 3 + radix], refs[3 + radix], refs[4 + radix :]
    nz = near.shape[1]
    if is_first:
        start_near(near, nx, nz)
    else:
        near[...] = near_in[...]
    group = Group(radix, stride, others, nx)
    own = [total[i * rows.span : (i + 1) * rows.span] for i in range(2)]
    ahead = group.ahead(near[: rows.span], near[rows.span : rows.map])
    write_rows(near, ahead)
    group.collect(near, False)
    whole = group.total(own)
    if final == 0:
        write_rows(outs[0], whole)
        return
    me, count = lax.axis_index("gy"), lax.axis_size("gy")
    for (senders, adjacent), out in zip(matchings(count, final, stride * radix), outs):
        up = look_up(senders) > me
        if not adjacent:
            write_rows(out, whole)
            continue

        @pl.when(up)
        def _():
            write_rows(out, whole)
            out[rows.map : rows.final] = last_info[: rows.info]

        @pl.when(jnp.logical_not(up))
        def _():
            out[: rows.map] = first_info[rows.info : rows.info + rows.rest]
            out[rows.map : rows.final] = first_info[: rows.info]


def full_message(nx, total, last_info, first_info, senders):
    rows = Rows(nx)
    onward = jnp.concatenate([total[: rows.map], last_info[: rows.info], first_info[rows.info : rows.info + rows.rest]])
    back = jnp.concatenate([total[: rows.map], first_info[: rows.info + rows.rest]])
    message = jnp.where(look_up(senders) > lax.axis_index("gy"), onward, back)
    return jnp.pad(message, ((0, -rows.full % 8), (0, 0)))


def third_kernel(radix, stride, *refs):
    st, extra, coarse, near_in = refs[:4]
    others, (out, sc, wide, near, done, sems) = refs[4 : 3 + radix], refs[3 + radix :]
    planes, rows, ext, nz = st.shape
    ny, nx = rows - 2, ext - 2 * PAD
    edge = edge_weights((ext, nz))
    blocks = ny // 2

    lay = Rows(nx)
    span = lay.span
    near[...] = near_in[...]
    group = Group(radix, stride, others, nx)
    if radix > 1:
        group.collect(near, True)
    gas_in = group.ahead(near[:span], near[span : lay.map])[1]
    at_high = lay.high + lay.info
    starts = [lay.low, lay.low + span, lay.high, lay.high + span, at_high, at_high + span]
    for k, v in enumerate([gas_in] + [near[start : start + span] for start in starts]):
        wide[k, : PAD - 2] = jnp.zeros((PAD - 2, nz), jnp.float32)
        wide[k, ext - PAD + 2 :] = jnp.zeros((PAD - 2, nz), jnp.float32)
        wide[k, pl.ds(PAD - 2, span, 2), :] = v
        wide[k, pl.ds(PAD - 1, span, 2), :] = v
    for k, start in enumerate((lay.low, lay.low + nx, lay.high, lay.high + nx)):
        start += lay.map
        wide[7 + k, :PAD] = jnp.zeros((PAD, nz), jnp.float32)
        wide[7 + k, ext - PAD :] = jnp.zeros((PAD, nz), jnp.float32)
        wide[7 + k, PAD : PAD + nx] = near[start : start + nx]

    gas_in = wide[0]
    last = ny + 1
    solid_low = wide[1] + wide[2] * gas_in
    sc[0, 0] = st[SA, 0] + solid_low
    sc[1, 0] = st[GA, 0] + gas_in

    def correct(j, carry):
        gas = coarse[2, j] * gas_in + coarse[3, j]
        solid = coarse[0, j] + coarse[1, j] * gas
        for i in (2 * j + 1, 2 * j + 2):
            sc[0, i] = st[SA, i] + solid
            sc[1, i] = st[GA, i] + gas
        return carry

    lax.fori_loop(0, blocks, correct, 0, unroll=3)
    gas = coarse[2, blocks - 1] * gas_in + coarse[3, blocks - 1]
    gas_high = wide[5] * gas + wide[4]
    solid_high = wide[3] + wide[6] * gas_high
    sc[0, last] = st[SA, last] + solid_high
    sc[1, last] = st[GA, last] + gas_high

    view = Fields(st, sc)
    for i, is_after, solid, gas in ((0, False, solid_low, gas_in), (last, True, solid_high, gas_high)):
        side = 3 if is_after else 0
        fy = extra[side + 2]
        to = 9 if is_after else 7
        rs = extra[side] + wide[to] + fy * solid
        rg = extra[side + 1] + wide[to + 1] + (CONDUCT if is_after else CONDUCT + FLOW) * gas
        res = outer_residual(view, i, SA, rs, rg, fy, edge, is_after)
        sc[2, i], sc[3, i] = relaxed(view, i, SA, *res)

    def sweep(k, carry):
        stores = []
        for r in range(GROUP):
            i = GROUP * k + 1 + r
            new_s, new_g = relaxed(view, i, SA, *row_residual(view, i, SA, edge))
            stores += [((2, i), new_s), ((3, i), new_g)]
        for at, value in stores:
            sc[at] = value
        return carry

    lax.fori_loop(0, ny // GROUP, sweep, 0)

    def leaving(k):
        part = pl.ds(GROUP * k, GROUP)
        return pltpu.make_async_copy(done.at[:, part], out.at[:, part], sems.at[k])

    def final(k, carry):
        stores = []
        for r in range(GROUP):
            i = GROUP * k + 1 + r
            new_s, new_g = last_relaxed(view, i, SB, edge, slice(PAD, PAD + nx))
            stores += [((0, i - 1), new_s), ((1, i - 1), new_g)]
        for at, value in stores:
            done[at] = value
        leaving(k).start()
        return carry

    lax.fori_loop(0, ny // GROUP, final, 0)
    for k in range(ny // GROUP):
        leaving(k).wait()


class Fields:
    def __init__(self, st, sc):
        self.st, self.sc = st, sc

    def __getitem__(self, at):
        return (self.sc if at[0] <= GB else self.st)[at]


def cost(rows, cells):
    return pl.CostEstimate(flops=50 * rows * cells, bytes_accessed=16 * 4 * rows * cells, transcendentals=0)


def swap(x, axis, first):
    pairs = []
    for i in range(first, lax.axis_size(axis) - 1, 2):
        pairs += [(i, i + 1), (i + 1, i)]
    return lax.ppermute(x, axis, pairs)


def shards(temps, right_side, exchange, coupling):
    temps, right_side = (jnp.transpose(a, (0, 2, 1, 3)) for a in (temps, right_side))
    exchange, coupling = (jnp.transpose(a, (1, 0, 2)) for a in (exchange, coupling))
    temps, right_side, exchange, coupling = (
        pltpu.with_memory_space_constraint(a, pltpu.HBM) for a in (temps, right_side, exchange, coupling)
    )
    ny, nx, nz = exchange.shape
    ext = nx + 2 * PAD
    f32 = functools.partial(jax.ShapeDtypeStruct, dtype=jnp.float32)

    strip = f32((strip_height(ny), nz))
    state = f32((PLANES, ny + 2, ext, nz))
    one, two, st = pl.pallas_call(
        pack_kernel,
        out_shape=(strip, strip, state),
        in_specs=[HBM] * 4,
        out_specs=(VMEM,) * 3,
        scratch_shapes=[pltpu.SemaphoreType.DMA((12,))],
        compiler_params=PARAMS,
        name="pack_x",
    )(temps, right_side, exchange, coupling)
    one, two = swap(one, "gx", 0), swap(two, "gx", 1)

    def letter(planes):
        return f32((planes, ext - 2 * CROP, nz))

    st, early = pl.pallas_call(
        conduct_kernel,
        out_shape=(state, f32((EARLY, nx, nz))),
        in_specs=[VMEM],
        out_specs=(VMEM,) * 2,
        input_output_aliases={0: 0},
        compiler_params=PARAMS,
        cost_estimate=cost(2 * ny, ext * nz),
        name="conduct",
    )(st)
    early = swap(early, "gy", 1)
    st, across = pl.pallas_call(
        first_kernel,
        out_shape=(state, f32((across_parts(ext)[1], nz))),
        in_specs=[VMEM] * 3,
        out_specs=(VMEM,) * 2,
        input_output_aliases={0: 0},
        compiler_params=PARAMS,
        name="first",
    )(st, one, two)
    st, *beside = pl.pallas_call(
        other_kernel,
        out_shape=(state,) + (letter(THIRD),) * (MESSAGE // THIRD),
        in_specs=[VMEM] * 3,
        out_specs=(VMEM,) * (1 + MESSAGE // THIRD),
        input_output_aliases={0: 0},
        compiler_params=PARAMS,
        name="other",
    )(st, one, two)
    across = swap(across, "gy", 1)

    rows = f32((4, ny // 2, ext, nz))
    st, coarse = pl.pallas_call(
        inner_kernel,
        out_shape=(state, rows),
        in_specs=[VMEM] * 2,
        out_specs=(VMEM,) * 2,
        input_output_aliases={0: 0},
        compiler_params=PARAMS,
        cost_estimate=cost(4 * ny, ext * nz),
        name="inner",
    )(st, early)

    beside = [swap(part, "gy", 0) for part in beside]

    lay = Rows(nx)

    def tall(height):
        return f32(((height + 7) // 8 * 8, nz))

    letter_room = pltpu.VMEM((MESSAGE, ext, nz), jnp.float32)
    more = f32((6, ext, nz))
    st, coarse, extra = pl.pallas_call(
        near_kernel,
        out_shape=(state, rows, more),
        in_specs=[VMEM] * (2 + len(beside)),
        out_specs=(VMEM,) * 3,
        scratch_shapes=[letter_room],
        input_output_aliases={0: 0, 1: 1},
        compiler_params=PARAMS,
        name="near",
    )(st, coarse, *beside)
    st, coarse, extra, total, last_info, first_info, message = pl.pallas_call(
        second_kernel,
        out_shape=(state, rows, more, tall(lay.map), tall(lay.info), tall(lay.info + lay.rest), tall(lay.full)),
        in_specs=[VMEM] * 5,
        out_specs=(VMEM,) * 7,
        scratch_shapes=[letter_room, pltpu.VMEM((8, ext, nz), jnp.float32)],
        input_output_aliases={0: 0, 1: 1, 2: 2},
        compiler_params=PARAMS,
        name="second",
    )(st, coarse, extra, early, across)

    near, messages = total, [message]
    count = lax.axis_size("gy")
    radices, stride = stages(count), 1
    for place, radix in enumerate(radices[:-1]):
        swaps = matchings(count, radix, stride)
        if place:
            messages = [full_message(nx, total, last_info, first_info, senders) for senders, _ in swaps]
        others = exchange_stage(messages, swaps)
        final = radices[-1] if place == len(radices) - 2 else 0
        following = matchings(count, final, stride * radix) if final else []
        outs = [tall(lay.final if adjacent else lay.map) for _, adjacent in following] if final else [tall(lay.map)]
        near, *messages = pl.pallas_call(
            functools.partial(join_kernel, radix, stride, final, nx, place == 0),
            out_shape=(tall(lay.near), *outs),
            in_specs=[VMEM] * (3 + radix),
            out_specs=(VMEM,) * (1 + len(outs)),
            compiler_params=PARAMS,
            name="join",
        )(total, last_info, first_info, near, *others)
        total = total if final else messages[0]
        stride *= radix
    got = exchange_stage(messages, matchings(count, radices[-1], stride))

    out = pl.pallas_call(
        functools.partial(third_kernel, radices[-1], stride),
        out_shape=f32((2, ny, nx, nz)),
        in_specs=[VMEM] * (4 + len(got)),
        out_specs=HBM,
        scratch_shapes=[
            pltpu.VMEM((4, ny + 2, ext, nz), jnp.float32),
            pltpu.VMEM((11, ext, nz), jnp.float32),
            pltpu.VMEM(tall(lay.near).shape, jnp.float32),
            pltpu.VMEM((2, ny, nx, nz), jnp.float32),
            pltpu.SemaphoreType.DMA((ny // GROUP,)),
        ],
        compiler_params=PARAMS,
        name="third",
    )(st, extra, coarse, near, *got)
    return jnp.transpose(out, (0, 2, 1, 3))


def solution(mesh):
    return jax.shard_map(
        shards,
        mesh=mesh,
        in_specs=(
            P(None, "gx", "gy", None),
            P(None, "gx", "gy", None),
            P("gx", "gy", None),
            P("gx", "gy", None),
        ),
        out_specs=P(None, "gx", "gy", None),
        check_vma=False,
    )
```

```python
import functools

import jax
import jax.numpy as jnp
from jax import lax
from jax.experimental import pallas as pl
from jax.experimental.pallas import tpu as pltpu
from jax.sharding import PartitionSpec as P

SOLID_CAP, GAS_CAP, FLOW, CONDUCT, RELAX, LUMP = 0.5, 0.02, 40.0, 0.05, 0.8, 0.25
GAS_SELF = GAS_CAP + 4.5 * CONDUCT

PAD = 8
WX = 5
CROP = 4
(SA, GA, SB, GB, K, C, RS, RG, FX, FZ, H, FY, ASS, ASG, AGG) = range(15)
PLANES = 15
(M_S, M_G, M_K, M_C, M_FY, M_1S, M_1G, M_2S, M_2G) = range(9)
MESSAGE, EARLY, THIRD = 9, 7, 3

GROUP = 6

VMEM = pl.BlockSpec(memory_space=pltpu.VMEM)
HBM = pl.BlockSpec(memory_space=pltpu.HBM)
PARAMS = pltpu.CompilerParams(vmem_limit_bytes=40 * 1024 * 1024)


def up_x(v):
    return pltpu.roll(v, v.shape[0] - 1, 0)


def down_x(v):
    return pltpu.roll(v, 1, 0)


def up_z(v):
    return pltpu.roll(v, v.shape[1] - 1, 1)


def down_z(v):
    return pltpu.roll(v, 1, 1)


def lanes(shape):
    return lax.broadcasted_iota(jnp.int32, shape, 1)


def x_mask(shape, nx):
    row = lax.broadcasted_iota(jnp.int32, shape, 0)
    place, count = lax.axis_index("gx"), lax.axis_size("gx")
    low = jnp.where(place == 0, PAD, PAD - WX)
    high = jnp.where(place == count - 1, PAD + nx, PAD + nx + WX)
    return jnp.where((row >= low) & (row < high), 1.0, 0.0).astype(jnp.float32)


PAIRS = ((SA, GA), (C, RS), (RG, K))
STRIP_ROWS = 8 * len(PAIRS)


def strip_height(ny):
    return ny * STRIP_ROWS + (ny + 7) // 8 * 8


def sublanes(nz):
    return lax.broadcasted_iota(jnp.int32, (8, nz), 0)


def conductivity_of(s, exchange):
    return 1.0 + 4.0 * exchange * s * s * s


def strip_side(s, g, k, rs, rg, c, low):
    row = sublanes(s.shape[1])
    inn, shift = (3, 7) if low else (4, 1)
    k_out, s_out, g_out = (pltpu.roll(v, shift, 0) for v in (k, s, g))
    rs = rs + jnp.where(row == inn, 0.5 * (k + k_out) * s_out, 0.0)
    rg = rg + jnp.where(row == inn, CONDUCT * g_out, 0.0)
    values = {SA: s, GA: g, K: k, RS: rs, RG: rg, C: c}
    tiles = []
    for a, b in PAIRS:
        a, b = values[a], values[b]
        a, b = (a, pltpu.roll(b, 4, 0)) if low else (pltpu.roll(a, 4, 0), b)
        tiles.append(jnp.where(row < 4, a, b))
    return tiles, (k[4:5] if low else k[3:4])


def pack_kernel(temps, right, exchange, coupling, one, two, st, sems):
    even = lax.axis_index("gx") % 2 == 0
    ny, nx, nz = exchange.shape
    halves = [(0, ny // 2), (ny // 2, ny - ny // 2)]
    copies = [[], []]
    for k, (plane, ref) in enumerate(
        ((SA, temps.at[0]), (K, exchange), (GA, temps.at[1]), (C, coupling), (RS, right.at[0]), (RG, right.at[1]))
    ):
        for h, (start, count) in enumerate(halves):
            to = st.at[plane, pl.ds(1 + start, count), pl.ds(PAD, nx)]
            copies[h].append(pltpu.make_async_copy(ref.at[pl.ds(start, count)], to, sems.at[6 * h + k]))
    for copy in copies[0] + copies[1]:
        copy.start()
    for i in range(1, ny + 1):
        for h, (start, count) in enumerate(halves):
            if i == start + 1:
                for copy in copies[h]:
                    copy.wait()
        sides = []
        for start in (PAD, PAD + nx - 8):
            s, g, e, rs, rg, c = (st[plane, i, start : start + 8] for plane in (SA, GA, K, RS, RG, C))
            sides.append(strip_side(s, g, conductivity_of(s, e), rs, rg, c, start == PAD))
        (low, low_k), (high, high_k) = sides
        for p in range(len(PAIRS)):
            part = slice((i - 1) * STRIP_ROWS + 8 * p, (i - 1) * STRIP_ROWS + 8 * p + 8)
            one[part] = jnp.where(even, high[p], low[p])
            two[part] = jnp.where(even, low[p], high[p])
        part = slice(ny * STRIP_ROWS + i - 1, ny * STRIP_ROWS + i)
        one[part] = jnp.where(even, high_k, low_k)
        two[part] = jnp.where(even, low_k, high_k)


def conduct_kernel(st_in, st, early):
    del st_in
    planes, rows, ext, nz = st.shape
    ny, nx = rows - 2, ext - 2 * PAD
    odd = lax.axis_index("gy") % 2 == 1
    own = slice(PAD, PAD + nx)
    for i in range(1, ny + 1):
        st[K, i, own] = conductivity_of(st[SA, i, own], st[K, i, own])
    for is_odd, e, d in ((True, ny, ny - 1), (False, 1, 2)):

        @pl.when(odd == is_odd)
        def _():
            s, s_d, g, g_d = st[SA, e, own], st[SA, d, own], st[GA, e, own], st[GA, d, own]
            c, k, k_d = st[C, e, own], st[K, e, own], st[K, d, own]
            fx, fz, h, _ = faces(k)
            fy = 0.5 * (k + k_d)
            part_s, part_g = inner(s, g, c, h, fx, fz, edge_weights((nx, nz)))
            m_1s, m_1g = first_partial(st[RS, e, own] + part_s, st[RG, e, own] + part_g, s, s_d, g, g_d, fy, is_odd)
            for plane, value in enumerate((s, g, k, c, fy, m_1s, m_1g)):
                early[plane] = value


def place_halo(st, one, two, y, nx):
    even = lax.axis_index("gx") % 2 == 0
    ny, row = st.shape[1] - 2, sublanes(st.shape[3])
    i = y + 1

    def received(part):
        a, b = one[part], two[part]
        return jnp.where(even, b, a), jnp.where(even, a, b)

    for p, (plane_a, plane_b) in enumerate(PAIRS):
        before, after = received(slice(y * STRIP_ROWS + 8 * p, y * STRIP_ROWS + 8 * p + 8))
        before = {plane_a: pltpu.roll(before, 4, 0), plane_b: before}
        after = {plane_a: after, plane_b: pltpu.roll(after, 4, 0)}
        for plane in (plane_a, plane_b):
            low, high = jnp.where(row >= 4, before[plane], 0.0), jnp.where(row < 4, after[plane], 0.0)
            if plane == K:
                k_low, k_high = received(slice(ny * STRIP_ROWS + y, ny * STRIP_ROWS + y + 1))
                low, high = jnp.where(row == 3, k_low, low), jnp.where(row == 4, k_high, high)
            st[plane, i, :PAD] = low
            st[plane, i, PAD + nx :] = high


def inner(s, g, c, h, fx, fz, edge):
    t = c * (s - g)
    flux_x = fx * (up_x(s) - s)
    flux_z = fz * (up_z(s) - s)
    part_s = (flux_x - down_x(flux_x)) + (flux_z - down_z(flux_z)) - h * s - t
    part_g = (
        t
        - GAS_SELF * g
        + CONDUCT * (up_x(g) + down_x(g))
        + edge[0] * up_z(g)
        + edge[1] * down_z(g)
    )
    return part_s, part_g


def edge_weights(shape):
    lane = lanes(shape)
    weight = jnp.float32(0.25 * CONDUCT)
    return jnp.where(lane == shape[1] - 1, 0.0, weight), jnp.where(lane == 0, 0.0, weight)


def row_inner(st, i, s_at, edge):
    return inner(st[s_at, i], st[s_at + 1, i], st[C, i], st[H, i], st[FX, i], st[FZ, i], edge)


def row_residual(st, i, s_at, edge):
    part_s, part_g = row_inner(st, i, s_at, edge)
    s, g, before = st[s_at, i], st[s_at + 1, i], st[s_at + 1, i - 1]
    part_s += st[FY, i] * (st[s_at, i + 1] - s) + st[FY, i - 1] * (st[s_at, i - 1] - s)
    part_g += CONDUCT * (st[s_at + 1, i + 1] + before) - FLOW * (g - before)
    return st[RS, i] + part_s, st[RG, i] + part_g


def relaxed(st, i, s_at, res_s, res_g):
    s = st[s_at, i] + st[ASS, i] * res_s + st[ASG, i] * res_g
    g = st[s_at + 1, i] + st[ASG, i] * res_s + st[AGG, i] * res_g
    return s, g


def faces(k):
    lane = lanes(k.shape)
    end = k.shape[1] - 1
    fx = 0.5 * (k + up_x(k))
    fz = jnp.where(lane == end, 0.0, 0.125 * (k + up_z(k)))
    h = SOLID_CAP + jnp.where((lane == 0) | (lane == end), 0.125 * k, 0.0)
    return fx, fz, h, h + (fx + down_x(fx)) + (fz + down_z(fz))


def inverse(diag, c, mask):
    gas_diag = (GAS_SELF + FLOW) + c
    inv = (RELAX * mask) / (diag * gas_diag - c * c)
    return inv * gas_diag, inv * c, inv * diag


def last_relaxed(st, i, s_at, edge, own):
    full_s, full_g = st[s_at, i], st[s_at + 1, i]
    s, g = full_s[own], full_g[own]
    flux_x = st[FX, i] * (up_x(full_s) - full_s)
    flux_z = st[FZ, i, own] * (up_z(s) - s)
    c, before = st[C, i, own], st[s_at + 1, i - 1, own]
    t = c * (s - g)
    res_s = st[RS, i, own] + (flux_x[own] - down_x(flux_x)[own]) + (flux_z - down_z(flux_z)) - st[H, i, own] * s - t
    res_s += st[FY, i, own] * (st[s_at, i + 1, own] - s) + st[FY, i - 1, own] * (st[s_at, i - 1, own] - s)
    res_g = st[RG, i, own] + t - GAS_SELF * g + edge[0][own] * up_z(g) + edge[1][own] * down_z(g)
    res_g += CONDUCT * (up_x(full_g)[own] + down_x(full_g)[own] + st[s_at + 1, i + 1, own] + before) - FLOW * (g - before)
    ss, sg, gg = st[ASS, i, own], st[ASG, i, own], st[AGG, i, own]
    return s + ss * res_s + sg * res_g, g + sg * res_s + gg * res_g


def grouped(rows, work):
    for start in range(0, len(rows), GROUP):
        stores = []
        for i in rows[start : start + GROUP]:
            stores += work(i)
        for ref, at, value in stores:
            ref[at] = value


def looped(first, last, size, work):
    def group(k, carry):
        grouped([first + size * k + r for r in range(size)], work)
        return carry

    lax.fori_loop(0, (last - first) // size, group, 0)
    grouped(list(range(last - (last - first) % size, last)), work)


def row_coefficients(st, i, mask):
    fx, fz, h, diag = faces(st[K, i])
    fy = 0.5 * (st[K, i] + st[K, i + 1])
    before = 0.5 * (st[K, i] + st[K, i - 1])
    ss, sg, gg = inverse(diag + st[C, i] + fy + before, st[C, i], mask)
    values = ((FX, fx), (FZ, fz), (H, h), (FY, fy), (ASS, ss), (ASG, sg), (AGG, gg))
    return [(st, (plane, i), v) for plane, v in values]


def row_sweep(st, i, source, target, edge):
    s, g = relaxed(st, i, source, *row_residual(st, i, source, edge))
    return [(st, (target, i), s), (st, (target + 1, i), g)]


def first_partial(res_s, res_g, s, s_d, g, g_d, fy, onward):
    return res_s + fy * (s_d - s), res_g + CONDUCT * g_d - FLOW * (g - g_d if onward else g)


def send_planes(st, onward, edge):
    ny = st.shape[1] - 2
    e, d, near = (ny, ny - 1, ny - 1) if onward else (1, 2, 1)
    fy, s, g, g_d = st[FY, near], st[SA, e], st[GA, e], st[GA, d]
    part_s, part_g = row_inner(st, e, SA, edge)
    m_1s, m_1g = first_partial(st[RS, e] + part_s, st[RG, e] + part_g, s, st[SA, d], g, g_d, fy, onward)
    m_2s = st[RS, e] + fy * st[SB, d]
    m_2g = st[RG, e] + (CONDUCT + FLOW if onward else CONDUCT) * st[GB, d]
    return [s, g, st[K, e], st[C, e], fy, m_1s, m_1g, m_2s, m_2g]


def across_parts(ext):
    parts, at = [], 0
    for k in range(EARLY, MESSAGE):
        parts.append((k, CROP, ext - CROP, at))
        at += ext - 2 * CROP
    for k in range(EARLY):
        more = 1 if k in (M_1S, M_1G) else 0
        for low, high in ((CROP, PAD + more), (ext - PAD - more, ext - CROP)):
            parts.append((k, low, high, at))
            at += high - low
    return parts, (at + 7) // 8 * 8


def write_across(ref, k, value):
    for plane, low, high, at in across_parts(value.shape[0])[0]:
        if plane == k:
            ref[at : at + high - low] = value[low:high]


def read_across(early, across, outer, k):
    ext = outer.shape[1]
    if k < EARLY:
        outer[k, PAD : ext - PAD] = early[k]
    for plane, low, high, at in across_parts(ext)[0]:
        if plane == k:
            outer[k, low:high] = across[at : at + high - low]


def write_beside(refs, k, value):
    refs[k // THIRD][k % THIRD] = value[CROP : value.shape[0] - CROP]


def read_beside(refs, outer, k):
    outer[k, CROP : outer.shape[1] - CROP] = refs[k // THIRD][k % THIRD]


def first_end(st, one, two, after, write):
    planes, rows, ext, nz = st.shape
    ny, nx = rows - 2, ext - 2 * PAD
    mask = x_mask((ext, nz), nx)
    edge = edge_weights((ext, nz))
    e, d, f = (ny, ny - 1, ny - 2) if after else (1, 2, 3)
    for i in (e, d, f):
        place_halo(st, one, two, i - 1, nx)
    fx, fz, h, diag = faces(st[K, e])
    st[FX, e], st[FZ, e], st[H, e] = fx, fz, h
    st[FY, min(e, d)] = 0.5 * (st[K, e] + st[K, d])
    st[FY, min(d, f)] = 0.5 * (st[K, d] + st[K, f])
    grouped([d], lambda i: row_coefficients(st, i, mask))
    grouped([d], lambda i: row_sweep(st, i, SA, SB, edge))
    for k, value in enumerate(send_planes(st, after, edge)):
        write(k, value)


def either_first(st, one, two, after, write):
    for is_after in (True, False):

        @pl.when(after == is_after)
        def _():
            first_end(st, one, two, is_after, write)


def first_kernel(st_in, one, two, st, across):
    del st_in
    either_first(st, one, two, lax.axis_index("gy") % 2 == 1, functools.partial(write_across, across))


def other_kernel(st_in, one, two, st, *beside):
    del st_in
    either_first(st, one, two, lax.axis_index("gy") % 2 == 0, functools.partial(write_beside, beside))
    planes, rows, ext, nz = st.shape
    ny, nx = rows - 2, ext - 2 * PAD
    mask = x_mask((ext, nz), nx)
    for y in range(3, ny - 3):
        place_halo(st, one, two, y, nx)
    grouped(list(range(3, ny - 1)), lambda i: row_coefficients(st, i, mask))


def outer_residual(st, i, s_at, rs, rg, fy_out, edge, after):
    part_s, part_g = row_inner(st, i, s_at, edge)
    s, g = st[s_at, i], st[s_at + 1, i]
    if after:
        part_s += st[FY, i - 1] * (st[s_at, i - 1] - s)
        part_g += (CONDUCT + FLOW) * st[s_at + 1, i - 1]
    else:
        part_s += st[FY, i] * (st[s_at, i + 1] - s)
        part_g += CONDUCT * st[s_at + 1, i + 1]
    return rs + part_s - fy_out * s, rg + part_g - FLOW * g


def pair_x(v):
    row = lax.broadcasted_iota(jnp.int32, v.shape, 0)
    return v + jnp.where(row % 2 == 0, up_x(v), down_x(v))


def coarse_coefficients(c_sum, k_sum):
    per_solid = 1.0 / (4.0 * SOLID_CAP + c_sum + LUMP * k_sum)
    ratio = c_sum * per_solid
    return per_solid, ratio, 1.0 / ((4.0 * GAS_CAP + 2.0 * FLOW) + c_sum - c_sum * ratio)


def coarse_row(st, coarse, j, mask, edge):
    i = 2 * j + 1
    res_s, res_g = row_residual(st, i, SA, edge)
    more_s, more_g = row_residual(st, i + 1, SA, edge)
    res_s, res_g = pair_x((res_s + more_s) * mask), pair_x((res_g + more_g) * mask)
    c_sum = pair_x(st[C, i] + st[C, i + 1])
    per_solid, ratio, per_gas = coarse_coefficients(c_sum, pair_x(st[K, i] + st[K, i + 1]))
    lead = res_s * per_solid
    values = (lead, ratio, (2.0 * FLOW) * per_gas, (res_g + c_sum * lead) * per_gas)
    return [(coarse, (k, j), v) for k, v in enumerate(values)]


def inner_kernel(st_in, early, st, coarse):
    del st_in, early
    planes, rows, ext, nz = st.shape
    ny, nx = rows - 2, ext - 2 * PAD
    shape = (ext, nz)
    mask = x_mask(shape, nx)
    edge = edge_weights(shape)
    looped(3, ny - 1, 4, lambda i: row_sweep(st, i, SA, SB, edge))
    looped(3, ny - 1, 4, lambda i: row_sweep(st, i, SB, SA, edge))
    grouped(list(range(2, ny // 2 - 2)), lambda j: coarse_row(st, coarse, j, mask, edge))


def end_work(st, coarse, extra, read, outer, is_after):
    planes, rows, ext, nz = st.shape
    ny, nx = rows - 2, ext - 2 * PAD
    me, count = lax.axis_index("gy"), lax.axis_size("gy")
    mask = x_mask((ext, nz), nx)
    inside = jnp.where(me == (count - 1 if is_after else 0), 0.0, mask)
    edge = edge_weights((ext, nz))
    zeros = jnp.zeros((PAD, nz), jnp.float32)
    for k in range(MESSAGE):
        outer[k, :PAD] = zeros
        outer[k, ext - PAD :] = zeros
        read(outer, k)

    o, e, near = (ny + 1, ny, ny) if is_after else (0, 1, 0)
    to_o = CONDUCT + FLOW if is_after else CONDUCT
    s_o, g_o, k_o, c_o, fy_out = (outer[plane] for plane in (M_S, M_G, M_K, M_C, M_FY))
    fy = 0.5 * (k_o + st[K, e])
    fx, fz, h, diag = faces(k_o)
    inv_o = inverse(diag + c_o + fy_out + fy, c_o, inside)
    fx_e, fz_e = st[FX, e], st[FZ, e]
    diag = st[H, e] + (fx_e + down_x(fx_e)) + (fz_e + down_z(fz_e)) + st[C, e] + fy
    inv_e = inverse(diag + st[FY, near - 1 if is_after else near + 1], st[C, e], mask)
    for plane, value in ((SA, s_o), (GA, g_o), (K, k_o), (C, c_o), (FX, fx), (FZ, fz), (H, h)):
        st[plane, o] = value
    st[FY, near] = fy
    for k in range(3):
        st[ASS + k, o], st[ASS + k, e] = inv_o[k], inv_e[k]

    res = outer[M_1S] + fy * (st[SA, e] - s_o), outer[M_1G] + to_o * st[GA, e]
    new_o = relaxed(st, o, SA, *res)
    stores = row_sweep(st, e, SA, SB, edge)
    st[SB, o], st[GB, o] = new_o
    for ref, at, value in stores:
        ref[at] = value
    res = outer_residual(st, o, SB, outer[M_2S], outer[M_2G], fy_out, edge, is_after)
    new_o = relaxed(st, o, SB, *res)
    ends = [e - 1, e] if is_after else [e, e + 1]
    grouped(ends, lambda i: row_sweep(st, i, SB, SA, edge))
    st[SA, o], st[GA, o] = new_o
    for k, plane in enumerate((M_2S, M_2G, M_FY)):
        extra[(3 if is_after else 0) + k] = outer[plane]
    blocks = ny // 2
    stores = []
    for j in (blocks - 2, blocks - 1) if is_after else (0, 1):
        stores += coarse_row(st, coarse, j, mask, edge)
    for ref, at, value in stores:
        ref[at] = value


def either_end(after, st, coarse, extra, read, outer):
    for is_after in (True, False):

        @pl.when(after == is_after)
        def _():
            end_work(st, coarse, extra, read, outer, is_after)


def near_kernel(st_in, coarse_in, *refs):
    beside, (st, coarse, extra, outer) = refs[:-4], refs[-4:]
    del st_in, coarse_in
    either_end(lax.axis_index("gy") % 2 == 0, st, coarse, extra, functools.partial(read_beside, beside), outer)


def second_kernel(st_in, coarse_in, extra_in, early, across, *refs):
    st, coarse, extra, total, last_info, first_info, message, outer, squeeze = refs
    del st_in, coarse_in, extra_in
    planes, rows, ext, nz = st.shape
    ny, nx = rows - 2, ext - 2 * PAD
    me = lax.axis_index("gy")
    either_end(me % 2 == 1, st, coarse, extra, functools.partial(read_across, early, across), outer)

    blocks = ny // 2
    for k in range(4):
        squeeze[k] = coarse[k, 0]
    slopes, offsets = coarse[2, 0], coarse[3, 0]
    for j in range(1, blocks):
        slope = coarse[2, j]
        slopes, offsets = slope * slopes, slope * offsets + coarse[3, j]
        coarse[2, j], coarse[3, j] = slopes, offsets
    squeeze[4], squeeze[5], squeeze[6], squeeze[7] = slopes, offsets, coarse[0, blocks - 1], coarse[1, blocks - 1]

    span = nx // 2 + 2
    lead, ratio, slope, offset, slopes, offsets, lead_last, ratio_last = (
        squeeze[k, pl.ds(PAD - 2, span, 2), :] for k in range(8)
    )
    part = slice(PAD, PAD + nx)

    def increments(d, face, gas):
        return [(st[FY, face] * (st[SA, d] - st[SB, d]))[part], (gas * (st[GA, d] - st[GB, d]))[part]]

    onward = [lead_last, ratio_last] + increments(ny - 1, ny - 1, CONDUCT + FLOW)
    back = [lead, offset] + increments(2, 1, CONDUCT) + [slope, ratio]
    write_rows(total, [slopes, offsets])
    write_rows(last_info, onward)
    write_rows(first_info, back)
    for go, info in ((True, onward), (False, back)):

        @pl.when((me % 2 == 0) == go)
        def _():
            write_rows(message, [slopes, offsets] + info)


def write_rows(ref, values):
    at = 0
    for value in values:
        ref[at : at + value.shape[0]] = value
        at += value.shape[0]


class Rows:
    def __init__(self, nx):
        self.span = nx // 2 + 2
        self.map = 2 * self.span
        self.info = self.map + 2 * nx
        self.rest = self.map
        self.final = self.map + self.info
        self.full = self.final + self.rest
        self.low = self.map
        self.high = self.low + self.info
        self.near = self.high + self.info + self.rest


def source(at, k, radix):
    if radix & (radix - 1) == 0:
        return at ^ k
    return (at + radix - k) % radix


def matchings(count, radix, stride):
    if (count, radix, stride) == (8, 4, 2):
        swaps = ((1, 2), (3, 4), (5, 6), (0, 7)), ((0, 4), (1, 6), (2, 5), (3, 7)), ((0, 3), (1, 5), (2, 6), (4, 7))
        out = []
        for pairs in swaps:
            senders = [0] * count
            for a, b in pairs:
                senders[a], senders[b] = b, a
            out.append((senders, len(out) == 0))
        return out
    out = []
    for k in range(1, radix):
        senders = []
        for me in range(count):
            at, low = me // stride % radix, me % stride
            senders.append(me - low + (source(at, k, radix) - at) * stride + (stride - 1 - low))
        out.append((senders, any(abs(source(at, k, radix) - at) == 1 for at in range(radix))))
    return sorted(out, key=lambda item: not item[1])


def look_up(table):
    me, value = lax.axis_index("gy"), jnp.int32(table[0])
    for k in range(1, len(table)):
        value = jnp.where(me == k, table[k], value)
    return value


def stages(count):
    if count % 2:
        return [1, count]
    out, rest = [2], count // 2
    while rest > 1:
        radix = next((r for r in (8, 4, 2) if rest % r == 0), rest)
        out.append(radix)
        rest //= radix
    return out if len(out) > 1 else out + [1]


def exchange_stage(messages, swaps):
    return [
        lax.ppermute(message, "gy", [(sender, me) for me, sender in enumerate(senders)])
        for (senders, near), message in zip(swaps, messages)
    ]


class Group:
    def __init__(self, radix, stride, others, nx):
        self.radix, self.others, self.nx = radix, others, nx
        me = lax.axis_index("gy")
        self.swaps = [
            (look_up([sender // stride % radix for sender in senders]), near)
            for senders, near in matchings(lax.axis_size("gy"), radix, stride)
        ]
        self.at = lax.rem(lax.div(me, stride), radix)
        low = lax.rem(me, stride)
        self.lowest, self.highest = low == 0, low == stride - 1

    def map_of(self, place, own):
        rows = Rows(self.nx)
        out = own
        for (sender, near), ref in zip(self.swaps, self.others):
            here = sender == place
            got = [ref[i * rows.span : (i + 1) * rows.span] for i in range(2)]
            out = got if out is None else [jnp.where(here, new, old) for new, old in zip(got, out)]
        return out

    def ahead(self, slope, offset):
        a, b = jnp.ones_like(slope), jnp.zeros_like(slope)
        for place in range(self.radix - 1):
            new_a, new_b = self.map_of(place, None)
            below = place < self.at
            a, b = jnp.where(below, new_a * a, a), jnp.where(below, new_a * b + new_b, b)
        return slope * a, slope * b + offset

    def total(self, own):
        a, b = self.map_of(0, own)
        for place in range(1, self.radix):
            new_a, new_b = self.map_of(place, own)
            a, b = new_a * a, new_a * b + new_b
        return a, b

    def collect(self, near, final):
        rows = Rows(self.nx)
        for (place, adjacent), ref in zip(self.swaps, self.others):
            if not adjacent:
                continue

            @pl.when(self.lowest & (place == self.at - 1))
            def _():
                near[rows.low : rows.low + rows.info] = ref[rows.map : rows.final]

            @pl.when(self.highest & (place == self.at + 1))
            def _():
                near[rows.high : rows.high + rows.info] = ref[rows.map : rows.final]
                rest = slice(0, rows.map) if final else slice(rows.final, rows.full)
                near[rows.high + rows.info : rows.near] = ref[rest]


def start_near(near, nx, nz):
    rows = Rows(nx)
    near[: rows.span] = jnp.ones((rows.span, nz), jnp.float32)
    near[rows.span :] = jnp.zeros((near.shape[0] - rows.span, nz), jnp.float32)


def join_kernel(radix, stride, final, nx, is_first, *refs):
    rows = Rows(nx)
    total, last_info, first_info, near_in = refs[:4]
    others, near, outs = refs[4 : 3 + radix], refs[3 + radix], refs[4 + radix :]
    nz = near.shape[1]
    if is_first:
        start_near(near, nx, nz)
    else:
        near[...] = near_in[...]
    group = Group(radix, stride, others, nx)
    own = [total[i * rows.span : (i + 1) * rows.span] for i in range(2)]
    ahead = group.ahead(near[: rows.span], near[rows.span : rows.map])
    write_rows(near, ahead)
    group.collect(near, False)
    whole = group.total(own)
    if final == 0:
        write_rows(outs[0], whole)
        return
    me, count = lax.axis_index("gy"), lax.axis_size("gy")
    for (senders, adjacent), out in zip(matchings(count, final, stride * radix), outs):
        up = look_up(senders) > me
        if not adjacent:
            write_rows(out, whole)
            continue

        @pl.when(up)
        def _():
            write_rows(out, whole)
            out[rows.map : rows.final] = last_info[: rows.info]

        @pl.when(jnp.logical_not(up))
        def _():
            out[: rows.map] = first_info[rows.info : rows.info + rows.rest]
            out[rows.map : rows.final] = first_info[: rows.info]


def full_message(nx, total, last_info, first_info, senders):
    rows = Rows(nx)
    onward = jnp.concatenate([total[: rows.map], last_info[: rows.info], first_info[rows.info : rows.info + rows.rest]])
    back = jnp.concatenate([total[: rows.map], first_info[: rows.info + rows.rest]])
    message = jnp.where(look_up(senders) > lax.axis_index("gy"), onward, back)
    return jnp.pad(message, ((0, -rows.full % 8), (0, 0)))


def third_kernel(radix, stride, *refs):
    st, extra, coarse, near_in = refs[:4]
    others, (out, sc, wide, near, done, sems) = refs[4 : 3 + radix], refs[3 + radix :]
    planes, rows, ext, nz = st.shape
    ny, nx = rows - 2, ext - 2 * PAD
    edge = edge_weights((ext, nz))
    blocks = ny // 2

    lay = Rows(nx)
    span = lay.span
    near[...] = near_in[...]
    group = Group(radix, stride, others, nx)
    if radix > 1:
        group.collect(near, True)
    gas_in = group.ahead(near[:span], near[span : lay.map])[1]
    at_high = lay.high + lay.info
    starts = [lay.low, lay.low + span, lay.high, lay.high + span, at_high, at_high + span]
    for k, v in enumerate([gas_in] + [near[start : start + span] for start in starts]):
        wide[k, : PAD - 2] = jnp.zeros((PAD - 2, nz), jnp.float32)
        wide[k, ext - PAD + 2 :] = jnp.zeros((PAD - 2, nz), jnp.float32)
        wide[k, pl.ds(PAD - 2, span, 2), :] = v
        wide[k, pl.ds(PAD - 1, span, 2), :] = v
    for k, start in enumerate((lay.low, lay.low + nx, lay.high, lay.high + nx)):
        start += lay.map
        wide[7 + k, :PAD] = jnp.zeros((PAD, nz), jnp.float32)
        wide[7 + k, ext - PAD :] = jnp.zeros((PAD, nz), jnp.float32)
        wide[7 + k, PAD : PAD + nx] = near[start : start + nx]

    gas_in = wide[0]
    last = ny + 1
    solid_low = wide[1] + wide[2] * gas_in
    sc[0, 0] = st[SA, 0] + solid_low
    sc[1, 0] = st[GA, 0] + gas_in

    def correct(j, carry):
        gas = coarse[2, j] * gas_in + coarse[3, j]
        solid = coarse[0, j] + coarse[1, j] * gas
        for i in (2 * j + 1, 2 * j + 2):
            sc[0, i] = st[SA, i] + solid
            sc[1, i] = st[GA, i] + gas
        return carry

    lax.fori_loop(0, blocks, correct, 0)
    gas = coarse[2, blocks - 1] * gas_in + coarse[3, blocks - 1]
    gas_high = wide[5] * gas + wide[4]
    solid_high = wide[3] + wide[6] * gas_high
    sc[0, last] = st[SA, last] + solid_high
    sc[1, last] = st[GA, last] + gas_high

    view = Fields(st, sc)
    for i, is_after, solid, gas in ((0, False, solid_low, gas_in), (last, True, solid_high, gas_high)):
        side = 3 if is_after else 0
        fy = extra[side + 2]
        to = 9 if is_after else 7
        rs = extra[side] + wide[to] + fy * solid
        rg = extra[side + 1] + wide[to + 1] + (CONDUCT if is_after else CONDUCT + FLOW) * gas
        res = outer_residual(view, i, SA, rs, rg, fy, edge, is_after)
        sc[2, i], sc[3, i] = relaxed(view, i, SA, *res)

    def sweep(k, carry):
        stores = []
        for r in range(GROUP):
            i = GROUP * k + 1 + r
            new_s, new_g = relaxed(view, i, SA, *row_residual(view, i, SA, edge))
            stores += [((2, i), new_s), ((3, i), new_g)]
        for at, value in stores:
            sc[at] = value
        return carry

    lax.fori_loop(0, ny // GROUP, sweep, 0)

    def leaving(k):
        part = pl.ds(GROUP * k, GROUP)
        return pltpu.make_async_copy(done.at[:, part], out.at[:, part], sems.at[k])

    def final(k, carry):
        stores = []
        for r in range(GROUP):
            i = GROUP * k + 1 + r
            new_s, new_g = last_relaxed(view, i, SB, edge, slice(PAD, PAD + nx))
            stores += [((0, i - 1), new_s), ((1, i - 1), new_g)]
        for at, value in stores:
            done[at] = value
        leaving(k).start()
        return carry

    lax.fori_loop(0, ny // GROUP, final, 0)
    for k in range(ny // GROUP):
        leaving(k).wait()


class Fields:
    def __init__(self, st, sc):
        self.st, self.sc = st, sc

    def __getitem__(self, at):
        return (self.sc if at[0] <= GB else self.st)[at]


def cost(rows, cells):
    return pl.CostEstimate(flops=50 * rows * cells, bytes_accessed=16 * 4 * rows * cells, transcendentals=0)


def swap(x, axis, first):
    pairs = []
    for i in range(first, lax.axis_size(axis) - 1, 2):
        pairs += [(i, i + 1), (i + 1, i)]
    return lax.ppermute(x, axis, pairs)


def shards(temps, right_side, exchange, coupling):
    temps, right_side = (jnp.transpose(a, (0, 2, 1, 3)) for a in (temps, right_side))
    exchange, coupling = (jnp.transpose(a, (1, 0, 2)) for a in (exchange, coupling))
    temps, right_side, exchange, coupling = (
        pltpu.with_memory_space_constraint(a, pltpu.HBM) for a in (temps, right_side, exchange, coupling)
    )
    ny, nx, nz = exchange.shape
    ext = nx + 2 * PAD
    f32 = functools.partial(jax.ShapeDtypeStruct, dtype=jnp.float32)

    strip = f32((strip_height(ny), nz))
    state = f32((PLANES, ny + 2, ext, nz))
    one, two, st = pl.pallas_call(
        pack_kernel,
        out_shape=(strip, strip, state),
        in_specs=[HBM] * 4,
        out_specs=(VMEM,) * 3,
        scratch_shapes=[pltpu.SemaphoreType.DMA((12,))],
        compiler_params=PARAMS,
        name="pack_x",
    )(temps, right_side, exchange, coupling)
    one, two = swap(one, "gx", 0), swap(two, "gx", 1)

    def letter(planes):
        return f32((planes, ext - 2 * CROP, nz))

    st, early = pl.pallas_call(
        conduct_kernel,
        out_shape=(state, f32((EARLY, nx, nz))),
        in_specs=[VMEM],
        out_specs=(VMEM,) * 2,
        input_output_aliases={0: 0},
        compiler_params=PARAMS,
        cost_estimate=cost(2 * ny, ext * nz),
        name="conduct",
    )(st)
    early = swap(early, "gy", 1)
    st, across = pl.pallas_call(
        first_kernel,
        out_shape=(state, f32((across_parts(ext)[1], nz))),
        in_specs=[VMEM] * 3,
        out_specs=(VMEM,) * 2,
        input_output_aliases={0: 0},
        compiler_params=PARAMS,
        name="first",
    )(st, one, two)
    st, *beside = pl.pallas_call(
        other_kernel,
        out_shape=(state,) + (letter(THIRD),) * (MESSAGE // THIRD),
        in_specs=[VMEM] * 3,
        out_specs=(VMEM,) * (1 + MESSAGE // THIRD),
        input_output_aliases={0: 0},
        compiler_params=PARAMS,
        name="other",
    )(st, one, two)
    across = swap(across, "gy", 1)

    rows = f32((4, ny // 2, ext, nz))
    st, coarse = pl.pallas_call(
        inner_kernel,
        out_shape=(state, rows),
        in_specs=[VMEM] * 2,
        out_specs=(VMEM,) * 2,
        input_output_aliases={0: 0},
        compiler_params=PARAMS,
        cost_estimate=cost(4 * ny, ext * nz),
        name="inner",
    )(st, early)

    beside = [swap(part, "gy", 0) for part in beside]

    lay = Rows(nx)

    def tall(height):
        return f32(((height + 7) // 8 * 8, nz))

    letter_room = pltpu.VMEM((MESSAGE, ext, nz), jnp.float32)
    more = f32((6, ext, nz))
    st, coarse, extra = pl.pallas_call(
        near_kernel,
        out_shape=(state, rows, more),
        in_specs=[VMEM] * (2 + len(beside)),
        out_specs=(VMEM,) * 3,
        scratch_shapes=[letter_room],
        input_output_aliases={0: 0, 1: 1},
        compiler_params=PARAMS,
        name="near",
    )(st, coarse, *beside)
    st, coarse, extra, total, last_info, first_info, message = pl.pallas_call(
        second_kernel,
        out_shape=(state, rows, more, tall(lay.map), tall(lay.info), tall(lay.info + lay.rest), tall(lay.full)),
        in_specs=[VMEM] * 5,
        out_specs=(VMEM,) * 7,
        scratch_shapes=[letter_room, pltpu.VMEM((8, ext, nz), jnp.float32)],
        input_output_aliases={0: 0, 1: 1, 2: 2},
        compiler_params=PARAMS,
        name="second",
    )(st, coarse, extra, early, across)

    near, messages = total, [message]
    count = lax.axis_size("gy")
    radices, stride = stages(count), 1
    for place, radix in enumerate(radices[:-1]):
        swaps = matchings(count, radix, stride)
        if place:
            messages = [full_message(nx, total, last_info, first_info, senders) for senders, _ in swaps]
        others = exchange_stage(messages, swaps)
        final = radices[-1] if place == len(radices) - 2 else 0
        following = matchings(count, final, stride * radix) if final else []
        outs = [tall(lay.final if adjacent else lay.map) for _, adjacent in following] if final else [tall(lay.map)]
        near, *messages = pl.pallas_call(
            functools.partial(join_kernel, radix, stride, final, nx, place == 0),
            out_shape=(tall(lay.near), *outs),
            in_specs=[VMEM] * (3 + radix),
            out_specs=(VMEM,) * (1 + len(outs)),
            compiler_params=PARAMS,
            name="join",
        )(total, last_info, first_info, near, *others)
        total = total if final else messages[0]
        stride *= radix
    got = exchange_stage(messages, matchings(count, radices[-1], stride))

    out = pl.pallas_call(
        functools.partial(third_kernel, radices[-1], stride),
        out_shape=f32((2, ny, nx, nz)),
        in_specs=[VMEM] * (4 + len(got)),
        out_specs=HBM,
        scratch_shapes=[
            pltpu.VMEM((4, ny + 2, ext, nz), jnp.float32),
            pltpu.VMEM((11, ext, nz), jnp.float32),
            pltpu.VMEM(tall(lay.near).shape, jnp.float32),
            pltpu.VMEM((2, ny, nx, nz), jnp.float32),
            pltpu.SemaphoreType.DMA((ny // GROUP,)),
        ],
        compiler_params=PARAMS,
        name="third",
    )(st, extra, coarse, near, *got)
    return jnp.transpose(out, (0, 2, 1, 3))


def solution(mesh):
    return jax.shard_map(
        shards,
        mesh=mesh,
        in_specs=(
            P(None, "gx", "gy", None),
            P(None, "gx", "gy", None),
            P("gx", "gy", None),
            P("gx", "gy", None),
        ),
        out_specs=P(None, "gx", "gy", None),
        check_vma=False,
    )
```
